32 devices in a mesh: dp: 16 (over z, y, x), tensor: 2 (over core).
Axes of the slice: x: 2, y: 2, z: 4, core: 2. Of those that a mesh axis runs over, the one named last changes fastest.
Arguments:
- latents: bfloat16 [4160, 1536], P(('dp', 'tensor')), may hold values from -6 to 6
- context: bfloat16 [8192, 1536], P('dp'), may hold values from -6 to 6
- cotangent: bfloat16 [4160, 1536], P(('dp', 'tensor')), may hold values from -6 to 6
- positions: int32 [3, 4160], P(None, 'dp'), may hold values from 0 to 63
- step_ids: int32 [16], P('dp'), may hold values from 0 to 15
- owners: int32 [118], replicated, may hold values from 0 to 15, as said below
- time_table: float32 [16, 6, 1536], replicated, may hold values from -3 to 3
- master: float32 [2, 144, 1536, 128], P('tensor', 'dp'), may hold values from -6 to 6
- first_moment: float32 [2, 144, 1536, 128], P('tensor', 'dp'), as said below
- second_moment: float32 [2, 144, 1536, 128], P('tensor', 'dp'), as said below
- head_params: float32 [2, 12160], P('tensor'), as said below
- head_first: float32 [2, 12160], P('tensor'), may hold values from -20 to 20
- head_second: float32 [2, 12160], P('tensor'), may hold values from 0.52 to 8.32
- shared_params: float32 [11, 1536], replicated, as said below
- shared_first: float32 [11, 1536], replicated, may hold values from -20 to 20
- shared_second: float32 [11, 1536], replicated, may hold values from 0.52 to 8.32
Outputs:
- block_out: bfloat16 [4160, 1536], P(('dp', 'tensor'))
- grad_latents: float32 [4160, 1536], P(('dp', 'tensor'))
- new_master: float32 [2, 144, 1536, 128], P('tensor', 'dp')
- new_first: float32 [2, 144, 1536, 128], P('tensor', 'dp')
- new_second: float32 [2, 144, 1536, 128], P('tensor', 'dp')
- new_head: float32 [2, 12160], P('tensor')
- new_head_first: float32 [2, 12160], P('tensor')
- new_head_second: float32 [2, 12160], P('tensor')
- new_shared: float32 [11, 1536], replicated
- new_shared_first: float32 [11, 1536], replicated
- new_shared_second: float32 [11, 1536], replicated
The draws below stay inside these ranges and needn't reach their ends.
Inputs may be any that keep to these rules, and one draw needn't show every extreme that they name: `owners`: no owner holds more than 9 blocks, and some owner holds exactly 9. `first_moment`: entries are finite, of both signs. `second_moment`: entries are positive. `head_params`: the gains among them are positive. `shared_params`: the norm gain row is positive.
All inputs are finite; a program needn't handle non-finite values.
Results may differ from the reference program's by a relative error of at most 0.014.
Values may be sent and summed in bfloat16 or wider, within the bound.
A program may use at most 512 MiB of HBM per device.

```python
import math
import jax
import jax.numpy as jnp
from jax import lax

D = 1536
HEADS = 12
HEAD = 128
FF = 8960
TEXT = 512
SEQ = 260
TSTEPS = 16
STEPC = 10
TILES = 118
SLOTS = 9
HEADVEC = 12160
TOKENS = 4160
TEXTS = 8192
N_DP = 16
N_TENSOR = 2


def owner_list(key):
    base = jax.random.fold_in(key, 101)
    key_heavy, key_rank, key_tiles = jax.random.split(base, 3)
    spots = N_DP * SLOTS
    heavy = jax.random.randint(key_heavy, (), 0, N_DP)
    ranking = jax.random.permutation(key_rank, spots)
    owner_of_spot = jnp.arange(spots) // SLOTS
    scores = ranking - spots * (owner_of_spot == heavy).astype(jnp.int32)
    ordered = jnp.argsort(scores, stable=True)
    chosen = jax.random.permutation(key_tiles, TILES)
    return (ordered[chosen] // SLOTS).astype(jnp.int32)


def spot_estimates(key):
    owners = owner_list(key)
    indices = jnp.arange(TILES, dtype=jnp.int32)
    same_owner = (owners[:, None] == owners[None, :]) & (indices[None, :] < indices[:, None])
    places = owners * SLOTS + jnp.sum(same_owner.astype(jnp.int32), axis=1)
    spots = jnp.arange(N_DP * SLOTS, dtype=jnp.int32)
    holder = jnp.sum(jnp.where(places[None, :] == spots[:, None], indices[None, :] + 1, 0), axis=1) - 1
    heads_here = HEADS // N_TENSOR
    blocks_here = FF // (HEAD * N_TENSOR)
    rows_tok = math.sqrt(TOKENS)
    rows_text = math.sqrt(TEXTS)
    scale_in = D ** (-0.5)
    scale_out = HEADS ** (-0.5)
    scale_down = FF ** (-0.5)
    estimate = jnp.where(indices < 3 * heads_here, 0.8 * scale_in * rows_tok, jnp.where(indices < 4 * heads_here, 0.06 * scale_out * rows_tok, jnp.where(indices < 5 * heads_here, 0.8 * scale_in * rows_tok, jnp.where(indices < 7 * heads_here, 0.8 * scale_in * rows_text, jnp.where(indices < 8 * heads_here, 0.1 * scale_out * rows_tok, jnp.where(indices < 8 * heads_here + blocks_here, 0.18 * scale_in * rows_tok, 0.4 * scale_down * rows_tok))))))
    estimate = estimate.astype(jnp.float32)
    fallback = jnp.mean(estimate)
    return jnp.where(holder >= 0, estimate[jnp.maximum(holder, 0)], fallback)


def draw_owners(key, part):
    return owner_list(key)


def draw_first_moment(key, part):
    scale = spot_estimates(key)
    noise = jax.random.normal(jax.random.fold_in(key, 202), (N_TENSOR, N_DP * SLOTS, D, HEAD), jnp.float32)
    return 0.1111 * scale[None, :, None, None] * noise


def draw_second_moment(key, part):
    scale = spot_estimates(key)
    factor = jnp.exp(jax.random.uniform(jax.random.fold_in(key, 303), (N_TENSOR, N_DP * SLOTS, D, HEAD), jnp.float32, math.log(0.5), math.log(8.0)))
    return 0.001001 * (scale * scale)[None, :, None, None] * factor


def draw_head_params(key, part):
    key_noise, key_gain = jax.random.split(jax.random.fold_in(key, 404))
    segment = jnp.arange(HEADVEC) // (D // N_TENSOR)
    is_gain = (segment == 3) | (segment == 4) | (segment == 8) | (segment == 9)
    noise = 0.5 * jax.random.normal(key_noise, (N_TENSOR, HEADVEC), jnp.float32)
    gains = jnp.exp(jax.random.uniform(key_gain, (N_TENSOR, HEADVEC), jnp.float32, math.log(0.5), math.log(2.0)))
    return jnp.where(is_gain[None, :], gains, noise)


def draw_shared_params(key, part):
    key_noise, key_gain = jax.random.split(jax.random.fold_in(key, 505))
    row_ids = jnp.arange(11)[:, None]
    noise = 0.5 * jax.random.normal(key_noise, (11, D), jnp.float32)
    gains = jnp.exp(jax.random.uniform(key_gain, (11, D), jnp.float32, math.log(0.5), math.log(2.0)))
    return jnp.where(row_ids == 3, gains, noise)


def touch_ends(array, rng, smallest, high):
    index_at = [jax.random.randint(jax.random.fold_in(rng, axis), (), 0, length) for axis, length in enumerate(array.shape)]
    widest = array.shape.index(max(array.shape))
    neighbour = index_at[:widest] + [(index_at[widest] + 1) % array.shape[widest]] + index_at[widest + 1:]
    return array.at[tuple(index_at)].set(smallest).at[tuple(neighbour)].set(high)


def block_scale(stream_key, dims, pieces, low, largest):
    factor_of, own = 1.0, jax.random.fold_in(stream_key, 6)
    for position, parts in pieces:
        heights = jnp.exp(jax.random.uniform(jax.random.fold_in(own, position), (parts,), jnp.float32, low / len(pieces), largest / len(pieces)))
        factor_of = factor_of * jnp.repeat(heights, dims[position] // parts).reshape([-1 if axis == position else 1 for axis in range(len(dims))])
    return factor_of


def bell_draw(stream_key, extent, scale, bound, pieces=(), kind=jnp.bfloat16):
    gain = block_scale(stream_key, extent, pieces, -0.22, 0.18) if pieces else 1.0
    result = jax.random.normal(stream_key, extent, jnp.float32) * scale * gain
    return jnp.minimum(jnp.maximum(result, -bound), bound).astype(kind)


def setup_inputs(seed: int = 0) -> dict:
    arg_keys = jax.random.split(jax.random.key(seed), 17)
    latents = bell_draw(arg_keys[0], (TOKENS, D), 1.0, 6.0, ((0, 32),))
    context = bell_draw(arg_keys[1], (TEXTS, D), 1.0, 6.0, ((0, 16),))
    cotangent = bell_draw(arg_keys[2], (TOKENS, D), 1.0, 6.0, ((0, 32),))
    positions = touch_ends(jax.random.randint(arg_keys[3], (3, TOKENS), 0, 64), jax.random.fold_in(arg_keys[3], 1), 0, 63).astype(jnp.int32)
    step_ids = touch_ends(jax.random.randint(arg_keys[4], (N_DP,), 0, TSTEPS), jax.random.fold_in(arg_keys[4], 1), 0, TSTEPS - 1).astype(jnp.int32)
    owners = draw_owners(jax.random.fold_in(arg_keys[16], 71), 0)
    time_table = bell_draw(arg_keys[6], (TSTEPS, 6, D), 0.5, 3.0, (), jnp.float32)
    master = bell_draw(arg_keys[7], (N_TENSOR, N_DP * SLOTS, D, HEAD), 1.0, 6.0, ((0, 2), (1, 16)), jnp.float32)
    first_moment = draw_first_moment(jax.random.fold_in(arg_keys[16], 71), 0)
    second_moment = draw_second_moment(jax.random.fold_in(arg_keys[16], 71), 0)
    head_params = draw_head_params(jax.random.fold_in(arg_keys[16], 71), 0)
    head_first = bell_draw(arg_keys[11], (N_TENSOR, HEADVEC), (0.055 * TOKENS ** 0.5), 20.0, ((0, 2),), jnp.float32)
    head_second = jnp.clip(jnp.exp(math.log(8.32) - 2.7725887 * jax.random.uniform(arg_keys[12], (N_TENSOR, HEADVEC), jnp.float32) ** block_scale(arg_keys[12], (N_TENSOR, HEADVEC), ((0, 2),), -0.2, 0.2)), 0.52, 8.32)
    shared_params = draw_shared_params(jax.random.fold_in(arg_keys[16], 71), 0)
    shared_first = bell_draw(arg_keys[14], (11, D), (0.055 * TOKENS ** 0.5), 20.0, (), jnp.float32)
    shared_second = jnp.clip(jnp.exp(jax.random.uniform(arg_keys[15], (11, D), jnp.float32, math.log(0.52), math.log(8.32))), 0.52, 8.32)
    return dict(latents=latents, context=context, cotangent=cotangent, positions=positions, step_ids=step_ids, owners=owners, time_table=time_table, master=master, first_moment=first_moment, second_moment=second_moment, head_params=head_params, head_first=head_first, head_second=head_second, shared_params=shared_params, shared_first=shared_first, shared_second=shared_second)


NORM_EPS = 1e-06
BETA_ONE = 0.9
BETA_TWO = 0.999
ADAM_EPS = 1e-08
TILE_RATE = 1.0
TILE_DECAY = 0.1
VECTOR_RATE = 0.5
GELU_COEF = 0.7978845608028654

@jax.custom_vjp
def low(v):
    return lax.optimization_barrier(v.astype(jnp.bfloat16)).astype(jnp.float32)

@jax.custom_vjp
def low_back(v):
    return v

def low_keep(v):
    return (low(v), None)

def low_pass(kept, grad):
    return (grad,)

def back_keep(v):
    return (v, None)

def back_low(kept, grad):
    return (low(grad),)
low.defvjp(low_keep, low_pass)
low_back.defvjp(back_keep, back_low)

def exact(form, left, right):
    return jnp.einsum(form, left, right, precision=lax.Precision.HIGHEST)

def layer_norm(inputs):
    centre = inputs - lax.optimization_barrier(jnp.mean(inputs, -1, keepdims=True))
    return centre * lax.rsqrt(lax.optimization_barrier(jnp.mean(centre * centre, -1, keepdims=True)) + NORM_EPS)

def head_rms(inputs, gain_vec):
    return inputs * lax.rsqrt(lax.optimization_barrier(jnp.mean(inputs * inputs, (-2, -1), keepdims=True)) + NORM_EPS) * gain_vec

def gelu_tanh(inputs):
    return 0.5 * inputs * (1.0 + jnp.tanh(GELU_COEF * (inputs + 0.044715 * inputs * inputs * inputs)))

def rotate(inputs):
    paired = inputs.reshape(inputs.shape[:-1] + (inputs.shape[-1] // 2, 2))
    return jnp.stack([-paired[..., 1], paired[..., 0]], -1).reshape(inputs.shape)

def rope(inputs, cos_tab, sin_tab):
    return inputs * cos_tab[..., None, :] + rotate(inputs) * sin_tab[..., None, :]

def rope_tables(token_places, head_size):
    sixths = head_size // 6
    frame_pairs = (head_size - 4 * sixths) // 2
    frame_freq = 10000.0 ** (-jnp.arange(frame_pairs, dtype=jnp.float32) / frame_pairs)
    side_freq = 10000.0 ** (-jnp.arange(sixths, dtype=jnp.float32) / sixths)
    spots = token_places.astype(jnp.float32)
    angles = jnp.concatenate([spots[0][..., None] * frame_freq, spots[1][..., None] * side_freq, spots[2][..., None] * side_freq], -1)
    angles = jnp.repeat(angles, 2, axis=-1)
    return (jnp.cos(angles), jnp.sin(angles))

def owner_layout(owners, slot_count, devices):
    indices = jnp.arange(owners.shape[0], dtype=jnp.int32)
    same_owner = (owners[:, None] == owners[None, :]) & (indices[None, :] < indices[:, None])
    slot_of = lax.optimization_barrier(jnp.sum(same_owner.astype(jnp.int32), axis=1))
    places = (owners * slot_count + slot_of).astype(jnp.int32)
    spots = jnp.arange(slot_count * devices, dtype=jnp.int32)
    holder = lax.optimization_barrier(jnp.sum(jnp.where(places[None, :] == spots[:, None], indices[None, :] + 1, 0), axis=1)) - 1
    return (places, holder.astype(jnp.int32))

def tile_scales(tile_count, heads_here, blocks_here):
    indices = jnp.arange(tile_count)
    scale_in = D ** (-0.5)
    scale_out = HEADS ** (-0.5)
    scale_down = FF ** (-0.5)
    scales = jnp.where(indices < 3 * heads_here, scale_in, jnp.where(indices < 4 * heads_here, scale_out, jnp.where(indices < 7 * heads_here, scale_in, jnp.where(indices < 8 * heads_here, scale_out, jnp.where(indices < 8 * heads_here + blocks_here, scale_in, scale_down)))))
    return scales.astype(jnp.float32)

def adam_step(weight, gradient, moment_one, moment_two, step_rate, decay_rate):
    first_new = BETA_ONE * moment_one + (1.0 - BETA_ONE) * gradient
    second_new = BETA_TWO * moment_two + (1.0 - BETA_TWO) * gradient * gradient
    first_hat = first_new / (1.0 - BETA_ONE ** STEPC)
    second_hat = second_new / (1.0 - BETA_TWO ** STEPC)
    weight_new = weight - step_rate * (first_hat / (jnp.sqrt(second_hat) + ADAM_EPS) + decay_rate * weight)
    return (weight_new, first_new, second_new)

def attention(query_low, key_low, value_low):
    scores = low_back(exact('bqhe,bkhe->bhqk', query_low, key_low) * HEAD ** (-0.5))
    row_max = lax.optimization_barrier(jnp.max(scores, -1, keepdims=True))
    expo = jnp.exp(scores - row_max)
    softmax_rows = low(expo / lax.optimization_barrier(jnp.sum(expo, -1, keepdims=True)))
    return low(low_back(exact('bhqk,bkhe->bqhe', softmax_rows, value_low)))

def block(params_in, inputs, ctx_group, temb_group, cos_tab, sin_tab, scales):
    used, head_vecs, shared = params_in
    tensors = used.shape[0]
    heads_here = HEADS // tensors
    blocks_here = FF // (HEAD * tensors)
    width_here = D // tensors
    scaled = low(used * scales[None, :, None, None])

    def heads_of(number):
        return scaled[:, number * heads_here:(number + 1) * heads_here].reshape(HEADS, D, HEAD)
    up_proj = scaled[:, 8 * heads_here:8 * heads_here + blocks_here].reshape(FF // HEAD, D, HEAD)
    down_proj = scaled[:, 8 * heads_here + blocks_here:].reshape(FF // HEAD, D, HEAD)

    def vec_of(number):
        return head_vecs[:, number * width_here:(number + 1) * width_here].reshape(HEADS, HEAD)
    up_bias = head_vecs[:, 10 * width_here:].reshape(FF // HEAD, HEAD)
    modul = shared[5:11][None] + temb_group
    normed = low(layer_norm(inputs) * (1.0 + modul[:, 1:2]) + modul[:, 0:1])
    query_pre = low_back(exact('bsd,hde->bshe', normed, heads_of(0)) + vec_of(0))
    key_pre = low_back(exact('bsd,hde->bshe', normed, heads_of(1)) + vec_of(1))
    value_low = low(low_back(exact('bsd,hde->bshe', normed, heads_of(2)) + vec_of(2)))
    query_low = low(rope(head_rms(query_pre, vec_of(3)), cos_tab, sin_tab))
    key_low = low(rope(head_rms(key_pre, vec_of(4)), cos_tab, sin_tab))
    heads_out = attention(query_low, key_low, value_low)
    branch_one = low_back(exact('bshe,hde->bsd', heads_out, heads_of(3)) + shared[0])
    after_one = inputs + modul[:, 2:3] * branch_one
    normed_two = low(layer_norm(after_one) * shared[3] + shared[4])
    cquery_pre = low_back(exact('bsd,hde->bshe', normed_two, heads_of(4)) + vec_of(5))
    ckey_pre = low_back(exact('bcd,hde->bche', ctx_group, heads_of(5)) + vec_of(6))
    cvalue_low = low(low_back(exact('bcd,hde->bche', ctx_group, heads_of(6)) + vec_of(7)))
    cquery_low = low(head_rms(cquery_pre, vec_of(8)))
    ckey_low = low(head_rms(ckey_pre, vec_of(9)))
    cross_out = attention(cquery_low, ckey_low, cvalue_low)
    branch_two = low_back(exact('bshe,hde->bsd', cross_out, heads_of(7)) + shared[1])
    after_two = after_one + branch_two
    normed_three = low(layer_norm(after_two) * (1.0 + modul[:, 4:5]) + modul[:, 3:4])
    hidden_pre = low_back(exact('bsd,fde->bsfe', normed_three, up_proj) + up_bias)
    hidden_low = low(gelu_tanh(hidden_pre))
    branch_three = low_back(exact('bsfe,fde->bsd', hidden_low, down_proj) + shared[2])
    return after_two + modul[:, 5:6] * branch_three

def reference(latents, context, cotangent, positions, step_ids, owners, time_table, master, first_moment, second_moment, head_params, head_first, head_second, shared_params, shared_first, shared_second):
    tensors = N_TENSOR
    devices = N_DP
    slot_count = master.shape[1] // devices
    tile_count = owners.shape[0]
    heads_here = HEADS // tensors
    blocks_here = FF // (HEAD * tensors)
    places, holder = owner_layout(owners, slot_count, devices)
    scales = tile_scales(tile_count, heads_here, blocks_here)
    used = master[:, places]
    params = (used, head_params, shared_params)
    per_group = 1
    while per_group * 2 <= max(1, 4096 // SEQ) and devices % (per_group * 2) == 0:
        per_group = per_group * 2
    count_groups = devices // per_group
    inputs_all = latents.astype(jnp.float32).reshape(count_groups, per_group, SEQ, D)
    ctx_all = context.astype(jnp.float32).reshape(count_groups, per_group, TEXT, D)
    cot_all = cotangent.astype(jnp.float32).reshape(count_groups, per_group, SEQ, D)
    temb_all = time_table[step_ids].reshape(count_groups, per_group, 6, D)
    place_all = positions.reshape(3, count_groups, per_group, SEQ).transpose(1, 0, 2, 3)

    def group_step(totals, items):
        inputs, ctx_group, temb_group, pos_group, cot_group = items
        cos_tab, sin_tab = rope_tables(pos_group, HEAD)

        def forward(params_in, inputs_in):
            return block(params_in, inputs_in, ctx_group, temb_group, cos_tab, sin_tab, scales)
        outputs, pullback = jax.vjp(forward, params, inputs)
        d_params, d_inputs = pullback(cot_group)
        return (jax.tree.map(jnp.add, totals, d_params), (outputs, d_inputs))
    zeros = jax.tree.map(jnp.zeros_like, params)
    totals, (outputs, d_inputs) = lax.scan(group_step, zeros, (inputs_all, ctx_all, temb_all, place_all, cot_all))
    block_out = outputs.reshape(TOKENS, D).astype(jnp.bfloat16)
    grad_latents = d_inputs.reshape(TOKENS, D)
    d_used, d_head, d_shared = totals
    filled = holder >= 0
    grad_slots = jnp.where(filled[None, :, None, None], d_used[:, jnp.maximum(holder, 0)], 0.0)
    new_w, new_m, new_v = adam_step(master, grad_slots, first_moment, second_moment, TILE_RATE, TILE_DECAY)
    mask = filled[None, :, None, None]
    new_master = jnp.where(mask, new_w, master)
    new_first = jnp.where(mask, new_m, first_moment)
    new_second = jnp.where(mask, new_v, second_moment)
    new_head, new_head_first, new_head_second = adam_step(head_params, d_head, head_first, head_second, VECTOR_RATE, 0.0)
    new_shared, new_shared_first, new_shared_second = adam_step(shared_params, d_shared, shared_first, shared_second, VECTOR_RATE, 0.0)
    return (block_out, grad_latents, new_master, new_first, new_second, new_head, new_head_first, new_head_second, new_shared, new_shared_first, new_shared_second)
```

```python
import functools

import jax
import jax.numpy as jnp
from jax import lax
from jax.experimental import pallas as pl
from jax.experimental.pallas import tpu as pltpu
from jax.sharding import PartitionSpec as P

D = 1536
HEADS = 12
HEAD = 128
FF = 8960
TSTEPS = 16
STEPC = 10


NORM_EPS = 1e-06
BETA_ONE = 0.9
BETA_TWO = 0.999
ADAM_EPS = 1e-08
TILE_RATE = 1.0
TILE_DECAY = 0.1
VECTOR_RATE = 0.5
GELU_COEF = 0.7978845608028654


def product(form, left, right):
    return jnp.einsum(form, left, right, preferred_element_type=jnp.float32)


def layer_norm(inputs):
    centre = inputs - jnp.mean(inputs, -1, keepdims=True)
    return centre * lax.rsqrt(jnp.mean(centre * centre, -1, keepdims=True) + NORM_EPS)


def gelu_tanh(inputs):
    return (
        0.5 * inputs * (1.0 + jnp.tanh(GELU_COEF * (inputs + 0.044715 * inputs * inputs * inputs)))
    )


def rotate(inputs):
    paired = inputs.reshape(inputs.shape[:-1] + (inputs.shape[-1] // 2, 2))
    return jnp.stack([-paired[..., 1], paired[..., 0]], -1).reshape(inputs.shape)


def rope(inputs, cos_tab, sin_tab):
    return inputs * cos_tab[..., None, :] + rotate(inputs) * sin_tab[..., None, :]


def rope_tables(token_places, head_size):
    sixths = head_size // 6
    frame_pairs = (head_size - 4 * sixths) // 2
    frame_freq = 10000.0 ** (-jnp.arange(frame_pairs, dtype=jnp.float32) / frame_pairs)
    side_freq = 10000.0 ** (-jnp.arange(sixths, dtype=jnp.float32) / sixths)
    spots = token_places.astype(jnp.float32)
    angles = jnp.concatenate(
        [
            spots[0][..., None] * frame_freq,
            spots[1][..., None] * side_freq,
            spots[2][..., None] * side_freq,
        ],
        -1,
    )
    angles = jnp.repeat(angles, 2, axis=-1)
    return (jnp.cos(angles), jnp.sin(angles))


def owner_layout(owners, slot_count, devices):
    indices = jnp.arange(owners.shape[0], dtype=jnp.int32)
    same_owner = (owners[:, None] == owners[None, :]) & (indices[None, :] < indices[:, None])
    slot_of = jnp.sum(same_owner.astype(jnp.int32), axis=1)
    places = owners * slot_count + slot_of
    spots = jnp.arange(slot_count * devices, dtype=jnp.int32)
    holder = (
        jnp.sum(jnp.where(places[None, :] == spots[:, None], indices[None, :] + 1, 0), axis=1) - 1
    )
    return (places, holder)


def tile_scales(tile_count, heads_here, blocks_here):
    indices = jnp.arange(tile_count)
    scale_in = D ** (-0.5)
    scale_out = HEADS ** (-0.5)
    scale_down = FF ** (-0.5)
    scales = jnp.where(
        indices < 3 * heads_here,
        scale_in,
        jnp.where(
            indices < 4 * heads_here,
            scale_out,
            jnp.where(
                indices < 7 * heads_here,
                scale_in,
                jnp.where(
                    indices < 8 * heads_here,
                    scale_out,
                    jnp.where(indices < 8 * heads_here + blocks_here, scale_in, scale_down),
                ),
            ),
        ),
    )
    return scales.astype(jnp.float32)


def tile_views(weights, heads_here, blocks_here):
    pieces = [weights[number * heads_here : (number + 1) * heads_here] for number in range(8)]
    start_up = 8 * heads_here
    pieces.append(weights[start_up : start_up + blocks_here])
    pieces.append(weights[start_up + blocks_here :])
    return pieces


def adam_step(weight, gradient, moment_one, moment_two, step_rate, decay_rate):
    first_new = BETA_ONE * moment_one + (1.0 - BETA_ONE) * gradient
    second_new = BETA_TWO * moment_two + (1.0 - BETA_TWO) * gradient * gradient
    first_hat = first_new / (1.0 - BETA_ONE**STEPC)
    second_hat = second_new / (1.0 - BETA_TWO**STEPC)
    weight_new = weight - step_rate * (
        first_hat / (jnp.sqrt(second_hat) + ADAM_EPS) + decay_rate * weight
    )
    return (weight_new, first_new, second_new)


def attend(query_low, key_low, value_low, scaling):
    scores = product("qhe,khe->hqk", query_low, key_low) * scaling
    row_max = jnp.max(scores, -1, keepdims=True)
    log_total = row_max + jnp.log(jnp.sum(jnp.exp(scores - row_max), -1, keepdims=True))
    softmax_low = jnp.exp(scores - log_total).astype(jnp.bfloat16)
    heads_out = product("hqk,khe->qhe", softmax_low, value_low).astype(jnp.bfloat16)
    return (log_total, heads_out)


def attend_back(query_low, key_low, value_low, log_total, d_heads, scaling):
    scores = product("qhe,khe->hqk", query_low, key_low) * scaling
    softmax_rows = jnp.exp(scores - log_total)
    d_softmax = product("qhe,khe->hqk", d_heads, value_low)
    d_scores = (
        softmax_rows * (d_softmax - jnp.sum(softmax_rows * d_softmax, -1, keepdims=True))
    ).astype(jnp.bfloat16)
    d_query = product("hqk,khe->qhe", d_scores, key_low) * scaling
    d_key = product("hqk,qhe->khe", d_scores, query_low) * scaling
    d_value = product("hqk,qhe->khe", softmax_rows.astype(jnp.bfloat16), d_heads)
    return (d_query, d_key, d_value)


def norm_stats(query_pre, key_pre):
    totals = pair_sums(
        jnp.sum(query_pre * query_pre, (1, 2)), jnp.sum(key_pre * key_pre, (1, 2))
    )
    return tuple((lax.rsqrt(total / D + NORM_EPS)[:, None, None] for total in totals))


def norm_back(query_pre, query_inv, query_gain, query_in, key_pre, key_inv, key_gain, key_in):
    totals = pair_sums(
        jnp.sum(query_pre * query_gain * query_in, (1, 2)),
        jnp.sum(key_pre * key_gain * key_in, (1, 2)),
    )
    results = []
    for pre_vals, inverse, gain_vec, incoming, total in (
        (query_pre, query_inv, query_gain, query_in, totals[0]),
        (key_pre, key_inv, key_gain, key_in, totals[1]),
    ):
        d_pre = inverse * (gain_vec * incoming) - pre_vals * inverse * inverse * inverse * (
            total[:, None, None] / D
        )
        d_gain = jnp.sum(incoming * pre_vals * inverse, 0)
        results.append(d_pre)
        results.append(d_gain)
    return results


MESH = pl.DeviceIdType.MESH
ANY = pl.BlockSpec(memory_space=pl.ANY)
MIB = 1 << 20


def chip_pairs():
    return lax.axis_size("dp") == 16 and lax.axis_size("tensor") == 2


def pair_rank():
    if chip_pairs():
        return (lax.axis_index("dp") // 4) % 2
    return lax.axis_index("tensor")


def pair_swap(value):
    if chip_pairs():
        return lax.ppermute(value, "dp", [(i, i ^ 4) for i in range(16)])
    return lax.ppermute(value, "tensor", [(0, 1), (1, 0)])


def pair_sums(*values):
    stacked = jnp.concatenate([v.reshape(-1) for v in values])
    total = stacked + pair_swap(stacked)
    out, at = [], 0
    for v in values:
        out.append(total[at : at + v.size].reshape(v.shape))
        at += v.size
    return tuple(out)


def home_swap(*values):
    if not chip_pairs():
        return values
    chip, core = lax.axis_index("dp"), lax.axis_index("tensor")
    away = (chip // 4) % 2 != core
    order = [
        (d * 2 + c, (d ^ 4) * 2 + 1 - c) for d in range(16) for c in range(2) if (d // 4) % 2 != c
    ]
    return tuple(
        jnp.where(away, lax.ppermute(v, ("dp", "tensor"), order), v) for v in values
    )


def place_of():
    chip, core = lax.axis_index("dp"), lax.axis_index("tensor")
    z, y, x = chip // 4, (chip // 2) % 2, chip % 2
    return chip, core, z, y, x


def column_of(z, y, x, k):
    high, low_bit = z // 2, z % 2
    if k & 2:
        high = 1 - high
    if k & 1:
        low_bit = 1 - low_bit
    return (2 * high + low_bit) * 4 + 2 * y + x


def greet(chip, core, z, y, x):
    barrier = pltpu.get_barrier_semaphore()
    friends = []
    for k in range(4):
        for flip in (0, 1):
            if k or flip:
                friends.append((column_of(z, y, x, k), core if flip == 0 else 1 - core))
    friends.append((column_of(z, y, 1 - x, 0), core))
    friends.append((column_of(z, 1 - y, x, 0), core))
    for friend in friends:
        pl.semaphore_signal(barrier, inc=1, device_id=friend, device_id_type=MESH)
    pl.semaphore_wait(barrier, len(friends))


def gather_kernel(own, out, near_s, local_s, col_r, x_s, x_r, y_s, y_r, ra_s, ra_r, rb_s, rb_r, sib_s, sib_r):
    chip, core, z, y, x = place_of()
    rank = z % 2
    half = own.shape[1] // 2
    part = half // 2
    at_x = column_of(z, y, 1 - x, 0)
    at_y = column_of(z, 1 - y, x, 0)
    greet(chip, core, z, y, x)

    def rows(ref, unit, first, count):
        return ref.at[unit, :, pl.ds(pl.multiple_of(first, 16), count), :]

    def remote(unit, first, count, send, recv, device):
        piece = rows(out, unit, first, count)
        return pltpu.make_async_remote_copy(
            src_ref=piece, dst_ref=piece, send_sem=send, recv_sem=recv,
            device_id=device, device_id_type=MESH,
        )

    started = []
    for j in range(2):
        zh = z // 2 if j == 0 else 1 - z // 2
        target = (2 * zh + core) * 4 + 2 * y + x
        for h in range(2):
            src = own.at[:, pl.ds(h * half, half), :]
            dst = out.at[chip, :, pl.ds(h * half, half), :]
            go = pltpu.make_async_remote_copy(
                src_ref=src, dst_ref=dst, send_sem=near_s.at[2 * j + h], recv_sem=col_r.at[z],
                device_id=(target, h), device_id_type=MESH,
            )
            if j == 0:
                here = pltpu.make_async_copy(src, dst, col_r.at[z])
                stays = jnp.logical_and(rank == core, core == h)

                @pl.when(stays)
                def _():
                    here.start()

                @pl.when(jnp.logical_not(stays))
                def _():
                    go.start()

                started.append((go, stays))
            else:
                go.start()
                started.append((go, None))

    def column_in(k):
        unit = column_of(z, y, x, k)
        source_z = unit // 4
        piece = rows(out, unit, core * half, half)
        pltpu.make_async_copy(piece, piece, col_r.at[source_z]).wait()
        to_x = remote(unit, core * half, half, x_s.at[k], x_r.at[k], (at_x, core))
        to_y = remote(unit, core * half, half, y_s.at[k], y_r.at[k], (at_y, core))
        to_sib = remote(unit, core * half, half, sib_s.at[k], sib_r.at[k], (chip, 1 - core))
        to_x.start()
        to_y.start()
        to_sib.start()
        return [to_x, to_y, to_sib]

    def side_in(k):
        ux = column_of(z, y, 1 - x, k)
        uy = column_of(z, 1 - y, x, k)
        remote(ux, core * half, half, x_s.at[k], x_r.at[k], (at_x, core)).wait_recv()
        on_y = remote(ux, core * half + part, part, rb_s.at[k], rb_r.at[k], (at_y, core))
        on_y.start()
        sib_x = remote(ux, core * half, half, sib_s.at[4 + k], sib_r.at[4 + k], (chip, 1 - core))
        sib_x.start()
        remote(uy, core * half, half, y_s.at[k], y_r.at[k], (at_y, core)).wait_recv()
        on_x = remote(uy, core * half, part, ra_s.at[k], ra_r.at[k], (at_x, core))
        on_x.start()
        sib_y = remote(uy, core * half, half, sib_s.at[8 + k], sib_r.at[8 + k], (chip, 1 - core))
        sib_y.start()
        return [on_y, sib_x, on_x, sib_y]

    def corner_in(k):
        unit = column_of(z, 1 - y, 1 - x, k)
        remote(unit, core * half, part, ra_s.at[k], ra_r.at[k], (at_x, core)).wait_recv()
        sib_a = remote(unit, core * half, part, sib_s.at[12 + k], sib_r.at[12 + k], (chip, 1 - core))
        sib_a.start()
        remote(unit, core * half + part, part, rb_s.at[k], rb_r.at[k], (at_y, core)).wait_recv()
        sib_b = remote(
            unit, core * half + part, part, sib_s.at[16 + k], sib_r.at[16 + k], (chip, 1 - core)
        )
        sib_b.start()
        return [sib_a, sib_b]

    sent = []
    for step in range(6):
        if step < 4:
            sent += column_in(step)
        if 1 <= step < 5:
            sent += side_in(step - 1)
        if step >= 2:
            sent += corner_in(step - 2)
    for copy in sent:
        copy.wait_send()
    for go, stays in started:
        if stays is None:
            go.wait_send()
        else:

            @pl.when(jnp.logical_not(stays))
            def _():
                go.wait_send()

    other = (1 - core) * half
    for k in range(4):
        for at, (yy, xx) in ((0, (y, x)), (4, (y, 1 - x)), (8, (1 - y, x))):
            remote(
                column_of(z, yy, xx, k), other, half, sib_s.at[at + k], sib_r.at[at + k],
                (chip, 1 - core),
            ).wait_recv()
        corner = column_of(z, 1 - y, 1 - x, k)
        remote(
            corner, other, part, sib_s.at[12 + k], sib_r.at[12 + k], (chip, 1 - core)
        ).wait_recv()
        remote(
            corner, other + part, part, sib_s.at[16 + k], sib_r.at[16 + k], (chip, 1 - core)
        ).wait_recv()


def gather_slots(scaled):
    if not chip_pairs():
        return lax.all_gather(scaled, "dp", axis=0, tiled=True)
    dma = pltpu.SemaphoreType.DMA
    counts = (4, 1, 4, 4, 4, 4, 4, 4, 4, 4, 4, 20, 20)
    everyone = pl.pallas_call(
        gather_kernel,
        out_shape=jax.ShapeDtypeStruct((16,) + scaled.shape, scaled.dtype),
        in_specs=[ANY],
        out_specs=ANY,
        scratch_shapes=[dma((n,)) for n in counts],
        compiler_params=pltpu.CompilerParams(
            collective_id=0, has_side_effects=True, vmem_limit_bytes=4 * MIB
        ),
    )(scaled)
    return everyone.reshape((-1,) + scaled.shape[1:])


def add_rows(*refs):
    *terms, total = refs
    slots, count, width = total.shape
    spec = pl.BlockSpec((1, count, width), lambda i: (i, 0, 0))

    def add(*blocks):
        *parts, result = blocks
        acc = parts[0][...].astype(jnp.float32)
        for one in parts[1:]:
            acc = acc + one[...].astype(jnp.float32)
        result[...] = acc.astype(result.dtype)

    pltpu.emit_pipeline(
        add, grid=(slots,), in_specs=[spec] * len(terms), out_specs=[spec]
    )(*terms, total)


def reduce_kernel(
    grads, final, from_sib, chip_sum, from_x, from_y, corner_a, corner_b,
    sib_s, sib_r, x_s, x_r, y_s, y_r, ca_s, ca_r, cb_s, cb_r, f_s, f_r,
):
    chip, core, z, y, x = place_of()
    rank = z % 2
    half = grads.shape[2] // 2
    part = half // 2
    at_x = column_of(z, y, 1 - x, 0)
    at_y = column_of(z, 1 - y, x, 0)
    greet(chip, core, z, y, x)

    def remote(src, dst, send, recv, device):
        return pltpu.make_async_remote_copy(
            src_ref=src, dst_ref=dst, send_sem=send, recv_sem=recv,
            device_id=device, device_id_type=MESH,
        )

    columns = ((1 - y, 1 - x), (y, 1 - x), (1 - y, x), (y, x))
    order = (3, 2, 1, 0)

    def sib_copy(q, k):
        unit = column_of(z, *columns[q], k)
        src = grads.at[unit, :, pl.ds(pl.multiple_of((1 - core) * half, 16), half), :]
        i = 4 * q + k
        return remote(src, from_sib.at[i], sib_s.at[i], sib_r.at[i], (chip, 1 - core))

    sent = []

    def start_sib(q, k):
        copy = sib_copy(q, k)
        copy.start()
        sent.append(copy)

    for k in order:
        for q in range(4):
            start_sib(q, k)

    def mine(q, k):
        unit = column_of(z, *columns[q], k)
        return grads.at[unit, :, pl.ds(pl.multiple_of(core * half, 16), half), :]

    def sub(ref, first):
        return ref.at[:, pl.ds(first, part), :]

    def own_sub(q, k, first):
        unit = column_of(z, *columns[q], k)
        return grads.at[
            unit, :, pl.ds(pl.multiple_of(core * half + first, 16), part), :
        ]

    def corner(k):
        i = k
        sib_copy(0, k).wait_recv()
        add_rows(mine(0, k), from_sib.at[i], chip_sum.at[i])
        a = remote(sub(chip_sum.at[i], 0), corner_a.at[k], ca_s.at[k], ca_r.at[k], (at_x, core))
        b = remote(sub(chip_sum.at[i], part), corner_b.at[k], cb_s.at[k], cb_r.at[k], (at_y, core))
        a.start()
        b.start()
        sent.extend([a, b])

    def sides(k):
        ix, iy = 4 + k, 8 + k
        sib_copy(1, k).wait_recv()
        sib_copy(2, k).wait_recv()
        add_rows(own_sub(1, k, 0), sub(from_sib.at[ix], 0), sub(chip_sum.at[ix], 0))
        add_rows(own_sub(2, k, part), sub(from_sib.at[iy], part), sub(chip_sum.at[iy], part))
        remote(
            sub(chip_sum.at[k], part), corner_b.at[k], cb_s.at[k], cb_r.at[k], (at_y, core)
        ).wait_recv()
        add_rows(
            own_sub(1, k, part), sub(from_sib.at[ix], part), corner_b.at[k],
            sub(chip_sum.at[ix], part),
        )
        to_x = remote(chip_sum.at[ix], from_x.at[k], x_s.at[k], x_r.at[k], (at_x, core))
        to_x.start()
        remote(
            sub(chip_sum.at[k], 0), corner_a.at[k], ca_s.at[k], ca_r.at[k], (at_x, core)
        ).wait_recv()
        add_rows(
            own_sub(2, k, 0), sub(from_sib.at[iy], 0), corner_a.at[k], sub(chip_sum.at[iy], 0)
        )
        to_y = remote(chip_sum.at[iy], from_y.at[k], y_s.at[k], y_r.at[k], (at_y, core))
        to_y.start()
        sent.extend([to_x, to_y])

    finals = []

    def centre(k):
        i = 12 + k
        sib_copy(3, k).wait_recv()
        remote(chip_sum.at[4 + k], from_x.at[k], x_s.at[k], x_r.at[k], (at_x, core)).wait_recv()
        remote(chip_sum.at[8 + k], from_y.at[k], y_s.at[k], y_r.at[k], (at_y, core)).wait_recv()
        add_rows(mine(3, k), from_sib.at[i], from_x.at[k], from_y.at[k], chip_sum.at[i])
        target = column_of(z, y, x, k)
        dst = final.at[z // 2, :, pl.ds(pl.multiple_of(core * half, 16), half), :]
        recv = f_r.at[2 * (z // 2) + core]
        go = remote(chip_sum.at[i], dst, f_s.at[k], recv, (target, rank))
        if k == 0:
            stays = rank == core
            here = pltpu.make_async_copy(chip_sum.at[i], dst, recv)

            @pl.when(stays)
            def _():
                here.start()

            @pl.when(jnp.logical_not(stays))
            def _():
                go.start()

            finals.append((go, stays))
        else:
            go.start()
            sent.append(go)

    for step in range(6):
        if step < 4:
            corner(order[step])
        if 1 <= step < 5:
            sides(order[step - 1])
        if step >= 2:
            centre(order[step - 2])
    for copy in sent:
        copy.wait_send()
    for go, stays in finals:

        @pl.when(jnp.logical_not(stays))
        def _():
            go.wait_send()

    for plane in range(2):
        for h in range(2):
            piece = final.at[plane, :, pl.ds(h * half, half), :]
            pltpu.make_async_copy(piece, piece, f_r.at[2 * plane + h]).wait()


def reduce_slots(grads, slot_count):
    if not chip_pairs():
        total = lax.psum_scatter(grads, "dp", scatter_dimension=0, tiled=True)
        return total, None
    width = grads.shape[1:]
    half = width[0] // 2
    dma = pltpu.SemaphoreType.DMA
    units = grads.reshape((16, slot_count) + width)

    def room(count, rows):
        return jax.ShapeDtypeStruct((count, slot_count, rows, width[1]), grads.dtype)

    counts = (16, 16) + (4,) * 12
    outs = pl.pallas_call(
        reduce_kernel,
        out_shape=[
            jax.ShapeDtypeStruct((2, slot_count) + width, grads.dtype),
            room(16, half), room(16, half), room(4, half), room(4, half),
            room(4, half // 2), room(4, half // 2),
        ],
        in_specs=[ANY],
        out_specs=[ANY] * 7,
        scratch_shapes=[dma((n,)) for n in counts[:12]],
        compiler_params=pltpu.CompilerParams(
            collective_id=1, has_side_effects=True, vmem_limit_bytes=16 * MIB
        ),
    )(units)
    return outs[0][0], outs[0][1]


def pick_blocks(everyone, places):
    shape = everyone.shape[1:]
    count = places.shape[0]

    def copy(_, src, dst):
        dst[...] = src[...]

    return pl.pallas_call(
        copy,
        grid_spec=pltpu.PrefetchScalarGridSpec(
            num_scalar_prefetch=1,
            grid=(count,),
            in_specs=[pl.BlockSpec((1,) + shape, lambda m, where: (where[m], 0, 0))],
            out_specs=pl.BlockSpec((1,) + shape, lambda m, where: (m, 0, 0)),
        ),
        out_shape=jax.ShapeDtypeStruct((count,) + shape, everyone.dtype),
    )(places, everyone)


def kind_of_blocks(tile_count, heads_here, blocks_here):
    number = jnp.arange(tile_count)
    kind = number // heads_here
    table = jnp.array([0, 0, 0, 1, 2, 3, 3, 4], jnp.int32)
    late = jnp.where(number < 8 * heads_here + blocks_here, 5, 6)
    return jnp.where(number < 8 * heads_here, table[jnp.minimum(kind, 7)], late).astype(jnp.int32)


def slot_grads(holder, kinds, rows, columns):
    depth = max(r.shape[0] for r in rows)

    def deep(value, axis):
        room = [(0, 0)] * value.ndim
        room[axis] = (0, depth - value.shape[axis])
        return jnp.pad(value, room)

    left = jnp.stack([deep(r, 0) for r in rows])
    right = jnp.concatenate([deep(c, 0) for c in columns], 1).transpose(1, 0, 2)
    slots = holder.shape[0]
    used = (holder >= 0).astype(jnp.int32)
    block = jnp.maximum(holder, 0)
    kind = kinds[block]
    width = rows[0].shape[1]
    lanes = right.shape[2]

    def multiply(kind_ref, block_ref, used_ref, left_ref, right_ref, out_ref):
        slot = pl.program_id(0)

        @pl.when(used_ref[slot] == 1)
        def _():
            out_ref[0] = lax.dot_general(
                left_ref[kind_ref[slot]],
                right_ref[0],
                (((0,), (0,)), ((), ())),
                preferred_element_type=jnp.float32,
            ).astype(out_ref.dtype)

        @pl.when(used_ref[slot] == 0)
        def _():
            out_ref[...] = jnp.zeros_like(out_ref)

    return pl.pallas_call(
        multiply,
        grid_spec=pltpu.PrefetchScalarGridSpec(
            num_scalar_prefetch=3,
            grid=(slots,),
            in_specs=[
                pl.BlockSpec(left.shape, lambda s, kd, b, u: (0, 0, 0)),
                pl.BlockSpec((1, depth, lanes), lambda s, kd, b, u: (b[s], 0, 0)),
            ],
            out_specs=pl.BlockSpec((1, width, lanes), lambda s, kd, b, u: (s, 0, 0)),
        ),
        out_shape=jax.ShapeDtypeStruct((slots, width, lanes), jnp.bfloat16),
        compiler_params=pltpu.CompilerParams(vmem_limit_bytes=48 * MIB),
    )(kind, block, used, left, right)


def adam_slots(first_part, second_part, master, moment_one, moment_two, slot_scale, filled):
    slot_count, width, lanes = master.shape[1:]
    parts = [first_part] if second_part is None else [first_part, second_part]
    count = len(parts)
    tall = width // 2

    def step(scale_ref, fill_ref, *refs):
        grads = refs[:count]
        weight, one, two, new_weight, new_one, new_two = refs[count:]
        slot = pl.program_id(0)

        @pl.when(fill_ref[slot] == 1)
        def _():
            total = grads[0][0].astype(jnp.float32)
            for more in grads[1:]:
                total = total + more[0].astype(jnp.float32)
            results = adam_step(
                weight[0, 0], total * scale_ref[slot], one[0, 0], two[0, 0], TILE_RATE, TILE_DECAY
            )
            for ref, value in zip((new_weight, new_one, new_two), results):
                ref[0, 0] = value

        @pl.when(fill_ref[slot] == 0)
        def _():
            new_weight[...] = weight[...]
            new_one[...] = one[...]
            new_two[...] = two[...]

    flat = pl.BlockSpec((1, tall, lanes), lambda s, i: (s, i, 0))
    deep = pl.BlockSpec((1, 1, tall, lanes), lambda s, i: (0, s, i, 0))
    scalars = pl.BlockSpec(memory_space=pltpu.SMEM)
    return pl.pallas_call(
        step,
        grid=(slot_count, 2),
        in_specs=[scalars, scalars] + [flat] * count + [deep] * 3,
        out_specs=[deep] * 3,
        out_shape=[jax.ShapeDtypeStruct(master.shape, jnp.float32)] * 3,
    )(slot_scale, filled.astype(jnp.int32), *parts, master, moment_one, moment_two)


def body(
    latents,
    context,
    cotangent,
    positions,
    step_ids,
    owners,
    time_table,
    master,
    first_moment,
    second_moment,
    head_params,
    head_first,
    head_second,
    shared_params,
    shared_first,
    shared_second,
):
    tensors = lax.axis_size("tensor")
    devices = lax.axis_size("dp")
    slot_count = master.shape[1]
    tile_count = owners.shape[0]
    heads_here = HEADS // tensors
    blocks_here = FF // (HEAD * tensors)
    width_here = D // tensors
    scaling = HEAD ** (-0.5)
    places, holder = owner_layout(owners, slot_count, devices)
    scales = tile_scales(tile_count, heads_here, blocks_here)
    my_slots = lax.dynamic_slice_in_dim(holder, lax.axis_index("dp") * slot_count, slot_count)
    rank = pair_rank()
    latents, context, cotangent, positions, step_ids, head_here = home_swap(
        latents, context, cotangent, positions, step_ids, head_params
    )
    filled = my_slots >= 0
    slot_scale = jnp.where(filled, scales[jnp.maximum(my_slots, 0)], 0.0)
    scaled = (master[0] * slot_scale[:, None, None]).astype(jnp.bfloat16)
    everyone = gather_slots(scaled)
    pieces = tile_views(pick_blocks(everyone, places), heads_here, blocks_here)
    vectors = head_here[0]

    def head_vector(number):
        return vectors[number * width_here : (number + 1) * width_here].reshape(heads_here, HEAD)

    bias_query, bias_key, bias_value, gain_query, gain_key = [
        head_vector(number) for number in range(5)
    ]
    cross_bias_q, cross_bias_k, cross_bias_v, cross_gain_q, cross_gain_k = [
        head_vector(number) for number in range(5, 10)
    ]
    up_bias = vectors[10 * width_here :].reshape(blocks_here, HEAD)
    chosen = (step_ids[0] == jnp.arange(TSTEPS)).astype(jnp.float32)
    modulation = shared_params[5:11] + jnp.einsum(
        "s,skd->kd", chosen, time_table, precision=lax.Precision.HIGHEST
    )
    shift_attn, scale_attn, gate_attn = (modulation[0], modulation[1], modulation[2])
    shift_ffn, scale_ffn, gate_ffn = (modulation[3], modulation[4], modulation[5])
    cos_tab, sin_tab = rope_tables(positions, HEAD)

    def mod_norm(inputs, shift_vec, scale_vec):
        return layer_norm(inputs) * (1.0 + scale_vec) + shift_vec

    def affine_norm(inputs, gain_vec, bias_vec):
        return layer_norm(inputs) * gain_vec + bias_vec

    def spread_rows(local_rows):
        other = pair_swap(local_rows)
        return jnp.where(
            rank == 0,
            jnp.concatenate([local_rows, other], 0),
            jnp.concatenate([other, local_rows], 0),
        )

    def merge_rows(summand):
        half = summand.shape[0] // 2
        mine = lax.dynamic_slice_in_dim(summand, rank * half, half, 0)
        theirs = lax.dynamic_slice_in_dim(summand, (1 - rank) * half, half, 0)
        return mine + pair_swap(theirs.astype(jnp.bfloat16)).astype(jnp.float32)

    spread_grads, merge_grads = spread_rows, merge_rows

    residual = latents.astype(jnp.float32)
    low_one = mod_norm(residual, shift_attn, scale_attn).astype(jnp.bfloat16)
    rows_one = spread_rows(low_one)
    query_pre = product("td,hde->the", rows_one, pieces[0]) + bias_query
    key_pre = product("td,hde->the", rows_one, pieces[1]) + bias_key
    value_low = (product("td,hde->the", rows_one, pieces[2]) + bias_value).astype(jnp.bfloat16)
    query_inv, key_inv = norm_stats(query_pre, key_pre)
    query_low = rope(query_pre * query_inv * gain_query, cos_tab, sin_tab).astype(jnp.bfloat16)
    key_low = rope(key_pre * key_inv * gain_key, cos_tab, sin_tab).astype(jnp.bfloat16)
    log_total, heads_out = attend(query_low, key_low, value_low, scaling)
    saved_one = (
        query_pre,
        key_pre,
        query_inv,
        key_inv,
        query_low,
        key_low,
        value_low,
        log_total,
        heads_out,
    )
    branch_one = merge_rows(product("the,hde->td", saved_one[-1], pieces[3])) + shared_params[0]
    after_one = residual + gate_attn * branch_one
    low_two = affine_norm(after_one, shared_params[3], shared_params[4]).astype(jnp.bfloat16)
    rows_two = spread_rows(low_two)
    query_pre = product("td,hde->the", rows_two, pieces[4]) + cross_bias_q
    key_pre = product("cd,hde->che", context, pieces[5]) + cross_bias_k
    value_low = (product("cd,hde->che", context, pieces[6]) + cross_bias_v).astype(jnp.bfloat16)
    query_inv, key_inv = norm_stats(query_pre, key_pre)
    query_low = (query_pre * query_inv * cross_gain_q).astype(jnp.bfloat16)
    key_low = (key_pre * key_inv * cross_gain_k).astype(jnp.bfloat16)
    log_total, heads_out = attend(query_low, key_low, value_low, scaling)
    saved_two = (
        query_pre,
        key_pre,
        query_inv,
        key_inv,
        query_low,
        key_low,
        value_low,
        log_total,
        heads_out,
    )
    branch_two = merge_rows(product("the,hde->td", saved_two[-1], pieces[7])) + shared_params[1]
    after_two = after_one + branch_two
    low_three = mod_norm(after_two, shift_ffn, scale_ffn).astype(jnp.bfloat16)
    rows_three = spread_rows(low_three)
    hidden_pre = product("td,fde->tfe", rows_three, pieces[8]) + up_bias
    saved_three = (hidden_pre, gelu_tanh(hidden_pre).astype(jnp.bfloat16))
    branch_three = merge_rows(product("tfe,fde->td", saved_three[1], pieces[9])) + shared_params[2]
    result = after_two + gate_ffn * branch_three
    output = result.astype(jnp.bfloat16)
    grad_res = cotangent.astype(jnp.float32)
    d_gate_ffn = jnp.sum(grad_res * branch_three, 0)
    grad_branch = (gate_ffn * grad_res).astype(jnp.bfloat16)
    d_down_bias = jnp.sum(grad_branch.astype(jnp.float32), 0)
    rows_grad = spread_grads(grad_branch)
    hidden_pre, hidden_low = saved_three
    rows_grad_three = rows_grad
    d_hidden = product("td,fde->tfe", rows_grad, pieces[9])
    d_hidden = jax.vjp(gelu_tanh, hidden_pre)[1](d_hidden)[0]
    d_hidden_low = d_hidden.astype(jnp.bfloat16)
    d_up_bias = jnp.sum(d_hidden_low.astype(jnp.float32), 0)
    grad_norm = merge_grads(product("tfe,fde->td", d_hidden_low, pieces[8]))
    d_inputs, d_shift_ffn, d_scale_ffn = jax.vjp(mod_norm, after_two, shift_ffn, scale_ffn)[1](
        grad_norm
    )
    grad_res = grad_res + d_inputs
    grad_branch = grad_res.astype(jnp.bfloat16)
    d_cross_bias_out = jnp.sum(grad_branch.astype(jnp.float32), 0)
    rows_grad = spread_grads(grad_branch)
    query_pre, key_pre, query_inv, key_inv, query_low, key_low, value_low, log_total, heads_out = (
        saved_two
    )
    rows_grad_two, cross_heads_out = rows_grad, heads_out
    d_heads = product("td,hde->the", rows_grad, pieces[7]).astype(jnp.bfloat16)
    d_query, d_key, d_value = attend_back(
        query_low, key_low, value_low, log_total, d_heads, scaling
    )
    d_query, d_cross_gain_q, d_key, d_cross_gain_k = norm_back(
        query_pre, query_inv, cross_gain_q, d_query, key_pre, key_inv, cross_gain_k, d_key
    )
    query_grad = d_query.astype(jnp.bfloat16)
    key_grad = d_key.astype(jnp.bfloat16)
    value_grad = d_value.astype(jnp.bfloat16)
    d_cross_bias_q = jnp.sum(query_grad.astype(jnp.float32), 0)
    d_cross_bias_k = jnp.sum(key_grad.astype(jnp.float32), 0)
    d_cross_bias_v = jnp.sum(value_grad.astype(jnp.float32), 0)
    cross_query_grad, cross_key_grad, cross_value_grad = query_grad, key_grad, value_grad
    grad_norm = merge_grads(product("the,hde->td", query_grad, pieces[4]))
    d_inputs, d_norm_gain, d_norm_bias = jax.vjp(
        affine_norm, after_one, shared_params[3], shared_params[4]
    )[1](grad_norm)
    grad_res = grad_res + d_inputs
    d_gate_attn = jnp.sum(grad_res * branch_one, 0)
    grad_branch = (gate_attn * grad_res).astype(jnp.bfloat16)
    d_self_bias_out = jnp.sum(grad_branch.astype(jnp.float32), 0)
    rows_grad = spread_grads(grad_branch)
    query_pre, key_pre, query_inv, key_inv, query_low, key_low, value_low, log_total, heads_out = (
        saved_one
    )
    d_heads = product("td,hde->the", rows_grad, pieces[3]).astype(jnp.bfloat16)
    d_query, d_key, d_value = attend_back(
        query_low, key_low, value_low, log_total, d_heads, scaling
    )
    turned_query = rope(d_query, cos_tab, -sin_tab)
    turned_key = rope(d_key, cos_tab, -sin_tab)
    d_query, d_gain_query, d_key, d_gain_key = norm_back(
        query_pre, query_inv, gain_query, turned_query, key_pre, key_inv, gain_key, turned_key
    )
    query_grad = d_query.astype(jnp.bfloat16)
    key_grad = d_key.astype(jnp.bfloat16)
    value_grad = d_value.astype(jnp.bfloat16)
    d_bias_query = jnp.sum(query_grad.astype(jnp.float32), 0)
    d_bias_key = jnp.sum(key_grad.astype(jnp.float32), 0)
    d_bias_value = jnp.sum(value_grad.astype(jnp.float32), 0)
    input_sum = (
        product("the,hde->td", query_grad, pieces[0])
        + product("the,hde->td", key_grad, pieces[1])
        + product("the,hde->td", value_grad, pieces[2])
    )
    grad_norm = merge_grads(input_sum)
    d_inputs, d_shift_attn, d_scale_attn = jax.vjp(mod_norm, residual, shift_attn, scale_attn)[1](
        grad_norm
    )
    grad_input = grad_res + d_inputs
    grads = slot_grads(
        holder,
        kind_of_blocks(tile_count, heads_here, blocks_here),
        (rows_one, rows_grad, rows_two, context, rows_grad_two, rows_three, rows_grad_three),
        (
            query_grad,
            key_grad,
            value_grad,
            heads_out,
            cross_query_grad,
            cross_key_grad,
            cross_value_grad,
            cross_heads_out,
            d_hidden_low,
            hidden_low,
        ),
    )
    first_part, second_part = reduce_slots(grads, slot_count)
    new_master, new_first, new_second = adam_slots(
        first_part, second_part, master, first_moment, second_moment, slot_scale, filled
    )
    head_grad = jnp.concatenate(
        [
            d_bias_query.reshape(-1),
            d_bias_key.reshape(-1),
            d_bias_value.reshape(-1),
            d_gain_query.reshape(-1),
            d_gain_key.reshape(-1),
            d_cross_bias_q.reshape(-1),
            d_cross_bias_k.reshape(-1),
            d_cross_bias_v.reshape(-1),
            d_cross_gain_q.reshape(-1),
            d_cross_gain_k.reshape(-1),
            d_up_bias.reshape(-1),
        ]
    )
    tensor_rank = lax.axis_index("tensor")
    head_padded = jnp.where(jnp.arange(tensors)[:, None] == rank, head_grad[None, :], 0.0)
    shared_grad = jnp.stack(
        [
            d_self_bias_out,
            d_cross_bias_out,
            d_down_bias,
            d_norm_gain,
            d_norm_bias,
            d_shift_attn,
            d_scale_attn,
            d_gate_attn,
            d_shift_ffn,
            d_scale_ffn,
            d_gate_ffn,
        ]
    )
    head_total, shared_total = lax.psum((head_padded, shared_grad), ("dp", "tensor"))
    mine_head = lax.dynamic_slice_in_dim(head_total, tensor_rank, 1, 0)
    new_head, new_head_first, new_head_second = adam_step(
        head_params, mine_head, head_first, head_second, VECTOR_RATE, 0.0
    )
    new_shared, new_shared_first, new_shared_second = adam_step(
        shared_params, shared_total, shared_first, shared_second, VECTOR_RATE, 0.0
    )
    output, grad_input = home_swap(output, grad_input)
    return (
        output,
        grad_input,
        new_master,
        new_first,
        new_second,
        new_head,
        new_head_first,
        new_head_second,
        new_shared,
        new_shared_first,
        new_shared_second,
    )


def solution(mesh):
    return jax.shard_map(
        body,
        mesh=mesh,
        in_specs=(
            P(("dp", "tensor"), None),
            P("dp", None),
            P(("dp", "tensor"), None),
            P(None, "dp"),
            P("dp"),
            P(),
            P(),
            P("tensor", "dp", None, None),
            P("tensor", "dp", None, None),
            P("tensor", "dp", None, None),
            P("tensor", None),
            P("tensor", None),
            P("tensor", None),
            P(),
            P(),
            P(),
        ),
        out_specs=(
            P(("dp", "tensor"), None),
            P(("dp", "tensor"), None),
            P("tensor", "dp", None, None),
            P("tensor", "dp", None, None),
            P("tensor", "dp", None, None),
            P("tensor", None),
            P("tensor", None),
            P("tensor", None),
            P(),
            P(),
            P(),
        ),
        check_vma=False,
    )
```

```python
import functools

import jax
import jax.numpy as jnp
from jax import lax
from jax.experimental import pallas as pl
from jax.experimental.pallas import tpu as pltpu
from jax.sharding import PartitionSpec as P

D = 1536
HEADS = 12
HEAD = 128
FF = 8960
TSTEPS = 16
STEPC = 10


NORM_EPS = 1e-06
BETA_ONE = 0.9
BETA_TWO = 0.999
ADAM_EPS = 1e-08
TILE_RATE = 1.0
TILE_DECAY = 0.1
VECTOR_RATE = 0.5
GELU_COEF = 0.7978845608028654


def product(form, left, right):
    return jnp.einsum(form, left, right, preferred_element_type=jnp.float32)


def layer_norm(inputs):
    centre = inputs - jnp.mean(inputs, -1, keepdims=True)
    return centre * lax.rsqrt(jnp.mean(centre * centre, -1, keepdims=True) + NORM_EPS)


def gelu_tanh(inputs):
    return (
        0.5 * inputs * (1.0 + jnp.tanh(GELU_COEF * (inputs + 0.044715 * inputs * inputs * inputs)))
    )


def rotate(inputs):
    paired = inputs.reshape(inputs.shape[:-1] + (inputs.shape[-1] // 2, 2))
    return jnp.stack([-paired[..., 1], paired[..., 0]], -1).reshape(inputs.shape)


def rope(inputs, cos_tab, sin_tab):
    return inputs * cos_tab[..., None, :] + rotate(inputs) * sin_tab[..., None, :]


def rope_tables(token_places, head_size):
    sixths = head_size // 6
    frame_pairs = (head_size - 4 * sixths) // 2
    frame_freq = 10000.0 ** (-jnp.arange(frame_pairs, dtype=jnp.float32) / frame_pairs)
    side_freq = 10000.0 ** (-jnp.arange(sixths, dtype=jnp.float32) / sixths)
    spots = token_places.astype(jnp.float32)
    angles = jnp.concatenate(
        [
            spots[0][..., None] * frame_freq,
            spots[1][..., None] * side_freq,
            spots[2][..., None] * side_freq,
        ],
        -1,
    )
    angles = jnp.repeat(angles, 2, axis=-1)
    return (jnp.cos(angles), jnp.sin(angles))


def owner_layout(owners, slot_count, devices):
    indices = jnp.arange(owners.shape[0], dtype=jnp.int32)
    same_owner = (owners[:, None] == owners[None, :]) & (indices[None, :] < indices[:, None])
    slot_of = jnp.sum(same_owner.astype(jnp.int32), axis=1)
    places = owners * slot_count + slot_of
    spots = jnp.arange(slot_count * devices, dtype=jnp.int32)
    holder = (
        jnp.sum(jnp.where(places[None, :] == spots[:, None], indices[None, :] + 1, 0), axis=1) - 1
    )
    return (places, holder)


def tile_scales(tile_count, heads_here, blocks_here):
    indices = jnp.arange(tile_count)
    scale_in = D ** (-0.5)
    scale_out = HEADS ** (-0.5)
    scale_down = FF ** (-0.5)
    scales = jnp.where(
        indices < 3 * heads_here,
        scale_in,
        jnp.where(
            indices < 4 * heads_here,
            scale_out,
            jnp.where(
                indices < 7 * heads_here,
                scale_in,
                jnp.where(
                    indices < 8 * heads_here,
                    scale_out,
                    jnp.where(indices < 8 * heads_here + blocks_here, scale_in, scale_down),
                ),
            ),
        ),
    )
    return scales.astype(jnp.float32)


def tile_views(weights, heads_here, blocks_here):
    pieces = [weights[number * heads_here : (number + 1) * heads_here] for number in range(8)]
    start_up = 8 * heads_here
    pieces.append(weights[start_up : start_up + blocks_here])
    pieces.append(weights[start_up + blocks_here :])
    return pieces


def adam_step(weight, gradient, moment_one, moment_two, step_rate, decay_rate):
    first_new = BETA_ONE * moment_one + (1.0 - BETA_ONE) * gradient
    second_new = BETA_TWO * moment_two + (1.0 - BETA_TWO) * gradient * gradient
    first_hat = first_new / (1.0 - BETA_ONE**STEPC)
    second_hat = second_new / (1.0 - BETA_TWO**STEPC)
    weight_new = weight - step_rate * (
        first_hat / (jnp.sqrt(second_hat) + ADAM_EPS) + decay_rate * weight
    )
    return (weight_new, first_new, second_new)


def attend(query_low, key_low, value_low, scaling):
    scores = product("qhe,khe->hqk", query_low, key_low) * scaling
    row_max = jnp.max(scores, -1, keepdims=True)
    log_total = row_max + jnp.log(jnp.sum(jnp.exp(scores - row_max), -1, keepdims=True))
    softmax_low = jnp.exp(scores - log_total).astype(jnp.bfloat16)
    heads_out = product("hqk,khe->qhe", softmax_low, value_low).astype(jnp.bfloat16)
    return (log_total, heads_out)


def attend_back(query_low, key_low, value_low, log_total, d_heads, scaling):
    scores = product("qhe,khe->hqk", query_low, key_low) * scaling
    softmax_rows = jnp.exp(scores - log_total)
    d_softmax = product("qhe,khe->hqk", d_heads, value_low)
    d_scores = (
        softmax_rows * (d_softmax - jnp.sum(softmax_rows * d_softmax, -1, keepdims=True))
    ).astype(jnp.bfloat16)
    d_query = product("hqk,khe->qhe", d_scores, key_low) * scaling
    d_key = product("hqk,qhe->khe", d_scores, query_low) * scaling
    d_value = product("hqk,qhe->khe", softmax_rows.astype(jnp.bfloat16), d_heads)
    return (d_query, d_key, d_value)


def norm_stats(query_pre, key_pre):
    totals = pair_sums(
        jnp.sum(query_pre * query_pre, (1, 2)), jnp.sum(key_pre * key_pre, (1, 2))
    )
    return tuple((lax.rsqrt(total / D + NORM_EPS)[:, None, None] for total in totals))


def norm_back(query_pre, query_inv, query_gain, query_in, key_pre, key_inv, key_gain, key_in):
    totals = pair_sums(
        jnp.sum(query_pre * query_gain * query_in, (1, 2)),
        jnp.sum(key_pre * key_gain * key_in, (1, 2)),
    )
    results = []
    for pre_vals, inverse, gain_vec, incoming, total in (
        (query_pre, query_inv, query_gain, query_in, totals[0]),
        (key_pre, key_inv, key_gain, key_in, totals[1]),
    ):
        d_pre = inverse * (gain_vec * incoming) - pre_vals * inverse * inverse * inverse * (
            total[:, None, None] / D
        )
        d_gain = jnp.sum(incoming * pre_vals * inverse, 0)
        results.append(d_pre)
        results.append(d_gain)
    return results


MESH = pl.DeviceIdType.MESH
ANY = pl.BlockSpec(memory_space=pl.ANY)
MIB = 1 << 20


def chip_pairs():
    return lax.axis_size("dp") == 16 and lax.axis_size("tensor") == 2


def pair_rank():
    if chip_pairs():
        return (lax.axis_index("dp") // 4) % 2
    return lax.axis_index("tensor")


def pair_swap(value):
    if chip_pairs():
        return lax.ppermute(value, "dp", [(i, i ^ 4) for i in range(16)])
    return lax.ppermute(value, "tensor", [(0, 1), (1, 0)])


def pair_sums(*values):
    stacked = jnp.concatenate([v.reshape(-1) for v in values])
    total = stacked + pair_swap(stacked)
    out, at = [], 0
    for v in values:
        out.append(total[at : at + v.size].reshape(v.shape))
        at += v.size
    return tuple(out)


def home_swap(*values):
    if not chip_pairs():
        return values
    chip, core = lax.axis_index("dp"), lax.axis_index("tensor")
    away = (chip // 4) % 2 != core
    order = [
        (d * 2 + c, (d ^ 4) * 2 + 1 - c) for d in range(16) for c in range(2) if (d // 4) % 2 != c
    ]
    return tuple(
        jnp.where(away, lax.ppermute(v, ("dp", "tensor"), order), v) for v in values
    )


def place_of():
    chip, core = lax.axis_index("dp"), lax.axis_index("tensor")
    z, y, x = chip // 4, (chip // 2) % 2, chip % 2
    return chip, core, z, y, x


def column_of(z, y, x, k):
    high, low_bit = z // 2, z % 2
    if k & 2:
        high = 1 - high
    if k & 1:
        low_bit = 1 - low_bit
    return (2 * high + low_bit) * 4 + 2 * y + x


def greet(chip, core, z, y, x):
    barrier = pltpu.get_barrier_semaphore()
    friends = []
    for k in range(4):
        for flip in (0, 1):
            if k or flip:
                friends.append((column_of(z, y, x, k), core if flip == 0 else 1 - core))
    friends.append((column_of(z, y, 1 - x, 0), core))
    friends.append((column_of(z, 1 - y, x, 0), core))
    for friend in friends:
        pl.semaphore_signal(barrier, inc=1, device_id=friend, device_id_type=MESH)
    pl.semaphore_wait(barrier, len(friends))


def gather_kernel(own, out, near_s, local_s, col_r, x_s, x_r, y_s, y_r, ra_s, ra_r, rb_s, rb_r, sib_s, sib_r):
    chip, core, z, y, x = place_of()
    rank = z % 2
    half = own.shape[1] // 2
    part = half // 2
    at_x = column_of(z, y, 1 - x, 0)
    at_y = column_of(z, 1 - y, x, 0)
    greet(chip, core, z, y, x)

    def rows(ref, unit, first, count):
        return ref.at[unit, :, pl.ds(pl.multiple_of(first, 16), count), :]

    def remote(unit, first, count, send, recv, device):
        piece = rows(out, unit, first, count)
        return pltpu.make_async_remote_copy(
            src_ref=piece, dst_ref=piece, send_sem=send, recv_sem=recv,
            device_id=device, device_id_type=MESH,
        )

    started = []
    for j in range(2):
        zh = z // 2 if j == 0 else 1 - z // 2
        target = (2 * zh + core) * 4 + 2 * y + x
        for h in range(2):
            src = own.at[:, pl.ds(h * half, half), :]
            dst = out.at[chip, :, pl.ds(h * half, half), :]
            go = pltpu.make_async_remote_copy(
                src_ref=src, dst_ref=dst, send_sem=near_s.at[2 * j + h], recv_sem=col_r.at[z],
                device_id=(target, h), device_id_type=MESH,
            )
            if j == 0:
                here = pltpu.make_async_copy(src, dst, col_r.at[z])
                stays = jnp.logical_and(rank == core, core == h)

                @pl.when(stays)
                def _():
                    here.start()

                @pl.when(jnp.logical_not(stays))
                def _():
                    go.start()

                started.append((go, stays))
            else:
                go.start()
                started.append((go, None))

    def column_in(k):
        unit = column_of(z, y, x, k)
        source_z = unit // 4
        piece = rows(out, unit, core * half, half)
        pltpu.make_async_copy(piece, piece, col_r.at[source_z]).wait()
        to_x = remote(unit, core * half, half, x_s.at[k], x_r.at[k], (at_x, core))
        to_y = remote(unit, core * half, half, y_s.at[k], y_r.at[k], (at_y, core))
        to_sib = remote(unit, core * half, half, sib_s.at[k], sib_r.at[k], (chip, 1 - core))
        to_x.start()
        to_y.start()
        to_sib.start()
        return [to_x, to_y, to_sib]

    def side_in(k):
        ux = column_of(z, y, 1 - x, k)
        uy = column_of(z, 1 - y, x, k)
        remote(ux, core * half, half, x_s.at[k], x_r.at[k], (at_x, core)).wait_recv()
        on_y = remote(ux, core * half + part, part, rb_s.at[k], rb_r.at[k], (at_y, core))
        on_y.start()
        sib_x = remote(ux, core * half, half, sib_s.at[4 + k], sib_r.at[4 + k], (chip, 1 - core))
        sib_x.start()
        remote(uy, core * half, half, y_s.at[k], y_r.at[k], (at_y, core)).wait_recv()
        on_x = remote(uy, core * half, part, ra_s.at[k], ra_r.at[k], (at_x, core))
        on_x.start()
        sib_y = remote(uy, core * half, half, sib_s.at[8 + k], sib_r.at[8 + k], (chip, 1 - core))
        sib_y.start()
        return [on_y, sib_x, on_x, sib_y]

    def corner_in(k):
        unit = column_of(z, 1 - y, 1 - x, k)
        remote(unit, core * half, part, ra_s.at[k], ra_r.at[k], (at_x, core)).wait_recv()
        sib_a = remote(unit, core * half, part, sib_s.at[12 + k], sib_r.at[12 + k], (chip, 1 - core))
        sib_a.start()
        remote(unit, core * half + part, part, rb_s.at[k], rb_r.at[k], (at_y, core)).wait_recv()
        sib_b = remote(
            unit, core * half + part, part, sib_s.at[16 + k], sib_r.at[16 + k], (chip, 1 - core)
        )
        sib_b.start()
        return [sib_a, sib_b]

    sent = []
    for step in range(6):
        if step < 4:
            sent += column_in(step)
        if 1 <= step < 5:
            sent += side_in(step - 1)
        if step >= 2:
            sent += corner_in(step - 2)
    for copy in sent:
        copy.wait_send()
    for go, stays in started:
        if stays is None:
            go.wait_send()
        else:

            @pl.when(jnp.logical_not(stays))
            def _():
                go.wait_send()

    other = (1 - core) * half
    for k in range(4):
        for at, (yy, xx) in ((0, (y, x)), (4, (y, 1 - x)), (8, (1 - y, x))):
            remote(
                column_of(z, yy, xx, k), other, half, sib_s.at[at + k], sib_r.at[at + k],
                (chip, 1 - core),
            ).wait_recv()
        corner = column_of(z, 1 - y, 1 - x, k)
        remote(
            corner, other, part, sib_s.at[12 + k], sib_r.at[12 + k], (chip, 1 - core)
        ).wait_recv()
        remote(
            corner, other + part, part, sib_s.at[16 + k], sib_r.at[16 + k], (chip, 1 - core)
        ).wait_recv()


def gather_slots(scaled):
    if not chip_pairs():
        return lax.all_gather(scaled, "dp", axis=0, tiled=True)
    dma = pltpu.SemaphoreType.DMA
    counts = (4, 1, 4, 4, 4, 4, 4, 4, 4, 4, 4, 20, 20)
    everyone = pl.pallas_call(
        gather_kernel,
        out_shape=jax.ShapeDtypeStruct((16,) + scaled.shape, scaled.dtype),
        in_specs=[ANY],
        out_specs=ANY,
        scratch_shapes=[dma((n,)) for n in counts],
        compiler_params=pltpu.CompilerParams(
            collective_id=0, has_side_effects=True, vmem_limit_bytes=4 * MIB
        ),
    )(scaled)
    return everyone.reshape((-1,) + scaled.shape[1:])


def toggled(z, y, x, flip_y, flip_x, k):
    high = (z // 2 + k // 2) % 2
    low_bit = (z % 2 + k % 2) % 2
    return (2 * high + low_bit) * 4 + 2 * ((y + flip_y) % 2) + (x + flip_x) % 2


def reduce_kernel(
    kind, block, left, right, vec_in,
    final, vec_out, to_sib, from_sib, chip_sum, from_x, from_y, corner_a, corner_b,
    vec_box, sib_s, sib_r, x_s, x_r, y_s, y_r, ca_s, ca_r, cb_s, cb_r, f_s, f_r, v_s, v_r,
):
    chip, core, z, y, x = place_of()
    rank = z % 2
    slots, width, lanes = final.shape[1:]
    half = width // 2
    part = half // 2
    at_x = toggled(z, y, x, 0, 1, 0)
    at_y = toggled(z, y, x, 1, 0, 0)
    greet(chip, core, z, y, x)
    sibling = (chip, 1 - core)
    mates = (
        sibling,
        (at_x, core),
        (at_y, core),
        (toggled(z, y, x, 0, 0, 1), core),
        (toggled(z, y, x, 0, 0, 2), core),
    )

    def remote(src, dst, send, recv, device):
        return pltpu.make_async_remote_copy(
            src_ref=src, dst_ref=dst, send_sem=send, recv_sem=recv,
            device_id=device, device_id_type=MESH,
        )

    def unit_of(q, k):
        return toggled(z, y, x, 1 - q % 2, 1 - q // 2, k)

    def sums(q, k, first, count, terms, total):
        base = unit_of(q, k) * slots
        spec = pl.BlockSpec((1, count, lanes), lambda i: (i, 0, 0))

        def add(*refs):
            *parts, result = refs
            slot = base + pl.program_id(0)
            rows = pl.ds(pl.multiple_of(first, 128), count)
            acc = jnp.dot(
                left[kind[slot], rows, :], right[block[slot]], preferred_element_type=jnp.float32
            )
            for one in parts:
                acc = acc + one[0].astype(jnp.float32)
            result[0] = acc.astype(result.dtype)

        pltpu.emit_pipeline(
            add, grid=(slots,), in_specs=[spec] * len(terms), out_specs=[spec]
        )(*terms, total)

    mine, other = core * half, (1 - core) * half

    def sib_copy(q, k):
        i = 4 * q + k
        return remote(to_sib.at[i], from_sib.at[i], sib_s.at[i], sib_r.at[i], sibling)

    def sub(ref, first):
        return ref.at[:, pl.ds(first, part), :]

    def a_copy(k):
        return remote(sub(chip_sum.at[k], 0), corner_a.at[k], ca_s.at[k], ca_r.at[k], (at_x, core))

    def b_copy(k):
        return remote(sub(chip_sum.at[k], part), corner_b.at[k], cb_s.at[k], cb_r.at[k], (at_y, core))

    def x_copy(k):
        return remote(chip_sum.at[4 + k], from_x.at[k], x_s.at[k], x_r.at[k], (at_x, core))

    def y_copy(k):
        return remote(chip_sum.at[8 + k], from_y.at[k], y_s.at[k], y_r.at[k], (at_y, core))

    def f_copy(k):
        dst = final.at[z // 2, :, pl.ds(pl.multiple_of(mine, 128), half), :]
        recv = f_r.at[2 * (z // 2) + core]
        return remote(
            chip_sum.at[12 + k], dst, f_s.at[k], recv, (toggled(z, y, x, 0, 0, k), rank)
        ), pltpu.make_async_copy(chip_sum.at[12 + k], dst, recv)

    def stays(k):
        return jnp.logical_and(k == 0, rank == core)

    def for_sibling(k):
        def one(q, carry):
            sums(q, k, other, half, (), to_sib.at[4 * q + k])
            sib_copy(q, k).start()
            return carry

        lax.fori_loop(0, 4, one, 0)

    def corner(k):
        sib_copy(0, k).wait_recv()
        sums(0, k, mine, half, (from_sib.at[k],), chip_sum.at[k])
        a_copy(k).start()
        b_copy(k).start()

    def sides(k):
        ix, iy = 4 + k, 8 + k
        sib_copy(1, k).wait_recv()
        sib_copy(2, k).wait_recv()
        sums(1, k, mine, part, (sub(from_sib.at[ix], 0),), sub(chip_sum.at[ix], 0))
        sums(2, k, mine + part, part, (sub(from_sib.at[iy], part),), sub(chip_sum.at[iy], part))
        b_copy(k).wait_recv()
        sums(
            1, k, mine + part, part, (sub(from_sib.at[ix], part), corner_b.at[k]),
            sub(chip_sum.at[ix], part),
        )
        x_copy(k).start()
        a_copy(k).wait_recv()
        sums(
            2, k, mine, part, (sub(from_sib.at[iy], 0), corner_a.at[k]), sub(chip_sum.at[iy], 0)
        )
        y_copy(k).start()

    def centre(k):
        sib_copy(3, k).wait_recv()
        x_copy(k).wait_recv()
        y_copy(k).wait_recv()
        sums(
            3, k, mine, half, (from_sib.at[12 + k], from_x.at[k], from_y.at[k]),
            chip_sum.at[12 + k],
        )
        go, here = f_copy(k)

        @pl.when(stays(k))
        def _():
            here.start()

        @pl.when(jnp.logical_not(stays(k)))
        def _():
            go.start()

    def vec_copy(i):
        return remote(vec_out, vec_box.at[i], v_s.at[i], v_r.at[i], mates[i])

    vec_out[...] = vec_in[...]

    def turn(step, carry):
        for i in range(5):

            @pl.when(step == i)
            def _():
                vec_copy(i).start()

        @pl.when(step < 4)
        def _():
            for_sibling(3 - step)
            corner(3 - step)

        @pl.when(jnp.logical_and(step >= 1, step < 5))
        def _():
            sides(4 - step)

        @pl.when(step >= 2)
        def _():
            centre(5 - step)

        for i in range(5):

            @pl.when(step == i)
            def _():
                vec_copy(i).wait()
                vec_out[...] = vec_out[...] + vec_box[i]

        return carry

    lax.fori_loop(0, 6, turn, 0)

    def settle(k, carry):
        for q in range(4):
            sib_copy(q, k).wait_send()
        a_copy(k).wait_send()
        b_copy(k).wait_send()
        x_copy(k).wait_send()
        y_copy(k).wait_send()

        @pl.when(jnp.logical_not(stays(k)))
        def _():
            f_copy(k)[0].wait_send()

        return carry

    lax.fori_loop(0, 4, settle, 0)
    for plane in range(2):
        for h in range(2):
            piece = final.at[plane, :, pl.ds(h * half, half), :]
            pltpu.make_async_copy(piece, piece, f_r.at[2 * plane + h]).wait()


def reduce_slots(holder, kinds, rows, columns, vector, slot_count):
    if not chip_pairs():
        grads = slot_grads(holder, kinds, rows, columns)
        total = lax.psum_scatter(grads, "dp", scatter_dimension=0, tiled=True)
        return [total], lax.psum(vector, ("dp", "tensor"))
    depth = max(r.shape[0] for r in rows)
    left = jnp.stack([jnp.pad(r, ((0, depth - r.shape[0]), (0, 0))).T for r in rows])
    lanes = columns[0].shape[2]
    right = [
        jnp.pad(c.transpose(1, 0, 2), ((0, 0), (0, depth - c.shape[0]), (0, 0))) for c in columns
    ]
    right = jnp.concatenate(right + [jnp.zeros((1, depth, lanes), right[0].dtype)], 0)
    block = jnp.where(holder >= 0, holder, right.shape[0] - 1)
    kind = kinds[jnp.maximum(holder, 0)]
    width = rows[0].shape[1]
    half = width // 2
    dma = pltpu.SemaphoreType.DMA
    scalars = pl.BlockSpec(memory_space=pltpu.SMEM)
    inside = pl.BlockSpec(memory_space=pltpu.VMEM)

    def room(count, tall):
        return jax.ShapeDtypeStruct((count, slot_count, tall, lanes), jnp.bfloat16)

    outs = pl.pallas_call(
        reduce_kernel,
        out_shape=[
            room(2, width), jax.ShapeDtypeStruct(vector.shape, vector.dtype),
            room(16, half), room(16, half), room(16, half), room(4, half), room(4, half),
            room(4, half // 2), room(4, half // 2),
        ],
        in_specs=[scalars, scalars, inside, inside, inside],
        out_specs=[ANY, inside] + [ANY] * 7,
        scratch_shapes=[pltpu.VMEM((5,) + vector.shape, vector.dtype)]
        + [dma((n,)) for n in (16, 16) + (4,) * 10 + (5, 5)],
        compiler_params=pltpu.CompilerParams(
            collective_id=1, has_side_effects=True, vmem_limit_bytes=56 * MIB
        ),
    )(kind, block, left, right, vector)
    return [outs[0][0], outs[0][1]], outs[1]


def pick_blocks(everyone, places):
    shape = everyone.shape[1:]
    count = places.shape[0]

    def copy(_, src, dst):
        dst[...] = src[...]

    return pl.pallas_call(
        copy,
        grid_spec=pltpu.PrefetchScalarGridSpec(
            num_scalar_prefetch=1,
            grid=(count,),
            in_specs=[pl.BlockSpec((1,) + shape, lambda m, where: (where[m], 0, 0))],
            out_specs=pl.BlockSpec((1,) + shape, lambda m, where: (m, 0, 0)),
        ),
        out_shape=jax.ShapeDtypeStruct((count,) + shape, everyone.dtype),
    )(places, everyone)


def kind_of_blocks(tile_count, heads_here, blocks_here):
    number = jnp.arange(tile_count)
    kind = number // heads_here
    table = jnp.array([0, 0, 0, 1, 2, 3, 3, 4], jnp.int32)
    late = jnp.where(number < 8 * heads_here + blocks_here, 5, 6)
    return jnp.where(number < 8 * heads_here, table[jnp.minimum(kind, 7)], late).astype(jnp.int32)


def slot_grads(holder, kinds, rows, columns):
    depth = max(r.shape[0] for r in rows)

    def deep(value, axis):
        room = [(0, 0)] * value.ndim
        room[axis] = (0, depth - value.shape[axis])
        return jnp.pad(value, room)

    left = jnp.stack([deep(r, 0) for r in rows])
    right = jnp.concatenate([deep(c, 0) for c in columns], 1).transpose(1, 0, 2)
    slots = holder.shape[0]
    used = (holder >= 0).astype(jnp.int32)
    block = jnp.maximum(holder, 0)
    kind = kinds[block]
    width = rows[0].shape[1]
    lanes = right.shape[2]

    def multiply(kind_ref, block_ref, used_ref, left_ref, right_ref, out_ref):
        slot = pl.program_id(0)

        @pl.when(used_ref[slot] == 1)
        def _():
            out_ref[0] = lax.dot_general(
                left_ref[kind_ref[slot]],
                right_ref[0],
                (((0,), (0,)), ((), ())),
                preferred_element_type=jnp.float32,
            ).astype(out_ref.dtype)

        @pl.when(used_ref[slot] == 0)
        def _():
            out_ref[...] = jnp.zeros_like(out_ref)

    return pl.pallas_call(
        multiply,
        grid_spec=pltpu.PrefetchScalarGridSpec(
            num_scalar_prefetch=3,
            grid=(slots,),
            in_specs=[
                pl.BlockSpec(left.shape, lambda s, kd, b, u: (0, 0, 0)),
                pl.BlockSpec((1, depth, lanes), lambda s, kd, b, u: (b[s], 0, 0)),
            ],
            out_specs=pl.BlockSpec((1, width, lanes), lambda s, kd, b, u: (s, 0, 0)),
        ),
        out_shape=jax.ShapeDtypeStruct((slots, width, lanes), jnp.bfloat16),
        compiler_params=pltpu.CompilerParams(vmem_limit_bytes=48 * MIB),
    )(kind, block, used, left, right)


def adam_slots(parts, master, moment_one, moment_two, slot_scale, filled):
    slot_count, width, lanes = master.shape[1:]
    count = len(parts)
    tall = width // 2

    def step(scale_ref, fill_ref, *refs):
        grads = refs[:count]
        weight, one, two, new_weight, new_one, new_two = refs[count:]
        slot = pl.program_id(0)

        @pl.when(fill_ref[slot] == 1)
        def _():
            total = grads[0][0].astype(jnp.float32)
            for more in grads[1:]:
                total = total + more[0].astype(jnp.float32)
            results = adam_step(
                weight[0, 0], total * scale_ref[slot], one[0, 0], two[0, 0], TILE_RATE, TILE_DECAY
            )
            for ref, value in zip((new_weight, new_one, new_two), results):
                ref[0, 0] = value

        @pl.when(fill_ref[slot] == 0)
        def _():
            new_weight[...] = weight[...]
            new_one[...] = one[...]
            new_two[...] = two[...]

    flat = pl.BlockSpec((1, tall, lanes), lambda s, i: (s, i, 0))
    deep = pl.BlockSpec((1, 1, tall, lanes), lambda s, i: (0, s, i, 0))
    scalars = pl.BlockSpec(memory_space=pltpu.SMEM)
    return pl.pallas_call(
        step,
        grid=(slot_count, 2),
        in_specs=[scalars, scalars] + [flat] * count + [deep] * 3,
        out_specs=[deep] * 3,
        out_shape=[jax.ShapeDtypeStruct(master.shape, jnp.float32)] * 3,
    )(slot_scale, filled.astype(jnp.int32), *parts, master, moment_one, moment_two)


def body(
    latents,
    context,
    cotangent,
    positions,
    step_ids,
    owners,
    time_table,
    master,
    first_moment,
    second_moment,
    head_params,
    head_first,
    head_second,
    shared_params,
    shared_first,
    shared_second,
):
    tensors = lax.axis_size("tensor")
    devices = lax.axis_size("dp")
    slot_count = master.shape[1]
    tile_count = owners.shape[0]
    heads_here = HEADS // tensors
    blocks_here = FF // (HEAD * tensors)
    width_here = D // tensors
    scaling = HEAD ** (-0.5)
    places, holder = owner_layout(owners, slot_count, devices)
    scales = tile_scales(tile_count, heads_here, blocks_here)
    my_slots = lax.dynamic_slice_in_dim(holder, lax.axis_index("dp") * slot_count, slot_count)
    rank = pair_rank()
    latents, context, cotangent, positions, step_ids, head_here = home_swap(
        latents, context, cotangent, positions, step_ids, head_params
    )
    filled = my_slots >= 0
    slot_scale = jnp.where(filled, scales[jnp.maximum(my_slots, 0)], 0.0)
    scaled = (master[0] * slot_scale[:, None, None]).astype(jnp.bfloat16)
    everyone = gather_slots(scaled)
    pieces = tile_views(pick_blocks(everyone, places), heads_here, blocks_here)
    vectors = head_here[0]

    def head_vector(number):
        return vectors[number * width_here : (number + 1) * width_here].reshape(heads_here, HEAD)

    bias_query, bias_key, bias_value, gain_query, gain_key = [
        head_vector(number) for number in range(5)
    ]
    cross_bias_q, cross_bias_k, cross_bias_v, cross_gain_q, cross_gain_k = [
        head_vector(number) for number in range(5, 10)
    ]
    up_bias = vectors[10 * width_here :].reshape(blocks_here, HEAD)
    chosen = (step_ids[0] == jnp.arange(TSTEPS)).astype(jnp.float32)
    modulation = shared_params[5:11] + jnp.einsum(
        "s,skd->kd", chosen, time_table, precision=lax.Precision.HIGHEST
    )
    shift_attn, scale_attn, gate_attn = (modulation[0], modulation[1], modulation[2])
    shift_ffn, scale_ffn, gate_ffn = (modulation[3], modulation[4], modulation[5])
    cos_tab, sin_tab = rope_tables(positions, HEAD)

    def mod_norm(inputs, shift_vec, scale_vec):
        return layer_norm(inputs) * (1.0 + scale_vec) + shift_vec

    def affine_norm(inputs, gain_vec, bias_vec):
        return layer_norm(inputs) * gain_vec + bias_vec

    def spread_rows(local_rows):
        other = pair_swap(local_rows)
        return jnp.where(
            rank == 0,
            jnp.concatenate([local_rows, other], 0),
            jnp.concatenate([other, local_rows], 0),
        )

    def merge_rows(summand):
        half = summand.shape[0] // 2
        mine = lax.dynamic_slice_in_dim(summand, rank * half, half, 0)
        theirs = lax.dynamic_slice_in_dim(summand, (1 - rank) * half, half, 0)
        return mine + pair_swap(theirs.astype(jnp.bfloat16)).astype(jnp.float32)

    spread_grads, merge_grads = spread_rows, merge_rows

    residual = latents.astype(jnp.float32)
    low_one = mod_norm(residual, shift_attn, scale_attn).astype(jnp.bfloat16)
    rows_one = spread_rows(low_one)
    query_pre = product("td,hde->the", rows_one, pieces[0]) + bias_query
    key_pre = product("td,hde->the", rows_one, pieces[1]) + bias_key
    value_low = (product("td,hde->the", rows_one, pieces[2]) + bias_value).astype(jnp.bfloat16)
    query_inv, key_inv = norm_stats(query_pre, key_pre)
    query_low = rope(query_pre * query_inv * gain_query, cos_tab, sin_tab).astype(jnp.bfloat16)
    key_low = rope(key_pre * key_inv * gain_key, cos_tab, sin_tab).astype(jnp.bfloat16)
    log_total, heads_out = attend(query_low, key_low, value_low, scaling)
    saved_one = (
        query_pre,
        key_pre,
        query_inv,
        key_inv,
        query_low,
        key_low,
        value_low,
        log_total,
        heads_out,
    )
    branch_one = merge_rows(product("the,hde->td", saved_one[-1], pieces[3])) + shared_params[0]
    after_one = residual + gate_attn * branch_one
    low_two = affine_norm(after_one, shared_params[3], shared_params[4]).astype(jnp.bfloat16)
    rows_two = spread_rows(low_two)
    query_pre = product("td,hde->the", rows_two, pieces[4]) + cross_bias_q
    key_pre = product("cd,hde->che", context, pieces[5]) + cross_bias_k
    value_low = (product("cd,hde->che", context, pieces[6]) + cross_bias_v).astype(jnp.bfloat16)
    query_inv, key_inv = norm_stats(query_pre, key_pre)
    query_low = (query_pre * query_inv * cross_gain_q).astype(jnp.bfloat16)
    key_low = (key_pre * key_inv * cross_gain_k).astype(jnp.bfloat16)
    log_total, heads_out = attend(query_low, key_low, value_low, scaling)
    saved_two = (
        query_pre,
        key_pre,
        query_inv,
        key_inv,
        query_low,
        key_low,
        value_low,
        log_total,
        heads_out,
    )
    branch_two = merge_rows(product("the,hde->td", saved_two[-1], pieces[7])) + shared_params[1]
    after_two = after_one + branch_two
    low_three = mod_norm(after_two, shift_ffn, scale_ffn).astype(jnp.bfloat16)
    rows_three = spread_rows(low_three)
    hidden_pre = product("td,fde->tfe", rows_three, pieces[8]) + up_bias
    saved_three = (hidden_pre, gelu_tanh(hidden_pre).astype(jnp.bfloat16))
    branch_three = merge_rows(product("tfe,fde->td", saved_three[1], pieces[9])) + shared_params[2]
    result = after_two + gate_ffn * branch_three
    output = result.astype(jnp.bfloat16)
    grad_res = cotangent.astype(jnp.float32)
    d_gate_ffn = jnp.sum(grad_res * branch_three, 0)
    grad_branch = (gate_ffn * grad_res).astype(jnp.bfloat16)
    d_down_bias = jnp.sum(grad_branch.astype(jnp.float32), 0)
    rows_grad = spread_grads(grad_branch)
    hidden_pre, hidden_low = saved_three
    rows_grad_three = rows_grad
    d_hidden = product("td,fde->tfe", rows_grad, pieces[9])
    d_hidden = jax.vjp(gelu_tanh, hidden_pre)[1](d_hidden)[0]
    d_hidden_low = d_hidden.astype(jnp.bfloat16)
    d_up_bias = jnp.sum(d_hidden_low.astype(jnp.float32), 0)
    grad_norm = merge_grads(product("tfe,fde->td", d_hidden_low, pieces[8]))
    d_inputs, d_shift_ffn, d_scale_ffn = jax.vjp(mod_norm, after_two, shift_ffn, scale_ffn)[1](
        grad_norm
    )
    grad_res = grad_res + d_inputs
    grad_branch = grad_res.astype(jnp.bfloat16)
    d_cross_bias_out = jnp.sum(grad_branch.astype(jnp.float32), 0)
    rows_grad = spread_grads(grad_branch)
    query_pre, key_pre, query_inv, key_inv, query_low, key_low, value_low, log_total, heads_out = (
        saved_two
    )
    rows_grad_two, cross_heads_out = rows_grad, heads_out
    d_heads = product("td,hde->the", rows_grad, pieces[7]).astype(jnp.bfloat16)
    d_query, d_key, d_value = attend_back(
        query_low, key_low, value_low, log_total, d_heads, scaling
    )
    d_query, d_cross_gain_q, d_key, d_cross_gain_k = norm_back(
        query_pre, query_inv, cross_gain_q, d_query, key_pre, key_inv, cross_gain_k, d_key
    )
    query_grad = d_query.astype(jnp.bfloat16)
    key_grad = d_key.astype(jnp.bfloat16)
    value_grad = d_value.astype(jnp.bfloat16)
    d_cross_bias_q = jnp.sum(query_grad.astype(jnp.float32), 0)
    d_cross_bias_k = jnp.sum(key_grad.astype(jnp.float32), 0)
    d_cross_bias_v = jnp.sum(value_grad.astype(jnp.float32), 0)
    cross_query_grad, cross_key_grad, cross_value_grad = query_grad, key_grad, value_grad
    grad_norm = merge_grads(product("the,hde->td", query_grad, pieces[4]))
    d_inputs, d_norm_gain, d_norm_bias = jax.vjp(
        affine_norm, after_one, shared_params[3], shared_params[4]
    )[1](grad_norm)
    grad_res = grad_res + d_inputs
    d_gate_attn = jnp.sum(grad_res * branch_one, 0)
    grad_branch = (gate_attn * grad_res).astype(jnp.bfloat16)
    d_self_bias_out = jnp.sum(grad_branch.astype(jnp.float32), 0)
    rows_grad = spread_grads(grad_branch)
    query_pre, key_pre, query_inv, key_inv, query_low, key_low, value_low, log_total, heads_out = (
        saved_one
    )
    d_heads = product("td,hde->the", rows_grad, pieces[3]).astype(jnp.bfloat16)
    d_query, d_key, d_value = attend_back(
        query_low, key_low, value_low, log_total, d_heads, scaling
    )
    turned_query = rope(d_query, cos_tab, -sin_tab)
    turned_key = rope(d_key, cos_tab, -sin_tab)
    d_query, d_gain_query, d_key, d_gain_key = norm_back(
        query_pre, query_inv, gain_query, turned_query, key_pre, key_inv, gain_key, turned_key
    )
    query_grad = d_query.astype(jnp.bfloat16)
    key_grad = d_key.astype(jnp.bfloat16)
    value_grad = d_value.astype(jnp.bfloat16)
    d_bias_query = jnp.sum(query_grad.astype(jnp.float32), 0)
    d_bias_key = jnp.sum(key_grad.astype(jnp.float32), 0)
    d_bias_value = jnp.sum(value_grad.astype(jnp.float32), 0)
    input_sum = (
        product("the,hde->td", query_grad, pieces[0])
        + product("the,hde->td", key_grad, pieces[1])
        + product("the,hde->td", value_grad, pieces[2])
    )
    grad_norm = merge_grads(input_sum)
    d_inputs, d_shift_attn, d_scale_attn = jax.vjp(mod_norm, residual, shift_attn, scale_attn)[1](
        grad_norm
    )
    grad_input = grad_res + d_inputs
    head_grad = jnp.concatenate(
        [
            d_bias_query.reshape(-1),
            d_bias_key.reshape(-1),
            d_bias_value.reshape(-1),
            d_gain_query.reshape(-1),
            d_gain_key.reshape(-1),
            d_cross_bias_q.reshape(-1),
            d_cross_bias_k.reshape(-1),
            d_cross_bias_v.reshape(-1),
            d_cross_gain_q.reshape(-1),
            d_cross_gain_k.reshape(-1),
            d_up_bias.reshape(-1),
        ]
    )
    tensor_rank = lax.axis_index("tensor")
    head_padded = jnp.where(jnp.arange(tensors)[:, None] == rank, head_grad[None, :], 0.0)
    shared_grad = jnp.stack(
        [
            d_self_bias_out,
            d_cross_bias_out,
            d_down_bias,
            d_norm_gain,
            d_norm_bias,
            d_shift_attn,
            d_scale_attn,
            d_gate_attn,
            d_shift_ffn,
            d_scale_ffn,
            d_gate_ffn,
        ]
    )
    vector = jnp.concatenate([head_padded.reshape(-1), shared_grad.reshape(-1)])
    vector = jnp.pad(vector, (0, -vector.shape[0] % 1024)).reshape(-1, 128)
    parts, vector = reduce_slots(
        holder,
        kind_of_blocks(tile_count, heads_here, blocks_here),
        (rows_one, rows_grad, rows_two, context, rows_grad_two, rows_three, rows_grad_three),
        (
            query_grad,
            key_grad,
            value_grad,
            heads_out,
            cross_query_grad,
            cross_key_grad,
            cross_value_grad,
            cross_heads_out,
            d_hidden_low,
            hidden_low,
        ),
        vector,
        slot_count,
    )
    new_master, new_first, new_second = adam_slots(
        parts, master, first_moment, second_moment, slot_scale, filled
    )
    vector = vector.reshape(-1)
    head_total = vector[: head_padded.size].reshape(head_padded.shape)
    shared_total = vector[head_padded.size : head_padded.size + shared_grad.size]
    shared_total = shared_total.reshape(shared_grad.shape)
    mine_head = lax.dynamic_slice_in_dim(head_total, tensor_rank, 1, 0)
    new_head, new_head_first, new_head_second = adam_step(
        head_params, mine_head, head_first, head_second, VECTOR_RATE, 0.0
    )
    new_shared, new_shared_first, new_shared_second = adam_step(
        shared_params, shared_total, shared_first, shared_second, VECTOR_RATE, 0.0
    )
    output, grad_input = home_swap(output, grad_input)
    return (
        output,
        grad_input,
        new_master,
        new_first,
        new_second,
        new_head,
        new_head_first,
        new_head_second,
        new_shared,
        new_shared_first,
        new_shared_second,
    )


def solution(mesh):
    return jax.shard_map(
        body,
        mesh=mesh,
        in_specs=(
            P(("dp", "tensor"), None),
            P("dp", None),
            P(("dp", "tensor"), None),
            P(None, "dp"),
            P("dp"),
            P(),
            P(),
            P("tensor", "dp", None, None),
            P("tensor", "dp", None, None),
            P("tensor", "dp", None, None),
            P("tensor", None),
            P("tensor", None),
            P("tensor", None),
            P(),
            P(),
            P(),
        ),
        out_specs=(
            P(("dp", "tensor"), None),
            P(("dp", "tensor"), None),
            P("tensor", "dp", None, None),
            P("tensor", "dp", None, None),
            P("tensor", "dp", None, None),
            P("tensor", None),
            P("tensor", None),
            P("tensor", None),
            P(),
            P(),
            P(),
        ),
        check_vma=False,
    )
```

```python
import functools

import jax
import jax.numpy as jnp
from jax import lax
from jax.experimental import pallas as pl
from jax.experimental.pallas import tpu as pltpu
from jax.sharding import PartitionSpec as P

D = 1536
HEADS = 12
HEAD = 128
FF = 8960
TSTEPS = 16
STEPC = 10


NORM_EPS = 1e-06
BETA_ONE = 0.9
BETA_TWO = 0.999
ADAM_EPS = 1e-08
TILE_RATE = 1.0
TILE_DECAY = 0.1
VECTOR_RATE = 0.5
GELU_COEF = 0.7978845608028654


def rope_tables(token_places, head_size):
    sixths = head_size // 6
    frame_pairs = (head_size - 4 * sixths) // 2
    frame_freq = 10000.0 ** (-jnp.arange(frame_pairs, dtype=jnp.float32) / frame_pairs)
    side_freq = 10000.0 ** (-jnp.arange(sixths, dtype=jnp.float32) / sixths)
    spots = token_places.astype(jnp.float32)
    angles = jnp.concatenate(
        [
            spots[0][..., None] * frame_freq,
            spots[1][..., None] * side_freq,
            spots[2][..., None] * side_freq,
        ],
        -1,
    )
    angles = jnp.repeat(angles, 2, axis=-1)
    return (jnp.cos(angles), jnp.sin(angles))


def owner_layout(owners, slot_count, devices):
    indices = jnp.arange(owners.shape[0], dtype=jnp.int32)
    same_owner = (owners[:, None] == owners[None, :]) & (indices[None, :] < indices[:, None])
    slot_of = jnp.sum(same_owner.astype(jnp.int32), axis=1)
    places = owners * slot_count + slot_of
    spots = jnp.arange(slot_count * devices, dtype=jnp.int32)
    holder = (
        jnp.sum(jnp.where(places[None, :] == spots[:, None], indices[None, :] + 1, 0), axis=1) - 1
    )
    return (places, holder)


def tile_scales(tile_count, heads_here, blocks_here):
    indices = jnp.arange(tile_count)
    scale_in = D ** (-0.5)
    scale_out = HEADS ** (-0.5)
    scale_down = FF ** (-0.5)
    scales = jnp.where(
        indices < 3 * heads_here,
        scale_in,
        jnp.where(
            indices < 4 * heads_here,
            scale_out,
            jnp.where(
                indices < 7 * heads_here,
                scale_in,
                jnp.where(
                    indices < 8 * heads_here,
                    scale_out,
                    jnp.where(indices < 8 * heads_here + blocks_here, scale_in, scale_down),
                ),
            ),
        ),
    )
    return scales.astype(jnp.float32)


def adam_step(weight, gradient, moment_one, moment_two, step_rate, decay_rate):
    first_new = BETA_ONE * moment_one + (1.0 - BETA_ONE) * gradient
    second_new = BETA_TWO * moment_two + (1.0 - BETA_TWO) * gradient * gradient
    first_hat = first_new / (1.0 - BETA_ONE**STEPC)
    second_hat = second_new / (1.0 - BETA_TWO**STEPC)
    weight_new = weight - step_rate * (
        first_hat / (jnp.sqrt(second_hat) + ADAM_EPS) + decay_rate * weight
    )
    return (weight_new, first_new, second_new)


MESH = pl.DeviceIdType.MESH
ANY = pl.BlockSpec(memory_space=pl.ANY)
MIB = 1 << 20


def chip_pairs():
    return lax.axis_size("dp") == 16 and lax.axis_size("tensor") == 2


def pair_rank():
    if chip_pairs():
        return (lax.axis_index("dp") // 4) % 2
    return lax.axis_index("tensor")


def pair_swap(value):
    if chip_pairs():
        return lax.ppermute(value, "dp", [(i, i ^ 4) for i in range(16)])
    return lax.ppermute(value, "tensor", [(0, 1), (1, 0)])


def pair_sums(*values):
    stacked = jnp.concatenate([v.reshape(-1) for v in values])
    total = stacked + pair_swap(stacked)
    out, at = [], 0
    for v in values:
        out.append(total[at : at + v.size].reshape(v.shape))
        at += v.size
    return tuple(out)


def home_swap(*values):
    if not chip_pairs():
        return values
    chip, core = lax.axis_index("dp"), lax.axis_index("tensor")
    away = (chip // 4) % 2 != core
    order = [
        (d * 2 + c, (d ^ 4) * 2 + 1 - c) for d in range(16) for c in range(2) if (d // 4) % 2 != c
    ]
    return tuple(
        jnp.where(away, lax.ppermute(v, ("dp", "tensor"), order), v) for v in values
    )


def place_of():
    chip, core = lax.axis_index("dp"), lax.axis_index("tensor")
    z, y, x = chip // 4, (chip // 2) % 2, chip % 2
    return chip, core, z, y, x


def column_of(z, y, x, k):
    high, low_bit = z // 2, z % 2
    if k & 2:
        high = 1 - high
    if k & 1:
        low_bit = 1 - low_bit
    return (2 * high + low_bit) * 4 + 2 * y + x


def greet(chip, core, z, y, x):
    barrier = pltpu.get_barrier_semaphore()
    friends = []
    for k in range(4):
        for flip in (0, 1):
            if k or flip:
                friends.append((column_of(z, y, x, k), core if flip == 0 else 1 - core))
    friends.append((column_of(z, y, 1 - x, 0), core))
    friends.append((column_of(z, 1 - y, x, 0), core))
    for friend in friends:
        pl.semaphore_signal(barrier, inc=1, device_id=friend, device_id_type=MESH)
    pl.semaphore_wait(barrier, len(friends))


def gather_kernel(own, out, near_s, local_s, col_r, x_s, x_r, y_s, y_r, ra_s, ra_r, rb_s, rb_r, sib_s, sib_r):
    chip, core, z, y, x = place_of()
    rank = z % 2
    half = own.shape[1] // 2
    part = half // 2
    at_x = column_of(z, y, 1 - x, 0)
    at_y = column_of(z, 1 - y, x, 0)
    greet(chip, core, z, y, x)

    def rows(ref, unit, first, count):
        return ref.at[unit, :, pl.ds(pl.multiple_of(first, 16), count), :]

    def remote(unit, first, count, send, recv, device):
        piece = rows(out, unit, first, count)
        return pltpu.make_async_remote_copy(
            src_ref=piece, dst_ref=piece, send_sem=send, recv_sem=recv,
            device_id=device, device_id_type=MESH,
        )

    started = []
    for j in range(2):
        zh = z // 2 if j == 0 else 1 - z // 2
        target = (2 * zh + core) * 4 + 2 * y + x
        for h in range(2):
            src = own.at[:, pl.ds(h * half, half), :]
            dst = out.at[chip, :, pl.ds(h * half, half), :]
            go = pltpu.make_async_remote_copy(
                src_ref=src, dst_ref=dst, send_sem=near_s.at[2 * j + h], recv_sem=col_r.at[z],
                device_id=(target, h), device_id_type=MESH,
            )
            if j == 0:
                here = pltpu.make_async_copy(src, dst, col_r.at[z])
                stays = jnp.logical_and(rank == core, core == h)

                @pl.when(stays)
                def _():
                    here.start()

                @pl.when(jnp.logical_not(stays))
                def _():
                    go.start()

                started.append((go, stays))
            else:
                go.start()
                started.append((go, None))

    def column_in(k):
        unit = column_of(z, y, x, k)
        source_z = unit // 4
        piece = rows(out, unit, core * half, half)
        pltpu.make_async_copy(piece, piece, col_r.at[source_z]).wait()
        to_x = remote(unit, core * half, half, x_s.at[k], x_r.at[k], (at_x, core))
        to_y = remote(unit, core * half, half, y_s.at[k], y_r.at[k], (at_y, core))
        to_sib = remote(unit, core * half, half, sib_s.at[k], sib_r.at[k], (chip, 1 - core))
        to_x.start()
        to_y.start()
        to_sib.start()
        return [to_x, to_y, to_sib]

    def side_in(k):
        ux = column_of(z, y, 1 - x, k)
        uy = column_of(z, 1 - y, x, k)
        remote(ux, core * half, half, x_s.at[k], x_r.at[k], (at_x, core)).wait_recv()
        on_y = remote(ux, core * half + part, part, rb_s.at[k], rb_r.at[k], (at_y, core))
        on_y.start()
        sib_x = remote(ux, core * half, half, sib_s.at[4 + k], sib_r.at[4 + k], (chip, 1 - core))
        sib_x.start()
        remote(uy, core * half, half, y_s.at[k], y_r.at[k], (at_y, core)).wait_recv()
        on_x = remote(uy, core * half, part, ra_s.at[k], ra_r.at[k], (at_x, core))
        on_x.start()
        sib_y = remote(uy, core * half, half, sib_s.at[8 + k], sib_r.at[8 + k], (chip, 1 - core))
        sib_y.start()
        return [on_y, sib_x, on_x, sib_y]

    def corner_in(k):
        unit = column_of(z, 1 - y, 1 - x, k)
        remote(unit, core * half, part, ra_s.at[k], ra_r.at[k], (at_x, core)).wait_recv()
        sib_a = remote(unit, core * half, part, sib_s.at[12 + k], sib_r.at[12 + k], (chip, 1 - core))
        sib_a.start()
        remote(unit, core * half + part, part, rb_s.at[k], rb_r.at[k], (at_y, core)).wait_recv()
        sib_b = remote(
            unit, core * half + part, part, sib_s.at[16 + k], sib_r.at[16 + k], (chip, 1 - core)
        )
        sib_b.start()
        return [sib_a, sib_b]

    sent = []
    for step in range(6):
        if step < 4:
            sent += column_in(step)
        if 1 <= step < 5:
            sent += side_in(step - 1)
        if step >= 2:
            sent += corner_in(step - 2)
    for copy in sent:
        copy.wait_send()
    for go, stays in started:
        if stays is None:
            go.wait_send()
        else:

            @pl.when(jnp.logical_not(stays))
            def _():
                go.wait_send()

    other = (1 - core) * half
    for k in range(4):
        for at, (yy, xx) in ((0, (y, x)), (4, (y, 1 - x)), (8, (1 - y, x))):
            remote(
                column_of(z, yy, xx, k), other, half, sib_s.at[at + k], sib_r.at[at + k],
                (chip, 1 - core),
            ).wait_recv()
        corner = column_of(z, 1 - y, 1 - x, k)
        remote(
            corner, other, part, sib_s.at[12 + k], sib_r.at[12 + k], (chip, 1 - core)
        ).wait_recv()
        remote(
            corner, other + part, part, sib_s.at[16 + k], sib_r.at[16 + k], (chip, 1 - core)
        ).wait_recv()


def gather_slots(scaled):
    if not chip_pairs():
        return lax.all_gather(scaled, "dp", axis=0, tiled=True)
    dma = pltpu.SemaphoreType.DMA
    counts = (4, 1, 4, 4, 4, 4, 4, 4, 4, 4, 4, 20, 20)
    everyone = pl.pallas_call(
        gather_kernel,
        out_shape=jax.ShapeDtypeStruct((16,) + scaled.shape, scaled.dtype),
        in_specs=[ANY],
        out_specs=ANY,
        scratch_shapes=[dma((n,)) for n in counts],
        compiler_params=pltpu.CompilerParams(
            collective_id=0, has_side_effects=True, vmem_limit_bytes=4 * MIB
        ),
    )(scaled)
    return everyone.reshape((-1,) + scaled.shape[1:])


def toggled(z, y, x, flip_y, flip_x, k):
    high = (z // 2 + k // 2) % 2
    low_bit = (z % 2 + k % 2) % 2
    return (2 * high + low_bit) * 4 + 2 * ((y + flip_y) % 2) + (x + flip_x) % 2


def reduce_kernel(
    kind, block, *refs,
):
    (
        *pieces, vec_in,
        final, vec_out, from_sib, from_x, from_y, corner_a, corner_b,
        left, right, ring, corners, side_x, side_y, middle, stage, vec_box,
        load_s, stage_s, sib_s, sib_r, x_s, x_r, y_s, y_r, ca_s, ca_r, cb_s, cb_r, f_s, f_r, v_s, v_r,
    ) = refs
    chip, core, z, y, x = place_of()
    rank = z % 2
    slots, width, lanes = final.shape[1:]
    half = width // 2
    part = half // 2
    at_x = toggled(z, y, x, 0, 1, 0)
    at_y = toggled(z, y, x, 1, 0, 0)
    sibling = (chip, 1 - core)
    mates = (
        sibling,
        (at_x, core),
        (at_y, core),
        (toggled(z, y, x, 0, 0, 1), core),
        (toggled(z, y, x, 0, 0, 2), core),
    )

    kinds = left.shape[0]
    depth = right.shape[1]
    loads = [
        pltpu.make_async_copy(pieces[i], left.at[i], load_s.at[i]) for i in range(kinds)
    ]
    first = 0
    blank = []
    for i, piece in enumerate(pieces[kinds:]):
        number, rows = piece.shape[:2]
        loads.append(
            pltpu.make_async_copy(
                piece, right.at[pl.ds(first, number), pl.ds(0, rows), :], load_s.at[kinds + i]
            )
        )
        if rows < depth:
            blank.append((first, number, rows))
        first += number
    for load in loads:
        load.start()
    for start, number, rows in blank:

        def clear(i, carry):
            right[start + i, pl.ds(rows, depth - rows), :] = jnp.zeros(
                (depth - rows, lanes), right.dtype
            )
            return carry

        lax.fori_loop(0, number, clear, 0)
    right[first] = jnp.zeros((depth, lanes), right.dtype)
    vec_out[...] = vec_in[...]
    greet(chip, core, z, y, x)
    for load in loads:
        load.wait()

    def remote(src, dst, send, recv, device):
        return pltpu.make_async_remote_copy(
            src_ref=src, dst_ref=dst, send_sem=send, recv_sem=recv,
            device_id=device, device_id_type=MESH,
        )

    def unit_of(q, k):
        return toggled(z, y, x, 1 - q % 2, 1 - q // 2, k)

    def sums(q, k, first, terms, total):
        base = unit_of(q, k) * slots
        count = total.shape[1]

        def one(i, carry):
            slot = base + i
            rows = pl.ds(pl.multiple_of(first, 128), count)
            acc = jnp.dot(
                left[kind[slot], rows, :], right[block[slot]], preferred_element_type=jnp.float32
            )
            for term in terms:
                acc = acc + term[i].astype(jnp.float32)
            total[i] = acc.astype(total.dtype)
            return carry

        lax.fori_loop(0, slots, one, 0)

    mine, other = core * half, (1 - core) * half

    def sub(ref, first):
        return ref.at[:, pl.ds(first, part), :]

    def sib_copy(q, k):
        i = 4 * q + k
        return remote(ring.at[q % 2], from_sib.at[i], sib_s.at[i], sib_r.at[i], sibling)

    def a_copy(k):
        return remote(
            sub(corners.at[k % 2], 0), corner_a.at[k], ca_s.at[k], ca_r.at[k], (at_x, core)
        )

    def b_copy(k):
        return remote(
            sub(corners.at[k % 2], part), corner_b.at[k], cb_s.at[k], cb_r.at[k], (at_y, core)
        )

    def x_copy(k):
        return remote(side_x.at[k % 2], from_x.at[k], x_s.at[k], x_r.at[k], (at_x, core))

    def y_copy(k):
        return remote(side_y.at[k % 2], from_y.at[k], y_s.at[k], y_r.at[k], (at_y, core))

    def f_copy(k):
        src = middle.at[k % 2]
        dst = final.at[z // 2, :, pl.ds(pl.multiple_of(mine, 128), half), :]
        recv = f_r.at[2 * (z // 2) + core]
        return remote(
            src, dst, f_s.at[k], recv, (toggled(z, y, x, 0, 0, k), rank)
        ), pltpu.make_async_copy(src, dst, recv)

    def stays(k):
        return jnp.logical_and(k == 0, rank == core)

    def staged(source, place, i):
        copy = pltpu.make_async_copy(source, place, stage_s.at[i])
        copy.start()
        return copy

    def for_sibling(k):
        def one(q, carry):
            @pl.when(jnp.logical_or(q >= 2, k < 3))
            def _():
                back = jnp.where(q >= 2, k, k + 1)
                sib_copy((q + 2) % 4, back).wait_send()

            sums(q, k, other, (), ring.at[q % 2])
            sib_copy(q, k).start()
            return carry

        lax.fori_loop(0, 4, one, 0)

    def corner(k):
        sib_copy(0, k).wait_recv()
        staged(from_sib.at[k], stage.at[0], 0).wait()

        @pl.when(k < 2)
        def _():
            a_copy(k + 2).wait_send()
            b_copy(k + 2).wait_send()

        sums(0, k, mine, (stage.at[0],), corners.at[k % 2])
        a_copy(k).start()
        b_copy(k).start()

    def sides(k):
        sib_copy(1, k).wait_recv()
        sib_copy(2, k).wait_recv()
        in_x = staged(from_sib.at[4 + k], stage.at[0], 0)
        in_y = staged(from_sib.at[8 + k], stage.at[1], 1)

        @pl.when(k < 2)
        def _():
            x_copy(k + 2).wait_send()
            y_copy(k + 2).wait_send()

        in_x.wait()
        sums(1, k, mine, (sub(stage.at[0], 0),), sub(side_x.at[k % 2], 0))
        b_copy(k).wait_recv()
        in_b = staged(corner_b.at[k], sub(stage.at[2], 0), 2)
        in_y.wait()
        sums(2, k, mine + part, (sub(stage.at[1], part),), sub(side_y.at[k % 2], part))
        in_b.wait()
        a_copy(k).wait_recv()
        in_a = staged(corner_a.at[k], sub(stage.at[2], part), 3)
        sums(
            1, k, mine + part, (sub(stage.at[0], part), sub(stage.at[2], 0)),
            sub(side_x.at[k % 2], part),
        )
        x_copy(k).start()
        in_a.wait()
        sums(2, k, mine, (sub(stage.at[1], 0), sub(stage.at[2], part)), sub(side_y.at[k % 2], 0))
        y_copy(k).start()

    def centre(k):
        sib_copy(3, k).wait_recv()
        in_sib = staged(from_sib.at[12 + k], stage.at[0], 0)
        x_copy(k).wait_recv()
        in_x = staged(from_x.at[k], stage.at[1], 1)
        y_copy(k).wait_recv()
        in_y = staged(from_y.at[k], stage.at[2], 2)

        @pl.when(k < 2)
        def _():
            f_copy(k + 2)[0].wait_send()

        in_sib.wait()
        in_x.wait()
        in_y.wait()
        sums(3, k, mine, (stage.at[0], stage.at[1], stage.at[2]), middle.at[k % 2])
        go, here = f_copy(k)

        @pl.when(stays(k))
        def _():
            here.start()

        @pl.when(jnp.logical_not(stays(k)))
        def _():
            go.start()

    def vec_copy(i):
        return remote(vec_out, vec_box.at[i], v_s.at[i], v_r.at[i], mates[i])

    def turn(step, carry):
        for i in range(5):

            @pl.when(step == i)
            def _():
                vec_copy(i).start()

        @pl.when(step < 4)
        def _():
            for_sibling(3 - step)
            corner(3 - step)

        @pl.when(jnp.logical_and(step >= 1, step < 5))
        def _():
            sides(4 - step)

        @pl.when(step >= 2)
        def _():
            centre(5 - step)

        for i in range(5):

            @pl.when(step == i)
            def _():
                vec_copy(i).wait()
                vec_out[...] = vec_out[...] + vec_box[i]

        return carry

    lax.fori_loop(0, 6, turn, 0)
    for q in (2, 3):
        sib_copy(q, 0).wait_send()
    for k in (1, 0):
        a_copy(k).wait_send()
        b_copy(k).wait_send()
        x_copy(k).wait_send()
        y_copy(k).wait_send()
    f_copy(1)[0].wait_send()

    @pl.when(rank != core)
    def _():
        f_copy(0)[0].wait_send()

    for plane in range(2):
        for h in range(2):
            piece = final.at[plane, :, pl.ds(h * half, half), :]
            pltpu.make_async_copy(piece, piece, f_r.at[2 * plane + h]).wait()


def reduce_slots(holder, kinds, rows, columns, vector, slot_count):
    if not chip_pairs():
        grads = slot_grads(holder, kinds, rows, columns)
        total = lax.psum_scatter(grads, "dp", scatter_dimension=0, tiled=True)
        return [total], lax.psum(vector, ("dp", "tensor"))
    depth = max(r.shape[0] for r in rows)
    left = [jnp.pad(r, ((0, depth - r.shape[0]), (0, 0))).T for r in rows]
    lanes = columns[0].shape[2]
    tiles = sum(c.shape[0] for c in columns)
    block = jnp.where(holder >= 0, holder, tiles)
    kind = kinds[jnp.maximum(holder, 0)]
    width = rows[0].shape[1]
    half = width // 2
    dma = pltpu.SemaphoreType.DMA
    scalars = pl.BlockSpec(memory_space=pltpu.SMEM)
    inside = pl.BlockSpec(memory_space=pltpu.VMEM)
    low = jnp.bfloat16

    def room(count, tall):
        return jax.ShapeDtypeStruct((count, slot_count, tall, lanes), low)

    def slab(count):
        return pltpu.VMEM((count, slot_count, half, lanes), low)

    outs = pl.pallas_call(
        reduce_kernel,
        out_shape=[
            room(2, width), jax.ShapeDtypeStruct(vector.shape, vector.dtype),
            room(16, half), room(4, half), room(4, half),
            room(4, half // 2), room(4, half // 2),
        ],
        in_specs=[scalars, scalars] + [ANY] * (len(left) + len(columns)) + [inside],
        out_specs=[ANY, inside] + [ANY] * 5,
        scratch_shapes=[
            pltpu.VMEM((len(left), width, depth), low),
            pltpu.VMEM((tiles + 1, depth, lanes), low),
            slab(2), slab(2), slab(2), slab(2), slab(2), slab(3),
            pltpu.VMEM((5,) + vector.shape, vector.dtype),
        ]
        + [dma((n,)) for n in (len(left) + len(columns), 4, 16, 16) + (4,) * 10 + (5, 5)],
        compiler_params=pltpu.CompilerParams(
            collective_id=1, has_side_effects=True, vmem_limit_bytes=58 * MIB
        ),
    )(kind, block, *left, *columns, vector)
    return [outs[0][0], outs[0][1]], outs[1]


def kind_of_blocks(tile_count, heads_here, blocks_here):
    number = jnp.arange(tile_count)
    kind = number // heads_here
    table = jnp.array([0, 0, 0, 1, 2, 3, 3, 4], jnp.int32)
    late = jnp.where(number < 8 * heads_here + blocks_here, 5, 6)
    return jnp.where(number < 8 * heads_here, table[jnp.minimum(kind, 7)], late).astype(jnp.int32)


def slot_grads(holder, kinds, rows, columns):
    depth = max(r.shape[0] for r in rows)

    def deep(value, axis):
        room = [(0, 0)] * value.ndim
        room[axis] = (0, depth - value.shape[axis])
        return jnp.pad(value, room)

    left = jnp.stack([deep(r, 0) for r in rows])
    right = jnp.concatenate([deep(c, 1) for c in columns], 0)
    slots = holder.shape[0]
    used = (holder >= 0).astype(jnp.int32)
    block = jnp.maximum(holder, 0)
    kind = kinds[block]
    width = rows[0].shape[1]
    lanes = right.shape[2]

    def multiply(kind_ref, block_ref, used_ref, left_ref, right_ref, out_ref):
        slot = pl.program_id(0)

        @pl.when(used_ref[slot] == 1)
        def _():
            out_ref[0] = lax.dot_general(
                left_ref[kind_ref[slot]],
                right_ref[0],
                (((0,), (0,)), ((), ())),
                preferred_element_type=jnp.float32,
            ).astype(out_ref.dtype)

        @pl.when(used_ref[slot] == 0)
        def _():
            out_ref[...] = jnp.zeros_like(out_ref)

    return pl.pallas_call(
        multiply,
        grid_spec=pltpu.PrefetchScalarGridSpec(
            num_scalar_prefetch=3,
            grid=(slots,),
            in_specs=[
                pl.BlockSpec(left.shape, lambda s, kd, b, u: (0, 0, 0)),
                pl.BlockSpec((1, depth, lanes), lambda s, kd, b, u: (b[s], 0, 0)),
            ],
            out_specs=pl.BlockSpec((1, width, lanes), lambda s, kd, b, u: (s, 0, 0)),
        ),
        out_shape=jax.ShapeDtypeStruct((slots, width, lanes), jnp.bfloat16),
        compiler_params=pltpu.CompilerParams(vmem_limit_bytes=48 * MIB),
    )(kind, block, used, left, right)


def adam_slots(parts, master, moment_one, moment_two, slot_scale, filled):
    slot_count, width, lanes = master.shape[1:]
    count = len(parts)
    tall = width // 2

    def step(scale_ref, fill_ref, *refs):
        grads = refs[:count]
        weight, one, two, new_weight, new_one, new_two = refs[count:]
        slot = pl.program_id(0)

        @pl.when(fill_ref[slot] == 1)
        def _():
            total = grads[0][0].astype(jnp.float32)
            for more in grads[1:]:
                total = total + more[0].astype(jnp.float32)
            results = adam_step(
                weight[0, 0], total * scale_ref[slot], one[0, 0], two[0, 0], TILE_RATE, TILE_DECAY
            )
            for ref, value in zip((new_weight, new_one, new_two), results):
                ref[0, 0] = value

        @pl.when(fill_ref[slot] == 0)
        def _():
            new_weight[...] = weight[...]
            new_one[...] = one[...]
            new_two[...] = two[...]

    flat = pl.BlockSpec((1, tall, lanes), lambda s, i: (s, i, 0))
    deep = pl.BlockSpec((1, 1, tall, lanes), lambda s, i: (0, s, i, 0))
    scalars = pl.BlockSpec(memory_space=pltpu.SMEM)
    return pl.pallas_call(
        step,
        grid=(slot_count, 2),
        in_specs=[scalars, scalars] + [flat] * count + [deep] * 3,
        out_specs=[deep] * 3,
        out_shape=[jax.ShapeDtypeStruct(master.shape, jnp.float32)] * 3,
    )(slot_scale, filled.astype(jnp.int32), *parts, master, moment_one, moment_two)


SCALING = HEAD ** (-0.5)
BF16 = jnp.bfloat16
F32 = jnp.float32


def nn(left, right):
    return jnp.dot(left, right, preferred_element_type=F32)


def nt(left, right):
    return lax.dot_general(left, right, (((1,), (1,)), ((), ())), preferred_element_type=F32)


def tn(left, right):
    return lax.dot_general(left, right, (((0,), (0,)), ((), ())), preferred_element_type=F32)


def normed(rows):
    centre = rows - jnp.mean(rows, -1, keepdims=True)
    inverse = lax.rsqrt(jnp.mean(centre * centre, -1, keepdims=True) + NORM_EPS)
    return centre * inverse, inverse


def normed_back(rows, grad):
    unit, inverse = normed(rows)
    mean = jnp.mean(grad, -1, keepdims=True)
    return (grad - mean - unit * jnp.mean(grad * unit, -1, keepdims=True)) * inverse, unit


def total_of(rows):
    return jnp.sum(rows, 0, keepdims=True)


def turned(rows, cos_tab, sin_tab):
    even = lax.broadcasted_iota(jnp.int32, rows.shape, 1) % 2 == 0
    partner = jnp.where(even, pltpu.roll(rows, HEAD - 1, 1), pltpu.roll(rows, 1, 1))
    return rows * cos_tab + partner * sin_tab


def wide(column):
    return jnp.broadcast_to(column, (column.shape[0], HEAD))


def pack_sums(for_rows, for_text=None):
    out = wide(for_rows)
    if for_text is None:
        return out
    lane = lax.broadcasted_iota(jnp.int32, out.shape, 1)
    count = for_text.shape[0] // 2
    rest = jnp.zeros((out.shape[0] - count, HEAD), F32)
    first = jnp.concatenate([wide(for_text[:count]), rest], 0)
    second = jnp.concatenate([wide(for_text[count:]), rest], 0)
    return jnp.where(lane < 32, out, jnp.where(lane < 64, first, second))


def unpack_text(sums, count):
    return jnp.concatenate([sums[: count // 2, 32:33], sums[: count // 2, 64:65]], 0)


def softmax(scores):
    expo = jnp.exp(scores - jnp.max(scores, -1, keepdims=True))
    return expo / jnp.sum(expo, -1, keepdims=True)


def self_scores(query_low, key_low, tokens):
    scores = nt(query_low, key_low) * SCALING
    lane = lax.broadcasted_iota(jnp.int32, scores.shape, 1)
    return jnp.where(lane < tokens, scores, -1e30)


def whole(array):
    zeros = (0,) * array.ndim
    return pl.BlockSpec(array.shape, lambda *_: zeros)


def block_at(first, stride=1):
    return pl.BlockSpec((1, D, HEAD), lambda i, where: (where[first + stride * i], 0, 0))


def call(body, places, grid, ins, outs, scratch=(), vmem=40):
    specs = [spec if spec is not None else whole(array) for array, spec in ins]
    shapes = [jax.ShapeDtypeStruct(shape, kind) for shape, kind, _ in outs]
    out_specs = [
        spec if spec is not None else whole(shape) for (_, _, spec), shape in zip(outs, shapes)
    ]
    return pl.pallas_call(
        body,
        grid_spec=pltpu.PrefetchScalarGridSpec(
            num_scalar_prefetch=1,
            grid=(grid,),
            in_specs=specs,
            out_specs=out_specs,
            scratch_shapes=list(scratch),
        ),
        out_shape=shapes,
        compiler_params=pltpu.CompilerParams(vmem_limit_bytes=vmem * MIB),
    )(places, *[array for array, _ in ins])


def head_lanes(rows):
    return pl.BlockSpec((rows, HEAD), lambda h, *_: (0, h))


def joined(refs):
    return jnp.concatenate([ref[0] for ref in refs], 1)


def project_self(places, everyone, rows, mod, vecs, heads):
    count = rows.shape[0]
    span = heads * HEAD

    def body(_, rows_ref, mod_ref, vec_ref, *refs):
        weights, (low, pre, value, sums, acc) = refs[:heads], refs[heads:]
        i = pl.program_id(0)

        @pl.when(i == 0)
        def _():
            unit, _ = normed(rows_ref[...])
            low[...] = (unit * (1.0 + mod_ref[1:2]) + mod_ref[0:1]).astype(BF16)

        made = nn(low[...], joined(weights))

        @pl.when(i == 0)
        def _():
            q = made + vec_ref[0:1]
            pre[0] = q
            acc[...] = wide(jnp.sum(q * q, -1, keepdims=True))

        @pl.when(i == 1)
        def _():
            k = made + vec_ref[1:2]
            pre[0] = k
            lane = lax.broadcasted_iota(jnp.int32, acc.shape, 1)
            sums[...] = jnp.where(lane < 64, acc[...], wide(jnp.sum(k * k, -1, keepdims=True)))

        @pl.when(i == 2)
        def _():
            value[...] = (made + vec_ref[2:3]).astype(BF16)

    return call(
        body, places, 3,
        [(rows, None), (mod, None), (vecs, None)]
        + [(everyone, block_at(h, heads)) for h in range(heads)],
        [
            ((count, D), BF16, None),
            ((2, count, span), F32, pl.BlockSpec((1, count, span), lambda i, _: (jnp.minimum(i, 1), 0, 0))),
            ((count, span), BF16, None),
            ((count, HEAD), F32, None),
        ],
        [pltpu.VMEM((count, HEAD), F32)],
    )


def attend_self(places, everyone, pre, value, sums, other, vecs, cos_tab, sin_tab, heads, tokens):
    count = value.shape[0]

    def body(_, pre_ref, value_ref, sum_ref, other_ref, vec_ref, cos_ref, sin_ref, weight, q_ref, k_ref, o_ref, y_ref, acc):
        h = pl.program_id(0)
        total = sum_ref[...] + other_ref[...]
        q_inv = lax.rsqrt(total[:, 0:1] / D + NORM_EPS)
        k_inv = lax.rsqrt(total[:, 64:65] / D + NORM_EPS)
        cos, sin = cos_ref[...], sin_ref[...]
        q = turned(pre_ref[0] * q_inv * vec_ref[3:4], cos, sin).astype(BF16)
        k = turned(pre_ref[1] * k_inv * vec_ref[4:5], cos, sin).astype(BF16)
        q_ref[...] = q
        k_ref[...] = k
        chance = softmax(self_scores(q, k, tokens))
        out = nn(chance.astype(BF16), value_ref[...]).astype(BF16)
        o_ref[0] = out
        part = nt(out, weight[0])

        @pl.when(h == 0)
        def _():
            acc[...] = part

        @pl.when(h > 0)
        def _():
            acc[...] = acc[...] + part

        @pl.when(h == heads - 1)
        def _():
            y_ref[...] = acc[...].astype(BF16)

    lanes = head_lanes(count)
    return call(
        body, places, heads,
        [
            (pre, pl.BlockSpec((2, count, HEAD), lambda h, _: (0, 0, h))),
            (value, lanes), (sums, None), (other, None),
            (vecs, head_lanes(vecs.shape[0])), (cos_tab, None), (sin_tab, None),
            (everyone, block_at(3 * heads)),
        ],
        [
            (value.shape, BF16, lanes),
            (value.shape, BF16, lanes),
            ((heads, count, HEAD), BF16, pl.BlockSpec((1, count, HEAD), lambda h, _: (h, 0, 0))),
            ((count, D), BF16, None),
        ],
        [pltpu.VMEM((count, D), F32)],
    )


def project_text(places, everyone, context, vecs, heads):
    count = context.shape[0]
    span = heads * HEAD

    def body(_, text_ref, vec_ref, *refs):
        weights, (key, value, sums) = refs[:heads], refs[heads:]
        i = pl.program_id(0)
        made = nn(text_ref[...], joined(weights))

        @pl.when(i == 0)
        def _():
            k = made + vec_ref[6:7]
            key[...] = k
            sums[...] = wide(jnp.sum(k * k, -1, keepdims=True))

        @pl.when(i == 1)
        def _():
            value[...] = (made + vec_ref[7:8]).astype(BF16)

    return call(
        body, places, 2,
        [(context, None), (vecs, None)]
        + [(everyone, block_at(5 * heads + h, heads)) for h in range(heads)],
        [((count, span), F32, None), ((count, span), BF16, None), ((count, HEAD), F32, None)],
    )


def project_cross(places, everyone, rows, part, other, mod, shared, vecs, text_sums, heads):
    count = rows.shape[0]
    span = heads * HEAD
    text = text_sums.shape[0]

    def body(_, rows_ref, part_ref, other_ref, mod_ref, shared_ref, vec_ref, text_ref, *refs):
        weights, (branch, after, low, pre, sums) = refs[:heads], refs[heads:]
        y = part_ref[...].astype(F32) + other_ref[...].astype(F32) + shared_ref[0:1]
        branch[...] = y
        x = rows_ref[...] + mod_ref[2:3] * y
        after[...] = x
        unit, _ = normed(x)
        a = (unit * shared_ref[3:4] + shared_ref[4:5]).astype(BF16)
        low[...] = a
        q = nn(a, joined(weights)) + vec_ref[5:6]
        pre[...] = q
        sums[...] = pack_sums(jnp.sum(q * q, -1, keepdims=True), text_ref[:, 0:1])

    return call(
        body, places, 1,
        [(v, None) for v in (rows, part, other, mod, shared, vecs, text_sums)]
        + [(everyone, block_at(4 * heads + h)) for h in range(heads)],
        [
            ((count, D), F32, None),
            ((count, D), F32, None),
            ((count, D), BF16, None),
            ((count, span), F32, None),
            ((count, HEAD), F32, None),
        ],
    )


def attend_cross(places, everyone, pre, key_pre, value, sums, other, vecs, heads):
    count, text = pre.shape[0], value.shape[0]

    def body(_, pre_ref, key_ref, value_ref, sum_ref, other_ref, vec_ref, weight, q_ref, k_ref, o_ref, y_ref, acc):
        h = pl.program_id(0)
        total = sum_ref[...] + other_ref[...]
        q_inv = lax.rsqrt(total[:, 0:1] / D + NORM_EPS)
        k_inv = lax.rsqrt(unpack_text(total, text) / D + NORM_EPS)
        q = (pre_ref[...] * q_inv * vec_ref[8:9]).astype(BF16)
        k = (key_ref[...] * k_inv * vec_ref[9:10]).astype(BF16)
        q_ref[...] = q
        k_ref[...] = k
        chance = softmax(nt(q, k) * SCALING)
        out = nn(chance.astype(BF16), value_ref[...]).astype(BF16)
        o_ref[0] = out
        part = nt(out, weight[0])

        @pl.when(h == 0)
        def _():
            acc[...] = part

        @pl.when(h > 0)
        def _():
            acc[...] = acc[...] + part

        @pl.when(h == heads - 1)
        def _():
            y_ref[...] = acc[...].astype(BF16)

    return call(
        body, places, heads,
        [
            (pre, head_lanes(count)), (key_pre, head_lanes(text)), (value, head_lanes(text)),
            (sums, None), (other, None), (vecs, head_lanes(vecs.shape[0])),
            (everyone, block_at(7 * heads)),
        ],
        [
            (pre.shape, BF16, head_lanes(count)),
            (value.shape, BF16, head_lanes(text)),
            ((heads, count, HEAD), BF16, pl.BlockSpec((1, count, HEAD), lambda h, _: (h, 0, 0))),
            ((count, D), BF16, None),
        ],
        [pltpu.VMEM((count, D), F32)],
    )


def feed_forward(places, everyone, after_one, part, other, mod, shared, cot, up_bias, heads, blocks):
    count = after_one.shape[0]
    group = max(g for g in (7, 5, 3, 1) if blocks % g == 0 and g <= 5)
    span = group * HEAD

    def body(_, after_ref, part_ref, other_ref, mod_ref, shared_ref, cot_ref, bias_ref, *refs):
        ups, downs = refs[:group], refs[group : 2 * group]
        after, low, grad, hidden, d_hidden, d_bias, y_ref, da_ref, y_acc, da_acc = refs[2 * group :]
        i = pl.program_id(0)

        @pl.when(i == 0)
        def _():
            x = after_ref[...] + part_ref[...].astype(F32) + other_ref[...].astype(F32)
            x = x + shared_ref[1:2]
            after[...] = x
            unit, _ = normed(x)
            low[...] = (unit * (1.0 + mod_ref[4:5]) + mod_ref[3:4]).astype(BF16)
            grad[...] = (mod_ref[5:6] * cot_ref[...]).astype(BF16)
            y_acc[...] = jnp.zeros_like(y_acc)
            da_acc[...] = jnp.zeros_like(da_acc)

        up, down = joined(ups), joined(downs)
        pre = nn(low[...], up) + bias_ref[...]
        square = pre * pre
        bent = jnp.tanh(GELU_COEF * (pre + 0.044715 * pre * square))
        act = (0.5 * pre * (1.0 + bent)).astype(BF16)
        slope = 0.5 * (1.0 + bent) + 0.5 * pre * (1.0 - bent * bent) * (
            GELU_COEF * (1.0 + 3.0 * 0.044715 * square)
        )
        dh = (nn(grad[...], down) * slope).astype(BF16)
        d_bias[...] = total_of(dh.astype(F32))
        for j in range(group):
            hidden[j] = act[:, j * HEAD : (j + 1) * HEAD]
            d_hidden[j] = dh[:, j * HEAD : (j + 1) * HEAD]
        y_acc[...] = y_acc[...] + nt(act, down)
        da_acc[...] = da_acc[...] + nt(dh, up)

        @pl.when(i == blocks // group - 1)
        def _():
            y_ref[...] = y_acc[...].astype(BF16)
            da_ref[...] = da_acc[...].astype(BF16)

    base = 8 * heads
    tall = pl.BlockSpec((group, count, HEAD), lambda i, _: (i, 0, 0))
    flat = pl.BlockSpec((1, span), lambda i, _: (0, i))
    return call(
        body, places, blocks // group,
        [(v, None) for v in (after_one, part, other, mod, shared, cot)]
        + [(up_bias, flat)]
        + [(everyone, block_at(base + j, group)) for j in range(group)]
        + [(everyone, block_at(base + blocks + j, group)) for j in range(group)],
        [
            ((count, D), F32, None),
            ((count, D), BF16, None),
            ((count, D), BF16, None),
            ((blocks, count, HEAD), BF16, tall),
            ((blocks, count, HEAD), BF16, tall),
            (up_bias.shape, F32, flat),
            ((count, D), BF16, None),
            ((count, D), BF16, None),
        ],
        [pltpu.VMEM((count, D), F32), pltpu.VMEM((count, D), F32)],
        vmem=48,
    )


def cross_back(places, everyone, cot, after_two, part, other, mod, query, key, value, pre, key_pre, vecs, heads):
    count, text = query.shape[0], key.shape[0]

    def body(_, cot_ref, after_ref, part_ref, other_ref, mod_ref, q_ref, k_ref, v_ref, pre_ref, key_ref, vec_ref, weight, dx_ref, low_ref, dq_ref, dk_ref, dv_ref, sums, q_acc, k_acc):
        h = pl.program_id(0)

        @pl.when(h == 0)
        def _():
            da = part_ref[...].astype(F32) + other_ref[...].astype(F32)
            back, _ = normed_back(after_ref[...], da * (1.0 + mod_ref[4:5]))
            dx = cot_ref[...] + back
            dx_ref[...] = dx
            low_ref[...] = dx.astype(BF16)
            q_acc[...] = jnp.zeros_like(q_acc)
            k_acc[...] = jnp.zeros_like(k_acc)

        do = nn(low_ref[...], weight[0]).astype(BF16)
        q, k = q_ref[...], k_ref[...]
        chance = softmax(nt(q, k) * SCALING)
        dp = nt(do, v_ref[...])
        ds = (chance * (dp - jnp.sum(chance * dp, -1, keepdims=True))).astype(BF16)
        dv_ref[0] = tn(chance.astype(BF16), do).astype(BF16)
        dq = nn(ds, k) * SCALING
        dk = tn(ds, q) * SCALING
        dq_ref[...] = dq
        dk_ref[...] = dk
        q_acc[...] = q_acc[...] + wide(jnp.sum(pre_ref[...] * vec_ref[8:9] * dq, -1, keepdims=True))
        k_acc[...] = k_acc[...] + wide(jnp.sum(key_ref[...] * vec_ref[9:10] * dk, -1, keepdims=True))

        @pl.when(h == heads - 1)
        def _():
            sums[...] = pack_sums(q_acc[:, 0:1], k_acc[:, 0:1])

    return call(
        body, places, heads,
        [(v, None) for v in (cot, after_two, part, other, mod)]
        + [
            (query, head_lanes(count)), (key, head_lanes(text)), (value, head_lanes(text)),
            (pre, head_lanes(count)), (key_pre, head_lanes(text)),
            (vecs, head_lanes(vecs.shape[0])), (everyone, block_at(7 * heads)),
        ],
        [
            ((count, D), F32, None),
            ((count, D), BF16, None),
            (query.shape, F32, head_lanes(count)),
            (key.shape, F32, head_lanes(text)),
            ((heads, text, HEAD), BF16, pl.BlockSpec((1, text, HEAD), lambda h, _: (h, 0, 0))),
            ((count, HEAD), F32, None),
        ],
        [pltpu.VMEM((count, HEAD), F32), pltpu.VMEM((text, HEAD), F32)],
    )


def norm_grad(pre, inverse, gain, incoming, total):
    grad = inverse * (gain * incoming) - pre * (inverse * inverse * inverse) * (total / D)
    low = grad.astype(BF16)
    return low, total_of(low.astype(F32)), total_of(incoming * pre * inverse)


def cross_back_rows(places, everyone, pre, key_pre, dq, dk, dv, squares, squares_other, sums, sums_other, vecs, heads):
    count, text = pre.shape[0], key_pre.shape[0]

    def body(_, pre_ref, key_ref, dq_ref, dk_ref, dv_ref, sq_ref, sqo_ref, sum_ref, sumo_ref, vec_ref, weight, gq_ref, gk_ref, vec_out, da_ref, acc):
        h = pl.program_id(0)
        squares_all = sq_ref[...] + sqo_ref[...]
        total = sum_ref[...] + sumo_ref[...]
        q_inv = lax.rsqrt(squares_all[:, 0:1] / D + NORM_EPS)
        k_inv = lax.rsqrt(unpack_text(squares_all, text) / D + NORM_EPS)
        low_q, bias_q, gain_q = norm_grad(pre_ref[...], q_inv, vec_ref[8:9], dq_ref[...], total[:, 0:1])
        low_k, bias_k, gain_k = norm_grad(
            key_ref[...], k_inv, vec_ref[9:10], dk_ref[...], unpack_text(total, text)
        )
        gq_ref[0] = low_q
        gk_ref[0] = low_k
        bias_v = total_of(dv_ref[0].astype(F32))
        vec_out[...] = jnp.concatenate(
            [bias_q, bias_k, bias_v, gain_q, gain_k, jnp.zeros((3, HEAD), F32)], 0
        )
        part = nt(low_q, weight[0])

        @pl.when(h == 0)
        def _():
            acc[...] = part

        @pl.when(h > 0)
        def _():
            acc[...] = acc[...] + part

        @pl.when(h == heads - 1)
        def _():
            da_ref[...] = acc[...].astype(BF16)

    tall = pl.BlockSpec((1, count, HEAD), lambda h, _: (h, 0, 0))
    tall_text = pl.BlockSpec((1, text, HEAD), lambda h, _: (h, 0, 0))
    return call(
        body, places, heads,
        [
            (pre, head_lanes(count)), (key_pre, head_lanes(text)), (dq, head_lanes(count)),
            (dk, head_lanes(text)), (dv, tall_text), (squares, None), (squares_other, None),
            (sums, None), (sums_other, None), (vecs, head_lanes(vecs.shape[0])),
            (everyone, block_at(4 * heads)),
        ],
        [
            ((heads, count, HEAD), BF16, tall),
            ((heads, text, HEAD), BF16, tall_text),
            ((8, heads * HEAD), F32, head_lanes(8)),
            ((count, D), BF16, None),
        ],
        [pltpu.VMEM((count, D), F32)],
    )


def self_back(places, everyone, dx_two, after_one, part, other, mod, shared, query, key, value, pre, vecs, cos_tab, sin_tab, heads, tokens):
    count = query.shape[0]

    def body(_, dx_in, after_ref, part_ref, other_ref, mod_ref, shared_ref, q_ref, k_ref, v_ref, pre_ref, vec_ref, cos_ref, sin_ref, weight, dx_ref, low_ref, d_ref, dv_ref, sums, q_acc, k_acc):
        h = pl.program_id(0)

        @pl.when(h == 0)
        def _():
            da = part_ref[...].astype(F32) + other_ref[...].astype(F32)
            back, _ = normed_back(after_ref[...], da * shared_ref[3:4])
            dx = dx_in[...] + back
            dx_ref[...] = dx
            low_ref[...] = (mod_ref[2:3] * dx).astype(BF16)
            q_acc[...] = jnp.zeros_like(q_acc)
            k_acc[...] = jnp.zeros_like(k_acc)

        do = nn(low_ref[...], weight[0]).astype(BF16)
        q, k = q_ref[...], k_ref[...]
        chance = softmax(self_scores(q, k, tokens))
        dp = nt(do, v_ref[...])
        ds = (chance * (dp - jnp.sum(chance * dp, -1, keepdims=True))).astype(BF16)
        dv_ref[0] = tn(chance.astype(BF16), do).astype(BF16)
        cos, sin = cos_ref[...], -sin_ref[...]
        dq = turned(nn(ds, k) * SCALING, cos, sin)
        dk = turned(tn(ds, q) * SCALING, cos, sin)
        d_ref[0] = dq
        d_ref[1] = dk
        q_acc[...] = q_acc[...] + wide(jnp.sum(pre_ref[0] * vec_ref[3:4] * dq, -1, keepdims=True))
        k_acc[...] = k_acc[...] + wide(jnp.sum(pre_ref[1] * vec_ref[4:5] * dk, -1, keepdims=True))

        @pl.when(h == heads - 1)
        def _():
            lane = lax.broadcasted_iota(jnp.int32, q_acc.shape, 1)
            sums[...] = jnp.where(lane < 64, q_acc[...], k_acc[...])

    lanes = head_lanes(count)
    pair = pl.BlockSpec((2, count, HEAD), lambda h, _: (0, 0, h))
    return call(
        body, places, heads,
        [(v, None) for v in (dx_two, after_one, part, other, mod, shared)]
        + [
            (query, lanes), (key, lanes), (value, lanes), (pre, pair),
            (vecs, head_lanes(vecs.shape[0])), (cos_tab, None), (sin_tab, None),
            (everyone, block_at(3 * heads)),
        ],
        [
            ((count, D), F32, None),
            ((count, D), BF16, None),
            (pre.shape, F32, pair),
            ((heads, count, HEAD), BF16, pl.BlockSpec((1, count, HEAD), lambda h, _: (h, 0, 0))),
            ((count, HEAD), F32, None),
        ],
        [pltpu.VMEM((count, HEAD), F32), pltpu.VMEM((count, HEAD), F32)],
    )


def self_back_rows(places, everyone, pre, grads, dv, squares, squares_other, sums, sums_other, vecs, heads):
    count = pre.shape[1]

    def body(_, pre_ref, d_ref, dv_ref, sq_ref, sqo_ref, sum_ref, sumo_ref, vec_ref, wq, wk, wv, gq_ref, gk_ref, vec_out, da_ref, acc):
        h = pl.program_id(0)
        squares_all = sq_ref[...] + sqo_ref[...]
        total = sum_ref[...] + sumo_ref[...]
        lows, biases, gains = [], [], []
        for n in range(2):
            inverse = lax.rsqrt(squares_all[:, 64 * n : 64 * n + 1] / D + NORM_EPS)
            low, bias, gain = norm_grad(
                pre_ref[n], inverse, vec_ref[3 + n : 4 + n], d_ref[n], total[:, 64 * n : 64 * n + 1]
            )
            lows.append(low)
            biases.append(bias)
            gains.append(gain)
        gq_ref[0] = lows[0]
        gk_ref[0] = lows[1]
        dv_low = dv_ref[0]
        bias_v = total_of(dv_low.astype(F32))
        vec_out[...] = jnp.concatenate(
            [biases[0], biases[1], bias_v, gains[0], gains[1], jnp.zeros((3, HEAD), F32)], 0
        )
        part = nt(
            jnp.concatenate([lows[0], lows[1], dv_low], 1),
            jnp.concatenate([wq[0], wk[0], wv[0]], 1),
        )

        @pl.when(h == 0)
        def _():
            acc[...] = part

        @pl.when(h > 0)
        def _():
            acc[...] = acc[...] + part

        @pl.when(h == heads - 1)
        def _():
            da_ref[...] = acc[...].astype(BF16)

    tall = pl.BlockSpec((1, count, HEAD), lambda h, _: (h, 0, 0))
    pair = pl.BlockSpec((2, count, HEAD), lambda h, _: (0, 0, h))
    return call(
        body, places, heads,
        [
            (pre, pair), (grads, pair), (dv, tall), (squares, None), (squares_other, None),
            (sums, None), (sums_other, None), (vecs, head_lanes(vecs.shape[0])),
            (everyone, block_at(0)), (everyone, block_at(heads)), (everyone, block_at(2 * heads)),
        ],
        [
            ((heads, count, HEAD), BF16, tall),
            ((heads, count, HEAD), BF16, tall),
            ((8, heads * HEAD), F32, head_lanes(8)),
            ((count, D), BF16, None),
        ],
        [pltpu.VMEM((count, D), F32)],
    )


def shared_sums(places, rows, after_one, after_two, low_grads, dx_one, branch, cot, das, y_three, shared):
    def body(_, x_ref, x1_ref, x2_ref, dy1, dy2, dy3, dx1_ref, y1_ref, cot_ref, da1, da3, da2, y3, shared_ref, out):
        def half(value):
            return 0.5 * total_of(value)

        out[0:1] = half(dy1[...].astype(F32))
        out[1:2] = half(dy2[...].astype(F32))
        out[2:3] = half(dy3[...].astype(F32))
        part = da3[...].astype(F32)
        out[3:4] = total_of(part * normed(x1_ref[...])[0])
        out[4:5] = total_of(part)
        part = da1[...].astype(F32)
        out[5:6] = total_of(part)
        out[6:7] = total_of(part * normed(x_ref[...])[0])
        out[7:8] = half(dx1_ref[...] * y1_ref[...])
        part = da2[...].astype(F32)
        out[8:9] = total_of(part)
        out[9:10] = total_of(part * normed(x2_ref[...])[0])
        out[10:11] = total_of(cot_ref[...] * (y3[...].astype(F32) + 0.5 * shared_ref[2:3]))

    return call(
        body, places, 1,
        [(v, None) for v in (rows, after_one, after_two, *low_grads, dx_one, branch, cot, *das, y_three, shared)],
        [(shared.shape, F32, None)],
        vmem=48,
    )[0]


def body(
    latents,
    context,
    cotangent,
    positions,
    step_ids,
    owners,
    time_table,
    master,
    first_moment,
    second_moment,
    head_params,
    head_first,
    head_second,
    shared_params,
    shared_first,
    shared_second,
):
    tensors = lax.axis_size("tensor")
    devices = lax.axis_size("dp")
    slot_count = master.shape[1]
    tile_count = owners.shape[0]
    heads_here = HEADS // tensors
    blocks_here = FF // (HEAD * tensors)
    width_here = D // tensors
    places, holder = owner_layout(owners, slot_count, devices)
    scales = tile_scales(tile_count, heads_here, blocks_here)
    my_slots = lax.dynamic_slice_in_dim(holder, lax.axis_index("dp") * slot_count, slot_count)
    rank = pair_rank()
    latents, context, cotangent, positions, step_ids, head_here = home_swap(
        latents, context, cotangent, positions, step_ids, head_params
    )
    filled = my_slots >= 0
    slot_scale = jnp.where(filled, scales[jnp.maximum(my_slots, 0)], 0.0)
    scaled = (master[0] * slot_scale[:, None, None]).astype(jnp.bfloat16)
    everyone = gather_slots(scaled)
    vectors = head_here[0]
    vecs = vectors[: 10 * width_here].reshape(10, width_here)
    up_bias = vectors[10 * width_here :].reshape(1, -1)
    chosen = (step_ids[0] == jnp.arange(TSTEPS)).astype(jnp.float32)
    mod = shared_params[5:11] + jnp.einsum(
        "s,skd->kd", chosen, time_table, precision=lax.Precision.HIGHEST
    )
    half = latents.shape[0]
    tokens = 2 * half
    count = -(-tokens // 16) * 16
    cos_tab, sin_tab = rope_tables(positions, HEAD)
    sin_tab = jnp.where(jnp.arange(HEAD) % 2 == 0, -sin_tab, sin_tab)
    cos_tab, sin_tab = (jnp.pad(t, ((0, count - tokens), (0, 0))) for t in (cos_tab, sin_tab))

    def all_rows(local_rows):
        other = pair_swap(local_rows)
        rows = jnp.where(
            rank == 0,
            jnp.concatenate([local_rows, other], 0),
            jnp.concatenate([other, local_rows], 0),
        )
        return jnp.pad(rows, ((0, count - tokens), (0, 0))).astype(jnp.float32)

    def own_rows(rows):
        return jnp.where(rank == 0, rows[:half], rows[half:tokens])

    def merged_rows(part):
        theirs = pair_swap(jnp.where(rank == 0, part[half:tokens], part[:half]))
        return own_rows(part).astype(jnp.float32) + theirs.astype(jnp.float32)

    rows = all_rows(latents)
    cot = all_rows(cotangent)
    low_one, pre_one, value_one, squares_one = project_self(
        places, everyone, rows, mod, vecs, heads_here
    )
    squares_one_other = pair_swap(squares_one)
    key_pre, value_two, text_squares = project_text(places, everyone, context, vecs, heads_here)
    query_one, key_one, heads_one, part_one = attend_self(
        places, everyone, pre_one, value_one, squares_one, squares_one_other, vecs, cos_tab,
        sin_tab, heads_here, tokens,
    )
    branch_one, after_one, low_two, pre_two, squares_two = project_cross(
        places, everyone, rows, part_one, pair_swap(part_one), mod, shared_params, vecs,
        text_squares, heads_here,
    )
    squares_two_other = pair_swap(squares_two)
    query_two, key_two, heads_two, part_two = attend_cross(
        places, everyone, pre_two, key_pre, value_two, squares_two, squares_two_other, vecs,
        heads_here,
    )
    after_two, low_three, grad_three, hidden, d_hidden, d_up_bias, y_three, da_two = feed_forward(
        places, everyone, after_one, part_two, pair_swap(part_two), mod, shared_params, cot,
        up_bias, heads_here, blocks_here,
    )
    dx_two, grad_two, dq_two, dk_two, dv_two, sums_two = cross_back(
        places, everyone, cot, after_two, da_two, pair_swap(da_two), mod, query_two, key_two,
        value_two, pre_two, key_pre, vecs, heads_here,
    )
    query_grad_two, key_grad_two, vecs_two, da_three = cross_back_rows(
        places, everyone, pre_two, key_pre, dq_two, dk_two, dv_two, squares_two,
        squares_two_other, sums_two, pair_swap(sums_two), vecs, heads_here,
    )
    dx_one, grad_one, d_one, dv_one, sums_one = self_back(
        places, everyone, dx_two, after_one, da_three, pair_swap(da_three), mod, shared_params,
        query_one, key_one, value_one, pre_one, vecs, cos_tab, sin_tab, heads_here, tokens,
    )
    query_grad_one, key_grad_one, vecs_one, da_one = self_back_rows(
        places, everyone, pre_one, d_one, dv_one, squares_one, squares_one_other, sums_one,
        pair_swap(sums_one), vecs, heads_here,
    )
    shared_grad = shared_sums(
        places, rows, after_one, after_two, (grad_one, grad_two, grad_three), dx_one,
        branch_one, cot, (da_one, da_three, da_two), y_three, shared_params,
    )
    result = own_rows(after_two) + mod[5] * (merged_rows(y_three) + shared_params[2])
    output = result.astype(jnp.bfloat16)
    back, _ = normed_back(own_rows(rows), merged_rows(da_one) * (1.0 + mod[1]))
    grad_input = own_rows(dx_one) + back
    head_grad = jnp.concatenate(
        [vecs_one[:5].reshape(-1), vecs_two[:5].reshape(-1), d_up_bias.reshape(-1)]
    )
    tensor_rank = lax.axis_index("tensor")
    head_padded = jnp.where(jnp.arange(tensors)[:, None] == rank, head_grad[None, :], 0.0)
    vector = jnp.concatenate([head_padded.reshape(-1), shared_grad.reshape(-1)])
    vector = jnp.pad(vector, (0, -vector.shape[0] % 1024)).reshape(-1, 128)
    parts, vector = reduce_slots(
        holder,
        kind_of_blocks(tile_count, heads_here, blocks_here),
        (low_one, grad_one, low_two, context, grad_two, low_three, grad_three),
        (
            query_grad_one,
            key_grad_one,
            dv_one,
            heads_one,
            query_grad_two,
            key_grad_two,
            dv_two,
            heads_two,
            d_hidden,
            hidden,
        ),
        vector,
        slot_count,
    )
    new_master, new_first, new_second = adam_slots(
        parts, master, first_moment, second_moment, slot_scale, filled
    )
    vector = vector.reshape(-1)
    head_total = vector[: head_padded.size].reshape(head_padded.shape)
    shared_total = vector[head_padded.size : head_padded.size + shared_grad.size]
    shared_total = shared_total.reshape(shared_grad.shape)
    mine_head = lax.dynamic_slice_in_dim(head_total, tensor_rank, 1, 0)
    new_head, new_head_first, new_head_second = adam_step(
        head_params, mine_head, head_first, head_second, VECTOR_RATE, 0.0
    )
    new_shared, new_shared_first, new_shared_second = adam_step(
        shared_params, shared_total, shared_first, shared_second, VECTOR_RATE, 0.0
    )
    output, grad_input = home_swap(output, grad_input)
    return (
        output,
        grad_input,
        new_master,
        new_first,
        new_second,
        new_head,
        new_head_first,
        new_head_second,
        new_shared,
        new_shared_first,
        new_shared_second,
    )


def solution(mesh):
    return jax.shard_map(
        body,
        mesh=mesh,
        in_specs=(
            P(("dp", "tensor"), None),
            P("dp", None),
            P(("dp", "tensor"), None),
            P(None, "dp"),
            P("dp"),
            P(),
            P(),
            P("tensor", "dp", None, None),
            P("tensor", "dp", None, None),
            P("tensor", "dp", None, None),
            P("tensor", None),
            P("tensor", None),
            P("tensor", None),
            P(),
            P(),
            P(),
        ),
        out_specs=(
            P(("dp", "tensor"), None),
            P(("dp", "tensor"), None),
            P("tensor", "dp", None, None),
            P("tensor", "dp", None, None),
            P("tensor", "dp", None, None),
            P("tensor", None),
            P("tensor", None),
            P("tensor", None),
            P(),
            P(),
            P(),
        ),
        check_vma=False,
    )
```

```python
import functools

import jax
import jax.numpy as jnp
from jax import lax
from jax.experimental import pallas as pl
from jax.experimental.pallas import tpu as pltpu
from jax.sharding import PartitionSpec as P

D = 1536
HEADS = 12
HEAD = 128
FF = 8960
TSTEPS = 16
STEPC = 10


NORM_EPS = 1e-06
BETA_ONE = 0.9
BETA_TWO = 0.999
ADAM_EPS = 1e-08
TILE_RATE = 1.0
TILE_DECAY = 0.1
VECTOR_RATE = 0.5
GELU_COEF = 0.7978845608028654


def rope_tables(token_places, head_size):
    sixths = head_size // 6
    frame_pairs = (head_size - 4 * sixths) // 2
    frame_freq = 10000.0 ** (-jnp.arange(frame_pairs, dtype=jnp.float32) / frame_pairs)
    side_freq = 10000.0 ** (-jnp.arange(sixths, dtype=jnp.float32) / sixths)
    spots = token_places.astype(jnp.float32)
    angles = jnp.concatenate(
        [
            spots[0][..., None] * frame_freq,
            spots[1][..., None] * side_freq,
            spots[2][..., None] * side_freq,
        ],
        -1,
    )
    angles = jnp.repeat(angles, 2, axis=-1)
    return (jnp.cos(angles), jnp.sin(angles))


def owner_layout(owners, slot_count, devices):
    indices = jnp.arange(owners.shape[0], dtype=jnp.int32)
    same_owner = (owners[:, None] == owners[None, :]) & (indices[None, :] < indices[:, None])
    slot_of = jnp.sum(same_owner.astype(jnp.int32), axis=1)
    places = owners * slot_count + slot_of
    spots = jnp.arange(slot_count * devices, dtype=jnp.int32)
    holder = (
        jnp.sum(jnp.where(places[None, :] == spots[:, None], indices[None, :] + 1, 0), axis=1) - 1
    )
    return (places, holder)


def tile_scales(tile_count, heads_here, blocks_here):
    indices = jnp.arange(tile_count)
    scale_in = D ** (-0.5)
    scale_out = HEADS ** (-0.5)
    scale_down = FF ** (-0.5)
    scales = jnp.where(
        indices < 3 * heads_here,
        scale_in,
        jnp.where(
            indices < 4 * heads_here,
            scale_out,
            jnp.where(
                indices < 7 * heads_here,
                scale_in,
                jnp.where(
                    indices < 8 * heads_here,
                    scale_out,
                    jnp.where(indices < 8 * heads_here + blocks_here, scale_in, scale_down),
                ),
            ),
        ),
    )
    return scales.astype(jnp.float32)


def adam_step(weight, gradient, moment_one, moment_two, step_rate, decay_rate):
    first_new = BETA_ONE * moment_one + (1.0 - BETA_ONE) * gradient
    second_new = BETA_TWO * moment_two + (1.0 - BETA_TWO) * gradient * gradient
    first_hat = first_new / (1.0 - BETA_ONE**STEPC)
    second_hat = second_new / (1.0 - BETA_TWO**STEPC)
    weight_new = weight - step_rate * (
        first_hat / (jnp.sqrt(second_hat) + ADAM_EPS) + decay_rate * weight
    )
    return (weight_new, first_new, second_new)


MESH = pl.DeviceIdType.MESH
ANY = pl.BlockSpec(memory_space=pl.ANY)
MIB = 1 << 20


def chip_pairs():
    return lax.axis_size("dp") == 16 and lax.axis_size("tensor") == 2


def pair_rank():
    if chip_pairs():
        return (lax.axis_index("dp") // 4) % 2
    return lax.axis_index("tensor")


def pair_swap(value):
    if chip_pairs():
        return lax.ppermute(value, "dp", [(i, i ^ 4) for i in range(16)])
    return lax.ppermute(value, "tensor", [(0, 1), (1, 0)])


def pair_sums(*values):
    stacked = jnp.concatenate([v.reshape(-1) for v in values])
    total = stacked + pair_swap(stacked)
    out, at = [], 0
    for v in values:
        out.append(total[at : at + v.size].reshape(v.shape))
        at += v.size
    return tuple(out)


def place_of():
    chip, core = lax.axis_index("dp"), lax.axis_index("tensor")
    z, y, x = chip // 4, (chip // 2) % 2, chip % 2
    return chip, core, z, y, x


def column_of(z, y, x, k):
    high, low_bit = z // 2, z % 2
    if k & 2:
        high = 1 - high
    if k & 1:
        low_bit = 1 - low_bit
    return (2 * high + low_bit) * 4 + 2 * y + x


def greet(chip, core, z, y, x):
    barrier = pltpu.get_barrier_semaphore()
    friends = []
    for k in range(4):
        for flip in (0, 1):
            if k or flip:
                friends.append((column_of(z, y, x, k), core if flip == 0 else 1 - core))
    friends.append((column_of(z, y, 1 - x, 0), core))
    friends.append((column_of(z, 1 - y, x, 0), core))
    for friend in friends:
        pl.semaphore_signal(barrier, inc=1, device_id=friend, device_id_type=MESH)
    pl.semaphore_wait(barrier, len(friends))


def gather_kernel(
    own, lat, cot, text, small, out, lats, cots, texts, smalls, clip_s, clip_r,
    near_s, col_r,
    x_s, x_r, y_s, y_r, ra_s, ra_r, rb_s, rb_r, sib_s, sib_r,
):
    chip, core, z, y, x = place_of()
    rank = z % 2
    half = own.shape[1] // 2
    part = half // 2
    at_x = column_of(z, y, 1 - x, 0)
    at_y = column_of(z, 1 - y, x, 0)
    greet(chip, core, z, y, x)

    def rows(ref, unit, first, count):
        return ref.at[unit, :, pl.ds(pl.multiple_of(first, 16), count), :]

    def remote(unit, first, count, send, recv, device):
        piece = rows(out, unit, first, count)
        return pltpu.make_async_remote_copy(
            src_ref=piece, dst_ref=piece, send_sem=send, recv_sem=recv,
            device_id=device, device_id_type=MESH,
        )

    started = []
    for j in range(2):
        zh = z // 2 if j == 0 else 1 - z // 2
        target = (2 * zh + core) * 4 + 2 * y + x
        for h in range(2):
            src = own.at[:, pl.ds(h * half, half), :]
            dst = out.at[chip, :, pl.ds(h * half, half), :]
            go = pltpu.make_async_remote_copy(
                src_ref=src, dst_ref=dst, send_sem=near_s.at[2 * j + h], recv_sem=col_r.at[z],
                device_id=(target, h), device_id_type=MESH,
            )
            if j == 0:
                here = pltpu.make_async_copy(src, dst, col_r.at[z])
                stays = jnp.logical_and(rank == core, core == h)

                @pl.when(stays)
                def _():
                    here.start()

                @pl.when(jnp.logical_not(stays))
                def _():
                    go.start()

                started.append((go, stays))
            else:
                go.start()
                started.append((go, None))

    pair_chip = column_of(z, y, x, 1)
    rows_of_text = text.shape[0] // 2

    def clip_pieces(h):
        share = pl.ds(h * rows_of_text, rows_of_text)
        return ((lat, lats.at[h]), (cot, cots.at[h]), (text.at[share], texts.at[share]))

    home = rank == core
    trade = pltpu.make_async_remote_copy(
        src_ref=small, dst_ref=smalls, send_sem=clip_s.at[6], recv_sem=clip_r.at[6],
        device_id=(pair_chip, 1 - core), device_id_type=MESH,
    )
    keep = pltpu.make_async_copy(small, smalls, clip_r.at[6])

    @pl.when(home)
    def _():
        keep.start()

    @pl.when(jnp.logical_not(home))
    def _():
        trade.start()

    def hand_out(h, n, wait):
        src, dst = clip_pieces(h)[n]
        far = pltpu.make_async_remote_copy(
            src_ref=src, dst_ref=dst, send_sem=clip_s.at[n], recv_sem=clip_r.at[3 * h + n],
            device_id=(pair_chip, rank), device_id_type=MESH,
        )
        near = pltpu.make_async_remote_copy(
            src_ref=src, dst_ref=dst, send_sem=clip_s.at[3 + n], recv_sem=clip_r.at[3 * h + n],
            device_id=(chip, 1 - core), device_id_type=MESH,
        )
        here = pltpu.make_async_copy(src, dst, clip_r.at[3 * h + n])

        @pl.when(core == h)
        def _():
            if wait:
                far.wait_send()
            else:
                far.start()

            @pl.when(home)
            def _():
                if not wait:
                    here.start()

            @pl.when(jnp.logical_not(home))
            def _():
                if wait:
                    near.wait_send()
                else:
                    near.start()

    for n in range(3):
        for h in range(2):
            hand_out(h, n, False)

    def column_in(k):
        unit = column_of(z, y, x, k)
        source_z = unit // 4
        piece = rows(out, unit, core * half, half)
        pltpu.make_async_copy(piece, piece, col_r.at[source_z]).wait()
        to_x = remote(unit, core * half, half, x_s.at[k], x_r.at[k], (at_x, core))
        to_y = remote(unit, core * half, half, y_s.at[k], y_r.at[k], (at_y, core))
        to_sib = remote(unit, core * half, half, sib_s.at[k], sib_r.at[k], (chip, 1 - core))
        to_x.start()
        to_y.start()
        to_sib.start()
        return [to_x, to_y, to_sib]

    def side_in(k):
        ux = column_of(z, y, 1 - x, k)
        uy = column_of(z, 1 - y, x, k)
        remote(ux, core * half, half, x_s.at[k], x_r.at[k], (at_x, core)).wait_recv()
        on_y = remote(ux, core * half + part, part, rb_s.at[k], rb_r.at[k], (at_y, core))
        on_y.start()
        sib_x = remote(ux, core * half, half, sib_s.at[4 + k], sib_r.at[4 + k], (chip, 1 - core))
        sib_x.start()
        remote(uy, core * half, half, y_s.at[k], y_r.at[k], (at_y, core)).wait_recv()
        on_x = remote(uy, core * half, part, ra_s.at[k], ra_r.at[k], (at_x, core))
        on_x.start()
        sib_y = remote(uy, core * half, half, sib_s.at[8 + k], sib_r.at[8 + k], (chip, 1 - core))
        sib_y.start()
        return [on_y, sib_x, on_x, sib_y]

    def corner_in(k):
        unit = column_of(z, 1 - y, 1 - x, k)
        remote(unit, core * half, part, ra_s.at[k], ra_r.at[k], (at_x, core)).wait_recv()
        sib_a = remote(unit, core * half, part, sib_s.at[12 + k], sib_r.at[12 + k], (chip, 1 - core))
        sib_a.start()
        remote(unit, core * half + part, part, rb_s.at[k], rb_r.at[k], (at_y, core)).wait_recv()
        sib_b = remote(
            unit, core * half + part, part, sib_s.at[16 + k], sib_r.at[16 + k], (chip, 1 - core)
        )
        sib_b.start()
        return [sib_a, sib_b]

    sent = []
    for step in range(6):
        if step < 4:
            sent += column_in(step)
        if 1 <= step < 5:
            sent += side_in(step - 1)
        if step >= 2:
            sent += corner_in(step - 2)
    for copy in sent:
        copy.wait_send()
    for go, stays in started:
        if stays is None:
            go.wait_send()
        else:

            @pl.when(jnp.logical_not(stays))
            def _():
                go.wait_send()

    for n in range(3):
        for h in range(2):
            hand_out(h, n, True)
            dst = clip_pieces(h)[n][1]
            pltpu.make_async_copy(dst, dst, clip_r.at[3 * h + n]).wait()

    @pl.when(jnp.logical_not(home))
    def _():
        trade.wait_send()

    pltpu.make_async_copy(smalls, smalls, clip_r.at[6]).wait()

    other = (1 - core) * half
    for k in range(4):
        for at, (yy, xx) in ((0, (y, x)), (4, (y, 1 - x)), (8, (1 - y, x))):
            remote(
                column_of(z, yy, xx, k), other, half, sib_s.at[at + k], sib_r.at[at + k],
                (chip, 1 - core),
            ).wait_recv()
        corner = column_of(z, 1 - y, 1 - x, k)
        remote(
            corner, other, part, sib_s.at[12 + k], sib_r.at[12 + k], (chip, 1 - core)
        ).wait_recv()
        remote(
            corner, other + part, part, sib_s.at[16 + k], sib_r.at[16 + k], (chip, 1 - core)
        ).wait_recv()


def gather_slots(scaled, lat, cot, text, small):
    if not chip_pairs():
        everyone = lax.all_gather(scaled, "dp", axis=0, tiled=True)
        lats, cots = (lax.all_gather(v, "tensor") for v in (lat, cot))
        return everyone, lats, cots, text, small
    dma = pltpu.SemaphoreType.DMA
    counts = (7, 7, 4, 4, 4, 4, 4, 4, 4, 4, 4, 4, 20, 20)
    everyone, *rest = pl.pallas_call(
        gather_kernel,
        out_shape=[
            jax.ShapeDtypeStruct((16,) + scaled.shape, scaled.dtype),
            jax.ShapeDtypeStruct((2,) + lat.shape, lat.dtype),
            jax.ShapeDtypeStruct((2,) + cot.shape, cot.dtype),
            jax.ShapeDtypeStruct(text.shape, text.dtype),
            jax.ShapeDtypeStruct(small.shape, small.dtype),
        ],
        in_specs=[ANY] * 5,
        out_specs=[ANY] * 5,
        scratch_shapes=[dma((n,)) for n in counts],
        compiler_params=pltpu.CompilerParams(
            collective_id=0, has_side_effects=True, vmem_limit_bytes=4 * MIB
        ),
    )(scaled, lat, cot, text, small)
    return everyone.reshape((-1,) + scaled.shape[1:]), *rest


def toggled(z, y, x, flip_y, flip_x, k):
    high = (z // 2 + k // 2) % 2
    low_bit = (z % 2 + k % 2) % 2
    return (2 * high + low_bit) * 4 + 2 * ((y + flip_y) % 2) + (x + flip_x) % 2


def reduce_kernel(
    kind, block, *refs,
):
    (
        *pieces, rows_in, after_in, dx_in, y_in, da_in, gains, vec_in,
        final, vec_out, result, result_grad, y_other, da_other, from_sib, from_x, from_y, corner_a, corner_b,
        left, right, ring, corners, side_x, side_y, middle, stage, vec_box,
        load_s, stage_s, sib_s, sib_r, x_s, x_r, y_s, y_r, ca_s, ca_r, cb_s, cb_r, f_s, f_r, v_s, v_r,
        end_s, end_r,
    ) = refs
    chip, core, z, y, x = place_of()
    rank = z % 2
    slots, width, lanes = final.shape[1:]
    half = width // 2
    part = half // 2
    at_x = toggled(z, y, x, 0, 1, 0)
    at_y = toggled(z, y, x, 1, 0, 0)
    sibling = (chip, 1 - core)
    mates = (
        sibling,
        (at_x, core),
        (at_y, core),
        (toggled(z, y, x, 0, 0, 1), core),
        (toggled(z, y, x, 0, 0, 2), core),
    )

    kinds = left.shape[0]
    depth = right.shape[1]
    loads = [
        pltpu.make_async_copy(pieces[i], left.at[i], load_s.at[i]) for i in range(kinds)
    ]
    first = 0
    blank = []
    for i, piece in enumerate(pieces[kinds:]):
        number, rows = piece.shape[:2]
        loads.append(
            pltpu.make_async_copy(
                piece, right.at[pl.ds(first, number), pl.ds(0, rows), :], load_s.at[kinds + i]
            )
        )
        if rows < depth:
            blank.append((first, number, rows))
        first += number
    for load in loads:
        load.start()
    for start, number, rows in blank:

        def clear(i, carry):
            right[start + i, pl.ds(rows, depth - rows), :] = jnp.zeros(
                (depth - rows, lanes), right.dtype
            )
            return carry

        lax.fori_loop(0, number, clear, 0)
    right[first] = jnp.zeros((depth, lanes), right.dtype)
    vec_out[...] = vec_in[...]
    greet(chip, core, z, y, x)
    for load in loads:
        load.wait()

    def remote(src, dst, send, recv, device):
        return pltpu.make_async_remote_copy(
            src_ref=src, dst_ref=dst, send_sem=send, recv_sem=recv,
            device_id=device, device_id_type=MESH,
        )

    def unit_of(q, k):
        return toggled(z, y, x, 1 - q % 2, 1 - q // 2, k)

    def sums(q, k, first, terms, total):
        base = unit_of(q, k) * slots
        count = total.shape[1]

        def one(i, carry):
            slot = base + i
            rows = pl.ds(pl.multiple_of(first, 128), count)
            acc = jnp.dot(
                left[kind[slot], rows, :], right[block[slot]], preferred_element_type=jnp.float32
            )
            for term in terms:
                acc = acc + term[i].astype(jnp.float32)
            total[i] = acc.astype(total.dtype)
            return carry

        lax.fori_loop(0, slots, one, 0)

    mine, other = core * half, (1 - core) * half

    def sub(ref, first):
        return ref.at[:, pl.ds(first, part), :]

    def sib_copy(q, k):
        i = 4 * q + k
        return remote(ring.at[q % 2], from_sib.at[i], sib_s.at[i], sib_r.at[i], sibling)

    def a_copy(k):
        return remote(
            sub(corners.at[k % 2], 0), corner_a.at[k], ca_s.at[k], ca_r.at[k], (at_x, core)
        )

    def b_copy(k):
        return remote(
            sub(corners.at[k % 2], part), corner_b.at[k], cb_s.at[k], cb_r.at[k], (at_y, core)
        )

    def x_copy(k):
        return remote(side_x.at[k % 2], from_x.at[k], x_s.at[k], x_r.at[k], (at_x, core))

    def y_copy(k):
        return remote(side_y.at[k % 2], from_y.at[k], y_s.at[k], y_r.at[k], (at_y, core))

    def f_copy(k):
        src = middle.at[k % 2]
        dst = final.at[z // 2, :, pl.ds(pl.multiple_of(mine, 128), half), :]
        recv = f_r.at[2 * (z // 2) + core]
        return remote(
            src, dst, f_s.at[k], recv, (toggled(z, y, x, 0, 0, k), rank)
        ), pltpu.make_async_copy(src, dst, recv)

    def stays(k):
        return jnp.logical_and(k == 0, rank == core)

    def staged(source, place, i):
        copy = pltpu.make_async_copy(source, place, stage_s.at[i])
        copy.start()
        return copy

    def for_sibling(k):
        def one(q, carry):
            @pl.when(jnp.logical_or(q >= 2, k < 3))
            def _():
                back = jnp.where(q >= 2, k, k + 1)
                sib_copy((q + 2) % 4, back).wait_send()

            sums(q, k, other, (), ring.at[q % 2])
            sib_copy(q, k).start()
            return carry

        lax.fori_loop(0, 4, one, 0)

    def corner(k):
        sib_copy(0, k).wait_recv()
        staged(from_sib.at[k], stage.at[0], 0).wait()

        @pl.when(k < 2)
        def _():
            a_copy(k + 2).wait_send()
            b_copy(k + 2).wait_send()

        sums(0, k, mine, (stage.at[0],), corners.at[k % 2])
        a_copy(k).start()
        b_copy(k).start()

    def sides(k):
        sib_copy(1, k).wait_recv()
        sib_copy(2, k).wait_recv()
        in_x = staged(from_sib.at[4 + k], stage.at[0], 0)
        in_y = staged(from_sib.at[8 + k], stage.at[1], 1)

        @pl.when(k < 2)
        def _():
            x_copy(k + 2).wait_send()
            y_copy(k + 2).wait_send()

        in_x.wait()
        sums(1, k, mine, (sub(stage.at[0], 0),), sub(side_x.at[k % 2], 0))
        b_copy(k).wait_recv()
        in_b = staged(corner_b.at[k], sub(stage.at[2], 0), 2)
        in_y.wait()
        sums(2, k, mine + part, (sub(stage.at[1], part),), sub(side_y.at[k % 2], part))
        in_b.wait()
        a_copy(k).wait_recv()
        in_a = staged(corner_a.at[k], sub(stage.at[2], part), 3)
        sums(
            1, k, mine + part, (sub(stage.at[0], part), sub(stage.at[2], 0)),
            sub(side_x.at[k % 2], part),
        )
        x_copy(k).start()
        in_a.wait()
        sums(2, k, mine, (sub(stage.at[1], 0), sub(stage.at[2], part)), sub(side_y.at[k % 2], 0))
        y_copy(k).start()

    def centre(k):
        sib_copy(3, k).wait_recv()
        in_sib = staged(from_sib.at[12 + k], stage.at[0], 0)
        x_copy(k).wait_recv()
        in_x = staged(from_x.at[k], stage.at[1], 1)
        y_copy(k).wait_recv()
        in_y = staged(from_y.at[k], stage.at[2], 2)

        @pl.when(k < 2)
        def _():
            f_copy(k + 2)[0].wait_send()

        in_sib.wait()
        in_x.wait()
        in_y.wait()
        sums(3, k, mine, (stage.at[0], stage.at[1], stage.at[2]), middle.at[k % 2])
        go, here = f_copy(k)

        @pl.when(stays(k))
        def _():
            here.start()

        @pl.when(jnp.logical_not(stays(k)))
        def _():
            go.start()

    home = rank == core
    pair_device = (toggled(z, y, x, 0, 0, 1), core)
    ends = [
        remote(y_in, y_other, end_s.at[0], end_r.at[0], pair_device),
        remote(da_in, da_other, end_s.at[1], end_r.at[1], pair_device),
        remote(result, result, end_s.at[2], end_r.at[2], sibling),
        remote(result_grad, result_grad, end_s.at[3], end_r.at[3], sibling),
    ]

    def finish_rows():
        ends[0].wait_recv()
        ends[1].wait_recv()
        tall = 16
        spec = pl.BlockSpec((tall, width), lambda i: (i, 0))

        def one(x_ref, x2_ref, dx_ref, y_ref, yo_ref, da_ref, dao_ref, out_ref, grad_ref):
            y_all = y_ref[...].astype(F32) + yo_ref[...].astype(F32) + gains[2:3]
            out_ref[...] = (x2_ref[...] + gains[0:1] * y_all).astype(out_ref.dtype)
            da = da_ref[...].astype(F32) + dao_ref[...].astype(F32)
            back, _ = normed_back(x_ref[...], da * (1.0 + gains[1:2]))
            grad_ref[...] = dx_ref[...] + back

        pltpu.emit_pipeline(
            one, grid=(rows_in.shape[0] // tall,), in_specs=[spec] * 7, out_specs=[spec] * 2
        )(rows_in, after_in, dx_in, y_in, y_other, da_in, da_other, result, result_grad)
        ends[2].start()
        ends[3].start()

    @pl.when(jnp.logical_not(home))
    def _():
        ends[0].start()
        ends[1].start()

    def vec_copy(i):
        return remote(vec_out, vec_box.at[i], v_s.at[i], v_r.at[i], mates[i])

    def turn(step, carry):
        for i in range(5):

            @pl.when(step == i)
            def _():
                vec_copy(i).start()

        @pl.when(step < 4)
        def _():
            for_sibling(3 - step)
            corner(3 - step)

        @pl.when(jnp.logical_and(step >= 1, step < 5))
        def _():
            sides(4 - step)

        @pl.when(jnp.logical_and(step == 4, home))
        def _():
            finish_rows()

        @pl.when(step >= 2)
        def _():
            centre(5 - step)

        for i in range(5):

            @pl.when(step == i)
            def _():
                vec_copy(i).wait()
                vec_out[...] = vec_out[...] + vec_box[i]

        return carry

    lax.fori_loop(0, 6, turn, 0)
    for q in (2, 3):
        sib_copy(q, 0).wait_send()
    for k in (1, 0):
        a_copy(k).wait_send()
        b_copy(k).wait_send()
        x_copy(k).wait_send()
        y_copy(k).wait_send()
    f_copy(1)[0].wait_send()

    @pl.when(home)
    def _():
        ends[2].wait_send()
        ends[3].wait_send()

    @pl.when(jnp.logical_not(home))
    def _():
        f_copy(0)[0].wait_send()
        ends[0].wait_send()
        ends[1].wait_send()
        ends[2].wait_recv()
        ends[3].wait_recv()

    for plane in range(2):
        for h in range(2):
            piece = final.at[plane, :, pl.ds(h * half, half), :]
            pltpu.make_async_copy(piece, piece, f_r.at[2 * plane + h]).wait()


def reduce_slots(holder, kinds, rows, columns, vector, ends, gains, slot_count):
    if not chip_pairs():
        grads = slot_grads(holder, kinds, rows, columns)
        total = lax.psum_scatter(grads, "dp", scatter_dimension=0, tiled=True)
        x, after, dx, y_part, da_part = ends
        y_all, da_all = (
            v.astype(F32) + pair_swap(v).astype(F32) for v in (y_part, da_part)
        )
        result = (after + gains[0] * (y_all + gains[2])).astype(BF16)
        back, _ = normed_back(x, da_all * (1.0 + gains[1]))
        return total[None], lax.psum(vector, ("dp", "tensor")), result, dx + back
    depth = max(r.shape[0] for r in rows)
    left = [jnp.pad(r, ((0, depth - r.shape[0]), (0, 0))).T for r in rows]
    lanes = columns[0].shape[2]
    tiles = sum(c.shape[0] for c in columns)
    block = jnp.where(holder >= 0, holder, tiles)
    kind = kinds[jnp.maximum(holder, 0)]
    width = rows[0].shape[1]
    half = width // 2
    dma = pltpu.SemaphoreType.DMA
    scalars = pl.BlockSpec(memory_space=pltpu.SMEM)
    inside = pl.BlockSpec(memory_space=pltpu.VMEM)
    low = jnp.bfloat16

    def room(count, tall):
        return jax.ShapeDtypeStruct((count, slot_count, tall, lanes), low)

    def slab(count):
        return pltpu.VMEM((count, slot_count, half, lanes), low)

    outs = pl.pallas_call(
        reduce_kernel,
        out_shape=[
            room(2, width), jax.ShapeDtypeStruct(vector.shape, vector.dtype),
            jax.ShapeDtypeStruct(ends[0].shape, low), jax.ShapeDtypeStruct(ends[0].shape, F32),
            jax.ShapeDtypeStruct(ends[0].shape, low), jax.ShapeDtypeStruct(ends[0].shape, low),
            room(16, half), room(4, half), room(4, half),
            room(4, half // 2), room(4, half // 2),
        ],
        in_specs=[scalars, scalars] + [ANY] * (len(left) + len(columns) + 5) + [inside] * 2,
        out_specs=[ANY, inside] + [ANY] * 9,
        scratch_shapes=[
            pltpu.VMEM((len(left), width, depth), low),
            pltpu.VMEM((tiles + 1, depth, lanes), low),
            slab(2), slab(2), slab(2), slab(2), slab(2), slab(3),
            pltpu.VMEM((5,) + vector.shape, vector.dtype),
        ]
        + [dma((n,)) for n in (len(left) + len(columns), 4, 16, 16) + (4,) * 10 + (5, 5, 4, 4)],
        compiler_params=pltpu.CompilerParams(
            collective_id=1, has_side_effects=True, vmem_limit_bytes=58 * MIB
        ),
    )(kind, block, *left, *columns, *ends, gains, vector)
    return outs[:4]


def kind_of_blocks(tile_count, heads_here, blocks_here):
    number = jnp.arange(tile_count)
    kind = number // heads_here
    table = jnp.array([0, 0, 0, 1, 2, 3, 3, 4], jnp.int32)
    late = jnp.where(number < 8 * heads_here + blocks_here, 5, 6)
    return jnp.where(number < 8 * heads_here, table[jnp.minimum(kind, 7)], late).astype(jnp.int32)


def slot_grads(holder, kinds, rows, columns):
    depth = max(r.shape[0] for r in rows)

    def deep(value, axis):
        room = [(0, 0)] * value.ndim
        room[axis] = (0, depth - value.shape[axis])
        return jnp.pad(value, room)

    left = jnp.stack([deep(r, 0) for r in rows])
    right = jnp.concatenate([deep(c, 1) for c in columns], 0)
    slots = holder.shape[0]
    used = (holder >= 0).astype(jnp.int32)
    block = jnp.maximum(holder, 0)
    kind = kinds[block]
    width = rows[0].shape[1]
    lanes = right.shape[2]

    def multiply(kind_ref, block_ref, used_ref, left_ref, right_ref, out_ref):
        slot = pl.program_id(0)

        @pl.when(used_ref[slot] == 1)
        def _():
            out_ref[0] = lax.dot_general(
                left_ref[kind_ref[slot]],
                right_ref[0],
                (((0,), (0,)), ((), ())),
                preferred_element_type=jnp.float32,
            ).astype(out_ref.dtype)

        @pl.when(used_ref[slot] == 0)
        def _():
            out_ref[...] = jnp.zeros_like(out_ref)

    return pl.pallas_call(
        multiply,
        grid_spec=pltpu.PrefetchScalarGridSpec(
            num_scalar_prefetch=3,
            grid=(slots,),
            in_specs=[
                pl.BlockSpec(left.shape, lambda s, kd, b, u: (0, 0, 0)),
                pl.BlockSpec((1, depth, lanes), lambda s, kd, b, u: (b[s], 0, 0)),
            ],
            out_specs=pl.BlockSpec((1, width, lanes), lambda s, kd, b, u: (s, 0, 0)),
        ),
        out_shape=jax.ShapeDtypeStruct((slots, width, lanes), jnp.bfloat16),
        compiler_params=pltpu.CompilerParams(vmem_limit_bytes=48 * MIB),
    )(kind, block, used, left, right)


def adam_slots(planes, master, moment_one, moment_two, slot_scale, filled):
    count, slot_count, width, lanes = planes.shape

    def step(scale_ref, fill_ref, grads, weight, one, two, new_weight, new_one, new_two):
        slot = pl.program_id(0)

        @pl.when(fill_ref[slot] == 1)
        def _():
            total = grads[0, 0].astype(jnp.float32)
            for n in range(1, count):
                total = total + grads[n, 0].astype(jnp.float32)
            results = adam_step(
                weight[0, 0], total * scale_ref[slot], one[0, 0], two[0, 0], TILE_RATE, TILE_DECAY
            )
            for ref, value in zip((new_weight, new_one, new_two), results):
                ref[0, 0] = value

        @pl.when(fill_ref[slot] == 0)
        def _():
            new_weight[...] = weight[...]
            new_one[...] = one[...]
            new_two[...] = two[...]

    deep = pl.BlockSpec((1, 1, width, lanes), lambda s: (0, s, 0, 0))
    scalars = pl.BlockSpec(memory_space=pltpu.SMEM)
    return pl.pallas_call(
        step,
        grid=(slot_count,),
        in_specs=[scalars, scalars, pl.BlockSpec((count, 1, width, lanes), lambda s: (0, s, 0, 0))]
        + [deep] * 3,
        out_specs=[deep] * 3,
        out_shape=[jax.ShapeDtypeStruct(master.shape, jnp.float32)] * 3,
        compiler_params=pltpu.CompilerParams(vmem_limit_bytes=32 * MIB),
    )(slot_scale, filled.astype(jnp.int32), planes, master, moment_one, moment_two)


SCALING = HEAD ** (-0.5)
BF16 = jnp.bfloat16
F32 = jnp.float32


def nn(left, right):
    return jnp.dot(left, right, preferred_element_type=F32)


def nt(left, right):
    return lax.dot_general(left, right, (((1,), (1,)), ((), ())), preferred_element_type=F32)


def tn(left, right):
    return lax.dot_general(left, right, (((0,), (0,)), ((), ())), preferred_element_type=F32)


def normed(rows):
    centre = rows - jnp.mean(rows, -1, keepdims=True)
    inverse = lax.rsqrt(jnp.mean(centre * centre, -1, keepdims=True) + NORM_EPS)
    return centre * inverse, inverse


def normed_back(rows, grad):
    unit, inverse = normed(rows)
    mean = jnp.mean(grad, -1, keepdims=True)
    return (grad - mean - unit * jnp.mean(grad * unit, -1, keepdims=True)) * inverse, unit


def total_of(rows):
    return jnp.sum(rows, 0, keepdims=True)


def turned(rows, cos_tab, sin_tab):
    even = lax.broadcasted_iota(jnp.int32, rows.shape, 1) % 2 == 0
    partner = jnp.where(even, pltpu.roll(rows, HEAD - 1, 1), pltpu.roll(rows, 1, 1))
    return rows * cos_tab + partner * sin_tab


def wide(column):
    return jnp.broadcast_to(column, (column.shape[0], HEAD))


def pack_sums(for_rows, for_text=None):
    out = wide(for_rows)
    if for_text is None:
        return out
    lane = lax.broadcasted_iota(jnp.int32, out.shape, 1)
    count = for_text.shape[0] // 2
    rest = jnp.zeros((out.shape[0] - count, HEAD), F32)
    first = jnp.concatenate([wide(for_text[:count]), rest], 0)
    second = jnp.concatenate([wide(for_text[count:]), rest], 0)
    return jnp.where(lane < 32, out, jnp.where(lane < 64, first, second))


def unpack_text(sums, count):
    return jnp.concatenate([sums[: count // 2, 32:33], sums[: count // 2, 64:65]], 0)


def softmax(scores):
    expo = jnp.exp(scores - jnp.max(scores, -1, keepdims=True))
    return expo / jnp.sum(expo, -1, keepdims=True)


def self_scores(query_low, key_low, tokens):
    scores = nt(query_low, key_low) * SCALING
    lane = lax.broadcasted_iota(jnp.int32, scores.shape, 1)
    return jnp.where(lane < tokens, scores, -1e30)


def whole(array):
    zeros = (0,) * array.ndim
    return pl.BlockSpec(array.shape, lambda *_: zeros)


def block_at(first, stride=1):
    return pl.BlockSpec((1, D, HEAD), lambda i, where: (where[first + stride * i], 0, 0))


def call(body, places, grid, ins, outs, scratch=(), vmem=40):
    specs = [spec if spec is not None else whole(array) for array, spec in ins]
    shapes = [jax.ShapeDtypeStruct(shape, kind) for shape, kind, _ in outs]
    out_specs = [
        spec if spec is not None else whole(shape) for (_, _, spec), shape in zip(outs, shapes)
    ]
    return pl.pallas_call(
        body,
        grid_spec=pltpu.PrefetchScalarGridSpec(
            num_scalar_prefetch=1,
            grid=(grid,),
            in_specs=specs,
            out_specs=out_specs,
            scratch_shapes=list(scratch),
        ),
        out_shape=shapes,
        compiler_params=pltpu.CompilerParams(vmem_limit_bytes=vmem * MIB),
    )(places, *[array for array, _ in ins])


def head_lanes(rows):
    return pl.BlockSpec((rows, HEAD), lambda h, *_: (0, h))


def joined(refs):
    return jnp.concatenate([ref[0] for ref in refs], 1)


def project_self(places, everyone, rows, mod, vecs, heads):
    count = rows.shape[0]
    span = heads * HEAD

    def body(_, rows_ref, mod_ref, vec_ref, *refs):
        weights, (low, pre, value, sums, acc) = refs[:heads], refs[heads:]
        i = pl.program_id(0)

        @pl.when(i == 0)
        def _():
            unit, _ = normed(rows_ref[...])
            low[...] = (unit * (1.0 + mod_ref[1:2]) + mod_ref[0:1]).astype(BF16)

        made = nn(low[...], joined(weights))

        @pl.when(i == 0)
        def _():
            q = made + vec_ref[0:1]
            pre[0] = q
            acc[...] = wide(jnp.sum(q * q, -1, keepdims=True))

        @pl.when(i == 1)
        def _():
            k = made + vec_ref[1:2]
            pre[0] = k
            lane = lax.broadcasted_iota(jnp.int32, acc.shape, 1)
            sums[...] = jnp.where(lane < 64, acc[...], wide(jnp.sum(k * k, -1, keepdims=True)))

        @pl.when(i == 2)
        def _():
            value[...] = (made + vec_ref[2:3]).astype(BF16)

    return call(
        body, places, 3,
        [(rows, None), (mod, None), (vecs, None)]
        + [(everyone, block_at(h, heads)) for h in range(heads)],
        [
            ((count, D), BF16, None),
            ((2, count, span), F32, pl.BlockSpec((1, count, span), lambda i, _: (jnp.minimum(i, 1), 0, 0))),
            ((count, span), BF16, None),
            ((count, HEAD), F32, None),
        ],
        [pltpu.VMEM((count, HEAD), F32)],
    )


def attend_self(places, everyone, pre, value, sums, other, vecs, cos_tab, sin_tab, heads, tokens):
    count = value.shape[0]

    def body(_, pre_ref, value_ref, sum_ref, other_ref, vec_ref, cos_ref, sin_ref, weight, q_ref, k_ref, o_ref, y_ref, acc):
        h = pl.program_id(0)
        total = sum_ref[...] + other_ref[...]
        q_inv = lax.rsqrt(total[:, 0:1] / D + NORM_EPS)
        k_inv = lax.rsqrt(total[:, 64:65] / D + NORM_EPS)
        cos, sin = cos_ref[...], sin_ref[...]
        q = turned(pre_ref[0] * q_inv * vec_ref[3:4], cos, sin).astype(BF16)
        k = turned(pre_ref[1] * k_inv * vec_ref[4:5], cos, sin).astype(BF16)
        q_ref[...] = q
        k_ref[...] = k
        chance = softmax(self_scores(q, k, tokens))
        out = nn(chance.astype(BF16), value_ref[...]).astype(BF16)
        o_ref[0] = out
        part = nt(out, weight[0])

        @pl.when(h == 0)
        def _():
            acc[...] = part

        @pl.when(h > 0)
        def _():
            acc[...] = acc[...] + part

        @pl.when(h == heads - 1)
        def _():
            y_ref[...] = acc[...].astype(BF16)

    lanes = head_lanes(count)
    return call(
        body, places, heads,
        [
            (pre, pl.BlockSpec((2, count, HEAD), lambda h, _: (0, 0, h))),
            (value, lanes), (sums, None), (other, None),
            (vecs, head_lanes(vecs.shape[0])), (cos_tab, None), (sin_tab, None),
            (everyone, block_at(3 * heads)),
        ],
        [
            (value.shape, BF16, lanes),
            (value.shape, BF16, lanes),
            ((heads, count, HEAD), BF16, pl.BlockSpec((1, count, HEAD), lambda h, _: (h, 0, 0))),
            ((count, D), BF16, None),
        ],
        [pltpu.VMEM((count, D), F32)],
    )


def project_text(places, everyone, context, vecs, heads):
    count = context.shape[0]
    span = heads * HEAD

    def body(_, text_ref, vec_ref, *refs):
        weights, (key, value, sums) = refs[:heads], refs[heads:]
        i = pl.program_id(0)
        made = nn(text_ref[...], joined(weights))

        @pl.when(i == 0)
        def _():
            k = made + vec_ref[6:7]
            key[...] = k
            sums[...] = wide(jnp.sum(k * k, -1, keepdims=True))

        @pl.when(i == 1)
        def _():
            value[...] = (made + vec_ref[7:8]).astype(BF16)

    return call(
        body, places, 2,
        [(context, None), (vecs, None)]
        + [(everyone, block_at(5 * heads + h, heads)) for h in range(heads)],
        [((count, span), F32, None), ((count, span), BF16, None), ((count, HEAD), F32, None)],
    )


def project_cross(places, everyone, rows, part, other, mod, shared, vecs, text_sums, heads):
    count = rows.shape[0]
    span = heads * HEAD
    text = text_sums.shape[0]

    def body(_, rows_ref, part_ref, other_ref, mod_ref, shared_ref, vec_ref, text_ref, *refs):
        weights, (branch, after, low, pre, sums) = refs[:heads], refs[heads:]
        y = part_ref[...].astype(F32) + other_ref[...].astype(F32) + shared_ref[0:1]
        branch[...] = y
        x = rows_ref[...] + mod_ref[2:3] * y
        after[...] = x
        unit, _ = normed(x)
        a = (unit * shared_ref[3:4] + shared_ref[4:5]).astype(BF16)
        low[...] = a
        q = nn(a, joined(weights)) + vec_ref[5:6]
        pre[...] = q
        sums[...] = pack_sums(jnp.sum(q * q, -1, keepdims=True), text_ref[:, 0:1])

    return call(
        body, places, 1,
        [(v, None) for v in (rows, part, other, mod, shared, vecs, text_sums)]
        + [(everyone, block_at(4 * heads + h)) for h in range(heads)],
        [
            ((count, D), F32, None),
            ((count, D), F32, None),
            ((count, D), BF16, None),
            ((count, span), F32, None),
            ((count, HEAD), F32, None),
        ],
    )


def attend_cross(places, everyone, pre, key_pre, value, sums, other, vecs, heads):
    count, text = pre.shape[0], value.shape[0]

    def body(_, pre_ref, key_ref, value_ref, sum_ref, other_ref, vec_ref, weight, q_ref, k_ref, o_ref, y_ref, acc):
        h = pl.program_id(0)
        total = sum_ref[...] + other_ref[...]
        q_inv = lax.rsqrt(total[:, 0:1] / D + NORM_EPS)
        k_inv = lax.rsqrt(unpack_text(total, text) / D + NORM_EPS)
        q = (pre_ref[...] * q_inv * vec_ref[8:9]).astype(BF16)
        k = (key_ref[...] * k_inv * vec_ref[9:10]).astype(BF16)
        q_ref[...] = q
        k_ref[...] = k
        chance = softmax(nt(q, k) * SCALING)
        out = nn(chance.astype(BF16), value_ref[...]).astype(BF16)
        o_ref[0] = out
        part = nt(out, weight[0])

        @pl.when(h == 0)
        def _():
            acc[...] = part

        @pl.when(h > 0)
        def _():
            acc[...] = acc[...] + part

        @pl.when(h == heads - 1)
        def _():
            y_ref[...] = acc[...].astype(BF16)

    return call(
        body, places, heads,
        [
            (pre, head_lanes(count)), (key_pre, head_lanes(text)), (value, head_lanes(text)),
            (sums, None), (other, None), (vecs, head_lanes(vecs.shape[0])),
            (everyone, block_at(7 * heads)),
        ],
        [
            (pre.shape, BF16, head_lanes(count)),
            (value.shape, BF16, head_lanes(text)),
            ((heads, count, HEAD), BF16, pl.BlockSpec((1, count, HEAD), lambda h, _: (h, 0, 0))),
            ((count, D), BF16, None),
        ],
        [pltpu.VMEM((count, D), F32)],
    )


def feed_forward(places, everyone, after_one, part, other, mod, shared, cot, up_bias, heads, blocks):
    count = after_one.shape[0]
    group = max(g for g in (7, 5, 3, 1) if blocks % g == 0 and g <= 5)
    span = group * HEAD

    def body(_, after_ref, part_ref, other_ref, mod_ref, shared_ref, cot_ref, bias_ref, *refs):
        ups, downs = refs[:group], refs[group : 2 * group]
        after, low, grad, hidden, d_hidden, d_bias, y_ref, da_ref, y_acc, da_acc = refs[2 * group :]
        i = pl.program_id(0)

        @pl.when(i == 0)
        def _():
            x = after_ref[...] + part_ref[...].astype(F32) + other_ref[...].astype(F32)
            x = x + shared_ref[1:2]
            after[...] = x
            unit, _ = normed(x)
            low[...] = (unit * (1.0 + mod_ref[4:5]) + mod_ref[3:4]).astype(BF16)
            grad[...] = (mod_ref[5:6] * cot_ref[...]).astype(BF16)
            y_acc[...] = jnp.zeros_like(y_acc)
            da_acc[...] = jnp.zeros_like(da_acc)

        up, down = joined(ups), joined(downs)
        pre = nn(low[...], up) + bias_ref[...]
        square = pre * pre
        bent = jnp.tanh(GELU_COEF * (pre + 0.044715 * pre * square))
        act = (0.5 * pre * (1.0 + bent)).astype(BF16)
        slope = 0.5 * (1.0 + bent) + 0.5 * pre * (1.0 - bent * bent) * (
            GELU_COEF * (1.0 + 3.0 * 0.044715 * square)
        )
        dh = (nn(grad[...], down) * slope).astype(BF16)
        d_bias[...] = total_of(dh.astype(F32))
        for j in range(group):
            hidden[j] = act[:, j * HEAD : (j + 1) * HEAD]
            d_hidden[j] = dh[:, j * HEAD : (j + 1) * HEAD]
        y_acc[...] = y_acc[...] + nt(act, down)
        da_acc[...] = da_acc[...] + nt(dh, up)

        @pl.when(i == blocks // group - 1)
        def _():
            y_ref[...] = y_acc[...].astype(BF16)
            da_ref[...] = da_acc[...].astype(BF16)

    base = 8 * heads
    tall = pl.BlockSpec((group, count, HEAD), lambda i, _: (i, 0, 0))
    flat = pl.BlockSpec((1, span), lambda i, _: (0, i))
    return call(
        body, places, blocks // group,
        [(v, None) for v in (after_one, part, other, mod, shared, cot)]
        + [(up_bias, flat)]
        + [(everyone, block_at(base + j, group)) for j in range(group)]
        + [(everyone, block_at(base + blocks + j, group)) for j in range(group)],
        [
            ((count, D), F32, None),
            ((count, D), BF16, None),
            ((count, D), BF16, None),
            ((blocks, count, HEAD), BF16, tall),
            ((blocks, count, HEAD), BF16, tall),
            (up_bias.shape, F32, flat),
            ((count, D), BF16, None),
            ((count, D), BF16, None),
        ],
        [pltpu.VMEM((count, D), F32), pltpu.VMEM((count, D), F32)],
        vmem=48,
    )


def cross_back(places, everyone, cot, after_two, part, other, mod, query, key, value, pre, key_pre, vecs, heads):
    count, text = query.shape[0], key.shape[0]

    def body(_, cot_ref, after_ref, part_ref, other_ref, mod_ref, q_ref, k_ref, v_ref, pre_ref, key_ref, vec_ref, weight, dx_ref, low_ref, dq_ref, dk_ref, dv_ref, sums, q_acc, k_acc):
        h = pl.program_id(0)

        @pl.when(h == 0)
        def _():
            da = part_ref[...].astype(F32) + other_ref[...].astype(F32)
            back, _ = normed_back(after_ref[...], da * (1.0 + mod_ref[4:5]))
            dx = cot_ref[...] + back
            dx_ref[...] = dx
            low_ref[...] = dx.astype(BF16)
            q_acc[...] = jnp.zeros_like(q_acc)
            k_acc[...] = jnp.zeros_like(k_acc)

        do = nn(low_ref[...], weight[0]).astype(BF16)
        q, k = q_ref[...], k_ref[...]
        chance = softmax(nt(q, k) * SCALING)
        dp = nt(do, v_ref[...])
        ds = (chance * (dp - jnp.sum(chance * dp, -1, keepdims=True))).astype(BF16)
        dv_ref[0] = tn(chance.astype(BF16), do).astype(BF16)
        dq = nn(ds, k) * SCALING
        dk = tn(ds, q) * SCALING
        dq_ref[...] = dq
        dk_ref[...] = dk
        q_acc[...] = q_acc[...] + wide(jnp.sum(pre_ref[...] * vec_ref[8:9] * dq, -1, keepdims=True))
        k_acc[...] = k_acc[...] + wide(jnp.sum(key_ref[...] * vec_ref[9:10] * dk, -1, keepdims=True))

        @pl.when(h == heads - 1)
        def _():
            sums[...] = pack_sums(q_acc[:, 0:1], k_acc[:, 0:1])

    return call(
        body, places, heads,
        [(v, None) for v in (cot, after_two, part, other, mod)]
        + [
            (query, head_lanes(count)), (key, head_lanes(text)), (value, head_lanes(text)),
            (pre, head_lanes(count)), (key_pre, head_lanes(text)),
            (vecs, head_lanes(vecs.shape[0])), (everyone, block_at(7 * heads)),
        ],
        [
            ((count, D), F32, None),
            ((count, D), BF16, None),
            (query.shape, F32, head_lanes(count)),
            (key.shape, F32, head_lanes(text)),
            ((heads, text, HEAD), BF16, pl.BlockSpec((1, text, HEAD), lambda h, _: (h, 0, 0))),
            ((count, HEAD), F32, None),
        ],
        [pltpu.VMEM((count, HEAD), F32), pltpu.VMEM((text, HEAD), F32)],
    )


def norm_grad(pre, inverse, gain, incoming, total):
    grad = inverse * (gain * incoming) - pre * (inverse * inverse * inverse) * (total / D)
    low = grad.astype(BF16)
    return low, total_of(low.astype(F32)), total_of(incoming * pre * inverse)


def cross_back_rows(places, everyone, pre, key_pre, dq, dk, dv, squares, squares_other, sums, sums_other, vecs, heads):
    count, text = pre.shape[0], key_pre.shape[0]

    def body(_, pre_ref, key_ref, dq_ref, dk_ref, dv_ref, sq_ref, sqo_ref, sum_ref, sumo_ref, vec_ref, weight, gq_ref, gk_ref, vec_out, da_ref, acc):
        h = pl.program_id(0)
        squares_all = sq_ref[...] + sqo_ref[...]
        total = sum_ref[...] + sumo_ref[...]
        q_inv = lax.rsqrt(squares_all[:, 0:1] / D + NORM_EPS)
        k_inv = lax.rsqrt(unpack_text(squares_all, text) / D + NORM_EPS)
        low_q, bias_q, gain_q = norm_grad(pre_ref[...], q_inv, vec_ref[8:9], dq_ref[...], total[:, 0:1])
        low_k, bias_k, gain_k = norm_grad(
            key_ref[...], k_inv, vec_ref[9:10], dk_ref[...], unpack_text(total, text)
        )
        gq_ref[0] = low_q
        gk_ref[0] = low_k
        bias_v = total_of(dv_ref[0].astype(F32))
        vec_out[...] = jnp.concatenate(
            [bias_q, bias_k, bias_v, gain_q, gain_k, jnp.zeros((3, HEAD), F32)], 0
        )
        part = nt(low_q, weight[0])

        @pl.when(h == 0)
        def _():
            acc[...] = part

        @pl.when(h > 0)
        def _():
            acc[...] = acc[...] + part

        @pl.when(h == heads - 1)
        def _():
            da_ref[...] = acc[...].astype(BF16)

    tall = pl.BlockSpec((1, count, HEAD), lambda h, _: (h, 0, 0))
    tall_text = pl.BlockSpec((1, text, HEAD), lambda h, _: (h, 0, 0))
    return call(
        body, places, heads,
        [
            (pre, head_lanes(count)), (key_pre, head_lanes(text)), (dq, head_lanes(count)),
            (dk, head_lanes(text)), (dv, tall_text), (squares, None), (squares_other, None),
            (sums, None), (sums_other, None), (vecs, head_lanes(vecs.shape[0])),
            (everyone, block_at(4 * heads)),
        ],
        [
            ((heads, count, HEAD), BF16, tall),
            ((heads, text, HEAD), BF16, tall_text),
            ((8, heads * HEAD), F32, head_lanes(8)),
            ((count, D), BF16, None),
        ],
        [pltpu.VMEM((count, D), F32)],
    )


def self_back(places, everyone, dx_two, after_one, part, other, mod, shared, query, key, value, pre, vecs, cos_tab, sin_tab, heads, tokens):
    count = query.shape[0]

    def body(_, dx_in, after_ref, part_ref, other_ref, mod_ref, shared_ref, q_ref, k_ref, v_ref, pre_ref, vec_ref, cos_ref, sin_ref, weight, dx_ref, low_ref, d_ref, dv_ref, sums, q_acc, k_acc):
        h = pl.program_id(0)

        @pl.when(h == 0)
        def _():
            da = part_ref[...].astype(F32) + other_ref[...].astype(F32)
            back, _ = normed_back(after_ref[...], da * shared_ref[3:4])
            dx = dx_in[...] + back
            dx_ref[...] = dx
            low_ref[...] = (mod_ref[2:3] * dx).astype(BF16)
            q_acc[...] = jnp.zeros_like(q_acc)
            k_acc[...] = jnp.zeros_like(k_acc)

        do = nn(low_ref[...], weight[0]).astype(BF16)
        q, k = q_ref[...], k_ref[...]
        chance = softmax(self_scores(q, k, tokens))
        dp = nt(do, v_ref[...])
        ds = (chance * (dp - jnp.sum(chance * dp, -1, keepdims=True))).astype(BF16)
        dv_ref[0] = tn(chance.astype(BF16), do).astype(BF16)
        cos, sin = cos_ref[...], -sin_ref[...]
        dq = turned(nn(ds, k) * SCALING, cos, sin)
        dk = turned(tn(ds, q) * SCALING, cos, sin)
        d_ref[0] = dq
        d_ref[1] = dk
        q_acc[...] = q_acc[...] + wide(jnp.sum(pre_ref[0] * vec_ref[3:4] * dq, -1, keepdims=True))
        k_acc[...] = k_acc[...] + wide(jnp.sum(pre_ref[1] * vec_ref[4:5] * dk, -1, keepdims=True))

        @pl.when(h == heads - 1)
        def _():
            lane = lax.broadcasted_iota(jnp.int32, q_acc.shape, 1)
            sums[...] = jnp.where(lane < 64, q_acc[...], k_acc[...])

    lanes = head_lanes(count)
    pair = pl.BlockSpec((2, count, HEAD), lambda h, _: (0, 0, h))
    return call(
        body, places, heads,
        [(v, None) for v in (dx_two, after_one, part, other, mod, shared)]
        + [
            (query, lanes), (key, lanes), (value, lanes), (pre, pair),
            (vecs, head_lanes(vecs.shape[0])), (cos_tab, None), (sin_tab, None),
            (everyone, block_at(3 * heads)),
        ],
        [
            ((count, D), F32, None),
            ((count, D), BF16, None),
            (pre.shape, F32, pair),
            ((heads, count, HEAD), BF16, pl.BlockSpec((1, count, HEAD), lambda h, _: (h, 0, 0))),
            ((count, HEAD), F32, None),
        ],
        [pltpu.VMEM((count, HEAD), F32), pltpu.VMEM((count, HEAD), F32)],
    )


def self_back_rows(places, everyone, pre, grads, dv, squares, squares_other, sums, sums_other, vecs, heads):
    count = pre.shape[1]

    def body(_, pre_ref, d_ref, dv_ref, sq_ref, sqo_ref, sum_ref, sumo_ref, vec_ref, wq, wk, wv, gq_ref, gk_ref, vec_out, da_ref, acc):
        h = pl.program_id(0)
        squares_all = sq_ref[...] + sqo_ref[...]
        total = sum_ref[...] + sumo_ref[...]
        lows, biases, gains = [], [], []
        for n in range(2):
            inverse = lax.rsqrt(squares_all[:, 64 * n : 64 * n + 1] / D + NORM_EPS)
            low, bias, gain = norm_grad(
                pre_ref[n], inverse, vec_ref[3 + n : 4 + n], d_ref[n], total[:, 64 * n : 64 * n + 1]
            )
            lows.append(low)
            biases.append(bias)
            gains.append(gain)
        gq_ref[0] = lows[0]
        gk_ref[0] = lows[1]
        dv_low = dv_ref[0]
        bias_v = total_of(dv_low.astype(F32))
        vec_out[...] = jnp.concatenate(
            [biases[0], biases[1], bias_v, gains[0], gains[1], jnp.zeros((3, HEAD), F32)], 0
        )
        part = nt(
            jnp.concatenate([lows[0], lows[1], dv_low], 1),
            jnp.concatenate([wq[0], wk[0], wv[0]], 1),
        )

        @pl.when(h == 0)
        def _():
            acc[...] = part

        @pl.when(h > 0)
        def _():
            acc[...] = acc[...] + part

        @pl.when(h == heads - 1)
        def _():
            da_ref[...] = acc[...].astype(BF16)

    tall = pl.BlockSpec((1, count, HEAD), lambda h, _: (h, 0, 0))
    pair = pl.BlockSpec((2, count, HEAD), lambda h, _: (0, 0, h))
    return call(
        body, places, heads,
        [
            (pre, pair), (grads, pair), (dv, tall), (squares, None), (squares_other, None),
            (sums, None), (sums_other, None), (vecs, head_lanes(vecs.shape[0])),
            (everyone, block_at(0)), (everyone, block_at(heads)), (everyone, block_at(2 * heads)),
        ],
        [
            ((heads, count, HEAD), BF16, tall),
            ((heads, count, HEAD), BF16, tall),
            ((8, heads * HEAD), F32, head_lanes(8)),
            ((count, D), BF16, None),
        ],
        [pltpu.VMEM((count, D), F32)],
    )


def shared_sums(places, rows, after_one, after_two, low_grads, dx_one, branch, cot, das, y_three, shared):
    def body(_, x_ref, x1_ref, x2_ref, dy1, dy2, dy3, dx1_ref, y1_ref, cot_ref, da1, da3, da2, y3, shared_ref, out):
        def half(value):
            return 0.5 * total_of(value)

        out[0:1] = half(dy1[...].astype(F32))
        out[1:2] = half(dy2[...].astype(F32))
        out[2:3] = half(dy3[...].astype(F32))
        part = da3[...].astype(F32)
        out[3:4] = total_of(part * normed(x1_ref[...])[0])
        out[4:5] = total_of(part)
        part = da1[...].astype(F32)
        out[5:6] = total_of(part)
        out[6:7] = total_of(part * normed(x_ref[...])[0])
        out[7:8] = half(dx1_ref[...] * y1_ref[...])
        part = da2[...].astype(F32)
        out[8:9] = total_of(part)
        out[9:10] = total_of(part * normed(x2_ref[...])[0])
        out[10:11] = total_of(cot_ref[...] * (y3[...].astype(F32) + 0.5 * shared_ref[2:3]))

    return call(
        body, places, 1,
        [(v, None) for v in (rows, after_one, after_two, *low_grads, dx_one, branch, cot, *das, y_three, shared)],
        [(shared.shape, F32, None)],
        vmem=48,
    )[0]


def body(
    latents,
    context,
    cotangent,
    positions,
    step_ids,
    owners,
    time_table,
    master,
    first_moment,
    second_moment,
    head_params,
    head_first,
    head_second,
    shared_params,
    shared_first,
    shared_second,
):
    tensors = lax.axis_size("tensor")
    devices = lax.axis_size("dp")
    slot_count = master.shape[1]
    tile_count = owners.shape[0]
    heads_here = HEADS // tensors
    blocks_here = FF // (HEAD * tensors)
    width_here = D // tensors
    places, holder = owner_layout(owners, slot_count, devices)
    scales = tile_scales(tile_count, heads_here, blocks_here)
    my_slots = lax.dynamic_slice_in_dim(holder, lax.axis_index("dp") * slot_count, slot_count)
    rank = pair_rank()
    filled = my_slots >= 0
    slot_scale = jnp.where(filled, scales[jnp.maximum(my_slots, 0)], 0.0)
    scaled = (master[0] * slot_scale[:, None, None]).astype(jnp.bfloat16)
    half = latents.shape[0]
    tokens = 2 * half
    count = -(-tokens // 16) * 16
    taller = ((0, -half % 16), (0, 0))
    small = jnp.concatenate(
        [
            head_params[0],
            positions.reshape(-1).astype(jnp.float32),
            step_ids.astype(jnp.float32),
        ]
    )
    packed = jnp.pad(small, (0, -small.shape[0] % 1024)).reshape(-1, HEAD)
    everyone, lats, cots, context, packed = gather_slots(
        scaled, jnp.pad(latents, taller), jnp.pad(cotangent, taller), context, packed
    )
    small = packed.reshape(-1)
    vectors = small[: head_params.shape[1]]
    small = small[head_params.shape[1] :]
    positions = small[: positions.size].reshape(positions.shape)
    step = small[positions.size]
    vecs = vectors[: 10 * width_here].reshape(10, width_here)
    up_bias = vectors[10 * width_here :].reshape(1, -1)
    chosen = (step == jnp.arange(TSTEPS)).astype(jnp.float32)
    mod = shared_params[5:11] + jnp.einsum(
        "s,skd->kd", chosen, time_table, precision=lax.Precision.HIGHEST
    )
    cos_tab, sin_tab = rope_tables(positions, HEAD)
    sin_tab = jnp.where(jnp.arange(HEAD) % 2 == 0, -sin_tab, sin_tab)
    cos_tab, sin_tab = (jnp.pad(t, ((0, count - tokens), (0, 0))) for t in (cos_tab, sin_tab))

    def all_rows(halves):
        rows = jnp.concatenate([halves[0, :half], halves[1, :half]], 0)
        return jnp.pad(rows, ((0, count - tokens), (0, 0))).astype(jnp.float32)

    rows, cot = all_rows(lats), all_rows(cots)
    low_one, pre_one, value_one, squares_one = project_self(
        places, everyone, rows, mod, vecs, heads_here
    )
    squares_one_other = pair_swap(squares_one)
    key_pre, value_two, text_squares = project_text(places, everyone, context, vecs, heads_here)
    query_one, key_one, heads_one, part_one = attend_self(
        places, everyone, pre_one, value_one, squares_one, squares_one_other, vecs, cos_tab,
        sin_tab, heads_here, tokens,
    )
    branch_one, after_one, low_two, pre_two, squares_two = project_cross(
        places, everyone, rows, part_one, pair_swap(part_one), mod, shared_params, vecs,
        text_squares, heads_here,
    )
    squares_two_other = pair_swap(squares_two)
    query_two, key_two, heads_two, part_two = attend_cross(
        places, everyone, pre_two, key_pre, value_two, squares_two, squares_two_other, vecs,
        heads_here,
    )
    after_two, low_three, grad_three, hidden, d_hidden, d_up_bias, y_three, da_two = feed_forward(
        places, everyone, after_one, part_two, pair_swap(part_two), mod, shared_params, cot,
        up_bias, heads_here, blocks_here,
    )
    dx_two, grad_two, dq_two, dk_two, dv_two, sums_two = cross_back(
        places, everyone, cot, after_two, da_two, pair_swap(da_two), mod, query_two, key_two,
        value_two, pre_two, key_pre, vecs, heads_here,
    )
    query_grad_two, key_grad_two, vecs_two, da_three = cross_back_rows(
        places, everyone, pre_two, key_pre, dq_two, dk_two, dv_two, squares_two,
        squares_two_other, sums_two, pair_swap(sums_two), vecs, heads_here,
    )
    dx_one, grad_one, d_one, dv_one, sums_one = self_back(
        places, everyone, dx_two, after_one, da_three, pair_swap(da_three), mod, shared_params,
        query_one, key_one, value_one, pre_one, vecs, cos_tab, sin_tab, heads_here, tokens,
    )
    query_grad_one, key_grad_one, vecs_one, da_one = self_back_rows(
        places, everyone, pre_one, d_one, dv_one, squares_one, squares_one_other, sums_one,
        pair_swap(sums_one), vecs, heads_here,
    )
    shared_grad = shared_sums(
        places, rows, after_one, after_two, (grad_one, grad_two, grad_three), dx_one,
        branch_one, cot, (da_one, da_three, da_two), y_three, shared_params,
    )
    head_grad = jnp.concatenate(
        [vecs_one[:5].reshape(-1), vecs_two[:5].reshape(-1), d_up_bias.reshape(-1)]
    )
    tensor_rank = lax.axis_index("tensor")
    head_padded = jnp.where(jnp.arange(tensors)[:, None] == rank, head_grad[None, :], 0.0)
    vector = jnp.concatenate([head_padded.reshape(-1), shared_grad.reshape(-1)])
    vector = jnp.pad(vector, (0, -vector.shape[0] % 1024)).reshape(-1, 128)
    parts, vector, output, grad_input = reduce_slots(
        holder,
        kind_of_blocks(tile_count, heads_here, blocks_here),
        (low_one, grad_one, low_two, context, grad_two, low_three, grad_three),
        (
            query_grad_one,
            key_grad_one,
            dv_one,
            heads_one,
            query_grad_two,
            key_grad_two,
            dv_two,
            heads_two,
            d_hidden,
            hidden,
        ),
        vector,
        (rows, after_two, dx_one, y_three, da_one),
        jnp.concatenate([mod[5:6], mod[1:2], shared_params[2:3], jnp.zeros((5, D), F32)], 0),
        slot_count,
    )
    output, grad_input = (
        jnp.where(lax.axis_index("tensor") == 0, v[:half], v[half:tokens])
        for v in (output, grad_input)
    )
    new_master, new_first, new_second = adam_slots(
        parts, master, first_moment, second_moment, slot_scale, filled
    )
    vector = vector.reshape(-1)
    head_total = vector[: head_padded.size].reshape(head_padded.shape)
    shared_total = vector[head_padded.size : head_padded.size + shared_grad.size]
    shared_total = shared_total.reshape(shared_grad.shape)
    mine_head = lax.dynamic_slice_in_dim(head_total, tensor_rank, 1, 0)
    new_head, new_head_first, new_head_second = adam_step(
        head_params, mine_head, head_first, head_second, VECTOR_RATE, 0.0
    )
    new_shared, new_shared_first, new_shared_second = adam_step(
        shared_params, shared_total, shared_first, shared_second, VECTOR_RATE, 0.0
    )
    return (
        output,
        grad_input,
        new_master,
        new_first,
        new_second,
        new_head,
        new_head_first,
        new_head_second,
        new_shared,
        new_shared_first,
        new_shared_second,
    )


def solution(mesh):
    return jax.shard_map(
        body,
        mesh=mesh,
        in_specs=(
            P(("dp", "tensor"), None),
            P("dp", None),
            P(("dp", "tensor"), None),
            P(None, "dp"),
            P("dp"),
            P(),
            P(),
            P("tensor", "dp", None, None),
            P("tensor", "dp", None, None),
            P("tensor", "dp", None, None),
            P("tensor", None),
            P("tensor", None),
            P("tensor", None),
            P(),
            P(),
            P(),
        ),
        out_specs=(
            P(("dp", "tensor"), None),
            P(("dp", "tensor"), None),
            P("tensor", "dp", None, None),
            P("tensor", "dp", None, None),
            P("tensor", "dp", None, None),
            P("tensor", None),
            P("tensor", None),
            P("tensor", None),
            P(),
            P(),
            P(),
        ),
        check_vma=False,
    )
```

```python
import functools

import jax
import jax.numpy as jnp
from jax import lax
from jax.experimental import pallas as pl
from jax.experimental.pallas import tpu as pltpu
from jax.sharding import PartitionSpec as P

D = 1536
HEADS = 12
HEAD = 128
FF = 8960
TSTEPS = 16
STEPC = 10


NORM_EPS = 1e-06
BETA_ONE = 0.9
BETA_TWO = 0.999
ADAM_EPS = 1e-08
TILE_RATE = 1.0
TILE_DECAY = 0.1
VECTOR_RATE = 0.5
GELU_COEF = 0.7978845608028654


def rope_tables(token_places, head_size):
    sixths = head_size // 6
    frame_pairs = (head_size - 4 * sixths) // 2
    frame_freq = 10000.0 ** (-jnp.arange(frame_pairs, dtype=jnp.float32) / frame_pairs)
    side_freq = 10000.0 ** (-jnp.arange(sixths, dtype=jnp.float32) / sixths)
    spots = token_places.astype(jnp.float32)
    angles = jnp.concatenate(
        [
            spots[0][..., None] * frame_freq,
            spots[1][..., None] * side_freq,
            spots[2][..., None] * side_freq,
        ],
        -1,
    )
    angles = jnp.repeat(angles, 2, axis=-1)
    return (jnp.cos(angles), jnp.sin(angles))


def owner_layout(owners, slot_count, devices):
    indices = jnp.arange(owners.shape[0], dtype=jnp.int32)
    same_owner = (owners[:, None] == owners[None, :]) & (indices[None, :] < indices[:, None])
    slot_of = jnp.sum(same_owner.astype(jnp.int32), axis=1)
    places = owners * slot_count + slot_of
    spots = jnp.arange(slot_count * devices, dtype=jnp.int32)
    holder = (
        jnp.sum(jnp.where(places[None, :] == spots[:, None], indices[None, :] + 1, 0), axis=1) - 1
    )
    return (places, holder)


def tile_scales(tile_count, heads_here, blocks_here):
    indices = jnp.arange(tile_count)
    scale_in = D ** (-0.5)
    scale_out = HEADS ** (-0.5)
    scale_down = FF ** (-0.5)
    scales = jnp.where(
        indices < 3 * heads_here,
        scale_in,
        jnp.where(
            indices < 4 * heads_here,
            scale_out,
            jnp.where(
                indices < 7 * heads_here,
                scale_in,
                jnp.where(
                    indices < 8 * heads_here,
                    scale_out,
                    jnp.where(indices < 8 * heads_here + blocks_here, scale_in, scale_down),
                ),
            ),
        ),
    )
    return scales.astype(jnp.float32)


def adam_step(weight, gradient, moment_one, moment_two, step_rate, decay_rate):
    first_new = BETA_ONE * moment_one + (1.0 - BETA_ONE) * gradient
    second_new = BETA_TWO * moment_two + (1.0 - BETA_TWO) * gradient * gradient
    first_hat = first_new / (1.0 - BETA_ONE**STEPC)
    second_hat = second_new / (1.0 - BETA_TWO**STEPC)
    weight_new = weight - step_rate * (
        first_hat / (jnp.sqrt(second_hat) + ADAM_EPS) + decay_rate * weight
    )
    return (weight_new, first_new, second_new)


MESH = pl.DeviceIdType.MESH
ANY = pl.BlockSpec(memory_space=pl.ANY)
MIB = 1 << 20


def chip_pairs():
    return lax.axis_size("dp") == 16 and lax.axis_size("tensor") == 2


def pair_rank():
    if chip_pairs():
        return (lax.axis_index("dp") // 4) % 2
    return lax.axis_index("tensor")


def pair_swap(value):
    if chip_pairs():
        return lax.ppermute(value, "dp", [(i, i ^ 4) for i in range(16)])
    return lax.ppermute(value, "tensor", [(0, 1), (1, 0)])


def pair_sums(*values):
    stacked = jnp.concatenate([v.reshape(-1) for v in values])
    total = stacked + pair_swap(stacked)
    out, at = [], 0
    for v in values:
        out.append(total[at : at + v.size].reshape(v.shape))
        at += v.size
    return tuple(out)


def place_of():
    chip, core = lax.axis_index("dp"), lax.axis_index("tensor")
    z, y, x = chip // 4, (chip // 2) % 2, chip % 2
    return chip, core, z, y, x


def column_of(z, y, x, k):
    high, low_bit = z // 2, z % 2
    if k & 2:
        high = 1 - high
    if k & 1:
        low_bit = 1 - low_bit
    return (2 * high + low_bit) * 4 + 2 * y + x


def greet(chip, core, z, y, x):
    barrier = pltpu.get_barrier_semaphore()
    friends = []
    for k in range(4):
        for flip in (0, 1):
            if k or flip:
                friends.append((column_of(z, y, x, k), core if flip == 0 else 1 - core))
    friends.append((column_of(z, y, 1 - x, 0), core))
    friends.append((column_of(z, 1 - y, x, 0), core))
    for friend in friends:
        pl.semaphore_signal(barrier, inc=1, device_id=friend, device_id_type=MESH)
    pl.semaphore_wait(barrier, len(friends))


def gather_kernel(
    own, lat, cot, text, small, out, lats, cots, texts, smalls, clip_s, clip_r,
    near_s, col_r,
    x_s, x_r, y_s, y_r, ra_s, ra_r, rb_s, rb_r, sib_s, sib_r,
):
    chip, core, z, y, x = place_of()
    rank = z % 2
    half = own.shape[1] // 2
    part = half // 2
    at_x = column_of(z, y, 1 - x, 0)
    at_y = column_of(z, 1 - y, x, 0)
    greet(chip, core, z, y, x)

    def rows(ref, unit, first, count):
        return ref.at[unit, :, pl.ds(pl.multiple_of(first, 16), count), :]

    def remote(unit, first, count, send, recv, device):
        piece = rows(out, unit, first, count)
        return pltpu.make_async_remote_copy(
            src_ref=piece, dst_ref=piece, send_sem=send, recv_sem=recv,
            device_id=device, device_id_type=MESH,
        )

    started = []
    for j in range(2):
        zh = z // 2 if j == 0 else 1 - z // 2
        target = (2 * zh + core) * 4 + 2 * y + x
        for h in range(2):
            src = own.at[:, pl.ds(h * half, half), :]
            dst = out.at[chip, :, pl.ds(h * half, half), :]
            go = pltpu.make_async_remote_copy(
                src_ref=src, dst_ref=dst, send_sem=near_s.at[2 * j + h], recv_sem=col_r.at[z],
                device_id=(target, h), device_id_type=MESH,
            )
            if j == 0:
                here = pltpu.make_async_copy(src, dst, col_r.at[z])
                stays = jnp.logical_and(rank == core, core == h)

                @pl.when(stays)
                def _():
                    here.start()

                @pl.when(jnp.logical_not(stays))
                def _():
                    go.start()

                started.append((go, stays))
            else:
                go.start()
                started.append((go, None))

    pair_chip = column_of(z, y, x, 1)
    rows_of_text = text.shape[0] // 2

    def clip_pieces(h):
        share = pl.ds(h * rows_of_text, rows_of_text)
        return ((lat, lats.at[h]), (cot, cots.at[h]), (text.at[share], texts.at[share]))

    home = rank == core
    trade = pltpu.make_async_remote_copy(
        src_ref=small, dst_ref=smalls, send_sem=clip_s.at[6], recv_sem=clip_r.at[6],
        device_id=(pair_chip, 1 - core), device_id_type=MESH,
    )
    keep = pltpu.make_async_copy(small, smalls, clip_r.at[6])

    @pl.when(home)
    def _():
        keep.start()

    @pl.when(jnp.logical_not(home))
    def _():
        trade.start()

    def hand_out(h, n, wait):
        src, dst = clip_pieces(h)[n]
        far = pltpu.make_async_remote_copy(
            src_ref=src, dst_ref=dst, send_sem=clip_s.at[n], recv_sem=clip_r.at[3 * h + n],
            device_id=(pair_chip, rank), device_id_type=MESH,
        )
        near = pltpu.make_async_remote_copy(
            src_ref=src, dst_ref=dst, send_sem=clip_s.at[3 + n], recv_sem=clip_r.at[3 * h + n],
            device_id=(chip, 1 - core), device_id_type=MESH,
        )
        here = pltpu.make_async_copy(src, dst, clip_r.at[3 * h + n])

        @pl.when(core == h)
        def _():
            if wait:
                far.wait_send()
            else:
                far.start()

            @pl.when(home)
            def _():
                if not wait:
                    here.start()

            @pl.when(jnp.logical_not(home))
            def _():
                if wait:
                    near.wait_send()
                else:
                    near.start()

    for n in range(3):
        for h in range(2):
            hand_out(h, n, False)

    def column_in(k):
        unit = column_of(z, y, x, k)
        source_z = unit // 4
        piece = rows(out, unit, core * half, half)
        pltpu.make_async_copy(piece, piece, col_r.at[source_z]).wait()
        to_x = remote(unit, core * half, half, x_s.at[k], x_r.at[k], (at_x, core))
        to_y = remote(unit, core * half, half, y_s.at[k], y_r.at[k], (at_y, core))
        to_sib = remote(unit, core * half, half, sib_s.at[k], sib_r.at[k], (chip, 1 - core))
        to_x.start()
        to_y.start()
        to_sib.start()
        return [to_x, to_y, to_sib]

    def side_in(k):
        ux = column_of(z, y, 1 - x, k)
        uy = column_of(z, 1 - y, x, k)
        remote(ux, core * half, half, x_s.at[k], x_r.at[k], (at_x, core)).wait_recv()
        on_y = remote(ux, core * half + part, part, rb_s.at[k], rb_r.at[k], (at_y, core))
        on_y.start()
        sib_x = remote(ux, core * half, half, sib_s.at[4 + k], sib_r.at[4 + k], (chip, 1 - core))
        sib_x.start()
        remote(uy, core * half, half, y_s.at[k], y_r.at[k], (at_y, core)).wait_recv()
        on_x = remote(uy, core * half, part, ra_s.at[k], ra_r.at[k], (at_x, core))
        on_x.start()
        sib_y = remote(uy, core * half, half, sib_s.at[8 + k], sib_r.at[8 + k], (chip, 1 - core))
        sib_y.start()
        return [on_y, sib_x, on_x, sib_y]

    def corner_in(k):
        unit = column_of(z, 1 - y, 1 - x, k)
        remote(unit, core * half, part, ra_s.at[k], ra_r.at[k], (at_x, core)).wait_recv()
        sib_a = remote(unit, core * half, part, sib_s.at[12 + k], sib_r.at[12 + k], (chip, 1 - core))
        sib_a.start()
        remote(unit, core * half + part, part, rb_s.at[k], rb_r.at[k], (at_y, core)).wait_recv()
        sib_b = remote(
            unit, core * half + part, part, sib_s.at[16 + k], sib_r.at[16 + k], (chip, 1 - core)
        )
        sib_b.start()
        return [sib_a, sib_b]

    sent = []
    for step in range(6):
        if step < 4:
            sent += column_in(step)
        if 1 <= step < 5:
            sent += side_in(step - 1)
        if step >= 2:
            sent += corner_in(step - 2)
    for copy in sent:
        copy.wait_send()
    for go, stays in started:
        if stays is None:
            go.wait_send()
        else:

            @pl.when(jnp.logical_not(stays))
            def _():
                go.wait_send()

    for n in range(3):
        for h in range(2):
            hand_out(h, n, True)
            dst = clip_pieces(h)[n][1]
            pltpu.make_async_copy(dst, dst, clip_r.at[3 * h + n]).wait()

    @pl.when(jnp.logical_not(home))
    def _():
        trade.wait_send()

    pltpu.make_async_copy(smalls, smalls, clip_r.at[6]).wait()

    other = (1 - core) * half
    for k in range(4):
        for at, (yy, xx) in ((0, (y, x)), (4, (y, 1 - x)), (8, (1 - y, x))):
            remote(
                column_of(z, yy, xx, k), other, half, sib_s.at[at + k], sib_r.at[at + k],
                (chip, 1 - core),
            ).wait_recv()
        corner = column_of(z, 1 - y, 1 - x, k)
        remote(
            corner, other, part, sib_s.at[12 + k], sib_r.at[12 + k], (chip, 1 - core)
        ).wait_recv()
        remote(
            corner, other + part, part, sib_s.at[16 + k], sib_r.at[16 + k], (chip, 1 - core)
        ).wait_recv()


def gather_slots(scaled, lat, cot, text, small):
    if not chip_pairs():
        everyone = lax.all_gather(scaled, "dp", axis=0, tiled=True)
        lats, cots = (lax.all_gather(v, "tensor") for v in (lat, cot))
        return everyone, lats, cots, text, small
    dma = pltpu.SemaphoreType.DMA
    counts = (7, 7, 4, 4, 4, 4, 4, 4, 4, 4, 4, 4, 20, 20)
    everyone, *rest = pl.pallas_call(
        gather_kernel,
        out_shape=[
            jax.ShapeDtypeStruct((16,) + scaled.shape, scaled.dtype),
            jax.ShapeDtypeStruct((2,) + lat.shape, lat.dtype),
            jax.ShapeDtypeStruct((2,) + cot.shape, cot.dtype),
            jax.ShapeDtypeStruct(text.shape, text.dtype),
            jax.ShapeDtypeStruct(small.shape, small.dtype),
        ],
        in_specs=[ANY] * 5,
        out_specs=[ANY] * 5,
        scratch_shapes=[dma((n,)) for n in counts],
        compiler_params=pltpu.CompilerParams(
            collective_id=0, has_side_effects=True, vmem_limit_bytes=4 * MIB
        ),
    )(scaled, lat, cot, text, small)
    return everyone.reshape((-1,) + scaled.shape[1:]), *rest


def toggled(z, y, x, flip_y, flip_x, k):
    high = (z // 2 + k // 2) % 2
    low_bit = (z % 2 + k % 2) % 2
    return (2 * high + low_bit) * 4 + 2 * ((y + flip_y) % 2) + (x + flip_x) % 2


def reduce_kernel(
    kind, block, *refs,
):
    (
        *pieces, rows_in, after_in, dx_in, y_in, da_in, gains, vec_in,
        final, vec_out, result, result_grad, y_other, da_other, from_sib, from_x, from_y, corner_a, corner_b,
        left, right, ring, corners, side_x, side_y, middle, stage, vec_box,
        load_s, stage_s, sib_s, sib_r, x_s, x_r, y_s, y_r, ca_s, ca_r, cb_s, cb_r, f_s, f_r, v_s, v_r,
        end_s, end_r,
    ) = refs
    chip, core, z, y, x = place_of()
    rank = z % 2
    slots, width, lanes = final.shape[1:]
    half = width // 2
    part = half // 2
    at_x = toggled(z, y, x, 0, 1, 0)
    at_y = toggled(z, y, x, 1, 0, 0)
    sibling = (chip, 1 - core)
    mates = (
        sibling,
        (at_x, core),
        (at_y, core),
        (toggled(z, y, x, 0, 0, 1), core),
        (toggled(z, y, x, 0, 0, 2), core),
    )

    kinds = left.shape[0]
    depth = right.shape[1]
    loads = [
        pltpu.make_async_copy(pieces[i], left.at[i], load_s.at[i]) for i in range(kinds)
    ]
    first = 0
    blank = []
    for i, piece in enumerate(pieces[kinds:]):
        number, rows = piece.shape[:2]
        loads.append(
            pltpu.make_async_copy(
                piece, right.at[pl.ds(first, number), pl.ds(0, rows), :], load_s.at[kinds + i]
            )
        )
        if rows < depth:
            blank.append((first, number, rows))
        first += number
    for load in loads:
        load.start()
    for start, number, rows in blank:

        def clear(i, carry):
            right[start + i, pl.ds(rows, depth - rows), :] = jnp.zeros(
                (depth - rows, lanes), right.dtype
            )
            return carry

        lax.fori_loop(0, number, clear, 0)
    right[first] = jnp.zeros((depth, lanes), right.dtype)
    vec_out[...] = vec_in[...]
    greet(chip, core, z, y, x)
    for load in loads:
        load.wait()

    def remote(src, dst, send, recv, device):
        return pltpu.make_async_remote_copy(
            src_ref=src, dst_ref=dst, send_sem=send, recv_sem=recv,
            device_id=device, device_id_type=MESH,
        )

    def unit_of(q, k):
        return toggled(z, y, x, 1 - q % 2, 1 - q // 2, k)

    def sums(q, k, first, terms, total):
        base = unit_of(q, k) * slots
        count = total.shape[1]

        def one(i, carry):
            slot = base + i
            rows = pl.ds(pl.multiple_of(first, 128), count)
            acc = jnp.dot(
                left[kind[slot], rows, :], right[block[slot]], preferred_element_type=jnp.float32
            )
            for term in terms:
                acc = acc + term[i].astype(jnp.float32)
            total[i] = acc.astype(total.dtype)
            return carry

        lax.fori_loop(0, slots, one, 0)

    mine, other = core * half, (1 - core) * half

    def sub(ref, first):
        return ref.at[:, pl.ds(first, part), :]

    def sib_copy(q, k):
        i = 4 * q + k
        return remote(ring.at[q % 2], from_sib.at[i], sib_s.at[i], sib_r.at[i], sibling)

    def a_copy(k):
        return remote(
            sub(corners.at[k % 2], 0), corner_a.at[k], ca_s.at[k], ca_r.at[k], (at_x, core)
        )

    def b_copy(k):
        return remote(
            sub(corners.at[k % 2], part), corner_b.at[k], cb_s.at[k], cb_r.at[k], (at_y, core)
        )

    def x_copy(k, n):
        rows = pl.ds(n * part, part)
        return remote(
            side_x.at[k % 2, :, rows, :], from_x.at[k, :, rows, :], x_s.at[4 * n + k],
            x_r.at[4 * n + k], (at_x, core),
        )

    def y_copy(k, n):
        rows = pl.ds((1 - n) * part, part)
        return remote(
            side_y.at[k % 2, :, rows, :], from_y.at[k, :, rows, :], y_s.at[4 * n + k],
            y_r.at[4 * n + k], (at_y, core),
        )

    def f_copy(k):
        src = middle.at[k % 2]
        dst = final.at[z // 2, :, pl.ds(pl.multiple_of(mine, 128), half), :]
        recv = f_r.at[2 * (z // 2) + core]
        return remote(
            src, dst, f_s.at[k], recv, (toggled(z, y, x, 0, 0, k), rank)
        ), pltpu.make_async_copy(src, dst, recv)

    def stays(k):
        return jnp.logical_and(k == 0, rank == core)

    def staged(source, place, i):
        copy = pltpu.make_async_copy(source, place, stage_s.at[i])
        copy.start()
        return copy

    def for_sibling(k):
        def one(q, carry):
            @pl.when(jnp.logical_or(q >= 2, k < 3))
            def _():
                back = jnp.where(q >= 2, k, k + 1)
                sib_copy((q + 2) % 4, back).wait_send()

            sums(q, k, other, (), ring.at[q % 2])
            sib_copy(q, k).start()
            return carry

        lax.fori_loop(0, 4, one, 0)

    def corner(k):
        sib_copy(0, k).wait_recv()
        staged(from_sib.at[k], stage.at[0], 0).wait()

        @pl.when(k < 2)
        def _():
            a_copy(k + 2).wait_send()
            b_copy(k + 2).wait_send()

        sums(0, k, mine, (stage.at[0],), corners.at[k % 2])
        a_copy(k).start()
        b_copy(k).start()

    def direct_sides(k):
        sib_copy(1, k).wait_recv()
        in_x = staged(from_sib.at[4 + k], stage.at[0], 0)
        sib_copy(2, k).wait_recv()
        in_y = staged(from_sib.at[8 + k], stage.at[1], 1)

        @pl.when(k < 2)
        def _():
            for n in range(2):
                x_copy(k + 2, n).wait_send()
                y_copy(k + 2, n).wait_send()

        in_x.wait()
        sums(1, k, mine, (sub(stage.at[0], 0),), sub(side_x.at[k % 2], 0))
        x_copy(k, 0).start()
        in_y.wait()
        sums(2, k, mine + part, (sub(stage.at[1], part),), sub(side_y.at[k % 2], part))
        y_copy(k, 0).start()

    def relayed_sides(k):
        b_copy(k).wait_recv()
        in_b = staged(corner_b.at[k], sub(stage.at[2], 0), 2)
        a_copy(k).wait_recv()
        in_a = staged(corner_a.at[k], sub(stage.at[2], part), 3)
        in_b.wait()
        sums(
            1, k, mine + part, (sub(stage.at[0], part), sub(stage.at[2], 0)),
            sub(side_x.at[k % 2], part),
        )
        x_copy(k, 1).start()
        in_a.wait()
        sums(2, k, mine, (sub(stage.at[1], 0), sub(stage.at[2], part)), sub(side_y.at[k % 2], 0))
        y_copy(k, 1).start()

    def centre(k):
        sib_copy(3, k).wait_recv()
        in_sib = staged(from_sib.at[12 + k], stage.at[0], 0)
        x_copy(k, 0).wait_recv()
        x_copy(k, 1).wait_recv()
        in_x = staged(from_x.at[k], stage.at[1], 1)
        y_copy(k, 0).wait_recv()
        y_copy(k, 1).wait_recv()
        in_y = staged(from_y.at[k], stage.at[2], 2)

        @pl.when(k < 2)
        def _():
            f_copy(k + 2)[0].wait_send()

        in_sib.wait()
        in_x.wait()
        in_y.wait()
        sums(3, k, mine, (stage.at[0], stage.at[1], stage.at[2]), middle.at[k % 2])
        go, here = f_copy(k)

        @pl.when(stays(k))
        def _():
            here.start()

        @pl.when(jnp.logical_not(stays(k)))
        def _():
            go.start()

    home = rank == core
    pair_device = (toggled(z, y, x, 0, 0, 1), core)
    ends = [
        remote(y_in, y_other, end_s.at[0], end_r.at[0], pair_device),
        remote(da_in, da_other, end_s.at[1], end_r.at[1], pair_device),
        remote(result, result, end_s.at[2], end_r.at[2], sibling),
        remote(result_grad, result_grad, end_s.at[3], end_r.at[3], sibling),
    ]

    def finish_rows():
        ends[0].wait_recv()
        ends[1].wait_recv()
        tall = 16
        spec = pl.BlockSpec((tall, width), lambda i: (i, 0))

        def one(x_ref, x2_ref, dx_ref, y_ref, yo_ref, da_ref, dao_ref, out_ref, grad_ref):
            y_all = y_ref[...].astype(F32) + yo_ref[...].astype(F32) + gains[2:3]
            out_ref[...] = (x2_ref[...] + gains[0:1] * y_all).astype(out_ref.dtype)
            da = da_ref[...].astype(F32) + dao_ref[...].astype(F32)
            back, _ = normed_back(x_ref[...], da * (1.0 + gains[1:2]))
            grad_ref[...] = dx_ref[...] + back

        pltpu.emit_pipeline(
            one, grid=(rows_in.shape[0] // tall,), in_specs=[spec] * 7, out_specs=[spec] * 2
        )(rows_in, after_in, dx_in, y_in, y_other, da_in, da_other, result, result_grad)
        ends[2].start()
        ends[3].start()

    @pl.when(jnp.logical_not(home))
    def _():
        ends[0].start()
        ends[1].start()

    def vec_copy(i):
        return remote(vec_out, vec_box.at[i], v_s.at[i], v_r.at[i], mates[i])

    def turn(step, carry):
        for i in range(5):

            @pl.when(step == i)
            def _():
                vec_copy(i).start()

        @pl.when(step < 4)
        def _():
            corner(3 - step)
            direct_sides(3 - step)

        @pl.when(step < 3)
        def _():
            for_sibling(2 - step)

        @pl.when(step < 4)
        def _():
            relayed_sides(3 - step)

        @pl.when(step >= 1)
        def _():
            centre(4 - step)

        @pl.when(jnp.logical_and(step == 3, home))
        def _():
            finish_rows()

        for i in range(5):

            @pl.when(step == i)
            def _():
                vec_copy(i).wait()
                vec_out[...] = vec_out[...] + vec_box[i]

        return carry

    for_sibling(3)
    lax.fori_loop(0, 5, turn, 0)
    for q in (2, 3):
        sib_copy(q, 0).wait_send()
    for k in (1, 0):
        a_copy(k).wait_send()
        b_copy(k).wait_send()
        for n in range(2):
            x_copy(k, n).wait_send()
            y_copy(k, n).wait_send()
    f_copy(1)[0].wait_send()

    @pl.when(home)
    def _():
        ends[2].wait_send()
        ends[3].wait_send()

    @pl.when(jnp.logical_not(home))
    def _():
        f_copy(0)[0].wait_send()
        ends[0].wait_send()
        ends[1].wait_send()
        ends[2].wait_recv()
        ends[3].wait_recv()

    for plane in range(2):
        for h in range(2):
            piece = final.at[plane, :, pl.ds(h * half, half), :]
            pltpu.make_async_copy(piece, piece, f_r.at[2 * plane + h]).wait()


def reduce_slots(holder, kinds, rows, columns, vector, ends, gains, slot_count):
    if not chip_pairs():
        grads = slot_grads(holder, kinds, [r.T for r in rows], columns)
        total = lax.psum_scatter(grads, "dp", scatter_dimension=0, tiled=True)
        x, after, dx, y_part, da_part = ends
        y_all, da_all = (
            v.astype(F32) + pair_swap(v).astype(F32) for v in (y_part, da_part)
        )
        result = (after + gains[0] * (y_all + gains[2])).astype(BF16)
        back, _ = normed_back(x, da_all * (1.0 + gains[1]))
        return total[None], lax.psum(vector, ("dp", "tensor")), result, dx + back
    left = rows
    width, depth = left[0].shape
    lanes = columns[0].shape[2]
    tiles = sum(c.shape[0] for c in columns)
    block = jnp.where(holder >= 0, holder, tiles)
    kind = kinds[jnp.maximum(holder, 0)]
    half = width // 2
    dma = pltpu.SemaphoreType.DMA
    scalars = pl.BlockSpec(memory_space=pltpu.SMEM)
    inside = pl.BlockSpec(memory_space=pltpu.VMEM)
    low = jnp.bfloat16

    def room(count, tall):
        return jax.ShapeDtypeStruct((count, slot_count, tall, lanes), low)

    def slab(count):
        return pltpu.VMEM((count, slot_count, half, lanes), low)

    outs = pl.pallas_call(
        reduce_kernel,
        out_shape=[
            room(2, width), jax.ShapeDtypeStruct(vector.shape, vector.dtype),
            jax.ShapeDtypeStruct(ends[0].shape, low), jax.ShapeDtypeStruct(ends[0].shape, F32),
            jax.ShapeDtypeStruct(ends[0].shape, low), jax.ShapeDtypeStruct(ends[0].shape, low),
            room(16, half), room(4, half), room(4, half),
            room(4, half // 2), room(4, half // 2),
        ],
        in_specs=[scalars, scalars] + [ANY] * (len(left) + len(columns) + 5) + [inside] * 2,
        out_specs=[ANY, inside] + [ANY] * 9,
        scratch_shapes=[
            pltpu.VMEM((len(left), width, depth), low),
            pltpu.VMEM((tiles + 1, depth, lanes), low),
            slab(2), slab(2), slab(2), slab(2), slab(2), slab(3),
            pltpu.VMEM((5,) + vector.shape, vector.dtype),
        ]
        + [dma((n,)) for n in (len(left) + len(columns), 4, 16, 16)
        + (8,) * 4 + (4,) * 6 + (5, 5, 4, 4)],
        compiler_params=pltpu.CompilerParams(
            collective_id=1, has_side_effects=True, vmem_limit_bytes=58 * MIB
        ),
    )(kind, block, *left, *columns, *ends, gains, vector)
    return outs[:4]


def kind_of_blocks(tile_count, heads_here, blocks_here):
    number = jnp.arange(tile_count)
    kind = number // heads_here
    table = jnp.array([0, 0, 0, 1, 2, 3, 3, 4], jnp.int32)
    late = jnp.where(number < 8 * heads_here + blocks_here, 5, 6)
    return jnp.where(number < 8 * heads_here, table[jnp.minimum(kind, 7)], late).astype(jnp.int32)


def slot_grads(holder, kinds, rows, columns):
    depth = max(r.shape[0] for r in rows)

    def deep(value, axis):
        room = [(0, 0)] * value.ndim
        room[axis] = (0, depth - value.shape[axis])
        return jnp.pad(value, room)

    left = jnp.stack([deep(r, 0) for r in rows])
    right = jnp.concatenate([deep(c, 1) for c in columns], 0)
    slots = holder.shape[0]
    used = (holder >= 0).astype(jnp.int32)
    block = jnp.maximum(holder, 0)
    kind = kinds[block]
    width = rows[0].shape[1]
    lanes = right.shape[2]

    def multiply(kind_ref, block_ref, used_ref, left_ref, right_ref, out_ref):
        slot = pl.program_id(0)

        @pl.when(used_ref[slot] == 1)
        def _():
            out_ref[0] = lax.dot_general(
                left_ref[kind_ref[slot]],
                right_ref[0],
                (((0,), (0,)), ((), ())),
                preferred_element_type=jnp.float32,
            ).astype(out_ref.dtype)

        @pl.when(used_ref[slot] == 0)
        def _():
            out_ref[...] = jnp.zeros_like(out_ref)

    return pl.pallas_call(
        multiply,
        grid_spec=pltpu.PrefetchScalarGridSpec(
            num_scalar_prefetch=3,
            grid=(slots,),
            in_specs=[
                pl.BlockSpec(left.shape, lambda s, kd, b, u: (0, 0, 0)),
                pl.BlockSpec((1, depth, lanes), lambda s, kd, b, u: (b[s], 0, 0)),
            ],
            out_specs=pl.BlockSpec((1, width, lanes), lambda s, kd, b, u: (s, 0, 0)),
        ),
        out_shape=jax.ShapeDtypeStruct((slots, width, lanes), jnp.bfloat16),
        compiler_params=pltpu.CompilerParams(vmem_limit_bytes=48 * MIB),
    )(kind, block, used, left, right)


def adam_slots(planes, master, moment_one, moment_two, slot_scale, filled):
    count, slot_count, width, lanes = planes.shape

    def step(scale_ref, fill_ref, grads, weight, one, two, new_weight, new_one, new_two):
        slot = pl.program_id(0)

        @pl.when(fill_ref[slot] == 1)
        def _():
            total = grads[0, 0].astype(jnp.float32)
            for n in range(1, count):
                total = total + grads[n, 0].astype(jnp.float32)
            results = adam_step(
                weight[0, 0], total * scale_ref[slot], one[0, 0], two[0, 0], TILE_RATE, TILE_DECAY
            )
            for ref, value in zip((new_weight, new_one, new_two), results):
                ref[0, 0] = value

        @pl.when(fill_ref[slot] == 0)
        def _():
            new_weight[...] = weight[...]
            new_one[...] = one[...]
            new_two[...] = two[...]

    deep = pl.BlockSpec((1, 1, width, lanes), lambda s: (0, s, 0, 0))
    scalars = pl.BlockSpec(memory_space=pltpu.SMEM)
    return pl.pallas_call(
        step,
        grid=(slot_count,),
        in_specs=[scalars, scalars, pl.BlockSpec((count, 1, width, lanes), lambda s: (0, s, 0, 0))]
        + [deep] * 3,
        out_specs=[deep] * 3,
        out_shape=[jax.ShapeDtypeStruct(master.shape, jnp.float32)] * 3,
        compiler_params=pltpu.CompilerParams(vmem_limit_bytes=32 * MIB),
    )(
        slot_scale,
        filled.astype(jnp.int32),
        *[
            pltpu.with_memory_space_constraint(v, pltpu.HBM)
            for v in (planes, master, moment_one, moment_two)
        ],
    )


SCALING = HEAD ** (-0.5)
BF16 = jnp.bfloat16
F32 = jnp.float32


def nn(left, right):
    return jnp.dot(left, right, preferred_element_type=F32)


def nt(left, right):
    return lax.dot_general(left, right, (((1,), (1,)), ((), ())), preferred_element_type=F32)


def tn(left, right):
    return lax.dot_general(left, right, (((0,), (0,)), ((), ())), preferred_element_type=F32)


def normed(rows):
    centre = rows - jnp.mean(rows, -1, keepdims=True)
    inverse = lax.rsqrt(jnp.mean(centre * centre, -1, keepdims=True) + NORM_EPS)
    return centre * inverse, inverse


def normed_back(rows, grad):
    unit, inverse = normed(rows)
    mean = jnp.mean(grad, -1, keepdims=True)
    return (grad - mean - unit * jnp.mean(grad * unit, -1, keepdims=True)) * inverse, unit


def total_of(rows):
    return jnp.sum(rows, 0, keepdims=True)


def turned(rows, cos_tab, sin_tab):
    even = lax.broadcasted_iota(jnp.int32, rows.shape, 1) % 2 == 0
    partner = jnp.where(even, pltpu.roll(rows, HEAD - 1, 1), pltpu.roll(rows, 1, 1))
    return rows * cos_tab + partner * sin_tab


def wide(column):
    return jnp.broadcast_to(column, (column.shape[0], HEAD))


def pack_sums(for_rows, for_text=None):
    out = wide(for_rows)
    if for_text is None:
        return out
    lane = lax.broadcasted_iota(jnp.int32, out.shape, 1)
    count = for_text.shape[0] // 2
    rest = jnp.zeros((out.shape[0] - count, HEAD), F32)
    first = jnp.concatenate([wide(for_text[:count]), rest], 0)
    second = jnp.concatenate([wide(for_text[count:]), rest], 0)
    return jnp.where(lane < 32, out, jnp.where(lane < 64, first, second))


def unpack_text(sums, count):
    return jnp.concatenate([sums[: count // 2, 32:33], sums[: count // 2, 64:65]], 0)


def softmax(scores):
    expo = jnp.exp(scores - jnp.max(scores, -1, keepdims=True))
    return expo / jnp.sum(expo, -1, keepdims=True)


def self_scores(query_low, key_low, tokens):
    scores = nt(query_low, key_low) * SCALING
    lane = lax.broadcasted_iota(jnp.int32, scores.shape, 1)
    return jnp.where(lane < tokens, scores, -1e30)


def whole(array):
    zeros = (0,) * len(array.shape)
    return pl.BlockSpec(array.shape, lambda *_: zeros)


def block_at(first, stride=1):
    return pl.BlockSpec((1, D, HEAD), lambda i, where: (where[first + stride * i], 0, 0))


def call(body, places, grid, ins, outs, scratch=(), vmem=24):
    specs = [spec if spec is not None else whole(array) for array, spec in ins]
    shapes = [pltpu.HBM(shape, kind) for shape, kind, _ in outs]
    out_specs = [
        spec if spec is not None else whole(shape) for (_, _, spec), shape in zip(outs, shapes)
    ]
    return pl.pallas_call(
        body,
        grid_spec=pltpu.PrefetchScalarGridSpec(
            num_scalar_prefetch=1,
            grid=(grid,),
            in_specs=specs,
            out_specs=out_specs,
            scratch_shapes=list(scratch),
        ),
        out_shape=shapes,
        compiler_params=pltpu.CompilerParams(vmem_limit_bytes=vmem * MIB),
    )(places, *[pltpu.with_memory_space_constraint(array, pltpu.HBM) for array, _ in ins])


def head_lanes(rows):
    return pl.BlockSpec((rows, HEAD), lambda h, *_: (0, h))


def joined(refs):
    return jnp.concatenate([ref[0] for ref in refs], 1)


def project_self(places, everyone, rows, mod, vecs, heads):
    count = rows.shape[0]
    span = heads * HEAD

    def body(_, rows_ref, mod_ref, vec_ref, *refs):
        weights, (low, pre, value, sums, acc) = refs[:heads], refs[heads:]
        i = pl.program_id(0)

        @pl.when(i == 0)
        def _():
            unit, _ = normed(rows_ref[...])
            low[...] = (unit * (1.0 + mod_ref[1:2]) + mod_ref[0:1]).astype(BF16)

        made = nn(low[...], joined(weights))

        @pl.when(i == 0)
        def _():
            q = made + vec_ref[0:1]
            pre[0] = q
            acc[...] = wide(jnp.sum(q * q, -1, keepdims=True))

        @pl.when(i == 1)
        def _():
            k = made + vec_ref[1:2]
            pre[0] = k
            lane = lax.broadcasted_iota(jnp.int32, acc.shape, 1)
            sums[...] = jnp.where(lane < 64, acc[...], wide(jnp.sum(k * k, -1, keepdims=True)))

        @pl.when(i == 2)
        def _():
            value[...] = (made + vec_ref[2:3]).astype(BF16)

    return call(
        body, places, 3,
        [(rows, None), (mod, None), (vecs, None)]
        + [(everyone, block_at(h, heads)) for h in range(heads)],
        [
            ((count, D), BF16, None),
            ((2, count, span), F32, pl.BlockSpec((1, count, span), lambda i, _: (jnp.minimum(i, 1), 0, 0))),
            ((count, span), BF16, None),
            ((count, HEAD), F32, None),
        ],
        [pltpu.VMEM((count, HEAD), F32)],
    )


def attend_self(places, everyone, pre, value, sums, other, vecs, cos_tab, sin_tab, heads, tokens):
    count = value.shape[0]

    def body(_, pre_ref, value_ref, sum_ref, other_ref, vec_ref, cos_ref, sin_ref, weight, q_ref, k_ref, o_ref, y_ref, acc):
        h = pl.program_id(0)
        total = sum_ref[...] + other_ref[...]
        q_inv = lax.rsqrt(total[:, 0:1] / D + NORM_EPS)
        k_inv = lax.rsqrt(total[:, 64:65] / D + NORM_EPS)
        cos, sin = cos_ref[...], sin_ref[...]
        q = turned(pre_ref[0] * q_inv * vec_ref[3:4], cos, sin).astype(BF16)
        k = turned(pre_ref[1] * k_inv * vec_ref[4:5], cos, sin).astype(BF16)
        q_ref[...] = q
        k_ref[...] = k
        chance = softmax(self_scores(q, k, tokens))
        out = nn(chance.astype(BF16), value_ref[...]).astype(BF16)
        o_ref[0] = out
        part = nt(out, weight[0])

        @pl.when(h == 0)
        def _():
            acc[...] = part

        @pl.when(h > 0)
        def _():
            acc[...] = acc[...] + part

        @pl.when(h == heads - 1)
        def _():
            y_ref[...] = acc[...].astype(BF16)

    lanes = head_lanes(count)
    return call(
        body, places, heads,
        [
            (pre, pl.BlockSpec((2, count, HEAD), lambda h, _: (0, 0, h))),
            (value, lanes), (sums, None), (other, None),
            (vecs, head_lanes(vecs.shape[0])), (cos_tab, None), (sin_tab, None),
            (everyone, block_at(3 * heads)),
        ],
        [
            (value.shape, BF16, lanes),
            (value.shape, BF16, lanes),
            ((heads, count, HEAD), BF16, pl.BlockSpec((1, count, HEAD), lambda h, _: (h, 0, 0))),
            ((count, D), BF16, None),
        ],
        [pltpu.VMEM((count, D), F32)],
    )


def project_text(places, everyone, context, vecs, heads):
    count = context.shape[0]
    span = heads * HEAD

    def body(_, text_ref, vec_ref, *refs):
        weights, (key, value, sums) = refs[:heads], refs[heads:]
        i = pl.program_id(0)
        made = nn(text_ref[...], joined(weights))

        @pl.when(i == 0)
        def _():
            k = made + vec_ref[6:7]
            key[...] = k
            sums[...] = wide(jnp.sum(k * k, -1, keepdims=True))

        @pl.when(i == 1)
        def _():
            value[...] = (made + vec_ref[7:8]).astype(BF16)

    return call(
        body, places, 2,
        [(context, None), (vecs, None)]
        + [(everyone, block_at(5 * heads + h, heads)) for h in range(heads)],
        [((count, span), F32, None), ((count, span), BF16, None), ((count, HEAD), F32, None)],
    )


def project_cross(places, everyone, rows, part, other, mod, shared, vecs, text_sums, heads):
    count = rows.shape[0]
    span = heads * HEAD
    text = text_sums.shape[0]

    def body(_, rows_ref, part_ref, other_ref, mod_ref, shared_ref, vec_ref, text_ref, *refs):
        weights, (branch, after, low, pre, sums) = refs[:heads], refs[heads:]
        y = part_ref[...].astype(F32) + other_ref[...].astype(F32) + shared_ref[0:1]
        branch[...] = y
        x = rows_ref[...] + mod_ref[2:3] * y
        after[...] = x
        unit, _ = normed(x)
        a = (unit * shared_ref[3:4] + shared_ref[4:5]).astype(BF16)
        low[...] = a
        q = nn(a, joined(weights)) + vec_ref[5:6]
        pre[...] = q
        sums[...] = pack_sums(jnp.sum(q * q, -1, keepdims=True), text_ref[:, 0:1])

    return call(
        body, places, 1,
        [(v, None) for v in (rows, part, other, mod, shared, vecs, text_sums)]
        + [(everyone, block_at(4 * heads + h)) for h in range(heads)],
        [
            ((count, D), F32, None),
            ((count, D), F32, None),
            ((count, D), BF16, None),
            ((count, span), F32, None),
            ((count, HEAD), F32, None),
        ],
    )


def attend_cross(places, everyone, pre, key_pre, value, sums, other, vecs, heads):
    count, text = pre.shape[0], value.shape[0]

    def body(_, pre_ref, key_ref, value_ref, sum_ref, other_ref, vec_ref, weight, q_ref, k_ref, o_ref, y_ref, acc):
        h = pl.program_id(0)
        total = sum_ref[...] + other_ref[...]
        q_inv = lax.rsqrt(total[:, 0:1] / D + NORM_EPS)
        k_inv = lax.rsqrt(unpack_text(total, text) / D + NORM_EPS)
        q = (pre_ref[...] * q_inv * vec_ref[8:9]).astype(BF16)
        k = (key_ref[...] * k_inv * vec_ref[9:10]).astype(BF16)
        q_ref[...] = q
        k_ref[...] = k
        chance = softmax(nt(q, k) * SCALING)
        out = nn(chance.astype(BF16), value_ref[...]).astype(BF16)
        o_ref[0] = out
        part = nt(out, weight[0])

        @pl.when(h == 0)
        def _():
            acc[...] = part

        @pl.when(h > 0)
        def _():
            acc[...] = acc[...] + part

        @pl.when(h == heads - 1)
        def _():
            y_ref[...] = acc[...].astype(BF16)

    return call(
        body, places, heads,
        [
            (pre, head_lanes(count)), (key_pre, head_lanes(text)), (value, head_lanes(text)),
            (sums, None), (other, None), (vecs, head_lanes(vecs.shape[0])),
            (everyone, block_at(7 * heads)),
        ],
        [
            (pre.shape, BF16, head_lanes(count)),
            (value.shape, BF16, head_lanes(text)),
            ((heads, count, HEAD), BF16, pl.BlockSpec((1, count, HEAD), lambda h, _: (h, 0, 0))),
            ((count, D), BF16, None),
        ],
        [pltpu.VMEM((count, D), F32)],
    )


def hidden_group(blocks):
    return max(g for g in (5, 4, 3, 2, 1) if blocks % g == 0)


def block_lanes(where, everyone, held, sems, first, group, steps):
    i = pl.program_id(0)

    def fetch(step, act):
        slot = step % 2
        for j in range(group):
            copy = pltpu.make_async_copy(
                everyone.at[where[first + step * group + j]],
                held.at[slot, :, pl.ds(j * HEAD, HEAD)],
                sems.at[slot, j],
            )
            copy.start() if act else copy.wait()

    @pl.when(i == 0)
    def _():
        fetch(0, True)

    @pl.when(i + 1 < steps)
    def _():
        fetch(i + 1, True)

    fetch(i, False)
    return held[i % 2]


def lanes_scratch(group):
    return [pltpu.VMEM((2, D, group * HEAD), BF16), pltpu.SemaphoreType.DMA((2, group))]


def hidden_back(places, everyone, mod, cot, heads, blocks):
    count = cot.shape[0]
    group = hidden_group(blocks)
    steps = blocks // group

    def body(where, weights, mod_ref, cot_ref, grad, out, held, sems):
        @pl.when(pl.program_id(0) == 0)
        def _():
            grad[...] = (mod_ref[5:6] * cot_ref[...]).astype(BF16)

        down = block_lanes(where, weights, held, sems, 8 * heads + blocks, group, steps)
        out[...] = nn(grad[...], down).astype(BF16)

    return call(
        body, places, steps,
        [(everyone, ANY), (mod, None), (cot, None)],
        [
            ((count, D), BF16, None),
            ((count, blocks * HEAD), BF16, pl.BlockSpec((count, group * HEAD), lambda i, _: (0, i))),
        ],
        lanes_scratch(group),
    )


def hidden_both(places, everyone, after_one, part, other, mod, shared, d_act, up_bias, heads, blocks):
    count = after_one.shape[0]
    group = hidden_group(blocks)
    steps = blocks // group
    span = group * HEAD

    def body(where, weights, after_ref, part_ref, other_ref, mod_ref, shared_ref, d_ref, bias_ref, after, low, hidden, d_hidden, d_bias, da_ref, acc, held, sems):
        i = pl.program_id(0)

        @pl.when(i == 0)
        def _():
            x = after_ref[...] + part_ref[...].astype(F32) + other_ref[...].astype(F32)
            x = x + shared_ref[1:2]
            after[...] = x
            unit, _ = normed(x)
            low[...] = (unit * (1.0 + mod_ref[4:5]) + mod_ref[3:4]).astype(BF16)
            acc[...] = jnp.zeros_like(acc)

        up = block_lanes(where, weights, held, sems, 8 * heads, group, steps)
        pre = nn(low[...], up) + bias_ref[...]
        square = pre * pre
        bent = jnp.tanh(GELU_COEF * (pre + 0.044715 * pre * square))
        act = (0.5 * pre * (1.0 + bent)).astype(BF16)
        slope = 0.5 * (1.0 + bent) + 0.5 * pre * (1.0 - bent * bent) * (
            GELU_COEF * (1.0 + 3.0 * 0.044715 * square)
        )
        dh = (d_ref[...].astype(F32) * slope).astype(BF16)
        d_bias[...] = total_of(dh.astype(F32))
        for j in range(group):
            hidden[j] = act[:, j * HEAD : (j + 1) * HEAD]
            d_hidden[j] = dh[:, j * HEAD : (j + 1) * HEAD]
        acc[...] = acc[...] + nt(dh, up)

        @pl.when(i == steps - 1)
        def _():
            da_ref[...] = acc[...].astype(BF16)

    tall = pl.BlockSpec((group, count, HEAD), lambda i, _: (i, 0, 0))
    flat = pl.BlockSpec((1, span), lambda i, _: (0, i))
    return call(
        body, places, steps,
        [(everyone, ANY)]
        + [(v, None) for v in (after_one, part, other, mod, shared)]
        + [(d_act, pl.BlockSpec((count, span), lambda i, _: (0, i))), (up_bias, flat)],
        [
            ((count, D), F32, None),
            ((count, D), BF16, None),
            ((blocks, count, HEAD), BF16, tall),
            ((blocks, count, HEAD), BF16, tall),
            (up_bias.shape, F32, flat),
            ((count, D), BF16, None),
        ],
        [pltpu.VMEM((count, D), F32)] + lanes_scratch(group),
        vmem=32,
    )


def hidden_out(places, everyone, hidden, heads):
    blocks, count = hidden.shape[:2]
    group = hidden_group(blocks)
    steps = blocks // group

    def body(where, weights, hidden_ref, y_ref, acc, held, sems):
        i = pl.program_id(0)
        down = block_lanes(where, weights, held, sems, 8 * heads + blocks, group, steps)
        part = nt(jnp.concatenate([hidden_ref[j] for j in range(group)], 1), down)

        @pl.when(i == 0)
        def _():
            acc[...] = part

        @pl.when(i > 0)
        def _():
            acc[...] = acc[...] + part

        @pl.when(i == steps - 1)
        def _():
            y_ref[...] = acc[...].astype(BF16)

    return call(
        body, places, steps,
        [(everyone, ANY), (hidden, pl.BlockSpec((group, count, HEAD), lambda i, _: (i, 0, 0)))],
        [((count, D), BF16, None)],
        [pltpu.VMEM((count, D), F32)] + lanes_scratch(group),
    )[0]


def cross_back(places, everyone, cot, after_two, part, other, mod, query, key, value, pre, key_pre, vecs, heads):
    count, text = query.shape[0], key.shape[0]

    def body(_, cot_ref, after_ref, part_ref, other_ref, mod_ref, q_ref, k_ref, v_ref, pre_ref, key_ref, vec_ref, weight, dx_ref, low_ref, dq_ref, dk_ref, dv_ref, sums, q_acc, k_acc):
        h = pl.program_id(0)

        @pl.when(h == 0)
        def _():
            da = part_ref[...].astype(F32) + other_ref[...].astype(F32)
            back, _ = normed_back(after_ref[...], da * (1.0 + mod_ref[4:5]))
            dx = cot_ref[...] + back
            dx_ref[...] = dx
            low_ref[...] = dx.astype(BF16)
            q_acc[...] = jnp.zeros_like(q_acc)
            k_acc[...] = jnp.zeros_like(k_acc)

        do = nn(low_ref[...], weight[0]).astype(BF16)
        q, k = q_ref[...], k_ref[...]
        chance = softmax(nt(q, k) * SCALING)
        dp = nt(do, v_ref[...])
        ds = (chance * (dp - jnp.sum(chance * dp, -1, keepdims=True))).astype(BF16)
        dv_ref[0] = tn(chance.astype(BF16), do).astype(BF16)
        dq = nn(ds, k) * SCALING
        dk = tn(ds, q) * SCALING
        dq_ref[...] = dq
        dk_ref[...] = dk
        q_acc[...] = q_acc[...] + wide(jnp.sum(pre_ref[...] * vec_ref[8:9] * dq, -1, keepdims=True))
        k_acc[...] = k_acc[...] + wide(jnp.sum(key_ref[...] * vec_ref[9:10] * dk, -1, keepdims=True))

        @pl.when(h == heads - 1)
        def _():
            sums[...] = pack_sums(q_acc[:, 0:1], k_acc[:, 0:1])

    return call(
        body, places, heads,
        [(v, None) for v in (cot, after_two, part, other, mod)]
        + [
            (query, head_lanes(count)), (key, head_lanes(text)), (value, head_lanes(text)),
            (pre, head_lanes(count)), (key_pre, head_lanes(text)),
            (vecs, head_lanes(vecs.shape[0])), (everyone, block_at(7 * heads)),
        ],
        [
            ((count, D), F32, None),
            ((count, D), BF16, None),
            (query.shape, F32, head_lanes(count)),
            (key.shape, F32, head_lanes(text)),
            ((heads, text, HEAD), BF16, pl.BlockSpec((1, text, HEAD), lambda h, _: (h, 0, 0))),
            ((count, HEAD), F32, None),
        ],
        [pltpu.VMEM((count, HEAD), F32), pltpu.VMEM((text, HEAD), F32)],
    )


def norm_grad(pre, inverse, gain, incoming, total):
    grad = inverse * (gain * incoming) - pre * (inverse * inverse * inverse) * (total / D)
    low = grad.astype(BF16)
    return low, total_of(low.astype(F32)), total_of(incoming * pre * inverse)


def cross_back_rows(places, everyone, pre, key_pre, dq, dk, dv, squares, squares_other, sums, sums_other, vecs, heads):
    count, text = pre.shape[0], key_pre.shape[0]

    def body(_, pre_ref, key_ref, dq_ref, dk_ref, dv_ref, sq_ref, sqo_ref, sum_ref, sumo_ref, vec_ref, weight, gq_ref, gk_ref, vec_out, da_ref, acc):
        h = pl.program_id(0)
        squares_all = sq_ref[...] + sqo_ref[...]
        total = sum_ref[...] + sumo_ref[...]
        q_inv = lax.rsqrt(squares_all[:, 0:1] / D + NORM_EPS)
        k_inv = lax.rsqrt(unpack_text(squares_all, text) / D + NORM_EPS)
        low_q, bias_q, gain_q = norm_grad(pre_ref[...], q_inv, vec_ref[8:9], dq_ref[...], total[:, 0:1])
        low_k, bias_k, gain_k = norm_grad(
            key_ref[...], k_inv, vec_ref[9:10], dk_ref[...], unpack_text(total, text)
        )
        gq_ref[0] = low_q
        gk_ref[0] = low_k
        bias_v = total_of(dv_ref[0].astype(F32))
        vec_out[...] = jnp.concatenate(
            [bias_q, bias_k, bias_v, gain_q, gain_k, jnp.zeros((3, HEAD), F32)], 0
        )
        part = nt(low_q, weight[0])

        @pl.when(h == 0)
        def _():
            acc[...] = part

        @pl.when(h > 0)
        def _():
            acc[...] = acc[...] + part

        @pl.when(h == heads - 1)
        def _():
            da_ref[...] = acc[...].astype(BF16)

    tall = pl.BlockSpec((1, count, HEAD), lambda h, _: (h, 0, 0))
    tall_text = pl.BlockSpec((1, text, HEAD), lambda h, _: (h, 0, 0))
    return call(
        body, places, heads,
        [
            (pre, head_lanes(count)), (key_pre, head_lanes(text)), (dq, head_lanes(count)),
            (dk, head_lanes(text)), (dv, tall_text), (squares, None), (squares_other, None),
            (sums, None), (sums_other, None), (vecs, head_lanes(vecs.shape[0])),
            (everyone, block_at(4 * heads)),
        ],
        [
            ((heads, count, HEAD), BF16, tall),
            ((heads, text, HEAD), BF16, tall_text),
            ((8, heads * HEAD), F32, head_lanes(8)),
            ((count, D), BF16, None),
        ],
        [pltpu.VMEM((count, D), F32)],
    )


def self_back(places, everyone, dx_two, after_one, part, other, mod, shared, branch, query, key, value, pre, vecs, cos_tab, sin_tab, heads, tokens):
    count = query.shape[0]

    def body(_, dx_in, after_ref, part_ref, other_ref, mod_ref, shared_ref, branch_ref, q_ref, k_ref, v_ref, pre_ref, vec_ref, cos_ref, sin_ref, weight, dx_ref, low_ref, d_ref, dv_ref, sums, vec_out, q_acc, k_acc):
        h = pl.program_id(0)

        @pl.when(h == 0)
        def _():
            da = part_ref[...].astype(F32) + other_ref[...].astype(F32)
            back, _ = normed_back(after_ref[...], da * shared_ref[3:4])
            dx = dx_in[...] + back
            dx_ref[...] = dx
            low = (mod_ref[2:3] * dx).astype(BF16)
            low_ref[...] = low
            vec_out[0:1] = 0.5 * total_of(low.astype(F32))
            vec_out[1:2] = 0.5 * total_of(dx * branch_ref[...])
            q_acc[...] = jnp.zeros_like(q_acc)
            k_acc[...] = jnp.zeros_like(k_acc)

        do = nn(low_ref[...], weight[0]).astype(BF16)
        q, k = q_ref[...], k_ref[...]
        chance = softmax(self_scores(q, k, tokens))
        dp = nt(do, v_ref[...])
        ds = (chance * (dp - jnp.sum(chance * dp, -1, keepdims=True))).astype(BF16)
        dv_ref[0] = tn(chance.astype(BF16), do).astype(BF16)
        cos, sin = cos_ref[...], -sin_ref[...]
        dq = turned(nn(ds, k) * SCALING, cos, sin)
        dk = turned(tn(ds, q) * SCALING, cos, sin)
        d_ref[0] = dq
        d_ref[1] = dk
        q_acc[...] = q_acc[...] + wide(jnp.sum(pre_ref[0] * vec_ref[3:4] * dq, -1, keepdims=True))
        k_acc[...] = k_acc[...] + wide(jnp.sum(pre_ref[1] * vec_ref[4:5] * dk, -1, keepdims=True))

        @pl.when(h == heads - 1)
        def _():
            lane = lax.broadcasted_iota(jnp.int32, q_acc.shape, 1)
            sums[...] = jnp.where(lane < 64, q_acc[...], k_acc[...])

    lanes = head_lanes(count)
    pair = pl.BlockSpec((2, count, HEAD), lambda h, _: (0, 0, h))
    return call(
        body, places, heads,
        [(v, None) for v in (dx_two, after_one, part, other, mod, shared, branch)]
        + [
            (query, lanes), (key, lanes), (value, lanes), (pre, pair),
            (vecs, head_lanes(vecs.shape[0])), (cos_tab, None), (sin_tab, None),
            (everyone, block_at(3 * heads)),
        ],
        [
            ((count, D), F32, None),
            ((count, D), BF16, None),
            (pre.shape, F32, pair),
            ((heads, count, HEAD), BF16, pl.BlockSpec((1, count, HEAD), lambda h, _: (h, 0, 0))),
            ((count, HEAD), F32, None),
            ((2, D), F32, None),
        ],
        [pltpu.VMEM((count, HEAD), F32), pltpu.VMEM((count, HEAD), F32)],
    )


def self_back_rows(places, everyone, rows, pre, grads, dv, squares, squares_other, sums, sums_other, vecs, heads):
    count = pre.shape[1]

    def body(_, rows_ref, pre_ref, d_ref, dv_ref, sq_ref, sqo_ref, sum_ref, sumo_ref, vec_ref, wq, wk, wv, gq_ref, gk_ref, vec_out, da_ref, row_out, acc):
        h = pl.program_id(0)
        squares_all = sq_ref[...] + sqo_ref[...]
        total = sum_ref[...] + sumo_ref[...]
        lows, biases, gains = [], [], []
        for n in range(2):
            inverse = lax.rsqrt(squares_all[:, 64 * n : 64 * n + 1] / D + NORM_EPS)
            low, bias, gain = norm_grad(
                pre_ref[n], inverse, vec_ref[3 + n : 4 + n], d_ref[n], total[:, 64 * n : 64 * n + 1]
            )
            lows.append(low)
            biases.append(bias)
            gains.append(gain)
        gq_ref[0] = lows[0]
        gk_ref[0] = lows[1]
        dv_low = dv_ref[0]
        bias_v = total_of(dv_low.astype(F32))
        vec_out[...] = jnp.concatenate(
            [biases[0], biases[1], bias_v, gains[0], gains[1], jnp.zeros((3, HEAD), F32)], 0
        )
        part = nt(
            jnp.concatenate([lows[0], lows[1], dv_low], 1),
            jnp.concatenate([wq[0], wk[0], wv[0]], 1),
        )

        @pl.when(h == 0)
        def _():
            acc[...] = part

        @pl.when(h > 0)
        def _():
            acc[...] = acc[...] + part

        @pl.when(h == heads - 1)
        def _():
            da = acc[...]
            da_ref[...] = da.astype(BF16)
            row_out[0:1] = total_of(da)
            row_out[1:2] = total_of(da * normed(rows_ref[...])[0])

    tall = pl.BlockSpec((1, count, HEAD), lambda h, _: (h, 0, 0))
    pair = pl.BlockSpec((2, count, HEAD), lambda h, _: (0, 0, h))
    return call(
        body, places, heads,
        [
            (rows, None), (pre, pair), (grads, pair), (dv, tall), (squares, None), (squares_other, None),
            (sums, None), (sums_other, None), (vecs, head_lanes(vecs.shape[0])),
            (everyone, block_at(0)), (everyone, block_at(heads)), (everyone, block_at(2 * heads)),
        ],
        [
            ((heads, count, HEAD), BF16, tall),
            ((heads, count, HEAD), BF16, tall),
            ((8, heads * HEAD), F32, head_lanes(8)),
            ((count, D), BF16, None),
            ((2, D), F32, None),
        ],
        [pltpu.VMEM((count, D), F32)],
    )


def shared_sums(places, after_one, after_two, grad_two, grad_three, cot, da_two, da_three, y_three, shared):
    def body(_, x1_ref, x2_ref, dy2, dy3, cot_ref, da2, da3, y3, shared_ref, out):
        out[...] = jnp.zeros_like(out)
        out[1:2] = 0.5 * total_of(dy2[...].astype(F32))
        out[2:3] = 0.5 * total_of(dy3[...].astype(F32))
        part = da3[...].astype(F32)
        out[3:4] = total_of(part * normed(x1_ref[...])[0])
        out[4:5] = total_of(part)
        part = da2[...].astype(F32)
        out[8:9] = total_of(part)
        out[9:10] = total_of(part * normed(x2_ref[...])[0])
        out[10:11] = total_of(cot_ref[...] * (y3[...].astype(F32) + 0.5 * shared_ref[2:3]))

    return call(
        body, places, 1,
        [(v, None) for v in (after_one, after_two, grad_two, grad_three, cot, da_two, da_three, y_three, shared)],
        [(shared.shape, F32, None)],
    )[0]


def body(
    latents,
    context,
    cotangent,
    positions,
    step_ids,
    owners,
    time_table,
    master,
    first_moment,
    second_moment,
    head_params,
    head_first,
    head_second,
    shared_params,
    shared_first,
    shared_second,
):
    tensors = lax.axis_size("tensor")
    devices = lax.axis_size("dp")
    slot_count = master.shape[1]
    tile_count = owners.shape[0]
    heads_here = HEADS // tensors
    blocks_here = FF // (HEAD * tensors)
    width_here = D // tensors
    places, holder = owner_layout(owners, slot_count, devices)
    scales = tile_scales(tile_count, heads_here, blocks_here)
    my_slots = lax.dynamic_slice_in_dim(holder, lax.axis_index("dp") * slot_count, slot_count)
    rank = pair_rank()
    filled = my_slots >= 0
    slot_scale = jnp.where(filled, scales[jnp.maximum(my_slots, 0)], 0.0)
    scaled = (master[0] * slot_scale[:, None, None]).astype(jnp.bfloat16)
    half = latents.shape[0]
    tokens = 2 * half
    count = -(-tokens // 16) * 16
    taller = ((0, -half % 16), (0, 0))
    small = jnp.concatenate(
        [
            head_params[0],
            positions.reshape(-1).astype(jnp.float32),
            step_ids.astype(jnp.float32),
        ]
    )
    packed = jnp.pad(small, (0, -small.shape[0] % 1024)).reshape(-1, HEAD)
    everyone, lats, cots, context, packed = gather_slots(
        scaled, jnp.pad(latents, taller), jnp.pad(cotangent, taller), context, packed
    )
    small = packed.reshape(-1)
    vectors = small[: head_params.shape[1]]
    small = small[head_params.shape[1] :]
    positions = small[: positions.size].reshape(positions.shape)
    step = small[positions.size]
    vecs = vectors[: 10 * width_here].reshape(10, width_here)
    up_bias = vectors[10 * width_here :].reshape(1, -1)
    chosen = (step == jnp.arange(TSTEPS)).astype(jnp.float32)
    mod = shared_params[5:11] + jnp.einsum(
        "s,skd->kd", chosen, time_table, precision=lax.Precision.HIGHEST
    )
    cos_tab, sin_tab = rope_tables(positions, HEAD)
    sin_tab = jnp.where(jnp.arange(HEAD) % 2 == 0, -sin_tab, sin_tab)
    cos_tab, sin_tab = (jnp.pad(t, ((0, count - tokens), (0, 0))) for t in (cos_tab, sin_tab))

    def all_rows(halves):
        rows = jnp.concatenate([halves[0, :half], halves[1, :half]], 0)
        return jnp.pad(rows, ((0, count - tokens), (0, 0))).astype(jnp.float32)

    def upright(rows):
        return jnp.pad(rows, ((0, context.shape[0] - rows.shape[0]), (0, 0))).T

    def beside(*values):
        return lax.optimization_barrier(values)

    rows, cot = all_rows(lats), all_rows(cots)
    low_one, pre_one, value_one, squares_one = project_self(
        places, everyone, rows, mod, vecs, heads_here
    )
    squares_one_other = pair_swap(squares_one)
    query_one, key_one, heads_one, part_one = attend_self(
        places, everyone, pre_one, value_one, squares_one, squares_one_other, vecs, cos_tab,
        sin_tab, heads_here, tokens,
    )
    part_one, context = beside(part_one, context)
    part_one_other = pair_swap(part_one)
    key_pre, value_two, text_squares = project_text(places, everyone, context, vecs, heads_here)
    left_context, left_one = upright(context), upright(low_one)
    part_one_other, key_pre, left_context, left_one = beside(
        part_one_other, key_pre, left_context, left_one
    )
    branch_one, after_one, low_two, pre_two, squares_two = project_cross(
        places, everyone, rows, part_one, part_one_other, mod, shared_params, vecs,
        text_squares, heads_here,
    )
    squares_two_other = pair_swap(squares_two)
    query_two, key_two, heads_two, part_two = attend_cross(
        places, everyone, pre_two, key_pre, value_two, squares_two, squares_two_other, vecs,
        heads_here,
    )
    part_two, cot, low_two = beside(part_two, cot, low_two)
    part_two_other = pair_swap(part_two)
    grad_three, d_act = hidden_back(places, everyone, mod, cot, heads_here, blocks_here)
    left_two, left_grad_three = upright(low_two), upright(grad_three)
    part_two_other, d_act, left_two, left_grad_three = beside(
        part_two_other, d_act, left_two, left_grad_three
    )
    after_two, low_three, hidden, d_hidden, d_up_bias, da_two = hidden_both(
        places, everyone, after_one, part_two, part_two_other, mod, shared_params, d_act, up_bias,
        heads_here, blocks_here,
    )
    da_two_other = pair_swap(da_two)
    y_three = hidden_out(places, everyone, hidden, heads_here)
    left_three = upright(low_three)
    da_two_other, y_three, left_three = beside(da_two_other, y_three, left_three)
    dx_two, grad_two, dq_two, dk_two, dv_two, sums_two = cross_back(
        places, everyone, cot, after_two, da_two, da_two_other, mod, query_two, key_two,
        value_two, pre_two, key_pre, vecs, heads_here,
    )
    query_grad_two, key_grad_two, vecs_two, da_three = cross_back_rows(
        places, everyone, pre_two, key_pre, dq_two, dk_two, dv_two, squares_two,
        squares_two_other, sums_two, pair_swap(sums_two), vecs, heads_here,
    )
    da_three_other = pair_swap(da_three)
    shared_grad = shared_sums(
        places, after_one, after_two, grad_two, grad_three, cot, da_two, da_three, y_three,
        shared_params,
    )
    left_grad_two = upright(grad_two)
    da_three_other, shared_grad, left_grad_two = beside(da_three_other, shared_grad, left_grad_two)
    dx_one, grad_one, d_one, dv_one, sums_one, rows_a = self_back(
        places, everyone, dx_two, after_one, da_three, da_three_other, mod, shared_params,
        branch_one, query_one, key_one, value_one, pre_one, vecs, cos_tab, sin_tab, heads_here,
        tokens,
    )
    query_grad_one, key_grad_one, vecs_one, da_one, rows_b = self_back_rows(
        places, everyone, rows, pre_one, d_one, dv_one, squares_one, squares_one_other, sums_one,
        pair_swap(sums_one), vecs, heads_here,
    )
    shared_grad = jnp.concatenate(
        [rows_a[0:1], shared_grad[1:5], rows_b, rows_a[1:2], shared_grad[8:]], 0
    )
    head_grad = jnp.concatenate(
        [vecs_one[:5].reshape(-1), vecs_two[:5].reshape(-1), d_up_bias.reshape(-1)]
    )
    tensor_rank = lax.axis_index("tensor")
    head_padded = jnp.where(jnp.arange(tensors)[:, None] == rank, head_grad[None, :], 0.0)
    vector = jnp.concatenate([head_padded.reshape(-1), shared_grad.reshape(-1)])
    vector = jnp.pad(vector, (0, -vector.shape[0] % 1024)).reshape(-1, 128)
    parts, vector, output, grad_input = reduce_slots(
        holder,
        kind_of_blocks(tile_count, heads_here, blocks_here),
        (left_one, upright(grad_one), left_two, left_context, left_grad_two, left_three, left_grad_three),
        (
            query_grad_one,
            key_grad_one,
            dv_one,
            heads_one,
            query_grad_two,
            key_grad_two,
            dv_two,
            heads_two,
            d_hidden,
            hidden,
        ),
        vector,
        (rows, after_two, dx_one, y_three, da_one),
        jnp.concatenate([mod[5:6], mod[1:2], shared_params[2:3], jnp.zeros((5, D), F32)], 0),
        slot_count,
    )
    output, grad_input = (
        jnp.where(lax.axis_index("tensor") == 0, v[:half], v[half:tokens])
        for v in (output, grad_input)
    )
    new_master, new_first, new_second = adam_slots(
        parts, master, first_moment, second_moment, slot_scale, filled
    )
    vector = vector.reshape(-1)
    head_total = vector[: head_padded.size].reshape(head_padded.shape)
    shared_total = vector[head_padded.size : head_padded.size + shared_grad.size]
    shared_total = shared_total.reshape(shared_grad.shape)
    mine_head = lax.dynamic_slice_in_dim(head_total, tensor_rank, 1, 0)
    new_head, new_head_first, new_head_second = adam_step(
        head_params, mine_head, head_first, head_second, VECTOR_RATE, 0.0
    )
    new_shared, new_shared_first, new_shared_second = adam_step(
        shared_params, shared_total, shared_first, shared_second, VECTOR_RATE, 0.0
    )
    return (
        output,
        grad_input,
        new_master,
        new_first,
        new_second,
        new_head,
        new_head_first,
        new_head_second,
        new_shared,
        new_shared_first,
        new_shared_second,
    )


def solution(mesh):
    return jax.shard_map(
        body,
        mesh=mesh,
        in_specs=(
            P(("dp", "tensor"), None),
            P("dp", None),
            P(("dp", "tensor"), None),
            P(None, "dp"),
            P("dp"),
            P(),
            P(),
            P("tensor", "dp", None, None),
            P("tensor", "dp", None, None),
            P("tensor", "dp", None, None),
            P("tensor", None),
            P("tensor", None),
            P("tensor", None),
            P(),
            P(),
            P(),
        ),
        out_specs=(
            P(("dp", "tensor"), None),
            P(("dp", "tensor"), None),
            P("tensor", "dp", None, None),
            P("tensor", "dp", None, None),
            P("tensor", "dp", None, None),
            P("tensor", None),
            P("tensor", None),
            P("tensor", None),
            P(),
            P(),
            P(),
        ),
        check_vma=False,
    )
```

```python
import functools

import jax
import jax.numpy as jnp
from jax import lax
from jax.experimental import pallas as pl
from jax.experimental.pallas import tpu as pltpu
from jax.sharding import PartitionSpec as P

D = 1536
HEADS = 12
HEAD = 128
FF = 8960
TSTEPS = 16
STEPC = 10


NORM_EPS = 1e-06
BETA_ONE = 0.9
BETA_TWO = 0.999
ADAM_EPS = 1e-08
TILE_RATE = 1.0
TILE_DECAY = 0.1
VECTOR_RATE = 0.5
GELU_COEF = 0.7978845608028654


def rope_tables(token_places, head_size):
    sixths = head_size // 6
    frame_pairs = (head_size - 4 * sixths) // 2
    frame_freq = 10000.0 ** (-jnp.arange(frame_pairs, dtype=jnp.float32) / frame_pairs)
    side_freq = 10000.0 ** (-jnp.arange(sixths, dtype=jnp.float32) / sixths)
    spots = token_places.astype(jnp.float32)
    angles = jnp.concatenate(
        [
            spots[0][..., None] * frame_freq,
            spots[1][..., None] * side_freq,
            spots[2][..., None] * side_freq,
        ],
        -1,
    )
    angles = jnp.repeat(angles, 2, axis=-1)
    return (jnp.cos(angles), jnp.sin(angles))


def owner_layout(owners, slot_count, devices):
    indices = jnp.arange(owners.shape[0], dtype=jnp.int32)
    same_owner = (owners[:, None] == owners[None, :]) & (indices[None, :] < indices[:, None])
    slot_of = jnp.sum(same_owner.astype(jnp.int32), axis=1)
    places = owners * slot_count + slot_of
    spots = jnp.arange(slot_count * devices, dtype=jnp.int32)
    holder = (
        jnp.sum(jnp.where(places[None, :] == spots[:, None], indices[None, :] + 1, 0), axis=1) - 1
    )
    return (places, holder)


def tile_scales(tile_count, heads_here, blocks_here):
    indices = jnp.arange(tile_count)
    scale_in = D ** (-0.5)
    scale_out = HEADS ** (-0.5)
    scale_down = FF ** (-0.5)
    scales = jnp.where(
        indices < 3 * heads_here,
        scale_in,
        jnp.where(
            indices < 4 * heads_here,
            scale_out,
            jnp.where(
                indices < 7 * heads_here,
                scale_in,
                jnp.where(
                    indices < 8 * heads_here,
                    scale_out,
                    jnp.where(indices < 8 * heads_here + blocks_here, scale_in, scale_down),
                ),
            ),
        ),
    )
    return scales.astype(jnp.float32)


def adam_step(weight, gradient, moment_one, moment_two, step_rate, decay_rate):
    first_new = BETA_ONE * moment_one + (1.0 - BETA_ONE) * gradient
    second_new = BETA_TWO * moment_two + (1.0 - BETA_TWO) * gradient * gradient
    first_hat = first_new / (1.0 - BETA_ONE**STEPC)
    second_hat = second_new / (1.0 - BETA_TWO**STEPC)
    weight_new = weight - step_rate * (
        first_hat / (jnp.sqrt(second_hat) + ADAM_EPS) + decay_rate * weight
    )
    return (weight_new, first_new, second_new)


MESH = pl.DeviceIdType.MESH
ANY = pl.BlockSpec(memory_space=pl.ANY)
MIB = 1 << 20


def chip_pairs():
    return lax.axis_size("dp") == 16 and lax.axis_size("tensor") == 2


def pair_rank():
    if chip_pairs():
        return (lax.axis_index("dp") // 4) % 2
    return lax.axis_index("tensor")


def pair_swap(value):
    if chip_pairs():
        return lax.ppermute(value, "dp", [(i, i ^ 4) for i in range(16)])
    return lax.ppermute(value, "tensor", [(0, 1), (1, 0)])


def pair_sums(*values):
    stacked = jnp.concatenate([v.reshape(-1) for v in values])
    total = stacked + pair_swap(stacked)
    out, at = [], 0
    for v in values:
        out.append(total[at : at + v.size].reshape(v.shape))
        at += v.size
    return tuple(out)


def place_of():
    chip, core = lax.axis_index("dp"), lax.axis_index("tensor")
    z, y, x = chip // 4, (chip // 2) % 2, chip % 2
    return chip, core, z, y, x


def column_of(z, y, x, k):
    high, low_bit = z // 2, z % 2
    if k & 2:
        high = 1 - high
    if k & 1:
        low_bit = 1 - low_bit
    return (2 * high + low_bit) * 4 + 2 * y + x


def greet(chip, core, z, y, x):
    barrier = pltpu.get_barrier_semaphore()
    friends = []
    for k in range(4):
        for flip in (0, 1):
            if k or flip:
                friends.append((column_of(z, y, x, k), core if flip == 0 else 1 - core))
    friends.append((column_of(z, y, 1 - x, 0), core))
    friends.append((column_of(z, 1 - y, x, 0), core))
    for friend in friends:
        pl.semaphore_signal(barrier, inc=1, device_id=friend, device_id_type=MESH)
    pl.semaphore_wait(barrier, len(friends))


def gather_kernel(
    own, lat, cot, text, small, out, lats, cots, texts, smalls, clip_s, clip_r,
    near_s, col_r,
    x_s, x_r, y_s, y_r, ra_s, ra_r, rb_s, rb_r, sib_s, sib_r,
):
    chip, core, z, y, x = place_of()
    rank = z % 2
    half = own.shape[1] // 2
    part = half // 2
    at_x = column_of(z, y, 1 - x, 0)
    at_y = column_of(z, 1 - y, x, 0)
    greet(chip, core, z, y, x)

    def rows(ref, unit, first, count):
        return ref.at[unit, :, pl.ds(pl.multiple_of(first, 16), count), :]

    def remote(unit, first, count, send, recv, device):
        piece = rows(out, unit, first, count)
        return pltpu.make_async_remote_copy(
            src_ref=piece, dst_ref=piece, send_sem=send, recv_sem=recv,
            device_id=device, device_id_type=MESH,
        )

    started = []
    for j in range(2):
        zh = z // 2 if j == 0 else 1 - z // 2
        target = (2 * zh + core) * 4 + 2 * y + x
        for h in range(2):
            src = own.at[:, pl.ds(h * half, half), :]
            dst = out.at[chip, :, pl.ds(h * half, half), :]
            go = pltpu.make_async_remote_copy(
                src_ref=src, dst_ref=dst, send_sem=near_s.at[2 * j + h], recv_sem=col_r.at[z],
                device_id=(target, h), device_id_type=MESH,
            )
            if j == 0:
                here = pltpu.make_async_copy(src, dst, col_r.at[z])
                stays = jnp.logical_and(rank == core, core == h)

                @pl.when(stays)
                def _():
                    here.start()

                @pl.when(jnp.logical_not(stays))
                def _():
                    go.start()

                started.append((go, stays))
            else:
                go.start()
                started.append((go, None))

    pair_chip = column_of(z, y, x, 1)
    rows_of_text = text.shape[0] // 2

    def clip_pieces(h):
        share = pl.ds(h * rows_of_text, rows_of_text)
        return ((lat, lats.at[h]), (cot, cots.at[h]), (text.at[share], texts.at[share]))

    home = rank == core
    trade = pltpu.make_async_remote_copy(
        src_ref=small, dst_ref=smalls, send_sem=clip_s.at[6], recv_sem=clip_r.at[6],
        device_id=(pair_chip, 1 - core), device_id_type=MESH,
    )
    keep = pltpu.make_async_copy(small, smalls, clip_r.at[6])

    @pl.when(home)
    def _():
        keep.start()

    @pl.when(jnp.logical_not(home))
    def _():
        trade.start()

    def hand_out(h, n, wait):
        src, dst = clip_pieces(h)[n]
        far = pltpu.make_async_remote_copy(
            src_ref=src, dst_ref=dst, send_sem=clip_s.at[n], recv_sem=clip_r.at[3 * h + n],
            device_id=(pair_chip, rank), device_id_type=MESH,
        )
        near = pltpu.make_async_remote_copy(
            src_ref=src, dst_ref=dst, send_sem=clip_s.at[3 + n], recv_sem=clip_r.at[3 * h + n],
            device_id=(chip, 1 - core), device_id_type=MESH,
        )
        here = pltpu.make_async_copy(src, dst, clip_r.at[3 * h + n])

        @pl.when(core == h)
        def _():
            if wait:
                far.wait_send()
            else:
                far.start()

            @pl.when(home)
            def _():
                if not wait:
                    here.start()

            @pl.when(jnp.logical_not(home))
            def _():
                if wait:
                    near.wait_send()
                else:
                    near.start()

    for n in range(3):
        for h in range(2):
            hand_out(h, n, False)

    def column_in(k):
        unit = column_of(z, y, x, k)
        source_z = unit // 4
        piece = rows(out, unit, core * half, half)
        pltpu.make_async_copy(piece, piece, col_r.at[source_z]).wait()
        to_x = remote(unit, core * half, half, x_s.at[k], x_r.at[k], (at_x, core))
        to_y = remote(unit, core * half, half, y_s.at[k], y_r.at[k], (at_y, core))
        to_sib = remote(unit, core * half, half, sib_s.at[k], sib_r.at[k], (chip, 1 - core))
        to_x.start()
        to_y.start()
        to_sib.start()
        return [to_x, to_y, to_sib]

    def side_in(k):
        ux = column_of(z, y, 1 - x, k)
        uy = column_of(z, 1 - y, x, k)
        remote(ux, core * half, half, x_s.at[k], x_r.at[k], (at_x, core)).wait_recv()
        on_y = remote(ux, core * half + part, part, rb_s.at[k], rb_r.at[k], (at_y, core))
        on_y.start()
        sib_x = remote(ux, core * half, half, sib_s.at[4 + k], sib_r.at[4 + k], (chip, 1 - core))
        sib_x.start()
        remote(uy, core * half, half, y_s.at[k], y_r.at[k], (at_y, core)).wait_recv()
        on_x = remote(uy, core * half, part, ra_s.at[k], ra_r.at[k], (at_x, core))
        on_x.start()
        sib_y = remote(uy, core * half, half, sib_s.at[8 + k], sib_r.at[8 + k], (chip, 1 - core))
        sib_y.start()
        return [on_y, sib_x, on_x, sib_y]

    def corner_in(k):
        unit = column_of(z, 1 - y, 1 - x, k)
        remote(unit, core * half, part, ra_s.at[k], ra_r.at[k], (at_x, core)).wait_recv()
        sib_a = remote(unit, core * half, part, sib_s.at[12 + k], sib_r.at[12 + k], (chip, 1 - core))
        sib_a.start()
        remote(unit, core * half + part, part, rb_s.at[k], rb_r.at[k], (at_y, core)).wait_recv()
        sib_b = remote(
            unit, core * half + part, part, sib_s.at[16 + k], sib_r.at[16 + k], (chip, 1 - core)
        )
        sib_b.start()
        return [sib_a, sib_b]

    sent = []
    for step in range(6):
        if step < 4:
            sent += column_in(step)
        if 1 <= step < 5:
            sent += side_in(step - 1)
        if step >= 2:
            sent += corner_in(step - 2)
    for copy in sent:
        copy.wait_send()
    for go, stays in started:
        if stays is None:
            go.wait_send()
        else:

            @pl.when(jnp.logical_not(stays))
            def _():
                go.wait_send()

    for n in range(3):
        for h in range(2):
            hand_out(h, n, True)
            dst = clip_pieces(h)[n][1]
            pltpu.make_async_copy(dst, dst, clip_r.at[3 * h + n]).wait()

    @pl.when(jnp.logical_not(home))
    def _():
        trade.wait_send()

    pltpu.make_async_copy(smalls, smalls, clip_r.at[6]).wait()

    other = (1 - core) * half
    for k in range(4):
        for at, (yy, xx) in ((0, (y, x)), (4, (y, 1 - x)), (8, (1 - y, x))):
            remote(
                column_of(z, yy, xx, k), other, half, sib_s.at[at + k], sib_r.at[at + k],
                (chip, 1 - core),
            ).wait_recv()
        corner = column_of(z, 1 - y, 1 - x, k)
        remote(
            corner, other, part, sib_s.at[12 + k], sib_r.at[12 + k], (chip, 1 - core)
        ).wait_recv()
        remote(
            corner, other + part, part, sib_s.at[16 + k], sib_r.at[16 + k], (chip, 1 - core)
        ).wait_recv()


def gather_slots(scaled, lat, cot, text, small):
    if not chip_pairs():
        everyone = lax.all_gather(scaled, "dp", axis=0, tiled=True)
        lats, cots = (lax.all_gather(v, "tensor") for v in (lat, cot))
        return everyone, lats, cots, text, small
    dma = pltpu.SemaphoreType.DMA
    counts = (7, 7, 4, 4, 4, 4, 4, 4, 4, 4, 4, 4, 20, 20)
    everyone, *rest = pl.pallas_call(
        gather_kernel,
        out_shape=[
            jax.ShapeDtypeStruct((16,) + scaled.shape, scaled.dtype),
            jax.ShapeDtypeStruct((2,) + lat.shape, lat.dtype),
            jax.ShapeDtypeStruct((2,) + cot.shape, cot.dtype),
            jax.ShapeDtypeStruct(text.shape, text.dtype),
            jax.ShapeDtypeStruct(small.shape, small.dtype),
        ],
        in_specs=[ANY] * 5,
        out_specs=[ANY] * 5,
        scratch_shapes=[dma((n,)) for n in counts],
        compiler_params=pltpu.CompilerParams(
            collective_id=0, has_side_effects=True, vmem_limit_bytes=4 * MIB
        ),
    )(scaled, lat, cot, text, small)
    return everyone.reshape((-1,) + scaled.shape[1:]), *rest


def toggled(z, y, x, flip_y, flip_x, k):
    high = (z // 2 + k // 2) % 2
    low_bit = (z % 2 + k % 2) % 2
    return (2 * high + low_bit) * 4 + 2 * ((y + flip_y) % 2) + (x + flip_x) % 2


def reduce_kernel(
    kind, block, *refs,
):
    (
        *pieces, rows_in, after_in, dx_in, y_in, da_in, gains, vec_in,
        final, vec_out, result, result_grad, y_other, da_other, from_sib, from_x, from_y, corner_a, corner_b,
        left, right, ring, corners, side_x, side_y, middle, stage, vec_box,
        load_s, stage_s, sib_s, sib_r, x_s, x_r, y_s, y_r, ca_s, ca_r, cb_s, cb_r, f_s, f_r, v_s, v_r,
        end_s, end_r,
    ) = refs
    chip, core, z, y, x = place_of()
    rank = z % 2
    slots, width, lanes = final.shape[1:]
    half = width // 2
    part = half // 2
    at_x = toggled(z, y, x, 0, 1, 0)
    at_y = toggled(z, y, x, 1, 0, 0)
    sibling = (chip, 1 - core)
    mates = (
        sibling,
        (at_x, core),
        (at_y, core),
        (toggled(z, y, x, 0, 0, 1), core),
        (toggled(z, y, x, 0, 0, 2), core),
    )

    kinds = left.shape[0]
    depth = right.shape[1]
    loads = [
        pltpu.make_async_copy(pieces[i], left.at[i], load_s.at[i]) for i in range(kinds)
    ]
    first = 0
    blank = []
    for i, piece in enumerate(pieces[kinds:]):
        number, rows = piece.shape[:2]
        loads.append(
            pltpu.make_async_copy(
                piece, right.at[pl.ds(first, number), pl.ds(0, rows), :], load_s.at[kinds + i]
            )
        )
        if rows < depth:
            blank.append((first, number, rows))
        first += number
    for load in loads:
        load.start()
    for start, number, rows in blank:

        def clear(i, carry):
            right[start + i, pl.ds(rows, depth - rows), :] = jnp.zeros(
                (depth - rows, lanes), right.dtype
            )
            return carry

        lax.fori_loop(0, number, clear, 0)
    right[first] = jnp.zeros((depth, lanes), right.dtype)
    vec_out[...] = vec_in[...]
    greet(chip, core, z, y, x)
    for load in loads:
        load.wait()

    def remote(src, dst, send, recv, device):
        return pltpu.make_async_remote_copy(
            src_ref=src, dst_ref=dst, send_sem=send, recv_sem=recv,
            device_id=device, device_id_type=MESH,
        )

    batch = ring.shape[1]
    batches = slots // batch
    turns = 4 * batches
    deep = corners.shape[0]

    def flips(s):
        return 3 - s // batches

    def sums(q, s, first, terms, total):
        unit = toggled(z, y, x, 1 - q % 2, 1 - q // 2, flips(s))
        base = unit * slots + (s % batches) * batch
        count = total.shape[1]

        def one(i, carry):
            slot = base + i
            rows = pl.ds(pl.multiple_of(first, 128), count)
            acc = jnp.dot(
                left[kind[slot], rows, :], right[block[slot]], preferred_element_type=jnp.float32
            )
            for term in terms:
                acc = acc + term[i].astype(jnp.float32)
            total[i] = acc.astype(total.dtype)
            return carry

        lax.fori_loop(0, batch, one, 0)

    mine, other = core * half, (1 - core) * half

    def sub(ref, first):
        return ref.at[:, pl.ds(first, part), :]

    def sib_copy(q, s):
        i = turns * q + s
        return remote(ring.at[q], from_sib.at[i], sib_s.at[i], sib_r.at[i], sibling)

    def a_copy(s):
        return remote(
            sub(corners.at[s % deep], 0), corner_a.at[s], ca_s.at[s], ca_r.at[s], (at_x, core)
        )

    def b_copy(s):
        return remote(
            sub(corners.at[s % deep], part), corner_b.at[s], cb_s.at[s], cb_r.at[s], (at_y, core)
        )

    def x_copy(s, n):
        rows = pl.ds(n * part, part)
        i = turns * n + s
        return remote(
            side_x.at[s % deep, :, rows, :], from_x.at[s, :, rows, :], x_s.at[i], x_r.at[i],
            (at_x, core),
        )

    def y_copy(s, n):
        rows = pl.ds((1 - n) * part, part)
        i = turns * n + s
        return remote(
            side_y.at[s % deep, :, rows, :], from_y.at[s, :, rows, :], y_s.at[i], y_r.at[i],
            (at_y, core),
        )

    def f_copy(s):
        src = middle.at[s % deep]
        g = s % batches
        dst = final.at[
            z // 2, pl.ds(g * batch, batch), pl.ds(pl.multiple_of(mine, 128), half), :
        ]
        recv = f_r.at[(2 * (z // 2) + core) * batches + g]
        target = (toggled(z, y, x, 0, 0, flips(s)), rank)
        return remote(src, dst, f_s.at[s], recv, target), pltpu.make_async_copy(src, dst, recv)

    def stays(s):
        return jnp.logical_and(s >= turns - batches, rank == core)

    def staged(source, place, i):
        copy = pltpu.make_async_copy(source, place, stage_s.at[i])
        copy.start()
        return copy

    def for_sibling(s):
        def one(q, carry):
            @pl.when(s >= 1)
            def _():
                sib_copy(q, s - 1).wait_send()

            sums(q, s, other, (), ring.at[q])
            sib_copy(q, s).start()
            return carry

        lax.fori_loop(0, 4, one, 0)

    def corner(s):
        sib_copy(0, s).wait_recv()
        in_sib = staged(from_sib.at[s], stage.at[0], 0)

        @pl.when(s >= deep)
        def _():
            a_copy(s - deep).wait_send()
            b_copy(s - deep).wait_send()

        in_sib.wait()
        sums(0, s, mine, (stage.at[0],), corners.at[s % deep])
        a_copy(s).start()
        b_copy(s).start()

    def direct_sides(s):
        sib_copy(1, s).wait_recv()
        in_x = staged(from_sib.at[turns + s], stage.at[0], 0)
        sib_copy(2, s).wait_recv()
        in_y = staged(from_sib.at[2 * turns + s], stage.at[1], 1)

        @pl.when(s >= deep)
        def _():
            for n in range(2):
                x_copy(s - deep, n).wait_send()
                y_copy(s - deep, n).wait_send()

        in_x.wait()
        sums(1, s, mine, (sub(stage.at[0], 0),), sub(side_x.at[s % deep], 0))
        x_copy(s, 0).start()
        in_y.wait()
        sums(2, s, mine + part, (sub(stage.at[1], part),), sub(side_y.at[s % deep], part))
        y_copy(s, 0).start()

    def relayed_sides(s):
        b_copy(s).wait_recv()
        in_b = staged(corner_b.at[s], sub(stage.at[2], 0), 2)
        a_copy(s).wait_recv()
        in_a = staged(corner_a.at[s], sub(stage.at[2], part), 3)
        in_b.wait()
        sums(
            1, s, mine + part, (sub(stage.at[0], part), sub(stage.at[2], 0)),
            sub(side_x.at[s % deep], part),
        )
        x_copy(s, 1).start()
        in_a.wait()
        sums(
            2, s, mine, (sub(stage.at[1], 0), sub(stage.at[2], part)), sub(side_y.at[s % deep], 0)
        )
        y_copy(s, 1).start()

    def centre(s):
        sib_copy(3, s).wait_recv()
        in_sib = staged(from_sib.at[3 * turns + s], stage.at[3], 4)
        x_copy(s, 0).wait_recv()
        x_copy(s, 1).wait_recv()
        in_x = staged(from_x.at[s], stage.at[4], 5)
        y_copy(s, 0).wait_recv()
        y_copy(s, 1).wait_recv()
        in_y = staged(from_y.at[s], stage.at[5], 6)

        @pl.when(s >= deep)
        def _():
            f_copy(s - deep)[0].wait_send()

        in_sib.wait()
        in_x.wait()
        in_y.wait()
        sums(3, s, mine, (stage.at[3], stage.at[4], stage.at[5]), middle.at[s % deep])
        go, here = f_copy(s)

        @pl.when(stays(s))
        def _():
            here.start()

        @pl.when(jnp.logical_not(stays(s)))
        def _():
            go.start()

    home = rank == core
    pair_device = (toggled(z, y, x, 0, 0, 1), core)
    ends = [
        remote(y_in, y_other, end_s.at[0], end_r.at[0], pair_device),
        remote(da_in, da_other, end_s.at[1], end_r.at[1], pair_device),
        remote(result, result, end_s.at[2], end_r.at[2], sibling),
        remote(result_grad, result_grad, end_s.at[3], end_r.at[3], sibling),
    ]

    def finish_rows():
        ends[0].wait_recv()
        ends[1].wait_recv()
        tall = 16
        spec = pl.BlockSpec((tall, width), lambda i: (i, 0))

        def one(x_ref, x2_ref, dx_ref, y_ref, yo_ref, da_ref, dao_ref, out_ref, grad_ref):
            y_all = y_ref[...].astype(F32) + yo_ref[...].astype(F32) + gains[2:3]
            out_ref[...] = (x2_ref[...] + gains[0:1] * y_all).astype(out_ref.dtype)
            da = da_ref[...].astype(F32) + dao_ref[...].astype(F32)
            back, _ = normed_back(x_ref[...], da * (1.0 + gains[1:2]))
            grad_ref[...] = dx_ref[...] + back

        pltpu.emit_pipeline(
            one, grid=(rows_in.shape[0] // tall,), in_specs=[spec] * 7, out_specs=[spec] * 2
        )(rows_in, after_in, dx_in, y_in, y_other, da_in, da_other, result, result_grad)
        ends[2].start()
        ends[3].start()

    @pl.when(jnp.logical_not(home))
    def _():
        ends[0].start()
        ends[1].start()

    def vec_copy(i):
        return remote(vec_out, vec_box.at[i], v_s.at[i], v_r.at[i], mates[i])

    def turn(step, carry):
        for i in range(5):

            @pl.when(step == i)
            def _():
                vec_copy(i).start()

        @pl.when(step < turns)
        def _():
            corner(step)
            direct_sides(step)

        @pl.when(step + 1 < turns)
        def _():
            for_sibling(step + 1)

        @pl.when(step >= 1)
        def _():
            centre(step - 1)

        @pl.when(step < turns)
        def _():
            relayed_sides(step)

        @pl.when(jnp.logical_and(step == turns - batches, home))
        def _():
            finish_rows()

        for i in range(5):

            @pl.when(step == i)
            def _():
                vec_copy(i).wait()
                vec_out[...] = vec_out[...] + vec_box[i]

        return carry

    for_sibling(0)
    lax.fori_loop(0, turns + 1, turn, 0)
    for q in range(4):
        sib_copy(q, turns - 1).wait_send()

    def settle(i, carry):
        s = turns - deep + i
        a_copy(s).wait_send()
        b_copy(s).wait_send()
        for n in range(2):
            x_copy(s, n).wait_send()
            y_copy(s, n).wait_send()

        @pl.when(jnp.logical_not(stays(s)))
        def _():
            f_copy(s)[0].wait_send()

        return carry

    lax.fori_loop(0, deep, settle, 0)

    @pl.when(home)
    def _():
        ends[2].wait_send()
        ends[3].wait_send()

    @pl.when(jnp.logical_not(home))
    def _():
        ends[0].wait_send()
        ends[1].wait_send()
        ends[2].wait_recv()
        ends[3].wait_recv()

    for plane in range(2):
        for h in range(2):
            for g in range(batches):
                piece = final.at[plane, pl.ds(g * batch, batch), pl.ds(h * half, half), :]
                recv = f_r.at[(2 * plane + h) * batches + g]
                pltpu.make_async_copy(piece, piece, recv).wait()


def reduce_slots(holder, kinds, rows, columns, vector, ends, gains, slot_count):
    if not chip_pairs():
        grads = slot_grads(holder, kinds, [r.T for r in rows], columns)
        total = lax.psum_scatter(grads, "dp", scatter_dimension=0, tiled=True)
        x, after, dx, y_part, da_part = ends
        y_all, da_all = (
            v.astype(F32) + pair_swap(v).astype(F32) for v in (y_part, da_part)
        )
        result = (after + gains[0] * (y_all + gains[2])).astype(BF16)
        back, _ = normed_back(x, da_all * (1.0 + gains[1]))
        return total[None], lax.psum(vector, ("dp", "tensor")), result, dx + back
    left = rows
    width, depth = left[0].shape
    lanes = columns[0].shape[2]
    tiles = sum(c.shape[0] for c in columns)
    block = jnp.where(holder >= 0, holder, tiles)
    kind = kinds[jnp.maximum(holder, 0)]
    half = width // 2
    dma = pltpu.SemaphoreType.DMA
    scalars = pl.BlockSpec(memory_space=pltpu.SMEM)
    inside = pl.BlockSpec(memory_space=pltpu.VMEM)
    low = jnp.bfloat16

    batch = max(n for n in (1, 2, 3) if slot_count % n == 0)
    turns = 4 * slot_count // batch
    deep = 3

    def room(count, tall):
        return jax.ShapeDtypeStruct((count, batch, tall, lanes), low)

    def slab(count):
        return pltpu.VMEM((count, batch, half, lanes), low)

    outs = pl.pallas_call(
        reduce_kernel,
        out_shape=[
            jax.ShapeDtypeStruct((2, slot_count, width, lanes), low),
            jax.ShapeDtypeStruct(vector.shape, vector.dtype),
            jax.ShapeDtypeStruct(ends[0].shape, low), jax.ShapeDtypeStruct(ends[0].shape, F32),
            jax.ShapeDtypeStruct(ends[0].shape, low), jax.ShapeDtypeStruct(ends[0].shape, low),
            room(4 * turns, half), room(turns, half), room(turns, half),
            room(turns, half // 2), room(turns, half // 2),
        ],
        in_specs=[scalars, scalars] + [ANY] * (len(left) + len(columns) + 5) + [inside] * 2,
        out_specs=[ANY, inside] + [ANY] * 9,
        scratch_shapes=[
            pltpu.VMEM((len(left), width, depth), low),
            pltpu.VMEM((tiles + 1, depth, lanes), low),
            slab(4), slab(deep), slab(deep), slab(deep), slab(deep), slab(6),
            pltpu.VMEM((5,) + vector.shape, vector.dtype),
        ]
        + [
            dma((n,))
            for n in (len(left) + len(columns), 7)
            + (4 * turns,) * 2
            + (2 * turns,) * 4
            + (turns,) * 6
            + (5, 5, 4, 4)
        ],
        compiler_params=pltpu.CompilerParams(
            collective_id=1, has_side_effects=True, vmem_limit_bytes=48 * MIB
        ),
    )(kind, block, *left, *columns, *ends, gains, vector)
    return outs[:4]


def kind_of_blocks(tile_count, heads_here, blocks_here):
    number = jnp.arange(tile_count)
    kind = number // heads_here
    table = jnp.array([0, 0, 0, 1, 2, 3, 3, 4], jnp.int32)
    late = jnp.where(number < 8 * heads_here + blocks_here, 5, 6)
    return jnp.where(number < 8 * heads_here, table[jnp.minimum(kind, 7)], late).astype(jnp.int32)


def slot_grads(holder, kinds, rows, columns):
    depth = max(r.shape[0] for r in rows)

    def deep(value, axis):
        room = [(0, 0)] * value.ndim
        room[axis] = (0, depth - value.shape[axis])
        return jnp.pad(value, room)

    left = jnp.stack([deep(r, 0) for r in rows])
    right = jnp.concatenate([deep(c, 1) for c in columns], 0)
    slots = holder.shape[0]
    used = (holder >= 0).astype(jnp.int32)
    block = jnp.maximum(holder, 0)
    kind = kinds[block]
    width = rows[0].shape[1]
    lanes = right.shape[2]

    def multiply(kind_ref, block_ref, used_ref, left_ref, right_ref, out_ref):
        slot = pl.program_id(0)

        @pl.when(used_ref[slot] == 1)
        def _():
            out_ref[0] = lax.dot_general(
                left_ref[kind_ref[slot]],
                right_ref[0],
                (((0,), (0,)), ((), ())),
                preferred_element_type=jnp.float32,
            ).astype(out_ref.dtype)

        @pl.when(used_ref[slot] == 0)
        def _():
            out_ref[...] = jnp.zeros_like(out_ref)

    return pl.pallas_call(
        multiply,
        grid_spec=pltpu.PrefetchScalarGridSpec(
            num_scalar_prefetch=3,
            grid=(slots,),
            in_specs=[
                pl.BlockSpec(left.shape, lambda s, kd, b, u: (0, 0, 0)),
                pl.BlockSpec((1, depth, lanes), lambda s, kd, b, u: (b[s], 0, 0)),
            ],
            out_specs=pl.BlockSpec((1, width, lanes), lambda s, kd, b, u: (s, 0, 0)),
        ),
        out_shape=jax.ShapeDtypeStruct((slots, width, lanes), jnp.bfloat16),
        compiler_params=pltpu.CompilerParams(vmem_limit_bytes=48 * MIB),
    )(kind, block, used, left, right)


def adam_slots(planes, master, moment_one, moment_two, slot_scale, filled):
    count, slot_count, width, lanes = planes.shape

    def step(scale_ref, fill_ref, grads, weight, one, two, new_weight, new_one, new_two):
        slot = pl.program_id(0)

        @pl.when(fill_ref[slot] == 1)
        def _():
            total = grads[0, 0].astype(jnp.float32)
            for n in range(1, count):
                total = total + grads[n, 0].astype(jnp.float32)
            results = adam_step(
                weight[0, 0], total * scale_ref[slot], one[0, 0], two[0, 0], TILE_RATE, TILE_DECAY
            )
            for ref, value in zip((new_weight, new_one, new_two), results):
                ref[0, 0] = value

        @pl.when(fill_ref[slot] == 0)
        def _():
            new_weight[...] = weight[...]
            new_one[...] = one[...]
            new_two[...] = two[...]

    deep = pl.BlockSpec((1, 1, width, lanes), lambda s: (0, s, 0, 0))
    scalars = pl.BlockSpec(memory_space=pltpu.SMEM)
    return pl.pallas_call(
        step,
        grid=(slot_count,),
        in_specs=[scalars, scalars, pl.BlockSpec((count, 1, width, lanes), lambda s: (0, s, 0, 0))]
        + [deep] * 3,
        out_specs=[deep] * 3,
        out_shape=[jax.ShapeDtypeStruct(master.shape, jnp.float32)] * 3,
        compiler_params=pltpu.CompilerParams(vmem_limit_bytes=32 * MIB),
    )(
        slot_scale,
        filled.astype(jnp.int32),
        *[
            pltpu.with_memory_space_constraint(v, pltpu.HBM)
            for v in (planes, master, moment_one, moment_two)
        ],
    )


SCALING = HEAD ** (-0.5)
BF16 = jnp.bfloat16
F32 = jnp.float32


def nn(left, right):
    return jnp.dot(left, right, preferred_element_type=F32)


def nt(left, right):
    return lax.dot_general(left, right, (((1,), (1,)), ((), ())), preferred_element_type=F32)


def tn(left, right):
    return lax.dot_general(left, right, (((0,), (0,)), ((), ())), preferred_element_type=F32)


def normed(rows):
    centre = rows - jnp.mean(rows, -1, keepdims=True)
    inverse = lax.rsqrt(jnp.mean(centre * centre, -1, keepdims=True) + NORM_EPS)
    return centre * inverse, inverse


def normed_back(rows, grad):
    unit, inverse = normed(rows)
    mean = jnp.mean(grad, -1, keepdims=True)
    return (grad - mean - unit * jnp.mean(grad * unit, -1, keepdims=True)) * inverse, unit


def total_of(rows):
    return jnp.sum(rows, 0, keepdims=True)


def turned(rows, cos_tab, sin_tab):
    even = lax.broadcasted_iota(jnp.int32, rows.shape, 1) % 2 == 0
    partner = jnp.where(even, pltpu.roll(rows, HEAD - 1, 1), pltpu.roll(rows, 1, 1))
    return rows * cos_tab + partner * sin_tab


def wide(column):
    return jnp.broadcast_to(column, (column.shape[0], HEAD))


def pack_sums(for_rows, for_text=None):
    out = wide(for_rows)
    if for_text is None:
        return out
    lane = lax.broadcasted_iota(jnp.int32, out.shape, 1)
    count = for_text.shape[0] // 2
    rest = jnp.zeros((out.shape[0] - count, HEAD), F32)
    first = jnp.concatenate([wide(for_text[:count]), rest], 0)
    second = jnp.concatenate([wide(for_text[count:]), rest], 0)
    return jnp.where(lane < 32, out, jnp.where(lane < 64, first, second))


def unpack_text(sums, count):
    return jnp.concatenate([sums[: count // 2, 32:33], sums[: count // 2, 64:65]], 0)


def softmax(scores):
    expo = jnp.exp(scores - jnp.max(scores, -1, keepdims=True))
    return expo / jnp.sum(expo, -1, keepdims=True)


def self_scores(query_low, key_low, tokens):
    scores = nt(query_low, key_low) * SCALING
    lane = lax.broadcasted_iota(jnp.int32, scores.shape, 1)
    return jnp.where(lane < tokens, scores, -1e30)


def whole(array):
    zeros = (0,) * len(array.shape)
    return pl.BlockSpec(array.shape, lambda *_: zeros)


def block_at(first, stride=1):
    return pl.BlockSpec((1, D, HEAD), lambda i, where: (where[first + stride * i], 0, 0))


def call(body, places, grid, ins, outs, scratch=(), vmem=24):
    specs = [spec if spec is not None else whole(array) for array, spec in ins]
    shapes = [pltpu.HBM(shape, kind) for shape, kind, _ in outs]
    out_specs = [
        spec if spec is not None else whole(shape) for (_, _, spec), shape in zip(outs, shapes)
    ]
    return pl.pallas_call(
        body,
        grid_spec=pltpu.PrefetchScalarGridSpec(
            num_scalar_prefetch=1,
            grid=(grid,),
            in_specs=specs,
            out_specs=out_specs,
            scratch_shapes=list(scratch),
        ),
        out_shape=shapes,
        compiler_params=pltpu.CompilerParams(vmem_limit_bytes=vmem * MIB),
    )(places, *[pltpu.with_memory_space_constraint(array, pltpu.HBM) for array, _ in ins])


def head_lanes(rows):
    return pl.BlockSpec((rows, HEAD), lambda h, *_: (0, h))


def joined(refs):
    return jnp.concatenate([ref[0] for ref in refs], 1)


def project_self(places, everyone, rows, mod, vecs, heads):
    count = rows.shape[0]
    span = heads * HEAD

    def body(_, rows_ref, mod_ref, vec_ref, *refs):
        weights, (low, pre, value, sums, acc) = refs[:heads], refs[heads:]
        i = pl.program_id(0)

        @pl.when(i == 0)
        def _():
            unit, _ = normed(rows_ref[...])
            low[...] = (unit * (1.0 + mod_ref[1:2]) + mod_ref[0:1]).astype(BF16)

        made = nn(low[...], joined(weights))

        @pl.when(i == 0)
        def _():
            q = made + vec_ref[0:1]
            pre[0] = q
            acc[...] = wide(jnp.sum(q * q, -1, keepdims=True))

        @pl.when(i == 1)
        def _():
            k = made + vec_ref[1:2]
            pre[0] = k
            lane = lax.broadcasted_iota(jnp.int32, acc.shape, 1)
            sums[...] = jnp.where(lane < 64, acc[...], wide(jnp.sum(k * k, -1, keepdims=True)))

        @pl.when(i == 2)
        def _():
            value[...] = (made + vec_ref[2:3]).astype(BF16)

    return call(
        body, places, 3,
        [(rows, None), (mod, None), (vecs, None)]
        + [(everyone, block_at(h, heads)) for h in range(heads)],
        [
            ((count, D), BF16, None),
            ((2, count, span), F32, pl.BlockSpec((1, count, span), lambda i, _: (jnp.minimum(i, 1), 0, 0))),
            ((count, span), BF16, None),
            ((count, HEAD), F32, None),
        ],
        [pltpu.VMEM((count, HEAD), F32)],
    )


def attend_self(places, everyone, pre, value, sums, other, vecs, cos_tab, sin_tab, heads, tokens):
    count = value.shape[0]

    def body(_, pre_ref, value_ref, sum_ref, other_ref, vec_ref, cos_ref, sin_ref, weight, q_ref, k_ref, o_ref, y_ref, acc):
        h = pl.program_id(0)
        total = sum_ref[...] + other_ref[...]
        q_inv = lax.rsqrt(total[:, 0:1] / D + NORM_EPS)
        k_inv = lax.rsqrt(total[:, 64:65] / D + NORM_EPS)
        cos, sin = cos_ref[...], sin_ref[...]
        q = turned(pre_ref[0] * q_inv * vec_ref[3:4], cos, sin).astype(BF16)
        k = turned(pre_ref[1] * k_inv * vec_ref[4:5], cos, sin).astype(BF16)
        q_ref[...] = q
        k_ref[...] = k
        chance = softmax(self_scores(q, k, tokens))
        out = nn(chance.astype(BF16), value_ref[...]).astype(BF16)
        o_ref[0] = out
        part = nt(out, weight[0])

        @pl.when(h == 0)
        def _():
            acc[...] = part

        @pl.when(h > 0)
        def _():
            acc[...] = acc[...] + part

        @pl.when(h == heads - 1)
        def _():
            y_ref[...] = acc[...].astype(BF16)

    lanes = head_lanes(count)
    return call(
        body, places, heads,
        [
            (pre, pl.BlockSpec((2, count, HEAD), lambda h, _: (0, 0, h))),
            (value, lanes), (sums, None), (other, None),
            (vecs, head_lanes(vecs.shape[0])), (cos_tab, None), (sin_tab, None),
            (everyone, block_at(3 * heads)),
        ],
        [
            (value.shape, BF16, lanes),
            (value.shape, BF16, lanes),
            ((heads, count, HEAD), BF16, pl.BlockSpec((1, count, HEAD), lambda h, _: (h, 0, 0))),
            ((count, D), BF16, None),
        ],
        [pltpu.VMEM((count, D), F32)],
    )


def project_text(places, everyone, context, vecs, heads):
    count = context.shape[0]
    span = heads * HEAD

    def body(_, text_ref, vec_ref, *refs):
        weights, (key, value, sums) = refs[:heads], refs[heads:]
        i = pl.program_id(0)
        made = nn(text_ref[...], joined(weights))

        @pl.when(i == 0)
        def _():
            k = made + vec_ref[6:7]
            key[...] = k
            sums[...] = wide(jnp.sum(k * k, -1, keepdims=True))

        @pl.when(i == 1)
        def _():
            value[...] = (made + vec_ref[7:8]).astype(BF16)

    return call(
        body, places, 2,
        [(context, None), (vecs, None)]
        + [(everyone, block_at(5 * heads + h, heads)) for h in range(heads)],
        [((count, span), F32, None), ((count, span), BF16, None), ((count, HEAD), F32, None)],
    )


def project_cross(places, everyone, rows, part, other, mod, shared, vecs, text_sums, heads):
    count = rows.shape[0]
    span = heads * HEAD
    text = text_sums.shape[0]

    def body(_, rows_ref, part_ref, other_ref, mod_ref, shared_ref, vec_ref, text_ref, *refs):
        weights, (branch, after, low, pre, sums) = refs[:heads], refs[heads:]
        y = part_ref[...].astype(F32) + other_ref[...].astype(F32) + shared_ref[0:1]
        branch[...] = y
        x = rows_ref[...] + mod_ref[2:3] * y
        after[...] = x
        unit, _ = normed(x)
        a = (unit * shared_ref[3:4] + shared_ref[4:5]).astype(BF16)
        low[...] = a
        q = nn(a, joined(weights)) + vec_ref[5:6]
        pre[...] = q
        sums[...] = pack_sums(jnp.sum(q * q, -1, keepdims=True), text_ref[:, 0:1])

    return call(
        body, places, 1,
        [(v, None) for v in (rows, part, other, mod, shared, vecs, text_sums)]
        + [(everyone, block_at(4 * heads + h)) for h in range(heads)],
        [
            ((count, D), F32, None),
            ((count, D), F32, None),
            ((count, D), BF16, None),
            ((count, span), F32, None),
            ((count, HEAD), F32, None),
        ],
    )


def attend_cross(places, everyone, pre, key_pre, value, sums, other, vecs, heads):
    count, text = pre.shape[0], value.shape[0]

    def body(_, pre_ref, key_ref, value_ref, sum_ref, other_ref, vec_ref, weight, q_ref, k_ref, o_ref, y_ref, acc):
        h = pl.program_id(0)
        total = sum_ref[...] + other_ref[...]
        q_inv = lax.rsqrt(total[:, 0:1] / D + NORM_EPS)
        k_inv = lax.rsqrt(unpack_text(total, text) / D + NORM_EPS)
        q = (pre_ref[...] * q_inv * vec_ref[8:9]).astype(BF16)
        k = (key_ref[...] * k_inv * vec_ref[9:10]).astype(BF16)
        q_ref[...] = q
        k_ref[...] = k
        chance = softmax(nt(q, k) * SCALING)
        out = nn(chance.astype(BF16), value_ref[...]).astype(BF16)
        o_ref[0] = out
        part = nt(out, weight[0])

        @pl.when(h == 0)
        def _():
            acc[...] = part

        @pl.when(h > 0)
        def _():
            acc[...] = acc[...] + part

        @pl.when(h == heads - 1)
        def _():
            y_ref[...] = acc[...].astype(BF16)

    return call(
        body, places, heads,
        [
            (pre, head_lanes(count)), (key_pre, head_lanes(text)), (value, head_lanes(text)),
            (sums, None), (other, None), (vecs, head_lanes(vecs.shape[0])),
            (everyone, block_at(7 * heads)),
        ],
        [
            (pre.shape, BF16, head_lanes(count)),
            (value.shape, BF16, head_lanes(text)),
            ((heads, count, HEAD), BF16, pl.BlockSpec((1, count, HEAD), lambda h, _: (h, 0, 0))),
            ((count, D), BF16, None),
        ],
        [pltpu.VMEM((count, D), F32)],
    )


def hidden_group(blocks):
    return max(g for g in (5, 4, 3, 2, 1) if blocks % g == 0)


def block_lanes(where, everyone, held, sems, first, group, steps):
    i = pl.program_id(0)

    def fetch(step, act):
        slot = step % 2
        for j in range(group):
            copy = pltpu.make_async_copy(
                everyone.at[where[first + step * group + j]],
                held.at[slot, :, pl.ds(j * HEAD, HEAD)],
                sems.at[slot, j],
            )
            copy.start() if act else copy.wait()

    @pl.when(i == 0)
    def _():
        fetch(0, True)

    @pl.when(i + 1 < steps)
    def _():
        fetch(i + 1, True)

    fetch(i, False)
    return held[i % 2]


def lanes_scratch(group):
    return [pltpu.VMEM((2, D, group * HEAD), BF16), pltpu.SemaphoreType.DMA((2, group))]


def hidden_back(places, everyone, mod, cot, heads, blocks):
    count = cot.shape[0]
    group = hidden_group(blocks)
    steps = blocks // group

    def body(where, weights, mod_ref, cot_ref, grad, out, held, sems):
        @pl.when(pl.program_id(0) == 0)
        def _():
            grad[...] = (mod_ref[5:6] * cot_ref[...]).astype(BF16)

        down = block_lanes(where, weights, held, sems, 8 * heads + blocks, group, steps)
        out[...] = nn(grad[...], down).astype(BF16)

    return call(
        body, places, steps,
        [(everyone, ANY), (mod, None), (cot, None)],
        [
            ((count, D), BF16, None),
            ((count, blocks * HEAD), BF16, pl.BlockSpec((count, group * HEAD), lambda i, _: (0, i))),
        ],
        lanes_scratch(group),
    )


def hidden_both(places, everyone, after_one, part, other, mod, shared, d_act, up_bias, heads, blocks):
    count = after_one.shape[0]
    group = hidden_group(blocks)
    steps = blocks // group
    span = group * HEAD

    def body(where, weights, after_ref, part_ref, other_ref, mod_ref, shared_ref, d_ref, bias_ref, after, low, hidden, d_hidden, d_bias, da_ref, acc, held, sems):
        i = pl.program_id(0)

        @pl.when(i == 0)
        def _():
            x = after_ref[...] + part_ref[...].astype(F32) + other_ref[...].astype(F32)
            x = x + shared_ref[1:2]
            after[...] = x
            unit, _ = normed(x)
            low[...] = (unit * (1.0 + mod_ref[4:5]) + mod_ref[3:4]).astype(BF16)
            acc[...] = jnp.zeros_like(acc)

        up = block_lanes(where, weights, held, sems, 8 * heads, group, steps)
        pre = nn(low[...], up) + bias_ref[...]
        square = pre * pre
        bent = jnp.tanh(GELU_COEF * (pre + 0.044715 * pre * square))
        act = (0.5 * pre * (1.0 + bent)).astype(BF16)
        slope = 0.5 * (1.0 + bent) + 0.5 * pre * (1.0 - bent * bent) * (
            GELU_COEF * (1.0 + 3.0 * 0.044715 * square)
        )
        dh = (d_ref[...].astype(F32) * slope).astype(BF16)
        d_bias[...] = total_of(dh.astype(F32))
        for j in range(group):
            hidden[j] = act[:, j * HEAD : (j + 1) * HEAD]
            d_hidden[j] = dh[:, j * HEAD : (j + 1) * HEAD]
        acc[...] = acc[...] + nt(dh, up)

        @pl.when(i == steps - 1)
        def _():
            da_ref[...] = acc[...].astype(BF16)

    tall = pl.BlockSpec((group, count, HEAD), lambda i, _: (i, 0, 0))
    flat = pl.BlockSpec((1, span), lambda i, _: (0, i))
    return call(
        body, places, steps,
        [(everyone, ANY)]
        + [(v, None) for v in (after_one, part, other, mod, shared)]
        + [(d_act, pl.BlockSpec((count, span), lambda i, _: (0, i))), (up_bias, flat)],
        [
            ((count, D), F32, None),
            ((count, D), BF16, None),
            ((blocks, count, HEAD), BF16, tall),
            ((blocks, count, HEAD), BF16, tall),
            (up_bias.shape, F32, flat),
            ((count, D), BF16, None),
        ],
        [pltpu.VMEM((count, D), F32)] + lanes_scratch(group),
        vmem=32,
    )


def hidden_out(places, everyone, hidden, heads):
    blocks, count = hidden.shape[:2]
    group = hidden_group(blocks)
    steps = blocks // group

    def body(where, weights, hidden_ref, y_ref, acc, held, sems):
        i = pl.program_id(0)
        down = block_lanes(where, weights, held, sems, 8 * heads + blocks, group, steps)
        part = nt(jnp.concatenate([hidden_ref[j] for j in range(group)], 1), down)

        @pl.when(i == 0)
        def _():
            acc[...] = part

        @pl.when(i > 0)
        def _():
            acc[...] = acc[...] + part

        @pl.when(i == steps - 1)
        def _():
            y_ref[...] = acc[...].astype(BF16)

    return call(
        body, places, steps,
        [(everyone, ANY), (hidden, pl.BlockSpec((group, count, HEAD), lambda i, _: (i, 0, 0)))],
        [((count, D), BF16, None)],
        [pltpu.VMEM((count, D), F32)] + lanes_scratch(group),
    )[0]


def cross_back(places, everyone, cot, after_two, part, other, mod, query, key, value, pre, key_pre, vecs, heads):
    count, text = query.shape[0], key.shape[0]

    def body(_, cot_ref, after_ref, part_ref, other_ref, mod_ref, q_ref, k_ref, v_ref, pre_ref, key_ref, vec_ref, weight, dx_ref, low_ref, dq_ref, dk_ref, dv_ref, sums, q_acc, k_acc):
        h = pl.program_id(0)

        @pl.when(h == 0)
        def _():
            da = part_ref[...].astype(F32) + other_ref[...].astype(F32)
            back, _ = normed_back(after_ref[...], da * (1.0 + mod_ref[4:5]))
            dx = cot_ref[...] + back
            dx_ref[...] = dx
            low_ref[...] = dx.astype(BF16)
            q_acc[...] = jnp.zeros_like(q_acc)
            k_acc[...] = jnp.zeros_like(k_acc)

        do = nn(low_ref[...], weight[0]).astype(BF16)
        q, k = q_ref[...], k_ref[...]
        chance = softmax(nt(q, k) * SCALING)
        dp = nt(do, v_ref[...])
        ds = (chance * (dp - jnp.sum(chance * dp, -1, keepdims=True))).astype(BF16)
        dv_ref[0] = tn(chance.astype(BF16), do).astype(BF16)
        dq = nn(ds, k) * SCALING
        dk = tn(ds, q) * SCALING
        dq_ref[...] = dq
        dk_ref[...] = dk
        q_acc[...] = q_acc[...] + wide(jnp.sum(pre_ref[...] * vec_ref[8:9] * dq, -1, keepdims=True))
        k_acc[...] = k_acc[...] + wide(jnp.sum(key_ref[...] * vec_ref[9:10] * dk, -1, keepdims=True))

        @pl.when(h == heads - 1)
        def _():
            sums[...] = pack_sums(q_acc[:, 0:1], k_acc[:, 0:1])

    return call(
        body, places, heads,
        [(v, None) for v in (cot, after_two, part, other, mod)]
        + [
            (query, head_lanes(count)), (key, head_lanes(text)), (value, head_lanes(text)),
            (pre, head_lanes(count)), (key_pre, head_lanes(text)),
            (vecs, head_lanes(vecs.shape[0])), (everyone, block_at(7 * heads)),
        ],
        [
            ((count, D), F32, None),
            ((count, D), BF16, None),
            (query.shape, F32, head_lanes(count)),
            (key.shape, F32, head_lanes(text)),
            ((heads, text, HEAD), BF16, pl.BlockSpec((1, text, HEAD), lambda h, _: (h, 0, 0))),
            ((count, HEAD), F32, None),
        ],
        [pltpu.VMEM((count, HEAD), F32), pltpu.VMEM((text, HEAD), F32)],
    )


def norm_grad(pre, inverse, gain, incoming, total):
    grad = inverse * (gain * incoming) - pre * (inverse * inverse * inverse) * (total / D)
    low = grad.astype(BF16)
    return low, total_of(low.astype(F32)), total_of(incoming * pre * inverse)


def cross_back_rows(places, everyone, pre, key_pre, dq, dk, dv, squares, squares_other, sums, sums_other, vecs, heads):
    count, text = pre.shape[0], key_pre.shape[0]

    def body(_, pre_ref, key_ref, dq_ref, dk_ref, dv_ref, sq_ref, sqo_ref, sum_ref, sumo_ref, vec_ref, weight, gq_ref, gk_ref, vec_out, da_ref, acc):
        h = pl.program_id(0)
        squares_all = sq_ref[...] + sqo_ref[...]
        total = sum_ref[...] + sumo_ref[...]
        q_inv = lax.rsqrt(squares_all[:, 0:1] / D + NORM_EPS)
        k_inv = lax.rsqrt(unpack_text(squares_all, text) / D + NORM_EPS)
        low_q, bias_q, gain_q = norm_grad(pre_ref[...], q_inv, vec_ref[8:9], dq_ref[...], total[:, 0:1])
        low_k, bias_k, gain_k = norm_grad(
            key_ref[...], k_inv, vec_ref[9:10], dk_ref[...], unpack_text(total, text)
        )
        gq_ref[0] = low_q
        gk_ref[0] = low_k
        bias_v = total_of(dv_ref[0].astype(F32))
        vec_out[...] = jnp.concatenate(
            [bias_q, bias_k, bias_v, gain_q, gain_k, jnp.zeros((3, HEAD), F32)], 0
        )
        part = nt(low_q, weight[0])

        @pl.when(h == 0)
        def _():
            acc[...] = part

        @pl.when(h > 0)
        def _():
            acc[...] = acc[...] + part

        @pl.when(h == heads - 1)
        def _():
            da_ref[...] = acc[...].astype(BF16)

    tall = pl.BlockSpec((1, count, HEAD), lambda h, _: (h, 0, 0))
    tall_text = pl.BlockSpec((1, text, HEAD), lambda h, _: (h, 0, 0))
    return call(
        body, places, heads,
        [
            (pre, head_lanes(count)), (key_pre, head_lanes(text)), (dq, head_lanes(count)),
            (dk, head_lanes(text)), (dv, tall_text), (squares, None), (squares_other, None),
            (sums, None), (sums_other, None), (vecs, head_lanes(vecs.shape[0])),
            (everyone, block_at(4 * heads)),
        ],
        [
            ((heads, count, HEAD), BF16, tall),
            ((heads, text, HEAD), BF16, tall_text),
            ((8, heads * HEAD), F32, head_lanes(8)),
            ((count, D), BF16, None),
        ],
        [pltpu.VMEM((count, D), F32)],
    )


def self_back(places, everyone, dx_two, after_one, part, other, mod, shared, branch, query, key, value, pre, vecs, cos_tab, sin_tab, heads, tokens):
    count = query.shape[0]

    def body(_, dx_in, after_ref, part_ref, other_ref, mod_ref, shared_ref, branch_ref, q_ref, k_ref, v_ref, pre_ref, vec_ref, cos_ref, sin_ref, weight, dx_ref, low_ref, d_ref, dv_ref, sums, vec_out, q_acc, k_acc):
        h = pl.program_id(0)

        @pl.when(h == 0)
        def _():
            da = part_ref[...].astype(F32) + other_ref[...].astype(F32)
            back, _ = normed_back(after_ref[...], da * shared_ref[3:4])
            dx = dx_in[...] + back
            dx_ref[...] = dx
            low = (mod_ref[2:3] * dx).astype(BF16)
            low_ref[...] = low
            vec_out[0:1] = 0.5 * total_of(low.astype(F32))
            vec_out[1:2] = 0.5 * total_of(dx * branch_ref[...])
            q_acc[...] = jnp.zeros_like(q_acc)
            k_acc[...] = jnp.zeros_like(k_acc)

        do = nn(low_ref[...], weight[0]).astype(BF16)
        q, k = q_ref[...], k_ref[...]
        chance = softmax(self_scores(q, k, tokens))
        dp = nt(do, v_ref[...])
        ds = (chance * (dp - jnp.sum(chance * dp, -1, keepdims=True))).astype(BF16)
        dv_ref[0] = tn(chance.astype(BF16), do).astype(BF16)
        cos, sin = cos_ref[...], -sin_ref[...]
        dq = turned(nn(ds, k) * SCALING, cos, sin)
        dk = turned(tn(ds, q) * SCALING, cos, sin)
        d_ref[0] = dq
        d_ref[1] = dk
        q_acc[...] = q_acc[...] + wide(jnp.sum(pre_ref[0] * vec_ref[3:4] * dq, -1, keepdims=True))
        k_acc[...] = k_acc[...] + wide(jnp.sum(pre_ref[1] * vec_ref[4:5] * dk, -1, keepdims=True))

        @pl.when(h == heads - 1)
        def _():
            lane = lax.broadcasted_iota(jnp.int32, q_acc.shape, 1)
            sums[...] = jnp.where(lane < 64, q_acc[...], k_acc[...])

    lanes = head_lanes(count)
    pair = pl.BlockSpec((2, count, HEAD), lambda h, _: (0, 0, h))
    return call(
        body, places, heads,
        [(v, None) for v in (dx_two, after_one, part, other, mod, shared, branch)]
        + [
            (query, lanes), (key, lanes), (value, lanes), (pre, pair),
            (vecs, head_lanes(vecs.shape[0])), (cos_tab, None), (sin_tab, None),
            (everyone, block_at(3 * heads)),
        ],
        [
            ((count, D), F32, None),
            ((count, D), BF16, None),
            (pre.shape, F32, pair),
            ((heads, count, HEAD), BF16, pl.BlockSpec((1, count, HEAD), lambda h, _: (h, 0, 0))),
            ((count, HEAD), F32, None),
            ((2, D), F32, None),
        ],
        [pltpu.VMEM((count, HEAD), F32), pltpu.VMEM((count, HEAD), F32)],
    )


def self_back_rows(places, everyone, rows, pre, grads, dv, squares, squares_other, sums, sums_other, vecs, heads):
    count = pre.shape[1]

    def body(_, rows_ref, pre_ref, d_ref, dv_ref, sq_ref, sqo_ref, sum_ref, sumo_ref, vec_ref, wq, wk, wv, gq_ref, gk_ref, vec_out, da_ref, row_out, acc):
        h = pl.program_id(0)
        squares_all = sq_ref[...] + sqo_ref[...]
        total = sum_ref[...] + sumo_ref[...]
        lows, biases, gains = [], [], []
        for n in range(2):
            inverse = lax.rsqrt(squares_all[:, 64 * n : 64 * n + 1] / D + NORM_EPS)
            low, bias, gain = norm_grad(
                pre_ref[n], inverse, vec_ref[3 + n : 4 + n], d_ref[n], total[:, 64 * n : 64 * n + 1]
            )
            lows.append(low)
            biases.append(bias)
            gains.append(gain)
        gq_ref[0] = lows[0]
        gk_ref[0] = lows[1]
        dv_low = dv_ref[0]
        bias_v = total_of(dv_low.astype(F32))
        vec_out[...] = jnp.concatenate(
            [biases[0], biases[1], bias_v, gains[0], gains[1], jnp.zeros((3, HEAD), F32)], 0
        )
        part = nt(
            jnp.concatenate([lows[0], lows[1], dv_low], 1),
            jnp.concatenate([wq[0], wk[0], wv[0]], 1),
        )

        @pl.when(h == 0)
        def _():
            acc[...] = part

        @pl.when(h > 0)
        def _():
            acc[...] = acc[...] + part

        @pl.when(h == heads - 1)
        def _():
            da = acc[...]
            da_ref[...] = da.astype(BF16)
            row_out[0:1] = total_of(da)
            row_out[1:2] = total_of(da * normed(rows_ref[...])[0])

    tall = pl.BlockSpec((1, count, HEAD), lambda h, _: (h, 0, 0))
    pair = pl.BlockSpec((2, count, HEAD), lambda h, _: (0, 0, h))
    return call(
        body, places, heads,
        [
            (rows, None), (pre, pair), (grads, pair), (dv, tall), (squares, None), (squares_other, None),
            (sums, None), (sums_other, None), (vecs, head_lanes(vecs.shape[0])),
            (everyone, block_at(0)), (everyone, block_at(heads)), (everyone, block_at(2 * heads)),
        ],
        [
            ((heads, count, HEAD), BF16, tall),
            ((heads, count, HEAD), BF16, tall),
            ((8, heads * HEAD), F32, head_lanes(8)),
            ((count, D), BF16, None),
            ((2, D), F32, None),
        ],
        [pltpu.VMEM((count, D), F32)],
    )


def shared_sums(places, after_one, after_two, grad_two, grad_three, cot, da_two, da_three, y_three, shared):
    def body(_, x1_ref, x2_ref, dy2, dy3, cot_ref, da2, da3, y3, shared_ref, out):
        out[...] = jnp.zeros_like(out)
        out[1:2] = 0.5 * total_of(dy2[...].astype(F32))
        out[2:3] = 0.5 * total_of(dy3[...].astype(F32))
        part = da3[...].astype(F32)
        out[3:4] = total_of(part * normed(x1_ref[...])[0])
        out[4:5] = total_of(part)
        part = da2[...].astype(F32)
        out[8:9] = total_of(part)
        out[9:10] = total_of(part * normed(x2_ref[...])[0])
        out[10:11] = total_of(cot_ref[...] * (y3[...].astype(F32) + 0.5 * shared_ref[2:3]))

    return call(
        body, places, 1,
        [(v, None) for v in (after_one, after_two, grad_two, grad_three, cot, da_two, da_three, y_three, shared)],
        [(shared.shape, F32, None)],
    )[0]


def body(
    latents,
    context,
    cotangent,
    positions,
    step_ids,
    owners,
    time_table,
    master,
    first_moment,
    second_moment,
    head_params,
    head_first,
    head_second,
    shared_params,
    shared_first,
    shared_second,
):
    tensors = lax.axis_size("tensor")
    devices = lax.axis_size("dp")
    slot_count = master.shape[1]
    tile_count = owners.shape[0]
    heads_here = HEADS // tensors
    blocks_here = FF // (HEAD * tensors)
    width_here = D // tensors
    places, holder = owner_layout(owners, slot_count, devices)
    scales = tile_scales(tile_count, heads_here, blocks_here)
    my_slots = lax.dynamic_slice_in_dim(holder, lax.axis_index("dp") * slot_count, slot_count)
    rank = pair_rank()
    filled = my_slots >= 0
    slot_scale = jnp.where(filled, scales[jnp.maximum(my_slots, 0)], 0.0)
    scaled = (master[0] * slot_scale[:, None, None]).astype(jnp.bfloat16)
    half = latents.shape[0]
    tokens = 2 * half
    count = -(-tokens // 16) * 16
    taller = ((0, -half % 16), (0, 0))
    small = jnp.concatenate(
        [
            head_params[0],
            positions.reshape(-1).astype(jnp.float32),
            step_ids.astype(jnp.float32),
        ]
    )
    packed = jnp.pad(small, (0, -small.shape[0] % 1024)).reshape(-1, HEAD)
    everyone, lats, cots, context, packed = gather_slots(
        scaled, jnp.pad(latents, taller), jnp.pad(cotangent, taller), context, packed
    )
    small = packed.reshape(-1)
    vectors = small[: head_params.shape[1]]
    small = small[head_params.shape[1] :]
    positions = small[: positions.size].reshape(positions.shape)
    step = small[positions.size]
    vecs = vectors[: 10 * width_here].reshape(10, width_here)
    up_bias = vectors[10 * width_here :].reshape(1, -1)
    chosen = (step == jnp.arange(TSTEPS)).astype(jnp.float32)
    mod = shared_params[5:11] + jnp.einsum(
        "s,skd->kd", chosen, time_table, precision=lax.Precision.HIGHEST
    )
    cos_tab, sin_tab = rope_tables(positions, HEAD)
    sin_tab = jnp.where(jnp.arange(HEAD) % 2 == 0, -sin_tab, sin_tab)
    cos_tab, sin_tab = (jnp.pad(t, ((0, count - tokens), (0, 0))) for t in (cos_tab, sin_tab))

    def all_rows(halves):
        rows = jnp.concatenate([halves[0, :half], halves[1, :half]], 0)
        return jnp.pad(rows, ((0, count - tokens), (0, 0))).astype(jnp.float32)

    def upright(rows):
        return jnp.pad(rows, ((0, context.shape[0] - rows.shape[0]), (0, 0))).T

    def beside(*values):
        return lax.optimization_barrier(values)

    rows, cot = all_rows(lats), all_rows(cots)
    low_one, pre_one, value_one, squares_one = project_self(
        places, everyone, rows, mod, vecs, heads_here
    )
    squares_one_other = pair_swap(squares_one)
    query_one, key_one, heads_one, part_one = attend_self(
        places, everyone, pre_one, value_one, squares_one, squares_one_other, vecs, cos_tab,
        sin_tab, heads_here, tokens,
    )
    part_one, context = beside(part_one, context)
    part_one_other = pair_swap(part_one)
    key_pre, value_two, text_squares = project_text(places, everyone, context, vecs, heads_here)
    left_context, left_one = upright(context), upright(low_one)
    part_one_other, key_pre, left_context, left_one = beside(
        part_one_other, key_pre, left_context, left_one
    )
    branch_one, after_one, low_two, pre_two, squares_two = project_cross(
        places, everyone, rows, part_one, part_one_other, mod, shared_params, vecs,
        text_squares, heads_here,
    )
    squares_two_other = pair_swap(squares_two)
    query_two, key_two, heads_two, part_two = attend_cross(
        places, everyone, pre_two, key_pre, value_two, squares_two, squares_two_other, vecs,
        heads_here,
    )
    part_two, cot, low_two = beside(part_two, cot, low_two)
    part_two_other = pair_swap(part_two)
    grad_three, d_act = hidden_back(places, everyone, mod, cot, heads_here, blocks_here)
    left_two, left_grad_three = upright(low_two), upright(grad_three)
    part_two_other, d_act, left_two, left_grad_three = beside(
        part_two_other, d_act, left_two, left_grad_three
    )
    after_two, low_three, hidden, d_hidden, d_up_bias, da_two = hidden_both(
        places, everyone, after_one, part_two, part_two_other, mod, shared_params, d_act, up_bias,
        heads_here, blocks_here,
    )
    da_two_other = pair_swap(da_two)
    y_three = hidden_out(places, everyone, hidden, heads_here)
    left_three = upright(low_three)
    da_two_other, y_three, left_three = beside(da_two_other, y_three, left_three)
    dx_two, grad_two, dq_two, dk_two, dv_two, sums_two = cross_back(
        places, everyone, cot, after_two, da_two, da_two_other, mod, query_two, key_two,
        value_two, pre_two, key_pre, vecs, heads_here,
    )
    query_grad_two, key_grad_two, vecs_two, da_three = cross_back_rows(
        places, everyone, pre_two, key_pre, dq_two, dk_two, dv_two, squares_two,
        squares_two_other, sums_two, pair_swap(sums_two), vecs, heads_here,
    )
    da_three_other = pair_swap(da_three)
    shared_grad = shared_sums(
        places, after_one, after_two, grad_two, grad_three, cot, da_two, da_three, y_three,
        shared_params,
    )
    left_grad_two = upright(grad_two)
    da_three_other, shared_grad, left_grad_two = beside(da_three_other, shared_grad, left_grad_two)
    dx_one, grad_one, d_one, dv_one, sums_one, rows_a = self_back(
        places, everyone, dx_two, after_one, da_three, da_three_other, mod, shared_params,
        branch_one, query_one, key_one, value_one, pre_one, vecs, cos_tab, sin_tab, heads_here,
        tokens,
    )
    query_grad_one, key_grad_one, vecs_one, da_one, rows_b = self_back_rows(
        places, everyone, rows, pre_one, d_one, dv_one, squares_one, squares_one_other, sums_one,
        pair_swap(sums_one), vecs, heads_here,
    )
    shared_grad = jnp.concatenate(
        [rows_a[0:1], shared_grad[1:5], rows_b, rows_a[1:2], shared_grad[8:]], 0
    )
    head_grad = jnp.concatenate(
        [vecs_one[:5].reshape(-1), vecs_two[:5].reshape(-1), d_up_bias.reshape(-1)]
    )
    tensor_rank = lax.axis_index("tensor")
    head_padded = jnp.where(jnp.arange(tensors)[:, None] == rank, head_grad[None, :], 0.0)
    vector = jnp.concatenate([head_padded.reshape(-1), shared_grad.reshape(-1)])
    vector = jnp.pad(vector, (0, -vector.shape[0] % 1024)).reshape(-1, 128)
    parts, vector, output, grad_input = reduce_slots(
        holder,
        kind_of_blocks(tile_count, heads_here, blocks_here),
        (left_one, upright(grad_one), left_two, left_context, left_grad_two, left_three, left_grad_three),
        (
            query_grad_one,
            key_grad_one,
            dv_one,
            heads_one,
            query_grad_two,
            key_grad_two,
            dv_two,
            heads_two,
            d_hidden,
            hidden,
        ),
        vector,
        (rows, after_two, dx_one, y_three, da_one),
        jnp.concatenate([mod[5:6], mod[1:2], shared_params[2:3], jnp.zeros((5, D), F32)], 0),
        slot_count,
    )
    output, grad_input = (
        jnp.where(lax.axis_index("tensor") == 0, v[:half], v[half:tokens])
        for v in (output, grad_input)
    )
    new_master, new_first, new_second = adam_slots(
        parts, master, first_moment, second_moment, slot_scale, filled
    )
    vector = vector.reshape(-1)
    head_total = vector[: head_padded.size].reshape(head_padded.shape)
    shared_total = vector[head_padded.size : head_padded.size + shared_grad.size]
    shared_total = shared_total.reshape(shared_grad.shape)
    mine_head = lax.dynamic_slice_in_dim(head_total, tensor_rank, 1, 0)
    new_head, new_head_first, new_head_second = adam_step(
        head_params, mine_head, head_first, head_second, VECTOR_RATE, 0.0
    )
    new_shared, new_shared_first, new_shared_second = adam_step(
        shared_params, shared_total, shared_first, shared_second, VECTOR_RATE, 0.0
    )
    return (
        output,
        grad_input,
        new_master,
        new_first,
        new_second,
        new_head,
        new_head_first,
        new_head_second,
        new_shared,
        new_shared_first,
        new_shared_second,
    )


def solution(mesh):
    return jax.shard_map(
        body,
        mesh=mesh,
        in_specs=(
            P(("dp", "tensor"), None),
            P("dp", None),
            P(("dp", "tensor"), None),
            P(None, "dp"),
            P("dp"),
            P(),
            P(),
            P("tensor", "dp", None, None),
            P("tensor", "dp", None, None),
            P("tensor", "dp", None, None),
            P("tensor", None),
            P("tensor", None),
            P("tensor", None),
            P(),
            P(),
            P(),
        ),
        out_specs=(
            P(("dp", "tensor"), None),
            P(("dp", "tensor"), None),
            P("tensor", "dp", None, None),
            P("tensor", "dp", None, None),
            P("tensor", "dp", None, None),
            P("tensor", None),
            P("tensor", None),
            P("tensor", None),
            P(),
            P(),
            P(),
        ),
        check_vma=False,
    )
```

```python
import functools

import jax
import jax.numpy as jnp
from jax import lax
from jax.experimental import pallas as pl
from jax.experimental.pallas import tpu as pltpu
from jax.sharding import PartitionSpec as P

D = 1536
HEADS = 12
HEAD = 128
FF = 8960
TSTEPS = 16
STEPC = 10


NORM_EPS = 1e-06
BETA_ONE = 0.9
BETA_TWO = 0.999
ADAM_EPS = 1e-08
TILE_RATE = 1.0
TILE_DECAY = 0.1
VECTOR_RATE = 0.5
GELU_COEF = 0.7978845608028654


def rope_tables(token_places, head_size):
    sixths = head_size // 6
    frame_pairs = (head_size - 4 * sixths) // 2
    frame_freq = 10000.0 ** (-jnp.arange(frame_pairs, dtype=jnp.float32) / frame_pairs)
    side_freq = 10000.0 ** (-jnp.arange(sixths, dtype=jnp.float32) / sixths)
    spots = token_places.astype(jnp.float32)
    angles = jnp.concatenate(
        [
            spots[0][..., None] * frame_freq,
            spots[1][..., None] * side_freq,
            spots[2][..., None] * side_freq,
        ],
        -1,
    )
    angles = jnp.repeat(angles, 2, axis=-1)
    return (jnp.cos(angles), jnp.sin(angles))


def owner_layout(owners, slot_count, devices):
    indices = jnp.arange(owners.shape[0], dtype=jnp.int32)
    same_owner = (owners[:, None] == owners[None, :]) & (indices[None, :] < indices[:, None])
    slot_of = jnp.sum(same_owner.astype(jnp.int32), axis=1)
    places = owners * slot_count + slot_of
    spots = jnp.arange(slot_count * devices, dtype=jnp.int32)
    holder = (
        jnp.sum(jnp.where(places[None, :] == spots[:, None], indices[None, :] + 1, 0), axis=1) - 1
    )
    return (places, holder)


def tile_scales(tile_count, heads_here, blocks_here):
    indices = jnp.arange(tile_count)
    scale_in = D ** (-0.5)
    scale_out = HEADS ** (-0.5)
    scale_down = FF ** (-0.5)
    scales = jnp.where(
        indices < 3 * heads_here,
        scale_in,
        jnp.where(
            indices < 4 * heads_here,
            scale_out,
            jnp.where(
                indices < 7 * heads_here,
                scale_in,
                jnp.where(
                    indices < 8 * heads_here,
                    scale_out,
                    jnp.where(indices < 8 * heads_here + blocks_here, scale_in, scale_down),
                ),
            ),
        ),
    )
    return scales.astype(jnp.float32)


def adam_step(weight, gradient, moment_one, moment_two, step_rate, decay_rate):
    first_new = BETA_ONE * moment_one + (1.0 - BETA_ONE) * gradient
    second_new = BETA_TWO * moment_two + (1.0 - BETA_TWO) * gradient * gradient
    first_hat = first_new / (1.0 - BETA_ONE**STEPC)
    second_hat = second_new / (1.0 - BETA_TWO**STEPC)
    weight_new = weight - step_rate * (
        first_hat / (jnp.sqrt(second_hat) + ADAM_EPS) + decay_rate * weight
    )
    return (weight_new, first_new, second_new)


MESH = pl.DeviceIdType.MESH
ANY = pl.BlockSpec(memory_space=pl.ANY)
MIB = 1 << 20


def chip_pairs():
    return lax.axis_size("dp") == 16 and lax.axis_size("tensor") == 2


def pair_rank():
    if chip_pairs():
        return (lax.axis_index("dp") // 4) % 2
    return lax.axis_index("tensor")


def pair_swap(value):
    if chip_pairs():
        return lax.ppermute(value, "dp", [(i, i ^ 4) for i in range(16)])
    return lax.ppermute(value, "tensor", [(0, 1), (1, 0)])


def pair_sums(*values):
    stacked = jnp.concatenate([v.reshape(-1) for v in values])
    total = stacked + pair_swap(stacked)
    out, at = [], 0
    for v in values:
        out.append(total[at : at + v.size].reshape(v.shape))
        at += v.size
    return tuple(out)


def place_of():
    chip, core = lax.axis_index("dp"), lax.axis_index("tensor")
    z, y, x = chip // 4, (chip // 2) % 2, chip % 2
    return chip, core, z, y, x


def column_of(z, y, x, k):
    high, low_bit = z // 2, z % 2
    if k & 2:
        high = 1 - high
    if k & 1:
        low_bit = 1 - low_bit
    return (2 * high + low_bit) * 4 + 2 * y + x


def greet(chip, core, z, y, x):
    barrier = pltpu.get_barrier_semaphore()
    friends = []
    for k in range(4):
        for flip in (0, 1):
            if k or flip:
                friends.append((column_of(z, y, x, k), core if flip == 0 else 1 - core))
    friends.append((column_of(z, y, 1 - x, 0), core))
    friends.append((column_of(z, 1 - y, x, 0), core))
    for friend in friends:
        pl.semaphore_signal(barrier, inc=1, device_id=friend, device_id_type=MESH)
    pl.semaphore_wait(barrier, len(friends))


def gather_kernel(
    own, lat, cot, text, small, out, lats, cots, texts, smalls, clip_s, clip_r,
    near_s, col_r, x_s, x_r, y_s, y_r, sib_s, sib_r,
):
    chip, core, z, y, x = place_of()
    rank = z % 2
    half = own.shape[1] // 2
    part = half // 2
    at_x = column_of(z, y, 1 - x, 0)
    at_y = column_of(z, 1 - y, x, 0)
    greet(chip, core, z, y, x)

    batch = max(n for n in (1, 2, 3) if own.shape[0] % n == 0)
    batches = own.shape[0] // batch
    turns = 4 * batches

    def case(s):
        late = jnp.maximum(s - batches, 0)
        k = jnp.where(s < batches, 0, 1 + late % 3)
        return k, jnp.where(s < batches, s, late // 3)

    def remote(unit, g, first, count, send, recv, device):
        piece = out.at[
            unit, pl.ds(g * batch, batch), pl.ds(pl.multiple_of(first, 16), count), :
        ]
        return pltpu.make_async_remote_copy(
            src_ref=piece, dst_ref=piece, send_sem=send, recv_sem=recv,
            device_id=device, device_id_type=MESH,
        )

    def own_copy(g, j, h):
        target = (toggled(z, y, x, 0, 0, 2 * j) // 8 * 8) + core * 4 + 2 * y + x
        part_of = (pl.ds(g * batch, batch), pl.ds(h * half, half))
        src = own.at[part_of[0], part_of[1], :]
        dst = out.at[chip, part_of[0], part_of[1], :]
        recv = col_r.at[z * batches + g]
        go = pltpu.make_async_remote_copy(
            src_ref=src, dst_ref=dst, send_sem=near_s.at[(2 * j + h) * batches + g],
            recv_sem=recv, device_id=(target, h), device_id_type=MESH,
        )
        return go, pltpu.make_async_copy(src, dst, recv)

    for g in range(batches):
        for j in range(2):
            for h in range(2):
                go, here = own_copy(g, j, h)
                if j == 1:
                    go.start()
                    continue
                stays = jnp.logical_and(rank == core, core == h)

                @pl.when(stays)
                def _():
                    here.start()

                @pl.when(jnp.logical_not(stays))
                def _():
                    go.start()

    pair_chip = column_of(z, y, x, 1)
    rows_of_text = text.shape[0] // 2

    def clip_pieces(h):
        share = pl.ds(h * rows_of_text, rows_of_text)
        return ((lat, lats.at[h]), (cot, cots.at[h]), (text.at[share], texts.at[share]))

    home = rank == core
    trade = pltpu.make_async_remote_copy(
        src_ref=small, dst_ref=smalls, send_sem=clip_s.at[6], recv_sem=clip_r.at[6],
        device_id=(pair_chip, 1 - core), device_id_type=MESH,
    )
    keep = pltpu.make_async_copy(small, smalls, clip_r.at[6])

    @pl.when(home)
    def _():
        keep.start()

    @pl.when(jnp.logical_not(home))
    def _():
        trade.start()

    def hand_out(h, n, wait):
        src, dst = clip_pieces(h)[n]
        far = pltpu.make_async_remote_copy(
            src_ref=src, dst_ref=dst, send_sem=clip_s.at[n], recv_sem=clip_r.at[3 * h + n],
            device_id=(pair_chip, rank), device_id_type=MESH,
        )
        near = pltpu.make_async_remote_copy(
            src_ref=src, dst_ref=dst, send_sem=clip_s.at[3 + n], recv_sem=clip_r.at[3 * h + n],
            device_id=(chip, 1 - core), device_id_type=MESH,
        )
        here = pltpu.make_async_copy(src, dst, clip_r.at[3 * h + n])

        @pl.when(core == h)
        def _():
            if wait:
                far.wait_send()
            else:
                far.start()

            @pl.when(home)
            def _():
                if not wait:
                    here.start()

            @pl.when(jnp.logical_not(home))
            def _():
                if wait:
                    near.wait_send()
                else:
                    near.start()

    for n in range(3):
        for h in range(2):
            hand_out(h, n, False)

    mine, other = core * half, (1 - core) * half
    sibling = (chip, 1 - core)

    def to_x(s, n):
        k, g = case(s)
        i = turns * n + s
        unit = toggled(z, y, x, n, 0, k)
        return remote(unit, g, mine, part if n else half, x_s.at[i], x_r.at[i], (at_x, core))

    def from_x(s, n):
        k, g = case(s)
        i = turns * n + s
        unit = toggled(z, y, x, n, 1, k)
        return remote(unit, g, mine, part if n else half, x_s.at[i], x_r.at[i], (at_x, core))

    def to_y(s, n):
        k, g = case(s)
        i = turns * n + s
        unit = toggled(z, y, x, 0, n, k)
        first, count = (mine + part, part) if n else (mine, half)
        return remote(unit, g, first, count, y_s.at[i], y_r.at[i], (at_y, core))

    def from_y(s, n):
        k, g = case(s)
        i = turns * n + s
        unit = toggled(z, y, x, 1, n, k)
        first, count = (mine + part, part) if n else (mine, half)
        return remote(unit, g, first, count, y_s.at[i], y_r.at[i], (at_y, core))

    def to_sib(s, n, away=False):
        k, g = case(s)
        i = turns * n + s
        unit = toggled(z, y, x, int(n in (2, 3, 4)), int(n in (1, 3, 4)), k)
        first = (other if away else mine) + (part if n == 4 else 0)
        return remote(
            unit, g, first, part if n >= 3 else half, sib_s.at[i], sib_r.at[i], sibling
        )

    def column_in(s):
        k, g = case(s)
        unit = toggled(z, y, x, 0, 0, k)
        piece = out.at[
            unit, pl.ds(g * batch, batch), pl.ds(pl.multiple_of(mine, 16), half), :
        ]
        pltpu.make_async_copy(piece, piece, col_r.at[unit // 4 * batches + g]).wait()
        to_x(s, 0).start()
        to_y(s, 0).start()
        to_sib(s, 0).start()

    def side_in(s):
        from_x(s, 0).wait_recv()
        to_y(s, 1).start()
        to_sib(s, 1).start()
        from_y(s, 0).wait_recv()
        to_x(s, 1).start()
        to_sib(s, 2).start()

    def corner_in(s):
        from_x(s, 1).wait_recv()
        to_sib(s, 3).start()
        from_y(s, 1).wait_recv()
        to_sib(s, 4).start()

    def turn(step, carry):
        @pl.when(step < turns)
        def _():
            column_in(step)

        @pl.when(jnp.logical_and(step >= 1, step < turns + 1))
        def _():
            side_in(step - 1)

        @pl.when(step >= 2)
        def _():
            corner_in(step - 2)

        return carry

    lax.fori_loop(0, turns + 2, turn, 0)

    def settle(s, carry):
        for n in range(2):
            to_x(s, n).wait_send()
            to_y(s, n).wait_send()
        for n in range(5):
            to_sib(s, n).wait_send()
            to_sib(s, n, True).wait_recv()
        return carry

    lax.fori_loop(0, turns, settle, 0)
    for g in range(batches):
        for j in range(2):
            for h in range(2):
                go, _ = own_copy(g, j, h)
                if j == 1:
                    go.wait_send()
                    continue

                @pl.when(jnp.logical_not(jnp.logical_and(rank == core, core == h)))
                def _():
                    go.wait_send()

    for n in range(3):
        for h in range(2):
            hand_out(h, n, True)
            dst = clip_pieces(h)[n][1]
            pltpu.make_async_copy(dst, dst, clip_r.at[3 * h + n]).wait()

    @pl.when(jnp.logical_not(home))
    def _():
        trade.wait_send()

    pltpu.make_async_copy(smalls, smalls, clip_r.at[6]).wait()


def gather_slots(scaled, lat, cot, text, small):
    if not chip_pairs():
        everyone = lax.all_gather(scaled, "dp", axis=0, tiled=True)
        lats, cots = (lax.all_gather(v, "tensor") for v in (lat, cot))
        return everyone, lats, cots, text, small
    dma = pltpu.SemaphoreType.DMA
    turns = 4 * scaled.shape[0] // max(n for n in (1, 2, 3) if scaled.shape[0] % n == 0)
    counts = (7, 7, turns, turns) + (2 * turns,) * 4 + (5 * turns,) * 2
    everyone, *rest = pl.pallas_call(
        gather_kernel,
        out_shape=[
            jax.ShapeDtypeStruct((16,) + scaled.shape, scaled.dtype),
            jax.ShapeDtypeStruct((2,) + lat.shape, lat.dtype),
            jax.ShapeDtypeStruct((2,) + cot.shape, cot.dtype),
            jax.ShapeDtypeStruct(text.shape, text.dtype),
            jax.ShapeDtypeStruct(small.shape, small.dtype),
        ],
        in_specs=[ANY] * 5,
        out_specs=[ANY] * 5,
        scratch_shapes=[dma((n,)) for n in counts],
        compiler_params=pltpu.CompilerParams(
            collective_id=0, has_side_effects=True, vmem_limit_bytes=4 * MIB
        ),
    )(scaled, lat, cot, text, small)
    return everyone.reshape((-1,) + scaled.shape[1:]), *rest


def toggled(z, y, x, flip_y, flip_x, k):
    high = (z // 2 + k // 2) % 2
    low_bit = (z % 2 + k % 2) % 2
    return (2 * high + low_bit) * 4 + 2 * ((y + flip_y) % 2) + (x + flip_x) % 2


def reduce_kernel(
    kind, block, *refs,
):
    (
        *pieces, rows_in, after_in, dx_in, y_in, da_in, gains, vec_in,
        final, vec_out, result, result_grad, y_other, da_other, from_sib, from_x, from_y, corner_a, corner_b,
        left, right, ring, corners, side_x, side_y, middle, stage, vec_box,
        load_s, stage_s, sib_s, sib_r, x_s, x_r, y_s, y_r, ca_s, ca_r, cb_s, cb_r, f_s, f_r, v_s, v_r,
        end_s, end_r,
    ) = refs
    chip, core, z, y, x = place_of()
    rank = z % 2
    slots, width, lanes = final.shape[1:]
    half = width // 2
    part = half // 2
    at_x = toggled(z, y, x, 0, 1, 0)
    at_y = toggled(z, y, x, 1, 0, 0)
    sibling = (chip, 1 - core)
    mates = (
        sibling,
        (at_x, core),
        (at_y, core),
        (toggled(z, y, x, 0, 0, 1), core),
        (toggled(z, y, x, 0, 0, 2), core),
    )

    kinds = left.shape[0]
    depth = right.shape[1]
    loads = [
        pltpu.make_async_copy(pieces[i], left.at[i], load_s.at[i]) for i in range(kinds)
    ]
    first = 0
    blank = []
    for i, piece in enumerate(pieces[kinds:]):
        number, rows = piece.shape[:2]
        loads.append(
            pltpu.make_async_copy(
                piece, right.at[pl.ds(first, number), pl.ds(0, rows), :], load_s.at[kinds + i]
            )
        )
        if rows < depth:
            blank.append((first, number, rows))
        first += number
    for load in loads:
        load.start()
    for start, number, rows in blank:

        def clear(i, carry):
            right[start + i, pl.ds(rows, depth - rows), :] = jnp.zeros(
                (depth - rows, lanes), right.dtype
            )
            return carry

        lax.fori_loop(0, number, clear, 0)
    right[first] = jnp.zeros((depth, lanes), right.dtype)
    vec_out[...] = vec_in[...]
    greet(chip, core, z, y, x)
    for load in loads:
        load.wait()

    def remote(src, dst, send, recv, device):
        return pltpu.make_async_remote_copy(
            src_ref=src, dst_ref=dst, send_sem=send, recv_sem=recv,
            device_id=device, device_id_type=MESH,
        )

    batch = ring.shape[1]
    batches = slots // batch
    turns = 4 * batches
    deep = corners.shape[0]

    def flips(s):
        return 3 - s // batches

    def sums(q, s, first, terms, total):
        unit = toggled(z, y, x, 1 - q % 2, 1 - q // 2, flips(s))
        base = unit * slots + (s % batches) * batch
        count = total.shape[1]

        def one(i, carry):
            slot = base + i
            rows = pl.ds(pl.multiple_of(first, 128), count)
            acc = jnp.dot(
                left[kind[slot], rows, :], right[block[slot]], preferred_element_type=jnp.float32
            )
            for term in terms:
                acc = acc + term[i].astype(jnp.float32)
            total[i] = acc.astype(total.dtype)
            return carry

        lax.fori_loop(0, batch, one, 0)

    mine, other = core * half, (1 - core) * half

    def sub(ref, first):
        return ref.at[:, pl.ds(first, part), :]

    def sib_copy(q, s):
        i = turns * q + s
        return remote(ring.at[q], from_sib.at[i], sib_s.at[i], sib_r.at[i], sibling)

    def a_copy(s):
        return remote(
            sub(corners.at[s % deep], 0), corner_a.at[s], ca_s.at[s], ca_r.at[s], (at_x, core)
        )

    def b_copy(s):
        return remote(
            sub(corners.at[s % deep], part), corner_b.at[s], cb_s.at[s], cb_r.at[s], (at_y, core)
        )

    def x_copy(s, n):
        rows = pl.ds(n * part, part)
        i = turns * n + s
        return remote(
            side_x.at[s % deep, :, rows, :], from_x.at[s, :, rows, :], x_s.at[i], x_r.at[i],
            (at_x, core),
        )

    def y_copy(s, n):
        rows = pl.ds((1 - n) * part, part)
        i = turns * n + s
        return remote(
            side_y.at[s % deep, :, rows, :], from_y.at[s, :, rows, :], y_s.at[i], y_r.at[i],
            (at_y, core),
        )

    def f_copy(s):
        src = middle.at[s % deep]
        g = s % batches
        dst = final.at[
            z // 2, pl.ds(g * batch, batch), pl.ds(pl.multiple_of(mine, 128), half), :
        ]
        recv = f_r.at[(2 * (z // 2) + core) * batches + g]
        target = (toggled(z, y, x, 0, 0, flips(s)), rank)
        return remote(src, dst, f_s.at[s], recv, target), pltpu.make_async_copy(src, dst, recv)

    def stays(s):
        return jnp.logical_and(s >= turns - batches, rank == core)

    def staged(source, place, i):
        copy = pltpu.make_async_copy(source, place, stage_s.at[i])
        copy.start()
        return copy

    def for_sibling(s):
        def one(q, carry):
            @pl.when(s >= 1)
            def _():
                sib_copy(q, s - 1).wait_send()

            sums(q, s, other, (), ring.at[q])
            sib_copy(q, s).start()
            return carry

        lax.fori_loop(0, 4, one, 0)

    def corner(s):
        sib_copy(0, s).wait_recv()
        in_sib = staged(from_sib.at[s], stage.at[0], 0)

        @pl.when(s >= deep)
        def _():
            a_copy(s - deep).wait_send()
            b_copy(s - deep).wait_send()

        in_sib.wait()
        sums(0, s, mine, (stage.at[0],), corners.at[s % deep])
        a_copy(s).start()
        b_copy(s).start()

    def direct_sides(s):
        sib_copy(1, s).wait_recv()
        in_x = staged(from_sib.at[turns + s], stage.at[0], 0)
        sib_copy(2, s).wait_recv()
        in_y = staged(from_sib.at[2 * turns + s], stage.at[1], 1)

        @pl.when(s >= deep)
        def _():
            for n in range(2):
                x_copy(s - deep, n).wait_send()
                y_copy(s - deep, n).wait_send()

        in_x.wait()
        sums(1, s, mine, (sub(stage.at[0], 0),), sub(side_x.at[s % deep], 0))
        x_copy(s, 0).start()
        in_y.wait()
        sums(2, s, mine + part, (sub(stage.at[1], part),), sub(side_y.at[s % deep], part))
        y_copy(s, 0).start()

    def relayed_sides(s):
        b_copy(s).wait_recv()
        in_b = staged(corner_b.at[s], sub(stage.at[2], 0), 2)
        a_copy(s).wait_recv()
        in_a = staged(corner_a.at[s], sub(stage.at[2], part), 3)
        in_b.wait()
        sums(
            1, s, mine + part, (sub(stage.at[0], part), sub(stage.at[2], 0)),
            sub(side_x.at[s % deep], part),
        )
        x_copy(s, 1).start()
        in_a.wait()
        sums(
            2, s, mine, (sub(stage.at[1], 0), sub(stage.at[2], part)), sub(side_y.at[s % deep], 0)
        )
        y_copy(s, 1).start()

    def centre(s):
        sib_copy(3, s).wait_recv()
        in_sib = staged(from_sib.at[3 * turns + s], stage.at[3], 4)
        x_copy(s, 0).wait_recv()
        x_copy(s, 1).wait_recv()
        in_x = staged(from_x.at[s], stage.at[4], 5)
        y_copy(s, 0).wait_recv()
        y_copy(s, 1).wait_recv()
        in_y = staged(from_y.at[s], stage.at[5], 6)

        @pl.when(s >= deep)
        def _():
            f_copy(s - deep)[0].wait_send()

        in_sib.wait()
        in_x.wait()
        in_y.wait()
        sums(3, s, mine, (stage.at[3], stage.at[4], stage.at[5]), middle.at[s % deep])
        go, here = f_copy(s)

        @pl.when(stays(s))
        def _():
            here.start()

        @pl.when(jnp.logical_not(stays(s)))
        def _():
            go.start()

    home = rank == core
    pair_device = (toggled(z, y, x, 0, 0, 1), core)
    ends = [
        remote(y_in, y_other, end_s.at[0], end_r.at[0], pair_device),
        remote(da_in, da_other, end_s.at[1], end_r.at[1], pair_device),
        remote(result, result, end_s.at[2], end_r.at[2], sibling),
        remote(result_grad, result_grad, end_s.at[3], end_r.at[3], sibling),
    ]

    def finish_rows():
        ends[0].wait_recv()
        ends[1].wait_recv()
        tall = 16
        spec = pl.BlockSpec((tall, width), lambda i: (i, 0))

        def one(x_ref, x2_ref, dx_ref, y_ref, yo_ref, da_ref, dao_ref, out_ref, grad_ref):
            y_all = y_ref[...].astype(F32) + yo_ref[...].astype(F32) + gains[2:3]
            out_ref[...] = (x2_ref[...] + gains[0:1] * y_all).astype(out_ref.dtype)
            da = da_ref[...].astype(F32) + dao_ref[...].astype(F32)
            back, _ = normed_back(x_ref[...], da * (1.0 + gains[1:2]))
            grad_ref[...] = dx_ref[...] + back

        pltpu.emit_pipeline(
            one, grid=(rows_in.shape[0] // tall,), in_specs=[spec] * 7, out_specs=[spec] * 2
        )(rows_in, after_in, dx_in, y_in, y_other, da_in, da_other, result, result_grad)
        ends[2].start()
        ends[3].start()

    @pl.when(jnp.logical_not(home))
    def _():
        ends[0].start()
        ends[1].start()

    def vec_copy(i):
        return remote(vec_out, vec_box.at[i], v_s.at[i], v_r.at[i], mates[i])

    def turn(step, carry):
        for i in range(5):

            @pl.when(step == i)
            def _():
                vec_copy(i).start()

        @pl.when(step < turns)
        def _():
            corner(step)
            direct_sides(step)

        @pl.when(step + 1 < turns)
        def _():
            for_sibling(step + 1)

        @pl.when(step >= 1)
        def _():
            centre(step - 1)

        @pl.when(step < turns)
        def _():
            relayed_sides(step)

        @pl.when(jnp.logical_and(step == turns - batches, home))
        def _():
            finish_rows()

        for i in range(5):

            @pl.when(step == i)
            def _():
                vec_copy(i).wait()
                vec_out[...] = vec_out[...] + vec_box[i]

        return carry

    for_sibling(0)
    lax.fori_loop(0, turns + 1, turn, 0)
    for q in range(4):
        sib_copy(q, turns - 1).wait_send()

    def settle(i, carry):
        s = turns - deep + i
        a_copy(s).wait_send()
        b_copy(s).wait_send()
        for n in range(2):
            x_copy(s, n).wait_send()
            y_copy(s, n).wait_send()

        @pl.when(jnp.logical_not(stays(s)))
        def _():
            f_copy(s)[0].wait_send()

        return carry

    lax.fori_loop(0, deep, settle, 0)

    @pl.when(home)
    def _():
        ends[2].wait_send()
        ends[3].wait_send()

    @pl.when(jnp.logical_not(home))
    def _():
        ends[0].wait_send()
        ends[1].wait_send()
        ends[2].wait_recv()
        ends[3].wait_recv()

    for plane in range(2):
        for h in range(2):
            for g in range(batches):
                piece = final.at[plane, pl.ds(g * batch, batch), pl.ds(h * half, half), :]
                recv = f_r.at[(2 * plane + h) * batches + g]
                pltpu.make_async_copy(piece, piece, recv).wait()


def reduce_slots(holder, kinds, rows, columns, vector, ends, gains, slot_count):
    if not chip_pairs():
        grads = slot_grads(holder, kinds, [r.T for r in rows], columns)
        total = lax.psum_scatter(grads, "dp", scatter_dimension=0, tiled=True)
        x, after, dx, y_part, da_part = ends
        y_all, da_all = (
            v.astype(F32) + pair_swap(v).astype(F32) for v in (y_part, da_part)
        )
        result = (after + gains[0] * (y_all + gains[2])).astype(BF16)
        back, _ = normed_back(x, da_all * (1.0 + gains[1]))
        return total[None], lax.psum(vector, ("dp", "tensor")), result, dx + back
    left = rows
    width, depth = left[0].shape
    lanes = columns[0].shape[2]
    tiles = sum(c.shape[0] for c in columns)
    block = jnp.where(holder >= 0, holder, tiles)
    kind = kinds[jnp.maximum(holder, 0)]
    half = width // 2
    dma = pltpu.SemaphoreType.DMA
    scalars = pl.BlockSpec(memory_space=pltpu.SMEM)
    inside = pl.BlockSpec(memory_space=pltpu.VMEM)
    low = jnp.bfloat16

    batch = max(n for n in (1, 2, 3) if slot_count % n == 0)
    turns = 4 * slot_count // batch
    deep = 3

    def room(count, tall):
        return jax.ShapeDtypeStruct((count, batch, tall, lanes), low)

    def slab(count):
        return pltpu.VMEM((count, batch, half, lanes), low)

    outs = pl.pallas_call(
        reduce_kernel,
        out_shape=[
            jax.ShapeDtypeStruct((2, slot_count, width, lanes), low),
            jax.ShapeDtypeStruct(vector.shape, vector.dtype),
            jax.ShapeDtypeStruct(ends[0].shape, low), jax.ShapeDtypeStruct(ends[0].shape, F32),
            jax.ShapeDtypeStruct(ends[0].shape, low), jax.ShapeDtypeStruct(ends[0].shape, low),
            room(4 * turns, half), room(turns, half), room(turns, half),
            room(turns, half // 2), room(turns, half // 2),
        ],
        in_specs=[scalars, scalars] + [ANY] * (len(left) + len(columns) + 5) + [inside] * 2,
        out_specs=[ANY, inside] + [ANY] * 9,
        scratch_shapes=[
            pltpu.VMEM((len(left), width, depth), low),
            pltpu.VMEM((tiles + 1, depth, lanes), low),
            slab(4), slab(deep), slab(deep), slab(deep), slab(deep), slab(6),
            pltpu.VMEM((5,) + vector.shape, vector.dtype),
        ]
        + [
            dma((n,))
            for n in (len(left) + len(columns), 7)
            + (4 * turns,) * 2
            + (2 * turns,) * 4
            + (turns,) * 6
            + (5, 5, 4, 4)
        ],
        compiler_params=pltpu.CompilerParams(
            collective_id=1, has_side_effects=True, vmem_limit_bytes=48 * MIB
        ),
    )(kind, block, *left, *columns, *ends, gains, vector)
    return outs[:4]


def kind_of_blocks(tile_count, heads_here, blocks_here):
    number = jnp.arange(tile_count)
    kind = number // heads_here
    table = jnp.array([0, 0, 0, 1, 2, 3, 3, 4], jnp.int32)
    late = jnp.where(number < 8 * heads_here + blocks_here, 5, 6)
    return jnp.where(number < 8 * heads_here, table[jnp.minimum(kind, 7)], late).astype(jnp.int32)


def slot_grads(holder, kinds, rows, columns):
    depth = max(r.shape[0] for r in rows)

    def deep(value, axis):
        room = [(0, 0)] * value.ndim
        room[axis] = (0, depth - value.shape[axis])
        return jnp.pad(value, room)

    left = jnp.stack([deep(r, 0) for r in rows])
    right = jnp.concatenate([deep(c, 1) for c in columns], 0)
    slots = holder.shape[0]
    used = (holder >= 0).astype(jnp.int32)
    block = jnp.maximum(holder, 0)
    kind = kinds[block]
    width = rows[0].shape[1]
    lanes = right.shape[2]

    def multiply(kind_ref, block_ref, used_ref, left_ref, right_ref, out_ref):
        slot = pl.program_id(0)

        @pl.when(used_ref[slot] == 1)
        def _():
            out_ref[0] = lax.dot_general(
                left_ref[kind_ref[slot]],
                right_ref[0],
                (((0,), (0,)), ((), ())),
                preferred_element_type=jnp.float32,
            ).astype(out_ref.dtype)

        @pl.when(used_ref[slot] == 0)
        def _():
            out_ref[...] = jnp.zeros_like(out_ref)

    return pl.pallas_call(
        multiply,
        grid_spec=pltpu.PrefetchScalarGridSpec(
            num_scalar_prefetch=3,
            grid=(slots,),
            in_specs=[
                pl.BlockSpec(left.shape, lambda s, kd, b, u: (0, 0, 0)),
                pl.BlockSpec((1, depth, lanes), lambda s, kd, b, u: (b[s], 0, 0)),
            ],
            out_specs=pl.BlockSpec((1, width, lanes), lambda s, kd, b, u: (s, 0, 0)),
        ),
        out_shape=jax.ShapeDtypeStruct((slots, width, lanes), jnp.bfloat16),
        compiler_params=pltpu.CompilerParams(vmem_limit_bytes=48 * MIB),
    )(kind, block, used, left, right)


def adam_slots(planes, master, moment_one, moment_two, slot_scale, filled):
    count, slot_count, width, lanes = planes.shape

    def step(scale_ref, fill_ref, grads, weight, one, two, new_weight, new_one, new_two):
        slot = pl.program_id(0)

        @pl.when(fill_ref[slot] == 1)
        def _():
            total = grads[0, 0].astype(jnp.float32)
            for n in range(1, count):
                total = total + grads[n, 0].astype(jnp.float32)
            results = adam_step(
                weight[0, 0], total * scale_ref[slot], one[0, 0], two[0, 0], TILE_RATE, TILE_DECAY
            )
            for ref, value in zip((new_weight, new_one, new_two), results):
                ref[0, 0] = value

        @pl.when(fill_ref[slot] == 0)
        def _():
            new_weight[...] = weight[...]
            new_one[...] = one[...]
            new_two[...] = two[...]

    deep = pl.BlockSpec((1, 1, width, lanes), lambda s: (0, s, 0, 0))
    scalars = pl.BlockSpec(memory_space=pltpu.SMEM)
    return pl.pallas_call(
        step,
        grid=(slot_count,),
        in_specs=[scalars, scalars, pl.BlockSpec((count, 1, width, lanes), lambda s: (0, s, 0, 0))]
        + [deep] * 3,
        out_specs=[deep] * 3,
        out_shape=[jax.ShapeDtypeStruct(master.shape, jnp.float32)] * 3,
        compiler_params=pltpu.CompilerParams(vmem_limit_bytes=32 * MIB),
    )(
        slot_scale,
        filled.astype(jnp.int32),
        *[
            pltpu.with_memory_space_constraint(v, pltpu.HBM)
            for v in (planes, master, moment_one, moment_two)
        ],
    )


SCALING = HEAD ** (-0.5)
BF16 = jnp.bfloat16
F32 = jnp.float32


def nn(left, right):
    return jnp.dot(left, right, preferred_element_type=F32)


def nt(left, right):
    return lax.dot_general(left, right, (((1,), (1,)), ((), ())), preferred_element_type=F32)


def tn(left, right):
    return lax.dot_general(left, right, (((0,), (0,)), ((), ())), preferred_element_type=F32)


def normed(rows):
    centre = rows - jnp.mean(rows, -1, keepdims=True)
    inverse = lax.rsqrt(jnp.mean(centre * centre, -1, keepdims=True) + NORM_EPS)
    return centre * inverse, inverse


def normed_back(rows, grad):
    unit, inverse = normed(rows)
    mean = jnp.mean(grad, -1, keepdims=True)
    return (grad - mean - unit * jnp.mean(grad * unit, -1, keepdims=True)) * inverse, unit


def total_of(rows):
    return jnp.sum(rows, 0, keepdims=True)


def turned(rows, cos_tab, sin_tab):
    even = lax.broadcasted_iota(jnp.int32, rows.shape, 1) % 2 == 0
    partner = jnp.where(even, pltpu.roll(rows, HEAD - 1, 1), pltpu.roll(rows, 1, 1))
    return rows * cos_tab + partner * sin_tab


def wide(column):
    return jnp.broadcast_to(column, (column.shape[0], HEAD))


def pack_sums(for_rows, for_text=None):
    out = wide(for_rows)
    if for_text is None:
        return out
    lane = lax.broadcasted_iota(jnp.int32, out.shape, 1)
    count = for_text.shape[0] // 2
    rest = jnp.zeros((out.shape[0] - count, HEAD), F32)
    first = jnp.concatenate([wide(for_text[:count]), rest], 0)
    second = jnp.concatenate([wide(for_text[count:]), rest], 0)
    return jnp.where(lane < 32, out, jnp.where(lane < 64, first, second))


def unpack_text(sums, count):
    return jnp.concatenate([sums[: count // 2, 32:33], sums[: count // 2, 64:65]], 0)


def softmax(scores):
    expo = jnp.exp(scores - jnp.max(scores, -1, keepdims=True))
    return expo / jnp.sum(expo, -1, keepdims=True)


def self_scores(query_low, key_low, tokens):
    scores = nt(query_low, key_low) * SCALING
    lane = lax.broadcasted_iota(jnp.int32, scores.shape, 1)
    return jnp.where(lane < tokens, scores, -1e30)


def whole(array):
    zeros = (0,) * len(array.shape)
    return pl.BlockSpec(array.shape, lambda *_: zeros)


def block_at(first, stride=1):
    return pl.BlockSpec((1, D, HEAD), lambda i, where: (where[first + stride * i], 0, 0))


def call(body, places, grid, ins, outs, scratch=(), vmem=24):
    specs = [spec if spec is not None else whole(array) for array, spec in ins]
    shapes = [pltpu.HBM(shape, kind) for shape, kind, _ in outs]
    out_specs = [
        spec if spec is not None else whole(shape) for (_, _, spec), shape in zip(outs, shapes)
    ]
    return pl.pallas_call(
        body,
        grid_spec=pltpu.PrefetchScalarGridSpec(
            num_scalar_prefetch=1,
            grid=(grid,),
            in_specs=specs,
            out_specs=out_specs,
            scratch_shapes=list(scratch),
        ),
        out_shape=shapes,
        compiler_params=pltpu.CompilerParams(vmem_limit_bytes=vmem * MIB),
    )(places, *[pltpu.with_memory_space_constraint(array, pltpu.HBM) for array, _ in ins])


def head_lanes(rows, per=1):
    return pl.BlockSpec((rows, per * HEAD), lambda h, *_: (0, h))


def heads_per_step(heads, most):
    return max(n for n in (1, 2, 3, 6) if heads % n == 0 and n <= most)


def lane_group(ref, j):
    return ref[:, j * HEAD : (j + 1) * HEAD]


def joined(refs):
    return jnp.concatenate([ref[0] for ref in refs], 1)


def project_self(places, everyone, rows, mod, vecs, heads):
    count = rows.shape[0]
    span = heads * HEAD

    def body(_, rows_ref, mod_ref, vec_ref, *refs):
        weights, (low, pre, value, sums, acc) = refs[:heads], refs[heads:]
        i = pl.program_id(0)

        @pl.when(i == 0)
        def _():
            unit, _ = normed(rows_ref[...])
            low[...] = (unit * (1.0 + mod_ref[1:2]) + mod_ref[0:1]).astype(BF16)

        made = nn(low[...], joined(weights))

        @pl.when(i == 0)
        def _():
            q = made + vec_ref[0:1]
            pre[0] = q
            acc[...] = wide(jnp.sum(q * q, -1, keepdims=True))

        @pl.when(i == 1)
        def _():
            k = made + vec_ref[1:2]
            pre[0] = k
            lane = lax.broadcasted_iota(jnp.int32, acc.shape, 1)
            sums[...] = jnp.where(lane < 64, acc[...], wide(jnp.sum(k * k, -1, keepdims=True)))

        @pl.when(i == 2)
        def _():
            value[...] = (made + vec_ref[2:3]).astype(BF16)

    return call(
        body, places, 3,
        [(rows, None), (mod, None), (vecs, None)]
        + [(everyone, block_at(h, heads)) for h in range(heads)],
        [
            ((count, D), BF16, None),
            ((2, count, span), F32, pl.BlockSpec((1, count, span), lambda i, _: (jnp.minimum(i, 1), 0, 0))),
            ((count, span), BF16, None),
            ((count, HEAD), F32, None),
        ],
        [pltpu.VMEM((count, HEAD), F32)],
    )


def attend_self(places, everyone, pre, value, sums, other, vecs, cos_tab, sin_tab, heads, tokens):
    count = value.shape[0]
    per = heads_per_step(heads, 2)
    steps = heads // per

    def body(_, pre_ref, value_ref, sum_ref, other_ref, vec_ref, cos_ref, sin_ref, *refs):
        weights, (q_ref, k_ref, o_ref, y_ref, acc) = refs[:per], refs[per:]
        h = pl.program_id(0)
        total = sum_ref[...] + other_ref[...]
        q_inv = lax.rsqrt(total[:, 0:1] / D + NORM_EPS)
        k_inv = lax.rsqrt(total[:, 64:65] / D + NORM_EPS)
        cos, sin = cos_ref[...], sin_ref[...]
        outs = []
        for j in range(per):
            lanes = slice(j * HEAD, (j + 1) * HEAD)
            q = turned(pre_ref[0, :, lanes] * q_inv * vec_ref[3:4, lanes], cos, sin).astype(BF16)
            k = turned(pre_ref[1, :, lanes] * k_inv * vec_ref[4:5, lanes], cos, sin).astype(BF16)
            q_ref[:, lanes] = q
            k_ref[:, lanes] = k
            chance = softmax(self_scores(q, k, tokens))
            out = nn(chance.astype(BF16), value_ref[:, lanes]).astype(BF16)
            o_ref[j] = out
            outs.append(out)
        part = nt(jnp.concatenate(outs, 1), joined(weights))

        @pl.when(h == 0)
        def _():
            acc[...] = part

        @pl.when(h > 0)
        def _():
            acc[...] = acc[...] + part

        @pl.when(h == steps - 1)
        def _():
            y_ref[...] = acc[...].astype(BF16)

    lanes = head_lanes(count, per)
    return call(
        body, places, steps,
        [
            (pre, pl.BlockSpec((2, count, per * HEAD), lambda h, _: (0, 0, h))),
            (value, lanes), (sums, None), (other, None),
            (vecs, head_lanes(vecs.shape[0], per)), (cos_tab, None), (sin_tab, None),
        ]
        + [(everyone, block_at(3 * heads + j, per)) for j in range(per)],
        [
            (value.shape, BF16, lanes),
            (value.shape, BF16, lanes),
            ((heads, count, HEAD), BF16, pl.BlockSpec((per, count, HEAD), lambda h, _: (h, 0, 0))),
            ((count, D), BF16, None),
        ],
        [pltpu.VMEM((count, D), F32)],
    )


def project_text(places, everyone, context, vecs, heads):
    count = context.shape[0]
    span = heads * HEAD

    def body(_, text_ref, vec_ref, *refs):
        weights, (key, value, sums) = refs[:heads], refs[heads:]
        i = pl.program_id(0)
        made = nn(text_ref[...], joined(weights))

        @pl.when(i == 0)
        def _():
            k = made + vec_ref[6:7]
            key[...] = k
            sums[...] = wide(jnp.sum(k * k, -1, keepdims=True))

        @pl.when(i == 1)
        def _():
            value[...] = (made + vec_ref[7:8]).astype(BF16)

    return call(
        body, places, 2,
        [(context, None), (vecs, None)]
        + [(everyone, block_at(5 * heads + h, heads)) for h in range(heads)],
        [((count, span), F32, None), ((count, span), BF16, None), ((count, HEAD), F32, None)],
    )


def project_cross(places, everyone, rows, part, other, mod, shared, vecs, text_sums, heads):
    count = rows.shape[0]
    span = heads * HEAD
    text = text_sums.shape[0]

    def body(_, rows_ref, part_ref, other_ref, mod_ref, shared_ref, vec_ref, text_ref, *refs):
        weights, (branch, after, low, pre, sums) = refs[:heads], refs[heads:]
        y = part_ref[...].astype(F32) + other_ref[...].astype(F32) + shared_ref[0:1]
        branch[...] = y
        x = rows_ref[...] + mod_ref[2:3] * y
        after[...] = x
        unit, _ = normed(x)
        a = (unit * shared_ref[3:4] + shared_ref[4:5]).astype(BF16)
        low[...] = a
        q = nn(a, joined(weights)) + vec_ref[5:6]
        pre[...] = q
        sums[...] = pack_sums(jnp.sum(q * q, -1, keepdims=True), text_ref[:, 0:1])

    return call(
        body, places, 1,
        [(v, None) for v in (rows, part, other, mod, shared, vecs, text_sums)]
        + [(everyone, block_at(4 * heads + h)) for h in range(heads)],
        [
            ((count, D), F32, None),
            ((count, D), F32, None),
            ((count, D), BF16, None),
            ((count, span), F32, None),
            ((count, HEAD), F32, None),
        ],
    )


def attend_cross(places, everyone, pre, key_pre, value, sums, other, vecs, heads):
    count, text = pre.shape[0], value.shape[0]
    per = heads_per_step(heads, 6)
    steps = heads // per

    def body(_, pre_ref, key_ref, value_ref, sum_ref, other_ref, vec_ref, *refs):
        weights, (q_ref, k_ref, o_ref, y_ref, acc) = refs[:per], refs[per:]
        h = pl.program_id(0)
        total = sum_ref[...] + other_ref[...]
        q_inv = lax.rsqrt(total[:, 0:1] / D + NORM_EPS)
        k_inv = lax.rsqrt(unpack_text(total, text) / D + NORM_EPS)
        outs = []
        for j in range(per):
            lanes = slice(j * HEAD, (j + 1) * HEAD)
            q = (pre_ref[:, lanes] * q_inv * vec_ref[8:9, lanes]).astype(BF16)
            k = (key_ref[:, lanes] * k_inv * vec_ref[9:10, lanes]).astype(BF16)
            q_ref[:, lanes] = q
            k_ref[:, lanes] = k
            chance = softmax(nt(q, k) * SCALING)
            out = nn(chance.astype(BF16), value_ref[:, lanes]).astype(BF16)
            o_ref[j] = out
            outs.append(out)
        part = nt(jnp.concatenate(outs, 1), joined(weights))

        @pl.when(h == 0)
        def _():
            acc[...] = part

        @pl.when(h > 0)
        def _():
            acc[...] = acc[...] + part

        @pl.when(h == steps - 1)
        def _():
            y_ref[...] = acc[...].astype(BF16)

    return call(
        body, places, steps,
        [
            (pre, head_lanes(count, per)), (key_pre, head_lanes(text, per)),
            (value, head_lanes(text, per)), (sums, None), (other, None),
            (vecs, head_lanes(vecs.shape[0], per)),
        ]
        + [(everyone, block_at(7 * heads + j, per)) for j in range(per)],
        [
            (pre.shape, BF16, head_lanes(count, per)),
            (value.shape, BF16, head_lanes(text, per)),
            ((heads, count, HEAD), BF16, pl.BlockSpec((per, count, HEAD), lambda h, _: (h, 0, 0))),
            ((count, D), BF16, None),
        ],
        [pltpu.VMEM((count, D), F32)],
        vmem=40,
    )


def hidden_group(blocks):
    return max(g for g in (7, 5, 4, 3, 2, 1) if blocks % g == 0)


def block_lanes(where, everyone, held, sems, first, group, steps):
    i = pl.program_id(0)

    def fetch(step, act):
        slot = step % 2
        for j in range(group):
            copy = pltpu.make_async_copy(
                everyone.at[where[first + step * group + j]],
                held.at[slot, :, pl.ds(j * HEAD, HEAD)],
                sems.at[slot, j],
            )
            copy.start() if act else copy.wait()

    @pl.when(i == 0)
    def _():
        fetch(0, True)

    @pl.when(i + 1 < steps)
    def _():
        fetch(i + 1, True)

    fetch(i, False)
    return held[i % 2]


def lanes_scratch(group):
    return [pltpu.VMEM((2, D, group * HEAD), BF16), pltpu.SemaphoreType.DMA((2, group))]


def hidden_back(places, everyone, mod, cot, heads, blocks):
    count = cot.shape[0]
    group = hidden_group(blocks)
    steps = blocks // group

    def body(where, weights, mod_ref, cot_ref, grad, out, held, sems):
        @pl.when(pl.program_id(0) == 0)
        def _():
            grad[...] = (mod_ref[5:6] * cot_ref[...]).astype(BF16)

        down = block_lanes(where, weights, held, sems, 8 * heads + blocks, group, steps)
        out[...] = nn(grad[...], down).astype(BF16)

    return call(
        body, places, steps,
        [(everyone, ANY), (mod, None), (cot, None)],
        [
            ((count, D), BF16, None),
            ((count, blocks * HEAD), BF16, pl.BlockSpec((count, group * HEAD), lambda i, _: (0, i))),
        ],
        lanes_scratch(group),
        vmem=40,
    )


def hidden_both(places, everyone, after_one, part, other, mod, shared, d_act, up_bias, heads, blocks):
    count = after_one.shape[0]
    group = hidden_group(blocks)
    steps = blocks // group
    span = group * HEAD

    def body(where, weights, after_ref, part_ref, other_ref, mod_ref, shared_ref, d_ref, bias_ref, after, low, hidden, d_hidden, d_bias, da_ref, acc, held, sems):
        i = pl.program_id(0)

        @pl.when(i == 0)
        def _():
            x = after_ref[...] + part_ref[...].astype(F32) + other_ref[...].astype(F32)
            x = x + shared_ref[1:2]
            after[...] = x
            unit, _ = normed(x)
            low[...] = (unit * (1.0 + mod_ref[4:5]) + mod_ref[3:4]).astype(BF16)
            acc[...] = jnp.zeros_like(acc)

        up = block_lanes(where, weights, held, sems, 8 * heads, group, steps)
        pre = nn(low[...], up) + bias_ref[...]
        square = pre * pre
        bent = jnp.tanh(GELU_COEF * (pre + 0.044715 * pre * square))
        act = (0.5 * pre * (1.0 + bent)).astype(BF16)
        slope = 0.5 * (1.0 + bent) + 0.5 * pre * (1.0 - bent * bent) * (
            GELU_COEF * (1.0 + 3.0 * 0.044715 * square)
        )
        dh = (d_ref[...].astype(F32) * slope).astype(BF16)
        d_bias[...] = total_of(dh.astype(F32))
        for j in range(group):
            hidden[j] = act[:, j * HEAD : (j + 1) * HEAD]
            d_hidden[j] = dh[:, j * HEAD : (j + 1) * HEAD]
        acc[...] = acc[...] + nt(dh, up)

        @pl.when(i == steps - 1)
        def _():
            da_ref[...] = acc[...].astype(BF16)

    tall = pl.BlockSpec((group, count, HEAD), lambda i, _: (i, 0, 0))
    flat = pl.BlockSpec((1, span), lambda i, _: (0, i))
    return call(
        body, places, steps,
        [(everyone, ANY)]
        + [(v, None) for v in (after_one, part, other, mod, shared)]
        + [(d_act, pl.BlockSpec((count, span), lambda i, _: (0, i))), (up_bias, flat)],
        [
            ((count, D), F32, None),
            ((count, D), BF16, None),
            ((blocks, count, HEAD), BF16, tall),
            ((blocks, count, HEAD), BF16, tall),
            (up_bias.shape, F32, flat),
            ((count, D), BF16, None),
        ],
        [pltpu.VMEM((count, D), F32)] + lanes_scratch(group),
        vmem=40,
    )


def hidden_out(places, everyone, hidden, heads):
    blocks, count = hidden.shape[:2]
    group = hidden_group(blocks)
    steps = blocks // group

    def body(where, weights, hidden_ref, y_ref, acc, held, sems):
        i = pl.program_id(0)
        down = block_lanes(where, weights, held, sems, 8 * heads + blocks, group, steps)
        part = nt(jnp.concatenate([hidden_ref[j] for j in range(group)], 1), down)

        @pl.when(i == 0)
        def _():
            acc[...] = part

        @pl.when(i > 0)
        def _():
            acc[...] = acc[...] + part

        @pl.when(i == steps - 1)
        def _():
            y_ref[...] = acc[...].astype(BF16)

    return call(
        body, places, steps,
        [(everyone, ANY), (hidden, pl.BlockSpec((group, count, HEAD), lambda i, _: (i, 0, 0)))],
        [((count, D), BF16, None)],
        [pltpu.VMEM((count, D), F32)] + lanes_scratch(group),
        vmem=40,
    )[0]


def cross_back(places, everyone, cot, after_two, part, other, mod, query, key, value, pre, key_pre, vecs, heads):
    count, text = query.shape[0], key.shape[0]
    per = heads_per_step(heads, 6)
    steps = heads // per

    def body(_, cot_ref, after_ref, part_ref, other_ref, mod_ref, q_ref, k_ref, v_ref, pre_ref, key_ref, vec_ref, *refs):
        weights, (dx_ref, low_ref, dq_ref, dk_ref, dv_ref, sums, q_acc, k_acc) = refs[:per], refs[per:]
        h = pl.program_id(0)

        @pl.when(h == 0)
        def _():
            da = part_ref[...].astype(F32) + other_ref[...].astype(F32)
            back, _ = normed_back(after_ref[...], da * (1.0 + mod_ref[4:5]))
            dx = cot_ref[...] + back
            dx_ref[...] = dx
            low_ref[...] = dx.astype(BF16)
            q_acc[...] = jnp.zeros_like(q_acc)
            k_acc[...] = jnp.zeros_like(k_acc)

        do_all = nn(low_ref[...], joined(weights)).astype(BF16)
        q_sums, k_sums = 0.0, 0.0
        for j in range(per):
            lanes = slice(j * HEAD, (j + 1) * HEAD)
            do = do_all[:, lanes]
            q, k = q_ref[:, lanes], k_ref[:, lanes]
            chance = softmax(nt(q, k) * SCALING)
            dp = nt(do, v_ref[:, lanes])
            ds = (chance * (dp - jnp.sum(chance * dp, -1, keepdims=True))).astype(BF16)
            dv_ref[j] = tn(chance.astype(BF16), do).astype(BF16)
            dq = nn(ds, k) * SCALING
            dk = tn(ds, q) * SCALING
            dq_ref[:, lanes] = dq
            dk_ref[:, lanes] = dk
            q_sums += pre_ref[:, lanes] * vec_ref[8:9, lanes] * dq
            k_sums += key_ref[:, lanes] * vec_ref[9:10, lanes] * dk
        q_acc[...] = q_acc[...] + q_sums
        k_acc[...] = k_acc[...] + k_sums

        @pl.when(h == steps - 1)
        def _():
            sums[...] = pack_sums(
                jnp.sum(q_acc[...], -1, keepdims=True), jnp.sum(k_acc[...], -1, keepdims=True)
            )

    return call(
        body, places, steps,
        [(v, None) for v in (cot, after_two, part, other, mod)]
        + [
            (query, head_lanes(count, per)), (key, head_lanes(text, per)),
            (value, head_lanes(text, per)), (pre, head_lanes(count, per)),
            (key_pre, head_lanes(text, per)), (vecs, head_lanes(vecs.shape[0], per)),
        ]
        + [(everyone, block_at(7 * heads + j, per)) for j in range(per)],
        [
            ((count, D), F32, None),
            ((count, D), BF16, None),
            (query.shape, F32, head_lanes(count, per)),
            (key.shape, F32, head_lanes(text, per)),
            ((heads, text, HEAD), BF16, pl.BlockSpec((per, text, HEAD), lambda h, _: (h, 0, 0))),
            ((count, HEAD), F32, None),
        ],
        [pltpu.VMEM((count, HEAD), F32), pltpu.VMEM((text, HEAD), F32)],
        vmem=48,
    )


def norm_grad(pre, inverse, gain, incoming, total):
    grad = inverse * (gain * incoming) - pre * (inverse * inverse * inverse) * (total / D)
    low = grad.astype(BF16)
    return low, total_of(low.astype(F32)), total_of(incoming * pre * inverse)


def cross_back_rows(places, everyone, pre, key_pre, dq, dk, dv, squares, squares_other, sums, sums_other, vecs, heads):
    count, text = pre.shape[0], key_pre.shape[0]
    per = heads_per_step(heads, 6)
    steps = heads // per

    def body(_, pre_ref, key_ref, dq_ref, dk_ref, dv_ref, sq_ref, sqo_ref, sum_ref, sumo_ref, vec_ref, *refs):
        weights, (gq_ref, gk_ref, vec_out, da_ref, acc) = refs[:per], refs[per:]
        h = pl.program_id(0)
        squares_all = sq_ref[...] + sqo_ref[...]
        total = sum_ref[...] + sumo_ref[...]
        q_inv = lax.rsqrt(squares_all[:, 0:1] / D + NORM_EPS)
        k_inv = lax.rsqrt(unpack_text(squares_all, text) / D + NORM_EPS)
        q_total, k_total = total[:, 0:1], unpack_text(total, text)
        lows = []
        for j in range(per):
            lanes = slice(j * HEAD, (j + 1) * HEAD)
            low_q, bias_q, gain_q = norm_grad(
                pre_ref[:, lanes], q_inv, vec_ref[8:9, lanes], dq_ref[:, lanes], q_total
            )
            low_k, bias_k, gain_k = norm_grad(
                key_ref[:, lanes], k_inv, vec_ref[9:10, lanes], dk_ref[:, lanes], k_total
            )
            gq_ref[j] = low_q
            gk_ref[j] = low_k
            lows.append(low_q)
            bias_v = total_of(dv_ref[j].astype(F32))
            vec_out[:, lanes] = jnp.concatenate(
                [bias_q, bias_k, bias_v, gain_q, gain_k, jnp.zeros((3, HEAD), F32)], 0
            )
        part = nt(jnp.concatenate(lows, 1), joined(weights))

        @pl.when(h == 0)
        def _():
            acc[...] = part

        @pl.when(h > 0)
        def _():
            acc[...] = acc[...] + part

        @pl.when(h == steps - 1)
        def _():
            da_ref[...] = acc[...].astype(BF16)

    tall = pl.BlockSpec((per, count, HEAD), lambda h, _: (h, 0, 0))
    tall_text = pl.BlockSpec((per, text, HEAD), lambda h, _: (h, 0, 0))
    return call(
        body, places, steps,
        [
            (pre, head_lanes(count, per)), (key_pre, head_lanes(text, per)),
            (dq, head_lanes(count, per)), (dk, head_lanes(text, per)), (dv, tall_text),
            (squares, None), (squares_other, None), (sums, None), (sums_other, None),
            (vecs, head_lanes(vecs.shape[0], per)),
        ]
        + [(everyone, block_at(4 * heads + j, per)) for j in range(per)],
        [
            ((heads, count, HEAD), BF16, tall),
            ((heads, text, HEAD), BF16, tall_text),
            ((8, heads * HEAD), F32, head_lanes(8, per)),
            ((count, D), BF16, None),
        ],
        [pltpu.VMEM((count, D), F32)],
        vmem=40,
    )


def self_back(places, everyone, dx_two, after_one, part, other, mod, shared, branch, query, key, value, pre, vecs, cos_tab, sin_tab, heads, tokens):
    count = query.shape[0]
    per = heads_per_step(heads, 2)
    steps = heads // per

    def body(_, dx_in, after_ref, part_ref, other_ref, mod_ref, shared_ref, branch_ref, q_ref, k_ref, v_ref, pre_ref, vec_ref, cos_ref, sin_ref, *refs):
        weights, (dx_ref, low_ref, d_ref, dv_ref, sums, vec_out, q_acc, k_acc) = refs[:per], refs[per:]
        h = pl.program_id(0)

        @pl.when(h == 0)
        def _():
            da = part_ref[...].astype(F32) + other_ref[...].astype(F32)
            back, _ = normed_back(after_ref[...], da * shared_ref[3:4])
            dx = dx_in[...] + back
            dx_ref[...] = dx
            low = (mod_ref[2:3] * dx).astype(BF16)
            low_ref[...] = low
            vec_out[0:1] = 0.5 * total_of(low.astype(F32))
            vec_out[1:2] = 0.5 * total_of(dx * branch_ref[...])
            q_acc[...] = jnp.zeros_like(q_acc)
            k_acc[...] = jnp.zeros_like(k_acc)

        do_all = nn(low_ref[...], joined(weights)).astype(BF16)
        cos, sin = cos_ref[...], -sin_ref[...]
        q_sums, k_sums = 0.0, 0.0
        for j in range(per):
            lanes = slice(j * HEAD, (j + 1) * HEAD)
            do = do_all[:, lanes]
            q, k = q_ref[:, lanes], k_ref[:, lanes]
            chance = softmax(self_scores(q, k, tokens))
            dp = nt(do, v_ref[:, lanes])
            ds = (chance * (dp - jnp.sum(chance * dp, -1, keepdims=True))).astype(BF16)
            dv_ref[j] = tn(chance.astype(BF16), do).astype(BF16)
            dq = turned(nn(ds, k) * SCALING, cos, sin)
            dk = turned(tn(ds, q) * SCALING, cos, sin)
            d_ref[0, :, lanes] = dq
            d_ref[1, :, lanes] = dk
            q_sums += pre_ref[0, :, lanes] * vec_ref[3:4, lanes] * dq
            k_sums += pre_ref[1, :, lanes] * vec_ref[4:5, lanes] * dk
        q_acc[...] = q_acc[...] + q_sums
        k_acc[...] = k_acc[...] + k_sums

        @pl.when(h == steps - 1)
        def _():
            lane = lax.broadcasted_iota(jnp.int32, q_acc.shape, 1)
            sums[...] = jnp.where(
                lane < 64,
                wide(jnp.sum(q_acc[...], -1, keepdims=True)),
                wide(jnp.sum(k_acc[...], -1, keepdims=True)),
            )

    lanes = head_lanes(count, per)
    pair = pl.BlockSpec((2, count, per * HEAD), lambda h, _: (0, 0, h))
    return call(
        body, places, steps,
        [(v, None) for v in (dx_two, after_one, part, other, mod, shared, branch)]
        + [
            (query, lanes), (key, lanes), (value, lanes), (pre, pair),
            (vecs, head_lanes(vecs.shape[0], per)), (cos_tab, None), (sin_tab, None),
        ]
        + [(everyone, block_at(3 * heads + j, per)) for j in range(per)],
        [
            ((count, D), F32, None),
            ((count, D), BF16, None),
            (pre.shape, F32, pair),
            ((heads, count, HEAD), BF16, pl.BlockSpec((per, count, HEAD), lambda h, _: (h, 0, 0))),
            ((count, HEAD), F32, None),
            ((2, D), F32, None),
        ],
        [pltpu.VMEM((count, HEAD), F32), pltpu.VMEM((count, HEAD), F32)],
        vmem=32,
    )


def self_back_rows(places, everyone, rows, pre, grads, dv, squares, squares_other, sums, sums_other, vecs, heads):
    count = pre.shape[1]
    per = heads_per_step(heads, 2)
    steps = heads // per

    def body(_, rows_ref, pre_ref, d_ref, dv_ref, sq_ref, sqo_ref, sum_ref, sumo_ref, vec_ref, *refs):
        weights, (gq_ref, gk_ref, vec_out, da_ref, row_out, acc) = refs[: 3 * per], refs[3 * per :]
        h = pl.program_id(0)
        squares_all = sq_ref[...] + sqo_ref[...]
        total = sum_ref[...] + sumo_ref[...]
        inverses = [
            lax.rsqrt(squares_all[:, n : n + 1] / D + NORM_EPS) for n in (0, 64)
        ]
        lows = []
        for j in range(per):
            lanes = slice(j * HEAD, (j + 1) * HEAD)
            biases, gains = [], []
            for n, out in enumerate((gq_ref, gk_ref)):
                low, bias, gain = norm_grad(
                    pre_ref[n, :, lanes], inverses[n], vec_ref[3 + n : 4 + n, lanes],
                    d_ref[n, :, lanes], total[:, 64 * n : 64 * n + 1],
                )
                out[j] = low
                lows.append(low)
                biases.append(bias)
                gains.append(gain)
            dv_low = dv_ref[j]
            lows.append(dv_low)
            vec_out[:, lanes] = jnp.concatenate(
                biases + [total_of(dv_low.astype(F32))] + gains + [jnp.zeros((3, HEAD), F32)], 0
            )
        part = nt(jnp.concatenate(lows, 1), joined(weights))

        @pl.when(h == 0)
        def _():
            acc[...] = part

        @pl.when(h > 0)
        def _():
            acc[...] = acc[...] + part

        @pl.when(h == steps - 1)
        def _():
            da = acc[...]
            da_ref[...] = da.astype(BF16)
            row_out[0:1] = total_of(da)
            row_out[1:2] = total_of(da * normed(rows_ref[...])[0])

    tall = pl.BlockSpec((per, count, HEAD), lambda h, _: (h, 0, 0))
    pair = pl.BlockSpec((2, count, per * HEAD), lambda h, _: (0, 0, h))
    return call(
        body, places, steps,
        [
            (rows, None), (pre, pair), (grads, pair), (dv, tall), (squares, None),
            (squares_other, None), (sums, None), (sums_other, None),
            (vecs, head_lanes(vecs.shape[0], per)),
        ]
        + [(everyone, block_at(n * heads + j, per)) for j in range(per) for n in range(3)],
        [
            ((heads, count, HEAD), BF16, tall),
            ((heads, count, HEAD), BF16, tall),
            ((8, heads * HEAD), F32, head_lanes(8, per)),
            ((count, D), BF16, None),
            ((2, D), F32, None),
        ],
        [pltpu.VMEM((count, D), F32)],
        vmem=40,
    )


def shared_sums(places, after_one, after_two, grad_two, grad_three, cot, da_two, da_three, y_three, shared):
    def body(_, x1_ref, x2_ref, dy2, dy3, cot_ref, da2, da3, y3, shared_ref, out):
        out[...] = jnp.zeros_like(out)
        out[1:2] = 0.5 * total_of(dy2[...].astype(F32))
        out[2:3] = 0.5 * total_of(dy3[...].astype(F32))
        part = da3[...].astype(F32)
        out[3:4] = total_of(part * normed(x1_ref[...])[0])
        out[4:5] = total_of(part)
        part = da2[...].astype(F32)
        out[8:9] = total_of(part)
        out[9:10] = total_of(part * normed(x2_ref[...])[0])
        out[10:11] = total_of(cot_ref[...] * (y3[...].astype(F32) + 0.5 * shared_ref[2:3]))

    return call(
        body, places, 1,
        [(v, None) for v in (after_one, after_two, grad_two, grad_three, cot, da_two, da_three, y_three, shared)],
        [(shared.shape, F32, None)],
    )[0]


def body(
    latents,
    context,
    cotangent,
    positions,
    step_ids,
    owners,
    time_table,
    master,
    first_moment,
    second_moment,
    head_params,
    head_first,
    head_second,
    shared_params,
    shared_first,
    shared_second,
):
    tensors = lax.axis_size("tensor")
    devices = lax.axis_size("dp")
    slot_count = master.shape[1]
    tile_count = owners.shape[0]
    heads_here = HEADS // tensors
    blocks_here = FF // (HEAD * tensors)
    width_here = D // tensors
    places, holder = owner_layout(owners, slot_count, devices)
    scales = tile_scales(tile_count, heads_here, blocks_here)
    my_slots = lax.dynamic_slice_in_dim(holder, lax.axis_index("dp") * slot_count, slot_count)
    rank = pair_rank()
    filled = my_slots >= 0
    slot_scale = jnp.where(filled, scales[jnp.maximum(my_slots, 0)], 0.0)
    scaled = (master[0] * slot_scale[:, None, None]).astype(jnp.bfloat16)
    half = latents.shape[0]
    tokens = 2 * half
    count = -(-tokens // 16) * 16
    taller = ((0, -half % 16), (0, 0))
    small = jnp.concatenate(
        [
            head_params[0],
            positions.reshape(-1).astype(jnp.float32),
            step_ids.astype(jnp.float32),
        ]
    )
    packed = jnp.pad(small, (0, -small.shape[0] % 1024)).reshape(-1, HEAD)
    everyone, lats, cots, context, packed = gather_slots(
        scaled, jnp.pad(latents, taller), jnp.pad(cotangent, taller), context, packed
    )
    small = packed.reshape(-1)
    vectors = small[: head_params.shape[1]]
    small = small[head_params.shape[1] :]
    positions = small[: positions.size].reshape(positions.shape)
    step = small[positions.size]
    vecs = vectors[: 10 * width_here].reshape(10, width_here)
    up_bias = vectors[10 * width_here :].reshape(1, -1)
    chosen = (step == jnp.arange(TSTEPS)).astype(jnp.float32)
    mod = shared_params[5:11] + jnp.einsum(
        "s,skd->kd", chosen, time_table, precision=lax.Precision.HIGHEST
    )
    cos_tab, sin_tab = rope_tables(positions, HEAD)
    sin_tab = jnp.where(jnp.arange(HEAD) % 2 == 0, -sin_tab, sin_tab)
    cos_tab, sin_tab = (jnp.pad(t, ((0, count - tokens), (0, 0))) for t in (cos_tab, sin_tab))

    def all_rows(halves):
        rows = jnp.concatenate([halves[0, :half], halves[1, :half]], 0)
        return jnp.pad(rows, ((0, count - tokens), (0, 0))).astype(jnp.float32)

    def upright(rows):
        return jnp.pad(rows, ((0, context.shape[0] - rows.shape[0]), (0, 0))).T

    def beside(*values):
        return lax.optimization_barrier(values)

    rows, cot = all_rows(lats), all_rows(cots)
    low_one, pre_one, value_one, squares_one = project_self(
        places, everyone, rows, mod, vecs, heads_here
    )
    squares_one_other = pair_swap(squares_one)
    query_one, key_one, heads_one, part_one = attend_self(
        places, everyone, pre_one, value_one, squares_one, squares_one_other, vecs, cos_tab,
        sin_tab, heads_here, tokens,
    )
    part_one, context = beside(part_one, context)
    part_one_other = pair_swap(part_one)
    key_pre, value_two, text_squares = project_text(places, everyone, context, vecs, heads_here)
    left_context, left_one = upright(context), upright(low_one)
    part_one_other, key_pre, left_context, left_one = beside(
        part_one_other, key_pre, left_context, left_one
    )
    branch_one, after_one, low_two, pre_two, squares_two = project_cross(
        places, everyone, rows, part_one, part_one_other, mod, shared_params, vecs,
        text_squares, heads_here,
    )
    squares_two_other = pair_swap(squares_two)
    query_two, key_two, heads_two, part_two = attend_cross(
        places, everyone, pre_two, key_pre, value_two, squares_two, squares_two_other, vecs,
        heads_here,
    )
    part_two, cot, low_two = beside(part_two, cot, low_two)
    part_two_other = pair_swap(part_two)
    grad_three, d_act = hidden_back(places, everyone, mod, cot, heads_here, blocks_here)
    left_two, left_grad_three = upright(low_two), upright(grad_three)
    part_two_other, d_act, left_two, left_grad_three = beside(
        part_two_other, d_act, left_two, left_grad_three
    )
    after_two, low_three, hidden, d_hidden, d_up_bias, da_two = hidden_both(
        places, everyone, after_one, part_two, part_two_other, mod, shared_params, d_act, up_bias,
        heads_here, blocks_here,
    )
    da_two_other = pair_swap(da_two)
    y_three = hidden_out(places, everyone, hidden, heads_here)
    left_three = upright(low_three)
    da_two_other, y_three, left_three = beside(da_two_other, y_three, left_three)
    dx_two, grad_two, dq_two, dk_two, dv_two, sums_two = cross_back(
        places, everyone, cot, after_two, da_two, da_two_other, mod, query_two, key_two,
        value_two, pre_two, key_pre, vecs, heads_here,
    )
    query_grad_two, key_grad_two, vecs_two, da_three = cross_back_rows(
        places, everyone, pre_two, key_pre, dq_two, dk_two, dv_two, squares_two,
        squares_two_other, sums_two, pair_swap(sums_two), vecs, heads_here,
    )
    da_three_other = pair_swap(da_three)
    shared_grad = shared_sums(
        places, after_one, after_two, grad_two, grad_three, cot, da_two, da_three, y_three,
        shared_params,
    )
    left_grad_two = upright(grad_two)
    da_three_other, shared_grad, left_grad_two = beside(da_three_other, shared_grad, left_grad_two)
    dx_one, grad_one, d_one, dv_one, sums_one, rows_a = self_back(
        places, everyone, dx_two, after_one, da_three, da_three_other, mod, shared_params,
        branch_one, query_one, key_one, value_one, pre_one, vecs, cos_tab, sin_tab, heads_here,
        tokens,
    )
    query_grad_one, key_grad_one, vecs_one, da_one, rows_b = self_back_rows(
        places, everyone, rows, pre_one, d_one, dv_one, squares_one, squares_one_other, sums_one,
        pair_swap(sums_one), vecs, heads_here,
    )
    shared_grad = jnp.concatenate(
        [rows_a[0:1], shared_grad[1:5], rows_b, rows_a[1:2], shared_grad[8:]], 0
    )
    head_grad = jnp.concatenate(
        [vecs_one[:5].reshape(-1), vecs_two[:5].reshape(-1), d_up_bias.reshape(-1)]
    )
    tensor_rank = lax.axis_index("tensor")
    head_padded = jnp.where(jnp.arange(tensors)[:, None] == rank, head_grad[None, :], 0.0)
    vector = jnp.concatenate([head_padded.reshape(-1), shared_grad.reshape(-1)])
    vector = jnp.pad(vector, (0, -vector.shape[0] % 1024)).reshape(-1, 128)
    parts, vector, output, grad_input = reduce_slots(
        holder,
        kind_of_blocks(tile_count, heads_here, blocks_here),
        (left_one, upright(grad_one), left_two, left_context, left_grad_two, left_three, left_grad_three),
        (
            query_grad_one,
            key_grad_one,
            dv_one,
            heads_one,
            query_grad_two,
            key_grad_two,
            dv_two,
            heads_two,
            d_hidden,
            hidden,
        ),
        vector,
        (rows, after_two, dx_one, y_three, da_one),
        jnp.concatenate([mod[5:6], mod[1:2], shared_params[2:3], jnp.zeros((5, D), F32)], 0),
        slot_count,
    )
    output, grad_input = (
        jnp.where(lax.axis_index("tensor") == 0, v[:half], v[half:tokens])
        for v in (output, grad_input)
    )
    new_master, new_first, new_second = adam_slots(
        parts, master, first_moment, second_moment, slot_scale, filled
    )
    vector = vector.reshape(-1)
    head_total = vector[: head_padded.size].reshape(head_padded.shape)
    shared_total = vector[head_padded.size : head_padded.size + shared_grad.size]
    shared_total = shared_total.reshape(shared_grad.shape)
    mine_head = lax.dynamic_slice_in_dim(head_total, tensor_rank, 1, 0)
    new_head, new_head_first, new_head_second = adam_step(
        head_params, mine_head, head_first, head_second, VECTOR_RATE, 0.0
    )
    new_shared, new_shared_first, new_shared_second = adam_step(
        shared_params, shared_total, shared_first, shared_second, VECTOR_RATE, 0.0
    )
    return (
        output,
        grad_input,
        new_master,
        new_first,
        new_second,
        new_head,
        new_head_first,
        new_head_second,
        new_shared,
        new_shared_first,
        new_shared_second,
    )


def solution(mesh):
    return jax.shard_map(
        body,
        mesh=mesh,
        in_specs=(
            P(("dp", "tensor"), None),
            P("dp", None),
            P(("dp", "tensor"), None),
            P(None, "dp"),
            P("dp"),
            P(),
            P(),
            P("tensor", "dp", None, None),
            P("tensor", "dp", None, None),
            P("tensor", "dp", None, None),
            P("tensor", None),
            P("tensor", None),
            P("tensor", None),
            P(),
            P(),
            P(),
        ),
        out_specs=(
            P(("dp", "tensor"), None),
            P(("dp", "tensor"), None),
            P("tensor", "dp", None, None),
            P("tensor", "dp", None, None),
            P("tensor", "dp", None, None),
            P("tensor", None),
            P("tensor", None),
            P("tensor", None),
            P(),
            P(),
            P(),
        ),
        check_vma=False,
    )
```

```python
import functools

import jax
import jax.numpy as jnp
from jax import lax
from jax.experimental import pallas as pl
from jax.experimental.pallas import tpu as pltpu
from jax.sharding import PartitionSpec as P

D = 1536
HEADS = 12
HEAD = 128
FF = 8960
TSTEPS = 16
STEPC = 10


NORM_EPS = 1e-06
BETA_ONE = 0.9
BETA_TWO = 0.999
ADAM_EPS = 1e-08
TILE_RATE = 1.0
TILE_DECAY = 0.1
VECTOR_RATE = 0.5
GELU_COEF = 0.7978845608028654


def rope_tables(token_places, head_size):
    sixths = head_size // 6
    frame_pairs = (head_size - 4 * sixths) // 2
    frame_freq = 10000.0 ** (-jnp.arange(frame_pairs, dtype=jnp.float32) / frame_pairs)
    side_freq = 10000.0 ** (-jnp.arange(sixths, dtype=jnp.float32) / sixths)
    spots = token_places.astype(jnp.float32)
    angles = jnp.concatenate(
        [
            spots[0][..., None] * frame_freq,
            spots[1][..., None] * side_freq,
            spots[2][..., None] * side_freq,
        ],
        -1,
    )
    angles = jnp.repeat(angles, 2, axis=-1)
    return (jnp.cos(angles), jnp.sin(angles))


def owner_layout(owners, slot_count, devices):
    indices = jnp.arange(owners.shape[0], dtype=jnp.int32)
    same_owner = (owners[:, None] == owners[None, :]) & (indices[None, :] < indices[:, None])
    slot_of = jnp.sum(same_owner.astype(jnp.int32), axis=1)
    places = owners * slot_count + slot_of
    spots = jnp.arange(slot_count * devices, dtype=jnp.int32)
    holder = (
        jnp.sum(jnp.where(places[None, :] == spots[:, None], indices[None, :] + 1, 0), axis=1) - 1
    )
    return (places, holder)


def tile_scales(tile_count, heads_here, blocks_here):
    indices = jnp.arange(tile_count)
    scale_in = D ** (-0.5)
    scale_out = HEADS ** (-0.5)
    scale_down = FF ** (-0.5)
    scales = jnp.where(
        indices < 3 * heads_here,
        scale_in,
        jnp.where(
            indices < 4 * heads_here,
            scale_out,
            jnp.where(
                indices < 7 * heads_here,
                scale_in,
                jnp.where(
                    indices < 8 * heads_here,
                    scale_out,
                    jnp.where(indices < 8 * heads_here + blocks_here, scale_in, scale_down),
                ),
            ),
        ),
    )
    return scales.astype(jnp.float32)


def adam_step(weight, gradient, moment_one, moment_two, step_rate, decay_rate):
    first_new = BETA_ONE * moment_one + (1.0 - BETA_ONE) * gradient
    second_new = BETA_TWO * moment_two + (1.0 - BETA_TWO) * gradient * gradient
    first_hat = first_new / (1.0 - BETA_ONE**STEPC)
    second_hat = second_new / (1.0 - BETA_TWO**STEPC)
    weight_new = weight - step_rate * (
        first_hat / (jnp.sqrt(second_hat) + ADAM_EPS) + decay_rate * weight
    )
    return (weight_new, first_new, second_new)


MESH = pl.DeviceIdType.MESH
ANY = pl.BlockSpec(memory_space=pl.ANY)
MIB = 1 << 20


def chip_pairs():
    return lax.axis_size("dp") == 16 and lax.axis_size("tensor") == 2


def pair_rank():
    if chip_pairs():
        return (lax.axis_index("dp") // 4) % 2
    return lax.axis_index("tensor")


def pair_swap(value):
    if chip_pairs():
        return lax.ppermute(value, "dp", [(i, i ^ 4) for i in range(16)])
    return lax.ppermute(value, "tensor", [(0, 1), (1, 0)])


def pair_sums(*values):
    stacked = jnp.concatenate([v.reshape(-1) for v in values])
    total = stacked + pair_swap(stacked)
    out, at = [], 0
    for v in values:
        out.append(total[at : at + v.size].reshape(v.shape))
        at += v.size
    return tuple(out)


def place_of():
    chip, core = lax.axis_index("dp"), lax.axis_index("tensor")
    z, y, x = chip // 4, (chip // 2) % 2, chip % 2
    return chip, core, z, y, x


def column_of(z, y, x, k):
    high, low_bit = z // 2, z % 2
    if k & 2:
        high = 1 - high
    if k & 1:
        low_bit = 1 - low_bit
    return (2 * high + low_bit) * 4 + 2 * y + x


def greet(chip, core, z, y, x):
    barrier = pltpu.get_barrier_semaphore()
    friends = []
    for k in range(4):
        for flip in (0, 1):
            if k or flip:
                friends.append((column_of(z, y, x, k), core if flip == 0 else 1 - core))
    friends.append((column_of(z, y, 1 - x, 0), core))
    friends.append((column_of(z, 1 - y, x, 0), core))
    for friend in friends:
        pl.semaphore_signal(barrier, inc=1, device_id=friend, device_id_type=MESH)
    pl.semaphore_wait(barrier, len(friends))


def gather_kernel(
    own, lat, cot, text, small, out, lats, cots, texts, smalls, clip_s, clip_r,
    near_s, col_r, x_s, x_r, y_s, y_r, sib_s, sib_r,
):
    chip, core, z, y, x = place_of()
    rank = z % 2
    half = own.shape[1] // 2
    part = half // 2
    at_x = column_of(z, y, 1 - x, 0)
    at_y = column_of(z, 1 - y, x, 0)
    greet(chip, core, z, y, x)

    batch = max(n for n in (1, 2, 3) if own.shape[0] % n == 0)
    batches = own.shape[0] // batch
    turns = 4 * batches

    def case(s):
        late = jnp.maximum(s - batches, 0)
        k = jnp.where(s < batches, 0, 1 + late % 3)
        return k, jnp.where(s < batches, s, late // 3)

    def remote(unit, g, first, count, send, recv, device):
        piece = out.at[
            unit, pl.ds(g * batch, batch), pl.ds(pl.multiple_of(first, 16), count), :
        ]
        return pltpu.make_async_remote_copy(
            src_ref=piece, dst_ref=piece, send_sem=send, recv_sem=recv,
            device_id=device, device_id_type=MESH,
        )

    def own_copy(g, j, h):
        target = (toggled(z, y, x, 0, 0, 2 * j) // 8 * 8) + core * 4 + 2 * y + x
        part_of = (pl.ds(g * batch, batch), pl.ds(h * half, half))
        src = own.at[part_of[0], part_of[1], :]
        dst = out.at[chip, part_of[0], part_of[1], :]
        recv = col_r.at[z * batches + g]
        go = pltpu.make_async_remote_copy(
            src_ref=src, dst_ref=dst, send_sem=near_s.at[(2 * j + h) * batches + g],
            recv_sem=recv, device_id=(target, h), device_id_type=MESH,
        )
        return go, pltpu.make_async_copy(src, dst, recv)

    for g in range(batches):
        for j in range(2):
            for h in range(2):
                go, here = own_copy(g, j, h)
                if j == 1:
                    go.start()
                    continue
                stays = jnp.logical_and(rank == core, core == h)

                @pl.when(stays)
                def _():
                    here.start()

                @pl.when(jnp.logical_not(stays))
                def _():
                    go.start()

    pair_chip = column_of(z, y, x, 1)
    rows_of_text = text.shape[0] // 2

    def clip_pieces(h):
        share = pl.ds(h * rows_of_text, rows_of_text)
        return ((lat, lats.at[h]), (cot, cots.at[h]), (text.at[share], texts.at[share]))

    home = rank == core
    trade = pltpu.make_async_remote_copy(
        src_ref=small, dst_ref=smalls, send_sem=clip_s.at[6], recv_sem=clip_r.at[6],
        device_id=(pair_chip, 1 - core), device_id_type=MESH,
    )
    keep = pltpu.make_async_copy(small, smalls, clip_r.at[6])

    @pl.when(home)
    def _():
        keep.start()

    @pl.when(jnp.logical_not(home))
    def _():
        trade.start()

    def hand_out(h, n, wait):
        src, dst = clip_pieces(h)[n]
        far = pltpu.make_async_remote_copy(
            src_ref=src, dst_ref=dst, send_sem=clip_s.at[n], recv_sem=clip_r.at[3 * h + n],
            device_id=(pair_chip, rank), device_id_type=MESH,
        )
        near = pltpu.make_async_remote_copy(
            src_ref=src, dst_ref=dst, send_sem=clip_s.at[3 + n], recv_sem=clip_r.at[3 * h + n],
            device_id=(chip, 1 - core), device_id_type=MESH,
        )
        here = pltpu.make_async_copy(src, dst, clip_r.at[3 * h + n])

        @pl.when(core == h)
        def _():
            if wait:
                far.wait_send()
            else:
                far.start()

            @pl.when(home)
            def _():
                if not wait:
                    here.start()

            @pl.when(jnp.logical_not(home))
            def _():
                if wait:
                    near.wait_send()
                else:
                    near.start()

    for n in range(3):
        for h in range(2):
            hand_out(h, n, False)

    mine, other = core * half, (1 - core) * half
    sibling = (chip, 1 - core)

    def to_x(s, n):
        k, g = case(s)
        i = turns * n + s
        unit = toggled(z, y, x, n, 0, k)
        return remote(unit, g, mine, part if n else half, x_s.at[i], x_r.at[i], (at_x, core))

    def from_x(s, n):
        k, g = case(s)
        i = turns * n + s
        unit = toggled(z, y, x, n, 1, k)
        return remote(unit, g, mine, part if n else half, x_s.at[i], x_r.at[i], (at_x, core))

    def to_y(s, n):
        k, g = case(s)
        i = turns * n + s
        unit = toggled(z, y, x, 0, n, k)
        first, count = (mine + part, part) if n else (mine, half)
        return remote(unit, g, first, count, y_s.at[i], y_r.at[i], (at_y, core))

    def from_y(s, n):
        k, g = case(s)
        i = turns * n + s
        unit = toggled(z, y, x, 1, n, k)
        first, count = (mine + part, part) if n else (mine, half)
        return remote(unit, g, first, count, y_s.at[i], y_r.at[i], (at_y, core))

    def to_sib(s, n, away=False):
        k, g = case(s)
        i = turns * n + s
        unit = toggled(z, y, x, int(n in (2, 3, 4)), int(n in (1, 3, 4)), k)
        first = (other if away else mine) + (part if n == 4 else 0)
        return remote(
            unit, g, first, part if n >= 3 else half, sib_s.at[i], sib_r.at[i], sibling
        )

    def column_in(s):
        k, g = case(s)
        unit = toggled(z, y, x, 0, 0, k)
        piece = out.at[
            unit, pl.ds(g * batch, batch), pl.ds(pl.multiple_of(mine, 16), half), :
        ]
        pltpu.make_async_copy(piece, piece, col_r.at[unit // 4 * batches + g]).wait()
        to_x(s, 0).start()
        to_y(s, 0).start()
        to_sib(s, 0).start()

    def side_in(s):
        from_x(s, 0).wait_recv()
        to_y(s, 1).start()
        to_sib(s, 1).start()
        from_y(s, 0).wait_recv()
        to_x(s, 1).start()
        to_sib(s, 2).start()

    def corner_in(s):
        from_x(s, 1).wait_recv()
        to_sib(s, 3).start()
        from_y(s, 1).wait_recv()
        to_sib(s, 4).start()

    def turn(step, carry):
        @pl.when(step < turns)
        def _():
            column_in(step)

        @pl.when(jnp.logical_and(step >= 1, step < turns + 1))
        def _():
            side_in(step - 1)

        @pl.when(step >= 2)
        def _():
            corner_in(step - 2)

        return carry

    lax.fori_loop(0, turns + 2, turn, 0)

    def settle(s, carry):
        for n in range(2):
            to_x(s, n).wait_send()
            to_y(s, n).wait_send()
        for n in range(5):
            to_sib(s, n).wait_send()
            to_sib(s, n, True).wait_recv()
        return carry

    lax.fori_loop(0, turns, settle, 0)
    for g in range(batches):
        for j in range(2):
            for h in range(2):
                go, _ = own_copy(g, j, h)
                if j == 1:
                    go.wait_send()
                    continue

                @pl.when(jnp.logical_not(jnp.logical_and(rank == core, core == h)))
                def _():
                    go.wait_send()

    for n in range(3):
        for h in range(2):
            hand_out(h, n, True)
            dst = clip_pieces(h)[n][1]
            pltpu.make_async_copy(dst, dst, clip_r.at[3 * h + n]).wait()

    @pl.when(jnp.logical_not(home))
    def _():
        trade.wait_send()

    pltpu.make_async_copy(smalls, smalls, clip_r.at[6]).wait()


def gather_slots(scaled, lat, cot, text, small):
    if not chip_pairs():
        everyone = lax.all_gather(scaled, "dp", axis=0, tiled=True)
        lats, cots = (lax.all_gather(v, "tensor") for v in (lat, cot))
        return everyone, lats, cots, text, small
    dma = pltpu.SemaphoreType.DMA
    turns = 4 * scaled.shape[0] // max(n for n in (1, 2, 3) if scaled.shape[0] % n == 0)
    counts = (7, 7, turns, turns) + (2 * turns,) * 4 + (5 * turns,) * 2
    everyone, *rest = pl.pallas_call(
        gather_kernel,
        out_shape=[
            jax.ShapeDtypeStruct((16,) + scaled.shape, scaled.dtype),
            jax.ShapeDtypeStruct((2,) + lat.shape, lat.dtype),
            jax.ShapeDtypeStruct((2,) + cot.shape, cot.dtype),
            jax.ShapeDtypeStruct(text.shape, text.dtype),
            jax.ShapeDtypeStruct(small.shape, small.dtype),
        ],
        in_specs=[ANY] * 5,
        out_specs=[ANY] * 5,
        scratch_shapes=[dma((n,)) for n in counts],
        compiler_params=pltpu.CompilerParams(
            collective_id=0, has_side_effects=True, vmem_limit_bytes=4 * MIB
        ),
    )(scaled, lat, cot, text, small)
    return everyone.reshape((-1,) + scaled.shape[1:]), *rest


def toggled(z, y, x, flip_y, flip_x, k):
    high = (z // 2 + k // 2) % 2
    low_bit = (z % 2 + k % 2) % 2
    return (2 * high + low_bit) * 4 + 2 * ((y + flip_y) % 2) + (x + flip_x) % 2


def reduce_kernel(
    kind, block, *refs,
):
    (
        *pieces, rows_in, after_in, dx_in, y_in, da_in, gains, vec_in,
        final, vec_out, result, result_grad, y_other, da_other, from_sib, from_x, from_y, corner_a, corner_b,
        left, right, ring, corners, side_x, side_y, middle, stage, vec_box, end_wide, end_low,
        load_s, stage_s, sib_s, sib_r, x_s, x_r, y_s, y_r, ca_s, ca_r, cb_s, cb_r, f_s, f_r, v_s, v_r,
        end_s, end_r, end_load,
    ) = refs
    chip, core, z, y, x = place_of()
    rank = z % 2
    slots, width, lanes = final.shape[1:]
    half = width // 2
    part = half // 2
    at_x = toggled(z, y, x, 0, 1, 0)
    at_y = toggled(z, y, x, 1, 0, 0)
    sibling = (chip, 1 - core)
    mates = (
        sibling,
        (at_x, core),
        (at_y, core),
        (toggled(z, y, x, 0, 0, 1), core),
        (toggled(z, y, x, 0, 0, 2), core),
    )

    kinds = left.shape[0]
    depth = right.shape[1]
    loads = []
    for i in range(kinds):
        columns = pieces[i].shape[1]
        loads.append(
            pltpu.make_async_copy(pieces[i], left.at[i, :, pl.ds(0, columns)], load_s.at[i])
        )
    first = 0
    blank = []
    for i, piece in enumerate(pieces[kinds:]):
        number, rows = piece.shape[:2]
        loads.append(
            pltpu.make_async_copy(
                piece, right.at[pl.ds(first, number), pl.ds(0, rows), :], load_s.at[kinds + i]
            )
        )
        if rows < depth:
            blank.append((first, number, rows))
        first += number
    for load in loads:
        load.start()
    for start, number, rows in blank:

        def clear(i, carry):
            right[start + i, pl.ds(rows, depth - rows), :] = jnp.zeros(
                (depth - rows, lanes), right.dtype
            )
            return carry

        lax.fori_loop(0, number, clear, 0)
    right[first] = jnp.zeros((depth, lanes), right.dtype)
    for i in range(kinds):
        columns = pieces[i].shape[1]
        if columns < depth:
            left[i, :, pl.ds(columns, depth - columns)] = jnp.zeros(
                (width, depth - columns), left.dtype
            )
    vec_out[...] = vec_in[...]
    greet(chip, core, z, y, x)
    for load in loads:
        load.wait()

    def remote(src, dst, send, recv, device):
        return pltpu.make_async_remote_copy(
            src_ref=src, dst_ref=dst, send_sem=send, recv_sem=recv,
            device_id=device, device_id_type=MESH,
        )

    batch = ring.shape[1]
    batches = slots // batch
    turns = 4 * batches
    deep = corners.shape[0]

    def flips(s):
        return 3 - s // batches

    def sums(q, s, first, terms, total):
        unit = toggled(z, y, x, 1 - q % 2, 1 - q // 2, flips(s))
        base = unit * slots + (s % batches) * batch
        count = total.shape[1]

        def one(i, carry):
            slot = base + i
            rows = pl.ds(pl.multiple_of(first, 128), count)
            acc = jnp.dot(
                left[kind[slot], rows, :], right[block[slot]], preferred_element_type=jnp.float32
            )
            for term in terms:
                acc = acc + term[i].astype(jnp.float32)
            total[i] = acc.astype(total.dtype)
            return carry

        lax.fori_loop(0, batch, one, 0)

    mine, other = core * half, (1 - core) * half

    def sub(ref, first):
        return ref.at[:, pl.ds(first, part), :]

    def sib_copy(q, s):
        i = turns * q + s
        return remote(ring.at[q], from_sib.at[i], sib_s.at[i], sib_r.at[i], sibling)

    def a_copy(s):
        return remote(
            sub(corners.at[s % deep], 0), corner_a.at[s], ca_s.at[s], ca_r.at[s], (at_x, core)
        )

    def b_copy(s):
        return remote(
            sub(corners.at[s % deep], part), corner_b.at[s], cb_s.at[s], cb_r.at[s], (at_y, core)
        )

    def x_copy(s, n):
        rows = pl.ds(n * part, part)
        i = turns * n + s
        return remote(
            side_x.at[s % deep, :, rows, :], from_x.at[s, :, rows, :], x_s.at[i], x_r.at[i],
            (at_x, core),
        )

    def y_copy(s, n):
        rows = pl.ds((1 - n) * part, part)
        i = turns * n + s
        return remote(
            side_y.at[s % deep, :, rows, :], from_y.at[s, :, rows, :], y_s.at[i], y_r.at[i],
            (at_y, core),
        )

    def f_copy(s):
        src = middle.at[s % deep]
        g = s % batches
        dst = final.at[
            z // 2, pl.ds(g * batch, batch), pl.ds(pl.multiple_of(mine, 128), half), :
        ]
        recv = f_r.at[(2 * (z // 2) + core) * batches + g]
        target = (toggled(z, y, x, 0, 0, flips(s)), rank)
        return remote(src, dst, f_s.at[s], recv, target), pltpu.make_async_copy(src, dst, recv)

    def stays(s):
        return jnp.logical_and(s >= turns - batches, rank == core)

    def for_sibling(s, low, high):
        def one(q, carry):
            @pl.when(s >= 1)
            def _():
                sib_copy(q, s - 1).wait_send()

            sums(q, s, other, (), ring.at[q])
            sib_copy(q, s).start()
            return carry

        lax.fori_loop(low, high, one, 0)

    def fetched(q, s):
        i = 2 * q + s % 2
        return pltpu.make_async_copy(from_sib.at[turns * q + s], stage.at[i], stage_s.at[i])

    def fetch(q, s):
        sib_copy(q, s).wait_recv()
        fetched(q, s).start()

    def taken(q, s):
        return stage.at[2 * q + s % 2]

    def corner(s):
        @pl.when(s >= deep)
        def _():
            a_copy(s - deep).wait_send()
            b_copy(s - deep).wait_send()

        fetched(0, s).wait()
        sums(0, s, mine, (taken(0, s),), corners.at[s % deep])
        a_copy(s).start()
        b_copy(s).start()

    def direct_sides(s):
        @pl.when(s >= deep)
        def _():
            for n in range(2):
                x_copy(s - deep, n).wait_send()
                y_copy(s - deep, n).wait_send()

        fetched(1, s).wait()
        sums(1, s, mine, (sub(taken(1, s), 0),), sub(side_x.at[s % deep], 0))
        x_copy(s, 0).start()
        fetched(2, s).wait()
        sums(2, s, mine + part, (sub(taken(2, s), part),), sub(side_y.at[s % deep], part))
        y_copy(s, 0).start()

    def relayed(s):
        return (
            pltpu.make_async_copy(corner_b.at[s], sub(stage.at[8], 0), stage_s.at[8]),
            pltpu.make_async_copy(corner_a.at[s], sub(stage.at[8], part), stage_s.at[9]),
        )

    def relayed_in(s):
        b_copy(s).wait_recv()
        relayed(s)[0].start()
        a_copy(s).wait_recv()
        relayed(s)[1].start()

    def relayed_sides(s):
        relayed(s)[0].wait()
        sums(
            1, s, mine + part, (sub(taken(1, s), part), sub(stage.at[8], 0)),
            sub(side_x.at[s % deep], part),
        )
        x_copy(s, 1).start()
        relayed(s)[1].wait()
        sums(
            2, s, mine, (sub(taken(2, s), 0), sub(stage.at[8], part)), sub(side_y.at[s % deep], 0)
        )
        y_copy(s, 1).start()

    def centre_terms(s):
        return (
            pltpu.make_async_copy(from_x.at[s], stage.at[9], stage_s.at[10]),
            pltpu.make_async_copy(from_y.at[s], stage.at[10], stage_s.at[11]),
        )

    def centre_in(s):
        for n, copies in enumerate((x_copy, y_copy)):
            copies(s, 0).wait_recv()
            copies(s, 1).wait_recv()
            centre_terms(s)[n].start()

    def centre(s):
        @pl.when(s >= deep)
        def _():
            f_copy(s - deep)[0].wait_send()

        fetched(3, s).wait()
        for term in centre_terms(s):
            term.wait()
        sums(3, s, mine, (taken(3, s), stage.at[9], stage.at[10]), middle.at[s % deep])
        go, here = f_copy(s)

        @pl.when(stays(s))
        def _():
            here.start()

        @pl.when(jnp.logical_not(stays(s)))
        def _():
            go.start()

    home = rank == core
    pair_device = (toggled(z, y, x, 0, 0, 1), core)
    ends = [
        remote(y_in, y_other, end_s.at[0], end_r.at[0], pair_device),
        remote(da_in, da_other, end_s.at[1], end_r.at[1], pair_device),
        remote(end_low.at[0], result, end_s.at[2], end_r.at[2], sibling),
        remote(end_wide.at[0], result_grad, end_s.at[3], end_r.at[3], sibling),
    ]
    end_loads = [
        pltpu.make_async_copy(src, dst, end_load.at[i])
        for i, (src, dst) in enumerate(
            (
                (rows_in, end_wide.at[0]), (after_in, end_wide.at[1]), (dx_in, end_wide.at[2]),
                (y_in, end_low.at[0]), (da_in, end_low.at[1]),
                (y_other, end_low.at[2]), (da_other, end_low.at[3]),
            )
        )
    ]
    end_stores = [
        pltpu.make_async_copy(end_low.at[0], result, end_load.at[7]),
        pltpu.make_async_copy(end_wide.at[0], result_grad, end_load.at[8]),
    ]

    def finish_rows():
        for n in range(2):
            ends[n].wait_recv()
            end_loads[5 + n].start()
        for load in end_loads:
            load.wait()
        tall = 16

        def one(i, carry):
            at = pl.ds(pl.multiple_of(i * tall, tall), tall)
            y_all = end_low[0, at].astype(F32) + end_low[2, at].astype(F32) + gains[2:3]
            end_low[0, at] = (end_wide[1, at] + gains[0:1] * y_all).astype(end_low.dtype)
            da = end_low[1, at].astype(F32) + end_low[3, at].astype(F32)
            back, _ = normed_back(end_wide[0, at], da * (1.0 + gains[1:2]))
            end_wide[0, at] = end_wide[2, at] + back
            return carry

        lax.fori_loop(0, rows_in.shape[0] // tall, one, 0)
        ends[2].start()
        ends[3].start()
        for store in end_stores:
            store.start()

    @pl.when(home)
    def _():
        for load in end_loads[:5]:
            load.start()

    @pl.when(jnp.logical_not(home))
    def _():
        ends[0].start()
        ends[1].start()

    def vec_copy(i):
        return remote(vec_out, vec_box.at[i], v_s.at[i], v_r.at[i], mates[i])

    def turn(step, carry):
        for i in range(5):

            @pl.when(step == i)
            def _():
                vec_copy(i).start()

        @pl.when(step + 1 < turns)
        def _():
            for_sibling(step + 1, 0, 4)

        @pl.when(step < turns)
        def _():
            relayed_in(step)

        @pl.when(step >= 1)
        def _():
            centre_in(step - 1)

        @pl.when(step + 1 < turns)
        def _():
            for q in range(3):
                fetch(q, step + 1)

        @pl.when(step < turns)
        def _():
            relayed_sides(step)

        @pl.when(step >= 1)
        def _():
            centre(step - 1)

        @pl.when(step + 1 < turns)
        def _():
            fetch(3, step + 1)
            corner(step + 1)
            direct_sides(step + 1)

        @pl.when(jnp.logical_and(step == 3, home))
        def _():
            finish_rows()

        for i in range(5):

            @pl.when(step == i)
            def _():
                vec_copy(i).wait()
                vec_out[...] = vec_out[...] + vec_box[i]

        return carry

    for_sibling(0, 0, 2)
    fetch(0, 0)
    corner(0)
    for_sibling(0, 2, 4)
    for q in range(1, 4):
        fetch(q, 0)
    direct_sides(0)
    lax.fori_loop(0, turns + 1, turn, 0)
    for q in range(4):
        sib_copy(q, turns - 1).wait_send()

    def settle(i, carry):
        s = turns - deep + i
        a_copy(s).wait_send()
        b_copy(s).wait_send()
        for n in range(2):
            x_copy(s, n).wait_send()
            y_copy(s, n).wait_send()

        @pl.when(jnp.logical_not(stays(s)))
        def _():
            f_copy(s)[0].wait_send()

        return carry

    lax.fori_loop(0, deep, settle, 0)

    @pl.when(home)
    def _():
        ends[2].wait_send()
        ends[3].wait_send()
        for store in end_stores:
            store.wait()

    @pl.when(jnp.logical_not(home))
    def _():
        ends[0].wait_send()
        ends[1].wait_send()
        ends[2].wait_recv()
        ends[3].wait_recv()

    for plane in range(2):
        for h in range(2):
            for g in range(batches):
                piece = final.at[plane, pl.ds(g * batch, batch), pl.ds(h * half, half), :]
                recv = f_r.at[(2 * plane + h) * batches + g]
                pltpu.make_async_copy(piece, piece, recv).wait()


def reduce_slots(holder, kinds, rows, columns, vector, ends, gains, slot_count):
    if not chip_pairs():
        grads = slot_grads(holder, kinds, [r.T for r in rows], columns)
        total = lax.psum_scatter(grads, "dp", scatter_dimension=0, tiled=True)
        x, after, dx, y_part, da_part = ends
        y_all, da_all = (
            v.astype(F32) + pair_swap(v).astype(F32) for v in (y_part, da_part)
        )
        result = (after + gains[0] * (y_all + gains[2])).astype(BF16)
        back, _ = normed_back(x, da_all * (1.0 + gains[1]))
        return total[None], lax.psum(vector, ("dp", "tensor")), result, dx + back
    left = rows
    width, depth = left[0].shape[0], max(r.shape[1] for r in rows)
    lanes = columns[0].shape[2]
    tiles = sum(c.shape[0] for c in columns)
    block = jnp.where(holder >= 0, holder, tiles)
    kind = kinds[jnp.maximum(holder, 0)]
    half = width // 2
    dma = pltpu.SemaphoreType.DMA
    scalars = pl.BlockSpec(memory_space=pltpu.SMEM)
    inside = pl.BlockSpec(memory_space=pltpu.VMEM)
    low = jnp.bfloat16

    batch = max(n for n in (1, 2, 3) if slot_count % n == 0)
    turns = 4 * slot_count // batch
    deep = 3

    def room(count, tall):
        return jax.ShapeDtypeStruct((count, batch, tall, lanes), low)

    def slab(count):
        return pltpu.VMEM((count, batch, half, lanes), low)

    outs = pl.pallas_call(
        reduce_kernel,
        out_shape=[
            jax.ShapeDtypeStruct((2, slot_count, width, lanes), low),
            jax.ShapeDtypeStruct(vector.shape, vector.dtype),
            jax.ShapeDtypeStruct(ends[0].shape, low), jax.ShapeDtypeStruct(ends[0].shape, F32),
            jax.ShapeDtypeStruct(ends[0].shape, low), jax.ShapeDtypeStruct(ends[0].shape, low),
            room(4 * turns, half), room(turns, half), room(turns, half),
            room(turns, half // 2), room(turns, half // 2),
        ],
        in_specs=[scalars, scalars] + [ANY] * (len(left) + len(columns) + 5) + [inside] * 2,
        out_specs=[ANY, inside] + [ANY] * 9,
        scratch_shapes=[
            pltpu.VMEM((len(left), width, depth), low),
            pltpu.VMEM((tiles + 1, depth, lanes), low),
            slab(4), slab(deep), slab(deep), slab(deep), slab(deep), slab(11),
            pltpu.VMEM((5,) + vector.shape, vector.dtype),
            pltpu.VMEM((3,) + ends[0].shape, F32),
            pltpu.VMEM((4,) + ends[0].shape, low),
        ]
        + [
            dma((n,))
            for n in (len(left) + len(columns), 12)
            + (4 * turns,) * 2
            + (2 * turns,) * 4
            + (turns,) * 6
            + (5, 5, 4, 4, 9)
        ],
        compiler_params=pltpu.CompilerParams(
            collective_id=1, has_side_effects=True, vmem_limit_bytes=58 * MIB
        ),
    )(kind, block, *left, *columns, *ends, gains, vector)
    return outs[:4]


def kind_of_blocks(tile_count, heads_here, blocks_here):
    number = jnp.arange(tile_count)
    kind = number // heads_here
    table = jnp.array([0, 0, 0, 1, 2, 3, 3, 4], jnp.int32)
    late = jnp.where(number < 8 * heads_here + blocks_here, 5, 6)
    return jnp.where(number < 8 * heads_here, table[jnp.minimum(kind, 7)], late).astype(jnp.int32)


def slot_grads(holder, kinds, rows, columns):
    depth = max(r.shape[0] for r in rows)

    def deep(value, axis):
        room = [(0, 0)] * value.ndim
        room[axis] = (0, depth - value.shape[axis])
        return jnp.pad(value, room)

    left = jnp.stack([deep(r, 0) for r in rows])
    right = jnp.concatenate([deep(c, 1) for c in columns], 0)
    slots = holder.shape[0]
    used = (holder >= 0).astype(jnp.int32)
    block = jnp.maximum(holder, 0)
    kind = kinds[block]
    width = rows[0].shape[1]
    lanes = right.shape[2]

    def multiply(kind_ref, block_ref, used_ref, left_ref, right_ref, out_ref):
        slot = pl.program_id(0)

        @pl.when(used_ref[slot] == 1)
        def _():
            out_ref[0] = lax.dot_general(
                left_ref[kind_ref[slot]],
                right_ref[0],
                (((0,), (0,)), ((), ())),
                preferred_element_type=jnp.float32,
            ).astype(out_ref.dtype)

        @pl.when(used_ref[slot] == 0)
        def _():
            out_ref[...] = jnp.zeros_like(out_ref)

    return pl.pallas_call(
        multiply,
        grid_spec=pltpu.PrefetchScalarGridSpec(
            num_scalar_prefetch=3,
            grid=(slots,),
            in_specs=[
                pl.BlockSpec(left.shape, lambda s, kd, b, u: (0, 0, 0)),
                pl.BlockSpec((1, depth, lanes), lambda s, kd, b, u: (b[s], 0, 0)),
            ],
            out_specs=pl.BlockSpec((1, width, lanes), lambda s, kd, b, u: (s, 0, 0)),
        ),
        out_shape=jax.ShapeDtypeStruct((slots, width, lanes), jnp.bfloat16),
        compiler_params=pltpu.CompilerParams(vmem_limit_bytes=48 * MIB),
    )(kind, block, used, left, right)


def adam_slots(planes, master, moment_one, moment_two, slot_scale, filled):
    count, slot_count, width, lanes = planes.shape

    def step(scale_ref, fill_ref, grads, weight, one, two, new_weight, new_one, new_two, grad_box, boxes, reads, writes):
        sources = (weight, one, two)
        targets = (new_weight, new_one, new_two)

        def load(slot):
            return [
                pltpu.make_async_copy(src.at[0, slot], boxes.at[n, slot], reads.at[n, slot])
                for n, src in enumerate(sources)
            ] + [
                pltpu.make_async_copy(
                    grads.at[n, slot], grad_box.at[n, slot], reads.at[3 + n, slot]
                )
                for n in range(count)
            ]

        def store(slot):
            return [
                pltpu.make_async_copy(boxes.at[n, slot], dst.at[0, slot], writes.at[n, slot])
                for n, dst in enumerate(targets)
            ]

        def begin(slot, carry):
            for copy in load(slot):
                copy.start()
            return carry

        def work(slot, carry):
            for copy in load(slot):
                copy.wait()

            @pl.when(fill_ref[slot] == 1)
            def _():
                total = grad_box[0, slot].astype(jnp.float32)
                for n in range(1, count):
                    total = total + grad_box[n, slot].astype(jnp.float32)
                results = adam_step(
                    boxes[0, slot], total * scale_ref[slot], boxes[1, slot], boxes[2, slot],
                    TILE_RATE, TILE_DECAY,
                )
                for n, value in enumerate(results):
                    boxes[n, slot] = value

            for copy in store(slot):
                copy.start()
            return carry

        def finish(slot, carry):
            for copy in store(slot):
                copy.wait()
            return carry

        for part in (begin, work, finish):
            lax.fori_loop(0, slot_count, part, 0)

    scalars = pl.BlockSpec(memory_space=pltpu.SMEM)
    return pl.pallas_call(
        step,
        in_specs=[scalars, scalars] + [ANY] * 4,
        out_specs=[ANY] * 3,
        out_shape=[pltpu.HBM(master.shape, jnp.float32)] * 3,
        scratch_shapes=[
            pltpu.VMEM((count, slot_count, width, lanes), planes.dtype),
            pltpu.VMEM((3, slot_count, width, lanes), jnp.float32),
            pltpu.SemaphoreType.DMA((3 + count, slot_count)),
            pltpu.SemaphoreType.DMA((3, slot_count)),
        ],
        compiler_params=pltpu.CompilerParams(vmem_limit_bytes=40 * MIB),
    )(
        slot_scale,
        filled.astype(jnp.int32),
        *[
            pltpu.with_memory_space_constraint(v, pltpu.HBM)
            for v in (planes, master, moment_one, moment_two)
        ],
    )


SCALING = HEAD ** (-0.5)
BF16 = jnp.bfloat16
F32 = jnp.float32


def nn(left, right):
    return jnp.dot(left, right, preferred_element_type=F32)


def nt(left, right):
    return lax.dot_general(left, right, (((1,), (1,)), ((), ())), preferred_element_type=F32)


def tn(left, right):
    return lax.dot_general(left, right, (((0,), (0,)), ((), ())), preferred_element_type=F32)


def normed(rows):
    centre = rows - jnp.mean(rows, -1, keepdims=True)
    inverse = lax.rsqrt(jnp.mean(centre * centre, -1, keepdims=True) + NORM_EPS)
    return centre * inverse, inverse


def normed_back(rows, grad):
    unit, inverse = normed(rows)
    mean = jnp.mean(grad, -1, keepdims=True)
    return (grad - mean - unit * jnp.mean(grad * unit, -1, keepdims=True)) * inverse, unit


def total_of(rows):
    return jnp.sum(rows, 0, keepdims=True)


def turned(rows, cos_tab, sin_tab):
    even = lax.broadcasted_iota(jnp.int32, rows.shape, 1) % 2 == 0
    partner = jnp.where(even, pltpu.roll(rows, HEAD - 1, 1), pltpu.roll(rows, 1, 1))
    return rows * cos_tab + partner * sin_tab


def wide(column):
    return jnp.broadcast_to(column, (column.shape[0], HEAD))


def pack_sums(for_rows, for_text=None):
    out = wide(for_rows)
    if for_text is None:
        return out
    lane = lax.broadcasted_iota(jnp.int32, out.shape, 1)
    count = for_text.shape[0] // 2
    rest = jnp.zeros((out.shape[0] - count, HEAD), F32)
    first = jnp.concatenate([wide(for_text[:count]), rest], 0)
    second = jnp.concatenate([wide(for_text[count:]), rest], 0)
    return jnp.where(lane < 32, out, jnp.where(lane < 64, first, second))


def unpack_text(sums, count):
    return jnp.concatenate([sums[: count // 2, 32:33], sums[: count // 2, 64:65]], 0)


def softmax(scores):
    expo = jnp.exp(scores - jnp.max(scores, -1, keepdims=True))
    return expo / jnp.sum(expo, -1, keepdims=True)


def self_scores(query_low, key_low, tokens):
    scores = nt(query_low, key_low) * SCALING
    lane = lax.broadcasted_iota(jnp.int32, scores.shape, 1)
    return jnp.where(lane < tokens, scores, -1e30)


def whole(array):
    zeros = (0,) * len(array.shape)
    return pl.BlockSpec(array.shape, lambda *_: zeros)


def block_at(first, stride=1):
    return pl.BlockSpec((1, D, HEAD), lambda i, where: (where[first + stride * i], 0, 0))


def call(body, places, grid, ins, outs, scratch=(), vmem=24):
    specs = [spec if spec is not None else whole(array) for array, spec in ins]
    shapes = [pltpu.HBM(shape, kind) for shape, kind, _ in outs]
    out_specs = [
        spec if spec is not None else whole(shape) for (_, _, spec), shape in zip(outs, shapes)
    ]
    return pl.pallas_call(
        body,
        grid_spec=pltpu.PrefetchScalarGridSpec(
            num_scalar_prefetch=1,
            grid=(grid,),
            in_specs=specs,
            out_specs=out_specs,
            scratch_shapes=list(scratch),
        ),
        out_shape=shapes,
        compiler_params=pltpu.CompilerParams(vmem_limit_bytes=vmem * MIB),
    )(places, *[pltpu.with_memory_space_constraint(array, pltpu.HBM) for array, _ in ins])


def head_lanes(rows, per=1):
    return pl.BlockSpec((rows, per * HEAD), lambda h, *_: (0, h))


def heads_per_step(heads, most):
    return max(n for n in (1, 2, 3, 6) if heads % n == 0 and n <= most)


def lane_group(ref, j):
    return ref[:, j * HEAD : (j + 1) * HEAD]


def joined(refs):
    return jnp.concatenate([ref[0] for ref in refs], 1)


def project_self(places, everyone, rows, mod, vecs, heads):
    count = rows.shape[0]
    span = heads * HEAD

    def body(_, rows_ref, mod_ref, vec_ref, *refs):
        weights, (low, pre, value, sums, acc) = refs[:heads], refs[heads:]
        i = pl.program_id(0)

        @pl.when(i == 0)
        def _():
            unit, _ = normed(rows_ref[...])
            low[...] = (unit * (1.0 + mod_ref[1:2]) + mod_ref[0:1]).astype(BF16)

        made = nn(low[...], joined(weights))

        @pl.when(i == 0)
        def _():
            q = made + vec_ref[0:1]
            pre[0] = q
            acc[...] = wide(jnp.sum(q * q, -1, keepdims=True))

        @pl.when(i == 1)
        def _():
            k = made + vec_ref[1:2]
            pre[0] = k
            lane = lax.broadcasted_iota(jnp.int32, acc.shape, 1)
            sums[...] = jnp.where(lane < 64, acc[...], wide(jnp.sum(k * k, -1, keepdims=True)))

        @pl.when(i == 2)
        def _():
            value[...] = (made + vec_ref[2:3]).astype(BF16)

    return call(
        body, places, 3,
        [(rows, None), (mod, None), (vecs, None)]
        + [(everyone, block_at(h, heads)) for h in range(heads)],
        [
            ((count, D), BF16, None),
            ((2, count, span), F32, pl.BlockSpec((1, count, span), lambda i, _: (jnp.minimum(i, 1), 0, 0))),
            ((count, span), BF16, None),
            ((count, HEAD), F32, None),
        ],
        [pltpu.VMEM((count, HEAD), F32)],
    )


def attend_self(places, everyone, pre, value, sums, other, vecs, cos_tab, sin_tab, heads, tokens):
    count = value.shape[0]
    per = heads_per_step(heads, 2)
    steps = heads // per

    def body(_, pre_ref, value_ref, sum_ref, other_ref, vec_ref, cos_ref, sin_ref, *refs):
        weights, (q_ref, k_ref, o_ref, y_ref, acc) = refs[:per], refs[per:]
        h = pl.program_id(0)
        total = sum_ref[...] + other_ref[...]
        q_inv = lax.rsqrt(total[:, 0:1] / D + NORM_EPS)
        k_inv = lax.rsqrt(total[:, 64:65] / D + NORM_EPS)
        cos, sin = cos_ref[...], sin_ref[...]
        outs = []
        for j in range(per):
            lanes = slice(j * HEAD, (j + 1) * HEAD)
            q = turned(pre_ref[0, :, lanes] * q_inv * vec_ref[3:4, lanes], cos, sin).astype(BF16)
            k = turned(pre_ref[1, :, lanes] * k_inv * vec_ref[4:5, lanes], cos, sin).astype(BF16)
            q_ref[:, lanes] = q
            k_ref[:, lanes] = k
            chance = softmax(self_scores(q, k, tokens))
            out = nn(chance.astype(BF16), value_ref[:, lanes]).astype(BF16)
            o_ref[j] = out
            outs.append(out)
        part = nt(jnp.concatenate(outs, 1), joined(weights))

        @pl.when(h == 0)
        def _():
            acc[...] = part

        @pl.when(h > 0)
        def _():
            acc[...] = acc[...] + part

        @pl.when(h == steps - 1)
        def _():
            y_ref[...] = acc[...].astype(BF16)

    lanes = head_lanes(count, per)
    return call(
        body, places, steps,
        [
            (pre, pl.BlockSpec((2, count, per * HEAD), lambda h, _: (0, 0, h))),
            (value, lanes), (sums, None), (other, None),
            (vecs, head_lanes(vecs.shape[0], per)), (cos_tab, None), (sin_tab, None),
        ]
        + [(everyone, block_at(3 * heads + j, per)) for j in range(per)],
        [
            (value.shape, BF16, lanes),
            (value.shape, BF16, lanes),
            ((heads, count, HEAD), BF16, pl.BlockSpec((per, count, HEAD), lambda h, _: (h, 0, 0))),
            ((count, D), BF16, None),
        ],
        [pltpu.VMEM((count, D), F32)],
    )


def project_text(places, everyone, context, vecs, heads):
    count = context.shape[0]
    span = heads * HEAD

    def body(_, text_ref, vec_ref, *refs):
        weights, (key, value, sums) = refs[:heads], refs[heads:]
        i = pl.program_id(0)
        made = nn(text_ref[...], joined(weights))

        @pl.when(i == 0)
        def _():
            k = made + vec_ref[6:7]
            key[...] = k
            sums[...] = wide(jnp.sum(k * k, -1, keepdims=True))

        @pl.when(i == 1)
        def _():
            value[...] = (made + vec_ref[7:8]).astype(BF16)

    return call(
        body, places, 2,
        [(context, None), (vecs, None)]
        + [(everyone, block_at(5 * heads + h, heads)) for h in range(heads)],
        [((count, span), F32, None), ((count, span), BF16, None), ((count, HEAD), F32, None)],
    )


def project_cross(places, everyone, rows, part, other, mod, shared, vecs, text_sums, heads):
    count = rows.shape[0]
    span = heads * HEAD
    text = text_sums.shape[0]

    def body(_, rows_ref, part_ref, other_ref, mod_ref, shared_ref, vec_ref, text_ref, *refs):
        weights, (branch, after, low, pre, sums) = refs[:heads], refs[heads:]
        y = part_ref[...].astype(F32) + other_ref[...].astype(F32) + shared_ref[0:1]
        branch[...] = y
        x = rows_ref[...] + mod_ref[2:3] * y
        after[...] = x
        unit, _ = normed(x)
        a = (unit * shared_ref[3:4] + shared_ref[4:5]).astype(BF16)
        low[...] = a
        q = nn(a, joined(weights)) + vec_ref[5:6]
        pre[...] = q
        sums[...] = pack_sums(jnp.sum(q * q, -1, keepdims=True), text_ref[:, 0:1])

    return call(
        body, places, 1,
        [(v, None) for v in (rows, part, other, mod, shared, vecs, text_sums)]
        + [(everyone, block_at(4 * heads + h)) for h in range(heads)],
        [
            ((count, D), F32, None),
            ((count, D), F32, None),
            ((count, D), BF16, None),
            ((count, span), F32, None),
            ((count, HEAD), F32, None),
        ],
    )


def attend_cross(places, everyone, pre, key_pre, value, sums, other, vecs, heads):
    count, text = pre.shape[0], value.shape[0]
    per = heads_per_step(heads, 6)
    steps = heads // per

    def body(_, pre_ref, key_ref, value_ref, sum_ref, other_ref, vec_ref, *refs):
        weights, (q_ref, k_ref, o_ref, y_ref, acc) = refs[:per], refs[per:]
        h = pl.program_id(0)
        total = sum_ref[...] + other_ref[...]
        q_inv = lax.rsqrt(total[:, 0:1] / D + NORM_EPS)
        k_inv = lax.rsqrt(unpack_text(total, text) / D + NORM_EPS)
        outs = []
        for j in range(per):
            lanes = slice(j * HEAD, (j + 1) * HEAD)
            q = (pre_ref[:, lanes] * q_inv * vec_ref[8:9, lanes]).astype(BF16)
            k = (key_ref[:, lanes] * k_inv * vec_ref[9:10, lanes]).astype(BF16)
            q_ref[:, lanes] = q
            k_ref[:, lanes] = k
            chance = softmax(nt(q, k) * SCALING)
            out = nn(chance.astype(BF16), value_ref[:, lanes]).astype(BF16)
            o_ref[j] = out
            outs.append(out)
        part = nt(jnp.concatenate(outs, 1), joined(weights))

        @pl.when(h == 0)
        def _():
            acc[...] = part

        @pl.when(h > 0)
        def _():
            acc[...] = acc[...] + part

        @pl.when(h == steps - 1)
        def _():
            y_ref[...] = acc[...].astype(BF16)

    return call(
        body, places, steps,
        [
            (pre, head_lanes(count, per)), (key_pre, head_lanes(text, per)),
            (value, head_lanes(text, per)), (sums, None), (other, None),
            (vecs, head_lanes(vecs.shape[0], per)),
        ]
        + [(everyone, block_at(7 * heads + j, per)) for j in range(per)],
        [
            (pre.shape, BF16, head_lanes(count, per)),
            (value.shape, BF16, head_lanes(text, per)),
            ((heads, count, HEAD), BF16, pl.BlockSpec((per, count, HEAD), lambda h, _: (h, 0, 0))),
            ((count, D), BF16, None),
        ],
        [pltpu.VMEM((count, D), F32)],
        vmem=40,
    )


def hidden_group(blocks):
    return max(g for g in (7, 5, 4, 3, 2, 1) if blocks % g == 0)


def block_lanes(where, everyone, held, sems, first, group, steps):
    i = pl.program_id(0)

    def fetch(step, act):
        slot = step % 2
        for j in range(group):
            copy = pltpu.make_async_copy(
                everyone.at[where[first + step * group + j]],
                held.at[slot, :, pl.ds(j * HEAD, HEAD)],
                sems.at[slot, j],
            )
            copy.start() if act else copy.wait()

    @pl.when(i == 0)
    def _():
        fetch(0, True)

    @pl.when(i + 1 < steps)
    def _():
        fetch(i + 1, True)

    fetch(i, False)
    return held[i % 2]


def lanes_scratch(group):
    return [pltpu.VMEM((2, D, group * HEAD), BF16), pltpu.SemaphoreType.DMA((2, group))]


def hidden_back(places, everyone, mod, cot, heads, blocks):
    count = cot.shape[0]
    group = hidden_group(blocks)
    steps = blocks // group

    def body(where, weights, mod_ref, cot_ref, grad, out, held, sems):
        @pl.when(pl.program_id(0) == 0)
        def _():
            grad[...] = (mod_ref[5:6] * cot_ref[...]).astype(BF16)

        down = block_lanes(where, weights, held, sems, 8 * heads + blocks, group, steps)
        out[...] = nn(grad[...], down).astype(BF16)

    return call(
        body, places, steps,
        [(everyone, ANY), (mod, None), (cot, None)],
        [
            ((count, D), BF16, None),
            ((count, blocks * HEAD), BF16, pl.BlockSpec((count, group * HEAD), lambda i, _: (0, i))),
        ],
        lanes_scratch(group),
        vmem=40,
    )


def hidden_both(places, everyone, after_one, part, other, mod, shared, d_act, up_bias, heads, blocks):
    count = after_one.shape[0]
    group = hidden_group(blocks)
    steps = blocks // group
    span = group * HEAD

    def body(where, weights, after_ref, part_ref, other_ref, mod_ref, shared_ref, d_ref, bias_ref, after, low, hidden, d_hidden, d_bias, da_ref, acc, held, sems):
        i = pl.program_id(0)

        @pl.when(i == 0)
        def _():
            x = after_ref[...] + part_ref[...].astype(F32) + other_ref[...].astype(F32)
            x = x + shared_ref[1:2]
            after[...] = x
            unit, _ = normed(x)
            low[...] = (unit * (1.0 + mod_ref[4:5]) + mod_ref[3:4]).astype(BF16)
            acc[...] = jnp.zeros_like(acc)

        up = block_lanes(where, weights, held, sems, 8 * heads, group, steps)
        pre = nn(low[...], up) + bias_ref[...]
        square = pre * pre
        bent = jnp.tanh(GELU_COEF * (pre + 0.044715 * pre * square))
        act = (0.5 * pre * (1.0 + bent)).astype(BF16)
        slope = 0.5 * (1.0 + bent) + 0.5 * pre * (1.0 - bent * bent) * (
            GELU_COEF * (1.0 + 3.0 * 0.044715 * square)
        )
        dh = (d_ref[...].astype(F32) * slope).astype(BF16)
        d_bias[...] = total_of(dh.astype(F32))
        for j in range(group):
            hidden[j] = act[:, j * HEAD : (j + 1) * HEAD]
            d_hidden[j] = dh[:, j * HEAD : (j + 1) * HEAD]
        acc[...] = acc[...] + nt(dh, up)

        @pl.when(i == steps - 1)
        def _():
            da_ref[...] = acc[...].astype(BF16)

    tall = pl.BlockSpec((group, count, HEAD), lambda i, _: (i, 0, 0))
    flat = pl.BlockSpec((1, span), lambda i, _: (0, i))
    return call(
        body, places, steps,
        [(everyone, ANY)]
        + [(v, None) for v in (after_one, part, other, mod, shared)]
        + [(d_act, pl.BlockSpec((count, span), lambda i, _: (0, i))), (up_bias, flat)],
        [
            ((count, D), F32, None),
            ((count, D), BF16, None),
            ((blocks, count, HEAD), BF16, tall),
            ((blocks, count, HEAD), BF16, tall),
            (up_bias.shape, F32, flat),
            ((count, D), BF16, None),
        ],
        [pltpu.VMEM((count, D), F32)] + lanes_scratch(group),
        vmem=40,
    )


def hidden_out(places, everyone, hidden, heads):
    blocks, count = hidden.shape[:2]
    group = hidden_group(blocks)
    steps = blocks // group

    def body(where, weights, hidden_ref, y_ref, acc, held, sems):
        i = pl.program_id(0)
        down = block_lanes(where, weights, held, sems, 8 * heads + blocks, group, steps)
        part = nt(jnp.concatenate([hidden_ref[j] for j in range(group)], 1), down)

        @pl.when(i == 0)
        def _():
            acc[...] = part

        @pl.when(i > 0)
        def _():
            acc[...] = acc[...] + part

        @pl.when(i == steps - 1)
        def _():
            y_ref[...] = acc[...].astype(BF16)

    return call(
        body, places, steps,
        [(everyone, ANY), (hidden, pl.BlockSpec((group, count, HEAD), lambda i, _: (i, 0, 0)))],
        [((count, D), BF16, None)],
        [pltpu.VMEM((count, D), F32)] + lanes_scratch(group),
        vmem=40,
    )[0]


def cross_back(places, everyone, cot, after_two, part, other, mod, query, key, value, pre, key_pre, vecs, heads):
    count, text = query.shape[0], key.shape[0]
    per = heads_per_step(heads, 6)
    steps = heads // per

    def body(_, cot_ref, after_ref, part_ref, other_ref, mod_ref, q_ref, k_ref, v_ref, pre_ref, key_ref, vec_ref, *refs):
        weights, (dx_ref, low_ref, dq_ref, dk_ref, dv_ref, sums, q_acc, k_acc) = refs[:per], refs[per:]
        h = pl.program_id(0)

        @pl.when(h == 0)
        def _():
            da = part_ref[...].astype(F32) + other_ref[...].astype(F32)
            back, _ = normed_back(after_ref[...], da * (1.0 + mod_ref[4:5]))
            dx = cot_ref[...] + back
            dx_ref[...] = dx
            low_ref[...] = dx.astype(BF16)
            q_acc[...] = jnp.zeros_like(q_acc)
            k_acc[...] = jnp.zeros_like(k_acc)

        do_all = nn(low_ref[...], joined(weights)).astype(BF16)
        q_sums, k_sums = 0.0, 0.0
        for j in range(per):
            lanes = slice(j * HEAD, (j + 1) * HEAD)
            do = do_all[:, lanes]
            q, k = q_ref[:, lanes], k_ref[:, lanes]
            chance = softmax(nt(q, k) * SCALING)
            dp = nt(do, v_ref[:, lanes])
            ds = (chance * (dp - jnp.sum(chance * dp, -1, keepdims=True))).astype(BF16)
            dv_ref[j] = tn(chance.astype(BF16), do).astype(BF16)
            dq = nn(ds, k) * SCALING
            dk = tn(ds, q) * SCALING
            dq_ref[:, lanes] = dq
            dk_ref[:, lanes] = dk
            q_sums += pre_ref[:, lanes] * vec_ref[8:9, lanes] * dq
            k_sums += key_ref[:, lanes] * vec_ref[9:10, lanes] * dk
        q_acc[...] = q_acc[...] + q_sums
        k_acc[...] = k_acc[...] + k_sums

        @pl.when(h == steps - 1)
        def _():
            sums[...] = pack_sums(
                jnp.sum(q_acc[...], -1, keepdims=True), jnp.sum(k_acc[...], -1, keepdims=True)
            )

    return call(
        body, places, steps,
        [(v, None) for v in (cot, after_two, part, other, mod)]
        + [
            (query, head_lanes(count, per)), (key, head_lanes(text, per)),
            (value, head_lanes(text, per)), (pre, head_lanes(count, per)),
            (key_pre, head_lanes(text, per)), (vecs, head_lanes(vecs.shape[0], per)),
        ]
        + [(everyone, block_at(7 * heads + j, per)) for j in range(per)],
        [
            ((count, D), F32, None),
            ((count, D), BF16, None),
            (query.shape, F32, head_lanes(count, per)),
            (key.shape, F32, head_lanes(text, per)),
            ((heads, text, HEAD), BF16, pl.BlockSpec((per, text, HEAD), lambda h, _: (h, 0, 0))),
            ((count, HEAD), F32, None),
        ],
        [pltpu.VMEM((count, HEAD), F32), pltpu.VMEM((text, HEAD), F32)],
        vmem=48,
    )


def norm_grad(pre, inverse, gain, incoming, total):
    grad = inverse * (gain * incoming) - pre * (inverse * inverse * inverse) * (total / D)
    low = grad.astype(BF16)
    return low, total_of(low.astype(F32)), total_of(incoming * pre * inverse)


def cross_back_rows(places, everyone, pre, key_pre, dq, dk, dv, squares, squares_other, sums, sums_other, vecs, heads):
    count, text = pre.shape[0], key_pre.shape[0]
    per = heads_per_step(heads, 6)
    steps = heads // per

    def body(_, pre_ref, key_ref, dq_ref, dk_ref, dv_ref, sq_ref, sqo_ref, sum_ref, sumo_ref, vec_ref, *refs):
        weights, (gq_ref, gk_ref, vec_out, da_ref, acc) = refs[:per], refs[per:]
        h = pl.program_id(0)
        squares_all = sq_ref[...] + sqo_ref[...]
        total = sum_ref[...] + sumo_ref[...]
        q_inv = lax.rsqrt(squares_all[:, 0:1] / D + NORM_EPS)
        k_inv = lax.rsqrt(unpack_text(squares_all, text) / D + NORM_EPS)
        q_total, k_total = total[:, 0:1], unpack_text(total, text)
        lows = []
        for j in range(per):
            lanes = slice(j * HEAD, (j + 1) * HEAD)
            low_q, bias_q, gain_q = norm_grad(
                pre_ref[:, lanes], q_inv, vec_ref[8:9, lanes], dq_ref[:, lanes], q_total
            )
            low_k, bias_k, gain_k = norm_grad(
                key_ref[:, lanes], k_inv, vec_ref[9:10, lanes], dk_ref[:, lanes], k_total
            )
            gq_ref[j] = low_q
            gk_ref[j] = low_k
            lows.append(low_q)
            bias_v = total_of(dv_ref[j].astype(F32))
            vec_out[:, lanes] = jnp.concatenate(
                [bias_q, bias_k, bias_v, gain_q, gain_k, jnp.zeros((3, HEAD), F32)], 0
            )
        part = nt(jnp.concatenate(lows, 1), joined(weights))

        @pl.when(h == 0)
        def _():
            acc[...] = part

        @pl.when(h > 0)
        def _():
            acc[...] = acc[...] + part

        @pl.when(h == steps - 1)
        def _():
            da_ref[...] = acc[...].astype(BF16)

    tall = pl.BlockSpec((per, count, HEAD), lambda h, _: (h, 0, 0))
    tall_text = pl.BlockSpec((per, text, HEAD), lambda h, _: (h, 0, 0))
    return call(
        body, places, steps,
        [
            (pre, head_lanes(count, per)), (key_pre, head_lanes(text, per)),
            (dq, head_lanes(count, per)), (dk, head_lanes(text, per)), (dv, tall_text),
            (squares, None), (squares_other, None), (sums, None), (sums_other, None),
            (vecs, head_lanes(vecs.shape[0], per)),
        ]
        + [(everyone, block_at(4 * heads + j, per)) for j in range(per)],
        [
            ((heads, count, HEAD), BF16, tall),
            ((heads, text, HEAD), BF16, tall_text),
            ((8, heads * HEAD), F32, head_lanes(8, per)),
            ((count, D), BF16, None),
        ],
        [pltpu.VMEM((count, D), F32)],
        vmem=40,
    )


def self_back(places, everyone, dx_two, after_one, part, other, mod, shared, branch, query, key, value, pre, vecs, cos_tab, sin_tab, heads, tokens):
    count = query.shape[0]
    per = heads_per_step(heads, 2)
    steps = heads // per

    def body(_, dx_in, after_ref, part_ref, other_ref, mod_ref, shared_ref, branch_ref, q_ref, k_ref, v_ref, pre_ref, vec_ref, cos_ref, sin_ref, *refs):
        weights, (dx_ref, low_ref, d_ref, dv_ref, sums, vec_out, q_acc, k_acc) = refs[:per], refs[per:]
        h = pl.program_id(0)

        @pl.when(h == 0)
        def _():
            da = part_ref[...].astype(F32) + other_ref[...].astype(F32)
            back, _ = normed_back(after_ref[...], da * shared_ref[3:4])
            dx = dx_in[...] + back
            dx_ref[...] = dx
            low = (mod_ref[2:3] * dx).astype(BF16)
            low_ref[...] = low
            vec_out[0:1] = 0.5 * total_of(low.astype(F32))
            vec_out[1:2] = 0.5 * total_of(dx * branch_ref[...])
            q_acc[...] = jnp.zeros_like(q_acc)
            k_acc[...] = jnp.zeros_like(k_acc)

        do_all = nn(low_ref[...], joined(weights)).astype(BF16)
        cos, sin = cos_ref[...], -sin_ref[...]
        q_sums, k_sums = 0.0, 0.0
        for j in range(per):
            lanes = slice(j * HEAD, (j + 1) * HEAD)
            do = do_all[:, lanes]
            q, k = q_ref[:, lanes], k_ref[:, lanes]
            chance = softmax(self_scores(q, k, tokens))
            dp = nt(do, v_ref[:, lanes])
            ds = (chance * (dp - jnp.sum(chance * dp, -1, keepdims=True))).astype(BF16)
            dv_ref[j] = tn(chance.astype(BF16), do).astype(BF16)
            dq = turned(nn(ds, k) * SCALING, cos, sin)
            dk = turned(tn(ds, q) * SCALING, cos, sin)
            d_ref[0, :, lanes] = dq
            d_ref[1, :, lanes] = dk
            q_sums += pre_ref[0, :, lanes] * vec_ref[3:4, lanes] * dq
            k_sums += pre_ref[1, :, lanes] * vec_ref[4:5, lanes] * dk
        q_acc[...] = q_acc[...] + q_sums
        k_acc[...] = k_acc[...] + k_sums

        @pl.when(h == steps - 1)
        def _():
            lane = lax.broadcasted_iota(jnp.int32, q_acc.shape, 1)
            sums[...] = jnp.where(
                lane < 64,
                wide(jnp.sum(q_acc[...], -1, keepdims=True)),
                wide(jnp.sum(k_acc[...], -1, keepdims=True)),
            )

    lanes = head_lanes(count, per)
    pair = pl.BlockSpec((2, count, per * HEAD), lambda h, _: (0, 0, h))
    return call(
        body, places, steps,
        [(v, None) for v in (dx_two, after_one, part, other, mod, shared, branch)]
        + [
            (query, lanes), (key, lanes), (value, lanes), (pre, pair),
            (vecs, head_lanes(vecs.shape[0], per)), (cos_tab, None), (sin_tab, None),
        ]
        + [(everyone, block_at(3 * heads + j, per)) for j in range(per)],
        [
            ((count, D), F32, None),
            ((count, D), BF16, None),
            (pre.shape, F32, pair),
            ((heads, count, HEAD), BF16, pl.BlockSpec((per, count, HEAD), lambda h, _: (h, 0, 0))),
            ((count, HEAD), F32, None),
            ((2, D), F32, None),
        ],
        [pltpu.VMEM((count, HEAD), F32), pltpu.VMEM((count, HEAD), F32)],
        vmem=32,
    )


def self_back_rows(places, everyone, rows, pre, grads, dv, squares, squares_other, sums, sums_other, vecs, heads):
    count = pre.shape[1]
    per = heads_per_step(heads, 2)
    steps = heads // per

    def body(_, rows_ref, pre_ref, d_ref, dv_ref, sq_ref, sqo_ref, sum_ref, sumo_ref, vec_ref, *refs):
        weights, (gq_ref, gk_ref, vec_out, da_ref, row_out, acc) = refs[: 3 * per], refs[3 * per :]
        h = pl.program_id(0)
        squares_all = sq_ref[...] + sqo_ref[...]
        total = sum_ref[...] + sumo_ref[...]
        inverses = [
            lax.rsqrt(squares_all[:, n : n + 1] / D + NORM_EPS) for n in (0, 64)
        ]
        lows = []
        for j in range(per):
            lanes = slice(j * HEAD, (j + 1) * HEAD)
            biases, gains = [], []
            for n, out in enumerate((gq_ref, gk_ref)):
                low, bias, gain = norm_grad(
                    pre_ref[n, :, lanes], inverses[n], vec_ref[3 + n : 4 + n, lanes],
                    d_ref[n, :, lanes], total[:, 64 * n : 64 * n + 1],
                )
                out[j] = low
                lows.append(low)
                biases.append(bias)
                gains.append(gain)
            dv_low = dv_ref[j]
            lows.append(dv_low)
            vec_out[:, lanes] = jnp.concatenate(
                biases + [total_of(dv_low.astype(F32))] + gains + [jnp.zeros((3, HEAD), F32)], 0
            )
        part = nt(jnp.concatenate(lows, 1), joined(weights))

        @pl.when(h == 0)
        def _():
            acc[...] = part

        @pl.when(h > 0)
        def _():
            acc[...] = acc[...] + part

        @pl.when(h == steps - 1)
        def _():
            da = acc[...]
            da_ref[...] = da.astype(BF16)
            row_out[0:1] = total_of(da)
            row_out[1:2] = total_of(da * normed(rows_ref[...])[0])

    tall = pl.BlockSpec((per, count, HEAD), lambda h, _: (h, 0, 0))
    pair = pl.BlockSpec((2, count, per * HEAD), lambda h, _: (0, 0, h))
    return call(
        body, places, steps,
        [
            (rows, None), (pre, pair), (grads, pair), (dv, tall), (squares, None),
            (squares_other, None), (sums, None), (sums_other, None),
            (vecs, head_lanes(vecs.shape[0], per)),
        ]
        + [(everyone, block_at(n * heads + j, per)) for j in range(per) for n in range(3)],
        [
            ((heads, count, HEAD), BF16, tall),
            ((heads, count, HEAD), BF16, tall),
            ((8, heads * HEAD), F32, head_lanes(8, per)),
            ((count, D), BF16, None),
            ((2, D), F32, None),
        ],
        [pltpu.VMEM((count, D), F32)],
        vmem=40,
    )


def shared_sums(places, after_one, after_two, grad_two, grad_three, cot, da_two, da_three, y_three, shared):
    def body(_, x1_ref, x2_ref, dy2, dy3, cot_ref, da2, da3, y3, shared_ref, out):
        out[...] = jnp.zeros_like(out)
        out[1:2] = 0.5 * total_of(dy2[...].astype(F32))
        out[2:3] = 0.5 * total_of(dy3[...].astype(F32))
        part = da3[...].astype(F32)
        out[3:4] = total_of(part * normed(x1_ref[...])[0])
        out[4:5] = total_of(part)
        part = da2[...].astype(F32)
        out[8:9] = total_of(part)
        out[9:10] = total_of(part * normed(x2_ref[...])[0])
        out[10:11] = total_of(cot_ref[...] * (y3[...].astype(F32) + 0.5 * shared_ref[2:3]))

    return call(
        body, places, 1,
        [(v, None) for v in (after_one, after_two, grad_two, grad_three, cot, da_two, da_three, y_three, shared)],
        [(shared.shape, F32, None)],
    )[0]


def body(
    latents,
    context,
    cotangent,
    positions,
    step_ids,
    owners,
    time_table,
    master,
    first_moment,
    second_moment,
    head_params,
    head_first,
    head_second,
    shared_params,
    shared_first,
    shared_second,
):
    tensors = lax.axis_size("tensor")
    devices = lax.axis_size("dp")
    slot_count = master.shape[1]
    tile_count = owners.shape[0]
    heads_here = HEADS // tensors
    blocks_here = FF // (HEAD * tensors)
    width_here = D // tensors
    places, holder = owner_layout(owners, slot_count, devices)
    scales = tile_scales(tile_count, heads_here, blocks_here)
    my_slots = lax.dynamic_slice_in_dim(holder, lax.axis_index("dp") * slot_count, slot_count)
    rank = pair_rank()
    filled = my_slots >= 0
    slot_scale = jnp.where(filled, scales[jnp.maximum(my_slots, 0)], 0.0)
    scaled = (master[0] * slot_scale[:, None, None]).astype(jnp.bfloat16)
    half = latents.shape[0]
    tokens = 2 * half
    count = -(-tokens // 16) * 16
    taller = ((0, -half % 16), (0, 0))
    small = jnp.concatenate(
        [
            head_params[0],
            positions.reshape(-1).astype(jnp.float32),
            step_ids.astype(jnp.float32),
        ]
    )
    packed = jnp.pad(small, (0, -small.shape[0] % 1024)).reshape(-1, HEAD)
    everyone, lats, cots, context, packed = gather_slots(
        scaled, jnp.pad(latents, taller), jnp.pad(cotangent, taller), context, packed
    )
    small = packed.reshape(-1)
    vectors = small[: head_params.shape[1]]
    small = small[head_params.shape[1] :]
    positions = small[: positions.size].reshape(positions.shape)
    step = small[positions.size]
    vecs = vectors[: 10 * width_here].reshape(10, width_here)
    up_bias = vectors[10 * width_here :].reshape(1, -1)
    chosen = (step == jnp.arange(TSTEPS)).astype(jnp.float32)
    mod = shared_params[5:11] + jnp.einsum(
        "s,skd->kd", chosen, time_table, precision=lax.Precision.HIGHEST
    )
    cos_tab, sin_tab = rope_tables(positions, HEAD)
    sin_tab = jnp.where(jnp.arange(HEAD) % 2 == 0, -sin_tab, sin_tab)
    cos_tab, sin_tab = (jnp.pad(t, ((0, count - tokens), (0, 0))) for t in (cos_tab, sin_tab))

    def all_rows(halves):
        rows = jnp.concatenate([halves[0, :half], halves[1, :half]], 0)
        return jnp.pad(rows, ((0, count - tokens), (0, 0))).astype(jnp.float32)

    def upright(rows):
        return jnp.pad(rows, ((0, -rows.shape[0] % HEAD), (0, 0))).T

    def beside(*values):
        return lax.optimization_barrier(values)

    rows, cot = all_rows(lats), all_rows(cots)
    low_one, pre_one, value_one, squares_one = project_self(
        places, everyone, rows, mod, vecs, heads_here
    )
    squares_one_other = pair_swap(squares_one)
    query_one, key_one, heads_one, part_one = attend_self(
        places, everyone, pre_one, value_one, squares_one, squares_one_other, vecs, cos_tab,
        sin_tab, heads_here, tokens,
    )
    part_one, context = beside(part_one, context)
    part_one_other = pair_swap(part_one)
    key_pre, value_two, text_squares = project_text(places, everyone, context, vecs, heads_here)
    left_context, left_one = upright(context), upright(low_one)
    part_one_other, key_pre, left_context, left_one = beside(
        part_one_other, key_pre, left_context, left_one
    )
    branch_one, after_one, low_two, pre_two, squares_two = project_cross(
        places, everyone, rows, part_one, part_one_other, mod, shared_params, vecs,
        text_squares, heads_here,
    )
    squares_two_other = pair_swap(squares_two)
    query_two, key_two, heads_two, part_two = attend_cross(
        places, everyone, pre_two, key_pre, value_two, squares_two, squares_two_other, vecs,
        heads_here,
    )
    part_two, cot, low_two = beside(part_two, cot, low_two)
    part_two_other = pair_swap(part_two)
    grad_three, d_act = hidden_back(places, everyone, mod, cot, heads_here, blocks_here)
    left_two, left_grad_three = upright(low_two), upright(grad_three)
    part_two_other, d_act, left_two, left_grad_three = beside(
        part_two_other, d_act, left_two, left_grad_three
    )
    after_two, low_three, hidden, d_hidden, d_up_bias, da_two = hidden_both(
        places, everyone, after_one, part_two, part_two_other, mod, shared_params, d_act, up_bias,
        heads_here, blocks_here,
    )
    da_two_other = pair_swap(da_two)
    y_three = hidden_out(places, everyone, hidden, heads_here)
    left_three = upright(low_three)
    da_two_other, y_three, left_three = beside(da_two_other, y_three, left_three)
    dx_two, grad_two, dq_two, dk_two, dv_two, sums_two = cross_back(
        places, everyone, cot, after_two, da_two, da_two_other, mod, query_two, key_two,
        value_two, pre_two, key_pre, vecs, heads_here,
    )
    query_grad_two, key_grad_two, vecs_two, da_three = cross_back_rows(
        places, everyone, pre_two, key_pre, dq_two, dk_two, dv_two, squares_two,
        squares_two_other, sums_two, pair_swap(sums_two), vecs, heads_here,
    )
    da_three_other = pair_swap(da_three)
    shared_grad = shared_sums(
        places, after_one, after_two, grad_two, grad_three, cot, da_two, da_three, y_three,
        shared_params,
    )
    left_grad_two = upright(grad_two)
    da_three_other, shared_grad, left_grad_two = beside(da_three_other, shared_grad, left_grad_two)
    dx_one, grad_one, d_one, dv_one, sums_one, rows_a = self_back(
        places, everyone, dx_two, after_one, da_three, da_three_other, mod, shared_params,
        branch_one, query_one, key_one, value_one, pre_one, vecs, cos_tab, sin_tab, heads_here,
        tokens,
    )
    query_grad_one, key_grad_one, vecs_one, da_one, rows_b = self_back_rows(
        places, everyone, rows, pre_one, d_one, dv_one, squares_one, squares_one_other, sums_one,
        pair_swap(sums_one), vecs, heads_here,
    )
    shared_grad = jnp.concatenate(
        [rows_a[0:1], shared_grad[1:5], rows_b, rows_a[1:2], shared_grad[8:]], 0
    )
    head_grad = jnp.concatenate(
        [vecs_one[:5].reshape(-1), vecs_two[:5].reshape(-1), d_up_bias.reshape(-1)]
    )
    tensor_rank = lax.axis_index("tensor")
    head_padded = jnp.where(jnp.arange(tensors)[:, None] == rank, head_grad[None, :], 0.0)
    vector = jnp.concatenate([head_padded.reshape(-1), shared_grad.reshape(-1)])
    vector = jnp.pad(vector, (0, -vector.shape[0] % 1024)).reshape(-1, 128)
    parts, vector, output, grad_input = reduce_slots(
        holder,
        kind_of_blocks(tile_count, heads_here, blocks_here),
        (left_one, upright(grad_one), left_two, left_context, left_grad_two, left_three, left_grad_three),
        (
            query_grad_one,
            key_grad_one,
            dv_one,
            heads_one,
            query_grad_two,
            key_grad_two,
            dv_two,
            heads_two,
            d_hidden,
            hidden,
        ),
        vector,
        (rows, after_two, dx_one, y_three, da_one),
        jnp.concatenate([mod[5:6], mod[1:2], shared_params[2:3], jnp.zeros((5, D), F32)], 0),
        slot_count,
    )
    output, grad_input = (
        jnp.where(lax.axis_index("tensor") == 0, v[:half], v[half:tokens])
        for v in (output, grad_input)
    )
    new_master, new_first, new_second = adam_slots(
        parts, master, first_moment, second_moment, slot_scale, filled
    )
    vector = vector.reshape(-1)
    head_total = vector[: head_padded.size].reshape(head_padded.shape)
    shared_total = vector[head_padded.size : head_padded.size + shared_grad.size]
    shared_total = shared_total.reshape(shared_grad.shape)
    mine_head = lax.dynamic_slice_in_dim(head_total, tensor_rank, 1, 0)
    new_head, new_head_first, new_head_second = adam_step(
        head_params, mine_head, head_first, head_second, VECTOR_RATE, 0.0
    )
    new_shared, new_shared_first, new_shared_second = adam_step(
        shared_params, shared_total, shared_first, shared_second, VECTOR_RATE, 0.0
    )
    return (
        output,
        grad_input,
        new_master,
        new_first,
        new_second,
        new_head,
        new_head_first,
        new_head_second,
        new_shared,
        new_shared_first,
        new_shared_second,
    )


def solution(mesh):
    return jax.shard_map(
        body,
        mesh=mesh,
        in_specs=(
            P(("dp", "tensor"), None),
            P("dp", None),
            P(("dp", "tensor"), None),
            P(None, "dp"),
            P("dp"),
            P(),
            P(),
            P("tensor", "dp", None, None),
            P("tensor", "dp", None, None),
            P("tensor", "dp", None, None),
            P("tensor", None),
            P("tensor", None),
            P("tensor", None),
            P(),
            P(),
            P(),
        ),
        out_specs=(
            P(("dp", "tensor"), None),
            P(("dp", "tensor"), None),
            P("tensor", "dp", None, None),
            P("tensor", "dp", None, None),
            P("tensor", "dp", None, None),
            P("tensor", None),
            P("tensor", None),
            P("tensor", None),
            P(),
            P(),
            P(),
        ),
        check_vma=False,
    )
```

```python
import functools

import jax
import jax.numpy as jnp
from jax import lax
from jax.experimental import pallas as pl
from jax.experimental.pallas import tpu as pltpu
from jax.sharding import PartitionSpec as P

D = 1536
HEADS = 12
HEAD = 128
FF = 8960
TSTEPS = 16
STEPC = 10


NORM_EPS = 1e-06
BETA_ONE = 0.9
BETA_TWO = 0.999
ADAM_EPS = 1e-08
TILE_RATE = 1.0
TILE_DECAY = 0.1
VECTOR_RATE = 0.5
GELU_COEF = 0.7978845608028654


def rope_tables(token_places, head_size):
    sixths = head_size // 6
    frame_pairs = (head_size - 4 * sixths) // 2
    frame_freq = 10000.0 ** (-jnp.arange(frame_pairs, dtype=jnp.float32) / frame_pairs)
    side_freq = 10000.0 ** (-jnp.arange(sixths, dtype=jnp.float32) / sixths)
    spots = token_places.astype(jnp.float32)
    angles = jnp.concatenate(
        [
            spots[0][..., None] * frame_freq,
            spots[1][..., None] * side_freq,
            spots[2][..., None] * side_freq,
        ],
        -1,
    )
    angles = jnp.repeat(angles, 2, axis=-1)
    return (jnp.cos(angles), jnp.sin(angles))


def owner_layout(owners, slot_count, devices):
    indices = jnp.arange(owners.shape[0], dtype=jnp.int32)
    same_owner = (owners[:, None] == owners[None, :]) & (indices[None, :] < indices[:, None])
    slot_of = jnp.sum(same_owner.astype(jnp.int32), axis=1)
    places = owners * slot_count + slot_of
    spots = jnp.arange(slot_count * devices, dtype=jnp.int32)
    holder = (
        jnp.sum(jnp.where(places[None, :] == spots[:, None], indices[None, :] + 1, 0), axis=1) - 1
    )
    return (places, holder)


def tile_scales(tile_count, heads_here, blocks_here):
    indices = jnp.arange(tile_count)
    scale_in = D ** (-0.5)
    scale_out = HEADS ** (-0.5)
    scale_down = FF ** (-0.5)
    scales = jnp.where(
        indices < 3 * heads_here,
        scale_in,
        jnp.where(
            indices < 4 * heads_here,
            scale_out,
            jnp.where(
                indices < 7 * heads_here,
                scale_in,
                jnp.where(
                    indices < 8 * heads_here,
                    scale_out,
                    jnp.where(indices < 8 * heads_here + blocks_here, scale_in, scale_down),
                ),
            ),
        ),
    )
    return scales.astype(jnp.float32)


def adam_step(weight, gradient, moment_one, moment_two, step_rate, decay_rate):
    first_new = BETA_ONE * moment_one + (1.0 - BETA_ONE) * gradient
    second_new = BETA_TWO * moment_two + (1.0 - BETA_TWO) * gradient * gradient
    first_hat = first_new / (1.0 - BETA_ONE**STEPC)
    second_hat = second_new / (1.0 - BETA_TWO**STEPC)
    weight_new = weight - step_rate * (
        first_hat / (jnp.sqrt(second_hat) + ADAM_EPS) + decay_rate * weight
    )
    return (weight_new, first_new, second_new)


MESH = pl.DeviceIdType.MESH
ANY = pl.BlockSpec(memory_space=pl.ANY)
MIB = 1 << 20


def chip_pairs():
    return lax.axis_size("dp") == 16 and lax.axis_size("tensor") == 2


def pair_rank():
    if chip_pairs():
        return (lax.axis_index("dp") // 4) % 2
    return lax.axis_index("tensor")


def pair_swap(value):
    if chip_pairs():
        return lax.ppermute(value, "dp", [(i, i ^ 4) for i in range(16)])
    return lax.ppermute(value, "tensor", [(0, 1), (1, 0)])


def pair_sums(*values):
    stacked = jnp.concatenate([v.reshape(-1) for v in values])
    total = stacked + pair_swap(stacked)
    out, at = [], 0
    for v in values:
        out.append(total[at : at + v.size].reshape(v.shape))
        at += v.size
    return tuple(out)


def place_of():
    chip, core = lax.axis_index("dp"), lax.axis_index("tensor")
    z, y, x = chip // 4, (chip // 2) % 2, chip % 2
    return chip, core, z, y, x


def column_of(z, y, x, k):
    high, low_bit = z // 2, z % 2
    if k & 2:
        high = 1 - high
    if k & 1:
        low_bit = 1 - low_bit
    return (2 * high + low_bit) * 4 + 2 * y + x


def greet(chip, core, z, y, x):
    barrier = pltpu.get_barrier_semaphore()
    friends = []
    for k in range(4):
        for flip in (0, 1):
            if k or flip:
                friends.append((column_of(z, y, x, k), core if flip == 0 else 1 - core))
    friends.append((column_of(z, y, 1 - x, 0), core))
    friends.append((column_of(z, 1 - y, x, 0), core))
    for friend in friends:
        pl.semaphore_signal(barrier, inc=1, device_id=friend, device_id_type=MESH)
    pl.semaphore_wait(barrier, len(friends))


def gather_kernel(
    own, lat, cot, text, small, out, lats, cots, texts, smalls, clip_s, clip_r,
    near_s, col_r, x_s, x_r, y_s, y_r, sib_s, sib_r,
):
    chip, core, z, y, x = place_of()
    rank = z % 2
    half = own.shape[1] // 2
    part = half // 2
    at_x = column_of(z, y, 1 - x, 0)
    at_y = column_of(z, 1 - y, x, 0)
    greet(chip, core, z, y, x)

    batch = max(n for n in (1, 2, 3) if own.shape[0] % n == 0)
    batches = own.shape[0] // batch
    turns = 4 * batches

    def case(s):
        late = jnp.maximum(s - batches, 0)
        k = jnp.where(s < batches, 0, 1 + late % 3)
        return k, jnp.where(s < batches, s, late // 3)

    def remote(unit, g, first, count, send, recv, device):
        piece = out.at[
            unit, pl.ds(g * batch, batch), pl.ds(pl.multiple_of(first, 16), count), :
        ]
        return pltpu.make_async_remote_copy(
            src_ref=piece, dst_ref=piece, send_sem=send, recv_sem=recv,
            device_id=device, device_id_type=MESH,
        )

    def own_copy(g, j, h):
        target = (toggled(z, y, x, 0, 0, 2 * j) // 8 * 8) + core * 4 + 2 * y + x
        part_of = (pl.ds(g * batch, batch), pl.ds(h * half, half))
        src = own.at[part_of[0], part_of[1], :]
        dst = out.at[chip, part_of[0], part_of[1], :]
        recv = col_r.at[z * batches + g]
        go = pltpu.make_async_remote_copy(
            src_ref=src, dst_ref=dst, send_sem=near_s.at[(2 * j + h) * batches + g],
            recv_sem=recv, device_id=(target, h), device_id_type=MESH,
        )
        return go, pltpu.make_async_copy(src, dst, recv)

    for g in range(batches):
        for j in range(2):
            for h in range(2):
                go, here = own_copy(g, j, h)
                if j == 1:
                    go.start()
                    continue
                stays = jnp.logical_and(rank == core, core == h)

                @pl.when(stays)
                def _():
                    here.start()

                @pl.when(jnp.logical_not(stays))
                def _():
                    go.start()

    pair_chip = column_of(z, y, x, 1)
    rows_of_text = text.shape[0] // 2

    def clip_pieces(h):
        share = pl.ds(h * rows_of_text, rows_of_text)
        return ((lat, lats.at[h]), (cot, cots.at[h]), (text.at[share], texts.at[share]))

    home = rank == core
    trade = pltpu.make_async_remote_copy(
        src_ref=small, dst_ref=smalls, send_sem=clip_s.at[6], recv_sem=clip_r.at[6],
        device_id=(pair_chip, 1 - core), device_id_type=MESH,
    )
    keep = pltpu.make_async_copy(small, smalls, clip_r.at[6])

    @pl.when(home)
    def _():
        keep.start()

    @pl.when(jnp.logical_not(home))
    def _():
        trade.start()

    def hand_out(h, n, wait):
        src, dst = clip_pieces(h)[n]
        far = pltpu.make_async_remote_copy(
            src_ref=src, dst_ref=dst, send_sem=clip_s.at[n], recv_sem=clip_r.at[3 * h + n],
            device_id=(pair_chip, rank), device_id_type=MESH,
        )
        near = pltpu.make_async_remote_copy(
            src_ref=src, dst_ref=dst, send_sem=clip_s.at[3 + n], recv_sem=clip_r.at[3 * h + n],
            device_id=(chip, 1 - core), device_id_type=MESH,
        )
        here = pltpu.make_async_copy(src, dst, clip_r.at[3 * h + n])

        @pl.when(core == h)
        def _():
            if wait:
                far.wait_send()
            else:
                far.start()

            @pl.when(home)
            def _():
                if not wait:
                    here.start()

            @pl.when(jnp.logical_not(home))
            def _():
                if wait:
                    near.wait_send()
                else:
                    near.start()

    for n in range(3):
        for h in range(2):
            hand_out(h, n, False)

    mine, other = core * half, (1 - core) * half
    sibling = (chip, 1 - core)

    def to_x(s, n):
        k, g = case(s)
        i = turns * n + s
        unit = toggled(z, y, x, n, 0, k)
        return remote(unit, g, mine, part if n else half, x_s.at[i], x_r.at[i], (at_x, core))

    def from_x(s, n):
        k, g = case(s)
        i = turns * n + s
        unit = toggled(z, y, x, n, 1, k)
        return remote(unit, g, mine, part if n else half, x_s.at[i], x_r.at[i], (at_x, core))

    def to_y(s, n):
        k, g = case(s)
        i = turns * n + s
        unit = toggled(z, y, x, 0, n, k)
        first, count = (mine + part, part) if n else (mine, half)
        return remote(unit, g, first, count, y_s.at[i], y_r.at[i], (at_y, core))

    def from_y(s, n):
        k, g = case(s)
        i = turns * n + s
        unit = toggled(z, y, x, 1, n, k)
        first, count = (mine + part, part) if n else (mine, half)
        return remote(unit, g, first, count, y_s.at[i], y_r.at[i], (at_y, core))

    def to_sib(s, n, away=False):
        k, g = case(s)
        i = turns * n + s
        unit = toggled(z, y, x, int(n in (2, 3, 4)), int(n in (1, 3, 4)), k)
        first = (other if away else mine) + (part if n == 4 else 0)
        return remote(
            unit, g, first, part if n >= 3 else half, sib_s.at[i], sib_r.at[i], sibling
        )

    def column_in(s):
        k, g = case(s)
        unit = toggled(z, y, x, 0, 0, k)
        piece = out.at[
            unit, pl.ds(g * batch, batch), pl.ds(pl.multiple_of(mine, 16), half), :
        ]
        pltpu.make_async_copy(piece, piece, col_r.at[unit // 4 * batches + g]).wait()
        to_x(s, 0).start()
        to_y(s, 0).start()
        to_sib(s, 0).start()

    def side_in(s):
        from_x(s, 0).wait_recv()
        to_y(s, 1).start()
        to_sib(s, 1).start()
        from_y(s, 0).wait_recv()
        to_x(s, 1).start()
        to_sib(s, 2).start()

    def corner_in(s):
        from_x(s, 1).wait_recv()
        to_sib(s, 3).start()
        from_y(s, 1).wait_recv()
        to_sib(s, 4).start()

    def turn(step, carry):
        @pl.when(step < turns)
        def _():
            column_in(step)

        @pl.when(jnp.logical_and(step >= 1, step < turns + 1))
        def _():
            side_in(step - 1)

        @pl.when(step >= 2)
        def _():
            corner_in(step - 2)

        return carry

    lax.fori_loop(0, turns + 2, turn, 0)

    def settle(s, carry):
        for n in range(2):
            to_x(s, n).wait_send()
            to_y(s, n).wait_send()
        for n in range(5):
            to_sib(s, n).wait_send()
            to_sib(s, n, True).wait_recv()
        return carry

    lax.fori_loop(0, turns, settle, 0)
    for g in range(batches):
        for j in range(2):
            for h in range(2):
                go, _ = own_copy(g, j, h)
                if j == 1:
                    go.wait_send()
                    continue

                @pl.when(jnp.logical_not(jnp.logical_and(rank == core, core == h)))
                def _():
                    go.wait_send()

    for n in range(3):
        for h in range(2):
            hand_out(h, n, True)
            dst = clip_pieces(h)[n][1]
            pltpu.make_async_copy(dst, dst, clip_r.at[3 * h + n]).wait()

    @pl.when(jnp.logical_not(home))
    def _():
        trade.wait_send()

    pltpu.make_async_copy(smalls, smalls, clip_r.at[6]).wait()


def gather_slots(scaled, lat, cot, text, small):
    if not chip_pairs():
        everyone = lax.all_gather(scaled, "dp", axis=0, tiled=True)
        lats, cots = (lax.all_gather(v, "tensor") for v in (lat, cot))
        return everyone, lats, cots, text, small
    dma = pltpu.SemaphoreType.DMA
    turns = 4 * scaled.shape[0] // max(n for n in (1, 2, 3) if scaled.shape[0] % n == 0)
    counts = (7, 7, turns, turns) + (2 * turns,) * 4 + (5 * turns,) * 2
    everyone, *rest = pl.pallas_call(
        gather_kernel,
        out_shape=[
            jax.ShapeDtypeStruct((16,) + scaled.shape, scaled.dtype),
            jax.ShapeDtypeStruct((2,) + lat.shape, lat.dtype),
            jax.ShapeDtypeStruct((2,) + cot.shape, cot.dtype),
            jax.ShapeDtypeStruct(text.shape, text.dtype),
            jax.ShapeDtypeStruct(small.shape, small.dtype),
        ],
        in_specs=[ANY] * 5,
        out_specs=[ANY] * 5,
        scratch_shapes=[dma((n,)) for n in counts],
        compiler_params=pltpu.CompilerParams(
            collective_id=0, has_side_effects=True, vmem_limit_bytes=4 * MIB
        ),
    )(scaled, lat, cot, text, small)
    return everyone.reshape((-1,) + scaled.shape[1:]), *rest


def toggled(z, y, x, flip_y, flip_x, k):
    high = (z // 2 + k // 2) % 2
    low_bit = (z % 2 + k % 2) % 2
    return (2 * high + low_bit) * 4 + 2 * ((y + flip_y) % 2) + (x + flip_x) % 2


def reduce_kernel(
    kind, block, *refs,
):
    (
        *pieces, rows_in, after_in, dx_in, y_in, da_in, gains, vec_in,
        final, vec_out, result, result_grad, y_other, da_other, from_sib, from_x, from_y, corner_a, corner_b,
        left, right, ring, corners, side_x, side_y, middle, stage, vec_box, end_wide, end_low,
        load_s, stage_s, sib_s, sib_r, x_s, x_r, y_s, y_r, ca_s, ca_r, cb_s, cb_r, f_s, f_r, v_s, v_r,
        end_s, end_r, end_load,
    ) = refs
    chip, core, z, y, x = place_of()
    rank = z % 2
    slots, width, lanes = final.shape[1:]
    half = width // 2
    part = half // 2
    at_x = toggled(z, y, x, 0, 1, 0)
    at_y = toggled(z, y, x, 1, 0, 0)
    sibling = (chip, 1 - core)
    mates = (
        sibling,
        (at_x, core),
        (at_y, core),
        (toggled(z, y, x, 0, 0, 1), core),
        (toggled(z, y, x, 0, 0, 2), core),
    )

    kinds = left.shape[0]
    depth = right.shape[1]
    loads = []
    for i in range(kinds):
        columns = pieces[i].shape[1]
        loads.append(
            pltpu.make_async_copy(pieces[i], left.at[i, :, pl.ds(0, columns)], load_s.at[i])
        )
    first = 0
    blank = []
    for i, piece in enumerate(pieces[kinds:]):
        number, rows = piece.shape[:2]
        loads.append(
            pltpu.make_async_copy(
                piece, right.at[pl.ds(first, number), pl.ds(0, rows), :], load_s.at[kinds + i]
            )
        )
        if rows < depth:
            blank.append((first, number, rows))
        first += number
    for load in loads:
        load.start()
    for start, number, rows in blank:

        def clear(i, carry):
            right[start + i, pl.ds(rows, depth - rows), :] = jnp.zeros(
                (depth - rows, lanes), right.dtype
            )
            return carry

        lax.fori_loop(0, number, clear, 0)
    right[first] = jnp.zeros((depth, lanes), right.dtype)
    for i in range(kinds):
        columns = pieces[i].shape[1]
        if columns < depth:
            left[i, :, pl.ds(columns, depth - columns)] = jnp.zeros(
                (width, depth - columns), left.dtype
            )
    vec_out[...] = vec_in[...]
    greet(chip, core, z, y, x)
    for load in loads:
        load.wait()

    def remote(src, dst, send, recv, device):
        return pltpu.make_async_remote_copy(
            src_ref=src, dst_ref=dst, send_sem=send, recv_sem=recv,
            device_id=device, device_id_type=MESH,
        )

    batch = ring.shape[1]
    batches = slots // batch
    turns = 4 * batches
    deep = corners.shape[0]

    def flips(s):
        return 3 - s // batches

    def sums(q, s, first, terms, total):
        unit = toggled(z, y, x, 1 - q % 2, 1 - q // 2, flips(s))
        base = unit * slots + (s % batches) * batch
        count = total.shape[1]

        def one(i, carry):
            slot = base + i
            rows = pl.ds(pl.multiple_of(first, 128), count)
            acc = jnp.dot(
                left[kind[slot], rows, :], right[block[slot]], preferred_element_type=jnp.float32
            )
            for term in terms:
                acc = acc + term[i].astype(jnp.float32)
            total[i] = acc.astype(total.dtype)
            return carry

        lax.fori_loop(0, batch, one, 0)

    mine, other = core * half, (1 - core) * half

    def sub(ref, first):
        return ref.at[:, pl.ds(first, part), :]

    def sib_copy(q, s):
        i = turns * q + s
        return remote(ring.at[q], from_sib.at[i], sib_s.at[i], sib_r.at[i], sibling)

    def a_copy(s):
        return remote(
            sub(corners.at[s % deep], 0), corner_a.at[s], ca_s.at[s], ca_r.at[s], (at_x, core)
        )

    def b_copy(s):
        return remote(
            sub(corners.at[s % deep], part), corner_b.at[s], cb_s.at[s], cb_r.at[s], (at_y, core)
        )

    def x_copy(s, n):
        rows = pl.ds(n * part, part)
        i = turns * n + s
        return remote(
            side_x.at[s % deep, :, rows, :], from_x.at[s, :, rows, :], x_s.at[i], x_r.at[i],
            (at_x, core),
        )

    def y_copy(s, n):
        rows = pl.ds((1 - n) * part, part)
        i = turns * n + s
        return remote(
            side_y.at[s % deep, :, rows, :], from_y.at[s, :, rows, :], y_s.at[i], y_r.at[i],
            (at_y, core),
        )

    def f_copy(s):
        src = middle.at[s % deep]
        g = s % batches
        dst = final.at[
            z // 2, pl.ds(g * batch, batch), pl.ds(pl.multiple_of(mine, 128), half), :
        ]
        recv = f_r.at[(2 * (z // 2) + core) * batches + g]
        target = (toggled(z, y, x, 0, 0, flips(s)), rank)
        return remote(src, dst, f_s.at[s], recv, target), pltpu.make_async_copy(src, dst, recv)

    def stays(s):
        return jnp.logical_and(s >= turns - batches, rank == core)

    def for_sibling(s, low, high):
        def one(q, carry):
            @pl.when(s >= 1)
            def _():
                sib_copy(q, s - 1).wait_send()

            sums(q, s, other, (), ring.at[q])
            sib_copy(q, s).start()
            return carry

        lax.fori_loop(low, high, one, 0)

    def fetched(q, s):
        i = 2 * q + s % 2
        return pltpu.make_async_copy(from_sib.at[turns * q + s], stage.at[i], stage_s.at[i])

    def fetch(q, s):
        sib_copy(q, s).wait_recv()
        fetched(q, s).start()

    def taken(q, s):
        return stage.at[2 * q + s % 2]

    def corner(s):
        @pl.when(s >= deep)
        def _():
            a_copy(s - deep).wait_send()
            b_copy(s - deep).wait_send()

        fetched(0, s).wait()
        sums(0, s, mine, (taken(0, s),), corners.at[s % deep])
        a_copy(s).start()
        b_copy(s).start()

    def direct_sides(s):
        @pl.when(s >= deep)
        def _():
            for n in range(2):
                x_copy(s - deep, n).wait_send()
                y_copy(s - deep, n).wait_send()

        fetched(1, s).wait()
        sums(1, s, mine, (sub(taken(1, s), 0),), sub(side_x.at[s % deep], 0))
        x_copy(s, 0).start()
        fetched(2, s).wait()
        sums(2, s, mine + part, (sub(taken(2, s), part),), sub(side_y.at[s % deep], part))
        y_copy(s, 0).start()

    def relayed(s):
        return (
            pltpu.make_async_copy(corner_b.at[s], sub(stage.at[8], 0), stage_s.at[8]),
            pltpu.make_async_copy(corner_a.at[s], sub(stage.at[8], part), stage_s.at[9]),
        )

    def relayed_in(s):
        b_copy(s).wait_recv()
        relayed(s)[0].start()
        a_copy(s).wait_recv()
        relayed(s)[1].start()

    def relayed_sides(s):
        relayed(s)[0].wait()
        sums(
            1, s, mine + part, (sub(taken(1, s), part), sub(stage.at[8], 0)),
            sub(side_x.at[s % deep], part),
        )
        x_copy(s, 1).start()
        relayed(s)[1].wait()
        sums(
            2, s, mine, (sub(taken(2, s), 0), sub(stage.at[8], part)), sub(side_y.at[s % deep], 0)
        )
        y_copy(s, 1).start()

    def centre_terms(s):
        return (
            pltpu.make_async_copy(from_x.at[s], stage.at[9], stage_s.at[10]),
            pltpu.make_async_copy(from_y.at[s], stage.at[10], stage_s.at[11]),
        )

    def centre_in(s):
        for n, copies in enumerate((x_copy, y_copy)):
            copies(s, 0).wait_recv()
            copies(s, 1).wait_recv()
            centre_terms(s)[n].start()

    def centre(s):
        @pl.when(s >= deep)
        def _():
            f_copy(s - deep)[0].wait_send()

        fetched(3, s).wait()
        for term in centre_terms(s):
            term.wait()
        sums(3, s, mine, (taken(3, s), stage.at[9], stage.at[10]), middle.at[s % deep])
        go, here = f_copy(s)

        @pl.when(stays(s))
        def _():
            here.start()

        @pl.when(jnp.logical_not(stays(s)))
        def _():
            go.start()

    home = rank == core
    pair_device = (toggled(z, y, x, 0, 0, 1), core)
    ends = [
        remote(y_in, y_other, end_s.at[0], end_r.at[0], pair_device),
        remote(da_in, da_other, end_s.at[1], end_r.at[1], pair_device),
        remote(end_low.at[0], result, end_s.at[2], end_r.at[2], sibling),
        remote(end_wide.at[0], result_grad, end_s.at[3], end_r.at[3], sibling),
    ]
    end_loads = [
        pltpu.make_async_copy(src, dst, end_load.at[i])
        for i, (src, dst) in enumerate(
            (
                (rows_in, end_wide.at[0]), (after_in, end_wide.at[1]), (dx_in, end_wide.at[2]),
                (y_in, end_low.at[0]), (da_in, end_low.at[1]),
                (y_other, end_low.at[2]), (da_other, end_low.at[3]),
            )
        )
    ]
    end_stores = [
        pltpu.make_async_copy(end_low.at[0], result, end_load.at[7]),
        pltpu.make_async_copy(end_wide.at[0], result_grad, end_load.at[8]),
    ]

    def finish_rows():
        for n in range(2):
            ends[n].wait_recv()
            end_loads[5 + n].start()
        for load in end_loads:
            load.wait()
        tall = 16

        def one(i, carry):
            at = pl.ds(pl.multiple_of(i * tall, tall), tall)
            y_all = end_low[0, at].astype(F32) + end_low[2, at].astype(F32) + gains[2:3]
            end_low[0, at] = (end_wide[1, at] + gains[0:1] * y_all).astype(end_low.dtype)
            da = end_low[1, at].astype(F32) + end_low[3, at].astype(F32)
            back, _ = normed_back(end_wide[0, at], da * (1.0 + gains[1:2]))
            end_wide[0, at] = end_wide[2, at] + back
            return carry

        lax.fori_loop(0, rows_in.shape[0] // tall, one, 0)
        ends[2].start()
        ends[3].start()
        for store in end_stores:
            store.start()

    @pl.when(home)
    def _():
        for load in end_loads[:5]:
            load.start()

    @pl.when(jnp.logical_not(home))
    def _():
        ends[0].start()
        ends[1].start()

    def vec_copy(i):
        return remote(vec_out, vec_box.at[i], v_s.at[i], v_r.at[i], mates[i])

    def turn(step, carry):
        for i in range(5):

            @pl.when(step == i)
            def _():
                vec_copy(i).start()

        @pl.when(step + 1 < turns)
        def _():
            corner(step + 1)
            direct_sides(step + 1)

        @pl.when(step + 2 < turns)
        def _():
            for_sibling(step + 2, 0, 4)

        @pl.when(step < turns)
        def _():
            relayed_in(step)

        @pl.when(step >= 1)
        def _():
            centre_in(step - 1)

        @pl.when(step < turns)
        def _():
            relayed_sides(step)

        @pl.when(step >= 1)
        def _():
            centre(step - 1)

        @pl.when(step + 2 < turns)
        def _():
            for q in range(3):
                fetch(q, step + 2)

        @pl.when(step + 1 < turns)
        def _():
            fetch(3, step + 1)

        @pl.when(jnp.logical_and(step == 3, home))
        def _():
            finish_rows()

        for i in range(5):

            @pl.when(step == i)
            def _():
                vec_copy(i).wait()
                vec_out[...] = vec_out[...] + vec_box[i]

        return carry

    for_sibling(0, 0, 2)
    fetch(0, 0)
    corner(0)
    for_sibling(0, 2, 4)
    for q in range(1, 4):
        fetch(q, 0)
    direct_sides(0)
    for_sibling(1, 0, 4)
    for q in range(3):
        fetch(q, 1)
    lax.fori_loop(0, turns + 1, turn, 0)
    for q in range(4):
        sib_copy(q, turns - 1).wait_send()

    def settle(i, carry):
        s = turns - deep + i
        a_copy(s).wait_send()
        b_copy(s).wait_send()
        for n in range(2):
            x_copy(s, n).wait_send()
            y_copy(s, n).wait_send()

        @pl.when(jnp.logical_not(stays(s)))
        def _():
            f_copy(s)[0].wait_send()

        return carry

    lax.fori_loop(0, deep, settle, 0)

    @pl.when(home)
    def _():
        ends[2].wait_send()
        ends[3].wait_send()
        for store in end_stores:
            store.wait()

    @pl.when(jnp.logical_not(home))
    def _():
        ends[0].wait_send()
        ends[1].wait_send()
        ends[2].wait_recv()
        ends[3].wait_recv()

    for plane in range(2):
        for h in range(2):
            for g in range(batches):
                piece = final.at[plane, pl.ds(g * batch, batch), pl.ds(h * half, half), :]
                recv = f_r.at[(2 * plane + h) * batches + g]
                pltpu.make_async_copy(piece, piece, recv).wait()


def reduce_slots(holder, kinds, rows, columns, vector, ends, gains, slot_count):
    if not chip_pairs():
        grads = slot_grads(holder, kinds, [r.T for r in rows], columns)
        total = lax.psum_scatter(grads, "dp", scatter_dimension=0, tiled=True)
        x, after, dx, y_part, da_part = ends
        y_all, da_all = (
            v.astype(F32) + pair_swap(v).astype(F32) for v in (y_part, da_part)
        )
        result = (after + gains[0] * (y_all + gains[2])).astype(BF16)
        back, _ = normed_back(x, da_all * (1.0 + gains[1]))
        return total[None], lax.psum(vector, ("dp", "tensor")), result, dx + back
    left = rows
    width, depth = left[0].shape[0], max(r.shape[1] for r in rows)
    lanes = columns[0].shape[2]
    tiles = sum(c.shape[0] for c in columns)
    block = jnp.where(holder >= 0, holder, tiles)
    kind = kinds[jnp.maximum(holder, 0)]
    half = width // 2
    dma = pltpu.SemaphoreType.DMA
    scalars = pl.BlockSpec(memory_space=pltpu.SMEM)
    inside = pl.BlockSpec(memory_space=pltpu.VMEM)
    low = jnp.bfloat16

    batch = max(n for n in (1, 2, 3) if slot_count % n == 0)
    turns = 4 * slot_count // batch
    deep = 3

    def room(count, tall):
        return jax.ShapeDtypeStruct((count, batch, tall, lanes), low)

    def slab(count):
        return pltpu.VMEM((count, batch, half, lanes), low)

    outs = pl.pallas_call(
        reduce_kernel,
        out_shape=[
            jax.ShapeDtypeStruct((2, slot_count, width, lanes), low),
            jax.ShapeDtypeStruct(vector.shape, vector.dtype),
            jax.ShapeDtypeStruct(ends[0].shape, low), jax.ShapeDtypeStruct(ends[0].shape, F32),
            jax.ShapeDtypeStruct(ends[0].shape, low), jax.ShapeDtypeStruct(ends[0].shape, low),
            room(4 * turns, half), room(turns, half), room(turns, half),
            room(turns, half // 2), room(turns, half // 2),
        ],
        in_specs=[scalars, scalars] + [ANY] * (len(left) + len(columns) + 5) + [inside] * 2,
        out_specs=[ANY, inside] + [ANY] * 9,
        scratch_shapes=[
            pltpu.VMEM((len(left), width, depth), low),
            pltpu.VMEM((tiles + 1, depth, lanes), low),
            slab(4), slab(deep), slab(deep), slab(deep), slab(deep), slab(11),
            pltpu.VMEM((5,) + vector.shape, vector.dtype),
            pltpu.VMEM((3,) + ends[0].shape, F32),
            pltpu.VMEM((4,) + ends[0].shape, low),
        ]
        + [
            dma((n,))
            for n in (len(left) + len(columns), 12)
            + (4 * turns,) * 2
            + (2 * turns,) * 4
            + (turns,) * 6
            + (5, 5, 4, 4, 9)
        ],
        compiler_params=pltpu.CompilerParams(
            collective_id=1, has_side_effects=True, vmem_limit_bytes=58 * MIB
        ),
    )(kind, block, *left, *columns, *ends, gains, vector)
    return outs[:4]


def kind_of_blocks(tile_count, heads_here, blocks_here):
    number = jnp.arange(tile_count)
    kind = number // heads_here
    table = jnp.array([0, 0, 0, 1, 2, 3, 3, 4], jnp.int32)
    late = jnp.where(number < 8 * heads_here + blocks_here, 5, 6)
    return jnp.where(number < 8 * heads_here, table[jnp.minimum(kind, 7)], late).astype(jnp.int32)


def slot_grads(holder, kinds, rows, columns):
    depth = max(r.shape[0] for r in rows)

    def deep(value, axis):
        room = [(0, 0)] * value.ndim
        room[axis] = (0, depth - value.shape[axis])
        return jnp.pad(value, room)

    left = jnp.stack([deep(r, 0) for r in rows])
    right = jnp.concatenate([deep(c, 1) for c in columns], 0)
    slots = holder.shape[0]
    used = (holder >= 0).astype(jnp.int32)
    block = jnp.maximum(holder, 0)
    kind = kinds[block]
    width = rows[0].shape[1]
    lanes = right.shape[2]

    def multiply(kind_ref, block_ref, used_ref, left_ref, right_ref, out_ref):
        slot = pl.program_id(0)

        @pl.when(used_ref[slot] == 1)
        def _():
            out_ref[0] = lax.dot_general(
                left_ref[kind_ref[slot]],
                right_ref[0],
                (((0,), (0,)), ((), ())),
                preferred_element_type=jnp.float32,
            ).astype(out_ref.dtype)

        @pl.when(used_ref[slot] == 0)
        def _():
            out_ref[...] = jnp.zeros_like(out_ref)

    return pl.pallas_call(
        multiply,
        grid_spec=pltpu.PrefetchScalarGridSpec(
            num_scalar_prefetch=3,
            grid=(slots,),
            in_specs=[
                pl.BlockSpec(left.shape, lambda s, kd, b, u: (0, 0, 0)),
                pl.BlockSpec((1, depth, lanes), lambda s, kd, b, u: (b[s], 0, 0)),
            ],
            out_specs=pl.BlockSpec((1, width, lanes), lambda s, kd, b, u: (s, 0, 0)),
        ),
        out_shape=jax.ShapeDtypeStruct((slots, width, lanes), jnp.bfloat16),
        compiler_params=pltpu.CompilerParams(vmem_limit_bytes=48 * MIB),
    )(kind, block, used, left, right)


def adam_slots(planes, master, moment_one, moment_two, slot_scale, filled):
    count, slot_count, width, lanes = planes.shape

    def step(scale_ref, fill_ref, grads, weight, one, two, new_weight, new_one, new_two, grad_box, boxes, reads, writes):
        sources = (weight, one, two)
        targets = (new_weight, new_one, new_two)

        def load(slot):
            return [
                pltpu.make_async_copy(src.at[0, slot], boxes.at[n, slot], reads.at[n, slot])
                for n, src in enumerate(sources)
            ] + [
                pltpu.make_async_copy(
                    grads.at[n, slot], grad_box.at[n, slot], reads.at[3 + n, slot]
                )
                for n in range(count)
            ]

        def store(slot):
            return [
                pltpu.make_async_copy(boxes.at[n, slot], dst.at[0, slot], writes.at[n, slot])
                for n, dst in enumerate(targets)
            ]

        def begin(slot, carry):
            for copy in load(slot):
                copy.start()
            return carry

        def work(slot, carry):
            for copy in load(slot):
                copy.wait()

            @pl.when(fill_ref[slot] == 1)
            def _():
                total = grad_box[0, slot].astype(jnp.float32)
                for n in range(1, count):
                    total = total + grad_box[n, slot].astype(jnp.float32)
                results = adam_step(
                    boxes[0, slot], total * scale_ref[slot], boxes[1, slot], boxes[2, slot],
                    TILE_RATE, TILE_DECAY,
                )
                for n, value in enumerate(results):
                    boxes[n, slot] = value

            for copy in store(slot):
                copy.start()
            return carry

        def finish(slot, carry):
            for copy in store(slot):
                copy.wait()
            return carry

        for part in (begin, work, finish):
            lax.fori_loop(0, slot_count, part, 0)

    scalars = pl.BlockSpec(memory_space=pltpu.SMEM)
    return pl.pallas_call(
        step,
        in_specs=[scalars, scalars] + [ANY] * 4,
        out_specs=[ANY] * 3,
        out_shape=[pltpu.HBM(master.shape, jnp.float32)] * 3,
        scratch_shapes=[
            pltpu.VMEM((count, slot_count, width, lanes), planes.dtype),
            pltpu.VMEM((3, slot_count, width, lanes), jnp.float32),
            pltpu.SemaphoreType.DMA((3 + count, slot_count)),
            pltpu.SemaphoreType.DMA((3, slot_count)),
        ],
        compiler_params=pltpu.CompilerParams(vmem_limit_bytes=40 * MIB),
    )(
        slot_scale,
        filled.astype(jnp.int32),
        *[
            pltpu.with_memory_space_constraint(v, pltpu.HBM)
            for v in (planes, master, moment_one, moment_two)
        ],
    )


SCALING = HEAD ** (-0.5)
BF16 = jnp.bfloat16
F32 = jnp.float32


def nn(left, right):
    return jnp.dot(left, right, preferred_element_type=F32)


def nt(left, right):
    return lax.dot_general(left, right, (((1,), (1,)), ((), ())), preferred_element_type=F32)


def tn(left, right):
    return lax.dot_general(left, right, (((0,), (0,)), ((), ())), preferred_element_type=F32)


def normed(rows):
    centre = rows - jnp.mean(rows, -1, keepdims=True)
    inverse = lax.rsqrt(jnp.mean(centre * centre, -1, keepdims=True) + NORM_EPS)
    return centre * inverse, inverse


def normed_back(rows, grad):
    unit, inverse = normed(rows)
    mean = jnp.mean(grad, -1, keepdims=True)
    return (grad - mean - unit * jnp.mean(grad * unit, -1, keepdims=True)) * inverse, unit


def total_of(rows):
    return jnp.sum(rows, 0, keepdims=True)


def turned(rows, cos_tab, sin_tab):
    even = lax.broadcasted_iota(jnp.int32, rows.shape, 1) % 2 == 0
    partner = jnp.where(even, pltpu.roll(rows, HEAD - 1, 1), pltpu.roll(rows, 1, 1))
    return rows * cos_tab + partner * sin_tab


def wide(column):
    return jnp.broadcast_to(column, (column.shape[0], HEAD))


def pack_sums(for_rows, for_text=None):
    out = wide(for_rows)
    if for_text is None:
        return out
    lane = lax.broadcasted_iota(jnp.int32, out.shape, 1)
    count = for_text.shape[0] // 2
    rest = jnp.zeros((out.shape[0] - count, HEAD), F32)
    first = jnp.concatenate([wide(for_text[:count]), rest], 0)
    second = jnp.concatenate([wide(for_text[count:]), rest], 0)
    return jnp.where(lane < 32, out, jnp.where(lane < 64, first, second))


def unpack_text(sums, count):
    return jnp.concatenate([sums[: count // 2, 32:33], sums[: count // 2, 64:65]], 0)


def softmax(scores):
    expo = jnp.exp(scores - jnp.max(scores, -1, keepdims=True))
    return expo / jnp.sum(expo, -1, keepdims=True)


def self_scores(query_low, key_low, tokens):
    scores = nt(query_low, key_low) * SCALING
    lane = lax.broadcasted_iota(jnp.int32, scores.shape, 1)
    return jnp.where(lane < tokens, scores, -1e30)


def whole(array):
    zeros = (0,) * len(array.shape)
    return pl.BlockSpec(array.shape, lambda *_: zeros)


def block_at(first, stride=1):
    return pl.BlockSpec((1, D, HEAD), lambda i, where: (where[first + stride * i], 0, 0))


def call(body, places, grid, ins, outs, scratch=(), vmem=24):
    specs = [spec if spec is not None else whole(array) for array, spec in ins]
    shapes = [pltpu.HBM(shape, kind) for shape, kind, _ in outs]
    out_specs = [
        spec if spec is not None else whole(shape) for (_, _, spec), shape in zip(outs, shapes)
    ]
    return pl.pallas_call(
        body,
        grid_spec=pltpu.PrefetchScalarGridSpec(
            num_scalar_prefetch=1,
            grid=(grid,),
            in_specs=specs,
            out_specs=out_specs,
            scratch_shapes=list(scratch),
        ),
        out_shape=shapes,
        compiler_params=pltpu.CompilerParams(vmem_limit_bytes=vmem * MIB),
    )(places, *[pltpu.with_memory_space_constraint(array, pltpu.HBM) for array, _ in ins])


def head_lanes(rows, per=1):
    return pl.BlockSpec((rows, per * HEAD), lambda h, *_: (0, h))


def heads_per_step(heads, most):
    return max(n for n in (1, 2, 3, 6) if heads % n == 0 and n <= most)


def lane_group(ref, j):
    return ref[:, j * HEAD : (j + 1) * HEAD]


def joined(refs):
    return jnp.concatenate([ref[0] for ref in refs], 1)


def project_self(places, everyone, rows, mod, vecs, heads):
    count = rows.shape[0]
    span = heads * HEAD

    def body(_, rows_ref, mod_ref, vec_ref, *refs):
        weights, (low, pre, value, sums, acc) = refs[:heads], refs[heads:]
        i = pl.program_id(0)

        @pl.when(i == 0)
        def _():
            unit, _ = normed(rows_ref[...])
            low[...] = (unit * (1.0 + mod_ref[1:2]) + mod_ref[0:1]).astype(BF16)

        made = nn(low[...], joined(weights))

        @pl.when(i == 0)
        def _():
            q = made + vec_ref[0:1]
            pre[0] = q
            acc[...] = wide(jnp.sum(q * q, -1, keepdims=True))

        @pl.when(i == 1)
        def _():
            k = made + vec_ref[1:2]
            pre[0] = k
            lane = lax.broadcasted_iota(jnp.int32, acc.shape, 1)
            sums[...] = jnp.where(lane < 64, acc[...], wide(jnp.sum(k * k, -1, keepdims=True)))

        @pl.when(i == 2)
        def _():
            value[...] = (made + vec_ref[2:3]).astype(BF16)

    return call(
        body, places, 3,
        [(rows, None), (mod, None), (vecs, None)]
        + [(everyone, block_at(h, heads)) for h in range(heads)],
        [
            ((count, D), BF16, None),
            ((2, count, span), F32, pl.BlockSpec((1, count, span), lambda i, _: (jnp.minimum(i, 1), 0, 0))),
            ((count, span), BF16, None),
            ((count, HEAD), F32, None),
        ],
        [pltpu.VMEM((count, HEAD), F32)],
    )


def attend_self(places, everyone, pre, value, sums, other, vecs, cos_tab, sin_tab, heads, tokens):
    count = value.shape[0]
    per = heads_per_step(heads, 2)
    steps = heads // per

    def body(_, pre_ref, value_ref, sum_ref, other_ref, vec_ref, cos_ref, sin_ref, *refs):
        weights, (q_ref, k_ref, o_ref, y_ref, acc) = refs[:per], refs[per:]
        h = pl.program_id(0)
        total = sum_ref[...] + other_ref[...]
        q_inv = lax.rsqrt(total[:, 0:1] / D + NORM_EPS)
        k_inv = lax.rsqrt(total[:, 64:65] / D + NORM_EPS)
        cos, sin = cos_ref[...], sin_ref[...]
        outs = []
        for j in range(per):
            lanes = slice(j * HEAD, (j + 1) * HEAD)
            q = turned(pre_ref[0, :, lanes] * q_inv * vec_ref[3:4, lanes], cos, sin).astype(BF16)
            k = turned(pre_ref[1, :, lanes] * k_inv * vec_ref[4:5, lanes], cos, sin).astype(BF16)
            q_ref[:, lanes] = q
            k_ref[:, lanes] = k
            chance = softmax(self_scores(q, k, tokens))
            out = nn(chance.astype(BF16), value_ref[:, lanes]).astype(BF16)
            o_ref[j] = out
            outs.append(out)
        part = nt(jnp.concatenate(outs, 1), joined(weights))

        @pl.when(h == 0)
        def _():
            acc[...] = part

        @pl.when(h > 0)
        def _():
            acc[...] = acc[...] + part

        @pl.when(h == steps - 1)
        def _():
            y_ref[...] = acc[...].astype(BF16)

    lanes = head_lanes(count, per)
    return call(
        body, places, steps,
        [
            (pre, pl.BlockSpec((2, count, per * HEAD), lambda h, _: (0, 0, h))),
            (value, lanes), (sums, None), (other, None),
            (vecs, head_lanes(vecs.shape[0], per)), (cos_tab, None), (sin_tab, None),
        ]
        + [(everyone, block_at(3 * heads + j, per)) for j in range(per)],
        [
            (value.shape, BF16, lanes),
            (value.shape, BF16, lanes),
            ((heads, count, HEAD), BF16, pl.BlockSpec((per, count, HEAD), lambda h, _: (h, 0, 0))),
            ((count, D), BF16, None),
        ],
        [pltpu.VMEM((count, D), F32)],
    )


def project_text(places, everyone, context, vecs, heads):
    count = context.shape[0]
    span = heads * HEAD

    def body(_, text_ref, vec_ref, *refs):
        weights, (key, value, sums) = refs[:heads], refs[heads:]
        i = pl.program_id(0)
        made = nn(text_ref[...], joined(weights))

        @pl.when(i == 0)
        def _():
            k = made + vec_ref[6:7]
            key[...] = k
            sums[...] = wide(jnp.sum(k * k, -1, keepdims=True))

        @pl.when(i == 1)
        def _():
            value[...] = (made + vec_ref[7:8]).astype(BF16)

    return call(
        body, places, 2,
        [(context, None), (vecs, None)]
        + [(everyone, block_at(5 * heads + h, heads)) for h in range(heads)],
        [((count, span), F32, None), ((count, span), BF16, None), ((count, HEAD), F32, None)],
    )


def project_cross(places, everyone, rows, part, other, mod, shared, vecs, text_sums, heads):
    count = rows.shape[0]
    span = heads * HEAD
    text = text_sums.shape[0]

    def body(_, rows_ref, part_ref, other_ref, mod_ref, shared_ref, vec_ref, text_ref, *refs):
        weights, (branch, after, low, pre, sums) = refs[:heads], refs[heads:]
        y = part_ref[...].astype(F32) + other_ref[...].astype(F32) + shared_ref[0:1]
        branch[...] = y
        x = rows_ref[...] + mod_ref[2:3] * y
        after[...] = x
        unit, _ = normed(x)
        a = (unit * shared_ref[3:4] + shared_ref[4:5]).astype(BF16)
        low[...] = a
        q = nn(a, joined(weights)) + vec_ref[5:6]
        pre[...] = q
        sums[...] = pack_sums(jnp.sum(q * q, -1, keepdims=True), text_ref[:, 0:1])

    return call(
        body, places, 1,
        [(v, None) for v in (rows, part, other, mod, shared, vecs, text_sums)]
        + [(everyone, block_at(4 * heads + h)) for h in range(heads)],
        [
            ((count, D), F32, None),
            ((count, D), F32, None),
            ((count, D), BF16, None),
            ((count, span), F32, None),
            ((count, HEAD), F32, None),
        ],
    )


def attend_cross(places, everyone, pre, key_pre, value, sums, other, vecs, heads):
    count, text = pre.shape[0], value.shape[0]
    per = heads_per_step(heads, 6)
    steps = heads // per

    def body(_, pre_ref, key_ref, value_ref, sum_ref, other_ref, vec_ref, *refs):
        weights, (q_ref, k_ref, o_ref, y_ref, acc) = refs[:per], refs[per:]
        h = pl.program_id(0)
        total = sum_ref[...] + other_ref[...]
        q_inv = lax.rsqrt(total[:, 0:1] / D + NORM_EPS)
        k_inv = lax.rsqrt(unpack_text(total, text) / D + NORM_EPS)
        outs = []
        for j in range(per):
            lanes = slice(j * HEAD, (j + 1) * HEAD)
            q = (pre_ref[:, lanes] * q_inv * vec_ref[8:9, lanes]).astype(BF16)
            k = (key_ref[:, lanes] * k_inv * vec_ref[9:10, lanes]).astype(BF16)
            q_ref[:, lanes] = q
            k_ref[:, lanes] = k
            chance = softmax(nt(q, k) * SCALING)
            out = nn(chance.astype(BF16), value_ref[:, lanes]).astype(BF16)
            o_ref[j] = out
            outs.append(out)
        part = nt(jnp.concatenate(outs, 1), joined(weights))

        @pl.when(h == 0)
        def _():
            acc[...] = part

        @pl.when(h > 0)
        def _():
            acc[...] = acc[...] + part

        @pl.when(h == steps - 1)
        def _():
            y_ref[...] = acc[...].astype(BF16)

    return call(
        body, places, steps,
        [
            (pre, head_lanes(count, per)), (key_pre, head_lanes(text, per)),
            (value, head_lanes(text, per)), (sums, None), (other, None),
            (vecs, head_lanes(vecs.shape[0], per)),
        ]
        + [(everyone, block_at(7 * heads + j, per)) for j in range(per)],
        [
            (pre.shape, BF16, head_lanes(count, per)),
            (value.shape, BF16, head_lanes(text, per)),
            ((heads, count, HEAD), BF16, pl.BlockSpec((per, count, HEAD), lambda h, _: (h, 0, 0))),
            ((count, D), BF16, None),
        ],
        [pltpu.VMEM((count, D), F32)],
        vmem=40,
    )


def hidden_group(blocks):
    return max(g for g in (7, 5, 4, 3, 2, 1) if blocks % g == 0)


def block_lanes(where, everyone, held, sems, first, group, steps):
    i = pl.program_id(0)

    def fetch(step, act):
        slot = step % 2
        for j in range(group):
            copy = pltpu.make_async_copy(
                everyone.at[where[first + step * group + j]],
                held.at[slot, :, pl.ds(j * HEAD, HEAD)],
                sems.at[slot, j],
            )
            copy.start() if act else copy.wait()

    @pl.when(i == 0)
    def _():
        fetch(0, True)

    @pl.when(i + 1 < steps)
    def _():
        fetch(i + 1, True)

    fetch(i, False)
    return held[i % 2]


def lanes_scratch(group):
    return [pltpu.VMEM((2, D, group * HEAD), BF16), pltpu.SemaphoreType.DMA((2, group))]


def hidden_back(places, everyone, mod, cot, heads, blocks):
    count = cot.shape[0]
    group = hidden_group(blocks)
    steps = blocks // group

    def body(where, weights, mod_ref, cot_ref, grad, out, held, sems):
        @pl.when(pl.program_id(0) == 0)
        def _():
            grad[...] = (mod_ref[5:6] * cot_ref[...]).astype(BF16)

        down = block_lanes(where, weights, held, sems, 8 * heads + blocks, group, steps)
        out[...] = nn(grad[...], down).astype(BF16)

    return call(
        body, places, steps,
        [(everyone, ANY), (mod, None), (cot, None)],
        [
            ((count, D), BF16, None),
            ((count, blocks * HEAD), BF16, pl.BlockSpec((count, group * HEAD), lambda i, _: (0, i))),
        ],
        lanes_scratch(group),
        vmem=40,
    )


def hidden_both(places, everyone, after_one, part, other, mod, shared, d_act, up_bias, heads, blocks):
    count = after_one.shape[0]
    group = hidden_group(blocks)
    steps = blocks // group
    span = group * HEAD

    def body(where, weights, after_ref, part_ref, other_ref, mod_ref, shared_ref, d_ref, bias_ref, after, low, hidden, d_hidden, d_bias, da_ref, acc, held, sems):
        i = pl.program_id(0)

        @pl.when(i == 0)
        def _():
            x = after_ref[...] + part_ref[...].astype(F32) + other_ref[...].astype(F32)
            x = x + shared_ref[1:2]
            after[...] = x
            unit, _ = normed(x)
            low[...] = (unit * (1.0 + mod_ref[4:5]) + mod_ref[3:4]).astype(BF16)
            acc[...] = jnp.zeros_like(acc)

        up = block_lanes(where, weights, held, sems, 8 * heads, group, steps)
        pre = nn(low[...], up) + bias_ref[...]
        square = pre * pre
        bent = jnp.tanh(GELU_COEF * (pre + 0.044715 * pre * square))
        act = (0.5 * pre * (1.0 + bent)).astype(BF16)
        slope = 0.5 * (1.0 + bent) + 0.5 * pre * (1.0 - bent * bent) * (
            GELU_COEF * (1.0 + 3.0 * 0.044715 * square)
        )
        dh = (d_ref[...].astype(F32) * slope).astype(BF16)
        d_bias[...] = total_of(dh.astype(F32))
        for j in range(group):
            hidden[j] = act[:, j * HEAD : (j + 1) * HEAD]
            d_hidden[j] = dh[:, j * HEAD : (j + 1) * HEAD]
        acc[...] = acc[...] + nt(dh, up)

        @pl.when(i == steps - 1)
        def _():
            da_ref[...] = acc[...].astype(BF16)

    tall = pl.BlockSpec((group, count, HEAD), lambda i, _: (i, 0, 0))
    flat = pl.BlockSpec((1, span), lambda i, _: (0, i))
    return call(
        body, places, steps,
        [(everyone, ANY)]
        + [(v, None) for v in (after_one, part, other, mod, shared)]
        + [(d_act, pl.BlockSpec((count, span), lambda i, _: (0, i))), (up_bias, flat)],
        [
            ((count, D), F32, None),
            ((count, D), BF16, None),
            ((blocks, count, HEAD), BF16, tall),
            ((blocks, count, HEAD), BF16, tall),
            (up_bias.shape, F32, flat),
            ((count, D), BF16, None),
        ],
        [pltpu.VMEM((count, D), F32)] + lanes_scratch(group),
        vmem=40,
    )


def hidden_out(places, everyone, hidden, heads):
    blocks, count = hidden.shape[:2]
    group = hidden_group(blocks)
    steps = blocks // group

    def body(where, weights, hidden_ref, y_ref, acc, held, sems):
        i = pl.program_id(0)
        down = block_lanes(where, weights, held, sems, 8 * heads + blocks, group, steps)
        part = nt(jnp.concatenate([hidden_ref[j] for j in range(group)], 1), down)

        @pl.when(i == 0)
        def _():
            acc[...] = part

        @pl.when(i > 0)
        def _():
            acc[...] = acc[...] + part

        @pl.when(i == steps - 1)
        def _():
            y_ref[...] = acc[...].astype(BF16)

    return call(
        body, places, steps,
        [(everyone, ANY), (hidden, pl.BlockSpec((group, count, HEAD), lambda i, _: (i, 0, 0)))],
        [((count, D), BF16, None)],
        [pltpu.VMEM((count, D), F32)] + lanes_scratch(group),
        vmem=40,
    )[0]


def cross_back(places, everyone, cot, after_two, part, other, mod, query, key, value, pre, key_pre, vecs, heads):
    count, text = query.shape[0], key.shape[0]
    per = heads_per_step(heads, 6)
    steps = heads // per

    def body(_, cot_ref, after_ref, part_ref, other_ref, mod_ref, q_ref, k_ref, v_ref, pre_ref, key_ref, vec_ref, *refs):
        weights, (dx_ref, low_ref, dq_ref, dk_ref, dv_ref, sums, q_acc, k_acc) = refs[:per], refs[per:]
        h = pl.program_id(0)

        @pl.when(h == 0)
        def _():
            da = part_ref[...].astype(F32) + other_ref[...].astype(F32)
            back, _ = normed_back(after_ref[...], da * (1.0 + mod_ref[4:5]))
            dx = cot_ref[...] + back
            dx_ref[...] = dx
            low_ref[...] = dx.astype(BF16)
            q_acc[...] = jnp.zeros_like(q_acc)
            k_acc[...] = jnp.zeros_like(k_acc)

        do_all = nn(low_ref[...], joined(weights)).astype(BF16)
        q_sums, k_sums = 0.0, 0.0
        for j in range(per):
            lanes = slice(j * HEAD, (j + 1) * HEAD)
            do = do_all[:, lanes]
            q, k = q_ref[:, lanes], k_ref[:, lanes]
            chance = softmax(nt(q, k) * SCALING)
            dp = nt(do, v_ref[:, lanes])
            ds = (chance * (dp - jnp.sum(chance * dp, -1, keepdims=True))).astype(BF16)
            dv_ref[j] = tn(chance.astype(BF16), do).astype(BF16)
            dq = nn(ds, k) * SCALING
            dk = tn(ds, q) * SCALING
            dq_ref[:, lanes] = dq
            dk_ref[:, lanes] = dk
            q_sums += pre_ref[:, lanes] * vec_ref[8:9, lanes] * dq
            k_sums += key_ref[:, lanes] * vec_ref[9:10, lanes] * dk
        q_acc[...] = q_acc[...] + q_sums
        k_acc[...] = k_acc[...] + k_sums

        @pl.when(h == steps - 1)
        def _():
            sums[...] = pack_sums(
                jnp.sum(q_acc[...], -1, keepdims=True), jnp.sum(k_acc[...], -1, keepdims=True)
            )

    return call(
        body, places, steps,
        [(v, None) for v in (cot, after_two, part, other, mod)]
        + [
            (query, head_lanes(count, per)), (key, head_lanes(text, per)),
            (value, head_lanes(text, per)), (pre, head_lanes(count, per)),
            (key_pre, head_lanes(text, per)), (vecs, head_lanes(vecs.shape[0], per)),
        ]
        + [(everyone, block_at(7 * heads + j, per)) for j in range(per)],
        [
            ((count, D), F32, None),
            ((count, D), BF16, None),
            (query.shape, F32, head_lanes(count, per)),
            (key.shape, F32, head_lanes(text, per)),
            ((heads, text, HEAD), BF16, pl.BlockSpec((per, text, HEAD), lambda h, _: (h, 0, 0))),
            ((count, HEAD), F32, None),
        ],
        [pltpu.VMEM((count, HEAD), F32), pltpu.VMEM((text, HEAD), F32)],
        vmem=48,
    )


def norm_grad(pre, inverse, gain, incoming, total):
    grad = inverse * (gain * incoming) - pre * (inverse * inverse * inverse) * (total / D)
    low = grad.astype(BF16)
    return low, total_of(low.astype(F32)), total_of(incoming * pre * inverse)


def cross_back_rows(places, everyone, pre, key_pre, dq, dk, dv, squares, squares_other, sums, sums_other, vecs, heads):
    count, text = pre.shape[0], key_pre.shape[0]
    per = heads_per_step(heads, 6)
    steps = heads // per

    def body(_, pre_ref, key_ref, dq_ref, dk_ref, dv_ref, sq_ref, sqo_ref, sum_ref, sumo_ref, vec_ref, *refs):
        weights, (gq_ref, gk_ref, vec_out, da_ref, acc) = refs[:per], refs[per:]
        h = pl.program_id(0)
        squares_all = sq_ref[...] + sqo_ref[...]
        total = sum_ref[...] + sumo_ref[...]
        q_inv = lax.rsqrt(squares_all[:, 0:1] / D + NORM_EPS)
        k_inv = lax.rsqrt(unpack_text(squares_all, text) / D + NORM_EPS)
        q_total, k_total = total[:, 0:1], unpack_text(total, text)
        lows = []
        for j in range(per):
            lanes = slice(j * HEAD, (j + 1) * HEAD)
            low_q, bias_q, gain_q = norm_grad(
                pre_ref[:, lanes], q_inv, vec_ref[8:9, lanes], dq_ref[:, lanes], q_total
            )
            low_k, bias_k, gain_k = norm_grad(
                key_ref[:, lanes], k_inv, vec_ref[9:10, lanes], dk_ref[:, lanes], k_total
            )
            gq_ref[j] = low_q
            gk_ref[j] = low_k
            lows.append(low_q)
            bias_v = total_of(dv_ref[j].astype(F32))
            vec_out[:, lanes] = jnp.concatenate(
                [bias_q, bias_k, bias_v, gain_q, gain_k, jnp.zeros((3, HEAD), F32)], 0
            )
        part = nt(jnp.concatenate(lows, 1), joined(weights))

        @pl.when(h == 0)
        def _():
            acc[...] = part

        @pl.when(h > 0)
        def _():
            acc[...] = acc[...] + part

        @pl.when(h == steps - 1)
        def _():
            da_ref[...] = acc[...].astype(BF16)

    tall = pl.BlockSpec((per, count, HEAD), lambda h, _: (h, 0, 0))
    tall_text = pl.BlockSpec((per, text, HEAD), lambda h, _: (h, 0, 0))
    return call(
        body, places, steps,
        [
            (pre, head_lanes(count, per)), (key_pre, head_lanes(text, per)),
            (dq, head_lanes(count, per)), (dk, head_lanes(text, per)), (dv, tall_text),
            (squares, None), (squares_other, None), (sums, None), (sums_other, None),
            (vecs, head_lanes(vecs.shape[0], per)),
        ]
        + [(everyone, block_at(4 * heads + j, per)) for j in range(per)],
        [
            ((heads, count, HEAD), BF16, tall),
            ((heads, text, HEAD), BF16, tall_text),
            ((8, heads * HEAD), F32, head_lanes(8, per)),
            ((count, D), BF16, None),
        ],
        [pltpu.VMEM((count, D), F32)],
        vmem=40,
    )


def self_back(places, everyone, dx_two, after_one, part, other, mod, shared, branch, query, key, value, pre, vecs, cos_tab, sin_tab, heads, tokens):
    count = query.shape[0]
    per = heads_per_step(heads, 2)
    steps = heads // per

    def body(_, dx_in, after_ref, part_ref, other_ref, mod_ref, shared_ref, branch_ref, q_ref, k_ref, v_ref, pre_ref, vec_ref, cos_ref, sin_ref, *refs):
        weights, (dx_ref, low_ref, d_ref, dv_ref, sums, vec_out, q_acc, k_acc) = refs[:per], refs[per:]
        h = pl.program_id(0)

        @pl.when(h == 0)
        def _():
            da = part_ref[...].astype(F32) + other_ref[...].astype(F32)
            back, _ = normed_back(after_ref[...], da * shared_ref[3:4])
            dx = dx_in[...] + back
            dx_ref[...] = dx
            low = (mod_ref[2:3] * dx).astype(BF16)
            low_ref[...] = low
            vec_out[0:1] = 0.5 * total_of(low.astype(F32))
            vec_out[1:2] = 0.5 * total_of(dx * branch_ref[...])
            q_acc[...] = jnp.zeros_like(q_acc)
            k_acc[...] = jnp.zeros_like(k_acc)

        do_all = nn(low_ref[...], joined(weights)).astype(BF16)
        cos, sin = cos_ref[...], -sin_ref[...]
        q_sums, k_sums = 0.0, 0.0
        for j in range(per):
            lanes = slice(j * HEAD, (j + 1) * HEAD)
            do = do_all[:, lanes]
            q, k = q_ref[:, lanes], k_ref[:, lanes]
            chance = softmax(self_scores(q, k, tokens))
            dp = nt(do, v_ref[:, lanes])
            ds = (chance * (dp - jnp.sum(chance * dp, -1, keepdims=True))).astype(BF16)
            dv_ref[j] = tn(chance.astype(BF16), do).astype(BF16)
            dq = turned(nn(ds, k) * SCALING, cos, sin)
            dk = turned(tn(ds, q) * SCALING, cos, sin)
            d_ref[0, :, lanes] = dq
            d_ref[1, :, lanes] = dk
            q_sums += pre_ref[0, :, lanes] * vec_ref[3:4, lanes] * dq
            k_sums += pre_ref[1, :, lanes] * vec_ref[4:5, lanes] * dk
        q_acc[...] = q_acc[...] + q_sums
        k_acc[...] = k_acc[...] + k_sums

        @pl.when(h == steps - 1)
        def _():
            lane = lax.broadcasted_iota(jnp.int32, q_acc.shape, 1)
            sums[...] = jnp.where(
                lane < 64,
                wide(jnp.sum(q_acc[...], -1, keepdims=True)),
                wide(jnp.sum(k_acc[...], -1, keepdims=True)),
            )

    lanes = head_lanes(count, per)
    pair = pl.BlockSpec((2, count, per * HEAD), lambda h, _: (0, 0, h))
    return call(
        body, places, steps,
        [(v, None) for v in (dx_two, after_one, part, other, mod, shared, branch)]
        + [
            (query, lanes), (key, lanes), (value, lanes), (pre, pair),
            (vecs, head_lanes(vecs.shape[0], per)), (cos_tab, None), (sin_tab, None),
        ]
        + [(everyone, block_at(3 * heads + j, per)) for j in range(per)],
        [
            ((count, D), F32, None),
            ((count, D), BF16, None),
            (pre.shape, F32, pair),
            ((heads, count, HEAD), BF16, pl.BlockSpec((per, count, HEAD), lambda h, _: (h, 0, 0))),
            ((count, HEAD), F32, None),
            ((2, D), F32, None),
        ],
        [pltpu.VMEM((count, HEAD), F32), pltpu.VMEM((count, HEAD), F32)],
        vmem=32,
    )


def self_back_rows(places, everyone, rows, pre, grads, dv, squares, squares_other, sums, sums_other, vecs, heads):
    count = pre.shape[1]
    per = heads_per_step(heads, 2)
    steps = heads // per

    def body(_, rows_ref, pre_ref, d_ref, dv_ref, sq_ref, sqo_ref, sum_ref, sumo_ref, vec_ref, *refs):
        weights, (gq_ref, gk_ref, vec_out, da_ref, row_out, acc) = refs[: 3 * per], refs[3 * per :]
        h = pl.program_id(0)
        squares_all = sq_ref[...] + sqo_ref[...]
        total = sum_ref[...] + sumo_ref[...]
        inverses = [
            lax.rsqrt(squares_all[:, n : n + 1] / D + NORM_EPS) for n in (0, 64)
        ]
        lows = []
        for j in range(per):
            lanes = slice(j * HEAD, (j + 1) * HEAD)
            biases, gains = [], []
            for n, out in enumerate((gq_ref, gk_ref)):
                low, bias, gain = norm_grad(
                    pre_ref[n, :, lanes], inverses[n], vec_ref[3 + n : 4 + n, lanes],
                    d_ref[n, :, lanes], total[:, 64 * n : 64 * n + 1],
                )
                out[j] = low
                lows.append(low)
                biases.append(bias)
                gains.append(gain)
            dv_low = dv_ref[j]
            lows.append(dv_low)
            vec_out[:, lanes] = jnp.concatenate(
                biases + [total_of(dv_low.astype(F32))] + gains + [jnp.zeros((3, HEAD), F32)], 0
            )
        part = nt(jnp.concatenate(lows, 1), joined(weights))

        @pl.when(h == 0)
        def _():
            acc[...] = part

        @pl.when(h > 0)
        def _():
            acc[...] = acc[...] + part

        @pl.when(h == steps - 1)
        def _():
            da = acc[...]
            da_ref[...] = da.astype(BF16)
            row_out[0:1] = total_of(da)
            row_out[1:2] = total_of(da * normed(rows_ref[...])[0])

    tall = pl.BlockSpec((per, count, HEAD), lambda h, _: (h, 0, 0))
    pair = pl.BlockSpec((2, count, per * HEAD), lambda h, _: (0, 0, h))
    return call(
        body, places, steps,
        [
            (rows, None), (pre, pair), (grads, pair), (dv, tall), (squares, None),
            (squares_other, None), (sums, None), (sums_other, None),
            (vecs, head_lanes(vecs.shape[0], per)),
        ]
        + [(everyone, block_at(n * heads + j, per)) for j in range(per) for n in range(3)],
        [
            ((heads, count, HEAD), BF16, tall),
            ((heads, count, HEAD), BF16, tall),
            ((8, heads * HEAD), F32, head_lanes(8, per)),
            ((count, D), BF16, None),
            ((2, D), F32, None),
        ],
        [pltpu.VMEM((count, D), F32)],
        vmem=40,
    )


def shared_sums(places, after_one, after_two, grad_two, grad_three, cot, da_two, da_three, y_three, shared):
    def body(_, x1_ref, x2_ref, dy2, dy3, cot_ref, da2, da3, y3, shared_ref, out):
        out[...] = jnp.zeros_like(out)
        out[1:2] = 0.5 * total_of(dy2[...].astype(F32))
        out[2:3] = 0.5 * total_of(dy3[...].astype(F32))
        part = da3[...].astype(F32)
        out[3:4] = total_of(part * normed(x1_ref[...])[0])
        out[4:5] = total_of(part)
        part = da2[...].astype(F32)
        out[8:9] = total_of(part)
        out[9:10] = total_of(part * normed(x2_ref[...])[0])
        out[10:11] = total_of(cot_ref[...] * (y3[...].astype(F32) + 0.5 * shared_ref[2:3]))

    return call(
        body, places, 1,
        [(v, None) for v in (after_one, after_two, grad_two, grad_three, cot, da_two, da_three, y_three, shared)],
        [(shared.shape, F32, None)],
    )[0]


def body(
    latents,
    context,
    cotangent,
    positions,
    step_ids,
    owners,
    time_table,
    master,
    first_moment,
    second_moment,
    head_params,
    head_first,
    head_second,
    shared_params,
    shared_first,
    shared_second,
):
    tensors = lax.axis_size("tensor")
    devices = lax.axis_size("dp")
    slot_count = master.shape[1]
    tile_count = owners.shape[0]
    heads_here = HEADS // tensors
    blocks_here = FF // (HEAD * tensors)
    width_here = D // tensors
    places, holder = owner_layout(owners, slot_count, devices)
    scales = tile_scales(tile_count, heads_here, blocks_here)
    my_slots = lax.dynamic_slice_in_dim(holder, lax.axis_index("dp") * slot_count, slot_count)
    rank = pair_rank()
    filled = my_slots >= 0
    slot_scale = jnp.where(filled, scales[jnp.maximum(my_slots, 0)], 0.0)
    scaled = (master[0] * slot_scale[:, None, None]).astype(jnp.bfloat16)
    half = latents.shape[0]
    tokens = 2 * half
    count = -(-tokens // 16) * 16
    taller = ((0, -half % 16), (0, 0))
    small = jnp.concatenate(
        [
            head_params[0],
            positions.reshape(-1).astype(jnp.float32),
            step_ids.astype(jnp.float32),
        ]
    )
    packed = jnp.pad(small, (0, -small.shape[0] % 1024)).reshape(-1, HEAD)
    everyone, lats, cots, context, packed = gather_slots(
        scaled, jnp.pad(latents, taller), jnp.pad(cotangent, taller), context, packed
    )
    small = packed.reshape(-1)
    vectors = small[: head_params.shape[1]]
    small = small[head_params.shape[1] :]
    positions = small[: positions.size].reshape(positions.shape)
    step = small[positions.size]
    vecs = vectors[: 10 * width_here].reshape(10, width_here)
    up_bias = vectors[10 * width_here :].reshape(1, -1)
    chosen = (step == jnp.arange(TSTEPS)).astype(jnp.float32)
    mod = shared_params[5:11] + jnp.einsum(
        "s,skd->kd", chosen, time_table, precision=lax.Precision.HIGHEST
    )
    cos_tab, sin_tab = rope_tables(positions, HEAD)
    sin_tab = jnp.where(jnp.arange(HEAD) % 2 == 0, -sin_tab, sin_tab)
    cos_tab, sin_tab = (jnp.pad(t, ((0, count - tokens), (0, 0))) for t in (cos_tab, sin_tab))

    def all_rows(halves):
        rows = jnp.concatenate([halves[0, :half], halves[1, :half]], 0)
        return jnp.pad(rows, ((0, count - tokens), (0, 0))).astype(jnp.float32)

    def upright(rows):
        return jnp.pad(rows, ((0, -rows.shape[0] % HEAD), (0, 0))).T

    def beside(*values):
        return lax.optimization_barrier(values)

    rows, cot = all_rows(lats), all_rows(cots)
    low_one, pre_one, value_one, squares_one = project_self(
        places, everyone, rows, mod, vecs, heads_here
    )
    squares_one_other = pair_swap(squares_one)
    query_one, key_one, heads_one, part_one = attend_self(
        places, everyone, pre_one, value_one, squares_one, squares_one_other, vecs, cos_tab,
        sin_tab, heads_here, tokens,
    )
    part_one, context = beside(part_one, context)
    part_one_other = pair_swap(part_one)
    key_pre, value_two, text_squares = project_text(places, everyone, context, vecs, heads_here)
    left_context, left_one = upright(context), upright(low_one)
    part_one_other, key_pre, left_context, left_one = beside(
        part_one_other, key_pre, left_context, left_one
    )
    branch_one, after_one, low_two, pre_two, squares_two = project_cross(
        places, everyone, rows, part_one, part_one_other, mod, shared_params, vecs,
        text_squares, heads_here,
    )
    squares_two_other = pair_swap(squares_two)
    query_two, key_two, heads_two, part_two = attend_cross(
        places, everyone, pre_two, key_pre, value_two, squares_two, squares_two_other, vecs,
        heads_here,
    )
    part_two, cot, low_two = beside(part_two, cot, low_two)
    part_two_other = pair_swap(part_two)
    grad_three, d_act = hidden_back(places, everyone, mod, cot, heads_here, blocks_here)
    left_two, left_grad_three = upright(low_two), upright(grad_three)
    part_two_other, d_act, left_two, left_grad_three = beside(
        part_two_other, d_act, left_two, left_grad_three
    )
    after_two, low_three, hidden, d_hidden, d_up_bias, da_two = hidden_both(
        places, everyone, after_one, part_two, part_two_other, mod, shared_params, d_act, up_bias,
        heads_here, blocks_here,
    )
    da_two_other = pair_swap(da_two)
    y_three = hidden_out(places, everyone, hidden, heads_here)
    left_three = upright(low_three)
    da_two_other, y_three, left_three = beside(da_two_other, y_three, left_three)
    dx_two, grad_two, dq_two, dk_two, dv_two, sums_two = cross_back(
        places, everyone, cot, after_two, da_two, da_two_other, mod, query_two, key_two,
        value_two, pre_two, key_pre, vecs, heads_here,
    )
    query_grad_two, key_grad_two, vecs_two, da_three = cross_back_rows(
        places, everyone, pre_two, key_pre, dq_two, dk_two, dv_two, squares_two,
        squares_two_other, sums_two, pair_swap(sums_two), vecs, heads_here,
    )
    da_three_other = pair_swap(da_three)
    shared_grad = shared_sums(
        places, after_one, after_two, grad_two, grad_three, cot, da_two, da_three, y_three,
        shared_params,
    )
    left_grad_two = upright(grad_two)
    da_three_other, shared_grad, left_grad_two = beside(da_three_other, shared_grad, left_grad_two)
    dx_one, grad_one, d_one, dv_one, sums_one, rows_a = self_back(
        places, everyone, dx_two, after_one, da_three, da_three_other, mod, shared_params,
        branch_one, query_one, key_one, value_one, pre_one, vecs, cos_tab, sin_tab, heads_here,
        tokens,
    )
    query_grad_one, key_grad_one, vecs_one, da_one, rows_b = self_back_rows(
        places, everyone, rows, pre_one, d_one, dv_one, squares_one, squares_one_other, sums_one,
        pair_swap(sums_one), vecs, heads_here,
    )
    shared_grad = jnp.concatenate(
        [rows_a[0:1], shared_grad[1:5], rows_b, rows_a[1:2], shared_grad[8:]], 0
    )
    head_grad = jnp.concatenate(
        [vecs_one[:5].reshape(-1), vecs_two[:5].reshape(-1), d_up_bias.reshape(-1)]
    )
    tensor_rank = lax.axis_index("tensor")
    head_padded = jnp.where(jnp.arange(tensors)[:, None] == rank, head_grad[None, :], 0.0)
    vector = jnp.concatenate([head_padded.reshape(-1), shared_grad.reshape(-1)])
    vector = jnp.pad(vector, (0, -vector.shape[0] % 1024)).reshape(-1, 128)
    parts, vector, output, grad_input = reduce_slots(
        holder,
        kind_of_blocks(tile_count, heads_here, blocks_here),
        (left_one, upright(grad_one), left_two, left_context, left_grad_two, left_three, left_grad_three),
        (
            query_grad_one,
            key_grad_one,
            dv_one,
            heads_one,
            query_grad_two,
            key_grad_two,
            dv_two,
            heads_two,
            d_hidden,
            hidden,
        ),
        vector,
        (rows, after_two, dx_one, y_three, da_one),
        jnp.concatenate([mod[5:6], mod[1:2], shared_params[2:3], jnp.zeros((5, D), F32)], 0),
        slot_count,
    )
    output, grad_input = (
        jnp.where(lax.axis_index("tensor") == 0, v[:half], v[half:tokens])
        for v in (output, grad_input)
    )
    new_master, new_first, new_second = adam_slots(
        parts, master, first_moment, second_moment, slot_scale, filled
    )
    vector = vector.reshape(-1)
    head_total = vector[: head_padded.size].reshape(head_padded.shape)
    shared_total = vector[head_padded.size : head_padded.size + shared_grad.size]
    shared_total = shared_total.reshape(shared_grad.shape)
    mine_head = lax.dynamic_slice_in_dim(head_total, tensor_rank, 1, 0)
    new_head, new_head_first, new_head_second = adam_step(
        head_params, mine_head, head_first, head_second, VECTOR_RATE, 0.0
    )
    new_shared, new_shared_first, new_shared_second = adam_step(
        shared_params, shared_total, shared_first, shared_second, VECTOR_RATE, 0.0
    )
    return (
        output,
        grad_input,
        new_master,
        new_first,
        new_second,
        new_head,
        new_head_first,
        new_head_second,
        new_shared,
        new_shared_first,
        new_shared_second,
    )


def solution(mesh):
    return jax.shard_map(
        body,
        mesh=mesh,
        in_specs=(
            P(("dp", "tensor"), None),
            P("dp", None),
            P(("dp", "tensor"), None),
            P(None, "dp"),
            P("dp"),
            P(),
            P(),
            P("tensor", "dp", None, None),
            P("tensor", "dp", None, None),
            P("tensor", "dp", None, None),
            P("tensor", None),
            P("tensor", None),
            P("tensor", None),
            P(),
            P(),
            P(),
        ),
        out_specs=(
            P(("dp", "tensor"), None),
            P(("dp", "tensor"), None),
            P("tensor", "dp", None, None),
            P("tensor", "dp", None, None),
            P("tensor", "dp", None, None),
            P("tensor", None),
            P("tensor", None),
            P("tensor", None),
            P(),
            P(),
            P(),
        ),
        check_vma=False,
    )
```

```python
import functools

import jax
import jax.numpy as jnp
from jax import lax
from jax.experimental import pallas as pl
from jax.experimental.pallas import tpu as pltpu
from jax.sharding import PartitionSpec as P

D = 1536
HEADS = 12
HEAD = 128
FF = 8960
TSTEPS = 16
STEPC = 10


NORM_EPS = 1e-06
BETA_ONE = 0.9
BETA_TWO = 0.999
ADAM_EPS = 1e-08
TILE_RATE = 1.0
TILE_DECAY = 0.1
VECTOR_RATE = 0.5
GELU_COEF = 0.7978845608028654


def rope_tables(token_places, head_size):
    sixths = head_size // 6
    frame_pairs = (head_size - 4 * sixths) // 2
    frame_freq = 10000.0 ** (-jnp.arange(frame_pairs, dtype=jnp.float32) / frame_pairs)
    side_freq = 10000.0 ** (-jnp.arange(sixths, dtype=jnp.float32) / sixths)
    spots = token_places.astype(jnp.float32)
    angles = jnp.concatenate(
        [
            spots[0][..., None] * frame_freq,
            spots[1][..., None] * side_freq,
            spots[2][..., None] * side_freq,
        ],
        -1,
    )
    angles = jnp.repeat(angles, 2, axis=-1)
    return (jnp.cos(angles), jnp.sin(angles))


def owner_layout(owners, slot_count, devices):
    indices = jnp.arange(owners.shape[0], dtype=jnp.int32)
    same_owner = (owners[:, None] == owners[None, :]) & (indices[None, :] < indices[:, None])
    slot_of = jnp.sum(same_owner.astype(jnp.int32), axis=1)
    places = owners * slot_count + slot_of
    spots = jnp.arange(slot_count * devices, dtype=jnp.int32)
    holder = (
        jnp.sum(jnp.where(places[None, :] == spots[:, None], indices[None, :] + 1, 0), axis=1) - 1
    )
    return (places, holder)


def tile_scales(tile_count, heads_here, blocks_here):
    indices = jnp.arange(tile_count)
    scale_in = D ** (-0.5)
    scale_out = HEADS ** (-0.5)
    scale_down = FF ** (-0.5)
    scales = jnp.where(
        indices < 3 * heads_here,
        scale_in,
        jnp.where(
            indices < 4 * heads_here,
            scale_out,
            jnp.where(
                indices < 7 * heads_here,
                scale_in,
                jnp.where(
                    indices < 8 * heads_here,
                    scale_out,
                    jnp.where(indices < 8 * heads_here + blocks_here, scale_in, scale_down),
                ),
            ),
        ),
    )
    return scales.astype(jnp.float32)


def adam_step(weight, gradient, moment_one, moment_two, step_rate, decay_rate):
    first_new = BETA_ONE * moment_one + (1.0 - BETA_ONE) * gradient
    second_new = BETA_TWO * moment_two + (1.0 - BETA_TWO) * gradient * gradient
    first_hat = first_new / (1.0 - BETA_ONE**STEPC)
    second_hat = second_new / (1.0 - BETA_TWO**STEPC)
    weight_new = weight - step_rate * (
        first_hat / (jnp.sqrt(second_hat) + ADAM_EPS) + decay_rate * weight
    )
    return (weight_new, first_new, second_new)


MESH = pl.DeviceIdType.MESH
ANY = pl.BlockSpec(memory_space=pl.ANY)
MIB = 1 << 20


def chip_pairs():
    return lax.axis_size("dp") == 16 and lax.axis_size("tensor") == 2


def pair_rank():
    if chip_pairs():
        return (lax.axis_index("dp") // 4) % 2
    return lax.axis_index("tensor")


def pair_swap(value):
    if chip_pairs():
        return lax.ppermute(value, "dp", [(i, i ^ 4) for i in range(16)])
    return lax.ppermute(value, "tensor", [(0, 1), (1, 0)])


def pair_sums(*values):
    stacked = jnp.concatenate([v.reshape(-1) for v in values])
    total = stacked + pair_swap(stacked)
    out, at = [], 0
    for v in values:
        out.append(total[at : at + v.size].reshape(v.shape))
        at += v.size
    return tuple(out)


def place_of():
    chip, core = lax.axis_index("dp"), lax.axis_index("tensor")
    z, y, x = chip // 4, (chip // 2) % 2, chip % 2
    return chip, core, z, y, x


def column_of(z, y, x, k):
    high, low_bit = z // 2, z % 2
    if k & 2:
        high = 1 - high
    if k & 1:
        low_bit = 1 - low_bit
    return (2 * high + low_bit) * 4 + 2 * y + x


def greet(chip, core, z, y, x):
    barrier = pltpu.get_barrier_semaphore()
    friends = []
    for k in range(4):
        for flip in (0, 1):
            if k or flip:
                friends.append((column_of(z, y, x, k), core if flip == 0 else 1 - core))
    friends.append((column_of(z, y, 1 - x, 0), core))
    friends.append((column_of(z, 1 - y, x, 0), core))
    for friend in friends:
        pl.semaphore_signal(barrier, inc=1, device_id=friend, device_id_type=MESH)
    pl.semaphore_wait(barrier, len(friends))


def gather_kernel(
    own, lat, cot, text, small, out, lats, cots, texts, smalls, clip_s, clip_r,
    near_s, col_r, x_s, x_r, y_s, y_r, sib_s, sib_r,
):
    chip, core, z, y, x = place_of()
    rank = z % 2
    half = own.shape[1] // 2
    part = half // 2
    at_x = column_of(z, y, 1 - x, 0)
    at_y = column_of(z, 1 - y, x, 0)
    greet(chip, core, z, y, x)

    batch = max(n for n in (1, 2, 3) if own.shape[0] % n == 0)
    batches = own.shape[0] // batch
    turns = 4 * batches

    def case(s):
        late = jnp.maximum(s - batches, 0)
        k = jnp.where(s < batches, 0, 1 + late % 3)
        return k, jnp.where(s < batches, s, late // 3)

    def remote(unit, g, first, count, send, recv, device):
        piece = out.at[
            unit, pl.ds(g * batch, batch), pl.ds(pl.multiple_of(first, 16), count), :
        ]
        return pltpu.make_async_remote_copy(
            src_ref=piece, dst_ref=piece, send_sem=send, recv_sem=recv,
            device_id=device, device_id_type=MESH,
        )

    def own_copy(g, j, h):
        target = (toggled(z, y, x, 0, 0, 2 * j) // 8 * 8) + core * 4 + 2 * y + x
        part_of = (pl.ds(g * batch, batch), pl.ds(h * half, half))
        src = own.at[part_of[0], part_of[1], :]
        dst = out.at[chip, part_of[0], part_of[1], :]
        recv = col_r.at[z * batches + g]
        go = pltpu.make_async_remote_copy(
            src_ref=src, dst_ref=dst, send_sem=near_s.at[(2 * j + h) * batches + g],
            recv_sem=recv, device_id=(target, h), device_id_type=MESH,
        )
        return go, pltpu.make_async_copy(src, dst, recv)

    for g in range(batches):
        for j in range(2):
            for h in range(2):
                go, here = own_copy(g, j, h)
                if j == 1:
                    go.start()
                    continue
                stays = jnp.logical_and(rank == core, core == h)

                @pl.when(stays)
                def _():
                    here.start()

                @pl.when(jnp.logical_not(stays))
                def _():
                    go.start()

    pair_chip = column_of(z, y, x, 1)
    rows_of_text = text.shape[0] // 2

    def clip_pieces(h):
        share = pl.ds(h * rows_of_text, rows_of_text)
        return ((lat, lats.at[h]), (cot, cots.at[h]), (text.at[share], texts.at[share]))

    home = rank == core
    trade = pltpu.make_async_remote_copy(
        src_ref=small, dst_ref=smalls, send_sem=clip_s.at[6], recv_sem=clip_r.at[6],
        device_id=(pair_chip, 1 - core), device_id_type=MESH,
    )
    keep = pltpu.make_async_copy(small, smalls, clip_r.at[6])

    @pl.when(home)
    def _():
        keep.start()

    @pl.when(jnp.logical_not(home))
    def _():
        trade.start()

    def hand_out(h, n, wait):
        src, dst = clip_pieces(h)[n]
        far = pltpu.make_async_remote_copy(
            src_ref=src, dst_ref=dst, send_sem=clip_s.at[n], recv_sem=clip_r.at[3 * h + n],
            device_id=(pair_chip, rank), device_id_type=MESH,
        )
        near = pltpu.make_async_remote_copy(
            src_ref=src, dst_ref=dst, send_sem=clip_s.at[3 + n], recv_sem=clip_r.at[3 * h + n],
            device_id=(chip, 1 - core), device_id_type=MESH,
        )
        here = pltpu.make_async_copy(src, dst, clip_r.at[3 * h + n])

        @pl.when(core == h)
        def _():
            if wait:
                far.wait_send()
            else:
                far.start()

            @pl.when(home)
            def _():
                if not wait:
                    here.start()

            @pl.when(jnp.logical_not(home))
            def _():
                if wait:
                    near.wait_send()
                else:
                    near.start()

    for n in range(3):
        for h in range(2):
            hand_out(h, n, False)

    mine, other = core * half, (1 - core) * half
    sibling = (chip, 1 - core)

    def to_x(s, n):
        k, g = case(s)
        i = turns * n + s
        unit = toggled(z, y, x, n, 0, k)
        return remote(unit, g, mine, part if n else half, x_s.at[i], x_r.at[i], (at_x, core))

    def from_x(s, n):
        k, g = case(s)
        i = turns * n + s
        unit = toggled(z, y, x, n, 1, k)
        return remote(unit, g, mine, part if n else half, x_s.at[i], x_r.at[i], (at_x, core))

    def to_y(s, n):
        k, g = case(s)
        i = turns * n + s
        unit = toggled(z, y, x, 0, n, k)
        first, count = (mine + part, part) if n else (mine, half)
        return remote(unit, g, first, count, y_s.at[i], y_r.at[i], (at_y, core))

    def from_y(s, n):
        k, g = case(s)
        i = turns * n + s
        unit = toggled(z, y, x, 1, n, k)
        first, count = (mine + part, part) if n else (mine, half)
        return remote(unit, g, first, count, y_s.at[i], y_r.at[i], (at_y, core))

    def to_sib(s, n, away=False):
        k, g = case(s)
        i = turns * n + s
        unit = toggled(z, y, x, int(n in (2, 3, 4)), int(n in (1, 3, 4)), k)
        first = (other if away else mine) + (part if n == 4 else 0)
        return remote(
            unit, g, first, part if n >= 3 else half, sib_s.at[i], sib_r.at[i], sibling
        )

    def column_in(s):
        k, g = case(s)
        unit = toggled(z, y, x, 0, 0, k)
        piece = out.at[
            unit, pl.ds(g * batch, batch), pl.ds(pl.multiple_of(mine, 16), half), :
        ]
        pltpu.make_async_copy(piece, piece, col_r.at[unit // 4 * batches + g]).wait()
        to_x(s, 0).start()
        to_y(s, 0).start()
        to_sib(s, 0).start()

    def side_in(s):
        from_x(s, 0).wait_recv()
        to_y(s, 1).start()
        to_sib(s, 1).start()
        from_y(s, 0).wait_recv()
        to_x(s, 1).start()
        to_sib(s, 2).start()

    def corner_in(s):
        from_x(s, 1).wait_recv()
        to_sib(s, 3).start()
        from_y(s, 1).wait_recv()
        to_sib(s, 4).start()

    def turn(step, carry):
        @pl.when(step < turns)
        def _():
            column_in(step)

        @pl.when(jnp.logical_and(step >= 1, step < turns + 1))
        def _():
            side_in(step - 1)

        @pl.when(step >= 2)
        def _():
            corner_in(step - 2)

        return carry

    lax.fori_loop(0, turns + 2, turn, 0)

    def settle(s, carry):
        for n in range(2):
            to_x(s, n).wait_send()
            to_y(s, n).wait_send()
        for n in range(5):
            to_sib(s, n).wait_send()
            to_sib(s, n, True).wait_recv()
        return carry

    lax.fori_loop(0, turns, settle, 0)
    for g in range(batches):
        for j in range(2):
            for h in range(2):
                go, _ = own_copy(g, j, h)
                if j == 1:
                    go.wait_send()
                    continue

                @pl.when(jnp.logical_not(jnp.logical_and(rank == core, core == h)))
                def _():
                    go.wait_send()

    for n in range(3):
        for h in range(2):
            hand_out(h, n, True)
            dst = clip_pieces(h)[n][1]
            pltpu.make_async_copy(dst, dst, clip_r.at[3 * h + n]).wait()

    @pl.when(jnp.logical_not(home))
    def _():
        trade.wait_send()

    pltpu.make_async_copy(smalls, smalls, clip_r.at[6]).wait()


def gather_slots(scaled, lat, cot, text, small):
    if not chip_pairs():
        everyone = lax.all_gather(scaled, "dp", axis=0, tiled=True)
        lats, cots = (lax.all_gather(v, "tensor") for v in (lat, cot))
        return everyone, lats, cots, text, small
    dma = pltpu.SemaphoreType.DMA
    turns = 4 * scaled.shape[0] // max(n for n in (1, 2, 3) if scaled.shape[0] % n == 0)
    counts = (7, 7, turns, turns) + (2 * turns,) * 4 + (5 * turns,) * 2
    everyone, *rest = pl.pallas_call(
        gather_kernel,
        out_shape=[
            jax.ShapeDtypeStruct((16,) + scaled.shape, scaled.dtype),
            jax.ShapeDtypeStruct((2,) + lat.shape, lat.dtype),
            jax.ShapeDtypeStruct((2,) + cot.shape, cot.dtype),
            jax.ShapeDtypeStruct(text.shape, text.dtype),
            jax.ShapeDtypeStruct(small.shape, small.dtype),
        ],
        in_specs=[ANY] * 5,
        out_specs=[ANY] * 5,
        scratch_shapes=[dma((n,)) for n in counts],
        compiler_params=pltpu.CompilerParams(
            collective_id=0, has_side_effects=True, vmem_limit_bytes=4 * MIB
        ),
    )(scaled, lat, cot, text, small)
    return everyone.reshape((-1,) + scaled.shape[1:]), *rest


def toggled(z, y, x, flip_y, flip_x, k):
    high = (z // 2 + k // 2) % 2
    low_bit = (z % 2 + k % 2) % 2
    return (2 * high + low_bit) * 4 + 2 * ((y + flip_y) % 2) + (x + flip_x) % 2


def reduce_kernel(
    kind, block, *refs,
):
    (
        *pieces, rows_in, after_in, dx_in, y_in, da_in, gains, vec_in,
        final, vec_out, result, result_grad, y_other, da_other, from_sib, from_x, from_y, corner_a, corner_b,
        left, right, ring, corners, side_x, side_y, middle, stage, vec_box, end_wide, end_low,
        load_s, stage_s, sib_s, sib_r, x_s, x_r, y_s, y_r, ca_s, ca_r, cb_s, cb_r, f_s, f_r, v_s, v_r,
        end_s, end_r, end_load,
    ) = refs
    chip, core, z, y, x = place_of()
    rank = z % 2
    slots, width, lanes = final.shape[1:]
    half = width // 2
    part = half // 2
    at_x = toggled(z, y, x, 0, 1, 0)
    at_y = toggled(z, y, x, 1, 0, 0)
    sibling = (chip, 1 - core)
    mates = (
        sibling,
        (at_x, core),
        (at_y, core),
        (toggled(z, y, x, 0, 0, 1), core),
        (toggled(z, y, x, 0, 0, 2), core),
    )

    kinds = left.shape[0]
    depth = right.shape[1]
    loads = []
    for i in range(kinds):
        columns = pieces[i].shape[1]
        loads.append(
            pltpu.make_async_copy(pieces[i], left.at[i, :, pl.ds(0, columns)], load_s.at[i])
        )
    first = 0
    blank = []
    for i, piece in enumerate(pieces[kinds:]):
        number, rows = piece.shape[:2]
        loads.append(
            pltpu.make_async_copy(
                piece, right.at[pl.ds(first, number), pl.ds(0, rows), :], load_s.at[kinds + i]
            )
        )
        if rows < depth:
            blank.append((first, number, rows))
        first += number
    for load in loads:
        load.start()
    for start, number, rows in blank:

        def clear(i, carry):
            right[start + i, pl.ds(rows, depth - rows), :] = jnp.zeros(
                (depth - rows, lanes), right.dtype
            )
            return carry

        lax.fori_loop(0, number, clear, 0)
    right[first] = jnp.zeros((depth, lanes), right.dtype)
    for i in range(kinds):
        columns = pieces[i].shape[1]
        if columns < depth:
            left[i, :, pl.ds(columns, depth - columns)] = jnp.zeros(
                (width, depth - columns), left.dtype
            )
    vec_out[...] = vec_in[...]
    greet(chip, core, z, y, x)
    for load in loads:
        load.wait()

    def remote(src, dst, send, recv, device):
        return pltpu.make_async_remote_copy(
            src_ref=src, dst_ref=dst, send_sem=send, recv_sem=recv,
            device_id=device, device_id_type=MESH,
        )

    batch = ring.shape[1]
    batches = slots // batch
    turns = 4 * batches
    deep = corners.shape[0]

    def flips(s):
        return 3 - s // batches

    def sums(q, s, first, terms, total):
        unit = toggled(z, y, x, 1 - q % 2, 1 - q // 2, flips(s))
        base = unit * slots + (s % batches) * batch
        count = total.shape[1]

        def one(i, carry):
            slot = base + i
            rows = pl.ds(pl.multiple_of(first, 128), count)
            acc = jnp.dot(
                left[kind[slot], rows, :], right[block[slot]], preferred_element_type=jnp.float32
            )
            for term in terms:
                acc = acc + term[i].astype(jnp.float32)
            total[i] = acc.astype(total.dtype)
            return carry

        lax.fori_loop(0, batch, one, 0)

    mine, other = core * half, (1 - core) * half

    def sub(ref, first):
        return ref.at[:, pl.ds(first, part), :]

    def sib_copy(q, s):
        i = turns * q + s
        return remote(ring.at[q], from_sib.at[i], sib_s.at[i], sib_r.at[i], sibling)

    def a_copy(s):
        return remote(
            sub(corners.at[s % deep], 0), corner_a.at[s], ca_s.at[s], ca_r.at[s], (at_x, core)
        )

    def b_copy(s):
        return remote(
            sub(corners.at[s % deep], part), corner_b.at[s], cb_s.at[s], cb_r.at[s], (at_y, core)
        )

    def x_copy(s, n):
        rows = pl.ds(n * part, part)
        i = turns * n + s
        return remote(
            side_x.at[s % deep, :, rows, :], from_x.at[s, :, rows, :], x_s.at[i], x_r.at[i],
            (at_x, core),
        )

    def y_copy(s, n):
        rows = pl.ds((1 - n) * part, part)
        i = turns * n + s
        return remote(
            side_y.at[s % deep, :, rows, :], from_y.at[s, :, rows, :], y_s.at[i], y_r.at[i],
            (at_y, core),
        )

    def f_copy(s):
        src = middle.at[s % deep]
        g = s % batches
        dst = final.at[
            z // 2, pl.ds(g * batch, batch), pl.ds(pl.multiple_of(mine, 128), half), :
        ]
        recv = f_r.at[(2 * (z // 2) + core) * batches + g]
        target = (toggled(z, y, x, 0, 0, flips(s)), rank)
        return remote(src, dst, f_s.at[s], recv, target), pltpu.make_async_copy(src, dst, recv)

    def stays(s):
        return jnp.logical_and(s >= turns - batches, rank == core)

    def for_sibling(s, low, high):
        def one(q, carry):
            @pl.when(s >= 1)
            def _():
                sib_copy(q, s - 1).wait_send()

            sums(q, s, other, (), ring.at[q])
            sib_copy(q, s).start()
            return carry

        lax.fori_loop(low, high, one, 0)

    def fetched(q, s):
        i = 2 * q + s % 2
        return pltpu.make_async_copy(from_sib.at[turns * q + s], stage.at[i], stage_s.at[i])

    def fetch(q, s):
        sib_copy(q, s).wait_recv()
        fetched(q, s).start()

    def taken(q, s):
        return stage.at[2 * q + s % 2]

    def corner(s):
        @pl.when(s >= deep)
        def _():
            a_copy(s - deep).wait_send()
            b_copy(s - deep).wait_send()

        fetched(0, s).wait()
        sums(0, s, mine, (taken(0, s),), corners.at[s % deep])
        a_copy(s).start()
        b_copy(s).start()

    def direct_sides(s):
        @pl.when(s >= deep)
        def _():
            for n in range(2):
                x_copy(s - deep, n).wait_send()
                y_copy(s - deep, n).wait_send()

        fetched(1, s).wait()
        sums(1, s, mine, (sub(taken(1, s), 0),), sub(side_x.at[s % deep], 0))
        x_copy(s, 0).start()
        fetched(2, s).wait()
        sums(2, s, mine + part, (sub(taken(2, s), part),), sub(side_y.at[s % deep], part))
        y_copy(s, 0).start()

    def relayed(s):
        return (
            pltpu.make_async_copy(corner_b.at[s], sub(stage.at[8], 0), stage_s.at[8]),
            pltpu.make_async_copy(corner_a.at[s], sub(stage.at[8], part), stage_s.at[9]),
        )

    def relayed_in(s):
        b_copy(s).wait_recv()
        relayed(s)[0].start()
        a_copy(s).wait_recv()
        relayed(s)[1].start()

    def relayed_sides(s):
        relayed(s)[0].wait()
        sums(
            1, s, mine + part, (sub(taken(1, s), part), sub(stage.at[8], 0)),
            sub(side_x.at[s % deep], part),
        )
        x_copy(s, 1).start()
        relayed(s)[1].wait()
        sums(
            2, s, mine, (sub(taken(2, s), 0), sub(stage.at[8], part)), sub(side_y.at[s % deep], 0)
        )
        y_copy(s, 1).start()

    def centre_terms(s):
        return (
            pltpu.make_async_copy(from_x.at[s], stage.at[9], stage_s.at[10]),
            pltpu.make_async_copy(from_y.at[s], stage.at[10], stage_s.at[11]),
        )

    def centre_in(s):
        for n, copies in enumerate((x_copy, y_copy)):
            copies(s, 0).wait_recv()
            copies(s, 1).wait_recv()
            centre_terms(s)[n].start()

    def centre(s):
        @pl.when(s >= deep)
        def _():
            f_copy(s - deep)[0].wait_send()

        fetched(3, s).wait()
        for term in centre_terms(s):
            term.wait()
        sums(3, s, mine, (taken(3, s), stage.at[9], stage.at[10]), middle.at[s % deep])
        go, here = f_copy(s)

        @pl.when(stays(s))
        def _():
            here.start()

        @pl.when(jnp.logical_not(stays(s)))
        def _():
            go.start()

    home = rank == core
    pair_device = (toggled(z, y, x, 0, 0, 1), core)
    ends = [
        remote(y_in, y_other, end_s.at[0], end_r.at[0], pair_device),
        remote(da_in, da_other, end_s.at[1], end_r.at[1], pair_device),
        remote(end_low.at[0], result, end_s.at[2], end_r.at[2], sibling),
        remote(end_wide.at[0], result_grad, end_s.at[3], end_r.at[3], sibling),
    ]
    end_loads = [
        pltpu.make_async_copy(src, dst, end_load.at[i])
        for i, (src, dst) in enumerate(
            (
                (rows_in, end_wide.at[0]), (after_in, end_wide.at[1]), (dx_in, end_wide.at[2]),
                (y_in, end_low.at[0]), (da_in, end_low.at[1]),
                (y_other, end_low.at[2]), (da_other, end_low.at[3]),
            )
        )
    ]
    end_stores = [
        pltpu.make_async_copy(end_low.at[0], result, end_load.at[7]),
        pltpu.make_async_copy(end_wide.at[0], result_grad, end_load.at[8]),
    ]

    def finish_rows():
        for n in range(2):
            ends[n].wait_recv()
            end_loads[5 + n].start()
        for load in end_loads:
            load.wait()
        tall = 16

        def one(i, carry):
            at = pl.ds(pl.multiple_of(i * tall, tall), tall)
            y_all = end_low[0, at].astype(F32) + end_low[2, at].astype(F32) + gains[2:3]
            end_low[0, at] = (end_wide[1, at] + gains[0:1] * y_all).astype(end_low.dtype)
            da = end_low[1, at].astype(F32) + end_low[3, at].astype(F32)
            back, _ = normed_back(end_wide[0, at], da * (1.0 + gains[1:2]))
            end_wide[0, at] = end_wide[2, at] + back
            return carry

        lax.fori_loop(0, rows_in.shape[0] // tall, one, 0)
        ends[2].start()
        ends[3].start()
        for store in end_stores:
            store.start()

    @pl.when(jnp.logical_not(home))
    def _():
        ends[0].start()
        ends[1].start()

    def vec_copy(i):
        return remote(vec_out, vec_box.at[i], v_s.at[i], v_r.at[i], mates[i])

    def turn(step, carry):
        for i in range(5):

            @pl.when(step == 2 * i)
            def _():
                vec_copy(i).start()

        @pl.when(step + 1 < turns)
        def _():
            corner(step + 1)
            direct_sides(step + 1)

        @pl.when(step + 2 < turns)
        def _():
            for_sibling(step + 2, 0, 4)

        @pl.when(step < turns)
        def _():
            relayed_in(step)

        @pl.when(step >= 1)
        def _():
            centre_in(step - 1)

        @pl.when(step < turns)
        def _():
            relayed_sides(step)

        @pl.when(step >= 1)
        def _():
            centre(step - 1)

        @pl.when(step + 2 < turns)
        def _():
            for q in range(3):
                fetch(q, step + 2)

        @pl.when(step + 1 < turns)
        def _():
            fetch(3, step + 1)

        @pl.when(jnp.logical_and(step == 1, home))
        def _():
            for load in end_loads[:5]:
                load.start()

        @pl.when(jnp.logical_and(step == 3, home))
        def _():
            finish_rows()

        for i in range(5):

            @pl.when(step == 2 * i + 1)
            def _():
                vec_copy(i).wait()
                vec_out[...] = vec_out[...] + vec_box[i]

        return carry

    for_sibling(0, 0, 2)
    fetch(0, 0)
    corner(0)
    for_sibling(0, 2, 4)
    for q in range(1, 4):
        fetch(q, 0)
    direct_sides(0)
    for_sibling(1, 0, 4)
    for q in range(3):
        fetch(q, 1)
    lax.fori_loop(0, turns + 1, turn, 0)
    for q in range(4):
        sib_copy(q, turns - 1).wait_send()

    def settle(i, carry):
        s = turns - deep + i
        a_copy(s).wait_send()
        b_copy(s).wait_send()
        for n in range(2):
            x_copy(s, n).wait_send()
            y_copy(s, n).wait_send()

        @pl.when(jnp.logical_not(stays(s)))
        def _():
            f_copy(s)[0].wait_send()

        return carry

    lax.fori_loop(0, deep, settle, 0)

    @pl.when(home)
    def _():
        ends[2].wait_send()
        ends[3].wait_send()
        for store in end_stores:
            store.wait()

    @pl.when(jnp.logical_not(home))
    def _():
        ends[0].wait_send()
        ends[1].wait_send()
        ends[2].wait_recv()
        ends[3].wait_recv()

    for plane in range(2):
        for h in range(2):
            for g in range(batches):
                piece = final.at[plane, pl.ds(g * batch, batch), pl.ds(h * half, half), :]
                recv = f_r.at[(2 * plane + h) * batches + g]
                pltpu.make_async_copy(piece, piece, recv).wait()


def reduce_slots(holder, kinds, rows, columns, vector, ends, gains, slot_count):
    if not chip_pairs():
        grads = slot_grads(holder, kinds, [r.T for r in rows], columns)
        total = lax.psum_scatter(grads, "dp", scatter_dimension=0, tiled=True)
        x, after, dx, y_part, da_part = ends
        y_all, da_all = (
            v.astype(F32) + pair_swap(v).astype(F32) for v in (y_part, da_part)
        )
        result = (after + gains[0] * (y_all + gains[2])).astype(BF16)
        back, _ = normed_back(x, da_all * (1.0 + gains[1]))
        return total[None], lax.psum(vector, ("dp", "tensor")), result, dx + back
    left = rows
    width, depth = left[0].shape[0], max(r.shape[1] for r in rows)
    lanes = columns[0].shape[2]
    tiles = sum(c.shape[0] for c in columns)
    block = jnp.where(holder >= 0, holder, tiles)
    kind = kinds[jnp.maximum(holder, 0)]
    half = width // 2
    dma = pltpu.SemaphoreType.DMA
    scalars = pl.BlockSpec(memory_space=pltpu.SMEM)
    inside = pl.BlockSpec(memory_space=pltpu.VMEM)
    low = jnp.bfloat16

    batch = max(n for n in (1, 2, 3) if slot_count % n == 0)
    turns = 4 * slot_count // batch
    deep = 3

    def room(count, tall):
        return jax.ShapeDtypeStruct((count, batch, tall, lanes), low)

    def slab(count):
        return pltpu.VMEM((count, batch, half, lanes), low)

    outs = pl.pallas_call(
        reduce_kernel,
        out_shape=[
            jax.ShapeDtypeStruct((2, slot_count, width, lanes), low),
            jax.ShapeDtypeStruct(vector.shape, vector.dtype),
            jax.ShapeDtypeStruct(ends[0].shape, low), jax.ShapeDtypeStruct(ends[0].shape, F32),
            jax.ShapeDtypeStruct(ends[0].shape, low), jax.ShapeDtypeStruct(ends[0].shape, low),
            room(4 * turns, half), room(turns, half), room(turns, half),
            room(turns, half // 2), room(turns, half // 2),
        ],
        in_specs=[scalars, scalars] + [ANY] * (len(left) + len(columns) + 5) + [inside] * 2,
        out_specs=[ANY, inside] + [ANY] * 9,
        scratch_shapes=[
            pltpu.VMEM((len(left), width, depth), low),
            pltpu.VMEM((tiles + 1, depth, lanes), low),
            slab(4), slab(deep), slab(deep), slab(deep), slab(deep), slab(11),
            pltpu.VMEM((5,) + vector.shape, vector.dtype),
            pltpu.VMEM((3,) + ends[0].shape, F32),
            pltpu.VMEM((4,) + ends[0].shape, low),
        ]
        + [
            dma((n,))
            for n in (len(left) + len(columns), 12)
            + (4 * turns,) * 2
            + (2 * turns,) * 4
            + (turns,) * 6
            + (5, 5, 4, 4, 9)
        ],
        compiler_params=pltpu.CompilerParams(
            collective_id=1, has_side_effects=True, vmem_limit_bytes=58 * MIB
        ),
    )(kind, block, *left, *columns, *ends, gains, vector)
    return outs[:4]


def kind_of_blocks(tile_count, heads_here, blocks_here):
    number = jnp.arange(tile_count)
    kind = number // heads_here
    table = jnp.array([0, 0, 0, 1, 2, 3, 3, 4], jnp.int32)
    late = jnp.where(number < 8 * heads_here + blocks_here, 5, 6)
    return jnp.where(number < 8 * heads_here, table[jnp.minimum(kind, 7)], late).astype(jnp.int32)


def slot_grads(holder, kinds, rows, columns):
    depth = max(r.shape[0] for r in rows)

    def deep(value, axis):
        room = [(0, 0)] * value.ndim
        room[axis] = (0, depth - value.shape[axis])
        return jnp.pad(value, room)

    left = jnp.stack([deep(r, 0) for r in rows])
    right = jnp.concatenate([deep(c, 1) for c in columns], 0)
    slots = holder.shape[0]
    used = (holder >= 0).astype(jnp.int32)
    block = jnp.maximum(holder, 0)
    kind = kinds[block]
    width = rows[0].shape[1]
    lanes = right.shape[2]

    def multiply(kind_ref, block_ref, used_ref, left_ref, right_ref, out_ref):
        slot = pl.program_id(0)

        @pl.when(used_ref[slot] == 1)
        def _():
            out_ref[0] = lax.dot_general(
                left_ref[kind_ref[slot]],
                right_ref[0],
                (((0,), (0,)), ((), ())),
                preferred_element_type=jnp.float32,
            ).astype(out_ref.dtype)

        @pl.when(used_ref[slot] == 0)
        def _():
            out_ref[...] = jnp.zeros_like(out_ref)

    return pl.pallas_call(
        multiply,
        grid_spec=pltpu.PrefetchScalarGridSpec(
            num_scalar_prefetch=3,
            grid=(slots,),
            in_specs=[
                pl.BlockSpec(left.shape, lambda s, kd, b, u: (0, 0, 0)),
                pl.BlockSpec((1, depth, lanes), lambda s, kd, b, u: (b[s], 0, 0)),
            ],
            out_specs=pl.BlockSpec((1, width, lanes), lambda s, kd, b, u: (s, 0, 0)),
        ),
        out_shape=jax.ShapeDtypeStruct((slots, width, lanes), jnp.bfloat16),
        compiler_params=pltpu.CompilerParams(vmem_limit_bytes=48 * MIB),
    )(kind, block, used, left, right)


def adam_slots(planes, master, moment_one, moment_two, slot_scale, filled):
    count, slot_count, width, lanes = planes.shape

    def step(scale_ref, fill_ref, grads, weight, one, two, new_weight, new_one, new_two, grad_box, boxes, reads, writes):
        sources = (weight, one, two)
        targets = (new_weight, new_one, new_two)

        def load(slot):
            return [
                pltpu.make_async_copy(src.at[0, slot], boxes.at[n, slot], reads.at[n, slot])
                for n, src in enumerate(sources)
            ] + [
                pltpu.make_async_copy(
                    grads.at[n, slot], grad_box.at[n, slot], reads.at[3 + n, slot]
                )
                for n in range(count)
            ]

        def store(slot):
            return [
                pltpu.make_async_copy(boxes.at[n, slot], dst.at[0, slot], writes.at[n, slot])
                for n, dst in enumerate(targets)
            ]

        def begin(slot, carry):
            for copy in load(slot):
                copy.start()
            return carry

        def work(slot, carry):
            for copy in load(slot):
                copy.wait()

            @pl.when(fill_ref[slot] == 1)
            def _():
                total = grad_box[0, slot].astype(jnp.float32)
                for n in range(1, count):
                    total = total + grad_box[n, slot].astype(jnp.float32)
                results = adam_step(
                    boxes[0, slot], total * scale_ref[slot], boxes[1, slot], boxes[2, slot],
                    TILE_RATE, TILE_DECAY,
                )
                for n, value in enumerate(results):
                    boxes[n, slot] = value

            for copy in store(slot):
                copy.start()
            return carry

        def finish(slot, carry):
            for copy in store(slot):
                copy.wait()
            return carry

        for part in (begin, work, finish):
            lax.fori_loop(0, slot_count, part, 0)

    scalars = pl.BlockSpec(memory_space=pltpu.SMEM)
    return pl.pallas_call(
        step,
        in_specs=[scalars, scalars] + [ANY] * 4,
        out_specs=[ANY] * 3,
        out_shape=[pltpu.HBM(master.shape, jnp.float32)] * 3,
        scratch_shapes=[
            pltpu.VMEM((count, slot_count, width, lanes), planes.dtype),
            pltpu.VMEM((3, slot_count, width, lanes), jnp.float32),
            pltpu.SemaphoreType.DMA((3 + count, slot_count)),
            pltpu.SemaphoreType.DMA((3, slot_count)),
        ],
        compiler_params=pltpu.CompilerParams(vmem_limit_bytes=40 * MIB),
    )(
        slot_scale,
        filled.astype(jnp.int32),
        *[
            pltpu.with_memory_space_constraint(v, pltpu.HBM)
            for v in (planes, master, moment_one, moment_two)
        ],
    )


SCALING = HEAD ** (-0.5)
BF16 = jnp.bfloat16
F32 = jnp.float32


def nn(left, right):
    return jnp.dot(left, right, preferred_element_type=F32)


def nt(left, right):
    return lax.dot_general(left, right, (((1,), (1,)), ((), ())), preferred_element_type=F32)


def tn(left, right):
    return lax.dot_general(left, right, (((0,), (0,)), ((), ())), preferred_element_type=F32)


def normed(rows):
    centre = rows - jnp.mean(rows, -1, keepdims=True)
    inverse = lax.rsqrt(jnp.mean(centre * centre, -1, keepdims=True) + NORM_EPS)
    return centre * inverse, inverse


def normed_back(rows, grad):
    unit, inverse = normed(rows)
    mean = jnp.mean(grad, -1, keepdims=True)
    return (grad - mean - unit * jnp.mean(grad * unit, -1, keepdims=True)) * inverse, unit


def total_of(rows):
    return jnp.sum(rows, 0, keepdims=True)


def turned(rows, cos_tab, sin_tab):
    even = lax.broadcasted_iota(jnp.int32, rows.shape, 1) % 2 == 0
    partner = jnp.where(even, pltpu.roll(rows, HEAD - 1, 1), pltpu.roll(rows, 1, 1))
    return rows * cos_tab + partner * sin_tab


def wide(column):
    return jnp.broadcast_to(column, (column.shape[0], HEAD))


def pack_sums(for_rows, for_text=None):
    out = wide(for_rows)
    if for_text is None:
        return out
    lane = lax.broadcasted_iota(jnp.int32, out.shape, 1)
    count = for_text.shape[0] // 2
    rest = jnp.zeros((out.shape[0] - count, HEAD), F32)
    first = jnp.concatenate([wide(for_text[:count]), rest], 0)
    second = jnp.concatenate([wide(for_text[count:]), rest], 0)
    return jnp.where(lane < 32, out, jnp.where(lane < 64, first, second))


def unpack_text(sums, count):
    return jnp.concatenate([sums[: count // 2, 32:33], sums[: count // 2, 64:65]], 0)


def softmax(scores):
    expo = jnp.exp(scores - jnp.max(scores, -1, keepdims=True))
    return expo / jnp.sum(expo, -1, keepdims=True)


def self_scores(query_low, key_low, tokens):
    scores = nt(query_low, key_low) * SCALING
    lane = lax.broadcasted_iota(jnp.int32, scores.shape, 1)
    return jnp.where(lane < tokens, scores, -1e30)


def whole(array):
    zeros = (0,) * len(array.shape)
    return pl.BlockSpec(array.shape, lambda *_: zeros)


def block_at(first, stride=1):
    return pl.BlockSpec((1, D, HEAD), lambda i, where: (where[first + stride * i], 0, 0))


def call(body, places, grid, ins, outs, scratch=(), vmem=24):
    specs = [spec if spec is not None else whole(array) for array, spec in ins]
    shapes = [pltpu.HBM(shape, kind) for shape, kind, _ in outs]
    out_specs = [
        spec if spec is not None else whole(shape) for (_, _, spec), shape in zip(outs, shapes)
    ]
    return pl.pallas_call(
        body,
        grid_spec=pltpu.PrefetchScalarGridSpec(
            num_scalar_prefetch=1,
            grid=(grid,),
            in_specs=specs,
            out_specs=out_specs,
            scratch_shapes=list(scratch),
        ),
        out_shape=shapes,
        compiler_params=pltpu.CompilerParams(vmem_limit_bytes=vmem * MIB),
    )(places, *[pltpu.with_memory_space_constraint(array, pltpu.HBM) for array, _ in ins])


def head_lanes(rows, per=1):
    return pl.BlockSpec((rows, per * HEAD), lambda h, *_: (0, h))


def heads_per_step(heads, most):
    return max(n for n in (1, 2, 3, 6) if heads % n == 0 and n <= most)


def lane_group(ref, j):
    return ref[:, j * HEAD : (j + 1) * HEAD]


def joined(refs):
    return jnp.concatenate([ref[0] for ref in refs], 1)


def project_self(places, everyone, rows, mod, vecs, heads):
    count = rows.shape[0]
    span = heads * HEAD

    def body(_, rows_ref, mod_ref, vec_ref, *refs):
        weights, (low, pre, value, sums, acc) = refs[:heads], refs[heads:]
        i = pl.program_id(0)

        @pl.when(i == 0)
        def _():
            unit, _ = normed(rows_ref[...])
            low[...] = (unit * (1.0 + mod_ref[1:2]) + mod_ref[0:1]).astype(BF16)

        made = nn(low[...], joined(weights))

        @pl.when(i == 0)
        def _():
            q = made + vec_ref[0:1]
            pre[0] = q
            acc[...] = wide(jnp.sum(q * q, -1, keepdims=True))

        @pl.when(i == 1)
        def _():
            k = made + vec_ref[1:2]
            pre[0] = k
            lane = lax.broadcasted_iota(jnp.int32, acc.shape, 1)
            sums[...] = jnp.where(lane < 64, acc[...], wide(jnp.sum(k * k, -1, keepdims=True)))

        @pl.when(i == 2)
        def _():
            value[...] = (made + vec_ref[2:3]).astype(BF16)

    return call(
        body, places, 3,
        [(rows, None), (mod, None), (vecs, None)]
        + [(everyone, block_at(h, heads)) for h in range(heads)],
        [
            ((count, D), BF16, None),
            ((2, count, span), F32, pl.BlockSpec((1, count, span), lambda i, _: (jnp.minimum(i, 1), 0, 0))),
            ((count, span), BF16, None),
            ((count, HEAD), F32, None),
        ],
        [pltpu.VMEM((count, HEAD), F32)],
    )


def attend_self(places, everyone, pre, value, sums, other, vecs, cos_tab, sin_tab, heads, tokens):
    count = value.shape[0]
    per = heads_per_step(heads, 2)
    steps = heads // per

    def body(_, pre_ref, value_ref, sum_ref, other_ref, vec_ref, cos_ref, sin_ref, *refs):
        weights, (q_ref, k_ref, o_ref, y_ref, acc) = refs[:per], refs[per:]
        h = pl.program_id(0)
        total = sum_ref[...] + other_ref[...]
        q_inv = lax.rsqrt(total[:, 0:1] / D + NORM_EPS)
        k_inv = lax.rsqrt(total[:, 64:65] / D + NORM_EPS)
        cos, sin = cos_ref[...], sin_ref[...]
        outs = []
        for j in range(per):
            lanes = slice(j * HEAD, (j + 1) * HEAD)
            q = turned(pre_ref[0, :, lanes] * q_inv * vec_ref[3:4, lanes], cos, sin).astype(BF16)
            k = turned(pre_ref[1, :, lanes] * k_inv * vec_ref[4:5, lanes], cos, sin).astype(BF16)
            q_ref[:, lanes] = q
            k_ref[:, lanes] = k
            chance = softmax(self_scores(q, k, tokens))
            out = nn(chance.astype(BF16), value_ref[:, lanes]).astype(BF16)
            o_ref[j] = out
            outs.append(out)
        part = nt(jnp.concatenate(outs, 1), joined(weights))

        @pl.when(h == 0)
        def _():
            acc[...] = part

        @pl.when(h > 0)
        def _():
            acc[...] = acc[...] + part

        @pl.when(h == steps - 1)
        def _():
            y_ref[...] = acc[...].astype(BF16)

    lanes = head_lanes(count, per)
    return call(
        body, places, steps,
        [
            (pre, pl.BlockSpec((2, count, per * HEAD), lambda h, _: (0, 0, h))),
            (value, lanes), (sums, None), (other, None),
            (vecs, head_lanes(vecs.shape[0], per)), (cos_tab, None), (sin_tab, None),
        ]
        + [(everyone, block_at(3 * heads + j, per)) for j in range(per)],
        [
            (value.shape, BF16, lanes),
            (value.shape, BF16, lanes),
            ((heads, count, HEAD), BF16, pl.BlockSpec((per, count, HEAD), lambda h, _: (h, 0, 0))),
            ((count, D), BF16, None),
        ],
        [pltpu.VMEM((count, D), F32)],
    )


def project_text(places, everyone, context, vecs, heads):
    count = context.shape[0]
    span = heads * HEAD

    def body(_, text_ref, vec_ref, *refs):
        weights, (key, value, sums) = refs[:heads], refs[heads:]
        i = pl.program_id(0)
        made = nn(text_ref[...], joined(weights))

        @pl.when(i == 0)
        def _():
            k = made + vec_ref[6:7]
            key[...] = k
            sums[...] = wide(jnp.sum(k * k, -1, keepdims=True))

        @pl.when(i == 1)
        def _():
            value[...] = (made + vec_ref[7:8]).astype(BF16)

    return call(
        body, places, 2,
        [(context, None), (vecs, None)]
        + [(everyone, block_at(5 * heads + h, heads)) for h in range(heads)],
        [((count, span), F32, None), ((count, span), BF16, None), ((count, HEAD), F32, None)],
    )


def project_cross(places, everyone, rows, part, other, mod, shared, vecs, text_sums, heads):
    count = rows.shape[0]
    span = heads * HEAD
    text = text_sums.shape[0]

    def body(_, rows_ref, part_ref, other_ref, mod_ref, shared_ref, vec_ref, text_ref, *refs):
        weights, (branch, after, low, pre, sums) = refs[:heads], refs[heads:]
        y = part_ref[...].astype(F32) + other_ref[...].astype(F32) + shared_ref[0:1]
        branch[...] = y
        x = rows_ref[...] + mod_ref[2:3] * y
        after[...] = x
        unit, _ = normed(x)
        a = (unit * shared_ref[3:4] + shared_ref[4:5]).astype(BF16)
        low[...] = a
        q = nn(a, joined(weights)) + vec_ref[5:6]
        pre[...] = q
        sums[...] = pack_sums(jnp.sum(q * q, -1, keepdims=True), text_ref[:, 0:1])

    return call(
        body, places, 1,
        [(v, None) for v in (rows, part, other, mod, shared, vecs, text_sums)]
        + [(everyone, block_at(4 * heads + h)) for h in range(heads)],
        [
            ((count, D), F32, None),
            ((count, D), F32, None),
            ((count, D), BF16, None),
            ((count, span), F32, None),
            ((count, HEAD), F32, None),
        ],
    )


def attend_cross(places, everyone, pre, key_pre, value, sums, other, vecs, heads):
    count, text = pre.shape[0], value.shape[0]
    per = heads_per_step(heads, 6)
    steps = heads // per

    def body(_, pre_ref, key_ref, value_ref, sum_ref, other_ref, vec_ref, *refs):
        weights, (q_ref, k_ref, o_ref, y_ref, acc) = refs[:per], refs[per:]
        h = pl.program_id(0)
        total = sum_ref[...] + other_ref[...]
        q_inv = lax.rsqrt(total[:, 0:1] / D + NORM_EPS)
        k_inv = lax.rsqrt(unpack_text(total, text) / D + NORM_EPS)
        outs = []
        for j in range(per):
            lanes = slice(j * HEAD, (j + 1) * HEAD)
            q = (pre_ref[:, lanes] * q_inv * vec_ref[8:9, lanes]).astype(BF16)
            k = (key_ref[:, lanes] * k_inv * vec_ref[9:10, lanes]).astype(BF16)
            q_ref[:, lanes] = q
            k_ref[:, lanes] = k
            chance = softmax(nt(q, k) * SCALING)
            out = nn(chance.astype(BF16), value_ref[:, lanes]).astype(BF16)
            o_ref[j] = out
            outs.append(out)
        part = nt(jnp.concatenate(outs, 1), joined(weights))

        @pl.when(h == 0)
        def _():
            acc[...] = part

        @pl.when(h > 0)
        def _():
            acc[...] = acc[...] + part

        @pl.when(h == steps - 1)
        def _():
            y_ref[...] = acc[...].astype(BF16)

    return call(
        body, places, steps,
        [
            (pre, head_lanes(count, per)), (key_pre, head_lanes(text, per)),
            (value, head_lanes(text, per)), (sums, None), (other, None),
            (vecs, head_lanes(vecs.shape[0], per)),
        ]
        + [(everyone, block_at(7 * heads + j, per)) for j in range(per)],
        [
            (pre.shape, BF16, head_lanes(count, per)),
            (value.shape, BF16, head_lanes(text, per)),
            ((heads, count, HEAD), BF16, pl.BlockSpec((per, count, HEAD), lambda h, _: (h, 0, 0))),
            ((count, D), BF16, None),
        ],
        [pltpu.VMEM((count, D), F32)],
        vmem=40,
    )


def hidden_group(blocks):
    return max(g for g in (7, 5, 4, 3, 2, 1) if blocks % g == 0)


def block_lanes(where, everyone, held, sems, first, group, steps):
    i = pl.program_id(0)

    def fetch(step, act):
        slot = step % 2
        for j in range(group):
            copy = pltpu.make_async_copy(
                everyone.at[where[first + step * group + j]],
                held.at[slot, :, pl.ds(j * HEAD, HEAD)],
                sems.at[slot, j],
            )
            copy.start() if act else copy.wait()

    @pl.when(i == 0)
    def _():
        fetch(0, True)

    @pl.when(i + 1 < steps)
    def _():
        fetch(i + 1, True)

    fetch(i, False)
    return held[i % 2]


def lanes_scratch(group):
    return [pltpu.VMEM((2, D, group * HEAD), BF16), pltpu.SemaphoreType.DMA((2, group))]


def hidden_back(places, everyone, mod, cot, heads, blocks):
    count = cot.shape[0]
    group = hidden_group(blocks)
    steps = blocks // group

    def body(where, weights, mod_ref, cot_ref, grad, out, held, sems):
        @pl.when(pl.program_id(0) == 0)
        def _():
            grad[...] = (mod_ref[5:6] * cot_ref[...]).astype(BF16)

        down = block_lanes(where, weights, held, sems, 8 * heads + blocks, group, steps)
        out[...] = nn(grad[...], down).astype(BF16)

    return call(
        body, places, steps,
        [(everyone, ANY), (mod, None), (cot, None)],
        [
            ((count, D), BF16, None),
            ((count, blocks * HEAD), BF16, pl.BlockSpec((count, group * HEAD), lambda i, _: (0, i))),
        ],
        lanes_scratch(group),
        vmem=40,
    )


def hidden_both(places, everyone, after_one, part, other, mod, shared, d_act, up_bias, heads, blocks):
    count = after_one.shape[0]
    group = hidden_group(blocks)
    steps = blocks // group
    span = group * HEAD

    def body(where, weights, after_ref, part_ref, other_ref, mod_ref, shared_ref, d_ref, bias_ref, after, low, hidden, d_hidden, d_bias, da_ref, acc, held, sems):
        i = pl.program_id(0)

        @pl.when(i == 0)
        def _():
            x = after_ref[...] + part_ref[...].astype(F32) + other_ref[...].astype(F32)
            x = x + shared_ref[1:2]
            after[...] = x
            unit, _ = normed(x)
            low[...] = (unit * (1.0 + mod_ref[4:5]) + mod_ref[3:4]).astype(BF16)
            acc[...] = jnp.zeros_like(acc)

        up = block_lanes(where, weights, held, sems, 8 * heads, group, steps)
        pre = nn(low[...], up) + bias_ref[...]
        square = pre * pre
        bent = jnp.tanh(GELU_COEF * (pre + 0.044715 * pre * square))
        act = (0.5 * pre * (1.0 + bent)).astype(BF16)
        slope = 0.5 * (1.0 + bent) + 0.5 * pre * (1.0 - bent * bent) * (
            GELU_COEF * (1.0 + 3.0 * 0.044715 * square)
        )
        dh = (d_ref[...].astype(F32) * slope).astype(BF16)
        d_bias[...] = total_of(dh.astype(F32))
        for j in range(group):
            hidden[j] = act[:, j * HEAD : (j + 1) * HEAD]
            d_hidden[j] = dh[:, j * HEAD : (j + 1) * HEAD]
        acc[...] = acc[...] + nt(dh, up)

        @pl.when(i == steps - 1)
        def _():
            da_ref[...] = acc[...].astype(BF16)

    tall = pl.BlockSpec((group, count, HEAD), lambda i, _: (i, 0, 0))
    flat = pl.BlockSpec((1, span), lambda i, _: (0, i))
    return call(
        body, places, steps,
        [(everyone, ANY)]
        + [(v, None) for v in (after_one, part, other, mod, shared)]
        + [(d_act, pl.BlockSpec((count, span), lambda i, _: (0, i))), (up_bias, flat)],
        [
            ((count, D), F32, None),
            ((count, D), BF16, None),
            ((blocks, count, HEAD), BF16, tall),
            ((blocks, count, HEAD), BF16, tall),
            (up_bias.shape, F32, flat),
            ((count, D), BF16, None),
        ],
        [pltpu.VMEM((count, D), F32)] + lanes_scratch(group),
        vmem=40,
    )


def hidden_out(places, everyone, hidden, heads):
    blocks, count = hidden.shape[:2]
    group = hidden_group(blocks)
    steps = blocks // group

    def body(where, weights, hidden_ref, y_ref, acc, held, sems):
        i = pl.program_id(0)
        down = block_lanes(where, weights, held, sems, 8 * heads + blocks, group, steps)
        part = nt(jnp.concatenate([hidden_ref[j] for j in range(group)], 1), down)

        @pl.when(i == 0)
        def _():
            acc[...] = part

        @pl.when(i > 0)
        def _():
            acc[...] = acc[...] + part

        @pl.when(i == steps - 1)
        def _():
            y_ref[...] = acc[...].astype(BF16)

    return call(
        body, places, steps,
        [(everyone, ANY), (hidden, pl.BlockSpec((group, count, HEAD), lambda i, _: (i, 0, 0)))],
        [((count, D), BF16, None)],
        [pltpu.VMEM((count, D), F32)] + lanes_scratch(group),
        vmem=40,
    )[0]


def cross_back(places, everyone, cot, after_two, part, other, mod, query, key, value, pre, key_pre, vecs, heads):
    count, text = query.shape[0], key.shape[0]
    per = heads_per_step(heads, 6)
    steps = heads // per

    def body(_, cot_ref, after_ref, part_ref, other_ref, mod_ref, q_ref, k_ref, v_ref, pre_ref, key_ref, vec_ref, *refs):
        weights, (dx_ref, low_ref, dq_ref, dk_ref, dv_ref, sums, q_acc, k_acc) = refs[:per], refs[per:]
        h = pl.program_id(0)

        @pl.when(h == 0)
        def _():
            da = part_ref[...].astype(F32) + other_ref[...].astype(F32)
            back, _ = normed_back(after_ref[...], da * (1.0 + mod_ref[4:5]))
            dx = cot_ref[...] + back
            dx_ref[...] = dx
            low_ref[...] = dx.astype(BF16)
            q_acc[...] = jnp.zeros_like(q_acc)
            k_acc[...] = jnp.zeros_like(k_acc)

        do_all = nn(low_ref[...], joined(weights)).astype(BF16)
        q_sums, k_sums = 0.0, 0.0
        for j in range(per):
            lanes = slice(j * HEAD, (j + 1) * HEAD)
            do = do_all[:, lanes]
            q, k = q_ref[:, lanes], k_ref[:, lanes]
            chance = softmax(nt(q, k) * SCALING)
            dp = nt(do, v_ref[:, lanes])
            ds = (chance * (dp - jnp.sum(chance * dp, -1, keepdims=True))).astype(BF16)
            dv_ref[j] = tn(chance.astype(BF16), do).astype(BF16)
            dq = nn(ds, k) * SCALING
            dk = tn(ds, q) * SCALING
            dq_ref[:, lanes] = dq
            dk_ref[:, lanes] = dk
            q_sums += pre_ref[:, lanes] * vec_ref[8:9, lanes] * dq
            k_sums += key_ref[:, lanes] * vec_ref[9:10, lanes] * dk
        q_acc[...] = q_acc[...] + q_sums
        k_acc[...] = k_acc[...] + k_sums

        @pl.when(h == steps - 1)
        def _():
            sums[...] = pack_sums(
                jnp.sum(q_acc[...], -1, keepdims=True), jnp.sum(k_acc[...], -1, keepdims=True)
            )

    return call(
        body, places, steps,
        [(v, None) for v in (cot, after_two, part, other, mod)]
        + [
            (query, head_lanes(count, per)), (key, head_lanes(text, per)),
            (value, head_lanes(text, per)), (pre, head_lanes(count, per)),
            (key_pre, head_lanes(text, per)), (vecs, head_lanes(vecs.shape[0], per)),
        ]
        + [(everyone, block_at(7 * heads + j, per)) for j in range(per)],
        [
            ((count, D), F32, None),
            ((count, D), BF16, None),
            (query.shape, F32, head_lanes(count, per)),
            (key.shape, F32, head_lanes(text, per)),
            ((heads, text, HEAD), BF16, pl.BlockSpec((per, text, HEAD), lambda h, _: (h, 0, 0))),
            ((count, HEAD), F32, None),
        ],
        [pltpu.VMEM((count, HEAD), F32), pltpu.VMEM((text, HEAD), F32)],
        vmem=48,
    )


def norm_grad(pre, inverse, gain, incoming, total):
    grad = inverse * (gain * incoming) - pre * (inverse * inverse * inverse) * (total / D)
    low = grad.astype(BF16)
    return low, total_of(low.astype(F32)), total_of(incoming * pre * inverse)


def cross_back_rows(places, everyone, pre, key_pre, dq, dk, dv, squares, squares_other, sums, sums_other, vecs, heads):
    count, text = pre.shape[0], key_pre.shape[0]
    per = heads_per_step(heads, 6)
    steps = heads // per

    def body(_, pre_ref, key_ref, dq_ref, dk_ref, dv_ref, sq_ref, sqo_ref, sum_ref, sumo_ref, vec_ref, *refs):
        weights, (gq_ref, gk_ref, vec_out, da_ref, acc) = refs[:per], refs[per:]
        h = pl.program_id(0)
        squares_all = sq_ref[...] + sqo_ref[...]
        total = sum_ref[...] + sumo_ref[...]
        q_inv = lax.rsqrt(squares_all[:, 0:1] / D + NORM_EPS)
        k_inv = lax.rsqrt(unpack_text(squares_all, text) / D + NORM_EPS)
        q_total, k_total = total[:, 0:1], unpack_text(total, text)
        lows = []
        for j in range(per):
            lanes = slice(j * HEAD, (j + 1) * HEAD)
            low_q, bias_q, gain_q = norm_grad(
                pre_ref[:, lanes], q_inv, vec_ref[8:9, lanes], dq_ref[:, lanes], q_total
            )
            low_k, bias_k, gain_k = norm_grad(
                key_ref[:, lanes], k_inv, vec_ref[9:10, lanes], dk_ref[:, lanes], k_total
            )
            gq_ref[j] = low_q
            gk_ref[j] = low_k
            lows.append(low_q)
            bias_v = total_of(dv_ref[j].astype(F32))
            vec_out[:, lanes] = jnp.concatenate(
                [bias_q, bias_k, bias_v, gain_q, gain_k, jnp.zeros((3, HEAD), F32)], 0
            )
        part = nt(jnp.concatenate(lows, 1), joined(weights))

        @pl.when(h == 0)
        def _():
            acc[...] = part

        @pl.when(h > 0)
        def _():
            acc[...] = acc[...] + part

        @pl.when(h == steps - 1)
        def _():
            da_ref[...] = acc[...].astype(BF16)

    tall = pl.BlockSpec((per, count, HEAD), lambda h, _: (h, 0, 0))
    tall_text = pl.BlockSpec((per, text, HEAD), lambda h, _: (h, 0, 0))
    return call(
        body, places, steps,
        [
            (pre, head_lanes(count, per)), (key_pre, head_lanes(text, per)),
            (dq, head_lanes(count, per)), (dk, head_lanes(text, per)), (dv, tall_text),
            (squares, None), (squares_other, None), (sums, None), (sums_other, None),
            (vecs, head_lanes(vecs.shape[0], per)),
        ]
        + [(everyone, block_at(4 * heads + j, per)) for j in range(per)],
        [
            ((heads, count, HEAD), BF16, tall),
            ((heads, text, HEAD), BF16, tall_text),
            ((8, heads * HEAD), F32, head_lanes(8, per)),
            ((count, D), BF16, None),
        ],
        [pltpu.VMEM((count, D), F32)],
        vmem=40,
    )


def self_back(places, everyone, dx_two, after_one, part, other, mod, shared, branch, query, key, value, pre, vecs, cos_tab, sin_tab, heads, tokens):
    count = query.shape[0]
    per = heads_per_step(heads, 2)
    steps = heads // per

    def body(_, dx_in, after_ref, part_ref, other_ref, mod_ref, shared_ref, branch_ref, q_ref, k_ref, v_ref, pre_ref, vec_ref, cos_ref, sin_ref, *refs):
        weights, (dx_ref, low_ref, d_ref, dv_ref, sums, vec_out, q_acc, k_acc) = refs[:per], refs[per:]
        h = pl.program_id(0)

        @pl.when(h == 0)
        def _():
            da = part_ref[...].astype(F32) + other_ref[...].astype(F32)
            back, _ = normed_back(after_ref[...], da * shared_ref[3:4])
            dx = dx_in[...] + back
            dx_ref[...] = dx
            low = (mod_ref[2:3] * dx).astype(BF16)
            low_ref[...] = low
            vec_out[0:1] = 0.5 * total_of(low.astype(F32))
            vec_out[1:2] = 0.5 * total_of(dx * branch_ref[...])
            q_acc[...] = jnp.zeros_like(q_acc)
            k_acc[...] = jnp.zeros_like(k_acc)

        do_all = nn(low_ref[...], joined(weights)).astype(BF16)
        cos, sin = cos_ref[...], -sin_ref[...]
        q_sums, k_sums = 0.0, 0.0
        for j in range(per):
            lanes = slice(j * HEAD, (j + 1) * HEAD)
            do = do_all[:, lanes]
            q, k = q_ref[:, lanes], k_ref[:, lanes]
            chance = softmax(self_scores(q, k, tokens))
            dp = nt(do, v_ref[:, lanes])
            ds = (chance * (dp - jnp.sum(chance * dp, -1, keepdims=True))).astype(BF16)
            dv_ref[j] = tn(chance.astype(BF16), do).astype(BF16)
            dq = turned(nn(ds, k) * SCALING, cos, sin)
            dk = turned(tn(ds, q) * SCALING, cos, sin)
            d_ref[0, :, lanes] = dq
            d_ref[1, :, lanes] = dk
            q_sums += pre_ref[0, :, lanes] * vec_ref[3:4, lanes] * dq
            k_sums += pre_ref[1, :, lanes] * vec_ref[4:5, lanes] * dk
        q_acc[...] = q_acc[...] + q_sums
        k_acc[...] = k_acc[...] + k_sums

        @pl.when(h == steps - 1)
        def _():
            lane = lax.broadcasted_iota(jnp.int32, q_acc.shape, 1)
            sums[...] = jnp.where(
                lane < 64,
                wide(jnp.sum(q_acc[...], -1, keepdims=True)),
                wide(jnp.sum(k_acc[...], -1, keepdims=True)),
            )

    lanes = head_lanes(count, per)
    pair = pl.BlockSpec((2, count, per * HEAD), lambda h, _: (0, 0, h))
    return call(
        body, places, steps,
        [(v, None) for v in (dx_two, after_one, part, other, mod, shared, branch)]
        + [
            (query, lanes), (key, lanes), (value, lanes), (pre, pair),
            (vecs, head_lanes(vecs.shape[0], per)), (cos_tab, None), (sin_tab, None),
        ]
        + [(everyone, block_at(3 * heads + j, per)) for j in range(per)],
        [
            ((count, D), F32, None),
            ((count, D), BF16, None),
            (pre.shape, F32, pair),
            ((heads, count, HEAD), BF16, pl.BlockSpec((per, count, HEAD), lambda h, _: (h, 0, 0))),
            ((count, HEAD), F32, None),
            ((2, D), F32, None),
        ],
        [pltpu.VMEM((count, HEAD), F32), pltpu.VMEM((count, HEAD), F32)],
        vmem=32,
    )


def self_back_rows(places, everyone, rows, pre, grads, dv, squares, squares_other, sums, sums_other, vecs, heads):
    count = pre.shape[1]
    per = heads_per_step(heads, 2)
    steps = heads // per

    def body(_, rows_ref, pre_ref, d_ref, dv_ref, sq_ref, sqo_ref, sum_ref, sumo_ref, vec_ref, *refs):
        weights, (gq_ref, gk_ref, vec_out, da_ref, row_out, acc) = refs[: 3 * per], refs[3 * per :]
        h = pl.program_id(0)
        squares_all = sq_ref[...] + sqo_ref[...]
        total = sum_ref[...] + sumo_ref[...]
        inverses = [
            lax.rsqrt(squares_all[:, n : n + 1] / D + NORM_EPS) for n in (0, 64)
        ]
        lows = []
        for j in range(per):
            lanes = slice(j * HEAD, (j + 1) * HEAD)
            biases, gains = [], []
            for n, out in enumerate((gq_ref, gk_ref)):
                low, bias, gain = norm_grad(
                    pre_ref[n, :, lanes], inverses[n], vec_ref[3 + n : 4 + n, lanes],
                    d_ref[n, :, lanes], total[:, 64 * n : 64 * n + 1],
                )
                out[j] = low
                lows.append(low)
                biases.append(bias)
                gains.append(gain)
            dv_low = dv_ref[j]
            lows.append(dv_low)
            vec_out[:, lanes] = jnp.concatenate(
                biases + [total_of(dv_low.astype(F32))] + gains + [jnp.zeros((3, HEAD), F32)], 0
            )
        part = nt(jnp.concatenate(lows, 1), joined(weights))

        @pl.when(h == 0)
        def _():
            acc[...] = part

        @pl.when(h > 0)
        def _():
            acc[...] = acc[...] + part

        @pl.when(h == steps - 1)
        def _():
            da = acc[...]
            da_ref[...] = da.astype(BF16)
            row_out[0:1] = total_of(da)
            row_out[1:2] = total_of(da * normed(rows_ref[...])[0])

    tall = pl.BlockSpec((per, count, HEAD), lambda h, _: (h, 0, 0))
    pair = pl.BlockSpec((2, count, per * HEAD), lambda h, _: (0, 0, h))
    return call(
        body, places, steps,
        [
            (rows, None), (pre, pair), (grads, pair), (dv, tall), (squares, None),
            (squares_other, None), (sums, None), (sums_other, None),
            (vecs, head_lanes(vecs.shape[0], per)),
        ]
        + [(everyone, block_at(n * heads + j, per)) for j in range(per) for n in range(3)],
        [
            ((heads, count, HEAD), BF16, tall),
            ((heads, count, HEAD), BF16, tall),
            ((8, heads * HEAD), F32, head_lanes(8, per)),
            ((count, D), BF16, None),
            ((2, D), F32, None),
        ],
        [pltpu.VMEM((count, D), F32)],
        vmem=40,
    )


def shared_sums(places, after_one, after_two, grad_two, grad_three, cot, da_two, da_three, y_three, shared):
    def body(_, x1_ref, x2_ref, dy2, dy3, cot_ref, da2, da3, y3, shared_ref, out):
        out[...] = jnp.zeros_like(out)
        out[1:2] = 0.5 * total_of(dy2[...].astype(F32))
        out[2:3] = 0.5 * total_of(dy3[...].astype(F32))
        part = da3[...].astype(F32)
        out[3:4] = total_of(part * normed(x1_ref[...])[0])
        out[4:5] = total_of(part)
        part = da2[...].astype(F32)
        out[8:9] = total_of(part)
        out[9:10] = total_of(part * normed(x2_ref[...])[0])
        out[10:11] = total_of(cot_ref[...] * (y3[...].astype(F32) + 0.5 * shared_ref[2:3]))

    return call(
        body, places, 1,
        [(v, None) for v in (after_one, after_two, grad_two, grad_three, cot, da_two, da_three, y_three, shared)],
        [(shared.shape, F32, None)],
    )[0]


def body(
    latents,
    context,
    cotangent,
    positions,
    step_ids,
    owners,
    time_table,
    master,
    first_moment,
    second_moment,
    head_params,
    head_first,
    head_second,
    shared_params,
    shared_first,
    shared_second,
):
    tensors = lax.axis_size("tensor")
    devices = lax.axis_size("dp")
    slot_count = master.shape[1]
    tile_count = owners.shape[0]
    heads_here = HEADS // tensors
    blocks_here = FF // (HEAD * tensors)
    width_here = D // tensors
    places, holder = owner_layout(owners, slot_count, devices)
    scales = tile_scales(tile_count, heads_here, blocks_here)
    my_slots = lax.dynamic_slice_in_dim(holder, lax.axis_index("dp") * slot_count, slot_count)
    rank = pair_rank()
    filled = my_slots >= 0
    slot_scale = jnp.where(filled, scales[jnp.maximum(my_slots, 0)], 0.0)
    scaled = (master[0] * slot_scale[:, None, None]).astype(jnp.bfloat16)
    half = latents.shape[0]
    tokens = 2 * half
    count = -(-tokens // 16) * 16
    taller = ((0, -half % 16), (0, 0))
    small = jnp.concatenate(
        [
            head_params[0],
            positions.reshape(-1).astype(jnp.float32),
            step_ids.astype(jnp.float32),
        ]
    )
    packed = jnp.pad(small, (0, -small.shape[0] % 1024)).reshape(-1, HEAD)
    everyone, lats, cots, context, packed = gather_slots(
        scaled, jnp.pad(latents, taller), jnp.pad(cotangent, taller), context, packed
    )
    small = packed.reshape(-1)
    vectors = small[: head_params.shape[1]]
    small = small[head_params.shape[1] :]
    positions = small[: positions.size].reshape(positions.shape)
    step = small[positions.size]
    vecs = vectors[: 10 * width_here].reshape(10, width_here)
    up_bias = vectors[10 * width_here :].reshape(1, -1)
    chosen = (step == jnp.arange(TSTEPS)).astype(jnp.float32)
    mod = shared_params[5:11] + jnp.einsum(
        "s,skd->kd", chosen, time_table, precision=lax.Precision.HIGHEST
    )
    cos_tab, sin_tab = rope_tables(positions, HEAD)
    sin_tab = jnp.where(jnp.arange(HEAD) % 2 == 0, -sin_tab, sin_tab)
    cos_tab, sin_tab = (jnp.pad(t, ((0, count - tokens), (0, 0))) for t in (cos_tab, sin_tab))

    def all_rows(halves):
        rows = jnp.concatenate([halves[0, :half], halves[1, :half]], 0)
        return jnp.pad(rows, ((0, count - tokens), (0, 0))).astype(jnp.float32)

    def upright(rows):
        return jnp.pad(rows, ((0, -rows.shape[0] % HEAD), (0, 0))).T

    def beside(*values):
        return lax.optimization_barrier(values)

    rows, cot = all_rows(lats), all_rows(cots)
    low_one, pre_one, value_one, squares_one = project_self(
        places, everyone, rows, mod, vecs, heads_here
    )
    squares_one_other = pair_swap(squares_one)
    query_one, key_one, heads_one, part_one = attend_self(
        places, everyone, pre_one, value_one, squares_one, squares_one_other, vecs, cos_tab,
        sin_tab, heads_here, tokens,
    )
    part_one, context = beside(part_one, context)
    part_one_other = pair_swap(part_one)
    key_pre, value_two, text_squares = project_text(places, everyone, context, vecs, heads_here)
    left_context, left_one = upright(context), upright(low_one)
    part_one_other, key_pre, left_context, left_one = beside(
        part_one_other, key_pre, left_context, left_one
    )
    branch_one, after_one, low_two, pre_two, squares_two = project_cross(
        places, everyone, rows, part_one, part_one_other, mod, shared_params, vecs,
        text_squares, heads_here,
    )
    squares_two_other = pair_swap(squares_two)
    query_two, key_two, heads_two, part_two = attend_cross(
        places, everyone, pre_two, key_pre, value_two, squares_two, squares_two_other, vecs,
        heads_here,
    )
    part_two, cot, low_two = beside(part_two, cot, low_two)
    part_two_other = pair_swap(part_two)
    grad_three, d_act = hidden_back(places, everyone, mod, cot, heads_here, blocks_here)
    left_two, left_grad_three = upright(low_two), upright(grad_three)
    part_two_other, d_act, left_two, left_grad_three = beside(
        part_two_other, d_act, left_two, left_grad_three
    )
    after_two, low_three, hidden, d_hidden, d_up_bias, da_two = hidden_both(
        places, everyone, after_one, part_two, part_two_other, mod, shared_params, d_act, up_bias,
        heads_here, blocks_here,
    )
    da_two_other = pair_swap(da_two)
    y_three = hidden_out(places, everyone, hidden, heads_here)
    left_three = upright(low_three)
    da_two_other, y_three, left_three = beside(da_two_other, y_three, left_three)
    dx_two, grad_two, dq_two, dk_two, dv_two, sums_two = cross_back(
        places, everyone, cot, after_two, da_two, da_two_other, mod, query_two, key_two,
        value_two, pre_two, key_pre, vecs, heads_here,
    )
    query_grad_two, key_grad_two, vecs_two, da_three = cross_back_rows(
        places, everyone, pre_two, key_pre, dq_two, dk_two, dv_two, squares_two,
        squares_two_other, sums_two, pair_swap(sums_two), vecs, heads_here,
    )
    da_three_other = pair_swap(da_three)
    shared_grad = shared_sums(
        places, after_one, after_two, grad_two, grad_three, cot, da_two, da_three, y_three,
        shared_params,
    )
    left_grad_two = upright(grad_two)
    da_three_other, shared_grad, left_grad_two = beside(da_three_other, shared_grad, left_grad_two)
    dx_one, grad_one, d_one, dv_one, sums_one, rows_a = self_back(
        places, everyone, dx_two, after_one, da_three, da_three_other, mod, shared_params,
        branch_one, query_one, key_one, value_one, pre_one, vecs, cos_tab, sin_tab, heads_here,
        tokens,
    )
    query_grad_one, key_grad_one, vecs_one, da_one, rows_b = self_back_rows(
        places, everyone, rows, pre_one, d_one, dv_one, squares_one, squares_one_other, sums_one,
        pair_swap(sums_one), vecs, heads_here,
    )
    shared_grad = jnp.concatenate(
        [rows_a[0:1], shared_grad[1:5], rows_b, rows_a[1:2], shared_grad[8:]], 0
    )
    head_grad = jnp.concatenate(
        [vecs_one[:5].reshape(-1), vecs_two[:5].reshape(-1), d_up_bias.reshape(-1)]
    )
    tensor_rank = lax.axis_index("tensor")
    head_padded = jnp.where(jnp.arange(tensors)[:, None] == rank, head_grad[None, :], 0.0)
    vector = jnp.concatenate([head_padded.reshape(-1), shared_grad.reshape(-1)])
    vector = jnp.pad(vector, (0, -vector.shape[0] % 1024)).reshape(-1, 128)
    parts, vector, output, grad_input = reduce_slots(
        holder,
        kind_of_blocks(tile_count, heads_here, blocks_here),
        (left_one, upright(grad_one), left_two, left_context, left_grad_two, left_three, left_grad_three),
        (
            query_grad_one,
            key_grad_one,
            dv_one,
            heads_one,
            query_grad_two,
            key_grad_two,
            dv_two,
            heads_two,
            d_hidden,
            hidden,
        ),
        vector,
        (rows, after_two, dx_one, y_three, da_one),
        jnp.concatenate([mod[5:6], mod[1:2], shared_params[2:3], jnp.zeros((5, D), F32)], 0),
        slot_count,
    )
    output, grad_input = (
        jnp.where(lax.axis_index("tensor") == 0, v[:half], v[half:tokens])
        for v in (output, grad_input)
    )
    new_master, new_first, new_second = adam_slots(
        parts, master, first_moment, second_moment, slot_scale, filled
    )
    vector = vector.reshape(-1)
    head_total = vector[: head_padded.size].reshape(head_padded.shape)
    shared_total = vector[head_padded.size : head_padded.size + shared_grad.size]
    shared_total = shared_total.reshape(shared_grad.shape)
    mine_head = lax.dynamic_slice_in_dim(head_total, tensor_rank, 1, 0)
    new_head, new_head_first, new_head_second = adam_step(
        head_params, mine_head, head_first, head_second, VECTOR_RATE, 0.0
    )
    new_shared, new_shared_first, new_shared_second = adam_step(
        shared_params, shared_total, shared_first, shared_second, VECTOR_RATE, 0.0
    )
    return (
        output,
        grad_input,
        new_master,
        new_first,
        new_second,
        new_head,
        new_head_first,
        new_head_second,
        new_shared,
        new_shared_first,
        new_shared_second,
    )


def solution(mesh):
    return jax.shard_map(
        body,
        mesh=mesh,
        in_specs=(
            P(("dp", "tensor"), None),
            P("dp", None),
            P(("dp", "tensor"), None),
            P(None, "dp"),
            P("dp"),
            P(),
            P(),
            P("tensor", "dp", None, None),
            P("tensor", "dp", None, None),
            P("tensor", "dp", None, None),
            P("tensor", None),
            P("tensor", None),
            P("tensor", None),
            P(),
            P(),
            P(),
        ),
        out_specs=(
            P(("dp", "tensor"), None),
            P(("dp", "tensor"), None),
            P("tensor", "dp", None, None),
            P("tensor", "dp", None, None),
            P("tensor", "dp", None, None),
            P("tensor", None),
            P("tensor", None),
            P("tensor", None),
            P(),
            P(),
            P(),
        ),
        check_vma=False,
    )
```

```python
import functools

import jax
import jax.numpy as jnp
from jax import lax
from jax.experimental import pallas as pl
from jax.experimental.pallas import tpu as pltpu
from jax.sharding import PartitionSpec as P

D = 1536
HEADS = 12
HEAD = 128
FF = 8960
TSTEPS = 16
STEPC = 10


NORM_EPS = 1e-06
BETA_ONE = 0.9
BETA_TWO = 0.999
ADAM_EPS = 1e-08
TILE_RATE = 1.0
TILE_DECAY = 0.1
VECTOR_RATE = 0.5
GELU_COEF = 0.7978845608028654


def rope_tables(token_places, head_size):
    sixths = head_size // 6
    frame_pairs = (head_size - 4 * sixths) // 2
    frame_freq = 10000.0 ** (-jnp.arange(frame_pairs, dtype=jnp.float32) / frame_pairs)
    side_freq = 10000.0 ** (-jnp.arange(sixths, dtype=jnp.float32) / sixths)
    spots = token_places.astype(jnp.float32)
    angles = jnp.concatenate(
        [
            spots[0][..., None] * frame_freq,
            spots[1][..., None] * side_freq,
            spots[2][..., None] * side_freq,
        ],
        -1,
    )
    angles = jnp.repeat(angles, 2, axis=-1)
    return (jnp.cos(angles), jnp.sin(angles))


def owner_layout(owners, slot_count, devices):
    indices = jnp.arange(owners.shape[0], dtype=jnp.int32)
    same_owner = (owners[:, None] == owners[None, :]) & (indices[None, :] < indices[:, None])
    slot_of = jnp.sum(same_owner.astype(jnp.int32), axis=1)
    places = owners * slot_count + slot_of
    spots = jnp.arange(slot_count * devices, dtype=jnp.int32)
    holder = (
        jnp.sum(jnp.where(places[None, :] == spots[:, None], indices[None, :] + 1, 0), axis=1) - 1
    )
    return (places, holder)


def tile_scales(tile_count, heads_here, blocks_here):
    indices = jnp.arange(tile_count)
    scale_in = D ** (-0.5)
    scale_out = HEADS ** (-0.5)
    scale_down = FF ** (-0.5)
    scales = jnp.where(
        indices < 3 * heads_here,
        scale_in,
        jnp.where(
            indices < 4 * heads_here,
            scale_out,
            jnp.where(
                indices < 7 * heads_here,
                scale_in,
                jnp.where(
                    indices < 8 * heads_here,
                    scale_out,
                    jnp.where(indices < 8 * heads_here + blocks_here, scale_in, scale_down),
                ),
            ),
        ),
    )
    return scales.astype(jnp.float32)


def adam_step(weight, gradient, moment_one, moment_two, step_rate, decay_rate):
    first_new = BETA_ONE * moment_one + (1.0 - BETA_ONE) * gradient
    second_new = BETA_TWO * moment_two + (1.0 - BETA_TWO) * gradient * gradient
    first_hat = first_new / (1.0 - BETA_ONE**STEPC)
    second_hat = second_new / (1.0 - BETA_TWO**STEPC)
    weight_new = weight - step_rate * (
        first_hat / (jnp.sqrt(second_hat) + ADAM_EPS) + decay_rate * weight
    )
    return (weight_new, first_new, second_new)


MESH = pl.DeviceIdType.MESH
ANY = pl.BlockSpec(memory_space=pl.ANY)
MIB = 1 << 20


def chip_pairs():
    return lax.axis_size("dp") == 16 and lax.axis_size("tensor") == 2


def pair_rank():
    if chip_pairs():
        return (lax.axis_index("dp") // 4) % 2
    return lax.axis_index("tensor")


def pair_swap(value):
    if chip_pairs():
        return lax.ppermute(value, "dp", [(i, i ^ 4) for i in range(16)])
    return lax.ppermute(value, "tensor", [(0, 1), (1, 0)])


def pair_sums(*values):
    stacked = jnp.concatenate([v.reshape(-1) for v in values])
    total = stacked + pair_swap(stacked)
    out, at = [], 0
    for v in values:
        out.append(total[at : at + v.size].reshape(v.shape))
        at += v.size
    return tuple(out)


def place_of():
    chip, core = lax.axis_index("dp"), lax.axis_index("tensor")
    z, y, x = chip // 4, (chip // 2) % 2, chip % 2
    return chip, core, z, y, x


def column_of(z, y, x, k):
    high, low_bit = z // 2, z % 2
    if k & 2:
        high = 1 - high
    if k & 1:
        low_bit = 1 - low_bit
    return (2 * high + low_bit) * 4 + 2 * y + x


def greet(chip, core, z, y, x):
    barrier = pltpu.get_barrier_semaphore()
    friends = []
    for k in range(4):
        for flip in (0, 1):
            if k or flip:
                friends.append((column_of(z, y, x, k), core if flip == 0 else 1 - core))
    friends.append((column_of(z, y, 1 - x, 0), core))
    friends.append((column_of(z, 1 - y, x, 0), core))
    for friend in friends:
        pl.semaphore_signal(barrier, inc=1, device_id=friend, device_id_type=MESH)
    pl.semaphore_wait(barrier, len(friends))


def gather_kernel(
    own, lat, cot, text, small, out, lats, cots, texts, smalls, clip_s, clip_r,
    near_s, col_r, x_s, x_r, y_s, y_r, sib_s, sib_r,
):
    chip, core, z, y, x = place_of()
    rank = z % 2
    half = own.shape[1] // 2
    part = half // 2
    at_x = column_of(z, y, 1 - x, 0)
    at_y = column_of(z, 1 - y, x, 0)
    greet(chip, core, z, y, x)

    batch = max(n for n in (1, 2, 3) if own.shape[0] % n == 0)
    batches = own.shape[0] // batch
    turns = 4 * batches

    def case(s):
        late = jnp.maximum(s - batches, 0)
        k = jnp.where(s < batches, 0, 1 + late % 3)
        return k, jnp.where(s < batches, s, late // 3)

    def remote(unit, g, first, count, send, recv, device):
        piece = out.at[
            unit, pl.ds(g * batch, batch), pl.ds(pl.multiple_of(first, 16), count), :
        ]
        return pltpu.make_async_remote_copy(
            src_ref=piece, dst_ref=piece, send_sem=send, recv_sem=recv,
            device_id=device, device_id_type=MESH,
        )

    def own_copy(g, j, h):
        target = (toggled(z, y, x, 0, 0, 2 * j) // 8 * 8) + core * 4 + 2 * y + x
        part_of = (pl.ds(g * batch, batch), pl.ds(h * half, half))
        src = own.at[part_of[0], part_of[1], :]
        dst = out.at[chip, part_of[0], part_of[1], :]
        recv = col_r.at[z * batches + g]
        go = pltpu.make_async_remote_copy(
            src_ref=src, dst_ref=dst, send_sem=near_s.at[(2 * j + h) * batches + g],
            recv_sem=recv, device_id=(target, h), device_id_type=MESH,
        )
        return go, pltpu.make_async_copy(src, dst, recv)

    for g in range(batches):
        for j in range(2):
            for h in range(2):
                go, here = own_copy(g, j, h)
                if j == 1:
                    go.start()
                    continue
                stays = jnp.logical_and(rank == core, core == h)

                @pl.when(stays)
                def _():
                    here.start()

                @pl.when(jnp.logical_not(stays))
                def _():
                    go.start()

    pair_chip = column_of(z, y, x, 1)
    rows_of_text = text.shape[0] // 2

    def clip_pieces(h):
        share = pl.ds(h * rows_of_text, rows_of_text)
        return ((lat, lats.at[h]), (cot, cots.at[h]), (text.at[share], texts.at[share]))

    home = rank == core
    trade = pltpu.make_async_remote_copy(
        src_ref=small, dst_ref=smalls, send_sem=clip_s.at[6], recv_sem=clip_r.at[6],
        device_id=(pair_chip, 1 - core), device_id_type=MESH,
    )
    keep = pltpu.make_async_copy(small, smalls, clip_r.at[6])

    @pl.when(home)
    def _():
        keep.start()

    @pl.when(jnp.logical_not(home))
    def _():
        trade.start()

    def hand_out(h, n, wait):
        src, dst = clip_pieces(h)[n]
        far = pltpu.make_async_remote_copy(
            src_ref=src, dst_ref=dst, send_sem=clip_s.at[n], recv_sem=clip_r.at[3 * h + n],
            device_id=(pair_chip, rank), device_id_type=MESH,
        )
        near = pltpu.make_async_remote_copy(
            src_ref=src, dst_ref=dst, send_sem=clip_s.at[3 + n], recv_sem=clip_r.at[3 * h + n],
            device_id=(chip, 1 - core), device_id_type=MESH,
        )
        here = pltpu.make_async_copy(src, dst, clip_r.at[3 * h + n])

        @pl.when(core == h)
        def _():
            if wait:
                far.wait_send()
            else:
                far.start()

            @pl.when(home)
            def _():
                if not wait:
                    here.start()

            @pl.when(jnp.logical_not(home))
            def _():
                if wait:
                    near.wait_send()
                else:
                    near.start()

    for n in range(3):
        for h in range(2):
            hand_out(h, n, False)

    mine, other = core * half, (1 - core) * half
    sibling = (chip, 1 - core)

    def to_x(s, n):
        k, g = case(s)
        i = turns * n + s
        unit = toggled(z, y, x, n, 0, k)
        return remote(unit, g, mine, part if n else half, x_s.at[i], x_r.at[i], (at_x, core))

    def from_x(s, n):
        k, g = case(s)
        i = turns * n + s
        unit = toggled(z, y, x, n, 1, k)
        return remote(unit, g, mine, part if n else half, x_s.at[i], x_r.at[i], (at_x, core))

    def to_y(s, n):
        k, g = case(s)
        i = turns * n + s
        unit = toggled(z, y, x, 0, n, k)
        first, count = (mine + part, part) if n else (mine, half)
        return remote(unit, g, first, count, y_s.at[i], y_r.at[i], (at_y, core))

    def from_y(s, n):
        k, g = case(s)
        i = turns * n + s
        unit = toggled(z, y, x, 1, n, k)
        first, count = (mine + part, part) if n else (mine, half)
        return remote(unit, g, first, count, y_s.at[i], y_r.at[i], (at_y, core))

    def to_sib(s, n, away=False):
        k, g = case(s)
        i = turns * n + s
        unit = toggled(z, y, x, int(n in (2, 3, 4)), int(n in (1, 3, 4)), k)
        first = (other if away else mine) + (part if n == 4 else 0)
        return remote(
            unit, g, first, part if n >= 3 else half, sib_s.at[i], sib_r.at[i], sibling
        )

    def column_in(s):
        k, g = case(s)
        unit = toggled(z, y, x, 0, 0, k)
        piece = out.at[
            unit, pl.ds(g * batch, batch), pl.ds(pl.multiple_of(mine, 16), half), :
        ]
        pltpu.make_async_copy(piece, piece, col_r.at[unit // 4 * batches + g]).wait()
        to_x(s, 0).start()
        to_y(s, 0).start()
        to_sib(s, 0).start()

    def side_in(s):
        from_x(s, 0).wait_recv()
        to_y(s, 1).start()
        to_sib(s, 1).start()
        from_y(s, 0).wait_recv()
        to_x(s, 1).start()
        to_sib(s, 2).start()

    def corner_in(s):
        from_x(s, 1).wait_recv()
        to_sib(s, 3).start()
        from_y(s, 1).wait_recv()
        to_sib(s, 4).start()

    def turn(step, carry):
        @pl.when(step < turns)
        def _():
            column_in(step)

        @pl.when(jnp.logical_and(step >= 1, step < turns + 1))
        def _():
            side_in(step - 1)

        @pl.when(step >= 2)
        def _():
            corner_in(step - 2)

        return carry

    lax.fori_loop(0, turns + 2, turn, 0)

    def settle(s, carry):
        for n in range(2):
            to_x(s, n).wait_send()
            to_y(s, n).wait_send()
        for n in range(5):
            to_sib(s, n).wait_send()
            to_sib(s, n, True).wait_recv()
        return carry

    lax.fori_loop(0, turns, settle, 0)
    for g in range(batches):
        for j in range(2):
            for h in range(2):
                go, _ = own_copy(g, j, h)
                if j == 1:
                    go.wait_send()
                    continue

                @pl.when(jnp.logical_not(jnp.logical_and(rank == core, core == h)))
                def _():
                    go.wait_send()

    for n in range(3):
        for h in range(2):
            hand_out(h, n, True)
            dst = clip_pieces(h)[n][1]
            pltpu.make_async_copy(dst, dst, clip_r.at[3 * h + n]).wait()

    @pl.when(jnp.logical_not(home))
    def _():
        trade.wait_send()

    pltpu.make_async_copy(smalls, smalls, clip_r.at[6]).wait()


def gather_slots(scaled, lat, cot, text, small):
    if not chip_pairs():
        everyone = lax.all_gather(scaled, "dp", axis=0, tiled=True)
        lats, cots = (lax.all_gather(v, "tensor") for v in (lat, cot))
        return everyone, lats, cots, text, small
    dma = pltpu.SemaphoreType.DMA
    turns = 4 * scaled.shape[0] // max(n for n in (1, 2, 3) if scaled.shape[0] % n == 0)
    counts = (7, 7, turns, turns) + (2 * turns,) * 4 + (5 * turns,) * 2
    everyone, *rest = pl.pallas_call(
        gather_kernel,
        out_shape=[
            pltpu.HBM((16,) + scaled.shape, scaled.dtype),
            pltpu.HBM((2,) + lat.shape, lat.dtype),
            pltpu.HBM((2,) + cot.shape, cot.dtype),
            pltpu.HBM(text.shape, text.dtype),
            pltpu.HBM(small.shape, small.dtype),
        ],
        in_specs=[ANY] * 5,
        out_specs=[ANY] * 5,
        scratch_shapes=[dma((n,)) for n in counts],
        compiler_params=pltpu.CompilerParams(
            collective_id=0, has_side_effects=True, vmem_limit_bytes=4 * MIB
        ),
    )(scaled, lat, cot, pltpu.with_memory_space_constraint(text, pltpu.HBM), small)
    return everyone.reshape((-1,) + scaled.shape[1:]), *rest


def toggled(z, y, x, flip_y, flip_x, k):
    high = (z // 2 + k // 2) % 2
    low_bit = (z % 2 + k % 2) % 2
    return (2 * high + low_bit) * 4 + 2 * ((y + flip_y) % 2) + (x + flip_x) % 2


def reduce_kernel(
    kind, block, *refs,
):
    (
        *pieces, rows_in, after_in, dx_in, y_in, da_in, gains, vec_in,
        final, vec_out, result, result_grad, y_other, da_other, from_sib, from_x, from_y, corner_a, corner_b,
        left, right, ring, corners, side_x, side_y, middle, stage, vec_box, end_wide, end_low,
        load_s, stage_s, sib_s, sib_r, x_s, x_r, y_s, y_r, ca_s, ca_r, cb_s, cb_r, f_s, f_r, v_s, v_r,
        end_s, end_r, end_load,
    ) = refs
    chip, core, z, y, x = place_of()
    rank = z % 2
    slots, width, lanes = final.shape[1:]
    half = width // 2
    part = half // 2
    at_x = toggled(z, y, x, 0, 1, 0)
    at_y = toggled(z, y, x, 1, 0, 0)
    sibling = (chip, 1 - core)
    mates = (
        sibling,
        (at_x, core),
        (at_y, core),
        (toggled(z, y, x, 0, 0, 1), core),
        (toggled(z, y, x, 0, 0, 2), core),
    )

    kinds = left.shape[0]
    depth = right.shape[1]
    loads = []
    for i in range(kinds):
        columns = pieces[i].shape[1]
        loads.append(
            pltpu.make_async_copy(pieces[i], left.at[i, :, pl.ds(0, columns)], load_s.at[i])
        )
    first = 0
    blank = []
    for i, piece in enumerate(pieces[kinds:]):
        number, rows = piece.shape[:2]
        loads.append(
            pltpu.make_async_copy(
                piece, right.at[pl.ds(first, number), pl.ds(0, rows), :], load_s.at[kinds + i]
            )
        )
        if rows < depth:
            blank.append((first, number, rows))
        first += number
    for load in loads:
        load.start()
    for start, number, rows in blank:

        def clear(i, carry):
            right[start + i, pl.ds(rows, depth - rows), :] = jnp.zeros(
                (depth - rows, lanes), right.dtype
            )
            return carry

        lax.fori_loop(0, number, clear, 0)
    right[first] = jnp.zeros((depth, lanes), right.dtype)
    for i in range(kinds):
        columns = pieces[i].shape[1]
        if columns < depth:
            left[i, :, pl.ds(columns, depth - columns)] = jnp.zeros(
                (width, depth - columns), left.dtype
            )
    vec_out[...] = vec_in[...]
    greet(chip, core, z, y, x)
    for load in loads:
        load.wait()

    def remote(src, dst, send, recv, device):
        return pltpu.make_async_remote_copy(
            src_ref=src, dst_ref=dst, send_sem=send, recv_sem=recv,
            device_id=device, device_id_type=MESH,
        )

    batch = ring.shape[1]
    batches = slots // batch
    turns = 4 * batches
    deep = corners.shape[0]

    def flips(s):
        return 3 - s // batches

    def sums(q, s, first, terms, total):
        unit = toggled(z, y, x, 1 - q % 2, 1 - q // 2, flips(s))
        base = unit * slots + (s % batches) * batch
        count = total.shape[1]

        def one(i, carry):
            slot = base + i
            rows = pl.ds(pl.multiple_of(first, 128), count)
            acc = jnp.dot(
                left[kind[slot], rows, :], right[block[slot]], preferred_element_type=jnp.float32
            )
            for term in terms:
                acc = acc + term[i].astype(jnp.float32)
            total[i] = acc.astype(total.dtype)
            return carry

        lax.fori_loop(0, batch, one, 0)

    mine, other = core * half, (1 - core) * half

    def sub(ref, first):
        return ref.at[:, pl.ds(first, part), :]

    def sib_copy(q, s):
        i = turns * q + s
        return remote(ring.at[q], from_sib.at[i], sib_s.at[i], sib_r.at[i], sibling)

    def a_copy(s):
        return remote(
            sub(corners.at[s % deep], 0), corner_a.at[s], ca_s.at[s], ca_r.at[s], (at_x, core)
        )

    def b_copy(s):
        return remote(
            sub(corners.at[s % deep], part), corner_b.at[s], cb_s.at[s], cb_r.at[s], (at_y, core)
        )

    def x_copy(s, n):
        rows = pl.ds(n * part, part)
        i = turns * n + s
        return remote(
            side_x.at[s % deep, :, rows, :], from_x.at[s, :, rows, :], x_s.at[i], x_r.at[i],
            (at_x, core),
        )

    def y_copy(s, n):
        rows = pl.ds((1 - n) * part, part)
        i = turns * n + s
        return remote(
            side_y.at[s % deep, :, rows, :], from_y.at[s, :, rows, :], y_s.at[i], y_r.at[i],
            (at_y, core),
        )

    def f_copy(s):
        src = middle.at[s % deep]
        g = s % batches
        dst = final.at[
            z // 2, pl.ds(g * batch, batch), pl.ds(pl.multiple_of(mine, 128), half), :
        ]
        recv = f_r.at[(2 * (z // 2) + core) * batches + g]
        target = (toggled(z, y, x, 0, 0, flips(s)), rank)
        return remote(src, dst, f_s.at[s], recv, target), pltpu.make_async_copy(src, dst, recv)

    def stays(s):
        return jnp.logical_and(s >= turns - batches, rank == core)

    def for_sibling(s, low, high):
        def one(q, carry):
            @pl.when(s >= 1)
            def _():
                sib_copy(q, s - 1).wait_send()

            sums(q, s, other, (), ring.at[q])
            sib_copy(q, s).start()
            return carry

        lax.fori_loop(low, high, one, 0)

    def fetched(q, s):
        i = 2 * q + s % 2
        return pltpu.make_async_copy(from_sib.at[turns * q + s], stage.at[i], stage_s.at[i])

    def fetch(q, s):
        sib_copy(q, s).wait_recv()
        fetched(q, s).start()

    def taken(q, s):
        return stage.at[2 * q + s % 2]

    def corner(s):
        @pl.when(s >= deep)
        def _():
            a_copy(s - deep).wait_send()
            b_copy(s - deep).wait_send()

        fetched(0, s).wait()
        sums(0, s, mine, (taken(0, s),), corners.at[s % deep])
        a_copy(s).start()
        b_copy(s).start()

    def direct_sides(s):
        @pl.when(s >= deep)
        def _():
            for n in range(2):
                x_copy(s - deep, n).wait_send()
                y_copy(s - deep, n).wait_send()

        fetched(1, s).wait()
        sums(1, s, mine, (sub(taken(1, s), 0),), sub(side_x.at[s % deep], 0))
        x_copy(s, 0).start()
        fetched(2, s).wait()
        sums(2, s, mine + part, (sub(taken(2, s), part),), sub(side_y.at[s % deep], part))
        y_copy(s, 0).start()

    def relayed(s):
        return (
            pltpu.make_async_copy(corner_b.at[s], sub(stage.at[8], 0), stage_s.at[8]),
            pltpu.make_async_copy(corner_a.at[s], sub(stage.at[8], part), stage_s.at[9]),
        )

    def relayed_in(s):
        b_copy(s).wait_recv()
        relayed(s)[0].start()
        a_copy(s).wait_recv()
        relayed(s)[1].start()

    def relayed_sides(s):
        relayed(s)[0].wait()
        sums(
            1, s, mine + part, (sub(taken(1, s), part), sub(stage.at[8], 0)),
            sub(side_x.at[s % deep], part),
        )
        x_copy(s, 1).start()
        relayed(s)[1].wait()
        sums(
            2, s, mine, (sub(taken(2, s), 0), sub(stage.at[8], part)), sub(side_y.at[s % deep], 0)
        )
        y_copy(s, 1).start()

    def centre_terms(s):
        return (
            pltpu.make_async_copy(from_x.at[s], stage.at[9], stage_s.at[10]),
            pltpu.make_async_copy(from_y.at[s], stage.at[10], stage_s.at[11]),
        )

    def centre_in(s):
        for n, copies in enumerate((x_copy, y_copy)):
            copies(s, 0).wait_recv()
            copies(s, 1).wait_recv()
            centre_terms(s)[n].start()

    def centre(s):
        @pl.when(s >= deep)
        def _():
            f_copy(s - deep)[0].wait_send()

        fetched(3, s).wait()
        for term in centre_terms(s):
            term.wait()
        sums(3, s, mine, (taken(3, s), stage.at[9], stage.at[10]), middle.at[s % deep])
        go, here = f_copy(s)

        @pl.when(stays(s))
        def _():
            here.start()

        @pl.when(jnp.logical_not(stays(s)))
        def _():
            go.start()

    home = rank == core
    pair_device = (toggled(z, y, x, 0, 0, 1), core)
    ends = [
        remote(y_in, y_other, end_s.at[0], end_r.at[0], pair_device),
        remote(da_in, da_other, end_s.at[1], end_r.at[1], pair_device),
        remote(end_low.at[0], result, end_s.at[2], end_r.at[2], sibling),
        remote(end_wide.at[0], result_grad, end_s.at[3], end_r.at[3], sibling),
    ]
    end_loads = [
        pltpu.make_async_copy(src, dst, end_load.at[i])
        for i, (src, dst) in enumerate(
            (
                (rows_in, end_wide.at[0]), (after_in, end_wide.at[1]), (dx_in, end_wide.at[2]),
                (y_in, end_low.at[0]), (da_in, end_low.at[1]),
                (y_other, end_low.at[2]), (da_other, end_low.at[3]),
            )
        )
    ]
    end_stores = [
        pltpu.make_async_copy(end_low.at[0], result, end_load.at[7]),
        pltpu.make_async_copy(end_wide.at[0], result_grad, end_load.at[8]),
    ]

    def finish_rows():
        for n in range(2):
            ends[n].wait_recv()
            end_loads[5 + n].start()
        for load in end_loads:
            load.wait()
        tall = 16

        def one(i, carry):
            at = pl.ds(pl.multiple_of(i * tall, tall), tall)
            y_all = end_low[0, at].astype(F32) + end_low[2, at].astype(F32) + gains[2:3]
            end_low[0, at] = (end_wide[1, at] + gains[0:1] * y_all).astype(end_low.dtype)
            da = end_low[1, at].astype(F32) + end_low[3, at].astype(F32)
            back, _ = normed_back(end_wide[0, at], da * (1.0 + gains[1:2]))
            end_wide[0, at] = end_wide[2, at] + back
            return carry

        lax.fori_loop(0, rows_in.shape[0] // tall, one, 0)
        ends[2].start()
        ends[3].start()
        for store in end_stores:
            store.start()

    @pl.when(jnp.logical_not(home))
    def _():
        ends[0].start()
        ends[1].start()

    def vec_copy(i):
        return remote(vec_out, vec_box.at[i], v_s.at[i], v_r.at[i], mates[i])

    def turn(step, carry):
        for i in range(5):

            @pl.when(step == 2 * i)
            def _():
                vec_copy(i).start()

        @pl.when(step + 1 < turns)
        def _():
            corner(step + 1)
            direct_sides(step + 1)

        @pl.when(step + 2 < turns)
        def _():
            for_sibling(step + 2, 0, 4)

        @pl.when(step < turns)
        def _():
            relayed_in(step)

        @pl.when(step >= 1)
        def _():
            centre_in(step - 1)

        @pl.when(step < turns)
        def _():
            relayed_sides(step)

        @pl.when(step >= 1)
        def _():
            centre(step - 1)

        @pl.when(step + 2 < turns)
        def _():
            for q in range(3):
                fetch(q, step + 2)

        @pl.when(step + 1 < turns)
        def _():
            fetch(3, step + 1)

        @pl.when(jnp.logical_and(step == 1, home))
        def _():
            for load in end_loads[:5]:
                load.start()

        @pl.when(jnp.logical_and(step == 3, home))
        def _():
            finish_rows()

        for i in range(5):

            @pl.when(step == 2 * i + 1)
            def _():
                vec_copy(i).wait()
                vec_out[...] = vec_out[...] + vec_box[i]

        return carry

    for_sibling(0, 0, 2)
    fetch(0, 0)
    corner(0)
    for_sibling(0, 2, 4)
    for q in range(1, 4):
        fetch(q, 0)
    direct_sides(0)
    for_sibling(1, 0, 4)
    for q in range(3):
        fetch(q, 1)
    lax.fori_loop(0, turns + 1, turn, 0)
    for q in range(4):
        sib_copy(q, turns - 1).wait_send()

    def settle(i, carry):
        s = turns - deep + i
        a_copy(s).wait_send()
        b_copy(s).wait_send()
        for n in range(2):
            x_copy(s, n).wait_send()
            y_copy(s, n).wait_send()

        @pl.when(jnp.logical_not(stays(s)))
        def _():
            f_copy(s)[0].wait_send()

        return carry

    lax.fori_loop(0, deep, settle, 0)

    @pl.when(home)
    def _():
        ends[2].wait_send()
        ends[3].wait_send()
        for store in end_stores:
            store.wait()

    @pl.when(jnp.logical_not(home))
    def _():
        ends[0].wait_send()
        ends[1].wait_send()
        ends[2].wait_recv()
        ends[3].wait_recv()

    for plane in range(2):
        for h in range(2):
            for g in range(batches):
                piece = final.at[plane, pl.ds(g * batch, batch), pl.ds(h * half, half), :]
                recv = f_r.at[(2 * plane + h) * batches + g]
                pltpu.make_async_copy(piece, piece, recv).wait()


def reduce_slots(holder, kinds, rows, columns, vector, ends, gains, slot_count):
    if not chip_pairs():
        grads = slot_grads(holder, kinds, [r.T for r in rows], columns)
        total = lax.psum_scatter(grads, "dp", scatter_dimension=0, tiled=True)
        x, after, dx, y_part, da_part = ends
        y_all, da_all = (
            v.astype(F32) + pair_swap(v).astype(F32) for v in (y_part, da_part)
        )
        result = (after + gains[0] * (y_all + gains[2])).astype(BF16)
        back, _ = normed_back(x, da_all * (1.0 + gains[1]))
        return total[None], lax.psum(vector, ("dp", "tensor")), result, dx + back
    left = rows
    width, depth = left[0].shape[0], max(r.shape[1] for r in rows)
    lanes = columns[0].shape[2]
    tiles = sum(c.shape[0] for c in columns)
    block = jnp.where(holder >= 0, holder, tiles)
    kind = kinds[jnp.maximum(holder, 0)]
    half = width // 2
    dma = pltpu.SemaphoreType.DMA
    scalars = pl.BlockSpec(memory_space=pltpu.SMEM)
    inside = pl.BlockSpec(memory_space=pltpu.VMEM)
    low = jnp.bfloat16

    batch = max(n for n in (1, 2, 3) if slot_count % n == 0)
    turns = 4 * slot_count // batch
    deep = 3

    def room(count, tall):
        return pltpu.HBM((count, batch, tall, lanes), low)

    def slab(count):
        return pltpu.VMEM((count, batch, half, lanes), low)

    outs = pl.pallas_call(
        reduce_kernel,
        out_shape=[
            pltpu.HBM((2, slot_count, width, lanes), low),
            jax.ShapeDtypeStruct(vector.shape, vector.dtype),
            pltpu.HBM(ends[0].shape, low), pltpu.HBM(ends[0].shape, F32),
            pltpu.HBM(ends[0].shape, low), pltpu.HBM(ends[0].shape, low),
            room(4 * turns, half), room(turns, half), room(turns, half),
            room(turns, half // 2), room(turns, half // 2),
        ],
        in_specs=[scalars, scalars] + [ANY] * (len(left) + len(columns) + 5) + [inside] * 2,
        out_specs=[ANY, inside] + [ANY] * 9,
        scratch_shapes=[
            pltpu.VMEM((len(left), width, depth), low),
            pltpu.VMEM((tiles + 1, depth, lanes), low),
            slab(4), slab(deep), slab(deep), slab(deep), slab(deep), slab(11),
            pltpu.VMEM((5,) + vector.shape, vector.dtype),
            pltpu.VMEM((3,) + ends[0].shape, F32),
            pltpu.VMEM((4,) + ends[0].shape, low),
        ]
        + [
            dma((n,))
            for n in (len(left) + len(columns), 12)
            + (4 * turns,) * 2
            + (2 * turns,) * 4
            + (turns,) * 6
            + (5, 5, 4, 4, 9)
        ],
        compiler_params=pltpu.CompilerParams(
            collective_id=1, has_side_effects=True, vmem_limit_bytes=58 * MIB
        ),
    )(
        kind,
        block,
        *[pltpu.with_memory_space_constraint(v, pltpu.HBM) for v in (*left, *columns, *ends)],
        gains,
        vector,
    )
    return outs[:4]


def kind_of_blocks(tile_count, heads_here, blocks_here):
    number = jnp.arange(tile_count)
    kind = number // heads_here
    table = jnp.array([0, 0, 0, 1, 2, 3, 3, 4], jnp.int32)
    late = jnp.where(number < 8 * heads_here + blocks_here, 5, 6)
    return jnp.where(number < 8 * heads_here, table[jnp.minimum(kind, 7)], late).astype(jnp.int32)


def slot_grads(holder, kinds, rows, columns):
    depth = max(r.shape[0] for r in rows)

    def deep(value, axis):
        room = [(0, 0)] * value.ndim
        room[axis] = (0, depth - value.shape[axis])
        return jnp.pad(value, room)

    left = jnp.stack([deep(r, 0) for r in rows])
    right = jnp.concatenate([deep(c, 1) for c in columns], 0)
    slots = holder.shape[0]
    used = (holder >= 0).astype(jnp.int32)
    block = jnp.maximum(holder, 0)
    kind = kinds[block]
    width = rows[0].shape[1]
    lanes = right.shape[2]

    def multiply(kind_ref, block_ref, used_ref, left_ref, right_ref, out_ref):
        slot = pl.program_id(0)

        @pl.when(used_ref[slot] == 1)
        def _():
            out_ref[0] = lax.dot_general(
                left_ref[kind_ref[slot]],
                right_ref[0],
                (((0,), (0,)), ((), ())),
                preferred_element_type=jnp.float32,
            ).astype(out_ref.dtype)

        @pl.when(used_ref[slot] == 0)
        def _():
            out_ref[...] = jnp.zeros_like(out_ref)

    return pl.pallas_call(
        multiply,
        grid_spec=pltpu.PrefetchScalarGridSpec(
            num_scalar_prefetch=3,
            grid=(slots,),
            in_specs=[
                pl.BlockSpec(left.shape, lambda s, kd, b, u: (0, 0, 0)),
                pl.BlockSpec((1, depth, lanes), lambda s, kd, b, u: (b[s], 0, 0)),
            ],
            out_specs=pl.BlockSpec((1, width, lanes), lambda s, kd, b, u: (s, 0, 0)),
        ),
        out_shape=jax.ShapeDtypeStruct((slots, width, lanes), jnp.bfloat16),
        compiler_params=pltpu.CompilerParams(vmem_limit_bytes=48 * MIB),
    )(kind, block, used, left, right)


def adam_slots(planes, master, moment_one, moment_two, slot_scale, filled):
    count, slot_count, width, lanes = planes.shape

    def step(scale_ref, fill_ref, grads, weight, one, two, new_weight, new_one, new_two, grad_box, boxes, reads, writes):
        sources = (weight, one, two)
        targets = (new_weight, new_one, new_two)

        def load(slot):
            return [
                pltpu.make_async_copy(src.at[0, slot], boxes.at[n, slot], reads.at[n, slot])
                for n, src in enumerate(sources)
            ] + [
                pltpu.make_async_copy(
                    grads.at[n, slot], grad_box.at[n, slot], reads.at[3 + n, slot]
                )
                for n in range(count)
            ]

        def store(slot):
            return [
                pltpu.make_async_copy(boxes.at[n, slot], dst.at[0, slot], writes.at[n, slot])
                for n, dst in enumerate(targets)
            ]

        def begin(slot, carry):
            for copy in load(slot):
                copy.start()
            return carry

        def work(slot, carry):
            for copy in load(slot):
                copy.wait()

            @pl.when(fill_ref[slot] == 1)
            def _():
                total = grad_box[0, slot].astype(jnp.float32)
                for n in range(1, count):
                    total = total + grad_box[n, slot].astype(jnp.float32)
                results = adam_step(
                    boxes[0, slot], total * scale_ref[slot], boxes[1, slot], boxes[2, slot],
                    TILE_RATE, TILE_DECAY,
                )
                for n, value in enumerate(results):
                    boxes[n, slot] = value

            for copy in store(slot):
                copy.start()
            return carry

        def finish(slot, carry):
            for copy in store(slot):
                copy.wait()
            return carry

        for part in (begin, work, finish):
            lax.fori_loop(0, slot_count, part, 0)

    scalars = pl.BlockSpec(memory_space=pltpu.SMEM)
    return pl.pallas_call(
        step,
        in_specs=[scalars, scalars] + [ANY] * 4,
        out_specs=[ANY] * 3,
        out_shape=[pltpu.HBM(master.shape, jnp.float32)] * 3,
        scratch_shapes=[
            pltpu.VMEM((count, slot_count, width, lanes), planes.dtype),
            pltpu.VMEM((3, slot_count, width, lanes), jnp.float32),
            pltpu.SemaphoreType.DMA((3 + count, slot_count)),
            pltpu.SemaphoreType.DMA((3, slot_count)),
        ],
        compiler_params=pltpu.CompilerParams(vmem_limit_bytes=40 * MIB),
    )(
        slot_scale,
        filled.astype(jnp.int32),
        *[
            pltpu.with_memory_space_constraint(v, pltpu.HBM)
            for v in (planes, master, moment_one, moment_two)
        ],
    )


SCALING = HEAD ** (-0.5)
BF16 = jnp.bfloat16
F32 = jnp.float32


def nn(left, right):
    return jnp.dot(left, right, preferred_element_type=F32)


def nt(left, right):
    return lax.dot_general(left, right, (((1,), (1,)), ((), ())), preferred_element_type=F32)


def tn(left, right):
    return lax.dot_general(left, right, (((0,), (0,)), ((), ())), preferred_element_type=F32)


def normed(rows):
    centre = rows - jnp.mean(rows, -1, keepdims=True)
    inverse = lax.rsqrt(jnp.mean(centre * centre, -1, keepdims=True) + NORM_EPS)
    return centre * inverse, inverse


def normed_back(rows, grad):
    unit, inverse = normed(rows)
    mean = jnp.mean(grad, -1, keepdims=True)
    return (grad - mean - unit * jnp.mean(grad * unit, -1, keepdims=True)) * inverse, unit


def total_of(rows):
    return jnp.sum(rows, 0, keepdims=True)


def turned(rows, cos_tab, sin_tab):
    even = lax.broadcasted_iota(jnp.int32, rows.shape, 1) % 2 == 0
    partner = jnp.where(even, pltpu.roll(rows, HEAD - 1, 1), pltpu.roll(rows, 1, 1))
    return rows * cos_tab + partner * sin_tab


def wide(column):
    return jnp.broadcast_to(column, (column.shape[0], HEAD))


def pack_sums(for_rows, for_text=None):
    out = wide(for_rows)
    if for_text is None:
        return out
    lane = lax.broadcasted_iota(jnp.int32, out.shape, 1)
    count = for_text.shape[0] // 2
    rest = jnp.zeros((out.shape[0] - count, HEAD), F32)
    first = jnp.concatenate([wide(for_text[:count]), rest], 0)
    second = jnp.concatenate([wide(for_text[count:]), rest], 0)
    return jnp.where(lane < 32, out, jnp.where(lane < 64, first, second))


def unpack_text(sums, count):
    return jnp.concatenate([sums[: count // 2, 32:33], sums[: count // 2, 64:65]], 0)


def softmax(scores):
    expo = jnp.exp(scores - jnp.max(scores, -1, keepdims=True))
    return expo / jnp.sum(expo, -1, keepdims=True)


def self_scores(query_low, key_low, tokens):
    scores = nt(query_low, key_low) * SCALING
    lane = lax.broadcasted_iota(jnp.int32, scores.shape, 1)
    return jnp.where(lane < tokens, scores, -1e30)


def whole(array):
    zeros = (0,) * len(array.shape)
    return pl.BlockSpec(array.shape, lambda *_: zeros)


def block_at(first, stride=1):
    return pl.BlockSpec((1, D, HEAD), lambda i, where: (where[first + stride * i], 0, 0))


def call(body, places, grid, ins, outs, scratch=(), vmem=24):
    specs = [spec if spec is not None else whole(array) for array, spec in ins]
    shapes = [pltpu.HBM(shape, kind) for shape, kind, _ in outs]
    out_specs = [
        spec if spec is not None else whole(shape) for (_, _, spec), shape in zip(outs, shapes)
    ]
    return pl.pallas_call(
        body,
        grid_spec=pltpu.PrefetchScalarGridSpec(
            num_scalar_prefetch=1,
            grid=(grid,),
            in_specs=specs,
            out_specs=out_specs,
            scratch_shapes=list(scratch),
        ),
        out_shape=shapes,
        compiler_params=pltpu.CompilerParams(vmem_limit_bytes=vmem * MIB),
    )(places, *[pltpu.with_memory_space_constraint(array, pltpu.HBM) for array, _ in ins])


def head_lanes(rows, per=1):
    return pl.BlockSpec((rows, per * HEAD), lambda h, *_: (0, h))


def heads_per_step(heads, most):
    return max(n for n in (1, 2, 3, 6) if heads % n == 0 and n <= most)


def lane_group(ref, j):
    return ref[:, j * HEAD : (j + 1) * HEAD]


def joined(refs):
    return jnp.concatenate([ref[0] for ref in refs], 1)


def project_self(places, everyone, rows, mod, vecs, heads):
    count = rows.shape[0]
    span = heads * HEAD

    def body(_, rows_ref, mod_ref, vec_ref, *refs):
        weights, (low, pre, value, sums, acc) = refs[:heads], refs[heads:]
        i = pl.program_id(0)

        @pl.when(i == 0)
        def _():
            unit, _ = normed(rows_ref[...])
            low[...] = (unit * (1.0 + mod_ref[1:2]) + mod_ref[0:1]).astype(BF16)

        made = nn(low[...], joined(weights))

        @pl.when(i == 0)
        def _():
            q = made + vec_ref[0:1]
            pre[0] = q
            acc[...] = wide(jnp.sum(q * q, -1, keepdims=True))

        @pl.when(i == 1)
        def _():
            k = made + vec_ref[1:2]
            pre[0] = k
            lane = lax.broadcasted_iota(jnp.int32, acc.shape, 1)
            sums[...] = jnp.where(lane < 64, acc[...], wide(jnp.sum(k * k, -1, keepdims=True)))

        @pl.when(i == 2)
        def _():
            value[...] = (made + vec_ref[2:3]).astype(BF16)

    return call(
        body, places, 3,
        [(rows, None), (mod, None), (vecs, None)]
        + [(everyone, block_at(h, heads)) for h in range(heads)],
        [
            ((count, D), BF16, None),
            ((2, count, span), F32, pl.BlockSpec((1, count, span), lambda i, _: (jnp.minimum(i, 1), 0, 0))),
            ((count, span), BF16, None),
            ((count, HEAD), F32, None),
        ],
        [pltpu.VMEM((count, HEAD), F32)],
    )


def attend_self(places, everyone, pre, value, sums, other, vecs, cos_tab, sin_tab, heads, tokens):
    count = value.shape[0]
    per = heads_per_step(heads, 2)
    steps = heads // per

    def body(_, pre_ref, value_ref, sum_ref, other_ref, vec_ref, cos_ref, sin_ref, *refs):
        weights, (q_ref, k_ref, o_ref, y_ref, acc) = refs[:per], refs[per:]
        h = pl.program_id(0)
        total = sum_ref[...] + other_ref[...]
        q_inv = lax.rsqrt(total[:, 0:1] / D + NORM_EPS)
        k_inv = lax.rsqrt(total[:, 64:65] / D + NORM_EPS)
        cos, sin = cos_ref[...], sin_ref[...]
        outs = []
        for j in range(per):
            lanes = slice(j * HEAD, (j + 1) * HEAD)
            q = turned(pre_ref[0, :, lanes] * q_inv * vec_ref[3:4, lanes], cos, sin).astype(BF16)
            k = turned(pre_ref[1, :, lanes] * k_inv * vec_ref[4:5, lanes], cos, sin).astype(BF16)
            q_ref[:, lanes] = q
            k_ref[:, lanes] = k
            chance = softmax(self_scores(q, k, tokens))
            out = nn(chance.astype(BF16), value_ref[:, lanes]).astype(BF16)
            o_ref[j] = out
            outs.append(out)
        part = nt(jnp.concatenate(outs, 1), joined(weights))

        @pl.when(h == 0)
        def _():
            acc[...] = part

        @pl.when(h > 0)
        def _():
            acc[...] = acc[...] + part

        @pl.when(h == steps - 1)
        def _():
            y_ref[...] = acc[...].astype(BF16)

    lanes = head_lanes(count, per)
    return call(
        body, places, steps,
        [
            (pre, pl.BlockSpec((2, count, per * HEAD), lambda h, _: (0, 0, h))),
            (value, lanes), (sums, None), (other, None),
            (vecs, head_lanes(vecs.shape[0], per)), (cos_tab, None), (sin_tab, None),
        ]
        + [(everyone, block_at(3 * heads + j, per)) for j in range(per)],
        [
            (value.shape, BF16, lanes),
            (value.shape, BF16, lanes),
            ((heads, count, HEAD), BF16, pl.BlockSpec((per, count, HEAD), lambda h, _: (h, 0, 0))),
            ((count, D), BF16, None),
        ],
        [pltpu.VMEM((count, D), F32)],
    )


def project_text(places, everyone, context, vecs, heads):
    count = context.shape[0]
    span = heads * HEAD

    def body(_, text_ref, vec_ref, *refs):
        weights, (key, value, sums) = refs[:heads], refs[heads:]
        i = pl.program_id(0)
        made = nn(text_ref[...], joined(weights))

        @pl.when(i == 0)
        def _():
            k = made + vec_ref[6:7]
            key[...] = k
            sums[...] = wide(jnp.sum(k * k, -1, keepdims=True))

        @pl.when(i == 1)
        def _():
            value[...] = (made + vec_ref[7:8]).astype(BF16)

    return call(
        body, places, 2,
        [(context, None), (vecs, None)]
        + [(everyone, block_at(5 * heads + h, heads)) for h in range(heads)],
        [((count, span), F32, None), ((count, span), BF16, None), ((count, HEAD), F32, None)],
    )


def project_cross(places, everyone, rows, part, other, mod, shared, vecs, text_sums, heads):
    count = rows.shape[0]
    span = heads * HEAD
    text = text_sums.shape[0]

    def body(_, rows_ref, part_ref, other_ref, mod_ref, shared_ref, vec_ref, text_ref, *refs):
        weights, (branch, after, low, pre, sums) = refs[:heads], refs[heads:]
        y = part_ref[...].astype(F32) + other_ref[...].astype(F32) + shared_ref[0:1]
        branch[...] = y
        x = rows_ref[...] + mod_ref[2:3] * y
        after[...] = x
        unit, _ = normed(x)
        a = (unit * shared_ref[3:4] + shared_ref[4:5]).astype(BF16)
        low[...] = a
        q = nn(a, joined(weights)) + vec_ref[5:6]
        pre[...] = q
        sums[...] = pack_sums(jnp.sum(q * q, -1, keepdims=True), text_ref[:, 0:1])

    return call(
        body, places, 1,
        [(v, None) for v in (rows, part, other, mod, shared, vecs, text_sums)]
        + [(everyone, block_at(4 * heads + h)) for h in range(heads)],
        [
            ((count, D), F32, None),
            ((count, D), F32, None),
            ((count, D), BF16, None),
            ((count, span), F32, None),
            ((count, HEAD), F32, None),
        ],
    )


def attend_cross(places, everyone, pre, key_pre, value, sums, other, vecs, heads):
    count, text = pre.shape[0], value.shape[0]
    per = heads_per_step(heads, 6)
    steps = heads // per

    def body(_, pre_ref, key_ref, value_ref, sum_ref, other_ref, vec_ref, *refs):
        weights, (q_ref, k_ref, o_ref, y_ref, acc) = refs[:per], refs[per:]
        h = pl.program_id(0)
        total = sum_ref[...] + other_ref[...]
        q_inv = lax.rsqrt(total[:, 0:1] / D + NORM_EPS)
        k_inv = lax.rsqrt(unpack_text(total, text) / D + NORM_EPS)
        outs = []
        for j in range(per):
            lanes = slice(j * HEAD, (j + 1) * HEAD)
            q = (pre_ref[:, lanes] * q_inv * vec_ref[8:9, lanes]).astype(BF16)
            k = (key_ref[:, lanes] * k_inv * vec_ref[9:10, lanes]).astype(BF16)
            q_ref[:, lanes] = q
            k_ref[:, lanes] = k
            chance = softmax(nt(q, k) * SCALING)
            out = nn(chance.astype(BF16), value_ref[:, lanes]).astype(BF16)
            o_ref[j] = out
            outs.append(out)
        part = nt(jnp.concatenate(outs, 1), joined(weights))

        @pl.when(h == 0)
        def _():
            acc[...] = part

        @pl.when(h > 0)
        def _():
            acc[...] = acc[...] + part

        @pl.when(h == steps - 1)
        def _():
            y_ref[...] = acc[...].astype(BF16)

    return call(
        body, places, steps,
        [
            (pre, head_lanes(count, per)), (key_pre, head_lanes(text, per)),
            (value, head_lanes(text, per)), (sums, None), (other, None),
            (vecs, head_lanes(vecs.shape[0], per)),
        ]
        + [(everyone, block_at(7 * heads + j, per)) for j in range(per)],
        [
            (pre.shape, BF16, head_lanes(count, per)),
            (value.shape, BF16, head_lanes(text, per)),
            ((heads, count, HEAD), BF16, pl.BlockSpec((per, count, HEAD), lambda h, _: (h, 0, 0))),
            ((count, D), BF16, None),
        ],
        [pltpu.VMEM((count, D), F32)],
        vmem=40,
    )


def hidden_group(blocks):
    return max(g for g in (7, 5, 4, 3, 2, 1) if blocks % g == 0)


def block_lanes(where, everyone, held, sems, first, group, steps):
    i = pl.program_id(0)

    def fetch(step, act):
        slot = step % 3
        for j in range(group):
            copy = pltpu.make_async_copy(
                everyone.at[where[first + step * group + j]],
                held.at[slot, :, pl.ds(j * HEAD, HEAD)],
                sems.at[slot, j],
            )
            copy.start() if act else copy.wait()

    @pl.when(i == 0)
    def _():
        fetch(0, True)
        if steps > 1:
            fetch(1, True)

    @pl.when(i + 2 < steps)
    def _():
        fetch(i + 2, True)

    fetch(i, False)
    return held[i % 3]


def lanes_scratch(group):
    return [pltpu.VMEM((3, D, group * HEAD), BF16), pltpu.SemaphoreType.DMA((3, group))]


def hidden_back(places, everyone, mod, cot, heads, blocks):
    count = cot.shape[0]
    group = hidden_group(blocks)
    steps = blocks // group

    def body(where, weights, mod_ref, cot_ref, grad, out, held, sems):
        @pl.when(pl.program_id(0) == 0)
        def _():
            grad[...] = (mod_ref[5:6] * cot_ref[...]).astype(BF16)

        down = block_lanes(where, weights, held, sems, 8 * heads + blocks, group, steps)
        out[...] = nn(grad[...], down).astype(BF16)

    return call(
        body, places, steps,
        [(everyone, ANY), (mod, None), (cot, None)],
        [
            ((count, D), BF16, None),
            ((count, blocks * HEAD), BF16, pl.BlockSpec((count, group * HEAD), lambda i, _: (0, i))),
        ],
        lanes_scratch(group),
        vmem=40,
    )


def hidden_both(places, everyone, after_one, part, other, mod, shared, d_act, up_bias, heads, blocks):
    count = after_one.shape[0]
    group = hidden_group(blocks)
    steps = blocks // group
    span = group * HEAD

    def body(where, weights, after_ref, part_ref, other_ref, mod_ref, shared_ref, d_ref, bias_ref, after, low, hidden, d_hidden, d_bias, da_ref, acc, held, sems):
        i = pl.program_id(0)

        @pl.when(i == 0)
        def _():
            x = after_ref[...] + part_ref[...].astype(F32) + other_ref[...].astype(F32)
            x = x + shared_ref[1:2]
            after[...] = x
            unit, _ = normed(x)
            low[...] = (unit * (1.0 + mod_ref[4:5]) + mod_ref[3:4]).astype(BF16)
            acc[...] = jnp.zeros_like(acc)

        up = block_lanes(where, weights, held, sems, 8 * heads, group, steps)
        pre = nn(low[...], up) + bias_ref[...]
        square = pre * pre
        bent = jnp.tanh(GELU_COEF * (pre + 0.044715 * pre * square))
        act = (0.5 * pre * (1.0 + bent)).astype(BF16)
        slope = 0.5 * (1.0 + bent) + 0.5 * pre * (1.0 - bent * bent) * (
            GELU_COEF * (1.0 + 3.0 * 0.044715 * square)
        )
        dh = (d_ref[...].astype(F32) * slope).astype(BF16)
        d_bias[...] = total_of(dh.astype(F32))
        for j in range(group):
            hidden[j] = act[:, j * HEAD : (j + 1) * HEAD]
            d_hidden[j] = dh[:, j * HEAD : (j + 1) * HEAD]
        acc[...] = acc[...] + nt(dh, up)

        @pl.when(i == steps - 1)
        def _():
            da_ref[...] = acc[...].astype(BF16)

    tall = pl.BlockSpec((group, count, HEAD), lambda i, _: (i, 0, 0))
    flat = pl.BlockSpec((1, span), lambda i, _: (0, i))
    return call(
        body, places, steps,
        [(everyone, ANY)]
        + [(v, None) for v in (after_one, part, other, mod, shared)]
        + [(d_act, pl.BlockSpec((count, span), lambda i, _: (0, i))), (up_bias, flat)],
        [
            ((count, D), F32, None),
            ((count, D), BF16, None),
            ((blocks, count, HEAD), BF16, tall),
            ((blocks, count, HEAD), BF16, tall),
            (up_bias.shape, F32, flat),
            ((count, D), BF16, None),
        ],
        [pltpu.VMEM((count, D), F32)] + lanes_scratch(group),
        vmem=40,
    )


def hidden_out(places, everyone, hidden, heads):
    blocks, count = hidden.shape[:2]
    group = hidden_group(blocks)
    steps = blocks // group

    def body(where, weights, hidden_ref, y_ref, acc, held, sems):
        i = pl.program_id(0)
        down = block_lanes(where, weights, held, sems, 8 * heads + blocks, group, steps)
        part = nt(jnp.concatenate([hidden_ref[j] for j in range(group)], 1), down)

        @pl.when(i == 0)
        def _():
            acc[...] = part

        @pl.when(i > 0)
        def _():
            acc[...] = acc[...] + part

        @pl.when(i == steps - 1)
        def _():
            y_ref[...] = acc[...].astype(BF16)

    return call(
        body, places, steps,
        [(everyone, ANY), (hidden, pl.BlockSpec((group, count, HEAD), lambda i, _: (i, 0, 0)))],
        [((count, D), BF16, None)],
        [pltpu.VMEM((count, D), F32)] + lanes_scratch(group),
        vmem=40,
    )[0]


def cross_back(places, everyone, cot, after_two, part, other, mod, query, key, value, pre, key_pre, vecs, heads):
    count, text = query.shape[0], key.shape[0]
    per = heads_per_step(heads, 6)
    steps = heads // per

    def body(_, cot_ref, after_ref, part_ref, other_ref, mod_ref, q_ref, k_ref, v_ref, pre_ref, key_ref, vec_ref, *refs):
        weights, (dx_ref, low_ref, dq_ref, dk_ref, dv_ref, sums, q_acc, k_acc) = refs[:per], refs[per:]
        h = pl.program_id(0)

        @pl.when(h == 0)
        def _():
            da = part_ref[...].astype(F32) + other_ref[...].astype(F32)
            back, _ = normed_back(after_ref[...], da * (1.0 + mod_ref[4:5]))
            dx = cot_ref[...] + back
            dx_ref[...] = dx
            low_ref[...] = dx.astype(BF16)
            q_acc[...] = jnp.zeros_like(q_acc)
            k_acc[...] = jnp.zeros_like(k_acc)

        do_all = nn(low_ref[...], joined(weights)).astype(BF16)
        q_sums, k_sums = 0.0, 0.0
        for j in range(per):
            lanes = slice(j * HEAD, (j + 1) * HEAD)
            do = do_all[:, lanes]
            q, k = q_ref[:, lanes], k_ref[:, lanes]
            chance = softmax(nt(q, k) * SCALING)
            dp = nt(do, v_ref[:, lanes])
            ds = (chance * (dp - jnp.sum(chance * dp, -1, keepdims=True))).astype(BF16)
            dv_ref[j] = tn(chance.astype(BF16), do).astype(BF16)
            dq = nn(ds, k) * SCALING
            dk = tn(ds, q) * SCALING
            dq_ref[:, lanes] = dq
            dk_ref[:, lanes] = dk
            q_sums += pre_ref[:, lanes] * vec_ref[8:9, lanes] * dq
            k_sums += key_ref[:, lanes] * vec_ref[9:10, lanes] * dk
        q_acc[...] = q_acc[...] + q_sums
        k_acc[...] = k_acc[...] + k_sums

        @pl.when(h == steps - 1)
        def _():
            sums[...] = pack_sums(
                jnp.sum(q_acc[...], -1, keepdims=True), jnp.sum(k_acc[...], -1, keepdims=True)
            )

    return call(
        body, places, steps,
        [(v, None) for v in (cot, after_two, part, other, mod)]
        + [
            (query, head_lanes(count, per)), (key, head_lanes(text, per)),
            (value, head_lanes(text, per)), (pre, head_lanes(count, per)),
            (key_pre, head_lanes(text, per)), (vecs, head_lanes(vecs.shape[0], per)),
        ]
        + [(everyone, block_at(7 * heads + j, per)) for j in range(per)],
        [
            ((count, D), F32, None),
            ((count, D), BF16, None),
            (query.shape, F32, head_lanes(count, per)),
            (key.shape, F32, head_lanes(text, per)),
            ((heads, text, HEAD), BF16, pl.BlockSpec((per, text, HEAD), lambda h, _: (h, 0, 0))),
            ((count, HEAD), F32, None),
        ],
        [pltpu.VMEM((count, HEAD), F32), pltpu.VMEM((text, HEAD), F32)],
        vmem=48,
    )


def norm_grad(pre, inverse, gain, incoming, total):
    grad = inverse * (gain * incoming) - pre * (inverse * inverse * inverse) * (total / D)
    low = grad.astype(BF16)
    return low, total_of(low.astype(F32)), total_of(incoming * pre * inverse)


def cross_back_rows(places, everyone, pre, key_pre, dq, dk, dv, squares, squares_other, sums, sums_other, vecs, heads):
    count, text = pre.shape[0], key_pre.shape[0]
    per = heads_per_step(heads, 6)
    steps = heads // per

    def body(_, pre_ref, key_ref, dq_ref, dk_ref, dv_ref, sq_ref, sqo_ref, sum_ref, sumo_ref, vec_ref, *refs):
        weights, (gq_ref, gk_ref, vec_out, da_ref, acc) = refs[:per], refs[per:]
        h = pl.program_id(0)
        squares_all = sq_ref[...] + sqo_ref[...]
        total = sum_ref[...] + sumo_ref[...]
        q_inv = lax.rsqrt(squares_all[:, 0:1] / D + NORM_EPS)
        k_inv = lax.rsqrt(unpack_text(squares_all, text) / D + NORM_EPS)
        q_total, k_total = total[:, 0:1], unpack_text(total, text)
        lows = []
        for j in range(per):
            lanes = slice(j * HEAD, (j + 1) * HEAD)
            low_q, bias_q, gain_q = norm_grad(
                pre_ref[:, lanes], q_inv, vec_ref[8:9, lanes], dq_ref[:, lanes], q_total
            )
            low_k, bias_k, gain_k = norm_grad(
                key_ref[:, lanes], k_inv, vec_ref[9:10, lanes], dk_ref[:, lanes], k_total
            )
            gq_ref[j] = low_q
            gk_ref[j] = low_k
            lows.append(low_q)
            bias_v = total_of(dv_ref[j].astype(F32))
            vec_out[:, lanes] = jnp.concatenate(
                [bias_q, bias_k, bias_v, gain_q, gain_k, jnp.zeros((3, HEAD), F32)], 0
            )
        part = nt(jnp.concatenate(lows, 1), joined(weights))

        @pl.when(h == 0)
        def _():
            acc[...] = part

        @pl.when(h > 0)
        def _():
            acc[...] = acc[...] + part

        @pl.when(h == steps - 1)
        def _():
            da_ref[...] = acc[...].astype(BF16)

    tall = pl.BlockSpec((per, count, HEAD), lambda h, _: (h, 0, 0))
    tall_text = pl.BlockSpec((per, text, HEAD), lambda h, _: (h, 0, 0))
    return call(
        body, places, steps,
        [
            (pre, head_lanes(count, per)), (key_pre, head_lanes(text, per)),
            (dq, head_lanes(count, per)), (dk, head_lanes(text, per)), (dv, tall_text),
            (squares, None), (squares_other, None), (sums, None), (sums_other, None),
            (vecs, head_lanes(vecs.shape[0], per)),
        ]
        + [(everyone, block_at(4 * heads + j, per)) for j in range(per)],
        [
            ((heads, count, HEAD), BF16, tall),
            ((heads, text, HEAD), BF16, tall_text),
            ((8, heads * HEAD), F32, head_lanes(8, per)),
            ((count, D), BF16, None),
        ],
        [pltpu.VMEM((count, D), F32)],
        vmem=40,
    )


def self_back(places, everyone, dx_two, after_one, part, other, mod, shared, branch, query, key, value, pre, vecs, cos_tab, sin_tab, heads, tokens):
    count = query.shape[0]
    per = heads_per_step(heads, 2)
    steps = heads // per

    def body(_, dx_in, after_ref, part_ref, other_ref, mod_ref, shared_ref, branch_ref, q_ref, k_ref, v_ref, pre_ref, vec_ref, cos_ref, sin_ref, *refs):
        weights, (dx_ref, low_ref, d_ref, dv_ref, sums, vec_out, q_acc, k_acc) = refs[:per], refs[per:]
        h = pl.program_id(0)

        @pl.when(h == 0)
        def _():
            da = part_ref[...].astype(F32) + other_ref[...].astype(F32)
            back, _ = normed_back(after_ref[...], da * shared_ref[3:4])
            dx = dx_in[...] + back
            dx_ref[...] = dx
            low = (mod_ref[2:3] * dx).astype(BF16)
            low_ref[...] = low
            vec_out[0:1] = 0.5 * total_of(low.astype(F32))
            vec_out[1:2] = 0.5 * total_of(dx * branch_ref[...])
            q_acc[...] = jnp.zeros_like(q_acc)
            k_acc[...] = jnp.zeros_like(k_acc)

        do_all = nn(low_ref[...], joined(weights)).astype(BF16)
        cos, sin = cos_ref[...], -sin_ref[...]
        q_sums, k_sums = 0.0, 0.0
        for j in range(per):
            lanes = slice(j * HEAD, (j + 1) * HEAD)
            do = do_all[:, lanes]
            q, k = q_ref[:, lanes], k_ref[:, lanes]
            chance = softmax(self_scores(q, k, tokens))
            dp = nt(do, v_ref[:, lanes])
            ds = (chance * (dp - jnp.sum(chance * dp, -1, keepdims=True))).astype(BF16)
            dv_ref[j] = tn(chance.astype(BF16), do).astype(BF16)
            dq = turned(nn(ds, k) * SCALING, cos, sin)
            dk = turned(tn(ds, q) * SCALING, cos, sin)
            d_ref[0, :, lanes] = dq
            d_ref[1, :, lanes] = dk
            q_sums += pre_ref[0, :, lanes] * vec_ref[3:4, lanes] * dq
            k_sums += pre_ref[1, :, lanes] * vec_ref[4:5, lanes] * dk
        q_acc[...] = q_acc[...] + q_sums
        k_acc[...] = k_acc[...] + k_sums

        @pl.when(h == steps - 1)
        def _():
            lane = lax.broadcasted_iota(jnp.int32, q_acc.shape, 1)
            sums[...] = jnp.where(
                lane < 64,
                wide(jnp.sum(q_acc[...], -1, keepdims=True)),
                wide(jnp.sum(k_acc[...], -1, keepdims=True)),
            )

    lanes = head_lanes(count, per)
    pair = pl.BlockSpec((2, count, per * HEAD), lambda h, _: (0, 0, h))
    return call(
        body, places, steps,
        [(v, None) for v in (dx_two, after_one, part, other, mod, shared, branch)]
        + [
            (query, lanes), (key, lanes), (value, lanes), (pre, pair),
            (vecs, head_lanes(vecs.shape[0], per)), (cos_tab, None), (sin_tab, None),
        ]
        + [(everyone, block_at(3 * heads + j, per)) for j in range(per)],
        [
            ((count, D), F32, None),
            ((count, D), BF16, None),
            (pre.shape, F32, pair),
            ((heads, count, HEAD), BF16, pl.BlockSpec((per, count, HEAD), lambda h, _: (h, 0, 0))),
            ((count, HEAD), F32, None),
            ((2, D), F32, None),
        ],
        [pltpu.VMEM((count, HEAD), F32), pltpu.VMEM((count, HEAD), F32)],
        vmem=32,
    )


def self_back_rows(places, everyone, rows, pre, grads, dv, squares, squares_other, sums, sums_other, vecs, heads):
    count = pre.shape[1]
    per = heads_per_step(heads, 2)
    steps = heads // per

    def body(_, rows_ref, pre_ref, d_ref, dv_ref, sq_ref, sqo_ref, sum_ref, sumo_ref, vec_ref, *refs):
        weights, (gq_ref, gk_ref, vec_out, da_ref, row_out, acc) = refs[: 3 * per], refs[3 * per :]
        h = pl.program_id(0)
        squares_all = sq_ref[...] + sqo_ref[...]
        total = sum_ref[...] + sumo_ref[...]
        inverses = [
            lax.rsqrt(squares_all[:, n : n + 1] / D + NORM_EPS) for n in (0, 64)
        ]
        lows = []
        for j in range(per):
            lanes = slice(j * HEAD, (j + 1) * HEAD)
            biases, gains = [], []
            for n, out in enumerate((gq_ref, gk_ref)):
                low, bias, gain = norm_grad(
                    pre_ref[n, :, lanes], inverses[n], vec_ref[3 + n : 4 + n, lanes],
                    d_ref[n, :, lanes], total[:, 64 * n : 64 * n + 1],
                )
                out[j] = low
                lows.append(low)
                biases.append(bias)
                gains.append(gain)
            dv_low = dv_ref[j]
            lows.append(dv_low)
            vec_out[:, lanes] = jnp.concatenate(
                biases + [total_of(dv_low.astype(F32))] + gains + [jnp.zeros((3, HEAD), F32)], 0
            )
        part = nt(jnp.concatenate(lows, 1), joined(weights))

        @pl.when(h == 0)
        def _():
            acc[...] = part

        @pl.when(h > 0)
        def _():
            acc[...] = acc[...] + part

        @pl.when(h == steps - 1)
        def _():
            da = acc[...]
            da_ref[...] = da.astype(BF16)
            row_out[0:1] = total_of(da)
            row_out[1:2] = total_of(da * normed(rows_ref[...])[0])

    tall = pl.BlockSpec((per, count, HEAD), lambda h, _: (h, 0, 0))
    pair = pl.BlockSpec((2, count, per * HEAD), lambda h, _: (0, 0, h))
    return call(
        body, places, steps,
        [
            (rows, None), (pre, pair), (grads, pair), (dv, tall), (squares, None),
            (squares_other, None), (sums, None), (sums_other, None),
            (vecs, head_lanes(vecs.shape[0], per)),
        ]
        + [(everyone, block_at(n * heads + j, per)) for j in range(per) for n in range(3)],
        [
            ((heads, count, HEAD), BF16, tall),
            ((heads, count, HEAD), BF16, tall),
            ((8, heads * HEAD), F32, head_lanes(8, per)),
            ((count, D), BF16, None),
            ((2, D), F32, None),
        ],
        [pltpu.VMEM((count, D), F32)],
        vmem=40,
    )


def shared_sums(places, after_one, after_two, grad_two, grad_three, cot, da_two, da_three, y_three, shared):
    def body(_, x1_ref, x2_ref, dy2, dy3, cot_ref, da2, da3, y3, shared_ref, out):
        out[...] = jnp.zeros_like(out)
        out[1:2] = 0.5 * total_of(dy2[...].astype(F32))
        out[2:3] = 0.5 * total_of(dy3[...].astype(F32))
        part = da3[...].astype(F32)
        out[3:4] = total_of(part * normed(x1_ref[...])[0])
        out[4:5] = total_of(part)
        part = da2[...].astype(F32)
        out[8:9] = total_of(part)
        out[9:10] = total_of(part * normed(x2_ref[...])[0])
        out[10:11] = total_of(cot_ref[...] * (y3[...].astype(F32) + 0.5 * shared_ref[2:3]))

    return call(
        body, places, 1,
        [(v, None) for v in (after_one, after_two, grad_two, grad_three, cot, da_two, da_three, y_three, shared)],
        [(shared.shape, F32, None)],
    )[0]


def body(
    latents,
    context,
    cotangent,
    positions,
    step_ids,
    owners,
    time_table,
    master,
    first_moment,
    second_moment,
    head_params,
    head_first,
    head_second,
    shared_params,
    shared_first,
    shared_second,
):
    tensors = lax.axis_size("tensor")
    devices = lax.axis_size("dp")
    slot_count = master.shape[1]
    tile_count = owners.shape[0]
    heads_here = HEADS // tensors
    blocks_here = FF // (HEAD * tensors)
    width_here = D // tensors
    places, holder = owner_layout(owners, slot_count, devices)
    scales = tile_scales(tile_count, heads_here, blocks_here)
    rank = pair_rank()
    my_slots = lax.axis_index("dp") * slot_count + jnp.arange(slot_count, dtype=jnp.int32)
    holds = places[None, :] == my_slots[:, None]
    slot_scale = jnp.sum(jnp.where(holds, scales[None, :], 0.0), axis=1)
    filled = jnp.any(holds, axis=1)
    scaled = (master[0] * slot_scale[:, None, None]).astype(jnp.bfloat16)
    half = latents.shape[0]
    tokens = 2 * half
    count = -(-tokens // 16) * 16
    taller = ((0, -half % 16), (0, 0))
    small = jnp.concatenate(
        [
            head_params[0],
            positions.reshape(-1).astype(jnp.float32),
            step_ids.astype(jnp.float32),
        ]
    )
    packed = jnp.pad(small, (0, -small.shape[0] % 1024)).reshape(-1, HEAD)
    everyone, lats, cots, context, packed = gather_slots(
        scaled, jnp.pad(latents, taller), jnp.pad(cotangent, taller), context, packed
    )
    small = packed.reshape(-1)
    vectors = small[: head_params.shape[1]]
    small = small[head_params.shape[1] :]
    positions = small[: positions.size].reshape(positions.shape)
    step = small[positions.size]
    vecs = vectors[: 10 * width_here].reshape(10, width_here)
    up_bias = vectors[10 * width_here :].reshape(1, -1)
    chosen = (step == jnp.arange(TSTEPS)).astype(jnp.float32)
    mod = shared_params[5:11] + jnp.einsum(
        "s,skd->kd", chosen, time_table, precision=lax.Precision.HIGHEST
    )
    cos_tab, sin_tab = rope_tables(positions, HEAD)
    sin_tab = jnp.where(jnp.arange(HEAD) % 2 == 0, -sin_tab, sin_tab)
    cos_tab, sin_tab = (jnp.pad(t, ((0, count - tokens), (0, 0))) for t in (cos_tab, sin_tab))

    def all_rows(halves):
        rows = jnp.concatenate([halves[0, :half], halves[1, :half]], 0)
        return jnp.pad(rows, ((0, count - tokens), (0, 0))).astype(jnp.float32)

    def upright(rows):
        return jnp.pad(rows, ((0, -rows.shape[0] % HEAD), (0, 0))).T

    def beside(*values):
        return lax.optimization_barrier(values)

    rows, cot = all_rows(lats), all_rows(cots)
    low_one, pre_one, value_one, squares_one = project_self(
        places, everyone, rows, mod, vecs, heads_here
    )
    squares_one_other = pair_swap(squares_one)
    query_one, key_one, heads_one, part_one = attend_self(
        places, everyone, pre_one, value_one, squares_one, squares_one_other, vecs, cos_tab,
        sin_tab, heads_here, tokens,
    )
    part_one, context = beside(part_one, context)
    part_one_other = pair_swap(part_one)
    key_pre, value_two, text_squares = project_text(places, everyone, context, vecs, heads_here)
    left_context, left_one = upright(context), upright(low_one)
    part_one_other, key_pre, left_context, left_one = beside(
        part_one_other, key_pre, left_context, left_one
    )
    branch_one, after_one, low_two, pre_two, squares_two = project_cross(
        places, everyone, rows, part_one, part_one_other, mod, shared_params, vecs,
        text_squares, heads_here,
    )
    squares_two_other = pair_swap(squares_two)
    query_two, key_two, heads_two, part_two = attend_cross(
        places, everyone, pre_two, key_pre, value_two, squares_two, squares_two_other, vecs,
        heads_here,
    )
    part_two, cot, low_two = beside(part_two, cot, low_two)
    part_two_other = pair_swap(part_two)
    grad_three, d_act = hidden_back(places, everyone, mod, cot, heads_here, blocks_here)
    left_two, left_grad_three = upright(low_two), upright(grad_three)
    part_two_other, d_act, left_two, left_grad_three = beside(
        part_two_other, d_act, left_two, left_grad_three
    )
    after_two, low_three, hidden, d_hidden, d_up_bias, da_two = hidden_both(
        places, everyone, after_one, part_two, part_two_other, mod, shared_params, d_act, up_bias,
        heads_here, blocks_here,
    )
    da_two_other = pair_swap(da_two)
    y_three = hidden_out(places, everyone, hidden, heads_here)
    left_three = upright(low_three)
    da_two_other, y_three, left_three = beside(da_two_other, y_three, left_three)
    dx_two, grad_two, dq_two, dk_two, dv_two, sums_two = cross_back(
        places, everyone, cot, after_two, da_two, da_two_other, mod, query_two, key_two,
        value_two, pre_two, key_pre, vecs, heads_here,
    )
    query_grad_two, key_grad_two, vecs_two, da_three = cross_back_rows(
        places, everyone, pre_two, key_pre, dq_two, dk_two, dv_two, squares_two,
        squares_two_other, sums_two, pair_swap(sums_two), vecs, heads_here,
    )
    da_three_other = pair_swap(da_three)
    shared_grad = shared_sums(
        places, after_one, after_two, grad_two, grad_three, cot, da_two, da_three, y_three,
        shared_params,
    )
    left_grad_two = upright(grad_two)
    da_three_other, shared_grad, left_grad_two = beside(da_three_other, shared_grad, left_grad_two)
    dx_one, grad_one, d_one, dv_one, sums_one, rows_a = self_back(
        places, everyone, dx_two, after_one, da_three, da_three_other, mod, shared_params,
        branch_one, query_one, key_one, value_one, pre_one, vecs, cos_tab, sin_tab, heads_here,
        tokens,
    )
    query_grad_one, key_grad_one, vecs_one, da_one, rows_b = self_back_rows(
        places, everyone, rows, pre_one, d_one, dv_one, squares_one, squares_one_other, sums_one,
        pair_swap(sums_one), vecs, heads_here,
    )
    shared_grad = jnp.concatenate(
        [rows_a[0:1], shared_grad[1:5], rows_b, rows_a[1:2], shared_grad[8:]], 0
    )
    head_grad = jnp.concatenate(
        [vecs_one[:5].reshape(-1), vecs_two[:5].reshape(-1), d_up_bias.reshape(-1)]
    )
    tensor_rank = lax.axis_index("tensor")
    head_padded = jnp.where(jnp.arange(tensors)[:, None] == rank, head_grad[None, :], 0.0)
    vector = jnp.concatenate([head_padded.reshape(-1), shared_grad.reshape(-1)])
    vector = jnp.pad(vector, (0, -vector.shape[0] % 1024)).reshape(-1, 128)
    parts, vector, output, grad_input = reduce_slots(
        holder,
        kind_of_blocks(tile_count, heads_here, blocks_here),
        (left_one, upright(grad_one), left_two, left_context, left_grad_two, left_three, left_grad_three),
        (
            query_grad_one,
            key_grad_one,
            dv_one,
            heads_one,
            query_grad_two,
            key_grad_two,
            dv_two,
            heads_two,
            d_hidden,
            hidden,
        ),
        vector,
        (rows, after_two, dx_one, y_three, da_one),
        jnp.concatenate([mod[5:6], mod[1:2], shared_params[2:3], jnp.zeros((5, D), F32)], 0),
        slot_count,
    )
    output, grad_input = (
        jnp.where(lax.axis_index("tensor") == 0, v[:half], v[half:tokens])
        for v in (output, grad_input)
    )
    new_master, new_first, new_second = adam_slots(
        parts, master, first_moment, second_moment, slot_scale, filled
    )
    vector = vector.reshape(-1)
    head_total = vector[: head_padded.size].reshape(head_padded.shape)
    shared_total = vector[head_padded.size : head_padded.size + shared_grad.size]
    shared_total = shared_total.reshape(shared_grad.shape)
    mine_head = lax.dynamic_slice_in_dim(head_total, tensor_rank, 1, 0)
    new_head, new_head_first, new_head_second = adam_step(
        head_params, mine_head, head_first, head_second, VECTOR_RATE, 0.0
    )
    new_shared, new_shared_first, new_shared_second = adam_step(
        shared_params, shared_total, shared_first, shared_second, VECTOR_RATE, 0.0
    )
    return (
        output,
        grad_input,
        new_master,
        new_first,
        new_second,
        new_head,
        new_head_first,
        new_head_second,
        new_shared,
        new_shared_first,
        new_shared_second,
    )


def solution(mesh):
    return jax.shard_map(
        body,
        mesh=mesh,
        in_specs=(
            P(("dp", "tensor"), None),
            P("dp", None),
            P(("dp", "tensor"), None),
            P(None, "dp"),
            P("dp"),
            P(),
            P(),
            P("tensor", "dp", None, None),
            P("tensor", "dp", None, None),
            P("tensor", "dp", None, None),
            P("tensor", None),
            P("tensor", None),
            P("tensor", None),
            P(),
            P(),
            P(),
        ),
        out_specs=(
            P(("dp", "tensor"), None),
            P(("dp", "tensor"), None),
            P("tensor", "dp", None, None),
            P("tensor", "dp", None, None),
            P("tensor", "dp", None, None),
            P("tensor", None),
            P("tensor", None),
            P("tensor", None),
            P(),
            P(),
            P(),
        ),
        check_vma=False,
    )
```

```python
import functools

import jax
import jax.numpy as jnp
from jax import lax
from jax.experimental import pallas as pl
from jax.experimental.pallas import tpu as pltpu
from jax.sharding import PartitionSpec as P

D = 1536
HEADS = 12
HEAD = 128
FF = 8960
TSTEPS = 16
STEPC = 10


NORM_EPS = 1e-06
BETA_ONE = 0.9
BETA_TWO = 0.999
ADAM_EPS = 1e-08
TILE_RATE = 1.0
TILE_DECAY = 0.1
VECTOR_RATE = 0.5
GELU_COEF = 0.7978845608028654


def rope_tables(token_places, head_size):
    sixths = head_size // 6
    frame_pairs = (head_size - 4 * sixths) // 2
    frame_freq = 10000.0 ** (-jnp.arange(frame_pairs, dtype=jnp.float32) / frame_pairs)
    side_freq = 10000.0 ** (-jnp.arange(sixths, dtype=jnp.float32) / sixths)
    spots = token_places.astype(jnp.float32)
    angles = jnp.concatenate(
        [
            spots[0][..., None] * frame_freq,
            spots[1][..., None] * side_freq,
            spots[2][..., None] * side_freq,
        ],
        -1,
    )
    angles = jnp.repeat(angles, 2, axis=-1)
    return (jnp.cos(angles), jnp.sin(angles))


def owner_layout(owners, slot_count, devices):
    indices = jnp.arange(owners.shape[0], dtype=jnp.int32)
    same_owner = (owners[:, None] == owners[None, :]) & (indices[None, :] < indices[:, None])
    slot_of = jnp.sum(same_owner.astype(jnp.int32), axis=1)
    places = owners * slot_count + slot_of
    spots = jnp.arange(slot_count * devices, dtype=jnp.int32)
    holder = (
        jnp.sum(jnp.where(places[None, :] == spots[:, None], indices[None, :] + 1, 0), axis=1) - 1
    )
    return (places, holder)


def tile_scales(tile_count, heads_here, blocks_here):
    indices = jnp.arange(tile_count)
    scale_in = D ** (-0.5)
    scale_out = HEADS ** (-0.5)
    scale_down = FF ** (-0.5)
    scales = jnp.where(
        indices < 3 * heads_here,
        scale_in,
        jnp.where(
            indices < 4 * heads_here,
            scale_out,
            jnp.where(
                indices < 7 * heads_here,
                scale_in,
                jnp.where(
                    indices < 8 * heads_here,
                    scale_out,
                    jnp.where(indices < 8 * heads_here + blocks_here, scale_in, scale_down),
                ),
            ),
        ),
    )
    return scales.astype(jnp.float32)


def adam_step(weight, gradient, moment_one, moment_two, step_rate, decay_rate):
    first_new = BETA_ONE * moment_one + (1.0 - BETA_ONE) * gradient
    second_new = BETA_TWO * moment_two + (1.0 - BETA_TWO) * gradient * gradient
    first_hat = first_new / (1.0 - BETA_ONE**STEPC)
    second_hat = second_new / (1.0 - BETA_TWO**STEPC)
    weight_new = weight - step_rate * (
        first_hat / (jnp.sqrt(second_hat) + ADAM_EPS) + decay_rate * weight
    )
    return (weight_new, first_new, second_new)


MESH = pl.DeviceIdType.MESH
ANY = pl.BlockSpec(memory_space=pl.ANY)
MIB = 1 << 20


def chip_pairs():
    return lax.axis_size("dp") == 16 and lax.axis_size("tensor") == 2


def pair_rank():
    if chip_pairs():
        return (lax.axis_index("dp") // 4) % 2
    return lax.axis_index("tensor")


def pair_swap(value):
    if chip_pairs():
        return lax.ppermute(value, "dp", [(i, i ^ 4) for i in range(16)])
    return lax.ppermute(value, "tensor", [(0, 1), (1, 0)])


def pair_sums(*values):
    stacked = jnp.concatenate([v.reshape(-1) for v in values])
    total = stacked + pair_swap(stacked)
    out, at = [], 0
    for v in values:
        out.append(total[at : at + v.size].reshape(v.shape))
        at += v.size
    return tuple(out)


def place_of():
    chip, core = lax.axis_index("dp"), lax.axis_index("tensor")
    z, y, x = chip // 4, (chip // 2) % 2, chip % 2
    return chip, core, z, y, x


def column_of(z, y, x, k):
    high, low_bit = z // 2, z % 2
    if k & 2:
        high = 1 - high
    if k & 1:
        low_bit = 1 - low_bit
    return (2 * high + low_bit) * 4 + 2 * y + x


def greet(chip, core, z, y, x):
    barrier = pltpu.get_barrier_semaphore()
    friends = []
    for k in range(4):
        for flip in (0, 1):
            if k or flip:
                friends.append((column_of(z, y, x, k), core if flip == 0 else 1 - core))
    for side in (core, 1 - core):
        friends.append((column_of(z, y, 1 - x, 0), side))
        friends.append((column_of(z, 1 - y, x, 0), side))
    for friend in friends:
        pl.semaphore_signal(barrier, inc=1, device_id=friend, device_id_type=MESH)
    pl.semaphore_wait(barrier, len(friends))


def gather_kernel(
    own, lat, cot, text, small, out, lats, cots, texts, smalls, relay_a, relay_b, clip_s, clip_r,
    out_s, out_r, over_s, over_r, near_s, col_r, x_s, x_r, y_s, y_r, sib_s, sib_r,
):
    chip, core, z, y, x = place_of()
    rank = z % 2
    half = own.shape[1] // 2
    part = half // 2
    at_x = column_of(z, y, 1 - x, 0)
    at_y = column_of(z, 1 - y, x, 0)
    greet(chip, core, z, y, x)

    batch = max(n for n in (1, 2, 3) if own.shape[0] % n == 0)
    batches = own.shape[0] // batch
    turns = 4 * batches
    mine, other = core * half, (1 - core) * half
    sibling = (chip, 1 - core)
    tail = pl.ds((batches - 1) * batch, batch)

    def outward(n, h):
        rows = pl.ds(h * half + n * part, part)
        return pltpu.make_async_remote_copy(
            src_ref=own.at[tail, rows, :], dst_ref=(relay_a, relay_b)[n].at[core],
            send_sem=out_s.at[2 * n + h], recv_sem=out_r.at[2 * n + core],
            device_id=((at_x, at_y)[n], h), device_id_type=MESH,
        )

    def case(s):
        late = jnp.maximum(s - batches, 0)
        k = jnp.where(s < batches, 0, 1 + late % 3)
        return k, jnp.where(s < batches, s, late // 3)

    def remote(unit, g, first, count, send, recv, device):
        piece = out.at[
            unit, pl.ds(g * batch, batch), pl.ds(pl.multiple_of(first, 16), count), :
        ]
        return pltpu.make_async_remote_copy(
            src_ref=piece, dst_ref=piece, send_sem=send, recv_sem=recv,
            device_id=device, device_id_type=MESH,
        )

    def own_copy(g, j, h):
        target = (toggled(z, y, x, 0, 0, 2 * j) // 8 * 8) + core * 4 + 2 * y + x
        part_of = (pl.ds(g * batch, batch), pl.ds(h * half, half))
        src = own.at[part_of[0], part_of[1], :]
        dst = out.at[chip, part_of[0], part_of[1], :]
        recv = col_r.at[z * batches + g]
        go = pltpu.make_async_remote_copy(
            src_ref=src, dst_ref=dst, send_sem=near_s.at[(2 * j + h) * batches + g],
            recv_sem=recv, device_id=(target, h), device_id_type=MESH,
        )
        return go, pltpu.make_async_copy(src, dst, recv)

    for n in range(2):
        for h in range(2):
            outward(n, h).start()
    for g in range(batches):
        for j in range(2):
            for h in range(2):
                go, here = own_copy(g, j, h)
                if j == 1:
                    go.start()
                    continue
                stays = jnp.logical_and(rank == core, core == h)

                @pl.when(stays)
                def _():
                    here.start()

                @pl.when(jnp.logical_not(stays))
                def _():
                    go.start()

    pair_chip = column_of(z, y, x, 1)
    rows_of_text = text.shape[0] // 2

    def clip_pieces(h):
        share = pl.ds(h * rows_of_text, rows_of_text)
        return ((lat, lats.at[h]), (cot, cots.at[h]), (text.at[share], texts.at[share]))

    home = rank == core
    trade = pltpu.make_async_remote_copy(
        src_ref=small, dst_ref=smalls, send_sem=clip_s.at[6], recv_sem=clip_r.at[6],
        device_id=(pair_chip, 1 - core), device_id_type=MESH,
    )
    keep = pltpu.make_async_copy(small, smalls, clip_r.at[6])

    @pl.when(home)
    def _():
        keep.start()

    @pl.when(jnp.logical_not(home))
    def _():
        trade.start()

    def hand_out(h, n, wait):
        src, dst = clip_pieces(h)[n]
        far = pltpu.make_async_remote_copy(
            src_ref=src, dst_ref=dst, send_sem=clip_s.at[n], recv_sem=clip_r.at[3 * h + n],
            device_id=(pair_chip, rank), device_id_type=MESH,
        )
        near = pltpu.make_async_remote_copy(
            src_ref=src, dst_ref=dst, send_sem=clip_s.at[3 + n], recv_sem=clip_r.at[3 * h + n],
            device_id=(chip, 1 - core), device_id_type=MESH,
        )
        here = pltpu.make_async_copy(src, dst, clip_r.at[3 * h + n])

        @pl.when(core == h)
        def _():
            if wait:
                far.wait_send()
            else:
                far.start()

            @pl.when(home)
            def _():
                if not wait:
                    here.start()

            @pl.when(jnp.logical_not(home))
            def _():
                if wait:
                    near.wait_send()
                else:
                    near.start()

    for n in range(3):
        for h in range(2):
            hand_out(h, n, False)


    def spans(n, wide):
        part_a, part_b = (mine, part), (mine + part, part)
        if wide:
            return part_b, part_a
        return (part_a, part_b) if n else ((mine, half), (mine, half))

    def over_x(s, n, wide, coming=0):
        k, g = case(s)
        i = turns * n + s
        first, count = spans(n, wide)[0]
        unit = toggled(z, y, x, n, coming, k)
        return remote(unit, g, first, count, x_s.at[i], x_r.at[i], (at_x, core))

    def over_y(s, n, wide, coming=0):
        k, g = case(s)
        i = turns * n + s
        first, count = spans(n, wide)[1]
        unit = toggled(z, y, x, coming, n, k)
        return remote(unit, g, first, count, y_s.at[i], y_r.at[i], (at_y, core))

    def to_sib(s, column, piece, away=False):
        k, g = case(s)
        i = turns * ({(0, 2): 0, (1, 2): 1, (2, 2): 2}.get((column, piece), 2 * column + piece - 1)) + s
        unit = toggled(z, y, x, column // 2, column % 2, k)
        first = (other if away else mine) + (part if piece == 1 else 0)
        count = half if piece == 2 else part
        return remote(unit, g, first, count, sib_s.at[i], sib_r.at[i], sibling)

    def column_in(s, wide):
        k, g = case(s)
        unit = toggled(z, y, x, 0, 0, k)
        piece = out.at[
            unit, pl.ds(g * batch, batch), pl.ds(pl.multiple_of(mine, 16), half), :
        ]
        pltpu.make_async_copy(piece, piece, col_r.at[unit // 4 * batches + g]).wait()
        over_x(s, 0, wide).start()
        over_y(s, 0, wide).start()
        to_sib(s, 0, 2).start()
        if wide:
            for n, (spot, first) in enumerate(((toggled(z, y, x, 0, 1, k), mine), (toggled(z, y, x, 1, 0, k), mine + part))):
                piece = out.at[
                    spot, pl.ds(g * batch, batch), pl.ds(pl.multiple_of(first, 16), part), :
                ]
                pltpu.make_async_copy(piece, piece, over_r.at[4 * n + spot // 4]).wait()
            over_y(s, 1, wide).start()
            to_sib(s, 1, 0).start()
            over_x(s, 1, wide).start()
            to_sib(s, 2, 1).start()

    def side_in(s, wide):
        over_x(s, 0, wide, 1).wait_recv()
        if wide:
            to_sib(s, 1, 1).start()
        else:
            over_y(s, 1, wide).start()
            to_sib(s, 1, 2).start()
        over_y(s, 0, wide, 1).wait_recv()
        if wide:
            to_sib(s, 2, 0).start()
        else:
            over_x(s, 1, wide).start()
            to_sib(s, 2, 2).start()

    def corner_in(s, wide):
        over_x(s, 1, wide, 1).wait_recv()
        to_sib(s, 3, 1 if wide else 0).start()
        over_y(s, 1, wide, 1).wait_recv()
        to_sib(s, 3, 0 if wide else 1).start()

    def either(s, act):
        _, g = case(s)
        wide = g == batches - 1

        @pl.when(wide)
        def _():
            act(s, True)

        @pl.when(jnp.logical_not(wide))
        def _():
            act(s, False)

    def onward(n, t, j):
        origin = (at_x, at_y)[n]
        src = (relay_a, relay_b)[n].at[t]
        rows = pl.ds(pl.multiple_of(mine + n * part, 16), part)
        dst = out.at[origin, tail, rows, :]
        high = (z // 2 + j) % 2
        recv = over_r.at[4 * n + z]
        go = pltpu.make_async_remote_copy(
            src_ref=src, dst_ref=dst, send_sem=over_s.at[4 * n + 2 * t + j], recv_sem=recv,
            device_id=((2 * high + t) * 4 + 2 * y + x, core), device_id_type=MESH,
        )
        return go, pltpu.make_async_copy(src, dst, recv)

    def pass_on(n):
        for t in range(2):
            piece = (relay_a, relay_b)[n].at[t]
            pltpu.make_async_copy(piece, piece, out_r.at[2 * n + t]).wait()
            for j in range(2):
                go, here = onward(n, t, j)
                if j == 1:
                    go.start()
                    continue

                @pl.when(rank == t)
                def _():
                    here.start()

                @pl.when(rank != t)
                def _():
                    go.start()

    def turn(step, carry):
        @pl.when(step < turns)
        def _():
            either(step, column_in)

        @pl.when(jnp.logical_and(step >= 1, step < turns + 1))
        def _():
            either(step - 1, side_in)

        @pl.when(step >= 2)
        def _():
            either(step - 2, corner_in)

        @pl.when(step == 0)
        def _():
            pass_on(0)
            pass_on(1)

        return carry

    lax.fori_loop(0, turns + 2, turn, 0)

    def close(s, wide):
        for n in range(2):
            over_x(s, n, wide).wait_send()
            over_y(s, n, wide).wait_send()
        pieces = [(0, 2), (3, 0), (3, 1)]
        pieces += [(1, 0), (1, 1), (2, 0), (2, 1)] if wide else [(1, 2), (2, 2)]
        for column, piece in pieces:
            to_sib(s, column, piece).wait_send()
            to_sib(s, column, piece, True).wait_recv()

    def settle(s, carry):
        either(s, close)
        return carry

    lax.fori_loop(0, turns, settle, 0)
    for n in range(2):
        for h in range(2):
            outward(n, h).wait_send()
        for t in range(2):
            onward(n, t, 1)[0].wait_send()

            @pl.when(rank != t)
            def _():
                onward(n, t, 0)[0].wait_send()

    for g in range(batches):
        for j in range(2):
            for h in range(2):
                go, _ = own_copy(g, j, h)
                if j == 1:
                    go.wait_send()
                    continue

                @pl.when(jnp.logical_not(jnp.logical_and(rank == core, core == h)))
                def _():
                    go.wait_send()

    for n in range(3):
        for h in range(2):
            hand_out(h, n, True)
            dst = clip_pieces(h)[n][1]
            pltpu.make_async_copy(dst, dst, clip_r.at[3 * h + n]).wait()

    @pl.when(jnp.logical_not(home))
    def _():
        trade.wait_send()

    pltpu.make_async_copy(smalls, smalls, clip_r.at[6]).wait()


def gather_slots(scaled, lat, cot, text, small):
    if not chip_pairs():
        everyone = lax.all_gather(scaled, "dp", axis=0, tiled=True)
        lats, cots = (lax.all_gather(v, "tensor") for v in (lat, cot))
        return everyone, lats, cots, text, small
    dma = pltpu.SemaphoreType.DMA
    turns = 4 * scaled.shape[0] // max(n for n in (1, 2, 3) if scaled.shape[0] % n == 0)
    counts = (7, 7, 4, 4, 8, 8, turns, turns) + (2 * turns,) * 4 + (7 * turns,) * 2
    batch = 4 * scaled.shape[0] // turns
    relay = pltpu.HBM((2, batch, scaled.shape[1] // 4, scaled.shape[2]), scaled.dtype)
    everyone, *rest = pl.pallas_call(
        gather_kernel,
        out_shape=[
            pltpu.HBM((16,) + scaled.shape, scaled.dtype),
            pltpu.HBM((2,) + lat.shape, lat.dtype),
            pltpu.HBM((2,) + cot.shape, cot.dtype),
            pltpu.HBM(text.shape, text.dtype),
            pltpu.HBM(small.shape, small.dtype),
            relay,
            relay,
        ],
        in_specs=[ANY] * 5,
        out_specs=[ANY] * 7,
        scratch_shapes=[dma((n,)) for n in counts],
        compiler_params=pltpu.CompilerParams(
            collective_id=0, has_side_effects=True, vmem_limit_bytes=4 * MIB
        ),
    )(scaled, lat, cot, pltpu.with_memory_space_constraint(text, pltpu.HBM), small)
    return everyone.reshape((-1,) + scaled.shape[1:]), *rest[:4]


def toggled(z, y, x, flip_y, flip_x, k):
    high = (z // 2 + k // 2) % 2
    low_bit = (z % 2 + k % 2) % 2
    return (2 * high + low_bit) * 4 + 2 * ((y + flip_y) % 2) + (x + flip_x) % 2


def reduce_kernel(
    kind, block, *refs,
):
    (
        *pieces, rows_in, after_in, dx_in, y_in, da_in, gains, vec_in,
        final, vec_out, result, result_grad, y_other, da_other, from_sib, from_x, from_y, corner_a, corner_b,
        left, right, ring, corners, side_x, side_y, middle, stage, vec_box, end_wide, end_low,
        load_s, stage_s, sib_s, sib_r, x_s, x_r, y_s, y_r, ca_s, ca_r, cb_s, cb_r, f_s, f_r, v_s, v_r,
        end_s, end_r, end_load,
    ) = refs
    chip, core, z, y, x = place_of()
    rank = z % 2
    slots, width, lanes = final.shape[1:]
    half = width // 2
    part = half // 2
    at_x = toggled(z, y, x, 0, 1, 0)
    at_y = toggled(z, y, x, 1, 0, 0)
    sibling = (chip, 1 - core)
    mates = (
        sibling,
        (at_x, core),
        (at_y, core),
        (toggled(z, y, x, 0, 0, 1), core),
        (toggled(z, y, x, 0, 0, 2), core),
    )

    kinds = left.shape[0]
    depth = right.shape[1]
    loads = []
    for i in range(kinds):
        columns = pieces[i].shape[1]
        loads.append(
            pltpu.make_async_copy(pieces[i], left.at[i, :, pl.ds(0, columns)], load_s.at[i])
        )
    first = 0
    blank = []
    for i, piece in enumerate(pieces[kinds:]):
        number, rows = piece.shape[:2]
        loads.append(
            pltpu.make_async_copy(
                piece, right.at[pl.ds(first, number), pl.ds(0, rows), :], load_s.at[kinds + i]
            )
        )
        if rows < depth:
            blank.append((first, number, rows))
        first += number
    for load in loads:
        load.start()
    for start, number, rows in blank:

        def clear(i, carry):
            right[start + i, pl.ds(rows, depth - rows), :] = jnp.zeros(
                (depth - rows, lanes), right.dtype
            )
            return carry

        lax.fori_loop(0, number, clear, 0)
    right[first] = jnp.zeros((depth, lanes), right.dtype)
    for i in range(kinds):
        columns = pieces[i].shape[1]
        if columns < depth:
            left[i, :, pl.ds(columns, depth - columns)] = jnp.zeros(
                (width, depth - columns), left.dtype
            )
    vec_out[...] = vec_in[...]
    greet(chip, core, z, y, x)
    for load in loads:
        load.wait()

    def remote(src, dst, send, recv, device):
        return pltpu.make_async_remote_copy(
            src_ref=src, dst_ref=dst, send_sem=send, recv_sem=recv,
            device_id=device, device_id_type=MESH,
        )

    batch = ring.shape[1]
    batches = slots // batch
    turns = 4 * batches
    deep = corners.shape[0]

    def flips(s):
        return 3 - s // batches

    def sums(q, s, first, terms, total):
        unit = toggled(z, y, x, 1 - q % 2, 1 - q // 2, flips(s))
        base = unit * slots + (s % batches) * batch
        count = total.shape[1]

        def one(i, carry):
            slot = base + i
            rows = pl.ds(pl.multiple_of(first, 128), count)
            acc = jnp.dot(
                left[kind[slot], rows, :], right[block[slot]], preferred_element_type=jnp.float32
            )
            for term in terms:
                acc = acc + term[i].astype(jnp.float32)
            total[i] = acc.astype(total.dtype)
            return carry

        lax.fori_loop(0, batch, one, 0)

    mine, other = core * half, (1 - core) * half

    def sub(ref, first):
        return ref.at[:, pl.ds(first, part), :]

    def sib_copy(q, s):
        i = turns * q + s
        return remote(ring.at[q], from_sib.at[i], sib_s.at[i], sib_r.at[i], sibling)

    def a_copy(s):
        return remote(
            sub(corners.at[s % deep], 0), corner_a.at[s], ca_s.at[s], ca_r.at[s], (at_x, core)
        )

    def b_copy(s):
        return remote(
            sub(corners.at[s % deep], part), corner_b.at[s], cb_s.at[s], cb_r.at[s], (at_y, core)
        )

    def x_copy(s, n):
        rows = pl.ds(n * part, part)
        i = turns * n + s
        return remote(
            side_x.at[s % deep, :, rows, :], from_x.at[s, :, rows, :], x_s.at[i], x_r.at[i],
            (at_x, core),
        )

    def y_copy(s, n):
        rows = pl.ds((1 - n) * part, part)
        i = turns * n + s
        return remote(
            side_y.at[s % deep, :, rows, :], from_y.at[s, :, rows, :], y_s.at[i], y_r.at[i],
            (at_y, core),
        )

    def f_copy(s):
        src = middle.at[s % deep]
        g = s % batches
        dst = final.at[
            z // 2, pl.ds(g * batch, batch), pl.ds(pl.multiple_of(mine, 128), half), :
        ]
        recv = f_r.at[(2 * (z // 2) + core) * batches + g]
        target = (toggled(z, y, x, 0, 0, flips(s)), rank)
        return remote(src, dst, f_s.at[s], recv, target), pltpu.make_async_copy(src, dst, recv)

    def stays(s):
        return jnp.logical_and(s >= turns - batches, rank == core)

    def for_sibling(s, low, high):
        def one(q, carry):
            @pl.when(s >= 1)
            def _():
                sib_copy(q, s - 1).wait_send()

            sums(q, s, other, (), ring.at[q])
            sib_copy(q, s).start()
            return carry

        lax.fori_loop(low, high, one, 0)

    def fetched(q, s):
        i = 2 * q + s % 2
        return pltpu.make_async_copy(from_sib.at[turns * q + s], stage.at[i], stage_s.at[i])

    def fetch(q, s):
        sib_copy(q, s).wait_recv()
        fetched(q, s).start()

    def taken(q, s):
        return stage.at[2 * q + s % 2]

    def corner(s):
        @pl.when(s >= deep)
        def _():
            a_copy(s - deep).wait_send()
            b_copy(s - deep).wait_send()

        fetched(0, s).wait()
        sums(0, s, mine, (taken(0, s),), corners.at[s % deep])
        a_copy(s).start()
        b_copy(s).start()

    def direct_sides(s):
        @pl.when(s >= deep)
        def _():
            for n in range(2):
                x_copy(s - deep, n).wait_send()
                y_copy(s - deep, n).wait_send()

        fetched(1, s).wait()
        sums(1, s, mine, (sub(taken(1, s), 0),), sub(side_x.at[s % deep], 0))
        x_copy(s, 0).start()
        fetched(2, s).wait()
        sums(2, s, mine + part, (sub(taken(2, s), part),), sub(side_y.at[s % deep], part))
        y_copy(s, 0).start()

    def relayed(s):
        return (
            pltpu.make_async_copy(corner_b.at[s], sub(stage.at[8], 0), stage_s.at[8]),
            pltpu.make_async_copy(corner_a.at[s], sub(stage.at[8], part), stage_s.at[9]),
        )

    def relayed_in(s):
        b_copy(s).wait_recv()
        relayed(s)[0].start()
        a_copy(s).wait_recv()
        relayed(s)[1].start()

    def relayed_sides(s):
        relayed(s)[0].wait()
        sums(
            1, s, mine + part, (sub(taken(1, s), part), sub(stage.at[8], 0)),
            sub(side_x.at[s % deep], part),
        )
        x_copy(s, 1).start()
        relayed(s)[1].wait()
        sums(
            2, s, mine, (sub(taken(2, s), 0), sub(stage.at[8], part)), sub(side_y.at[s % deep], 0)
        )
        y_copy(s, 1).start()

    def centre_terms(s):
        return (
            pltpu.make_async_copy(from_x.at[s], stage.at[9], stage_s.at[10]),
            pltpu.make_async_copy(from_y.at[s], stage.at[10], stage_s.at[11]),
        )

    def centre_in(s):
        for n, copies in enumerate((x_copy, y_copy)):
            copies(s, 0).wait_recv()
            copies(s, 1).wait_recv()
            centre_terms(s)[n].start()

    def centre(s):
        @pl.when(s >= deep)
        def _():
            f_copy(s - deep)[0].wait_send()

        fetched(3, s).wait()
        for term in centre_terms(s):
            term.wait()
        sums(3, s, mine, (taken(3, s), stage.at[9], stage.at[10]), middle.at[s % deep])
        go, here = f_copy(s)

        @pl.when(stays(s))
        def _():
            here.start()

        @pl.when(jnp.logical_not(stays(s)))
        def _():
            go.start()

    home = rank == core
    pair_device = (toggled(z, y, x, 0, 0, 1), core)
    ends = [
        remote(y_in, y_other, end_s.at[0], end_r.at[0], pair_device),
        remote(da_in, da_other, end_s.at[1], end_r.at[1], pair_device),
        remote(end_low.at[0], result, end_s.at[2], end_r.at[2], sibling),
        remote(end_wide.at[0], result_grad, end_s.at[3], end_r.at[3], sibling),
    ]
    end_loads = [
        pltpu.make_async_copy(src, dst, end_load.at[i])
        for i, (src, dst) in enumerate(
            (
                (rows_in, end_wide.at[0]), (after_in, end_wide.at[1]), (dx_in, end_wide.at[2]),
                (y_in, end_low.at[0]), (da_in, end_low.at[1]),
                (y_other, end_low.at[2]), (da_other, end_low.at[3]),
            )
        )
    ]
    end_stores = [
        pltpu.make_async_copy(end_low.at[0], result, end_load.at[7]),
        pltpu.make_async_copy(end_wide.at[0], result_grad, end_load.at[8]),
    ]

    def finish_rows():
        for n in range(2):
            ends[n].wait_recv()
            end_loads[5 + n].start()
        for load in end_loads:
            load.wait()
        tall = 16

        def one(i, carry):
            at = pl.ds(pl.multiple_of(i * tall, tall), tall)
            y_all = end_low[0, at].astype(F32) + end_low[2, at].astype(F32) + gains[2:3]
            end_low[0, at] = (end_wide[1, at] + gains[0:1] * y_all).astype(end_low.dtype)
            da = end_low[1, at].astype(F32) + end_low[3, at].astype(F32)
            back, _ = normed_back(end_wide[0, at], da * (1.0 + gains[1:2]))
            end_wide[0, at] = end_wide[2, at] + back
            return carry

        lax.fori_loop(0, rows_in.shape[0] // tall, one, 0)
        ends[2].start()
        ends[3].start()
        for store in end_stores:
            store.start()

    @pl.when(jnp.logical_not(home))
    def _():
        ends[0].start()
        ends[1].start()

    def vec_copy(i):
        return remote(vec_out, vec_box.at[i], v_s.at[i], v_r.at[i], mates[i])

    def turn(step, carry):
        for i in range(5):

            @pl.when(step == 2 * i)
            def _():
                vec_copy(i).start()

        @pl.when(step + 1 < turns)
        def _():
            corner(step + 1)
            direct_sides(step + 1)

        @pl.when(step + 2 < turns)
        def _():
            for_sibling(step + 2, 0, 4)

        @pl.when(step < turns)
        def _():
            relayed_in(step)

        @pl.when(step >= 1)
        def _():
            centre_in(step - 1)

        @pl.when(step < turns)
        def _():
            relayed_sides(step)

        @pl.when(step >= 1)
        def _():
            centre(step - 1)

        @pl.when(step + 2 < turns)
        def _():
            for q in range(3):
                fetch(q, step + 2)

        @pl.when(step + 1 < turns)
        def _():
            fetch(3, step + 1)

        @pl.when(jnp.logical_and(step == 1, home))
        def _():
            for load in end_loads[:5]:
                load.start()

        @pl.when(jnp.logical_and(step == 3, home))
        def _():
            finish_rows()

        for i in range(5):

            @pl.when(step == 2 * i + 1)
            def _():
                vec_copy(i).wait()
                vec_out[...] = vec_out[...] + vec_box[i]

        return carry

    for_sibling(0, 0, 2)
    fetch(0, 0)
    corner(0)
    for_sibling(0, 2, 4)
    for q in range(1, 4):
        fetch(q, 0)
    direct_sides(0)
    for_sibling(1, 0, 4)
    for q in range(3):
        fetch(q, 1)
    lax.fori_loop(0, turns + 1, turn, 0)
    for q in range(4):
        sib_copy(q, turns - 1).wait_send()

    def settle(i, carry):
        s = turns - deep + i
        a_copy(s).wait_send()
        b_copy(s).wait_send()
        for n in range(2):
            x_copy(s, n).wait_send()
            y_copy(s, n).wait_send()

        @pl.when(jnp.logical_not(stays(s)))
        def _():
            f_copy(s)[0].wait_send()

        return carry

    lax.fori_loop(0, deep, settle, 0)

    @pl.when(home)
    def _():
        ends[2].wait_send()
        ends[3].wait_send()
        for store in end_stores:
            store.wait()

    @pl.when(jnp.logical_not(home))
    def _():
        ends[0].wait_send()
        ends[1].wait_send()
        ends[2].wait_recv()
        ends[3].wait_recv()

    for plane in range(2):
        for h in range(2):
            for g in range(batches):
                piece = final.at[plane, pl.ds(g * batch, batch), pl.ds(h * half, half), :]
                recv = f_r.at[(2 * plane + h) * batches + g]
                pltpu.make_async_copy(piece, piece, recv).wait()


def reduce_slots(holder, kinds, rows, columns, vector, ends, gains, slot_count):
    if not chip_pairs():
        grads = slot_grads(holder, kinds, [r.T for r in rows], columns)
        total = lax.psum_scatter(grads, "dp", scatter_dimension=0, tiled=True)
        x, after, dx, y_part, da_part = ends
        y_all, da_all = (
            v.astype(F32) + pair_swap(v).astype(F32) for v in (y_part, da_part)
        )
        result = (after + gains[0] * (y_all + gains[2])).astype(BF16)
        back, _ = normed_back(x, da_all * (1.0 + gains[1]))
        return total[None], lax.psum(vector, ("dp", "tensor")), result, dx + back
    left = rows
    width, depth = left[0].shape[0], max(r.shape[1] for r in rows)
    lanes = columns[0].shape[2]
    tiles = sum(c.shape[0] for c in columns)
    block = jnp.where(holder >= 0, holder, tiles)
    kind = kinds[jnp.maximum(holder, 0)]
    half = width // 2
    dma = pltpu.SemaphoreType.DMA
    scalars = pl.BlockSpec(memory_space=pltpu.SMEM)
    inside = pl.BlockSpec(memory_space=pltpu.VMEM)
    low = jnp.bfloat16

    batch = max(n for n in (1, 2, 3) if slot_count % n == 0)
    turns = 4 * slot_count // batch
    deep = 3

    def room(count, tall):
        return pltpu.HBM((count, batch, tall, lanes), low)

    def slab(count):
        return pltpu.VMEM((count, batch, half, lanes), low)

    outs = pl.pallas_call(
        reduce_kernel,
        out_shape=[
            pltpu.HBM((2, slot_count, width, lanes), low),
            jax.ShapeDtypeStruct(vector.shape, vector.dtype),
            pltpu.HBM(ends[0].shape, low), pltpu.HBM(ends[0].shape, F32),
            pltpu.HBM(ends[0].shape, low), pltpu.HBM(ends[0].shape, low),
            room(4 * turns, half), room(turns, half), room(turns, half),
            room(turns, half // 2), room(turns, half // 2),
        ],
        in_specs=[scalars, scalars] + [ANY] * (len(left) + len(columns) + 5) + [inside] * 2,
        out_specs=[ANY, inside] + [ANY] * 9,
        scratch_shapes=[
            pltpu.VMEM((len(left), width, depth), low),
            pltpu.VMEM((tiles + 1, depth, lanes), low),
            slab(4), slab(deep), slab(deep), slab(deep), slab(deep), slab(11),
            pltpu.VMEM((5,) + vector.shape, vector.dtype),
            pltpu.VMEM((3,) + ends[0].shape, F32),
            pltpu.VMEM((4,) + ends[0].shape, low),
        ]
        + [
            dma((n,))
            for n in (len(left) + len(columns), 12)
            + (4 * turns,) * 2
            + (2 * turns,) * 4
            + (turns,) * 6
            + (5, 5, 4, 4, 9)
        ],
        compiler_params=pltpu.CompilerParams(
            collective_id=1, has_side_effects=True, vmem_limit_bytes=58 * MIB
        ),
    )(
        kind,
        block,
        *[pltpu.with_memory_space_constraint(v, pltpu.HBM) for v in (*left, *columns, *ends)],
        gains,
        vector,
    )
    return outs[:4]


def kind_of_blocks(tile_count, heads_here, blocks_here):
    number = jnp.arange(tile_count)
    kind = number // heads_here
    table = jnp.array([0, 0, 0, 1, 2, 3, 3, 4], jnp.int32)
    late = jnp.where(number < 8 * heads_here + blocks_here, 5, 6)
    return jnp.where(number < 8 * heads_here, table[jnp.minimum(kind, 7)], late).astype(jnp.int32)


def slot_grads(holder, kinds, rows, columns):
    depth = max(r.shape[0] for r in rows)

    def deep(value, axis):
        room = [(0, 0)] * value.ndim
        room[axis] = (0, depth - value.shape[axis])
        return jnp.pad(value, room)

    left = jnp.stack([deep(r, 0) for r in rows])
    right = jnp.concatenate([deep(c, 1) for c in columns], 0)
    slots = holder.shape[0]
    used = (holder >= 0).astype(jnp.int32)
    block = jnp.maximum(holder, 0)
    kind = kinds[block]
    width = rows[0].shape[1]
    lanes = right.shape[2]

    def multiply(kind_ref, block_ref, used_ref, left_ref, right_ref, out_ref):
        slot = pl.program_id(0)

        @pl.when(used_ref[slot] == 1)
        def _():
            out_ref[0] = lax.dot_general(
                left_ref[kind_ref[slot]],
                right_ref[0],
                (((0,), (0,)), ((), ())),
                preferred_element_type=jnp.float32,
            ).astype(out_ref.dtype)

        @pl.when(used_ref[slot] == 0)
        def _():
            out_ref[...] = jnp.zeros_like(out_ref)

    return pl.pallas_call(
        multiply,
        grid_spec=pltpu.PrefetchScalarGridSpec(
            num_scalar_prefetch=3,
            grid=(slots,),
            in_specs=[
                pl.BlockSpec(left.shape, lambda s, kd, b, u: (0, 0, 0)),
                pl.BlockSpec((1, depth, lanes), lambda s, kd, b, u: (b[s], 0, 0)),
            ],
            out_specs=pl.BlockSpec((1, width, lanes), lambda s, kd, b, u: (s, 0, 0)),
        ),
        out_shape=jax.ShapeDtypeStruct((slots, width, lanes), jnp.bfloat16),
        compiler_params=pltpu.CompilerParams(vmem_limit_bytes=48 * MIB),
    )(kind, block, used, left, right)


def adam_slots(planes, master, moment_one, moment_two, slot_scale, filled):
    count, slot_count, width, lanes = planes.shape

    def step(scale_ref, fill_ref, grads, weight, one, two, new_weight, new_one, new_two, grad_box, boxes, reads, writes):
        sources = (weight, one, two)
        targets = (new_weight, new_one, new_two)

        def load(slot):
            return [
                pltpu.make_async_copy(src.at[0, slot], boxes.at[n, slot], reads.at[n, slot])
                for n, src in enumerate(sources)
            ] + [
                pltpu.make_async_copy(
                    grads.at[n, slot], grad_box.at[n, slot], reads.at[3 + n, slot]
                )
                for n in range(count)
            ]

        def store(slot):
            return [
                pltpu.make_async_copy(boxes.at[n, slot], dst.at[0, slot], writes.at[n, slot])
                for n, dst in enumerate(targets)
            ]

        def begin(slot, carry):
            for copy in load(slot):
                copy.start()
            return carry

        def work(slot, carry):
            for copy in load(slot):
                copy.wait()

            @pl.when(fill_ref[slot] == 1)
            def _():
                total = grad_box[0, slot].astype(jnp.float32)
                for n in range(1, count):
                    total = total + grad_box[n, slot].astype(jnp.float32)
                results = adam_step(
                    boxes[0, slot], total * scale_ref[slot], boxes[1, slot], boxes[2, slot],
                    TILE_RATE, TILE_DECAY,
                )
                for n, value in enumerate(results):
                    boxes[n, slot] = value

            for copy in store(slot):
                copy.start()
            return carry

        def finish(slot, carry):
            for copy in store(slot):
                copy.wait()
            return carry

        for part in (begin, work, finish):
            lax.fori_loop(0, slot_count, part, 0)

    scalars = pl.BlockSpec(memory_space=pltpu.SMEM)
    return pl.pallas_call(
        step,
        in_specs=[scalars, scalars] + [ANY] * 4,
        out_specs=[ANY] * 3,
        out_shape=[pltpu.HBM(master.shape, jnp.float32)] * 3,
        scratch_shapes=[
            pltpu.VMEM((count, slot_count, width, lanes), planes.dtype),
            pltpu.VMEM((3, slot_count, width, lanes), jnp.float32),
            pltpu.SemaphoreType.DMA((3 + count, slot_count)),
            pltpu.SemaphoreType.DMA((3, slot_count)),
        ],
        compiler_params=pltpu.CompilerParams(vmem_limit_bytes=40 * MIB),
    )(
        slot_scale,
        filled.astype(jnp.int32),
        *[
            pltpu.with_memory_space_constraint(v, pltpu.HBM)
            for v in (planes, master, moment_one, moment_two)
        ],
    )


SCALING = HEAD ** (-0.5)
BF16 = jnp.bfloat16
F32 = jnp.float32


def nn(left, right):
    return jnp.dot(left, right, preferred_element_type=F32)


def nt(left, right):
    return lax.dot_general(left, right, (((1,), (1,)), ((), ())), preferred_element_type=F32)


def tn(left, right):
    return lax.dot_general(left, right, (((0,), (0,)), ((), ())), preferred_element_type=F32)


def normed(rows):
    centre = rows - jnp.mean(rows, -1, keepdims=True)
    inverse = lax.rsqrt(jnp.mean(centre * centre, -1, keepdims=True) + NORM_EPS)
    return centre * inverse, inverse


def normed_back(rows, grad):
    unit, inverse = normed(rows)
    mean = jnp.mean(grad, -1, keepdims=True)
    return (grad - mean - unit * jnp.mean(grad * unit, -1, keepdims=True)) * inverse, unit


def total_of(rows):
    return jnp.sum(rows, 0, keepdims=True)


def turned(rows, cos_tab, sin_tab):
    even = lax.broadcasted_iota(jnp.int32, rows.shape, 1) % 2 == 0
    partner = jnp.where(even, pltpu.roll(rows, HEAD - 1, 1), pltpu.roll(rows, 1, 1))
    return rows * cos_tab + partner * sin_tab


def wide(column):
    return jnp.broadcast_to(column, (column.shape[0], HEAD))


def pack_sums(for_rows, for_text=None):
    out = wide(for_rows)
    if for_text is None:
        return out
    lane = lax.broadcasted_iota(jnp.int32, out.shape, 1)
    count = for_text.shape[0] // 2
    rest = jnp.zeros((out.shape[0] - count, HEAD), F32)
    first = jnp.concatenate([wide(for_text[:count]), rest], 0)
    second = jnp.concatenate([wide(for_text[count:]), rest], 0)
    return jnp.where(lane < 32, out, jnp.where(lane < 64, first, second))


def unpack_text(sums, count):
    return jnp.concatenate([sums[: count // 2, 32:33], sums[: count // 2, 64:65]], 0)


def softmax(scores):
    expo = jnp.exp(scores - jnp.max(scores, -1, keepdims=True))
    return expo / jnp.sum(expo, -1, keepdims=True)


def self_scores(query_low, key_low, tokens):
    scores = nt(query_low, key_low) * SCALING
    lane = lax.broadcasted_iota(jnp.int32, scores.shape, 1)
    return jnp.where(lane < tokens, scores, -1e30)


def whole(array):
    zeros = (0,) * len(array.shape)
    return pl.BlockSpec(array.shape, lambda *_: zeros)


def block_at(first, stride=1):
    return pl.BlockSpec((1, D, HEAD), lambda i, where: (where[first + stride * i], 0, 0))


def call(body, places, grid, ins, outs, scratch=(), vmem=24):
    specs = [spec if spec is not None else whole(array) for array, spec in ins]
    shapes = [pltpu.HBM(shape, kind) for shape, kind, _ in outs]
    out_specs = [
        spec if spec is not None else whole(shape) for (_, _, spec), shape in zip(outs, shapes)
    ]
    return pl.pallas_call(
        body,
        grid_spec=pltpu.PrefetchScalarGridSpec(
            num_scalar_prefetch=1,
            grid=(grid,),
            in_specs=specs,
            out_specs=out_specs,
            scratch_shapes=list(scratch),
        ),
        out_shape=shapes,
        compiler_params=pltpu.CompilerParams(vmem_limit_bytes=vmem * MIB),
    )(places, *[pltpu.with_memory_space_constraint(array, pltpu.HBM) for array, _ in ins])


def head_lanes(rows, per=1):
    return pl.BlockSpec((rows, per * HEAD), lambda h, *_: (0, h))


def heads_per_step(heads, most):
    return max(n for n in (1, 2, 3, 6) if heads % n == 0 and n <= most)


def lane_group(ref, j):
    return ref[:, j * HEAD : (j + 1) * HEAD]


def joined(refs):
    return jnp.concatenate([ref[0] for ref in refs], 1)


def project_self(places, everyone, rows, mod, vecs, heads):
    count = rows.shape[0]
    span = heads * HEAD

    def body(_, rows_ref, mod_ref, vec_ref, *refs):
        weights, (low, pre, value, sums, acc) = refs[:heads], refs[heads:]
        i = pl.program_id(0)

        @pl.when(i == 0)
        def _():
            unit, _ = normed(rows_ref[...])
            low[...] = (unit * (1.0 + mod_ref[1:2]) + mod_ref[0:1]).astype(BF16)

        made = nn(low[...], joined(weights))

        @pl.when(i == 0)
        def _():
            q = made + vec_ref[0:1]
            pre[0] = q
            acc[...] = wide(jnp.sum(q * q, -1, keepdims=True))

        @pl.when(i == 1)
        def _():
            k = made + vec_ref[1:2]
            pre[0] = k
            lane = lax.broadcasted_iota(jnp.int32, acc.shape, 1)
            sums[...] = jnp.where(lane < 64, acc[...], wide(jnp.sum(k * k, -1, keepdims=True)))

        @pl.when(i == 2)
        def _():
            value[...] = (made + vec_ref[2:3]).astype(BF16)

    return call(
        body, places, 3,
        [(rows, None), (mod, None), (vecs, None)]
        + [(everyone, block_at(h, heads)) for h in range(heads)],
        [
            ((count, D), BF16, None),
            ((2, count, span), F32, pl.BlockSpec((1, count, span), lambda i, _: (jnp.minimum(i, 1), 0, 0))),
            ((count, span), BF16, None),
            ((count, HEAD), F32, None),
        ],
        [pltpu.VMEM((count, HEAD), F32)],
    )


def attend_self(places, everyone, pre, value, sums, other, vecs, cos_tab, sin_tab, heads, tokens):
    count = value.shape[0]
    per = heads_per_step(heads, 2)
    steps = heads // per

    def body(_, pre_ref, value_ref, sum_ref, other_ref, vec_ref, cos_ref, sin_ref, *refs):
        weights, (q_ref, k_ref, o_ref, y_ref, acc) = refs[:per], refs[per:]
        h = pl.program_id(0)
        total = sum_ref[...] + other_ref[...]
        q_inv = lax.rsqrt(total[:, 0:1] / D + NORM_EPS)
        k_inv = lax.rsqrt(total[:, 64:65] / D + NORM_EPS)
        cos, sin = cos_ref[...], sin_ref[...]
        outs = []
        for j in range(per):
            lanes = slice(j * HEAD, (j + 1) * HEAD)
            q = turned(pre_ref[0, :, lanes] * q_inv * vec_ref[3:4, lanes], cos, sin).astype(BF16)
            k = turned(pre_ref[1, :, lanes] * k_inv * vec_ref[4:5, lanes], cos, sin).astype(BF16)
            q_ref[:, lanes] = q
            k_ref[:, lanes] = k
            chance = softmax(self_scores(q, k, tokens))
            out = nn(chance.astype(BF16), value_ref[:, lanes]).astype(BF16)
            o_ref[j] = out
            outs.append(out)
        part = nt(jnp.concatenate(outs, 1), joined(weights))

        @pl.when(h == 0)
        def _():
            acc[...] = part

        @pl.when(h > 0)
        def _():
            acc[...] = acc[...] + part

        @pl.when(h == steps - 1)
        def _():
            y_ref[...] = acc[...].astype(BF16)

    lanes = head_lanes(count, per)
    return call(
        body, places, steps,
        [
            (pre, pl.BlockSpec((2, count, per * HEAD), lambda h, _: (0, 0, h))),
            (value, lanes), (sums, None), (other, None),
            (vecs, head_lanes(vecs.shape[0], per)), (cos_tab, None), (sin_tab, None),
        ]
        + [(everyone, block_at(3 * heads + j, per)) for j in range(per)],
        [
            (value.shape, BF16, lanes),
            (value.shape, BF16, lanes),
            ((heads, count, HEAD), BF16, pl.BlockSpec((per, count, HEAD), lambda h, _: (h, 0, 0))),
            ((count, D), BF16, None),
        ],
        [pltpu.VMEM((count, D), F32)],
    )


def project_text(places, everyone, context, vecs, heads):
    count = context.shape[0]
    span = heads * HEAD

    def body(_, text_ref, vec_ref, *refs):
        weights, (key, value, sums) = refs[:heads], refs[heads:]
        i = pl.program_id(0)
        made = nn(text_ref[...], joined(weights))

        @pl.when(i == 0)
        def _():
            k = made + vec_ref[6:7]
            key[...] = k
            sums[...] = wide(jnp.sum(k * k, -1, keepdims=True))

        @pl.when(i == 1)
        def _():
            value[...] = (made + vec_ref[7:8]).astype(BF16)

    return call(
        body, places, 2,
        [(context, None), (vecs, None)]
        + [(everyone, block_at(5 * heads + h, heads)) for h in range(heads)],
        [((count, span), F32, None), ((count, span), BF16, None), ((count, HEAD), F32, None)],
    )


def project_cross(places, everyone, rows, part, other, mod, shared, vecs, text_sums, heads):
    count = rows.shape[0]
    span = heads * HEAD
    text = text_sums.shape[0]

    def body(_, rows_ref, part_ref, other_ref, mod_ref, shared_ref, vec_ref, text_ref, *refs):
        weights, (branch, after, low, pre, sums) = refs[:heads], refs[heads:]
        y = part_ref[...].astype(F32) + other_ref[...].astype(F32) + shared_ref[0:1]
        branch[...] = y
        x = rows_ref[...] + mod_ref[2:3] * y
        after[...] = x
        unit, _ = normed(x)
        a = (unit * shared_ref[3:4] + shared_ref[4:5]).astype(BF16)
        low[...] = a
        q = nn(a, joined(weights)) + vec_ref[5:6]
        pre[...] = q
        sums[...] = pack_sums(jnp.sum(q * q, -1, keepdims=True), text_ref[:, 0:1])

    return call(
        body, places, 1,
        [(v, None) for v in (rows, part, other, mod, shared, vecs, text_sums)]
        + [(everyone, block_at(4 * heads + h)) for h in range(heads)],
        [
            ((count, D), F32, None),
            ((count, D), F32, None),
            ((count, D), BF16, None),
            ((count, span), F32, None),
            ((count, HEAD), F32, None),
        ],
    )


def attend_cross(places, everyone, pre, key_pre, value, sums, other, vecs, heads):
    count, text = pre.shape[0], value.shape[0]
    per = heads_per_step(heads, 6)
    steps = heads // per

    def body(_, pre_ref, key_ref, value_ref, sum_ref, other_ref, vec_ref, *refs):
        weights, (q_ref, k_ref, o_ref, y_ref, acc) = refs[:per], refs[per:]
        h = pl.program_id(0)
        total = sum_ref[...] + other_ref[...]
        q_inv = lax.rsqrt(total[:, 0:1] / D + NORM_EPS)
        k_inv = lax.rsqrt(unpack_text(total, text) / D + NORM_EPS)
        outs = []
        for j in range(per):
            lanes = slice(j * HEAD, (j + 1) * HEAD)
            q = (pre_ref[:, lanes] * q_inv * vec_ref[8:9, lanes]).astype(BF16)
            k = (key_ref[:, lanes] * k_inv * vec_ref[9:10, lanes]).astype(BF16)
            q_ref[:, lanes] = q
            k_ref[:, lanes] = k
            chance = softmax(nt(q, k) * SCALING)
            out = nn(chance.astype(BF16), value_ref[:, lanes]).astype(BF16)
            o_ref[j] = out
            outs.append(out)
        part = nt(jnp.concatenate(outs, 1), joined(weights))

        @pl.when(h == 0)
        def _():
            acc[...] = part

        @pl.when(h > 0)
        def _():
            acc[...] = acc[...] + part

        @pl.when(h == steps - 1)
        def _():
            y_ref[...] = acc[...].astype(BF16)

    return call(
        body, places, steps,
        [
            (pre, head_lanes(count, per)), (key_pre, head_lanes(text, per)),
            (value, head_lanes(text, per)), (sums, None), (other, None),
            (vecs, head_lanes(vecs.shape[0], per)),
        ]
        + [(everyone, block_at(7 * heads + j, per)) for j in range(per)],
        [
            (pre.shape, BF16, head_lanes(count, per)),
            (value.shape, BF16, head_lanes(text, per)),
            ((heads, count, HEAD), BF16, pl.BlockSpec((per, count, HEAD), lambda h, _: (h, 0, 0))),
            ((count, D), BF16, None),
        ],
        [pltpu.VMEM((count, D), F32)],
        vmem=40,
    )


def hidden_group(blocks):
    return max(g for g in (7, 5, 4, 3, 2, 1) if blocks % g == 0)


def block_lanes(where, everyone, held, sems, first, group, steps):
    i = pl.program_id(0)

    def fetch(step, act):
        slot = step % 3
        for j in range(group):
            copy = pltpu.make_async_copy(
                everyone.at[where[first + step * group + j]],
                held.at[slot, :, pl.ds(j * HEAD, HEAD)],
                sems.at[slot, j],
            )
            copy.start() if act else copy.wait()

    @pl.when(i == 0)
    def _():
        fetch(0, True)
        if steps > 1:
            fetch(1, True)

    @pl.when(i + 2 < steps)
    def _():
        fetch(i + 2, True)

    fetch(i, False)
    return held[i % 3]


def lanes_scratch(group):
    return [pltpu.VMEM((3, D, group * HEAD), BF16), pltpu.SemaphoreType.DMA((3, group))]


def hidden_back(places, everyone, mod, cot, heads, blocks):
    count = cot.shape[0]
    group = hidden_group(blocks)
    steps = blocks // group

    def body(where, weights, mod_ref, cot_ref, grad, out, held, sems):
        @pl.when(pl.program_id(0) == 0)
        def _():
            grad[...] = (mod_ref[5:6] * cot_ref[...]).astype(BF16)

        down = block_lanes(where, weights, held, sems, 8 * heads + blocks, group, steps)
        out[...] = nn(grad[...], down).astype(BF16)

    return call(
        body, places, steps,
        [(everyone, ANY), (mod, None), (cot, None)],
        [
            ((count, D), BF16, None),
            ((count, blocks * HEAD), BF16, pl.BlockSpec((count, group * HEAD), lambda i, _: (0, i))),
        ],
        lanes_scratch(group),
        vmem=40,
    )


def hidden_both(places, everyone, after_one, part, other, mod, shared, d_act, up_bias, heads, blocks):
    count = after_one.shape[0]
    group = hidden_group(blocks)
    steps = blocks // group
    span = group * HEAD

    def body(where, weights, after_ref, part_ref, other_ref, mod_ref, shared_ref, d_ref, bias_ref, after, low, hidden, d_hidden, d_bias, da_ref, acc, held, sems):
        i = pl.program_id(0)

        @pl.when(i == 0)
        def _():
            x = after_ref[...] + part_ref[...].astype(F32) + other_ref[...].astype(F32)
            x = x + shared_ref[1:2]
            after[...] = x
            unit, _ = normed(x)
            low[...] = (unit * (1.0 + mod_ref[4:5]) + mod_ref[3:4]).astype(BF16)
            acc[...] = jnp.zeros_like(acc)

        up = block_lanes(where, weights, held, sems, 8 * heads, group, steps)
        pre = nn(low[...], up) + bias_ref[...]
        square = pre * pre
        bent = jnp.tanh(GELU_COEF * (pre + 0.044715 * pre * square))
        act = (0.5 * pre * (1.0 + bent)).astype(BF16)
        slope = 0.5 * (1.0 + bent) + 0.5 * pre * (1.0 - bent * bent) * (
            GELU_COEF * (1.0 + 3.0 * 0.044715 * square)
        )
        dh = (d_ref[...].astype(F32) * slope).astype(BF16)
        d_bias[...] = total_of(dh.astype(F32))
        for j in range(group):
            hidden[j] = act[:, j * HEAD : (j + 1) * HEAD]
            d_hidden[j] = dh[:, j * HEAD : (j + 1) * HEAD]
        acc[...] = acc[...] + nt(dh, up)

        @pl.when(i == steps - 1)
        def _():
            da_ref[...] = acc[...].astype(BF16)

    tall = pl.BlockSpec((group, count, HEAD), lambda i, _: (i, 0, 0))
    flat = pl.BlockSpec((1, span), lambda i, _: (0, i))
    return call(
        body, places, steps,
        [(everyone, ANY)]
        + [(v, None) for v in (after_one, part, other, mod, shared)]
        + [(d_act, pl.BlockSpec((count, span), lambda i, _: (0, i))), (up_bias, flat)],
        [
            ((count, D), F32, None),
            ((count, D), BF16, None),
            ((blocks, count, HEAD), BF16, tall),
            ((blocks, count, HEAD), BF16, tall),
            (up_bias.shape, F32, flat),
            ((count, D), BF16, None),
        ],
        [pltpu.VMEM((count, D), F32)] + lanes_scratch(group),
        vmem=40,
    )


def hidden_out(places, everyone, hidden, heads):
    blocks, count = hidden.shape[:2]
    group = hidden_group(blocks)
    steps = blocks // group

    def body(where, weights, hidden_ref, y_ref, acc, held, sems):
        i = pl.program_id(0)
        down = block_lanes(where, weights, held, sems, 8 * heads + blocks, group, steps)
        part = nt(jnp.concatenate([hidden_ref[j] for j in range(group)], 1), down)

        @pl.when(i == 0)
        def _():
            acc[...] = part

        @pl.when(i > 0)
        def _():
            acc[...] = acc[...] + part

        @pl.when(i == steps - 1)
        def _():
            y_ref[...] = acc[...].astype(BF16)

    return call(
        body, places, steps,
        [(everyone, ANY), (hidden, pl.BlockSpec((group, count, HEAD), lambda i, _: (i, 0, 0)))],
        [((count, D), BF16, None)],
        [pltpu.VMEM((count, D), F32)] + lanes_scratch(group),
        vmem=40,
    )[0]


def cross_back(places, everyone, cot, after_two, part, other, mod, query, key, value, pre, key_pre, vecs, heads):
    count, text = query.shape[0], key.shape[0]
    per = heads_per_step(heads, 6)
    steps = heads // per

    def body(_, cot_ref, after_ref, part_ref, other_ref, mod_ref, q_ref, k_ref, v_ref, pre_ref, key_ref, vec_ref, *refs):
        weights, (dx_ref, low_ref, dq_ref, dk_ref, dv_ref, sums, q_acc, k_acc) = refs[:per], refs[per:]
        h = pl.program_id(0)

        @pl.when(h == 0)
        def _():
            da = part_ref[...].astype(F32) + other_ref[...].astype(F32)
            back, _ = normed_back(after_ref[...], da * (1.0 + mod_ref[4:5]))
            dx = cot_ref[...] + back
            dx_ref[...] = dx
            low_ref[...] = dx.astype(BF16)
            q_acc[...] = jnp.zeros_like(q_acc)
            k_acc[...] = jnp.zeros_like(k_acc)

        do_all = nn(low_ref[...], joined(weights)).astype(BF16)
        q_sums, k_sums = 0.0, 0.0
        for j in range(per):
            lanes = slice(j * HEAD, (j + 1) * HEAD)
            do = do_all[:, lanes]
            q, k = q_ref[:, lanes], k_ref[:, lanes]
            chance = softmax(nt(q, k) * SCALING)
            dp = nt(do, v_ref[:, lanes])
            ds = (chance * (dp - jnp.sum(chance * dp, -1, keepdims=True))).astype(BF16)
            dv_ref[j] = tn(chance.astype(BF16), do).astype(BF16)
            dq = nn(ds, k) * SCALING
            dk = tn(ds, q) * SCALING
            dq_ref[:, lanes] = dq
            dk_ref[:, lanes] = dk
            q_sums += pre_ref[:, lanes] * vec_ref[8:9, lanes] * dq
            k_sums += key_ref[:, lanes] * vec_ref[9:10, lanes] * dk
        q_acc[...] = q_acc[...] + q_sums
        k_acc[...] = k_acc[...] + k_sums

        @pl.when(h == steps - 1)
        def _():
            sums[...] = pack_sums(
                jnp.sum(q_acc[...], -1, keepdims=True), jnp.sum(k_acc[...], -1, keepdims=True)
            )

    return call(
        body, places, steps,
        [(v, None) for v in (cot, after_two, part, other, mod)]
        + [
            (query, head_lanes(count, per)), (key, head_lanes(text, per)),
            (value, head_lanes(text, per)), (pre, head_lanes(count, per)),
            (key_pre, head_lanes(text, per)), (vecs, head_lanes(vecs.shape[0], per)),
        ]
        + [(everyone, block_at(7 * heads + j, per)) for j in range(per)],
        [
            ((count, D), F32, None),
            ((count, D), BF16, None),
            (query.shape, F32, head_lanes(count, per)),
            (key.shape, F32, head_lanes(text, per)),
            ((heads, text, HEAD), BF16, pl.BlockSpec((per, text, HEAD), lambda h, _: (h, 0, 0))),
            ((count, HEAD), F32, None),
        ],
        [pltpu.VMEM((count, HEAD), F32), pltpu.VMEM((text, HEAD), F32)],
        vmem=48,
    )


def norm_grad(pre, inverse, gain, incoming, total):
    grad = inverse * (gain * incoming) - pre * (inverse * inverse * inverse) * (total / D)
    low = grad.astype(BF16)
    return low, total_of(low.astype(F32)), total_of(incoming * pre * inverse)


def cross_back_rows(places, everyone, pre, key_pre, dq, dk, dv, squares, squares_other, sums, sums_other, vecs, heads):
    count, text = pre.shape[0], key_pre.shape[0]
    per = heads_per_step(heads, 6)
    steps = heads // per

    def body(_, pre_ref, key_ref, dq_ref, dk_ref, dv_ref, sq_ref, sqo_ref, sum_ref, sumo_ref, vec_ref, *refs):
        weights, (gq_ref, gk_ref, vec_out, da_ref, acc) = refs[:per], refs[per:]
        h = pl.program_id(0)
        squares_all = sq_ref[...] + sqo_ref[...]
        total = sum_ref[...] + sumo_ref[...]
        q_inv = lax.rsqrt(squares_all[:, 0:1] / D + NORM_EPS)
        k_inv = lax.rsqrt(unpack_text(squares_all, text) / D + NORM_EPS)
        q_total, k_total = total[:, 0:1], unpack_text(total, text)
        lows = []
        for j in range(per):
            lanes = slice(j * HEAD, (j + 1) * HEAD)
            low_q, bias_q, gain_q = norm_grad(
                pre_ref[:, lanes], q_inv, vec_ref[8:9, lanes], dq_ref[:, lanes], q_total
            )
            low_k, bias_k, gain_k = norm_grad(
                key_ref[:, lanes], k_inv, vec_ref[9:10, lanes], dk_ref[:, lanes], k_total
            )
            gq_ref[j] = low_q
            gk_ref[j] = low_k
            lows.append(low_q)
            bias_v = total_of(dv_ref[j].astype(F32))
            vec_out[:, lanes] = jnp.concatenate(
                [bias_q, bias_k, bias_v, gain_q, gain_k, jnp.zeros((3, HEAD), F32)], 0
            )
        part = nt(jnp.concatenate(lows, 1), joined(weights))

        @pl.when(h == 0)
        def _():
            acc[...] = part

        @pl.when(h > 0)
        def _():
            acc[...] = acc[...] + part

        @pl.when(h == steps - 1)
        def _():
            da_ref[...] = acc[...].astype(BF16)

    tall = pl.BlockSpec((per, count, HEAD), lambda h, _: (h, 0, 0))
    tall_text = pl.BlockSpec((per, text, HEAD), lambda h, _: (h, 0, 0))
    return call(
        body, places, steps,
        [
            (pre, head_lanes(count, per)), (key_pre, head_lanes(text, per)),
            (dq, head_lanes(count, per)), (dk, head_lanes(text, per)), (dv, tall_text),
            (squares, None), (squares_other, None), (sums, None), (sums_other, None),
            (vecs, head_lanes(vecs.shape[0], per)),
        ]
        + [(everyone, block_at(4 * heads + j, per)) for j in range(per)],
        [
            ((heads, count, HEAD), BF16, tall),
            ((heads, text, HEAD), BF16, tall_text),
            ((8, heads * HEAD), F32, head_lanes(8, per)),
            ((count, D), BF16, None),
        ],
        [pltpu.VMEM((count, D), F32)],
        vmem=40,
    )


def self_back(places, everyone, dx_two, after_one, part, other, mod, shared, branch, query, key, value, pre, vecs, cos_tab, sin_tab, heads, tokens):
    count = query.shape[0]
    per = heads_per_step(heads, 2)
    steps = heads // per

    def body(_, dx_in, after_ref, part_ref, other_ref, mod_ref, shared_ref, branch_ref, q_ref, k_ref, v_ref, pre_ref, vec_ref, cos_ref, sin_ref, *refs):
        weights, (dx_ref, low_ref, d_ref, dv_ref, sums, vec_out, q_acc, k_acc) = refs[:per], refs[per:]
        h = pl.program_id(0)

        @pl.when(h == 0)
        def _():
            da = part_ref[...].astype(F32) + other_ref[...].astype(F32)
            back, _ = normed_back(after_ref[...], da * shared_ref[3:4])
            dx = dx_in[...] + back
            dx_ref[...] = dx
            low = (mod_ref[2:3] * dx).astype(BF16)
            low_ref[...] = low
            vec_out[0:1] = 0.5 * total_of(low.astype(F32))
            vec_out[1:2] = 0.5 * total_of(dx * branch_ref[...])
            q_acc[...] = jnp.zeros_like(q_acc)
            k_acc[...] = jnp.zeros_like(k_acc)

        do_all = nn(low_ref[...], joined(weights)).astype(BF16)
        cos, sin = cos_ref[...], -sin_ref[...]
        q_sums, k_sums = 0.0, 0.0
        for j in range(per):
            lanes = slice(j * HEAD, (j + 1) * HEAD)
            do = do_all[:, lanes]
            q, k = q_ref[:, lanes], k_ref[:, lanes]
            chance = softmax(self_scores(q, k, tokens))
            dp = nt(do, v_ref[:, lanes])
            ds = (chance * (dp - jnp.sum(chance * dp, -1, keepdims=True))).astype(BF16)
            dv_ref[j] = tn(chance.astype(BF16), do).astype(BF16)
            dq = turned(nn(ds, k) * SCALING, cos, sin)
            dk = turned(tn(ds, q) * SCALING, cos, sin)
            d_ref[0, :, lanes] = dq
            d_ref[1, :, lanes] = dk
            q_sums += pre_ref[0, :, lanes] * vec_ref[3:4, lanes] * dq
            k_sums += pre_ref[1, :, lanes] * vec_ref[4:5, lanes] * dk
        q_acc[...] = q_acc[...] + q_sums
        k_acc[...] = k_acc[...] + k_sums

        @pl.when(h == steps - 1)
        def _():
            lane = lax.broadcasted_iota(jnp.int32, q_acc.shape, 1)
            sums[...] = jnp.where(
                lane < 64,
                wide(jnp.sum(q_acc[...], -1, keepdims=True)),
                wide(jnp.sum(k_acc[...], -1, keepdims=True)),
            )

    lanes = head_lanes(count, per)
    pair = pl.BlockSpec((2, count, per * HEAD), lambda h, _: (0, 0, h))
    return call(
        body, places, steps,
        [(v, None) for v in (dx_two, after_one, part, other, mod, shared, branch)]
        + [
            (query, lanes), (key, lanes), (value, lanes), (pre, pair),
            (vecs, head_lanes(vecs.shape[0], per)), (cos_tab, None), (sin_tab, None),
        ]
        + [(everyone, block_at(3 * heads + j, per)) for j in range(per)],
        [
            ((count, D), F32, None),
            ((count, D), BF16, None),
            (pre.shape, F32, pair),
            ((heads, count, HEAD), BF16, pl.BlockSpec((per, count, HEAD), lambda h, _: (h, 0, 0))),
            ((count, HEAD), F32, None),
            ((2, D), F32, None),
        ],
        [pltpu.VMEM((count, HEAD), F32), pltpu.VMEM((count, HEAD), F32)],
        vmem=32,
    )


def self_back_rows(places, everyone, rows, pre, grads, dv, squares, squares_other, sums, sums_other, vecs, heads):
    count = pre.shape[1]
    per = heads_per_step(heads, 2)
    steps = heads // per

    def body(_, rows_ref, pre_ref, d_ref, dv_ref, sq_ref, sqo_ref, sum_ref, sumo_ref, vec_ref, *refs):
        weights, (gq_ref, gk_ref, vec_out, da_ref, row_out, acc) = refs[: 3 * per], refs[3 * per :]
        h = pl.program_id(0)
        squares_all = sq_ref[...] + sqo_ref[...]
        total = sum_ref[...] + sumo_ref[...]
        inverses = [
            lax.rsqrt(squares_all[:, n : n + 1] / D + NORM_EPS) for n in (0, 64)
        ]
        lows = []
        for j in range(per):
            lanes = slice(j * HEAD, (j + 1) * HEAD)
            biases, gains = [], []
            for n, out in enumerate((gq_ref, gk_ref)):
                low, bias, gain = norm_grad(
                    pre_ref[n, :, lanes], inverses[n], vec_ref[3 + n : 4 + n, lanes],
                    d_ref[n, :, lanes], total[:, 64 * n : 64 * n + 1],
                )
                out[j] = low
                lows.append(low)
                biases.append(bias)
                gains.append(gain)
            dv_low = dv_ref[j]
            lows.append(dv_low)
            vec_out[:, lanes] = jnp.concatenate(
                biases + [total_of(dv_low.astype(F32))] + gains + [jnp.zeros((3, HEAD), F32)], 0
            )
        part = nt(jnp.concatenate(lows, 1), joined(weights))

        @pl.when(h == 0)
        def _():
            acc[...] = part

        @pl.when(h > 0)
        def _():
            acc[...] = acc[...] + part

        @pl.when(h == steps - 1)
        def _():
            da = acc[...]
            da_ref[...] = da.astype(BF16)
            row_out[0:1] = total_of(da)
            row_out[1:2] = total_of(da * normed(rows_ref[...])[0])

    tall = pl.BlockSpec((per, count, HEAD), lambda h, _: (h, 0, 0))
    pair = pl.BlockSpec((2, count, per * HEAD), lambda h, _: (0, 0, h))
    return call(
        body, places, steps,
        [
            (rows, None), (pre, pair), (grads, pair), (dv, tall), (squares, None),
            (squares_other, None), (sums, None), (sums_other, None),
            (vecs, head_lanes(vecs.shape[0], per)),
        ]
        + [(everyone, block_at(n * heads + j, per)) for j in range(per) for n in range(3)],
        [
            ((heads, count, HEAD), BF16, tall),
            ((heads, count, HEAD), BF16, tall),
            ((8, heads * HEAD), F32, head_lanes(8, per)),
            ((count, D), BF16, None),
            ((2, D), F32, None),
        ],
        [pltpu.VMEM((count, D), F32)],
        vmem=40,
    )


def shared_sums(places, after_one, after_two, grad_two, grad_three, cot, da_two, da_three, y_three, shared):
    def body(_, x1_ref, x2_ref, dy2, dy3, cot_ref, da2, da3, y3, shared_ref, out):
        out[...] = jnp.zeros_like(out)
        out[1:2] = 0.5 * total_of(dy2[...].astype(F32))
        out[2:3] = 0.5 * total_of(dy3[...].astype(F32))
        part = da3[...].astype(F32)
        out[3:4] = total_of(part * normed(x1_ref[...])[0])
        out[4:5] = total_of(part)
        part = da2[...].astype(F32)
        out[8:9] = total_of(part)
        out[9:10] = total_of(part * normed(x2_ref[...])[0])
        out[10:11] = total_of(cot_ref[...] * (y3[...].astype(F32) + 0.5 * shared_ref[2:3]))

    return call(
        body, places, 1,
        [(v, None) for v in (after_one, after_two, grad_two, grad_three, cot, da_two, da_three, y_three, shared)],
        [(shared.shape, F32, None)],
    )[0]


def body(
    latents,
    context,
    cotangent,
    positions,
    step_ids,
    owners,
    time_table,
    master,
    first_moment,
    second_moment,
    head_params,
    head_first,
    head_second,
    shared_params,
    shared_first,
    shared_second,
):
    tensors = lax.axis_size("tensor")
    devices = lax.axis_size("dp")
    slot_count = master.shape[1]
    tile_count = owners.shape[0]
    heads_here = HEADS // tensors
    blocks_here = FF // (HEAD * tensors)
    width_here = D // tensors
    places, holder = owner_layout(owners, slot_count, devices)
    scales = tile_scales(tile_count, heads_here, blocks_here)
    rank = pair_rank()
    my_slots = lax.axis_index("dp") * slot_count + jnp.arange(slot_count, dtype=jnp.int32)
    holds = places[None, :] == my_slots[:, None]
    slot_scale = jnp.sum(jnp.where(holds, scales[None, :], 0.0), axis=1)
    filled = jnp.any(holds, axis=1)
    scaled = (master[0] * slot_scale[:, None, None]).astype(jnp.bfloat16)
    half = latents.shape[0]
    tokens = 2 * half
    count = -(-tokens // 16) * 16
    taller = ((0, -half % 16), (0, 0))
    small = jnp.concatenate(
        [
            head_params[0],
            positions.reshape(-1).astype(jnp.float32),
            step_ids.astype(jnp.float32),
        ]
    )
    packed = jnp.pad(small, (0, -small.shape[0] % 1024)).reshape(-1, HEAD)
    everyone, lats, cots, context, packed = gather_slots(
        scaled, jnp.pad(latents, taller), jnp.pad(cotangent, taller), context, packed
    )
    small = packed.reshape(-1)
    vectors = small[: head_params.shape[1]]
    small = small[head_params.shape[1] :]
    positions = small[: positions.size].reshape(positions.shape)
    step = small[positions.size]
    vecs = vectors[: 10 * width_here].reshape(10, width_here)
    up_bias = vectors[10 * width_here :].reshape(1, -1)
    chosen = (step == jnp.arange(TSTEPS)).astype(jnp.float32)
    mod = shared_params[5:11] + jnp.einsum(
        "s,skd->kd", chosen, time_table, precision=lax.Precision.HIGHEST
    )
    cos_tab, sin_tab = rope_tables(positions, HEAD)
    sin_tab = jnp.where(jnp.arange(HEAD) % 2 == 0, -sin_tab, sin_tab)
    cos_tab, sin_tab = (jnp.pad(t, ((0, count - tokens), (0, 0))) for t in (cos_tab, sin_tab))

    def all_rows(halves):
        rows = jnp.concatenate([halves[0, :half], halves[1, :half]], 0)
        return jnp.pad(rows, ((0, count - tokens), (0, 0))).astype(jnp.float32)

    def upright(rows):
        return jnp.pad(rows, ((0, -rows.shape[0] % HEAD), (0, 0))).T

    def beside(*values):
        return lax.optimization_barrier(values)

    rows, cot = all_rows(lats), all_rows(cots)
    low_one, pre_one, value_one, squares_one = project_self(
        places, everyone, rows, mod, vecs, heads_here
    )
    squares_one_other = pair_swap(squares_one)
    query_one, key_one, heads_one, part_one = attend_self(
        places, everyone, pre_one, value_one, squares_one, squares_one_other, vecs, cos_tab,
        sin_tab, heads_here, tokens,
    )
    part_one, context = beside(part_one, context)
    part_one_other = pair_swap(part_one)
    key_pre, value_two, text_squares = project_text(places, everyone, context, vecs, heads_here)
    left_context, left_one = upright(context), upright(low_one)
    part_one_other, key_pre, left_context, left_one = beside(
        part_one_other, key_pre, left_context, left_one
    )
    branch_one, after_one, low_two, pre_two, squares_two = project_cross(
        places, everyone, rows, part_one, part_one_other, mod, shared_params, vecs,
        text_squares, heads_here,
    )
    squares_two_other = pair_swap(squares_two)
    query_two, key_two, heads_two, part_two = attend_cross(
        places, everyone, pre_two, key_pre, value_two, squares_two, squares_two_other, vecs,
        heads_here,
    )
    part_two, cot, low_two = beside(part_two, cot, low_two)
    part_two_other = pair_swap(part_two)
    grad_three, d_act = hidden_back(places, everyone, mod, cot, heads_here, blocks_here)
    left_two, left_grad_three = upright(low_two), upright(grad_three)
    part_two_other, d_act, left_two, left_grad_three = beside(
        part_two_other, d_act, left_two, left_grad_three
    )
    after_two, low_three, hidden, d_hidden, d_up_bias, da_two = hidden_both(
        places, everyone, after_one, part_two, part_two_other, mod, shared_params, d_act, up_bias,
        heads_here, blocks_here,
    )
    da_two_other = pair_swap(da_two)
    y_three = hidden_out(places, everyone, hidden, heads_here)
    left_three = upright(low_three)
    da_two_other, y_three, left_three = beside(da_two_other, y_three, left_three)
    dx_two, grad_two, dq_two, dk_two, dv_two, sums_two = cross_back(
        places, everyone, cot, after_two, da_two, da_two_other, mod, query_two, key_two,
        value_two, pre_two, key_pre, vecs, heads_here,
    )
    query_grad_two, key_grad_two, vecs_two, da_three = cross_back_rows(
        places, everyone, pre_two, key_pre, dq_two, dk_two, dv_two, squares_two,
        squares_two_other, sums_two, pair_swap(sums_two), vecs, heads_here,
    )
    da_three_other = pair_swap(da_three)
    shared_grad = shared_sums(
        places, after_one, after_two, grad_two, grad_three, cot, da_two, da_three, y_three,
        shared_params,
    )
    left_grad_two = upright(grad_two)
    da_three_other, shared_grad, left_grad_two = beside(da_three_other, shared_grad, left_grad_two)
    dx_one, grad_one, d_one, dv_one, sums_one, rows_a = self_back(
        places, everyone, dx_two, after_one, da_three, da_three_other, mod, shared_params,
        branch_one, query_one, key_one, value_one, pre_one, vecs, cos_tab, sin_tab, heads_here,
        tokens,
    )
    query_grad_one, key_grad_one, vecs_one, da_one, rows_b = self_back_rows(
        places, everyone, rows, pre_one, d_one, dv_one, squares_one, squares_one_other, sums_one,
        pair_swap(sums_one), vecs, heads_here,
    )
    shared_grad = jnp.concatenate(
        [rows_a[0:1], shared_grad[1:5], rows_b, rows_a[1:2], shared_grad[8:]], 0
    )
    head_grad = jnp.concatenate(
        [vecs_one[:5].reshape(-1), vecs_two[:5].reshape(-1), d_up_bias.reshape(-1)]
    )
    tensor_rank = lax.axis_index("tensor")
    head_padded = jnp.where(jnp.arange(tensors)[:, None] == rank, head_grad[None, :], 0.0)
    vector = jnp.concatenate([head_padded.reshape(-1), shared_grad.reshape(-1)])
    vector = jnp.pad(vector, (0, -vector.shape[0] % 1024)).reshape(-1, 128)
    parts, vector, output, grad_input = reduce_slots(
        holder,
        kind_of_blocks(tile_count, heads_here, blocks_here),
        (left_one, upright(grad_one), left_two, left_context, left_grad_two, left_three, left_grad_three),
        (
            query_grad_one,
            key_grad_one,
            dv_one,
            heads_one,
            query_grad_two,
            key_grad_two,
            dv_two,
            heads_two,
            d_hidden,
            hidden,
        ),
        vector,
        (rows, after_two, dx_one, y_three, da_one),
        jnp.concatenate([mod[5:6], mod[1:2], shared_params[2:3], jnp.zeros((5, D), F32)], 0),
        slot_count,
    )
    output, grad_input = (
        lax.dynamic_slice_in_dim(v, lax.axis_index("tensor") * half, half, 0)
        for v in (output, grad_input)
    )
    new_master, new_first, new_second = adam_slots(
        parts, master, first_moment, second_moment, slot_scale, filled
    )
    vector = vector.reshape(-1)
    head_total = vector[: head_padded.size].reshape(head_padded.shape)
    shared_total = vector[head_padded.size : head_padded.size + shared_grad.size]
    shared_total = shared_total.reshape(shared_grad.shape)
    mine_head = lax.dynamic_slice_in_dim(head_total, tensor_rank, 1, 0)
    new_head, new_head_first, new_head_second = adam_step(
        head_params, mine_head, head_first, head_second, VECTOR_RATE, 0.0
    )
    new_shared, new_shared_first, new_shared_second = adam_step(
        shared_params, shared_total, shared_first, shared_second, VECTOR_RATE, 0.0
    )
    return (
        output,
        grad_input,
        new_master,
        new_first,
        new_second,
        new_head,
        new_head_first,
        new_head_second,
        new_shared,
        new_shared_first,
        new_shared_second,
    )


def solution(mesh):
    return jax.shard_map(
        body,
        mesh=mesh,
        in_specs=(
            P(("dp", "tensor"), None),
            P("dp", None),
            P(("dp", "tensor"), None),
            P(None, "dp"),
            P("dp"),
            P(),
            P(),
            P("tensor", "dp", None, None),
            P("tensor", "dp", None, None),
            P("tensor", "dp", None, None),
            P("tensor", None),
            P("tensor", None),
            P("tensor", None),
            P(),
            P(),
            P(),
        ),
        out_specs=(
            P(("dp", "tensor"), None),
            P(("dp", "tensor"), None),
            P("tensor", "dp", None, None),
            P("tensor", "dp", None, None),
            P("tensor", "dp", None, None),
            P("tensor", None),
            P("tensor", None),
            P("tensor", None),
            P(),
            P(),
            P(),
        ),
        check_vma=False,
    )
```

```python
import functools

import jax
import jax.numpy as jnp
from jax import lax
from jax.experimental import pallas as pl
from jax.experimental.pallas import tpu as pltpu
from jax.sharding import PartitionSpec as P

D = 1536
HEADS = 12
HEAD = 128
FF = 8960
TSTEPS = 16
STEPC = 10


NORM_EPS = 1e-06
BETA_ONE = 0.9
BETA_TWO = 0.999
ADAM_EPS = 1e-08
TILE_RATE = 1.0
TILE_DECAY = 0.1
VECTOR_RATE = 0.5
GELU_COEF = 0.7978845608028654


def rope_tables(token_places, head_size):
    sixths = head_size // 6
    frame_pairs = (head_size - 4 * sixths) // 2
    frame_freq = 10000.0 ** (-jnp.arange(frame_pairs, dtype=jnp.float32) / frame_pairs)
    side_freq = 10000.0 ** (-jnp.arange(sixths, dtype=jnp.float32) / sixths)
    spots = token_places.astype(jnp.float32)
    angles = jnp.concatenate(
        [
            spots[0][..., None] * frame_freq,
            spots[1][..., None] * side_freq,
            spots[2][..., None] * side_freq,
        ],
        -1,
    )
    angles = jnp.repeat(angles, 2, axis=-1)
    return (jnp.cos(angles), jnp.sin(angles))


def owner_layout(owners, slot_count, devices):
    indices = jnp.arange(owners.shape[0], dtype=jnp.int32)
    same_owner = (owners[:, None] == owners[None, :]) & (indices[None, :] < indices[:, None])
    slot_of = jnp.sum(same_owner.astype(jnp.int32), axis=1)
    places = owners * slot_count + slot_of
    spots = jnp.arange(slot_count * devices, dtype=jnp.int32)
    holder = (
        jnp.sum(jnp.where(places[None, :] == spots[:, None], indices[None, :] + 1, 0), axis=1) - 1
    )
    return (places, holder)


def tile_scales(tile_count, heads_here, blocks_here):
    indices = jnp.arange(tile_count)
    scale_in = D ** (-0.5)
    scale_out = HEADS ** (-0.5)
    scale_down = FF ** (-0.5)
    scales = jnp.where(
        indices < 3 * heads_here,
        scale_in,
        jnp.where(
            indices < 4 * heads_here,
            scale_out,
            jnp.where(
                indices < 7 * heads_here,
                scale_in,
                jnp.where(
                    indices < 8 * heads_here,
                    scale_out,
                    jnp.where(indices < 8 * heads_here + blocks_here, scale_in, scale_down),
                ),
            ),
        ),
    )
    return scales.astype(jnp.float32)


def adam_step(weight, gradient, moment_one, moment_two, step_rate, decay_rate):
    first_new = BETA_ONE * moment_one + (1.0 - BETA_ONE) * gradient
    second_new = BETA_TWO * moment_two + (1.0 - BETA_TWO) * gradient * gradient
    first_hat = first_new / (1.0 - BETA_ONE**STEPC)
    second_hat = second_new / (1.0 - BETA_TWO**STEPC)
    weight_new = weight - step_rate * (
        first_hat / (jnp.sqrt(second_hat) + ADAM_EPS) + decay_rate * weight
    )
    return (weight_new, first_new, second_new)


MESH = pl.DeviceIdType.MESH
ANY = pl.BlockSpec(memory_space=pl.ANY)
MIB = 1 << 20


def chip_pairs():
    return lax.axis_size("dp") == 16 and lax.axis_size("tensor") == 2


def pair_rank():
    if chip_pairs():
        return (lax.axis_index("dp") // 4) % 2
    return lax.axis_index("tensor")


def pair_swap(value):
    if chip_pairs():
        return lax.ppermute(value, "dp", [(i, i ^ 4) for i in range(16)])
    return lax.ppermute(value, "tensor", [(0, 1), (1, 0)])


def pair_sums(*values):
    stacked = jnp.concatenate([v.reshape(-1) for v in values])
    total = stacked + pair_swap(stacked)
    out, at = [], 0
    for v in values:
        out.append(total[at : at + v.size].reshape(v.shape))
        at += v.size
    return tuple(out)


def place_of():
    chip, core = lax.axis_index("dp"), lax.axis_index("tensor")
    z, y, x = chip // 4, (chip // 2) % 2, chip % 2
    return chip, core, z, y, x


def column_of(z, y, x, k):
    high, low_bit = z // 2, z % 2
    if k & 2:
        high = 1 - high
    if k & 1:
        low_bit = 1 - low_bit
    return (2 * high + low_bit) * 4 + 2 * y + x


def greet(chip, core, z, y, x):
    barrier = pltpu.get_barrier_semaphore()
    friends = []
    for k in range(4):
        for flip in (0, 1):
            if k or flip:
                friends.append((column_of(z, y, x, k), core if flip == 0 else 1 - core))
    for side in (core, 1 - core):
        friends.append((column_of(z, y, 1 - x, 0), side))
        friends.append((column_of(z, 1 - y, x, 0), side))
    for friend in friends:
        pl.semaphore_signal(barrier, inc=1, device_id=friend, device_id_type=MESH)
    pl.semaphore_wait(barrier, len(friends))


def gather_kernel(
    own, lat, cot, text, small, out, lats, cots, texts, smalls, relay_a, relay_b, clip_s, clip_r,
    out_s, out_r, over_s, over_r, near_s, col_r, x_s, x_r, y_s, y_r, sib_s, sib_r,
):
    chip, core, z, y, x = place_of()
    rank = z % 2
    half = own.shape[1] // 2
    part = half // 2
    at_x = column_of(z, y, 1 - x, 0)
    at_y = column_of(z, 1 - y, x, 0)
    greet(chip, core, z, y, x)

    batch = max(n for n in (1, 2, 3) if own.shape[0] % n == 0)
    batches = own.shape[0] // batch
    turns = 4 * batches
    mine, other = core * half, (1 - core) * half
    sibling = (chip, 1 - core)
    tail = pl.ds((batches - 1) * batch, batch)

    def outward(n, h):
        rows = pl.ds(h * half + n * part, part)
        return pltpu.make_async_remote_copy(
            src_ref=own.at[tail, rows, :], dst_ref=(relay_a, relay_b)[n].at[core],
            send_sem=out_s.at[2 * n + h], recv_sem=out_r.at[2 * n + core],
            device_id=((at_x, at_y)[n], h), device_id_type=MESH,
        )

    def case(s):
        late = jnp.maximum(s - batches, 0)
        k = jnp.where(s < batches, 0, 1 + late % 3)
        return k, jnp.where(s < batches, s, late // 3)

    def remote(unit, g, first, count, send, recv, device):
        piece = out.at[
            unit, pl.ds(g * batch, batch), pl.ds(pl.multiple_of(first, 16), count), :
        ]
        return pltpu.make_async_remote_copy(
            src_ref=piece, dst_ref=piece, send_sem=send, recv_sem=recv,
            device_id=device, device_id_type=MESH,
        )

    def own_copy(g, j, h):
        target = (toggled(z, y, x, 0, 0, 2 * j) // 8 * 8) + core * 4 + 2 * y + x
        part_of = (pl.ds(g * batch, batch), pl.ds(h * half, half))
        src = own.at[part_of[0], part_of[1], :]
        dst = out.at[chip, part_of[0], part_of[1], :]
        recv = col_r.at[z * batches + g]
        go = pltpu.make_async_remote_copy(
            src_ref=src, dst_ref=dst, send_sem=near_s.at[(2 * j + h) * batches + g],
            recv_sem=recv, device_id=(target, h), device_id_type=MESH,
        )
        return go, pltpu.make_async_copy(src, dst, recv)

    for n in range(2):
        for h in range(2):
            outward(n, h).start()
    for g in range(batches):
        for j in range(2):
            for h in range(2):
                go, here = own_copy(g, j, h)
                if j == 1:
                    go.start()
                    continue
                stays = jnp.logical_and(rank == core, core == h)

                @pl.when(stays)
                def _():
                    here.start()

                @pl.when(jnp.logical_not(stays))
                def _():
                    go.start()

    pair_chip = column_of(z, y, x, 1)
    rows_of_text = text.shape[0] // 2

    def clip_pieces(h):
        share = pl.ds(h * rows_of_text, rows_of_text)
        return ((lat, lats.at[h]), (cot, cots.at[h]), (text.at[share], texts.at[share]))

    home = rank == core
    trade = pltpu.make_async_remote_copy(
        src_ref=small, dst_ref=smalls, send_sem=clip_s.at[6], recv_sem=clip_r.at[6],
        device_id=(pair_chip, 1 - core), device_id_type=MESH,
    )
    keep = pltpu.make_async_copy(small, smalls, clip_r.at[6])

    @pl.when(home)
    def _():
        keep.start()

    @pl.when(jnp.logical_not(home))
    def _():
        trade.start()

    def hand_out(h, n, wait):
        src, dst = clip_pieces(h)[n]
        far = pltpu.make_async_remote_copy(
            src_ref=src, dst_ref=dst, send_sem=clip_s.at[n], recv_sem=clip_r.at[3 * h + n],
            device_id=(pair_chip, rank), device_id_type=MESH,
        )
        near = pltpu.make_async_remote_copy(
            src_ref=src, dst_ref=dst, send_sem=clip_s.at[3 + n], recv_sem=clip_r.at[3 * h + n],
            device_id=(chip, 1 - core), device_id_type=MESH,
        )
        here = pltpu.make_async_copy(src, dst, clip_r.at[3 * h + n])

        @pl.when(core == h)
        def _():
            if wait:
                far.wait_send()
            else:
                far.start()

            @pl.when(home)
            def _():
                if not wait:
                    here.start()

            @pl.when(jnp.logical_not(home))
            def _():
                if wait:
                    near.wait_send()
                else:
                    near.start()

    for n in range(3):
        for h in range(2):
            hand_out(h, n, False)


    def spans(n, wide):
        part_a, part_b = (mine, part), (mine + part, part)
        if wide:
            return part_b, part_a
        return (part_a, part_b) if n else ((mine, half), (mine, half))

    def over_x(s, n, wide, coming=0):
        k, g = case(s)
        i = turns * n + s
        first, count = spans(n, wide)[0]
        unit = toggled(z, y, x, n, coming, k)
        return remote(unit, g, first, count, x_s.at[i], x_r.at[i], (at_x, core))

    def over_y(s, n, wide, coming=0):
        k, g = case(s)
        i = turns * n + s
        first, count = spans(n, wide)[1]
        unit = toggled(z, y, x, coming, n, k)
        return remote(unit, g, first, count, y_s.at[i], y_r.at[i], (at_y, core))

    def to_sib(s, column, piece, away=False):
        k, g = case(s)
        i = turns * ({(0, 2): 0, (1, 2): 1, (2, 2): 2}.get((column, piece), 2 * column + piece - 1)) + s
        unit = toggled(z, y, x, column // 2, column % 2, k)
        first = (other if away else mine) + (part if piece == 1 else 0)
        count = half if piece == 2 else part
        return remote(unit, g, first, count, sib_s.at[i], sib_r.at[i], sibling)

    def column_in(s, wide):
        k, g = case(s)
        unit = toggled(z, y, x, 0, 0, k)
        piece = out.at[
            unit, pl.ds(g * batch, batch), pl.ds(pl.multiple_of(mine, 16), half), :
        ]
        pltpu.make_async_copy(piece, piece, col_r.at[unit // 4 * batches + g]).wait()
        over_x(s, 0, wide).start()
        over_y(s, 0, wide).start()
        to_sib(s, 0, 2).start()
        if wide:
            for n, (spot, first) in enumerate(((toggled(z, y, x, 0, 1, k), mine), (toggled(z, y, x, 1, 0, k), mine + part))):
                piece = out.at[
                    spot, pl.ds(g * batch, batch), pl.ds(pl.multiple_of(first, 16), part), :
                ]
                pltpu.make_async_copy(piece, piece, over_r.at[4 * n + spot // 4]).wait()
            over_y(s, 1, wide).start()
            to_sib(s, 1, 0).start()
            over_x(s, 1, wide).start()
            to_sib(s, 2, 1).start()

    def side_in(s, wide):
        over_x(s, 0, wide, 1).wait_recv()
        if wide:
            to_sib(s, 1, 1).start()
        else:
            over_y(s, 1, wide).start()
            to_sib(s, 1, 2).start()
        over_y(s, 0, wide, 1).wait_recv()
        if wide:
            to_sib(s, 2, 0).start()
        else:
            over_x(s, 1, wide).start()
            to_sib(s, 2, 2).start()

    def corner_in(s, wide):
        over_x(s, 1, wide, 1).wait_recv()
        to_sib(s, 3, 1 if wide else 0).start()
        over_y(s, 1, wide, 1).wait_recv()
        to_sib(s, 3, 0 if wide else 1).start()

    def either(s, act):
        _, g = case(s)
        wide = g == batches - 1

        @pl.when(wide)
        def _():
            act(s, True)

        @pl.when(jnp.logical_not(wide))
        def _():
            act(s, False)

    def onward(n, t, j):
        origin = (at_x, at_y)[n]
        src = (relay_a, relay_b)[n].at[t]
        rows = pl.ds(pl.multiple_of(mine + n * part, 16), part)
        dst = out.at[origin, tail, rows, :]
        high = (z // 2 + j) % 2
        recv = over_r.at[4 * n + z]
        go = pltpu.make_async_remote_copy(
            src_ref=src, dst_ref=dst, send_sem=over_s.at[4 * n + 2 * t + j], recv_sem=recv,
            device_id=((2 * high + t) * 4 + 2 * y + x, core), device_id_type=MESH,
        )
        return go, pltpu.make_async_copy(src, dst, recv)

    def pass_on(n):
        for t in range(2):
            piece = (relay_a, relay_b)[n].at[t]
            pltpu.make_async_copy(piece, piece, out_r.at[2 * n + t]).wait()
            for j in range(2):
                go, here = onward(n, t, j)
                if j == 1:
                    go.start()
                    continue

                @pl.when(rank == t)
                def _():
                    here.start()

                @pl.when(rank != t)
                def _():
                    go.start()

    def turn(step, carry):
        @pl.when(step < turns)
        def _():
            either(step, column_in)

        @pl.when(jnp.logical_and(step >= 1, step < turns + 1))
        def _():
            either(step - 1, side_in)

        @pl.when(step >= 2)
        def _():
            either(step - 2, corner_in)

        @pl.when(step == 0)
        def _():
            pass_on(0)
            pass_on(1)

        return carry

    lax.fori_loop(0, turns + 2, turn, 0)

    def close(s, wide):
        for n in range(2):
            over_x(s, n, wide).wait_send()
            over_y(s, n, wide).wait_send()
        pieces = [(0, 2), (3, 0), (3, 1)]
        pieces += [(1, 0), (1, 1), (2, 0), (2, 1)] if wide else [(1, 2), (2, 2)]
        for column, piece in pieces:
            to_sib(s, column, piece).wait_send()
            to_sib(s, column, piece, True).wait_recv()

    def settle(s, carry):
        either(s, close)
        return carry

    lax.fori_loop(0, turns, settle, 0)
    for n in range(2):
        for h in range(2):
            outward(n, h).wait_send()
        for t in range(2):
            onward(n, t, 1)[0].wait_send()

            @pl.when(rank != t)
            def _():
                onward(n, t, 0)[0].wait_send()

    for g in range(batches):
        for j in range(2):
            for h in range(2):
                go, _ = own_copy(g, j, h)
                if j == 1:
                    go.wait_send()
                    continue

                @pl.when(jnp.logical_not(jnp.logical_and(rank == core, core == h)))
                def _():
                    go.wait_send()

    for n in range(3):
        for h in range(2):
            hand_out(h, n, True)
            dst = clip_pieces(h)[n][1]
            pltpu.make_async_copy(dst, dst, clip_r.at[3 * h + n]).wait()

    @pl.when(jnp.logical_not(home))
    def _():
        trade.wait_send()

    pltpu.make_async_copy(smalls, smalls, clip_r.at[6]).wait()


def gather_slots(scaled, lat, cot, text, small):
    if not chip_pairs():
        everyone = lax.all_gather(scaled, "dp", axis=0, tiled=True)
        lats, cots = (lax.all_gather(v, "tensor") for v in (lat, cot))
        return everyone, lats, cots, text, small
    dma = pltpu.SemaphoreType.DMA
    turns = 4 * scaled.shape[0] // max(n for n in (1, 2, 3) if scaled.shape[0] % n == 0)
    counts = (7, 7, 4, 4, 8, 8, turns, turns) + (2 * turns,) * 4 + (7 * turns,) * 2
    batch = 4 * scaled.shape[0] // turns
    relay = pltpu.HBM((2, batch, scaled.shape[1] // 4, scaled.shape[2]), scaled.dtype)
    everyone, *rest = pl.pallas_call(
        gather_kernel,
        out_shape=[
            pltpu.HBM((16,) + scaled.shape, scaled.dtype),
            pltpu.HBM((2,) + lat.shape, lat.dtype),
            pltpu.HBM((2,) + cot.shape, cot.dtype),
            pltpu.HBM(text.shape, text.dtype),
            pltpu.HBM(small.shape, small.dtype),
            relay,
            relay,
        ],
        in_specs=[ANY] * 5,
        out_specs=[ANY] * 7,
        scratch_shapes=[dma((n,)) for n in counts],
        compiler_params=pltpu.CompilerParams(
            collective_id=0, has_side_effects=True, vmem_limit_bytes=4 * MIB
        ),
    )(scaled, lat, cot, pltpu.with_memory_space_constraint(text, pltpu.HBM), small)
    return everyone.reshape((-1,) + scaled.shape[1:]), *rest[:4]


def toggled(z, y, x, flip_y, flip_x, k):
    high = (z // 2 + k // 2) % 2
    low_bit = (z % 2 + k % 2) % 2
    return (2 * high + low_bit) * 4 + 2 * ((y + flip_y) % 2) + (x + flip_x) % 2


def reduce_kernel(
    kind, block, *refs,
):
    (
        *pieces, rows_in, after_in, dx_in, y_in, da_in, gains, vec_in,
        final, vec_out, result, result_grad, y_other, da_other, from_sib, from_x, from_y, corner_a, corner_b,
        left, right, ring, corners, side_x, side_y, middle, stage, vec_box, end_wide, end_low,
        load_s, stage_s, sib_s, sib_r, x_s, x_r, y_s, y_r, ca_s, ca_r, cb_s, cb_r, f_s, f_r, v_s, v_r,
        end_s, end_r, end_load,
    ) = refs
    chip, core, z, y, x = place_of()
    rank = z % 2
    slots, width, lanes = final.shape[1:]
    half = width // 2
    part = half // 2
    at_x = toggled(z, y, x, 0, 1, 0)
    at_y = toggled(z, y, x, 1, 0, 0)
    sibling = (chip, 1 - core)
    mates = (
        sibling,
        (at_x, core),
        (at_y, core),
        (toggled(z, y, x, 0, 0, 1), core),
        (toggled(z, y, x, 0, 0, 2), core),
    )

    kinds = left.shape[0]
    depth = right.shape[1]
    loads = []
    for i in range(kinds):
        columns = pieces[i].shape[1]
        loads.append(
            pltpu.make_async_copy(pieces[i], left.at[i, :, pl.ds(0, columns)], load_s.at[i])
        )
    first = 0
    blank = []
    for i, piece in enumerate(pieces[kinds:]):
        number, rows = piece.shape[:2]
        loads.append(
            pltpu.make_async_copy(
                piece, right.at[pl.ds(first, number), pl.ds(0, rows), :], load_s.at[kinds + i]
            )
        )
        if rows < depth:
            blank.append((first, number, rows))
        first += number
    for load in loads:
        load.start()
    for start, number, rows in blank:

        def clear(i, carry):
            right[start + i, pl.ds(rows, depth - rows), :] = jnp.zeros(
                (depth - rows, lanes), right.dtype
            )
            return carry

        lax.fori_loop(0, number, clear, 0)
    right[first] = jnp.zeros((depth, lanes), right.dtype)
    for i in range(kinds):
        columns = pieces[i].shape[1]
        if columns < depth:
            left[i, :, pl.ds(columns, depth - columns)] = jnp.zeros(
                (width, depth - columns), left.dtype
            )
    vec_out[...] = vec_in[...]
    greet(chip, core, z, y, x)
    for load in loads:
        load.wait()

    def remote(src, dst, send, recv, device):
        return pltpu.make_async_remote_copy(
            src_ref=src, dst_ref=dst, send_sem=send, recv_sem=recv,
            device_id=device, device_id_type=MESH,
        )

    batch = ring.shape[1]
    batches = slots // batch
    turns = 4 * batches
    deep = corners.shape[0]

    def flips(s):
        return 3 - s // batches

    def sums(q, s, first, terms, total):
        unit = toggled(z, y, x, 1 - q % 2, 1 - q // 2, flips(s))
        base = unit * slots + (s % batches) * batch
        count = total.shape[1]

        def one(i, carry):
            slot = base + i
            rows = pl.ds(pl.multiple_of(first, 128), count)
            acc = jnp.dot(
                left[kind[slot], rows, :], right[block[slot]], preferred_element_type=jnp.float32
            )
            for term in terms:
                acc = acc + term[i].astype(jnp.float32)
            total[i] = acc.astype(total.dtype)
            return carry

        lax.fori_loop(0, batch, one, 0)

    mine, other = core * half, (1 - core) * half

    def sub(ref, first):
        return ref.at[:, pl.ds(first, part), :]

    def sib_copy(q, s):
        i = turns * q + s
        return remote(ring.at[q], from_sib.at[i], sib_s.at[i], sib_r.at[i], sibling)

    def a_copy(s):
        return remote(
            sub(corners.at[s % deep], 0), corner_a.at[s], ca_s.at[s], ca_r.at[s], (at_x, core)
        )

    def b_copy(s):
        return remote(
            sub(corners.at[s % deep], part), corner_b.at[s], cb_s.at[s], cb_r.at[s], (at_y, core)
        )

    def x_copy(s, n):
        rows = pl.ds(n * part, part)
        i = turns * n + s
        return remote(
            side_x.at[s % deep, :, rows, :], from_x.at[s, :, rows, :], x_s.at[i], x_r.at[i],
            (at_x, core),
        )

    def y_copy(s, n):
        rows = pl.ds((1 - n) * part, part)
        i = turns * n + s
        return remote(
            side_y.at[s % deep, :, rows, :], from_y.at[s, :, rows, :], y_s.at[i], y_r.at[i],
            (at_y, core),
        )

    def f_copy(s):
        src = middle.at[s % deep]
        g = s % batches
        dst = final.at[
            z // 2, pl.ds(g * batch, batch), pl.ds(pl.multiple_of(mine, 128), half), :
        ]
        recv = f_r.at[(2 * (z // 2) + core) * batches + g]
        target = (toggled(z, y, x, 0, 0, flips(s)), rank)
        return remote(src, dst, f_s.at[s], recv, target), pltpu.make_async_copy(src, dst, recv)

    def stays(s):
        return jnp.logical_and(s >= turns - batches, rank == core)

    def for_sibling(s, low, high):
        def one(q, carry):
            @pl.when(s >= 1)
            def _():
                sib_copy(q, s - 1).wait_send()

            sums(q, s, other, (), ring.at[q])
            sib_copy(q, s).start()
            return carry

        lax.fori_loop(low, high, one, 0)

    def fetched(q, s):
        i = 2 * q + s % 2
        return pltpu.make_async_copy(from_sib.at[turns * q + s], stage.at[i], stage_s.at[i])

    def fetch(q, s):
        sib_copy(q, s).wait_recv()
        fetched(q, s).start()

    def taken(q, s):
        return stage.at[2 * q + s % 2]

    def corner(s):
        @pl.when(s >= deep)
        def _():
            a_copy(s - deep).wait_send()
            b_copy(s - deep).wait_send()

        fetched(0, s).wait()
        sums(0, s, mine, (taken(0, s),), corners.at[s % deep])
        a_copy(s).start()
        b_copy(s).start()

    def direct_sides(s):
        @pl.when(s >= deep)
        def _():
            for n in range(2):
                x_copy(s - deep, n).wait_send()
                y_copy(s - deep, n).wait_send()

        fetched(1, s).wait()
        sums(1, s, mine, (sub(taken(1, s), 0),), sub(side_x.at[s % deep], 0))
        x_copy(s, 0).start()
        fetched(2, s).wait()
        sums(2, s, mine + part, (sub(taken(2, s), part),), sub(side_y.at[s % deep], part))
        y_copy(s, 0).start()

    def relayed(s):
        return (
            pltpu.make_async_copy(corner_b.at[s], sub(stage.at[8], 0), stage_s.at[8]),
            pltpu.make_async_copy(corner_a.at[s], sub(stage.at[8], part), stage_s.at[9]),
        )

    def relayed_in(s):
        b_copy(s).wait_recv()
        relayed(s)[0].start()
        a_copy(s).wait_recv()
        relayed(s)[1].start()

    def relayed_sides(s):
        relayed(s)[0].wait()
        sums(
            1, s, mine + part, (sub(taken(1, s), part), sub(stage.at[8], 0)),
            sub(side_x.at[s % deep], part),
        )
        x_copy(s, 1).start()
        relayed(s)[1].wait()
        sums(
            2, s, mine, (sub(taken(2, s), 0), sub(stage.at[8], part)), sub(side_y.at[s % deep], 0)
        )
        y_copy(s, 1).start()

    def centre_terms(s):
        return (
            pltpu.make_async_copy(from_x.at[s], stage.at[9], stage_s.at[10]),
            pltpu.make_async_copy(from_y.at[s], stage.at[10], stage_s.at[11]),
        )

    def centre_in(s):
        for n, copies in enumerate((x_copy, y_copy)):
            copies(s, 0).wait_recv()
            copies(s, 1).wait_recv()
            centre_terms(s)[n].start()

    def centre(s):
        @pl.when(s >= deep)
        def _():
            f_copy(s - deep)[0].wait_send()

        fetched(3, s).wait()
        for term in centre_terms(s):
            term.wait()
        sums(3, s, mine, (taken(3, s), stage.at[9], stage.at[10]), middle.at[s % deep])
        go, here = f_copy(s)

        @pl.when(stays(s))
        def _():
            here.start()

        @pl.when(jnp.logical_not(stays(s)))
        def _():
            go.start()

    home = rank == core
    pair_device = (toggled(z, y, x, 0, 0, 1), core)
    ends = [
        remote(y_in, y_other, end_s.at[0], end_r.at[0], pair_device),
        remote(da_in, da_other, end_s.at[1], end_r.at[1], pair_device),
        remote(end_low.at[0], result, end_s.at[2], end_r.at[2], sibling),
        remote(end_wide.at[0], result_grad, end_s.at[3], end_r.at[3], sibling),
    ]
    end_loads = [
        pltpu.make_async_copy(src, dst, end_load.at[i])
        for i, (src, dst) in enumerate(
            (
                (rows_in, end_wide.at[0]), (after_in, end_wide.at[1]), (dx_in, end_wide.at[2]),
                (y_in, end_low.at[0]), (da_in, end_low.at[1]),
                (y_other, end_low.at[2]), (da_other, end_low.at[3]),
            )
        )
    ]
    end_stores = [
        pltpu.make_async_copy(end_low.at[0], result, end_load.at[7]),
        pltpu.make_async_copy(end_wide.at[0], result_grad, end_load.at[8]),
    ]

    def finish_rows():
        for n in range(2):
            ends[n].wait_recv()
            end_loads[5 + n].start()
        for load in end_loads:
            load.wait()
        tall = 16

        def one(i, carry):
            at = pl.ds(pl.multiple_of(i * tall, tall), tall)
            y_all = end_low[0, at].astype(F32) + end_low[2, at].astype(F32) + gains[2:3]
            end_low[0, at] = (end_wide[1, at] + gains[0:1] * y_all).astype(end_low.dtype)
            da = end_low[1, at].astype(F32) + end_low[3, at].astype(F32)
            back, _ = normed_back(end_wide[0, at], da * (1.0 + gains[1:2]))
            end_wide[0, at] = end_wide[2, at] + back
            return carry

        lax.fori_loop(0, rows_in.shape[0] // tall, one, 0)
        ends[2].start()
        ends[3].start()
        for store in end_stores:
            store.start()

    @pl.when(jnp.logical_not(home))
    def _():
        ends[0].start()
        ends[1].start()

    def vec_copy(i):
        return remote(vec_out, vec_box.at[i], v_s.at[i], v_r.at[i], mates[i])

    def turn(step, carry):
        for i in range(5):

            @pl.when(step == 2 * i)
            def _():
                vec_copy(i).start()

        @pl.when(step + 2 < turns)
        def _():
            for_sibling(step + 2, 0, 4)

        @pl.when(step + 1 < turns)
        def _():
            corner(step + 1)
            direct_sides(step + 1)

        @pl.when(step < turns)
        def _():
            relayed_in(step)

        @pl.when(step >= 1)
        def _():
            centre_in(step - 1)

        @pl.when(step < turns)
        def _():
            relayed_sides(step)

        @pl.when(step >= 1)
        def _():
            centre(step - 1)

        @pl.when(step + 2 < turns)
        def _():
            for q in range(3):
                fetch(q, step + 2)

        @pl.when(step + 1 < turns)
        def _():
            fetch(3, step + 1)

        @pl.when(jnp.logical_and(step == 1, home))
        def _():
            for load in end_loads[:5]:
                load.start()

        @pl.when(jnp.logical_and(step == 3, home))
        def _():
            finish_rows()

        for i in range(5):

            @pl.when(step == 2 * i + 1)
            def _():
                vec_copy(i).wait()
                vec_out[...] = vec_out[...] + vec_box[i]

        return carry

    for_sibling(0, 0, 2)
    fetch(0, 0)
    corner(0)
    for_sibling(0, 2, 4)
    for q in range(1, 4):
        fetch(q, 0)
    direct_sides(0)
    for_sibling(1, 0, 4)
    for q in range(3):
        fetch(q, 1)
    lax.fori_loop(0, turns + 1, turn, 0)
    for q in range(4):
        sib_copy(q, turns - 1).wait_send()

    def settle(i, carry):
        s = turns - deep + i
        a_copy(s).wait_send()
        b_copy(s).wait_send()
        for n in range(2):
            x_copy(s, n).wait_send()
            y_copy(s, n).wait_send()

        @pl.when(jnp.logical_not(stays(s)))
        def _():
            f_copy(s)[0].wait_send()

        return carry

    lax.fori_loop(0, deep, settle, 0)

    @pl.when(home)
    def _():
        ends[2].wait_send()
        ends[3].wait_send()
        for store in end_stores:
            store.wait()

    @pl.when(jnp.logical_not(home))
    def _():
        ends[0].wait_send()
        ends[1].wait_send()
        ends[2].wait_recv()
        ends[3].wait_recv()

    for plane in range(2):
        for h in range(2):
            for g in range(batches):
                piece = final.at[plane, pl.ds(g * batch, batch), pl.ds(h * half, half), :]
                recv = f_r.at[(2 * plane + h) * batches + g]
                pltpu.make_async_copy(piece, piece, recv).wait()


def reduce_slots(holder, kinds, rows, columns, vector, ends, gains, slot_count):
    if not chip_pairs():
        grads = slot_grads(holder, kinds, [r.T for r in rows], columns)
        total = lax.psum_scatter(grads, "dp", scatter_dimension=0, tiled=True)
        x, after, dx, y_part, da_part = ends
        y_all, da_all = (
            v.astype(F32) + pair_swap(v).astype(F32) for v in (y_part, da_part)
        )
        result = (after + gains[0] * (y_all + gains[2])).astype(BF16)
        back, _ = normed_back(x, da_all * (1.0 + gains[1]))
        return total[None], lax.psum(vector, ("dp", "tensor")), result, dx + back
    left = rows
    width, depth = left[0].shape[0], max(r.shape[1] for r in rows)
    lanes = columns[0].shape[2]
    tiles = sum(c.shape[0] for c in columns)
    block = jnp.where(holder >= 0, holder, tiles)
    kind = kinds[jnp.maximum(holder, 0)]
    half = width // 2
    dma = pltpu.SemaphoreType.DMA
    scalars = pl.BlockSpec(memory_space=pltpu.SMEM)
    inside = pl.BlockSpec(memory_space=pltpu.VMEM)
    low = jnp.bfloat16

    batch = max(n for n in (1, 2, 3) if slot_count % n == 0)
    turns = 4 * slot_count // batch
    deep = 3

    def room(count, tall):
        return pltpu.HBM((count, batch, tall, lanes), low)

    def slab(count):
        return pltpu.VMEM((count, batch, half, lanes), low)

    outs = pl.pallas_call(
        reduce_kernel,
        out_shape=[
            pltpu.HBM((2, slot_count, width, lanes), low),
            jax.ShapeDtypeStruct(vector.shape, vector.dtype),
            pltpu.HBM(ends[0].shape, low), pltpu.HBM(ends[0].shape, F32),
            pltpu.HBM(ends[0].shape, low), pltpu.HBM(ends[0].shape, low),
            room(4 * turns, half), room(turns, half), room(turns, half),
            room(turns, half // 2), room(turns, half // 2),
        ],
        in_specs=[scalars, scalars] + [ANY] * (len(left) + len(columns) + 5) + [inside] * 2,
        out_specs=[ANY, inside] + [ANY] * 9,
        scratch_shapes=[
            pltpu.VMEM((len(left), width, depth), low),
            pltpu.VMEM((tiles + 1, depth, lanes), low),
            slab(4), slab(deep), slab(deep), slab(deep), slab(deep), slab(11),
            pltpu.VMEM((5,) + vector.shape, vector.dtype),
            pltpu.VMEM((3,) + ends[0].shape, F32),
            pltpu.VMEM((4,) + ends[0].shape, low),
        ]
        + [
            dma((n,))
            for n in (len(left) + len(columns), 12)
            + (4 * turns,) * 2
            + (2 * turns,) * 4
            + (turns,) * 6
            + (5, 5, 4, 4, 9)
        ],
        compiler_params=pltpu.CompilerParams(
            collective_id=1, has_side_effects=True, vmem_limit_bytes=58 * MIB
        ),
    )(
        kind,
        block,
        *[pltpu.with_memory_space_constraint(v, pltpu.HBM) for v in (*left, *columns, *ends)],
        gains,
        vector,
    )
    return outs[:4]


def kind_of_blocks(tile_count, heads_here, blocks_here):
    number = jnp.arange(tile_count)
    kind = number // heads_here
    table = jnp.array([0, 0, 0, 1, 2, 3, 3, 4], jnp.int32)
    late = jnp.where(number < 8 * heads_here + blocks_here, 5, 6)
    return jnp.where(number < 8 * heads_here, table[jnp.minimum(kind, 7)], late).astype(jnp.int32)


def slot_grads(holder, kinds, rows, columns):
    depth = max(r.shape[0] for r in rows)

    def deep(value, axis):
        room = [(0, 0)] * value.ndim
        room[axis] = (0, depth - value.shape[axis])
        return jnp.pad(value, room)

    left = jnp.stack([deep(r, 0) for r in rows])
    right = jnp.concatenate([deep(c, 1) for c in columns], 0)
    slots = holder.shape[0]
    used = (holder >= 0).astype(jnp.int32)
    block = jnp.maximum(holder, 0)
    kind = kinds[block]
    width = rows[0].shape[1]
    lanes = right.shape[2]

    def multiply(kind_ref, block_ref, used_ref, left_ref, right_ref, out_ref):
        slot = pl.program_id(0)

        @pl.when(used_ref[slot] == 1)
        def _():
            out_ref[0] = lax.dot_general(
                left_ref[kind_ref[slot]],
                right_ref[0],
                (((0,), (0,)), ((), ())),
                preferred_element_type=jnp.float32,
            ).astype(out_ref.dtype)

        @pl.when(used_ref[slot] == 0)
        def _():
            out_ref[...] = jnp.zeros_like(out_ref)

    return pl.pallas_call(
        multiply,
        grid_spec=pltpu.PrefetchScalarGridSpec(
            num_scalar_prefetch=3,
            grid=(slots,),
            in_specs=[
                pl.BlockSpec(left.shape, lambda s, kd, b, u: (0, 0, 0)),
                pl.BlockSpec((1, depth, lanes), lambda s, kd, b, u: (b[s], 0, 0)),
            ],
            out_specs=pl.BlockSpec((1, width, lanes), lambda s, kd, b, u: (s, 0, 0)),
        ),
        out_shape=jax.ShapeDtypeStruct((slots, width, lanes), jnp.bfloat16),
        compiler_params=pltpu.CompilerParams(vmem_limit_bytes=48 * MIB),
    )(kind, block, used, left, right)


def adam_slots(planes, master, moment_one, moment_two, slot_scale, filled):
    count, slot_count, width, lanes = planes.shape

    def step(scale_ref, fill_ref, grads, weight, one, two, new_weight, new_one, new_two, grad_box, boxes, reads, writes):
        sources = (weight, one, two)
        targets = (new_weight, new_one, new_two)

        def load(slot):
            return [
                pltpu.make_async_copy(src.at[0, slot], boxes.at[n, slot], reads.at[n, slot])
                for n, src in enumerate(sources)
            ] + [
                pltpu.make_async_copy(
                    grads.at[n, slot], grad_box.at[n, slot], reads.at[3 + n, slot]
                )
                for n in range(count)
            ]

        def store(slot):
            return [
                pltpu.make_async_copy(boxes.at[n, slot], dst.at[0, slot], writes.at[n, slot])
                for n, dst in enumerate(targets)
            ]

        def begin(slot, carry):
            for copy in load(slot):
                copy.start()
            return carry

        def work(slot, carry):
            for copy in load(slot):
                copy.wait()

            @pl.when(fill_ref[slot] == 1)
            def _():
                total = grad_box[0, slot].astype(jnp.float32)
                for n in range(1, count):
                    total = total + grad_box[n, slot].astype(jnp.float32)
                results = adam_step(
                    boxes[0, slot], total * scale_ref[slot], boxes[1, slot], boxes[2, slot],
                    TILE_RATE, TILE_DECAY,
                )
                for n, value in enumerate(results):
                    boxes[n, slot] = value

            for copy in store(slot):
                copy.start()
            return carry

        def finish(slot, carry):
            for copy in store(slot):
                copy.wait()
            return carry

        for part in (begin, work, finish):
            lax.fori_loop(0, slot_count, part, 0)

    scalars = pl.BlockSpec(memory_space=pltpu.SMEM)
    return pl.pallas_call(
        step,
        in_specs=[scalars, scalars] + [ANY] * 4,
        out_specs=[ANY] * 3,
        out_shape=[pltpu.HBM(master.shape, jnp.float32)] * 3,
        scratch_shapes=[
            pltpu.VMEM((count, slot_count, width, lanes), planes.dtype),
            pltpu.VMEM((3, slot_count, width, lanes), jnp.float32),
            pltpu.SemaphoreType.DMA((3 + count, slot_count)),
            pltpu.SemaphoreType.DMA((3, slot_count)),
        ],
        compiler_params=pltpu.CompilerParams(vmem_limit_bytes=40 * MIB),
    )(
        slot_scale,
        filled.astype(jnp.int32),
        *[
            pltpu.with_memory_space_constraint(v, pltpu.HBM)
            for v in (planes, master, moment_one, moment_two)
        ],
    )


SCALING = HEAD ** (-0.5)
BF16 = jnp.bfloat16
F32 = jnp.float32


def nn(left, right):
    return jnp.dot(left, right, preferred_element_type=F32)


def nt(left, right):
    return lax.dot_general(left, right, (((1,), (1,)), ((), ())), preferred_element_type=F32)


def tn(left, right):
    return lax.dot_general(left, right, (((0,), (0,)), ((), ())), preferred_element_type=F32)


def normed(rows):
    centre = rows - jnp.mean(rows, -1, keepdims=True)
    inverse = lax.rsqrt(jnp.mean(centre * centre, -1, keepdims=True) + NORM_EPS)
    return centre * inverse, inverse


def normed_back(rows, grad):
    unit, inverse = normed(rows)
    mean = jnp.mean(grad, -1, keepdims=True)
    return (grad - mean - unit * jnp.mean(grad * unit, -1, keepdims=True)) * inverse, unit


def total_of(rows):
    return jnp.sum(rows, 0, keepdims=True)


def turned(rows, cos_tab, sin_tab):
    even = lax.broadcasted_iota(jnp.int32, rows.shape, 1) % 2 == 0
    partner = jnp.where(even, pltpu.roll(rows, HEAD - 1, 1), pltpu.roll(rows, 1, 1))
    return rows * cos_tab + partner * sin_tab


def wide(column):
    return jnp.broadcast_to(column, (column.shape[0], HEAD))


def pack_sums(for_rows, for_text=None):
    out = wide(for_rows)
    if for_text is None:
        return out
    lane = lax.broadcasted_iota(jnp.int32, out.shape, 1)
    count = for_text.shape[0] // 2
    rest = jnp.zeros((out.shape[0] - count, HEAD), F32)
    first = jnp.concatenate([wide(for_text[:count]), rest], 0)
    second = jnp.concatenate([wide(for_text[count:]), rest], 0)
    return jnp.where(lane < 32, out, jnp.where(lane < 64, first, second))


def unpack_text(sums, count):
    return jnp.concatenate([sums[: count // 2, 32:33], sums[: count // 2, 64:65]], 0)


def softmax(scores):
    expo = jnp.exp(scores - jnp.max(scores, -1, keepdims=True))
    return expo / jnp.sum(expo, -1, keepdims=True)


def self_scores(query_low, key_low, tokens):
    scores = nt(query_low, key_low) * SCALING
    lane = lax.broadcasted_iota(jnp.int32, scores.shape, 1)
    return jnp.where(lane < tokens, scores, -1e30)


def whole(array):
    zeros = (0,) * len(array.shape)
    return pl.BlockSpec(array.shape, lambda *_: zeros)


def block_at(first, stride=1):
    return pl.BlockSpec((1, D, HEAD), lambda i, where: (where[first + stride * i], 0, 0))


def call(body, places, grid, ins, outs, scratch=(), vmem=24):
    specs = [spec if spec is not None else whole(array) for array, spec in ins]
    shapes = [pltpu.HBM(shape, kind) for shape, kind, _ in outs]
    out_specs = [
        spec if spec is not None else whole(shape) for (_, _, spec), shape in zip(outs, shapes)
    ]
    return pl.pallas_call(
        body,
        grid_spec=pltpu.PrefetchScalarGridSpec(
            num_scalar_prefetch=1,
            grid=(grid,),
            in_specs=specs,
            out_specs=out_specs,
            scratch_shapes=list(scratch),
        ),
        out_shape=shapes,
        compiler_params=pltpu.CompilerParams(vmem_limit_bytes=vmem * MIB),
    )(places, *[pltpu.with_memory_space_constraint(array, pltpu.HBM) for array, _ in ins])


def head_lanes(rows, per=1):
    return pl.BlockSpec((rows, per * HEAD), lambda h, *_: (0, h))


def heads_per_step(heads, most):
    return max(n for n in (1, 2, 3, 6) if heads % n == 0 and n <= most)


def lane_group(ref, j):
    return ref[:, j * HEAD : (j + 1) * HEAD]


def joined(refs):
    return jnp.concatenate([ref[0] for ref in refs], 1)


def project_self(places, everyone, rows, mod, vecs, heads):
    count = rows.shape[0]
    span = heads * HEAD

    def body(_, rows_ref, mod_ref, vec_ref, *refs):
        weights, (low, pre, value, sums, acc) = refs[:heads], refs[heads:]
        i = pl.program_id(0)

        @pl.when(i == 0)
        def _():
            unit, _ = normed(rows_ref[...])
            low[...] = (unit * (1.0 + mod_ref[1:2]) + mod_ref[0:1]).astype(BF16)

        made = nn(low[...], joined(weights))

        @pl.when(i == 0)
        def _():
            q = made + vec_ref[0:1]
            pre[0] = q
            acc[...] = wide(jnp.sum(q * q, -1, keepdims=True))

        @pl.when(i == 1)
        def _():
            k = made + vec_ref[1:2]
            pre[0] = k
            lane = lax.broadcasted_iota(jnp.int32, acc.shape, 1)
            sums[...] = jnp.where(lane < 64, acc[...], wide(jnp.sum(k * k, -1, keepdims=True)))

        @pl.when(i == 2)
        def _():
            value[...] = (made + vec_ref[2:3]).astype(BF16)

    return call(
        body, places, 3,
        [(rows, None), (mod, None), (vecs, None)]
        + [(everyone, block_at(h, heads)) for h in range(heads)],
        [
            ((count, D), BF16, None),
            ((2, count, span), F32, pl.BlockSpec((1, count, span), lambda i, _: (jnp.minimum(i, 1), 0, 0))),
            ((count, span), BF16, None),
            ((count, HEAD), F32, None),
        ],
        [pltpu.VMEM((count, HEAD), F32)],
    )


def attend_self(places, everyone, pre, value, sums, other, vecs, cos_tab, sin_tab, heads, tokens):
    count = value.shape[0]
    per = heads_per_step(heads, 2)
    steps = heads // per

    def body(_, pre_ref, value_ref, sum_ref, other_ref, vec_ref, cos_ref, sin_ref, *refs):
        weights, (q_ref, k_ref, o_ref, y_ref, acc) = refs[:per], refs[per:]
        h = pl.program_id(0)
        total = sum_ref[...] + other_ref[...]
        q_inv = lax.rsqrt(total[:, 0:1] / D + NORM_EPS)
        k_inv = lax.rsqrt(total[:, 64:65] / D + NORM_EPS)
        cos, sin = cos_ref[...], sin_ref[...]
        outs = []
        for j in range(per):
            lanes = slice(j * HEAD, (j + 1) * HEAD)
            q = turned(pre_ref[0, :, lanes] * q_inv * vec_ref[3:4, lanes], cos, sin).astype(BF16)
            k = turned(pre_ref[1, :, lanes] * k_inv * vec_ref[4:5, lanes], cos, sin).astype(BF16)
            q_ref[:, lanes] = q
            k_ref[:, lanes] = k
            chance = softmax(self_scores(q, k, tokens))
            out = nn(chance.astype(BF16), value_ref[:, lanes]).astype(BF16)
            o_ref[j] = out
            outs.append(out)
        part = nt(jnp.concatenate(outs, 1), joined(weights))

        @pl.when(h == 0)
        def _():
            acc[...] = part

        @pl.when(h > 0)
        def _():
            acc[...] = acc[...] + part

        @pl.when(h == steps - 1)
        def _():
            y_ref[...] = acc[...].astype(BF16)

    lanes = head_lanes(count, per)
    return call(
        body, places, steps,
        [
            (pre, pl.BlockSpec((2, count, per * HEAD), lambda h, _: (0, 0, h))),
            (value, lanes), (sums, None), (other, None),
            (vecs, head_lanes(vecs.shape[0], per)), (cos_tab, None), (sin_tab, None),
        ]
        + [(everyone, block_at(3 * heads + j, per)) for j in range(per)],
        [
            (value.shape, BF16, lanes),
            (value.shape, BF16, lanes),
            ((heads, count, HEAD), BF16, pl.BlockSpec((per, count, HEAD), lambda h, _: (h, 0, 0))),
            ((count, D), BF16, None),
        ],
        [pltpu.VMEM((count, D), F32)],
    )


def project_text(places, everyone, context, vecs, heads):
    count = context.shape[0]
    span = heads * HEAD

    def body(_, text_ref, vec_ref, *refs):
        weights, (key, value, sums) = refs[:heads], refs[heads:]
        i = pl.program_id(0)
        made = nn(text_ref[...], joined(weights))

        @pl.when(i == 0)
        def _():
            k = made + vec_ref[6:7]
            key[...] = k
            sums[...] = wide(jnp.sum(k * k, -1, keepdims=True))

        @pl.when(i == 1)
        def _():
            value[...] = (made + vec_ref[7:8]).astype(BF16)

    return call(
        body, places, 2,
        [(context, None), (vecs, None)]
        + [(everyone, block_at(5 * heads + h, heads)) for h in range(heads)],
        [((count, span), F32, None), ((count, span), BF16, None), ((count, HEAD), F32, None)],
    )


def project_cross(places, everyone, rows, part, other, mod, shared, vecs, text_sums, heads):
    count = rows.shape[0]
    span = heads * HEAD
    text = text_sums.shape[0]

    def body(_, rows_ref, part_ref, other_ref, mod_ref, shared_ref, vec_ref, text_ref, *refs):
        weights, (branch, after, low, pre, sums) = refs[:heads], refs[heads:]
        y = part_ref[...].astype(F32) + other_ref[...].astype(F32) + shared_ref[0:1]
        branch[...] = y
        x = rows_ref[...] + mod_ref[2:3] * y
        after[...] = x
        unit, _ = normed(x)
        a = (unit * shared_ref[3:4] + shared_ref[4:5]).astype(BF16)
        low[...] = a
        q = nn(a, joined(weights)) + vec_ref[5:6]
        pre[...] = q
        sums[...] = pack_sums(jnp.sum(q * q, -1, keepdims=True), text_ref[:, 0:1])

    return call(
        body, places, 1,
        [(v, None) for v in (rows, part, other, mod, shared, vecs, text_sums)]
        + [(everyone, block_at(4 * heads + h)) for h in range(heads)],
        [
            ((count, D), F32, None),
            ((count, D), F32, None),
            ((count, D), BF16, None),
            ((count, span), F32, None),
            ((count, HEAD), F32, None),
        ],
    )


def attend_cross(places, everyone, pre, key_pre, value, sums, other, vecs, heads):
    count, text = pre.shape[0], value.shape[0]
    per = heads_per_step(heads, 6)
    steps = heads // per

    def body(_, pre_ref, key_ref, value_ref, sum_ref, other_ref, vec_ref, *refs):
        weights, (q_ref, k_ref, o_ref, y_ref, acc) = refs[:per], refs[per:]
        h = pl.program_id(0)
        total = sum_ref[...] + other_ref[...]
        q_inv = lax.rsqrt(total[:, 0:1] / D + NORM_EPS)
        k_inv = lax.rsqrt(unpack_text(total, text) / D + NORM_EPS)
        outs = []
        for j in range(per):
            lanes = slice(j * HEAD, (j + 1) * HEAD)
            q = (pre_ref[:, lanes] * q_inv * vec_ref[8:9, lanes]).astype(BF16)
            k = (key_ref[:, lanes] * k_inv * vec_ref[9:10, lanes]).astype(BF16)
            q_ref[:, lanes] = q
            k_ref[:, lanes] = k
            chance = softmax(nt(q, k) * SCALING)
            out = nn(chance.astype(BF16), value_ref[:, lanes]).astype(BF16)
            o_ref[j] = out
            outs.append(out)
        part = nt(jnp.concatenate(outs, 1), joined(weights))

        @pl.when(h == 0)
        def _():
            acc[...] = part

        @pl.when(h > 0)
        def _():
            acc[...] = acc[...] + part

        @pl.when(h == steps - 1)
        def _():
            y_ref[...] = acc[...].astype(BF16)

    return call(
        body, places, steps,
        [
            (pre, head_lanes(count, per)), (key_pre, head_lanes(text, per)),
            (value, head_lanes(text, per)), (sums, None), (other, None),
            (vecs, head_lanes(vecs.shape[0], per)),
        ]
        + [(everyone, block_at(7 * heads + j, per)) for j in range(per)],
        [
            (pre.shape, BF16, head_lanes(count, per)),
            (value.shape, BF16, head_lanes(text, per)),
            ((heads, count, HEAD), BF16, pl.BlockSpec((per, count, HEAD), lambda h, _: (h, 0, 0))),
            ((count, D), BF16, None),
        ],
        [pltpu.VMEM((count, D), F32)],
        vmem=40,
    )


def hidden_group(blocks):
    return max(g for g in (7, 5, 4, 3, 2, 1) if blocks % g == 0)


def block_lanes(where, everyone, held, sems, first, group, steps):
    i = pl.program_id(0)

    def fetch(step, act):
        slot = step % 3
        for j in range(group):
            copy = pltpu.make_async_copy(
                everyone.at[where[first + step * group + j]],
                held.at[slot, :, pl.ds(j * HEAD, HEAD)],
                sems.at[slot, j],
            )
            copy.start() if act else copy.wait()

    @pl.when(i == 0)
    def _():
        fetch(0, True)
        if steps > 1:
            fetch(1, True)

    @pl.when(i + 2 < steps)
    def _():
        fetch(i + 2, True)

    fetch(i, False)
    return held[i % 3]


def lanes_scratch(group):
    return [pltpu.VMEM((3, D, group * HEAD), BF16), pltpu.SemaphoreType.DMA((3, group))]


def hidden_back(places, everyone, mod, cot, heads, blocks):
    count = cot.shape[0]
    group = hidden_group(blocks)
    steps = blocks // group

    def body(where, weights, mod_ref, cot_ref, grad, out, held, sems):
        @pl.when(pl.program_id(0) == 0)
        def _():
            grad[...] = (mod_ref[5:6] * cot_ref[...]).astype(BF16)

        down = block_lanes(where, weights, held, sems, 8 * heads + blocks, group, steps)
        out[...] = nn(grad[...], down).astype(BF16)

    return call(
        body, places, steps,
        [(everyone, ANY), (mod, None), (cot, None)],
        [
            ((count, D), BF16, None),
            ((count, blocks * HEAD), BF16, pl.BlockSpec((count, group * HEAD), lambda i, _: (0, i))),
        ],
        lanes_scratch(group),
        vmem=40,
    )


def hidden_both(places, everyone, after_one, part, other, mod, shared, d_act, up_bias, heads, blocks):
    count = after_one.shape[0]
    group = hidden_group(blocks)
    steps = blocks // group
    span = group * HEAD

    def body(where, weights, after_ref, part_ref, other_ref, mod_ref, shared_ref, d_ref, bias_ref, after, low, hidden, d_hidden, d_bias, da_ref, acc, held, sems):
        i = pl.program_id(0)

        @pl.when(i == 0)
        def _():
            x = after_ref[...] + part_ref[...].astype(F32) + other_ref[...].astype(F32)
            x = x + shared_ref[1:2]
            after[...] = x
            unit, _ = normed(x)
            low[...] = (unit * (1.0 + mod_ref[4:5]) + mod_ref[3:4]).astype(BF16)
            acc[...] = jnp.zeros_like(acc)

        up = block_lanes(where, weights, held, sems, 8 * heads, group, steps)
        pre = nn(low[...], up) + bias_ref[...]
        square = pre * pre
        bent = jnp.tanh(GELU_COEF * (pre + 0.044715 * pre * square))
        act = (0.5 * pre * (1.0 + bent)).astype(BF16)
        slope = 0.5 * (1.0 + bent) + 0.5 * pre * (1.0 - bent * bent) * (
            GELU_COEF * (1.0 + 3.0 * 0.044715 * square)
        )
        dh = (d_ref[...].astype(F32) * slope).astype(BF16)
        d_bias[...] = total_of(dh.astype(F32))
        for j in range(group):
            hidden[j] = act[:, j * HEAD : (j + 1) * HEAD]
            d_hidden[j] = dh[:, j * HEAD : (j + 1) * HEAD]
        acc[...] = acc[...] + nt(dh, up)

        @pl.when(i == steps - 1)
        def _():
            da_ref[...] = acc[...].astype(BF16)

    tall = pl.BlockSpec((group, count, HEAD), lambda i, _: (i, 0, 0))
    flat = pl.BlockSpec((1, span), lambda i, _: (0, i))
    return call(
        body, places, steps,
        [(everyone, ANY)]
        + [(v, None) for v in (after_one, part, other, mod, shared)]
        + [(d_act, pl.BlockSpec((count, span), lambda i, _: (0, i))), (up_bias, flat)],
        [
            ((count, D), F32, None),
            ((count, D), BF16, None),
            ((blocks, count, HEAD), BF16, tall),
            ((blocks, count, HEAD), BF16, tall),
            (up_bias.shape, F32, flat),
            ((count, D), BF16, None),
        ],
        [pltpu.VMEM((count, D), F32)] + lanes_scratch(group),
        vmem=40,
    )


def hidden_out(places, everyone, hidden, heads):
    blocks, count = hidden.shape[:2]
    group = hidden_group(blocks)
    steps = blocks // group

    def body(where, weights, hidden_ref, y_ref, acc, held, sems):
        i = pl.program_id(0)
        down = block_lanes(where, weights, held, sems, 8 * heads + blocks, group, steps)
        part = nt(jnp.concatenate([hidden_ref[j] for j in range(group)], 1), down)

        @pl.when(i == 0)
        def _():
            acc[...] = part

        @pl.when(i > 0)
        def _():
            acc[...] = acc[...] + part

        @pl.when(i == steps - 1)
        def _():
            y_ref[...] = acc[...].astype(BF16)

    return call(
        body, places, steps,
        [(everyone, ANY), (hidden, pl.BlockSpec((group, count, HEAD), lambda i, _: (i, 0, 0)))],
        [((count, D), BF16, None)],
        [pltpu.VMEM((count, D), F32)] + lanes_scratch(group),
        vmem=40,
    )[0]


def cross_back(places, everyone, cot, after_two, part, other, mod, query, key, value, pre, key_pre, vecs, heads):
    count, text = query.shape[0], key.shape[0]
    per = heads_per_step(heads, 6)
    steps = heads // per

    def body(_, cot_ref, after_ref, part_ref, other_ref, mod_ref, q_ref, k_ref, v_ref, pre_ref, key_ref, vec_ref, *refs):
        weights, (dx_ref, low_ref, dq_ref, dk_ref, dv_ref, sums, q_acc, k_acc) = refs[:per], refs[per:]
        h = pl.program_id(0)

        @pl.when(h == 0)
        def _():
            da = part_ref[...].astype(F32) + other_ref[...].astype(F32)
            back, _ = normed_back(after_ref[...], da * (1.0 + mod_ref[4:5]))
            dx = cot_ref[...] + back
            dx_ref[...] = dx
            low_ref[...] = dx.astype(BF16)
            q_acc[...] = jnp.zeros_like(q_acc)
            k_acc[...] = jnp.zeros_like(k_acc)

        do_all = nn(low_ref[...], joined(weights)).astype(BF16)
        q_sums, k_sums = 0.0, 0.0
        for j in range(per):
            lanes = slice(j * HEAD, (j + 1) * HEAD)
            do = do_all[:, lanes]
            q, k = q_ref[:, lanes], k_ref[:, lanes]
            chance = softmax(nt(q, k) * SCALING)
            dp = nt(do, v_ref[:, lanes])
            ds = (chance * (dp - jnp.sum(chance * dp, -1, keepdims=True))).astype(BF16)
            dv_ref[j] = tn(chance.astype(BF16), do).astype(BF16)
            dq = nn(ds, k) * SCALING
            dk = tn(ds, q) * SCALING
            dq_ref[:, lanes] = dq
            dk_ref[:, lanes] = dk
            q_sums += pre_ref[:, lanes] * vec_ref[8:9, lanes] * dq
            k_sums += key_ref[:, lanes] * vec_ref[9:10, lanes] * dk
        q_acc[...] = q_acc[...] + q_sums
        k_acc[...] = k_acc[...] + k_sums

        @pl.when(h == steps - 1)
        def _():
            sums[...] = pack_sums(
                jnp.sum(q_acc[...], -1, keepdims=True), jnp.sum(k_acc[...], -1, keepdims=True)
            )

    return call(
        body, places, steps,
        [(v, None) for v in (cot, after_two, part, other, mod)]
        + [
            (query, head_lanes(count, per)), (key, head_lanes(text, per)),
            (value, head_lanes(text, per)), (pre, head_lanes(count, per)),
            (key_pre, head_lanes(text, per)), (vecs, head_lanes(vecs.shape[0], per)),
        ]
        + [(everyone, block_at(7 * heads + j, per)) for j in range(per)],
        [
            ((count, D), F32, None),
            ((count, D), BF16, None),
            (query.shape, F32, head_lanes(count, per)),
            (key.shape, F32, head_lanes(text, per)),
            ((heads, text, HEAD), BF16, pl.BlockSpec((per, text, HEAD), lambda h, _: (h, 0, 0))),
            ((count, HEAD), F32, None),
        ],
        [pltpu.VMEM((count, HEAD), F32), pltpu.VMEM((text, HEAD), F32)],
        vmem=48,
    )


def norm_grad(pre, inverse, gain, incoming, total):
    grad = inverse * (gain * incoming) - pre * (inverse * inverse * inverse) * (total / D)
    low = grad.astype(BF16)
    return low, total_of(low.astype(F32)), total_of(incoming * pre * inverse)


def cross_back_rows(places, everyone, pre, key_pre, dq, dk, dv, squares, squares_other, sums, sums_other, vecs, heads):
    count, text = pre.shape[0], key_pre.shape[0]
    per = heads_per_step(heads, 6)
    steps = heads // per

    def body(_, pre_ref, key_ref, dq_ref, dk_ref, dv_ref, sq_ref, sqo_ref, sum_ref, sumo_ref, vec_ref, *refs):
        weights, (gq_ref, gk_ref, vec_out, da_ref, acc) = refs[:per], refs[per:]
        h = pl.program_id(0)
        squares_all = sq_ref[...] + sqo_ref[...]
        total = sum_ref[...] + sumo_ref[...]
        q_inv = lax.rsqrt(squares_all[:, 0:1] / D + NORM_EPS)
        k_inv = lax.rsqrt(unpack_text(squares_all, text) / D + NORM_EPS)
        q_total, k_total = total[:, 0:1], unpack_text(total, text)
        lows = []
        for j in range(per):
            lanes = slice(j * HEAD, (j + 1) * HEAD)
            low_q, bias_q, gain_q = norm_grad(
                pre_ref[:, lanes], q_inv, vec_ref[8:9, lanes], dq_ref[:, lanes], q_total
            )
            low_k, bias_k, gain_k = norm_grad(
                key_ref[:, lanes], k_inv, vec_ref[9:10, lanes], dk_ref[:, lanes], k_total
            )
            gq_ref[j] = low_q
            gk_ref[j] = low_k
            lows.append(low_q)
            bias_v = total_of(dv_ref[j].astype(F32))
            vec_out[:, lanes] = jnp.concatenate(
                [bias_q, bias_k, bias_v, gain_q, gain_k, jnp.zeros((3, HEAD), F32)], 0
            )
        part = nt(jnp.concatenate(lows, 1), joined(weights))

        @pl.when(h == 0)
        def _():
            acc[...] = part

        @pl.when(h > 0)
        def _():
            acc[...] = acc[...] + part

        @pl.when(h == steps - 1)
        def _():
            da_ref[...] = acc[...].astype(BF16)

    tall = pl.BlockSpec((per, count, HEAD), lambda h, _: (h, 0, 0))
    tall_text = pl.BlockSpec((per, text, HEAD), lambda h, _: (h, 0, 0))
    return call(
        body, places, steps,
        [
            (pre, head_lanes(count, per)), (key_pre, head_lanes(text, per)),
            (dq, head_lanes(count, per)), (dk, head_lanes(text, per)), (dv, tall_text),
            (squares, None), (squares_other, None), (sums, None), (sums_other, None),
            (vecs, head_lanes(vecs.shape[0], per)),
        ]
        + [(everyone, block_at(4 * heads + j, per)) for j in range(per)],
        [
            ((heads, count, HEAD), BF16, tall),
            ((heads, text, HEAD), BF16, tall_text),
            ((8, heads * HEAD), F32, head_lanes(8, per)),
            ((count, D), BF16, None),
        ],
        [pltpu.VMEM((count, D), F32)],
        vmem=40,
    )


def self_back(places, everyone, dx_two, after_one, part, other, mod, shared, branch, query, key, value, pre, vecs, cos_tab, sin_tab, heads, tokens):
    count = query.shape[0]
    per = heads_per_step(heads, 2)
    steps = heads // per

    def body(_, dx_in, after_ref, part_ref, other_ref, mod_ref, shared_ref, branch_ref, q_ref, k_ref, v_ref, pre_ref, vec_ref, cos_ref, sin_ref, *refs):
        weights, (dx_ref, low_ref, d_ref, dv_ref, sums, vec_out, q_acc, k_acc) = refs[:per], refs[per:]
        h = pl.program_id(0)

        @pl.when(h == 0)
        def _():
            da = part_ref[...].astype(F32) + other_ref[...].astype(F32)
            back, _ = normed_back(after_ref[...], da * shared_ref[3:4])
            dx = dx_in[...] + back
            dx_ref[...] = dx
            low = (mod_ref[2:3] * dx).astype(BF16)
            low_ref[...] = low
            vec_out[0:1] = 0.5 * total_of(low.astype(F32))
            vec_out[1:2] = 0.5 * total_of(dx * branch_ref[...])
            q_acc[...] = jnp.zeros_like(q_acc)
            k_acc[...] = jnp.zeros_like(k_acc)

        do_all = nn(low_ref[...], joined(weights)).astype(BF16)
        cos, sin = cos_ref[...], -sin_ref[...]
        q_sums, k_sums = 0.0, 0.0
        for j in range(per):
            lanes = slice(j * HEAD, (j + 1) * HEAD)
            do = do_all[:, lanes]
            q, k = q_ref[:, lanes], k_ref[:, lanes]
            chance = softmax(self_scores(q, k, tokens))
            dp = nt(do, v_ref[:, lanes])
            ds = (chance * (dp - jnp.sum(chance * dp, -1, keepdims=True))).astype(BF16)
            dv_ref[j] = tn(chance.astype(BF16), do).astype(BF16)
            dq = turned(nn(ds, k) * SCALING, cos, sin)
            dk = turned(tn(ds, q) * SCALING, cos, sin)
            d_ref[0, :, lanes] = dq
            d_ref[1, :, lanes] = dk
            q_sums += pre_ref[0, :, lanes] * vec_ref[3:4, lanes] * dq
            k_sums += pre_ref[1, :, lanes] * vec_ref[4:5, lanes] * dk
        q_acc[...] = q_acc[...] + q_sums
        k_acc[...] = k_acc[...] + k_sums

        @pl.when(h == steps - 1)
        def _():
            lane = lax.broadcasted_iota(jnp.int32, q_acc.shape, 1)
            sums[...] = jnp.where(
                lane < 64,
                wide(jnp.sum(q_acc[...], -1, keepdims=True)),
                wide(jnp.sum(k_acc[...], -1, keepdims=True)),
            )

    lanes = head_lanes(count, per)
    pair = pl.BlockSpec((2, count, per * HEAD), lambda h, _: (0, 0, h))
    return call(
        body, places, steps,
        [(v, None) for v in (dx_two, after_one, part, other, mod, shared, branch)]
        + [
            (query, lanes), (key, lanes), (value, lanes), (pre, pair),
            (vecs, head_lanes(vecs.shape[0], per)), (cos_tab, None), (sin_tab, None),
        ]
        + [(everyone, block_at(3 * heads + j, per)) for j in range(per)],
        [
            ((count, D), F32, None),
            ((count, D), BF16, None),
            (pre.shape, F32, pair),
            ((heads, count, HEAD), BF16, pl.BlockSpec((per, count, HEAD), lambda h, _: (h, 0, 0))),
            ((count, HEAD), F32, None),
            ((2, D), F32, None),
        ],
        [pltpu.VMEM((count, HEAD), F32), pltpu.VMEM((count, HEAD), F32)],
        vmem=32,
    )


def self_back_rows(places, everyone, rows, pre, grads, dv, squares, squares_other, sums, sums_other, vecs, heads):
    count = pre.shape[1]
    per = heads_per_step(heads, 2)
    steps = heads // per

    def body(_, rows_ref, pre_ref, d_ref, dv_ref, sq_ref, sqo_ref, sum_ref, sumo_ref, vec_ref, *refs):
        weights, (gq_ref, gk_ref, vec_out, da_ref, row_out, acc) = refs[: 3 * per], refs[3 * per :]
        h = pl.program_id(0)
        squares_all = sq_ref[...] + sqo_ref[...]
        total = sum_ref[...] + sumo_ref[...]
        inverses = [
            lax.rsqrt(squares_all[:, n : n + 1] / D + NORM_EPS) for n in (0, 64)
        ]
        lows = []
        for j in range(per):
            lanes = slice(j * HEAD, (j + 1) * HEAD)
            biases, gains = [], []
            for n, out in enumerate((gq_ref, gk_ref)):
                low, bias, gain = norm_grad(
                    pre_ref[n, :, lanes], inverses[n], vec_ref[3 + n : 4 + n, lanes],
                    d_ref[n, :, lanes], total[:, 64 * n : 64 * n + 1],
                )
                out[j] = low
                lows.append(low)
                biases.append(bias)
                gains.append(gain)
            dv_low = dv_ref[j]
            lows.append(dv_low)
            vec_out[:, lanes] = jnp.concatenate(
                biases + [total_of(dv_low.astype(F32))] + gains + [jnp.zeros((3, HEAD), F32)], 0
            )
        part = nt(jnp.concatenate(lows, 1), joined(weights))

        @pl.when(h == 0)
        def _():
            acc[...] = part

        @pl.when(h > 0)
        def _():
            acc[...] = acc[...] + part

        @pl.when(h == steps - 1)
        def _():
            da = acc[...]
            da_ref[...] = da.astype(BF16)
            row_out[0:1] = total_of(da)
            row_out[1:2] = total_of(da * normed(rows_ref[...])[0])

    tall = pl.BlockSpec((per, count, HEAD), lambda h, _: (h, 0, 0))
    pair = pl.BlockSpec((2, count, per * HEAD), lambda h, _: (0, 0, h))
    return call(
        body, places, steps,
        [
            (rows, None), (pre, pair), (grads, pair), (dv, tall), (squares, None),
            (squares_other, None), (sums, None), (sums_other, None),
            (vecs, head_lanes(vecs.shape[0], per)),
        ]
        + [(everyone, block_at(n * heads + j, per)) for j in range(per) for n in range(3)],
        [
            ((heads, count, HEAD), BF16, tall),
            ((heads, count, HEAD), BF16, tall),
            ((8, heads * HEAD), F32, head_lanes(8, per)),
            ((count, D), BF16, None),
            ((2, D), F32, None),
        ],
        [pltpu.VMEM((count, D), F32)],
        vmem=40,
    )


def shared_sums(places, after_one, after_two, grad_two, grad_three, cot, da_two, da_three, y_three, shared):
    def body(_, x1_ref, x2_ref, dy2, dy3, cot_ref, da2, da3, y3, shared_ref, out):
        out[...] = jnp.zeros_like(out)
        out[1:2] = 0.5 * total_of(dy2[...].astype(F32))
        out[2:3] = 0.5 * total_of(dy3[...].astype(F32))
        part = da3[...].astype(F32)
        out[3:4] = total_of(part * normed(x1_ref[...])[0])
        out[4:5] = total_of(part)
        part = da2[...].astype(F32)
        out[8:9] = total_of(part)
        out[9:10] = total_of(part * normed(x2_ref[...])[0])
        out[10:11] = total_of(cot_ref[...] * (y3[...].astype(F32) + 0.5 * shared_ref[2:3]))

    return call(
        body, places, 1,
        [(v, None) for v in (after_one, after_two, grad_two, grad_three, cot, da_two, da_three, y_three, shared)],
        [(shared.shape, F32, None)],
    )[0]


def body(
    latents,
    context,
    cotangent,
    positions,
    step_ids,
    owners,
    time_table,
    master,
    first_moment,
    second_moment,
    head_params,
    head_first,
    head_second,
    shared_params,
    shared_first,
    shared_second,
):
    tensors = lax.axis_size("tensor")
    devices = lax.axis_size("dp")
    slot_count = master.shape[1]
    tile_count = owners.shape[0]
    heads_here = HEADS // tensors
    blocks_here = FF // (HEAD * tensors)
    width_here = D // tensors
    places, holder = owner_layout(owners, slot_count, devices)
    scales = tile_scales(tile_count, heads_here, blocks_here)
    rank = pair_rank()
    my_slots = lax.axis_index("dp") * slot_count + jnp.arange(slot_count, dtype=jnp.int32)
    holds = places[None, :] == my_slots[:, None]
    slot_scale = jnp.sum(jnp.where(holds, scales[None, :], 0.0), axis=1)
    filled = jnp.any(holds, axis=1)
    scaled = (master[0] * slot_scale[:, None, None]).astype(jnp.bfloat16)
    half = latents.shape[0]
    tokens = 2 * half
    count = -(-tokens // 16) * 16
    taller = ((0, -half % 16), (0, 0))
    small = jnp.concatenate(
        [
            head_params[0],
            positions.reshape(-1).astype(jnp.float32),
            step_ids.astype(jnp.float32),
        ]
    )
    packed = jnp.pad(small, (0, -small.shape[0] % 1024)).reshape(-1, HEAD)
    everyone, lats, cots, context, packed = gather_slots(
        scaled, jnp.pad(latents, taller), jnp.pad(cotangent, taller), context, packed
    )
    small = packed.reshape(-1)
    vectors = small[: head_params.shape[1]]
    small = small[head_params.shape[1] :]
    positions = small[: positions.size].reshape(positions.shape)
    step = small[positions.size]
    vecs = vectors[: 10 * width_here].reshape(10, width_here)
    up_bias = vectors[10 * width_here :].reshape(1, -1)
    chosen = (step == jnp.arange(TSTEPS)).astype(jnp.float32)
    mod = shared_params[5:11] + jnp.einsum(
        "s,skd->kd", chosen, time_table, precision=lax.Precision.HIGHEST
    )
    cos_tab, sin_tab = rope_tables(positions, HEAD)
    sin_tab = jnp.where(jnp.arange(HEAD) % 2 == 0, -sin_tab, sin_tab)
    cos_tab, sin_tab = (jnp.pad(t, ((0, count - tokens), (0, 0))) for t in (cos_tab, sin_tab))

    def all_rows(halves):
        rows = jnp.concatenate([halves[0, :half], halves[1, :half]], 0)
        return jnp.pad(rows, ((0, count - tokens), (0, 0))).astype(jnp.float32)

    def upright(rows):
        return jnp.pad(rows, ((0, -rows.shape[0] % HEAD), (0, 0))).T

    def beside(*values):
        return lax.optimization_barrier(values)

    rows, cot = all_rows(lats), all_rows(cots)
    low_one, pre_one, value_one, squares_one = project_self(
        places, everyone, rows, mod, vecs, heads_here
    )
    squares_one_other = pair_swap(squares_one)
    query_one, key_one, heads_one, part_one = attend_self(
        places, everyone, pre_one, value_one, squares_one, squares_one_other, vecs, cos_tab,
        sin_tab, heads_here, tokens,
    )
    part_one, context = beside(part_one, context)
    part_one_other = pair_swap(part_one)
    key_pre, value_two, text_squares = project_text(places, everyone, context, vecs, heads_here)
    left_context, left_one = upright(context), upright(low_one)
    part_one_other, key_pre, left_context, left_one = beside(
        part_one_other, key_pre, left_context, left_one
    )
    branch_one, after_one, low_two, pre_two, squares_two = project_cross(
        places, everyone, rows, part_one, part_one_other, mod, shared_params, vecs,
        text_squares, heads_here,
    )
    squares_two_other = pair_swap(squares_two)
    query_two, key_two, heads_two, part_two = attend_cross(
        places, everyone, pre_two, key_pre, value_two, squares_two, squares_two_other, vecs,
        heads_here,
    )
    part_two, cot, low_two = beside(part_two, cot, low_two)
    part_two_other = pair_swap(part_two)
    grad_three, d_act = hidden_back(places, everyone, mod, cot, heads_here, blocks_here)
    left_two, left_grad_three = upright(low_two), upright(grad_three)
    part_two_other, d_act, left_two, left_grad_three = beside(
        part_two_other, d_act, left_two, left_grad_three
    )
    after_two, low_three, hidden, d_hidden, d_up_bias, da_two = hidden_both(
        places, everyone, after_one, part_two, part_two_other, mod, shared_params, d_act, up_bias,
        heads_here, blocks_here,
    )
    da_two_other = pair_swap(da_two)
    y_three = hidden_out(places, everyone, hidden, heads_here)
    left_three = upright(low_three)
    da_two_other, y_three, left_three = beside(da_two_other, y_three, left_three)
    dx_two, grad_two, dq_two, dk_two, dv_two, sums_two = cross_back(
        places, everyone, cot, after_two, da_two, da_two_other, mod, query_two, key_two,
        value_two, pre_two, key_pre, vecs, heads_here,
    )
    query_grad_two, key_grad_two, vecs_two, da_three = cross_back_rows(
        places, everyone, pre_two, key_pre, dq_two, dk_two, dv_two, squares_two,
        squares_two_other, sums_two, pair_swap(sums_two), vecs, heads_here,
    )
    da_three_other = pair_swap(da_three)
    shared_grad = shared_sums(
        places, after_one, after_two, grad_two, grad_three, cot, da_two, da_three, y_three,
        shared_params,
    )
    left_grad_two = upright(grad_two)
    da_three_other, shared_grad, left_grad_two = beside(da_three_other, shared_grad, left_grad_two)
    dx_one, grad_one, d_one, dv_one, sums_one, rows_a = self_back(
        places, everyone, dx_two, after_one, da_three, da_three_other, mod, shared_params,
        branch_one, query_one, key_one, value_one, pre_one, vecs, cos_tab, sin_tab, heads_here,
        tokens,
    )
    query_grad_one, key_grad_one, vecs_one, da_one, rows_b = self_back_rows(
        places, everyone, rows, pre_one, d_one, dv_one, squares_one, squares_one_other, sums_one,
        pair_swap(sums_one), vecs, heads_here,
    )
    shared_grad = jnp.concatenate(
        [rows_a[0:1], shared_grad[1:5], rows_b, rows_a[1:2], shared_grad[8:]], 0
    )
    head_grad = jnp.concatenate(
        [vecs_one[:5].reshape(-1), vecs_two[:5].reshape(-1), d_up_bias.reshape(-1)]
    )
    tensor_rank = lax.axis_index("tensor")
    head_padded = jnp.where(jnp.arange(tensors)[:, None] == rank, head_grad[None, :], 0.0)
    vector = jnp.concatenate([head_padded.reshape(-1), shared_grad.reshape(-1)])
    vector = jnp.pad(vector, (0, -vector.shape[0] % 1024)).reshape(-1, 128)
    parts, vector, output, grad_input = reduce_slots(
        holder,
        kind_of_blocks(tile_count, heads_here, blocks_here),
        (left_one, upright(grad_one), left_two, left_context, left_grad_two, left_three, left_grad_three),
        (
            query_grad_one,
            key_grad_one,
            dv_one,
            heads_one,
            query_grad_two,
            key_grad_two,
            dv_two,
            heads_two,
            d_hidden,
            hidden,
        ),
        vector,
        (rows, after_two, dx_one, y_three, da_one),
        jnp.concatenate([mod[5:6], mod[1:2], shared_params[2:3], jnp.zeros((5, D), F32)], 0),
        slot_count,
    )
    output, grad_input = (
        lax.dynamic_slice_in_dim(v, lax.axis_index("tensor") * half, half, 0)
        for v in (output, grad_input)
    )
    new_master, new_first, new_second = adam_slots(
        parts, master, first_moment, second_moment, slot_scale, filled
    )
    vector = vector.reshape(-1)
    head_total = vector[: head_padded.size].reshape(head_padded.shape)
    shared_total = vector[head_padded.size : head_padded.size + shared_grad.size]
    shared_total = shared_total.reshape(shared_grad.shape)
    mine_head = lax.dynamic_slice_in_dim(head_total, tensor_rank, 1, 0)
    new_head, new_head_first, new_head_second = adam_step(
        head_params, mine_head, head_first, head_second, VECTOR_RATE, 0.0
    )
    new_shared, new_shared_first, new_shared_second = adam_step(
        shared_params, shared_total, shared_first, shared_second, VECTOR_RATE, 0.0
    )
    return (
        output,
        grad_input,
        new_master,
        new_first,
        new_second,
        new_head,
        new_head_first,
        new_head_second,
        new_shared,
        new_shared_first,
        new_shared_second,
    )


def solution(mesh):
    return jax.shard_map(
        body,
        mesh=mesh,
        in_specs=(
            P(("dp", "tensor"), None),
            P("dp", None),
            P(("dp", "tensor"), None),
            P(None, "dp"),
            P("dp"),
            P(),
            P(),
            P("tensor", "dp", None, None),
            P("tensor", "dp", None, None),
            P("tensor", "dp", None, None),
            P("tensor", None),
            P("tensor", None),
            P("tensor", None),
            P(),
            P(),
            P(),
        ),
        out_specs=(
            P(("dp", "tensor"), None),
            P(("dp", "tensor"), None),
            P("tensor", "dp", None, None),
            P("tensor", "dp", None, None),
            P("tensor", "dp", None, None),
            P("tensor", None),
            P("tensor", None),
            P("tensor", None),
            P(),
            P(),
            P(),
        ),
        check_vma=False,
    )
```
